32 devices in a mesh: maps: 4 (over y, x), rows: 8 (over z, core).
Axes of the slice: x: 2, y: 2, z: 4, core: 2. Of those that a mesh axis runs over, the one named last changes fastest.
Arguments:
- block_input: bfloat16 [12, 16, 60, 512], P('maps', 'rows'), may hold values from -42 to 42, as said below
- conv_weights: bfloat16 [3, 3, 3, 512, 512], replicated, may hold values from -0.09375 to 0.09375
- norm_gains: float32 [3, 512], replicated, may hold values from 0.1 to 1.9
- norm_shifts: float32 [3, 512], replicated, may hold values from -3 to 3
- map_width: int32 [12], replicated, may hold values from 50 to 60, as said below
- map_group: int32 [12], replicated, may hold values from 0 to 2, as said below
- pool_index: int32 [12, 8, 30, 512], P('maps', 'rows'), may hold values from 0 to 3
- task_mask: int32 [12, 3], P('maps'), may hold values 0 or 1
- task_weights: float32 [3], replicated, may hold values from 0.5 to 2
- task_grads: bfloat16 [3, 12, 8, 30, 512], P(None, 'maps', 'rows'), may hold values from -6 to 6
Outputs:
- pooled: bfloat16 [12, 8, 30, 512], P('maps', 'rows')
- input_grad: float32 [12, 16, 60, 512], P('maps', 'rows')
- kernel_grads: float32 [3, 3, 3, 512, 512], replicated
- gain_grads: float32 [3, 512], replicated
- shift_grads: float32 [3, 512], replicated
The draws below stay inside these ranges and needn't reach their ends.
Inputs may be any that keep to these rules, and one draw needn't show every extreme that they name: `block_input`: maps have row scales that differ within a map and a scale per map. `map_width`: every map is 60 or 60 - 2 * (5) columns wide, and exactly 4 maps are the narrower; columns past a map's width are not part of it. `map_group`: each domain holds exactly 4 maps.
All inputs are finite; a program needn't handle non-finite values. No bound on the sum of `task_mask` on one device may be relied on, other than what follows from the above.
Results may differ from the reference program's by a relative error of at most 0.009.
Values may be sent and summed in bfloat16 or wider, within the bound.
A program may use at most 192 MiB of HBM per device.

```python
import math
import jax
import jax.numpy as jnp
from jax import lax

CH = 512
LAYERS = 3
DOMAINS = 3
TASKS = 3
WIDTH = 60
MAPS = 12
HEIGHT = 16


def draw_block_input(key, part):
    key = jax.random.fold_in(key, 3)
    seeds = jax.random.split(key, 3)
    position = jnp.arange(HEIGHT, dtype=jnp.float32) / (HEIGHT - 1)
    ground = jnp.clip(jax.random.normal(seeds[0], (MAPS, HEIGHT, WIDTH, CH), jnp.float32), -4.0, 4.0)
    rising = 1.0 + 2.0 * position
    across = jax.random.uniform(seeds[1], (WIDTH,), jnp.float32, 0.5, 1.5)
    per_map = jnp.exp(jax.random.uniform(seeds[2], (MAPS,), jnp.float32, -0.6931472, 0.6931472))
    return (ground * rising[None, :, None, None] * across[None, None, :, None] * per_map[:, None, None, None]).astype(jnp.bfloat16)


def draw_map_width(key, part):
    key = jax.random.fold_in(key, 5)
    shuffled = jax.random.permutation(key, MAPS)
    narrow = shuffled < MAPS // 3
    return jnp.where(narrow, WIDTH - 2 * (WIDTH // 12), WIDTH).astype(jnp.int32)


def draw_map_group(key, part):
    key = jax.random.fold_in(key, 7)
    shuffled = jax.random.permutation(key, MAPS)
    return (shuffled % DOMAINS).astype(jnp.int32)


def set_ends(array, stream_key, smallest, top_value):
    longest = array.shape.index(max(array.shape))
    spots = []
    for shift in (0, 1):
        where = [jax.random.randint(jax.random.fold_in(stream_key, axis), (), 0, length) for axis, length in enumerate(array.shape)]
        where[longest] = (where[longest] + shift) % array.shape[longest]
        spots.append(tuple(where))
    return array.at[spots[0]].set(smallest).at[spots[1]].set(top_value)


def levels(key, shape, cuts, least, high):
    loudness, own = 1.0, jax.random.fold_in(key, 6)
    for dim, blocks in cuts:
        heights = jnp.exp(jax.random.uniform(jax.random.fold_in(own, dim), (blocks,), jnp.float32, least / len(cuts), high / len(cuts)))
        loudness = loudness * jnp.repeat(heights, shape[dim] // blocks).reshape([-1 if axis == dim else 1 for axis in range(len(shape))])
    return loudness


def gaussian(rng, shape, spread, most, pieces=(), kind=jnp.bfloat16):
    result = jax.random.normal(rng, shape, jnp.float32) * spread
    if len(pieces) > 0:
        result = levels(rng, shape, pieces, -0.22, 0.18) * result
    return jnp.clip(result, min=-most, max=most).astype(kind)


def setup_inputs(seed: int = 0) -> dict:
    splits = jax.random.split(jax.random.key(seed), 11)
    return {
        "block_input": draw_block_input(jax.random.fold_in(splits[10], 71), 0),
        "conv_weights": gaussian(splits[1], (LAYERS, 3, 3, CH, CH), (9 * CH) ** -0.5, 0.09375),
        "norm_gains": jnp.clip(1.0 + 0.18 * jax.random.normal(splits[2], (LAYERS, CH), jnp.float32), 0.1, 1.9),
        "norm_shifts": gaussian(splits[3], (LAYERS, CH), 0.5, 3.0, (), jnp.float32),
        "map_width": draw_map_width(jax.random.fold_in(splits[10], 71), 0),
        "map_group": draw_map_group(jax.random.fold_in(splits[10], 71), 0),
        "pool_index": set_ends(jax.random.randint(splits[6], (MAPS, HEIGHT // 2, WIDTH // 2, CH), 0, 4), jax.random.fold_in(splits[6], 1), 0, 3).astype(jnp.int32),
        "task_mask": set_ends((jax.random.randint(splits[7], (MAPS, TASKS), 0, 3) < 2).astype(jnp.int32), jax.random.fold_in(splits[7], 1), 0, 1),
        "task_weights": jnp.clip(jnp.exp(jax.random.uniform(splits[8], (TASKS,), jnp.float32, math.log(0.5), math.log(2.0))), 0.5, 2.0),
        "task_grads": gaussian(splits[9], (TASKS, MAPS, HEIGHT // 2, WIDTH // 2, CH), 1.0, 6.0, ((1, 4), (2, 8))),
    }


epsilon = 1e-05
highest = lax.Precision.HIGHEST

@jax.custom_vjp
def low(v):
    return lax.optimization_barrier(v.astype(jnp.bfloat16)).astype(jnp.float32)

@jax.custom_vjp
def low_back(v):
    return v

def low_keep(v):
    return (low(v), None)

def low_pass(kept, grad):
    return (grad,)

def back_keep(v):
    return (v, None)

def back_low(kept, grad):
    return (low(grad),)
low.defvjp(low_keep, low_pass)
low_back.defvjp(back_keep, back_low)

def convolve(activation, kernel):
    return lax.conv_general_dilated(activation, kernel, (1, 1), ((1, 1), (1, 1)), dimension_numbers=('NHWC', 'HWIO', 'NHWC'), precision=highest)

def reference(block_input, conv_weights, norm_gains, norm_shifts, map_width, map_group, pool_index, task_mask, task_weights, task_grads):
    columns = jnp.arange(WIDTH, dtype=jnp.int32)
    inside = (columns[None, :] < map_width[:, None]).astype(jnp.float32)[:, None, :, None]
    member = (map_group[:, None] == jnp.arange(DOMAINS, dtype=jnp.int32)[None, :]).astype(jnp.float32)
    counts = lax.optimization_barrier(jnp.sum(member * (HEIGHT * map_width).astype(jnp.float32)[:, None], 0))[:, None]
    picked = [(pool_index == number).astype(jnp.float32) for number in range(4)]

    def forward(first_input, kernels, gains, shifts):
        activation = first_input * inside
        for layer_index in range(LAYERS):
            product = low_back(convolve(low(activation), kernels[layer_index]))
            average = jnp.einsum('md,mc->dc', member, lax.optimization_barrier(jnp.sum(product * inside, (1, 2))), precision=highest) / counts
            centred = product - jnp.einsum('md,dc->mc', member, average, precision=highest)[:, None, None, :]
            variance = jnp.einsum('md,mc->dc', member, lax.optimization_barrier(jnp.sum(centred * centred * inside, (1, 2))), precision=highest) / counts
            scaling = jnp.einsum('md,dc->mc', member, lax.rsqrt(variance + epsilon), precision=highest)[:, None, None, :]
            normed = centred * scaling * gains[layer_index] + shifts[layer_index]
            activation = jax.nn.silu(normed) * inside
        windows = activation.reshape(MAPS, HEIGHT // 2, 2, WIDTH // 2, 2, CH)
        pooled = jnp.zeros((MAPS, HEIGHT // 2, WIDTH // 2, CH), jnp.float32)
        for row_half in range(2):
            for col_half in range(2):
                pooled = pooled + picked[2 * row_half + col_half] * windows[:, :, row_half, :, col_half, :]
        return pooled
    task_scale = task_weights[:, None] * task_mask.T.astype(jnp.float32)
    cotangent = lax.optimization_barrier(jnp.sum(task_scale[:, :, None, None, None] * task_grads.astype(jnp.float32), 0))
    first_input = block_input.astype(jnp.float32)
    kernels = conv_weights.astype(jnp.float32)
    pooled, pullback = jax.vjp(forward, first_input, kernels, norm_gains, norm_shifts)
    input_grad, kernel_grads, gain_grads, shift_grads = pullback(cotangent)
    return (pooled.astype(jnp.bfloat16), input_grad, kernel_grads, gain_grads, shift_grads)
```

```python
import functools

import jax
import jax.numpy as jnp
from jax import lax
from jax.experimental import pallas as pl
from jax.experimental.pallas import tpu as pltpu
from jax.sharding import PartitionSpec as P

MESH = pl.DeviceIdType.MESH
epsilon = 1e-05
PAD = 64
LAYERS = 3
TAPS = 9
UNITS = LAYERS * TAPS
PLANE = 4
F32 = jnp.float32
BF16 = jnp.bfloat16


def each(first, last, body):
    if last - first <= 8:
        for k in range(first, last):
            body(k)
    else:
        lax.fori_loop(first, last, lambda k, s: (body(k), s)[1], 0)


def block_kernel(
    chips,
    height,
    x_ref,
    w_ref,
    gain_ref,
    shift_ref,
    width_ref,
    group_ref,
    index_ref,
    tmask_ref,
    tweight_ref,
    tgrad_ref,
    pooled_ref,
    ig_ref,
    kg_ref,
    sums_ref,
    wa,
    wb,
    wc,
    act_own,
    act_oth,
    act_t,
    zbuf,
    dh,
    dyb,
    dz_own,
    dz_oth,
    dz_t,
    prod,
    gsrc,
    gbuf,
    hrow,
    pbuf,
    igbuf,
    st1,
    st2,
    coef,
    nall,
    inv_t,
    cnt_t,
    avg_t,
    scl_t,
    tb_t,
    ta_t,
    sums_own,
    terms,
    r1,
    r2,
    r3,
    fin,
    w_sem,
    x_s,
    x_r,
    g_s,
    g_r,
    st1_s,
    st1_r,
    st2_s,
    st2_r,
    zh_s,
    zh_r,
    dh_s,
    dh_r,
    act_s,
    act_r,
    dz_s,
    dz_r,
    out_s,
    out_r,
    out_l,
    r1_s,
    r1_r,
    r2_s,
    r2_r,
    r3_s,
    r3_r,
    az_s,
    az_r,
    ab_s,
    ab_r,
    aa_s,
    aa_r,
    ap_s,
    ap_r,
    loc_s,
):
    maps_here = x_ref.shape[0]
    columns = x_ref.shape[2]
    half = x_ref.shape[3] // 2
    tasks = tgrad_ref.shape[0]
    pooled_columns = tgrad_ref.shape[3]
    lanes = half // 128
    band = 4
    pixels = maps_here * band * PAD
    owners = min(chips, 8)
    piece = (half // 2) // owners
    m = lax.axis_index("maps")
    r = lax.axis_index("rows")
    c = lax.rem(r, 2)
    z = lax.div(r, 2)
    other = 1 - c
    first_map = m * maps_here
    x_bit = lax.rem(m, 2)
    y_bit = lax.div(m, 2)
    x_peer = m + 1 - 2 * x_bit
    y_peer = m + 2 - 4 * y_bit
    up_there = z > 0
    down_there = z < chips - 1
    row8 = lax.broadcasted_iota(jnp.int32, (8, half), 0)
    column = lax.broadcasted_iota(jnp.int32, (PAD, half), 0)

    def remote(src, dst, send, recv, mm, zz, cc):
        return pltpu.make_async_remote_copy(
            src_ref=src,
            dst_ref=dst,
            send_sem=send,
            recv_sem=recv,
            device_id=(mm, zz * 2 + cc),
            device_id_type=MESH,
        )

    def own_half(v):
        return jnp.where(c == 0, v[..., :half], v[..., half:])

    def width_of(a):
        return width_ref[first_map + a]

    own_at = pl.ds(pl.multiple_of(c * half, half), half)
    oth_at = pl.ds(pl.multiple_of(other * half, half), half)

    def weight_copy(l, n):
        dst = (wa, wb, wc)[n]
        k_at, o_at = ((own_at, own_at), (oth_at, own_at), (own_at, oth_at))[n]
        return pltpu.make_async_copy(w_ref.at[l, :, :, k_at, o_at], dst.at[l], w_sem.at[l, n])

    for l in range(LAYERS):
        weight_copy(l, 0).start()
        weight_copy(l, 1).start()
    for l in range(LAYERS):
        weight_copy(LAYERS - 1 - l, 2).start()

    barrier = pltpu.get_barrier_semaphore()

    def greet(k):
        rr = lax.rem(r + k, 2 * chips)
        pl.semaphore_signal(barrier, inc=1, device_id=(m, rr), device_id_type=MESH)

    each(1, 2 * chips, greet)
    for k in range(1, PLANE):
        pl.semaphore_signal(
            barrier, inc=1, device_id=(lax.rem(m + k, PLANE), r), device_id_type=MESH
        )

    mine = pl.ds(1 + 2 * c, 2)
    for a in range(maps_here):
        inside = lax.broadcasted_iota(jnp.int32, (columns, 2 * half), 0) < width_of(a)
        for rr in range(2):
            v = jnp.where(inside, x_ref[a, rr].astype(F32), 0.0).astype(BF16)
            at = 1 + 2 * c + rr
            act_own[0, a, at, pl.ds(48, 16), :] = jnp.zeros((16, half), BF16)
            act_oth[0, a, at, pl.ds(48, 16), :] = jnp.zeros((16, half), BF16)
            act_own[0, a, at, pl.ds(0, columns), :] = own_half(v)
            act_oth[0, a, at, pl.ds(0, columns), :] = jnp.where(
                c == 0, v[:, half:], v[:, :half]
            )

    @pl.when(z == 0)
    def _():
        act_own[0, :, 0] = jnp.zeros((maps_here, PAD, half), BF16)
        act_oth[0, :, 0] = jnp.zeros((maps_here, PAD, half), BF16)

    @pl.when(z == chips - 1)
    def _():
        act_own[0, :, 5] = jnp.zeros((maps_here, PAD, half), BF16)
        act_oth[0, :, 5] = jnp.zeros((maps_here, PAD, half), BF16)

    gsrc[...] = jnp.zeros(gsrc.shape, F32)
    for a in range(maps_here):
        total = None
        for t in range(tasks):
            scale = tweight_ref[t] * tmask_ref[a, t].astype(F32)
            term = tgrad_ref[t, a, 0].astype(F32) * scale
            total = term if total is None else total + term
        position = index_ref[a, 0].astype(F32)
        for h in range(2):
            gsrc[h, 0, a, pl.ds(0, pooled_columns), :] = total[:, h * half : (h + 1) * half]
            gsrc[h, 1, a, pl.ds(0, pooled_columns), :] = position[:, h * half : (h + 1) * half]
    gbuf[1 + c] = gsrc[c]

    pl.semaphore_wait(barrier, 2 * chips - 1 + PLANE - 1)

    x_partner = (
        remote(act_own.at[0, :, mine], act_oth.at[0, :, mine], x_s.at[0], x_r.at[0], m, z, other),
        remote(act_oth.at[0, :, mine], act_own.at[0, :, mine], x_s.at[1], x_r.at[1], m, z, other),
    )
    g_partner = remote(gsrc.at[other], gbuf.at[1 + c], g_s.at[0], g_r.at[0], m, z, other)

    def x_halo(n, src_row, dst_row, zz):
        cc = (c, c, other, other, c, other)[n]
        low = dst_row == band + 1
        if n >= 4:
            src, dst = gsrc.at[cc], gbuf.at[3 if low else 0]
            return remote(src, dst, g_s.at[n - 3], g_r.at[1 if low else 2], m, zz, cc)
        src = (act_own, act_oth, act_own, act_oth)[n].at[0, :, src_row]
        dst = (act_own, act_oth, act_oth, act_own)[n].at[0, :, dst_row]
        return remote(src, dst, x_s.at[2 + n], x_r.at[(2 if low else 4) + n % 2], m, zz, cc)

    for copy in x_partner:
        copy.start()

    @pl.when(jnp.logical_and(c == 0, up_there))
    def _():
        for n in range(6):
            x_halo(n, 1, 5, z - 1).start()

    @pl.when(jnp.logical_and(c == 1, down_there))
    def _():
        for n in range(6):
            x_halo(n, 4, 0, z + 1).start()

    g_partner.start()

    for mm in range(PLANE):
        sizes = jnp.zeros((8, half), F32)
        for b in range(maps_here):
            sizes = jnp.where(
                row8 == b, (width_ref[mm * maps_here + b] * height).astype(F32), sizes
            )
        nall[mm] = sizes
    inside_sizes = jnp.zeros((8, half), F32)
    for b in range(maps_here):
        inside_sizes = jnp.where(row8 == b, (width_of(b) * band).astype(F32), inside_sizes)
    inv_t[0] = inside_sizes
    inv_t[1] = jnp.where(row8 < maps_here, 1.0 / jnp.maximum(inside_sizes, 1.0), 0.0)
    counts = jnp.ones((8, half), F32)
    for a in range(maps_here):
        total = jnp.zeros((1, half), F32)
        for mm in range(PLANE):
            same = jnp.zeros((8, half), F32)
            for b in range(maps_here):
                alike = group_ref[first_map + a] == group_ref[mm * maps_here + b]
                same = jnp.where(row8 == b, jnp.where(alike, 1.0, 0.0), same)
            coef[a, mm] = same
            total = total + jnp.sum(same * nall[mm], 0, keepdims=True)
        counts = jnp.where(row8 == a, total, counts)
    cnt_t[...] = counts

    def z_copy(e, k):
        zz = lax.rem(z + k, chips)
        return remote(st1.at[e, z], st1.at[e, z], st1_s.at[e, k], st1_r.at[e, z], m, zz, c)

    def z_arrival(e, k):
        zz = lax.rem(z + k, chips)
        return remote(st1.at[e, zz], st1.at[e, zz], st1_s.at[e, k], st1_r.at[e, zz], m, zz, c)

    def m_copy(e, k):
        mm = lax.rem(m + k, PLANE)
        return remote(st2.at[e, m], st2.at[e, m], st2_s.at[e, k], st2_r.at[e, m], mm, z, c)

    def m_arrival(e, k):
        mm = lax.rem(m + k, PLANE)
        return remote(st2.at[e, mm], st2.at[e, mm], st2_s.at[e, k], st2_r.at[e, mm], mm, z, c)

    def send_z(e, tile):
        st1[e, z] = tile
        each(1, chips, lambda k: z_copy(e, k).start())

    def wait_z(e):
        each(1, chips, lambda k: z_arrival(e, k).wait_recv())
        each(1, chips, lambda k: z_copy(e, k).wait_send())

    def send_m(e, tile):
        st2[e, m] = tile
        each(1, PLANE, lambda k: m_copy(e, k).start())

    def wait_m(e):
        each(1, PLANE, lambda k: m_arrival(e, k).wait_recv())
        each(1, PLANE, lambda k: m_copy(e, k).wait_send())

    def products(source, l, starts, kernel, transposed, fresh):
        parts = [
            source[l, :, s : s + band].reshape(pixels, half) for s in starts
        ]
        lhs = jnp.concatenate(parts, 1)
        for j in range(3):
            if transposed:
                rhs = jnp.concatenate([kernel[l, i, j] for i in range(3)], 1)
                got = lax.dot_general(
                    lhs, rhs, (((1,), (1,)), ((), ())), preferred_element_type=F32
                )
            else:
                rhs = kernel[l, :, j].reshape(3 * half, half)
                got = jnp.dot(lhs, rhs, preferred_element_type=F32)
            if fresh:
                prod[j] = got
            else:
                prod[j] = prod[j] + got

    def shifted(a, rr, before, behind):
        at = pl.ds(pl.multiple_of((a * band + rr) * PAD, PAD), PAD)
        return (
            prod[1, at, :]
            + pltpu.roll(prod[before, at, :], 1, 0)
            + pltpu.roll(prod[behind, at, :], PAD - 1, 0)
        )

    def row_of(table, l, a):
        return table[l, pl.ds(a, 1), :]

    def gain_of(l):
        return own_half(gain_ref[pl.ds(l, 1), :])

    def shift_of(l):
        return own_half(shift_ref[pl.ds(l, 1), :])

    def limit(a, rr):
        w = width_of(a)
        if rr == 0:
            return jnp.where(up_there, w, 0)
        if rr == band + 1:
            return jnp.where(down_there, w, 0)
        return w

    def z_halo(l, way):
        if way == 0:
            return remote(zbuf.at[l, :, 1], zbuf.at[l, :, 5], zh_s.at[l, 0], zh_r.at[l, 0], m, z - 1, c)
        return remote(zbuf.at[l, :, 4], zbuf.at[l, :, 0], zh_s.at[l, 1], zh_r.at[l, 1], m, z + 1, c)

    def dh_halo(l, way):
        if way == 0:
            return remote(dh.at[l, :, 1], dh.at[l, :, 5], dh_s.at[l, 0], dh_r.at[l, 0], m, z - 1, c)
        return remote(dh.at[l, :, 4], dh.at[l, :, 0], dh_s.at[l, 1], dh_r.at[l, 1], m, z + 1, c)

    def start_halo(halo, l):
        @pl.when(up_there)
        def _():
            halo(l, 0).start()

        @pl.when(down_there)
        def _():
            halo(l, 1).start()

    def wait_halo(halo, l):
        @pl.when(up_there)
        def _():
            halo(l, 1).wait_recv()
            halo(l, 0).wait_send()

        @pl.when(down_there)
        def _():
            halo(l, 0).wait_recv()
            halo(l, 1).wait_send()

    def act_copy(l):
        return remote(act_own.at[l], act_oth.at[l], act_s.at[l], act_r.at[l], m, z, other)

    def dz_copy(l):
        return remote(dz_own.at[l], dz_oth.at[l], dz_s.at[l], dz_r.at[l], m, z, other)

    for copy in x_partner:
        copy.wait()

    @pl.when(up_there)
    def _():
        for n in (0, 1, 4):
            x_halo(n, 4, 0, z - 1).wait_recv()

    @pl.when(down_there)
    def _():
        for n in (0, 1, 4):
            x_halo(n, 1, 5, z + 1).wait_recv()

    @pl.when(jnp.logical_and(c == 0, up_there))
    def _():
        for n in range(6):
            x_halo(n, 1, 5, z - 1).wait_send()

    @pl.when(jnp.logical_and(c == 1, down_there))
    def _():
        for n in range(6):
            x_halo(n, 4, 0, z + 1).wait_send()

    g_partner.wait()

    def forward(l, carry):
        weight_copy(l, 0).wait()
        products(act_own, l, (0, 1, 2), wa, False, True)
        weight_copy(l, 1).wait()

        @pl.when(l > 0)
        def _():
            act_copy(l).wait_recv()

        products(act_oth, l, (0, 1, 2), wb, False, False)

        def collect(a, tile):
            inside = column < width_of(a)
            total = jnp.zeros((PAD, half), F32)
            for rr in range(band):
                v = shifted(a, rr, 0, 2)
                zbuf[l, a, 1 + rr] = v
                total = total + jnp.where(inside, v, 0.0)
            total = jnp.sum(total, 0, keepdims=True)
            mean = total / (width_of(a) * band).astype(F32)
            square = jnp.zeros((PAD, half), F32)
            for rr in range(band):
                v = jnp.where(inside, zbuf[l, a, 1 + rr] - mean, 0.0)
                square = square + v * v
            square = jnp.sum(square, 0, keepdims=True)
            tile = jnp.where(row8 == a, total, tile)
            return jnp.where(row8 == a + maps_here, square, tile)

        tile = lax.fori_loop(0, maps_here, collect, jnp.zeros((8, half), F32))
        send_z(l, tile)
        start_halo(z_halo, l)
        for i in range(3):
            act_t[l, i, 0] = act_own[l, :, i : i + band].reshape(pixels, half).T
        wait_z(l)
        sizes, inverse = inv_t[0], inv_t[1]
        total = st1[l, 0]
        for zz in range(1, chips):
            total = total + st1[l, zz]
        mean = total * inverse * (1.0 / chips)
        square = jnp.zeros((8, half), F32)
        for zz in range(chips):
            v = st1[l, zz]
            gap = v * inverse - mean
            square = square + pltpu.roll(v, 8 - maps_here, 0) + sizes * gap * gap
        tile = jnp.where(row8 < maps_here, mean, pltpu.roll(square, maps_here, 0))
        send_m(l, jnp.where(row8 < 2 * maps_here, tile, 0.0))
        for i in range(3):
            act_t[l, i, 1] = act_oth[l, :, i : i + band].reshape(pixels, half).T
        wait_m(l)
        averages = jnp.zeros((8, half), F32)
        scalings = jnp.zeros((8, half), F32)
        for a in range(maps_here):
            count = cnt_t[a : a + 1, :]
            average = jnp.zeros((8, half), F32)
            for mm in range(PLANE):
                average = average + coef[a, mm] * nall[mm] * st2[l, mm]
            average = jnp.sum(average, 0, keepdims=True) / count
            variance = jnp.zeros((8, half), F32)
            for mm in range(PLANE):
                v = st2[l, mm]
                gap = v - average
                variance = variance + coef[a, mm] * (
                    pltpu.roll(v, 8 - maps_here, 0) + nall[mm] * gap * gap
                )
            variance = jnp.sum(variance, 0, keepdims=True) / count
            averages = jnp.where(row8 == a, average, averages)
            scalings = jnp.where(row8 == a, lax.rsqrt(variance + epsilon), scalings)
        avg_t[l] = averages
        scl_t[l] = scalings
        wait_halo(z_halo, l)

        def activate(a, s):
            average = row_of(avg_t, l, a)
            factor = row_of(scl_t, l, a) * gain_of(l)
            shift = shift_of(l)
            for rr in range(band + 2):
                y = (zbuf[l, a, rr] - average) * factor + shift
                h = jnp.where(column < limit(a, rr), y * jax.nn.sigmoid(y), 0.0)
                act_own[l + 1, a, rr] = h.astype(BF16)
            return s

        lax.fori_loop(0, maps_here, activate, 0)

        @pl.when(l < LAYERS - 1)
        def _():
            act_copy(l + 1).start()

        return carry

    lax.fori_loop(0, LAYERS, forward, 0)

    def unpool(a, s):
        for rr in range(band + 2):
            slot, lower = (rr + 1) // 2, (rr + 1) % 2
            g = gbuf[slot, 0, a]
            position = gbuf[slot, 1, a]
            for b in range(2):
                v = jnp.where(position == float(2 * lower + b), g, 0.0)
                for n in range(lanes):
                    hrow[n, pl.ds(b, PAD // 2, stride=2), :] = v[:, n * 128 : (n + 1) * 128]
            dh[LAYERS, a, rr] = jnp.concatenate([hrow[n] for n in range(lanes)], 1)
        return s

    lax.fori_loop(0, maps_here, unpool, 0)

    def pool():
        def one(a, s):
            for pr in range(2):
                total = jnp.zeros((PAD // 2, half), F32)
                position = gbuf[1 + pr, 1, a]
                for lower in range(2):
                    v = act_own[LAYERS, a, 1 + 2 * pr + lower].astype(F32)
                    for n in range(lanes):
                        hrow[n] = v[:, n * 128 : (n + 1) * 128]
                    for b in range(2):
                        v = jnp.concatenate(
                            [hrow[n, pl.ds(b, PAD // 2, stride=2), :] for n in range(lanes)], 1
                        )
                        total = total + jnp.where(position == float(2 * lower + b), v, 0.0)
                pbuf[pr, a] = total.astype(BF16)
            return s

        lax.fori_loop(0, maps_here, one, 0)

    def order(q):
        swap = lax.rem(q, 2)
        keep = 1 - swap
        return (
            keep * x_peer + swap * y_peer,
            keep * x_bit + swap * y_bit,
            keep * y_peer + swap * x_peer,
            keep * y_bit + swap * x_bit,
        )

    def c1(q):
        peer, bit, _, _ = order(q)
        return remote(terms.at[q, 1 - bit], r1.at[q], r1_s.at[q], r1_r.at[q], peer, z, c)

    def second_rows(bit):
        return pl.ds(pl.multiple_of(bit * (half // 2), half // 2), half // 2)

    def c2(q):
        _, _, peer, bit = order(q)
        return remote(r1.at[q, second_rows(1 - bit)], r2.at[q], r2_s.at[q], r2_r.at[q], peer, z, c)

    def piece_rows(p):
        return pl.ds(pl.multiple_of(p * piece, piece), piece)

    def c3(q, p):
        slot = lax.rem(z - p + chips - 1, chips)
        return remote(
            r2.at[q, piece_rows(p)], r3.at[q, slot], r3_s.at[q, p], r3_r.at[q, slot], m, p, c
        )

    def unit_of(q):
        k = lax.div(q, TAPS)
        return (LAYERS - 1 - k) * TAPS + (q - k * TAPS)

    def region(q, start, size):
        start = pl.multiple_of(start, piece)
        return kg_ref.at[unit_of(q), pl.ds(start, size), own_at]

    def base(q):
        _, first_bit, _, second_bit = order(q)
        return first_bit * half + second_bit * (half // 2)

    def cz(q, p, zz):
        return remote(
            fin.at[q],
            region(q, base(q) + p * piece, piece),
            az_s.at[q, zz],
            az_r.at[q, p],
            m,
            zz,
            c,
        )

    def cl(q):
        return pltpu.make_async_copy(
            fin.at[q], region(q, base(q) + z * piece, piece), loc_s.at[q]
        )

    def cb(q):
        _, _, peer, _ = order(q)
        part = region(q, base(q), half // 2)
        return remote(part, part, ab_s.at[q], ab_r.at[q], peer, z, c)

    def ca(q):
        peer, bit, _, _ = order(q)
        part = region(q, bit * half, half)
        return remote(part, part, aa_s.at[q], aa_r.at[q], peer, z, c)

    def cp(q):
        part = region(q, 0, 2 * half)
        return remote(part, part, ap_s.at[q], ap_r.at[q], m, z, other)

    def weight_terms(l, first, last):
        def one(t, s):
            i = lax.div(t, 3)
            j = t - 3 * i
            got = jnp.dot(
                act_t[l, i].reshape(2 * half, pixels), dz_t[j], preferred_element_type=F32
            ).astype(BF16)
            q = (LAYERS - 1 - l) * TAPS + t
            terms[q, c] = got[:half]
            terms[q, other] = got[half:]
            c1(q).start()
            return s

        lax.fori_loop(first, last, one, 0)

    def backward(k, carry):
        l = LAYERS - 1 - k
        gain, shift = gain_of(l), shift_of(l)

        def gradient(a, rr):
            zhat = (zbuf[l, a, rr] - row_of(avg_t, l, a)) * row_of(scl_t, l, a)
            y = zhat * gain + shift
            s = jax.nn.sigmoid(y)
            dy = dh[l + 1, a, rr] * (s * (1.0 + y * (1.0 - s)))
            dy = jnp.where(column < limit(a, rr), dy, 0.0)
            dyb[a, rr] = dy
            return dy, zhat

        def collect(a, tile):
            plain = jnp.zeros((PAD, half), F32)
            crossed = jnp.zeros((PAD, half), F32)
            for rr in range(1, band + 1):
                dy, zhat = gradient(a, rr)
                plain = plain + dy
                crossed = crossed + dy * zhat
            plain = jnp.sum(plain, 0, keepdims=True)
            crossed = jnp.sum(crossed, 0, keepdims=True)
            tile = jnp.where(row8 == a, plain, tile)
            return jnp.where(row8 == a + maps_here, crossed, tile)

        e = LAYERS + l
        tile = lax.fori_loop(0, maps_here, collect, jnp.zeros((8, half), F32))
        send_z(e, tile)

        @pl.when(k > 0)
        def _():
            weight_terms(l + 1, 0, 5)

        wait_z(e)
        total = st1[e, 0]
        for zz in range(1, chips):
            total = total + st1[e, zz]
        send_m(e, total)

        @pl.when(k > 0)
        def _():
            weight_terms(l + 1, 5, TAPS)
            wait_halo(dh_halo, l + 1)

        @pl.when(k == 0)
        def _():
            pool()

        def edges(a, s):
            gradient(a, 0)
            gradient(a, band + 1)
            return s

        lax.fori_loop(0, maps_here, edges, 0)
        wait_m(e)
        total = st2[e, 0]
        for mm in range(1, PLANE):
            total = total + st2[e, mm]
        sums_own[pl.ds(l, 1), :] = jnp.sum(
            jnp.where(row8 >= maps_here, total, 0.0), 0, keepdims=True
        )
        sums_own[pl.ds(LAYERS + l, 1), :] = jnp.sum(
            jnp.where(row8 < maps_here, total, 0.0), 0, keepdims=True
        )
        plains = jnp.zeros((8, half), F32)
        crosses = jnp.zeros((8, half), F32)
        for a in range(maps_here):
            plain = jnp.zeros((8, half), F32)
            crossed = jnp.zeros((8, half), F32)
            for mm in range(PLANE):
                v = st2[e, mm]
                plain = plain + coef[a, mm] * v
                crossed = crossed + coef[a, mm] * pltpu.roll(v, 8 - maps_here, 0)
            count = cnt_t[a : a + 1, :]
            plain = gain * (jnp.sum(plain, 0, keepdims=True) / count)
            crossed = gain * (jnp.sum(crossed, 0, keepdims=True) / count)
            plains = jnp.where(row8 == a, plain, plains)
            crosses = jnp.where(row8 == a, crossed, crosses)
        tb_t[0] = plains
        ta_t[0] = crosses

        def settle(a, s):
            average, scaling = row_of(avg_t, l, a), row_of(scl_t, l, a)
            plain, crossed = row_of(tb_t, 0, a), row_of(ta_t, 0, a)
            for rr in range(band + 2):
                zhat = (zbuf[l, a, rr] - average) * scaling
                v = scaling * (dyb[a, rr] * gain - plain - zhat * crossed)
                v = jnp.where(column < limit(a, rr), v, 0.0)
                rounded = v.astype(BF16)
                dz_own[l, a, rr] = rounded
                if 0 < rr <= band:
                    at = pl.ds(pl.multiple_of((a * band + rr - 1) * PAD, PAD), PAD)
                    dz_t[1, at, :] = rounded
                    dz_t[0, at, :] = pltpu.roll(v, PAD - 1, 0).astype(BF16)
                    dz_t[2, at, :] = pltpu.roll(v, 1, 0).astype(BF16)
            return s

        lax.fori_loop(0, maps_here, settle, 0)
        dz_copy(l).start()
        products(dz_own, l, (2, 1, 0), wa, True, True)
        weight_copy(l, 2).wait()
        dz_copy(l).wait_recv()
        products(dz_oth, l, (2, 1, 0), wc, True, False)

        def gather(a, s):
            for rr in range(band):
                dh[l, a, 1 + rr] = shifted(a, rr, 2, 0)
            return s

        lax.fori_loop(0, maps_here, gather, 0)

        @pl.when(l > 0)
        def _():
            start_halo(dh_halo, l)

        return carry

    lax.fori_loop(0, LAYERS, backward, 0)
    weight_terms(0, 0, TAPS)

    def input_rows(a, s):
        for rr in range(band):
            igbuf[rr // 2, a, rr % 2] = jnp.where(
                column < width_of(a), dh[0, a, 1 + rr], 0.0
            )
        return s

    lax.fori_loop(0, maps_here, input_rows, 0)

    outs = (
        (
            remote(igbuf.at[other], ig_ref.at[c], out_s.at[0], out_r.at[0], m, z, other),
            pltpu.make_async_copy(igbuf.at[c], ig_ref.at[c], out_l.at[0]),
        ),
        (
            remote(pbuf.at[other], pooled_ref.at[c], out_s.at[1], out_r.at[1], m, z, other),
            pltpu.make_async_copy(pbuf.at[c], pooled_ref.at[c], out_l.at[1]),
        ),
        (
            remote(sums_own, sums_ref.at[c], out_s.at[2], out_r.at[2], m, z, other),
            pltpu.make_async_copy(sums_own, sums_ref.at[c], out_l.at[2]),
        ),
    )
    for there, here in outs:
        there.start()
        here.start()

    def within(q):
        return jnp.logical_and(q >= 0, q < UNITS)

    def drain(s, carry):
        @pl.when(within(s - 5))
        def _():
            q = s - 5
            ca(q).wait_recv()
            cp(q).start()

        @pl.when(within(s - 4))
        def _():
            q = s - 4
            cb(q).wait_recv()
            ca(q).start()

        @pl.when(within(s - 3))
        def _():
            q = s - 3

            def arrived(k):
                p = lax.rem(z + k, chips)

                @pl.when(p < owners)
                def _():
                    cz(q, p, p).wait_recv()

            each(1, chips, arrived)

            @pl.when(z < owners)
            def _():
                cl(q).wait()

            cb(q).start()

        @pl.when(within(s - 2))
        def _():
            q = s - 2

            @pl.when(z < owners)
            def _():
                total = r2[q, piece_rows(z)].astype(F32)
                for k in range(chips - 1):
                    remote(
                        r2.at[q, piece_rows(0)],
                        r3.at[q, k],
                        r3_s.at[q, 0],
                        r3_r.at[q, k],
                        m,
                        z,
                        c,
                    ).wait_recv()
                for k in range(chips - 1):
                    total = total + r3[q, k].astype(F32)
                fin[q] = total.astype(BF16)
                each(1, chips, lambda k: cz(q, z, lax.rem(z + k, chips)).start())
                cl(q).start()

        @pl.when(within(s - 1))
        def _():
            q = s - 1
            _, _, _, bit = order(q)
            c2(q).wait_recv()
            r2[q] = (r2[q].astype(F32) + r1[q, second_rows(bit)].astype(F32)).astype(BF16)

            def give(k):
                p = lax.rem(z + k, chips)

                @pl.when(p < owners)
                def _():
                    c3(q, p).start()

            each(1, chips, give)

        @pl.when(within(s))
        def _():
            q = s
            _, bit, _, _ = order(q)
            c1(q).wait_recv()
            r1[q] = (r1[q].astype(F32) + terms[q, bit].astype(F32)).astype(BF16)
            c2(q).start()

        return carry

    lax.fori_loop(0, UNITS + 6, drain, 0)

    def finish(q, carry):
        cp(q).wait()
        ca(q).wait_send()
        cb(q).wait_send()
        c1(q).wait_send()
        c2(q).wait_send()

        def given(k):
            p = lax.rem(z + k, chips)

            @pl.when(p < owners)
            def _():
                c3(q, p).wait_send()

        each(1, chips, given)

        @pl.when(z < owners)
        def _():
            each(1, chips, lambda k: cz(q, z, lax.rem(z + k, chips)).wait_send())

        return carry

    lax.fori_loop(0, UNITS, finish, 0)
    for l in range(1, LAYERS):
        act_copy(l).wait_send()
    for l in range(LAYERS):
        dz_copy(l).wait_send()
    for there, here in outs:
        there.wait()
        here.wait()


def solution(mesh):
    chips = mesh.shape["rows"] // 2

    def per_device(
        block_input,
        conv_weights,
        norm_gains,
        norm_shifts,
        map_width,
        map_group,
        pool_index,
        task_mask,
        task_weights,
        task_grads,
    ):
        maps_here, rows_here, columns, channels = block_input.shape
        pooled_columns = pool_index.shape[2]
        height = rows_here * mesh.shape["rows"]
        half = channels // 2
        band = 2 * rows_here
        pixels = maps_here * band * PAD
        owners = min(chips, 8)
        piece = half // 2 // owners
        rounds = 2 * LAYERS
        vmem, dma = pltpu.VMEM, pltpu.SemaphoreType.DMA
        tile = (maps_here, band + 2, PAD, half)
        whole = pl.BlockSpec(memory_space=pltpu.VMEM)
        scalars = pl.BlockSpec(memory_space=pltpu.SMEM)
        anywhere = pl.BlockSpec(memory_space=pl.ANY)
        pooled, ig, kg, sums = pl.pallas_call(
            functools.partial(block_kernel, chips, height),
            out_shape=(
                jax.ShapeDtypeStruct((2, maps_here, PAD // 2, half), BF16),
                jax.ShapeDtypeStruct((2, maps_here, rows_here, PAD, half), F32),
                jax.ShapeDtypeStruct((UNITS, channels, channels), BF16),
                jax.ShapeDtypeStruct((2, 8, half), F32),
            ),
            in_specs=[whole, anywhere, whole, whole, scalars, scalars, whole, scalars, scalars, whole],
            out_specs=[anywhere] * 4,
            scratch_shapes=[
                vmem((LAYERS, 3, 3, half, half), BF16),
                vmem((LAYERS, 3, 3, half, half), BF16),
                vmem((LAYERS, 3, 3, half, half), BF16),
                vmem((LAYERS + 1,) + tile, BF16),
                vmem((LAYERS,) + tile, BF16),
                vmem((LAYERS, 3, 2, half, pixels), BF16),
                vmem((LAYERS,) + tile, F32),
                vmem((LAYERS + 1,) + tile, F32),
                vmem(tile, F32),
                vmem((LAYERS,) + tile, BF16),
                vmem((LAYERS,) + tile, BF16),
                vmem((3, pixels, half), BF16),
                vmem((3, pixels, half), F32),
                vmem((2, 2, maps_here, PAD // 2, half), F32),
                vmem((4, 2, maps_here, PAD // 2, half), F32),
                vmem((half // 128, PAD, 128), F32),
                vmem((2, maps_here, PAD // 2, half), BF16),
                vmem((2, maps_here, rows_here, PAD, half), F32),
                vmem((rounds, chips, 8, half), F32),
                vmem((rounds, PLANE, 8, half), F32),
                vmem((maps_here, PLANE, 8, half), F32),
                vmem((PLANE, 8, half), F32),
                vmem((2, 8, half), F32),
                vmem((8, half), F32),
                vmem((LAYERS, 8, half), F32),
                vmem((LAYERS, 8, half), F32),
                vmem((1, 8, half), F32),
                vmem((1, 8, half), F32),
                vmem((8, half), F32),
                vmem((UNITS, 2, half, half), BF16),
                vmem((UNITS, half, half), BF16),
                vmem((UNITS, half // 2, half), BF16),
                vmem((UNITS, chips - 1, piece, half), BF16),
                vmem((UNITS, piece, half), BF16),
                dma((LAYERS, 3)),
                dma((6,)),
                dma((6,)),
                dma((3,)),
                dma((3,)),
                dma((rounds, chips)),
                dma((rounds, chips)),
                dma((rounds, PLANE)),
                dma((rounds, PLANE)),
                dma((LAYERS, 2)),
                dma((LAYERS, 2)),
                dma((LAYERS, 2)),
                dma((LAYERS, 2)),
                dma((LAYERS,)),
                dma((LAYERS,)),
                dma((LAYERS,)),
                dma((LAYERS,)),
                dma((3,)),
                dma((3,)),
                dma((3,)),
                dma((UNITS,)),
                dma((UNITS,)),
                dma((UNITS,)),
                dma((UNITS,)),
                dma((UNITS, owners)),
                dma((UNITS, chips - 1)),
                dma((UNITS, chips)),
                dma((UNITS, owners)),
                dma((UNITS,)),
                dma((UNITS,)),
                dma((UNITS,)),
                dma((UNITS,)),
                dma((UNITS,)),
                dma((UNITS,)),
                dma((UNITS,)),
            ],
            compiler_params=pltpu.CompilerParams(
                collective_id=0,
                has_side_effects=True,
                vmem_limit_bytes=63 * 1024 * 1024,
            ),
        )(
            block_input,
            conv_weights,
            norm_gains,
            norm_shifts,
            map_width,
            map_group,
            pool_index,
            task_mask,
            task_weights,
            task_grads,
        )
        pooled = jnp.concatenate([pooled[0], pooled[1]], -1)[:, None, :pooled_columns]
        input_grad = jnp.concatenate([ig[0], ig[1]], -1)[:, :, :columns]
        sums = jnp.concatenate([sums[0], sums[1]], -1)
        return (
            pooled,
            input_grad,
            kg.astype(F32).reshape(conv_weights.shape),
            sums[:LAYERS],
            sums[LAYERS : 2 * LAYERS],
        )

    return jax.shard_map(
        per_device,
        mesh=mesh,
        in_specs=(
            P("maps", "rows", None, None),
            P(),
            P(),
            P(),
            P(),
            P(),
            P("maps", "rows", None, None),
            P("maps", None),
            P(),
            P(None, "maps", "rows", None, None),
        ),
        out_specs=(P("maps", "rows", None, None), P("maps", "rows", None, None), P(), P(), P()),
        check_vma=False,
    )
```

```python
import functools

import jax
import jax.numpy as jnp
from jax import lax
from jax.experimental import pallas as pl
from jax.experimental.pallas import tpu as pltpu
from jax.sharding import PartitionSpec as P

MESH = pl.DeviceIdType.MESH
epsilon = 1e-05
PAD = 64
LAYERS = 3
TAPS = 9
UNITS = LAYERS * TAPS
PLANE = 4
F32 = jnp.float32
BF16 = jnp.bfloat16


def each(first, last, body):
    if last - first <= 8:
        for k in range(first, last):
            body(k)
    else:
        lax.fori_loop(first, last, lambda k, s: (body(k), s)[1], 0)


def block_kernel(
    chips,
    height,
    x_ref,
    w_ref,
    gain_ref,
    shift_ref,
    width_ref,
    group_ref,
    index_ref,
    tmask_ref,
    tweight_ref,
    tgrad_ref,
    pooled_ref,
    ig_ref,
    terms,
    sums_ref,
    wa,
    wb,
    wc,
    act_own,
    act_oth,
    act_t,
    zbuf,
    dh,
    dyb,
    dz_own,
    dz_oth,
    dz_t,
    prod,
    gsrc,
    gbuf,
    hrow,
    pbuf,
    igbuf,
    st1,
    st2,
    coef,
    nall,
    inv_t,
    cnt_t,
    avg_t,
    scl_t,
    tb_t,
    ta_t,
    sums_own,
    w_sem,
    x_s,
    x_r,
    g_s,
    g_r,
    st1_s,
    st1_r,
    st2_s,
    st2_r,
    zh_s,
    zh_r,
    dh_s,
    dh_r,
    act_s,
    act_r,
    dz_s,
    dz_r,
    out_s,
    out_r,
    out_l,
):
    maps_here = x_ref.shape[0]
    columns = x_ref.shape[2]
    half = x_ref.shape[3] // 2
    tasks = tgrad_ref.shape[0]
    pooled_columns = tgrad_ref.shape[3]
    lanes = half // 128
    band = 4
    pixels = maps_here * band * PAD
    m = lax.axis_index("maps")
    r = lax.axis_index("rows")
    c = lax.rem(r, 2)
    z = lax.div(r, 2)
    other = 1 - c
    first_map = m * maps_here
    up_there = z > 0
    down_there = z < chips - 1
    row8 = lax.broadcasted_iota(jnp.int32, (8, half), 0)
    column = lax.broadcasted_iota(jnp.int32, (PAD, half), 0)

    def remote(src, dst, send, recv, mm, zz, cc):
        return pltpu.make_async_remote_copy(
            src_ref=src,
            dst_ref=dst,
            send_sem=send,
            recv_sem=recv,
            device_id=(mm, zz * 2 + cc),
            device_id_type=MESH,
        )

    def own_half(v):
        return jnp.where(c == 0, v[..., :half], v[..., half:])

    def width_of(a):
        return width_ref[first_map + a]

    own_at = pl.ds(pl.multiple_of(c * half, half), half)
    oth_at = pl.ds(pl.multiple_of(other * half, half), half)

    def weight_copy(l, n):
        dst = (wa, wb, wc)[n]
        k_at, o_at = ((own_at, own_at), (oth_at, own_at), (own_at, oth_at))[n]
        return pltpu.make_async_copy(w_ref.at[l, :, :, k_at, o_at], dst.at[l], w_sem.at[l, n])

    for l in range(LAYERS):
        weight_copy(l, 0).start()
        weight_copy(l, 1).start()
    for l in range(LAYERS):
        weight_copy(LAYERS - 1 - l, 2).start()

    barrier = pltpu.get_barrier_semaphore()

    def greet(k):
        rr = lax.rem(r + k, 2 * chips)
        pl.semaphore_signal(barrier, inc=1, device_id=(m, rr), device_id_type=MESH)

    each(1, 2 * chips, greet)
    for k in range(1, PLANE):
        pl.semaphore_signal(
            barrier, inc=1, device_id=(lax.rem(m + k, PLANE), r), device_id_type=MESH
        )

    mine = pl.ds(1 + 2 * c, 2)
    for a in range(maps_here):
        inside = lax.broadcasted_iota(jnp.int32, (columns, 2 * half), 0) < width_of(a)
        for rr in range(2):
            v = jnp.where(inside, x_ref[a, rr].astype(F32), 0.0).astype(BF16)
            at = 1 + 2 * c + rr
            act_own[0, a, at, pl.ds(48, 16), :] = jnp.zeros((16, half), BF16)
            act_oth[0, a, at, pl.ds(48, 16), :] = jnp.zeros((16, half), BF16)
            act_own[0, a, at, pl.ds(0, columns), :] = own_half(v)
            act_oth[0, a, at, pl.ds(0, columns), :] = jnp.where(
                c == 0, v[:, half:], v[:, :half]
            )

    @pl.when(z == 0)
    def _():
        act_own[0, :, 0] = jnp.zeros((maps_here, PAD, half), BF16)
        act_oth[0, :, 0] = jnp.zeros((maps_here, PAD, half), BF16)

    @pl.when(z == chips - 1)
    def _():
        act_own[0, :, 5] = jnp.zeros((maps_here, PAD, half), BF16)
        act_oth[0, :, 5] = jnp.zeros((maps_here, PAD, half), BF16)

    gsrc[...] = jnp.zeros(gsrc.shape, F32)
    for a in range(maps_here):
        total = None
        for t in range(tasks):
            scale = tweight_ref[t] * tmask_ref[a, t].astype(F32)
            term = tgrad_ref[t, a, 0].astype(F32) * scale
            total = term if total is None else total + term
        position = index_ref[a, 0].astype(F32)
        for h in range(2):
            gsrc[h, 0, a, pl.ds(0, pooled_columns), :] = total[:, h * half : (h + 1) * half]
            gsrc[h, 1, a, pl.ds(0, pooled_columns), :] = position[:, h * half : (h + 1) * half]
    gbuf[1 + c] = gsrc[c]

    pl.semaphore_wait(barrier, 2 * chips - 1 + PLANE - 1)

    x_partner = (
        remote(act_own.at[0, :, mine], act_oth.at[0, :, mine], x_s.at[0], x_r.at[0], m, z, other),
        remote(act_oth.at[0, :, mine], act_own.at[0, :, mine], x_s.at[1], x_r.at[1], m, z, other),
    )
    g_partner = remote(gsrc.at[other], gbuf.at[1 + c], g_s.at[0], g_r.at[0], m, z, other)

    def x_halo(n, src_row, dst_row, zz):
        cc = (c, c, other, other, c, other)[n]
        low = dst_row == band + 1
        if n >= 4:
            src, dst = gsrc.at[cc], gbuf.at[3 if low else 0]
            return remote(src, dst, g_s.at[n - 3], g_r.at[1 if low else 2], m, zz, cc)
        src = (act_own, act_oth, act_own, act_oth)[n].at[0, :, src_row]
        dst = (act_own, act_oth, act_oth, act_own)[n].at[0, :, dst_row]
        return remote(src, dst, x_s.at[2 + n], x_r.at[(2 if low else 4) + n % 2], m, zz, cc)

    for copy in x_partner:
        copy.start()

    @pl.when(jnp.logical_and(c == 0, up_there))
    def _():
        for n in range(6):
            x_halo(n, 1, 5, z - 1).start()

    @pl.when(jnp.logical_and(c == 1, down_there))
    def _():
        for n in range(6):
            x_halo(n, 4, 0, z + 1).start()

    g_partner.start()

    for mm in range(PLANE):
        sizes = jnp.zeros((8, half), F32)
        for b in range(maps_here):
            sizes = jnp.where(
                row8 == b, (width_ref[mm * maps_here + b] * height).astype(F32), sizes
            )
        nall[mm] = sizes
    inside_sizes = jnp.zeros((8, half), F32)
    for b in range(maps_here):
        inside_sizes = jnp.where(row8 == b, (width_of(b) * band).astype(F32), inside_sizes)
    inv_t[0] = inside_sizes
    inv_t[1] = jnp.where(row8 < maps_here, 1.0 / jnp.maximum(inside_sizes, 1.0), 0.0)
    counts = jnp.ones((8, half), F32)
    for a in range(maps_here):
        total = jnp.zeros((1, half), F32)
        for mm in range(PLANE):
            same = jnp.zeros((8, half), F32)
            for b in range(maps_here):
                alike = group_ref[first_map + a] == group_ref[mm * maps_here + b]
                same = jnp.where(row8 == b, jnp.where(alike, 1.0, 0.0), same)
            coef[a, mm] = same
            total = total + jnp.sum(same * nall[mm], 0, keepdims=True)
        counts = jnp.where(row8 == a, total, counts)
    cnt_t[...] = counts

    def z_copy(e, k):
        zz = lax.rem(z + k, chips)
        return remote(st1.at[e, z], st1.at[e, z], st1_s.at[e, k], st1_r.at[e, z], m, zz, c)

    def z_arrival(e, k):
        zz = lax.rem(z + k, chips)
        return remote(st1.at[e, zz], st1.at[e, zz], st1_s.at[e, k], st1_r.at[e, zz], m, zz, c)

    def m_copy(e, k):
        mm = lax.rem(m + k, PLANE)
        return remote(st2.at[e, m], st2.at[e, m], st2_s.at[e, k], st2_r.at[e, m], mm, z, c)

    def m_arrival(e, k):
        mm = lax.rem(m + k, PLANE)
        return remote(st2.at[e, mm], st2.at[e, mm], st2_s.at[e, k], st2_r.at[e, mm], mm, z, c)

    def send_z(e, tile):
        st1[e, z] = tile
        each(1, chips, lambda k: z_copy(e, k).start())

    def wait_z(e):
        each(1, chips, lambda k: z_arrival(e, k).wait_recv())
        each(1, chips, lambda k: z_copy(e, k).wait_send())

    def send_m(e, tile):
        st2[e, m] = tile
        each(1, PLANE, lambda k: m_copy(e, k).start())

    def wait_m(e):
        each(1, PLANE, lambda k: m_arrival(e, k).wait_recv())
        each(1, PLANE, lambda k: m_copy(e, k).wait_send())

    def products(source, l, starts, kernel, transposed, fresh):
        parts = [
            source[l, :, s : s + band].reshape(pixels, half) for s in starts
        ]
        lhs = jnp.concatenate(parts, 1)
        for j in range(3):
            if transposed:
                rhs = jnp.concatenate([kernel[l, i, j] for i in range(3)], 1)
                got = lax.dot_general(
                    lhs, rhs, (((1,), (1,)), ((), ())), preferred_element_type=F32
                )
            else:
                rhs = kernel[l, :, j].reshape(3 * half, half)
                got = jnp.dot(lhs, rhs, preferred_element_type=F32)
            if fresh:
                prod[j] = got
            else:
                prod[j] = prod[j] + got

    def shifted(a, rr, before, behind):
        at = pl.ds(pl.multiple_of((a * band + rr) * PAD, PAD), PAD)
        return (
            prod[1, at, :]
            + pltpu.roll(prod[before, at, :], 1, 0)
            + pltpu.roll(prod[behind, at, :], PAD - 1, 0)
        )

    def row_of(table, l, a):
        return table[l, pl.ds(a, 1), :]

    def gain_of(l):
        return own_half(gain_ref[pl.ds(l, 1), :])

    def shift_of(l):
        return own_half(shift_ref[pl.ds(l, 1), :])

    def limit(a, rr):
        w = width_of(a)
        if rr == 0:
            return jnp.where(up_there, w, 0)
        if rr == band + 1:
            return jnp.where(down_there, w, 0)
        return w

    def z_halo(l, way):
        if way == 0:
            return remote(zbuf.at[l, :, 1], zbuf.at[l, :, 5], zh_s.at[l, 0], zh_r.at[l, 0], m, z - 1, c)
        return remote(zbuf.at[l, :, 4], zbuf.at[l, :, 0], zh_s.at[l, 1], zh_r.at[l, 1], m, z + 1, c)

    def dh_halo(l, way):
        if way == 0:
            return remote(dh.at[l, :, 1], dh.at[l, :, 5], dh_s.at[l, 0], dh_r.at[l, 0], m, z - 1, c)
        return remote(dh.at[l, :, 4], dh.at[l, :, 0], dh_s.at[l, 1], dh_r.at[l, 1], m, z + 1, c)

    def start_halo(halo, l):
        @pl.when(up_there)
        def _():
            halo(l, 0).start()

        @pl.when(down_there)
        def _():
            halo(l, 1).start()

    def wait_halo(halo, l):
        @pl.when(up_there)
        def _():
            halo(l, 1).wait_recv()
            halo(l, 0).wait_send()

        @pl.when(down_there)
        def _():
            halo(l, 0).wait_recv()
            halo(l, 1).wait_send()

    def act_copy(l):
        return remote(act_own.at[l], act_oth.at[l], act_s.at[l], act_r.at[l], m, z, other)

    def dz_copy(l):
        return remote(dz_own.at[l], dz_oth.at[l], dz_s.at[l], dz_r.at[l], m, z, other)

    for copy in x_partner:
        copy.wait()

    @pl.when(up_there)
    def _():
        for n in (0, 1, 4):
            x_halo(n, 4, 0, z - 1).wait_recv()

    @pl.when(down_there)
    def _():
        for n in (0, 1, 4):
            x_halo(n, 1, 5, z + 1).wait_recv()

    @pl.when(jnp.logical_and(c == 0, up_there))
    def _():
        for n in range(6):
            x_halo(n, 1, 5, z - 1).wait_send()

    @pl.when(jnp.logical_and(c == 1, down_there))
    def _():
        for n in range(6):
            x_halo(n, 4, 0, z + 1).wait_send()

    g_partner.wait()

    def forward(l, carry):
        weight_copy(l, 0).wait()
        products(act_own, l, (0, 1, 2), wa, False, True)
        weight_copy(l, 1).wait()

        @pl.when(l > 0)
        def _():
            act_copy(l).wait_recv()

        products(act_oth, l, (0, 1, 2), wb, False, False)

        def collect(a, tile):
            inside = column < width_of(a)
            total = jnp.zeros((PAD, half), F32)
            for rr in range(band):
                v = shifted(a, rr, 0, 2)
                zbuf[l, a, 1 + rr] = v
                total = total + jnp.where(inside, v, 0.0)
            total = jnp.sum(total, 0, keepdims=True)
            mean = total / (width_of(a) * band).astype(F32)
            square = jnp.zeros((PAD, half), F32)
            for rr in range(band):
                v = jnp.where(inside, zbuf[l, a, 1 + rr] - mean, 0.0)
                square = square + v * v
            square = jnp.sum(square, 0, keepdims=True)
            tile = jnp.where(row8 == a, total, tile)
            return jnp.where(row8 == a + maps_here, square, tile)

        tile = lax.fori_loop(0, maps_here, collect, jnp.zeros((8, half), F32))
        send_z(l, tile)
        start_halo(z_halo, l)
        for i in range(3):
            act_t[l, i, 0] = act_own[l, :, i : i + band].reshape(pixels, half).T
        wait_z(l)
        sizes, inverse = inv_t[0], inv_t[1]
        total = st1[l, 0]
        for zz in range(1, chips):
            total = total + st1[l, zz]
        mean = total * inverse * (1.0 / chips)
        square = jnp.zeros((8, half), F32)
        for zz in range(chips):
            v = st1[l, zz]
            gap = v * inverse - mean
            square = square + pltpu.roll(v, 8 - maps_here, 0) + sizes * gap * gap
        tile = jnp.where(row8 < maps_here, mean, pltpu.roll(square, maps_here, 0))
        send_m(l, jnp.where(row8 < 2 * maps_here, tile, 0.0))
        for i in range(3):
            act_t[l, i, 1] = act_oth[l, :, i : i + band].reshape(pixels, half).T
        wait_m(l)
        averages = jnp.zeros((8, half), F32)
        scalings = jnp.zeros((8, half), F32)
        for a in range(maps_here):
            count = cnt_t[a : a + 1, :]
            average = jnp.zeros((8, half), F32)
            for mm in range(PLANE):
                average = average + coef[a, mm] * nall[mm] * st2[l, mm]
            average = jnp.sum(average, 0, keepdims=True) / count
            variance = jnp.zeros((8, half), F32)
            for mm in range(PLANE):
                v = st2[l, mm]
                gap = v - average
                variance = variance + coef[a, mm] * (
                    pltpu.roll(v, 8 - maps_here, 0) + nall[mm] * gap * gap
                )
            variance = jnp.sum(variance, 0, keepdims=True) / count
            averages = jnp.where(row8 == a, average, averages)
            scalings = jnp.where(row8 == a, lax.rsqrt(variance + epsilon), scalings)
        avg_t[l] = averages
        scl_t[l] = scalings
        wait_halo(z_halo, l)

        def activate(a, s):
            average = row_of(avg_t, l, a)
            factor = row_of(scl_t, l, a) * gain_of(l)
            shift = shift_of(l)
            for rr in range(band + 2):
                y = (zbuf[l, a, rr] - average) * factor + shift
                h = jnp.where(column < limit(a, rr), y * jax.nn.sigmoid(y), 0.0)
                act_own[l + 1, a, rr] = h.astype(BF16)
            return s

        lax.fori_loop(0, maps_here, activate, 0)

        @pl.when(l < LAYERS - 1)
        def _():
            act_copy(l + 1).start()

        return carry

    lax.fori_loop(0, LAYERS, forward, 0)

    def unpool(a, s):
        for rr in range(band + 2):
            slot, lower = (rr + 1) // 2, (rr + 1) % 2
            g = gbuf[slot, 0, a]
            position = gbuf[slot, 1, a]
            for b in range(2):
                v = jnp.where(position == float(2 * lower + b), g, 0.0)
                for n in range(lanes):
                    hrow[n, pl.ds(b, PAD // 2, stride=2), :] = v[:, n * 128 : (n + 1) * 128]
            dh[LAYERS, a, rr] = jnp.concatenate([hrow[n] for n in range(lanes)], 1)
        return s

    lax.fori_loop(0, maps_here, unpool, 0)

    def pool():
        def one(a, s):
            for pr in range(2):
                total = jnp.zeros((PAD // 2, half), F32)
                position = gbuf[1 + pr, 1, a]
                for lower in range(2):
                    v = act_own[LAYERS, a, 1 + 2 * pr + lower].astype(F32)
                    for n in range(lanes):
                        hrow[n] = v[:, n * 128 : (n + 1) * 128]
                    for b in range(2):
                        v = jnp.concatenate(
                            [hrow[n, pl.ds(b, PAD // 2, stride=2), :] for n in range(lanes)], 1
                        )
                        total = total + jnp.where(position == float(2 * lower + b), v, 0.0)
                pbuf[pr, a] = total.astype(BF16)
            return s

        lax.fori_loop(0, maps_here, one, 0)

    def weight_terms(l, first, last):
        def one(t, s):
            i = lax.div(t, 3)
            j = t - 3 * i
            got = jnp.dot(
                act_t[l, i].reshape(2 * half, pixels), dz_t[j], preferred_element_type=F32
            ).astype(BF16)
            q = (LAYERS - 1 - l) * TAPS + t
            terms[q, c] = got[:half]
            terms[q, other] = got[half:]
            return s

        lax.fori_loop(first, last, one, 0)

    def backward(k, carry):
        l = LAYERS - 1 - k
        gain, shift = gain_of(l), shift_of(l)

        def gradient(a, rr):
            zhat = (zbuf[l, a, rr] - row_of(avg_t, l, a)) * row_of(scl_t, l, a)
            y = zhat * gain + shift
            s = jax.nn.sigmoid(y)
            dy = dh[l + 1, a, rr] * (s * (1.0 + y * (1.0 - s)))
            dy = jnp.where(column < limit(a, rr), dy, 0.0)
            dyb[a, rr] = dy
            return dy, zhat

        def collect(a, tile):
            plain = jnp.zeros((PAD, half), F32)
            crossed = jnp.zeros((PAD, half), F32)
            for rr in range(1, band + 1):
                dy, zhat = gradient(a, rr)
                plain = plain + dy
                crossed = crossed + dy * zhat
            plain = jnp.sum(plain, 0, keepdims=True)
            crossed = jnp.sum(crossed, 0, keepdims=True)
            tile = jnp.where(row8 == a, plain, tile)
            return jnp.where(row8 == a + maps_here, crossed, tile)

        e = LAYERS + l
        tile = lax.fori_loop(0, maps_here, collect, jnp.zeros((8, half), F32))
        send_z(e, tile)

        @pl.when(k > 0)
        def _():
            weight_terms(l + 1, 0, 5)

        wait_z(e)
        total = st1[e, 0]
        for zz in range(1, chips):
            total = total + st1[e, zz]
        send_m(e, total)

        @pl.when(k > 0)
        def _():
            weight_terms(l + 1, 5, TAPS)
            wait_halo(dh_halo, l + 1)

        @pl.when(k == 0)
        def _():
            pool()

        def edges(a, s):
            gradient(a, 0)
            gradient(a, band + 1)
            return s

        lax.fori_loop(0, maps_here, edges, 0)
        wait_m(e)
        total = st2[e, 0]
        for mm in range(1, PLANE):
            total = total + st2[e, mm]
        sums_own[pl.ds(l, 1), :] = jnp.sum(
            jnp.where(row8 >= maps_here, total, 0.0), 0, keepdims=True
        )
        sums_own[pl.ds(LAYERS + l, 1), :] = jnp.sum(
            jnp.where(row8 < maps_here, total, 0.0), 0, keepdims=True
        )
        plains = jnp.zeros((8, half), F32)
        crosses = jnp.zeros((8, half), F32)
        for a in range(maps_here):
            plain = jnp.zeros((8, half), F32)
            crossed = jnp.zeros((8, half), F32)
            for mm in range(PLANE):
                v = st2[e, mm]
                plain = plain + coef[a, mm] * v
                crossed = crossed + coef[a, mm] * pltpu.roll(v, 8 - maps_here, 0)
            count = cnt_t[a : a + 1, :]
            plain = gain * (jnp.sum(plain, 0, keepdims=True) / count)
            crossed = gain * (jnp.sum(crossed, 0, keepdims=True) / count)
            plains = jnp.where(row8 == a, plain, plains)
            crosses = jnp.where(row8 == a, crossed, crosses)
        tb_t[0] = plains
        ta_t[0] = crosses

        def settle(a, s):
            average, scaling = row_of(avg_t, l, a), row_of(scl_t, l, a)
            plain, crossed = row_of(tb_t, 0, a), row_of(ta_t, 0, a)
            for rr in range(band + 2):
                zhat = (zbuf[l, a, rr] - average) * scaling
                v = scaling * (dyb[a, rr] * gain - plain - zhat * crossed)
                v = jnp.where(column < limit(a, rr), v, 0.0)
                rounded = v.astype(BF16)
                dz_own[l, a, rr] = rounded
                if 0 < rr <= band:
                    at = pl.ds(pl.multiple_of((a * band + rr - 1) * PAD, PAD), PAD)
                    dz_t[1, at, :] = rounded
                    dz_t[0, at, :] = pltpu.roll(v, PAD - 1, 0).astype(BF16)
                    dz_t[2, at, :] = pltpu.roll(v, 1, 0).astype(BF16)
            return s

        lax.fori_loop(0, maps_here, settle, 0)
        dz_copy(l).start()
        products(dz_own, l, (2, 1, 0), wa, True, True)
        weight_copy(l, 2).wait()
        dz_copy(l).wait_recv()
        products(dz_oth, l, (2, 1, 0), wc, True, False)

        def gather(a, s):
            for rr in range(band):
                dh[l, a, 1 + rr] = shifted(a, rr, 2, 0)
            return s

        lax.fori_loop(0, maps_here, gather, 0)

        @pl.when(l > 0)
        def _():
            start_halo(dh_halo, l)

        return carry

    lax.fori_loop(0, LAYERS, backward, 0)
    weight_terms(0, 0, TAPS)

    def input_rows(a, s):
        for rr in range(band):
            igbuf[rr // 2, a, rr % 2] = jnp.where(
                column < width_of(a), dh[0, a, 1 + rr], 0.0
            )
        return s

    lax.fori_loop(0, maps_here, input_rows, 0)

    outs = (
        (
            remote(igbuf.at[other], ig_ref.at[c], out_s.at[0], out_r.at[0], m, z, other),
            pltpu.make_async_copy(igbuf.at[c], ig_ref.at[c], out_l.at[0]),
        ),
        (
            remote(pbuf.at[other], pooled_ref.at[c], out_s.at[1], out_r.at[1], m, z, other),
            pltpu.make_async_copy(pbuf.at[c], pooled_ref.at[c], out_l.at[1]),
        ),
        (
            remote(sums_own, sums_ref.at[c], out_s.at[2], out_r.at[2], m, z, other),
            pltpu.make_async_copy(sums_own, sums_ref.at[c], out_l.at[2]),
        ),
    )
    for there, here in outs:
        there.start()
        here.start()

    for l in range(1, LAYERS):
        act_copy(l).wait_send()
    for l in range(LAYERS):
        dz_copy(l).wait_send()
    for there, here in outs:
        there.wait()
        here.wait()


def reduce_kernel(
    chips,
    terms,
    kg_ref,
    r1,
    r2,
    r3,
    fin,
    r1_s,
    r1_r,
    r2_s,
    r2_r,
    r3_s,
    r3_r,
    az_s,
    az_r,
    ab_s,
    ab_r,
    aa_s,
    aa_r,
    ap_s,
    ap_r,
    loc_s,
):
    half = r1.shape[2]
    owners = min(chips, 8)
    piece = (half // 2) // owners
    m = lax.axis_index("maps")
    r = lax.axis_index("rows")
    c = lax.rem(r, 2)
    z = lax.div(r, 2)
    other = 1 - c
    x_bit = lax.rem(m, 2)
    y_bit = lax.div(m, 2)
    x_peer = m + 1 - 2 * x_bit
    y_peer = m + 2 - 4 * y_bit
    own_at = pl.ds(pl.multiple_of(c * half, half), half)

    def remote(src, dst, send, recv, mm, zz, cc):
        return pltpu.make_async_remote_copy(
            src_ref=src,
            dst_ref=dst,
            send_sem=send,
            recv_sem=recv,
            device_id=(mm, zz * 2 + cc),
            device_id_type=MESH,
        )

    barrier = pltpu.get_barrier_semaphore()

    def greet(k):
        rr = lax.rem(r + k, 2 * chips)
        pl.semaphore_signal(barrier, inc=1, device_id=(m, rr), device_id_type=MESH)

    each(1, 2 * chips, greet)
    for k in range(1, PLANE):
        pl.semaphore_signal(
            barrier, inc=1, device_id=(lax.rem(m + k, PLANE), r), device_id_type=MESH
        )
    pl.semaphore_wait(barrier, 2 * chips - 1 + PLANE - 1)

    def order(q):
        swap = lax.rem(q, 2)
        keep = 1 - swap
        return (
            keep * x_peer + swap * y_peer,
            keep * x_bit + swap * y_bit,
            keep * y_peer + swap * x_peer,
            keep * y_bit + swap * x_bit,
        )

    def c1(q):
        peer, bit, _, _ = order(q)
        return remote(terms.at[q, 1 - bit], r1.at[q], r1_s.at[q], r1_r.at[q], peer, z, c)

    def second_rows(bit):
        return pl.ds(pl.multiple_of(bit * (half // 2), half // 2), half // 2)

    def c2(q):
        _, _, peer, bit = order(q)
        return remote(r1.at[q, second_rows(1 - bit)], r2.at[q], r2_s.at[q], r2_r.at[q], peer, z, c)

    def piece_rows(p):
        return pl.ds(pl.multiple_of(p * piece, piece), piece)

    def c3(q, p):
        slot = lax.rem(z - p + chips - 1, chips)
        return remote(
            r2.at[q, piece_rows(p)], r3.at[q, slot], r3_s.at[q, p], r3_r.at[q, slot], m, p, c
        )

    def unit_of(q):
        k = lax.div(q, TAPS)
        return (LAYERS - 1 - k) * TAPS + (q - k * TAPS)

    def region(q, start, size):
        start = pl.multiple_of(start, piece)
        return kg_ref.at[unit_of(q), pl.ds(start, size), own_at]

    def base(q):
        _, first_bit, _, second_bit = order(q)
        return first_bit * half + second_bit * (half // 2)

    def cz(q, p, zz):
        return remote(
            fin.at[q],
            region(q, base(q) + p * piece, piece),
            az_s.at[q, zz],
            az_r.at[q, p],
            m,
            zz,
            c,
        )

    def cl(q):
        return pltpu.make_async_copy(
            fin.at[q], region(q, base(q) + z * piece, piece), loc_s.at[q]
        )

    def cb(q):
        _, _, peer, _ = order(q)
        part = region(q, base(q), half // 2)
        return remote(part, part, ab_s.at[q], ab_r.at[q], peer, z, c)

    def ca(q):
        peer, bit, _, _ = order(q)
        part = region(q, bit * half, half)
        return remote(part, part, aa_s.at[q], aa_r.at[q], peer, z, c)

    def cp(q):
        part = region(q, 0, 2 * half)
        return remote(part, part, ap_s.at[q], ap_r.at[q], m, z, other)

    def begin(q, carry):
        c1(q).start()
        return carry

    lax.fori_loop(0, UNITS, begin, 0)

    def within(q):
        return jnp.logical_and(q >= 0, q < UNITS)

    def drain(s, carry):
        @pl.when(within(s - 5))
        def _():
            q = s - 5
            ca(q).wait_recv()
            cp(q).start()

        @pl.when(within(s - 4))
        def _():
            q = s - 4
            cb(q).wait_recv()
            ca(q).start()

        @pl.when(within(s - 3))
        def _():
            q = s - 3

            def arrived(k):
                p = lax.rem(z + k, chips)

                @pl.when(p < owners)
                def _():
                    cz(q, p, p).wait_recv()

            each(1, chips, arrived)

            @pl.when(z < owners)
            def _():
                cl(q).wait()

            cb(q).start()

        @pl.when(within(s - 2))
        def _():
            q = s - 2

            @pl.when(z < owners)
            def _():
                total = r2[q, piece_rows(z)].astype(F32)
                for k in range(chips - 1):
                    remote(
                        r2.at[q, piece_rows(0)],
                        r3.at[q, k],
                        r3_s.at[q, 0],
                        r3_r.at[q, k],
                        m,
                        z,
                        c,
                    ).wait_recv()
                for k in range(chips - 1):
                    total = total + r3[q, k].astype(F32)
                fin[q] = total.astype(BF16)
                each(1, chips, lambda k: cz(q, z, lax.rem(z + k, chips)).start())
                cl(q).start()

        @pl.when(within(s - 1))
        def _():
            q = s - 1
            _, _, _, bit = order(q)
            c2(q).wait_recv()
            r2[q] = (r2[q].astype(F32) + r1[q, second_rows(bit)].astype(F32)).astype(BF16)

            def give(k):
                p = lax.rem(z + k, chips)

                @pl.when(p < owners)
                def _():
                    c3(q, p).start()

            each(1, chips, give)

        @pl.when(within(s))
        def _():
            q = s
            _, bit, _, _ = order(q)
            c1(q).wait_recv()
            r1[q] = (r1[q].astype(F32) + terms[q, bit].astype(F32)).astype(BF16)
            c2(q).start()

        return carry

    lax.fori_loop(0, UNITS + 6, drain, 0)

    def finish(q, carry):
        cp(q).wait()
        ca(q).wait_send()
        cb(q).wait_send()
        c1(q).wait_send()
        c2(q).wait_send()

        def given(k):
            p = lax.rem(z + k, chips)

            @pl.when(p < owners)
            def _():
                c3(q, p).wait_send()

        each(1, chips, given)

        @pl.when(z < owners)
        def _():
            each(1, chips, lambda k: cz(q, z, lax.rem(z + k, chips)).wait_send())

        return carry

    lax.fori_loop(0, UNITS, finish, 0)


def solution(mesh):
    chips = mesh.shape["rows"] // 2

    def per_device(
        block_input,
        conv_weights,
        norm_gains,
        norm_shifts,
        map_width,
        map_group,
        pool_index,
        task_mask,
        task_weights,
        task_grads,
    ):
        maps_here, rows_here, columns, channels = block_input.shape
        pooled_columns = pool_index.shape[2]
        height = rows_here * mesh.shape["rows"]
        half = channels // 2
        band = 2 * rows_here
        pixels = maps_here * band * PAD
        owners = min(chips, 8)
        piece = half // 2 // owners
        rounds = 2 * LAYERS
        vmem, dma = pltpu.VMEM, pltpu.SemaphoreType.DMA
        tile = (maps_here, band + 2, PAD, half)
        whole = pl.BlockSpec(memory_space=pltpu.VMEM)
        scalars = pl.BlockSpec(memory_space=pltpu.SMEM)
        anywhere = pl.BlockSpec(memory_space=pl.ANY)
        pooled, ig, terms, sums = pl.pallas_call(
            functools.partial(block_kernel, chips, height),
            out_shape=(
                jax.ShapeDtypeStruct((2, maps_here, PAD // 2, half), BF16),
                jax.ShapeDtypeStruct((2, maps_here, rows_here, PAD, half), F32),
                jax.ShapeDtypeStruct((UNITS, 2, half, half), BF16),
                jax.ShapeDtypeStruct((2, 8, half), F32),
            ),
            in_specs=[whole, anywhere, whole, whole, scalars, scalars, whole, scalars, scalars, whole],
            out_specs=[anywhere, anywhere, whole, anywhere],
            scratch_shapes=[
                vmem((LAYERS, 3, 3, half, half), BF16),
                vmem((LAYERS, 3, 3, half, half), BF16),
                vmem((LAYERS, 3, 3, half, half), BF16),
                vmem((LAYERS + 1,) + tile, BF16),
                vmem((LAYERS,) + tile, BF16),
                vmem((LAYERS, 3, 2, half, pixels), BF16),
                vmem((LAYERS,) + tile, F32),
                vmem((LAYERS + 1,) + tile, F32),
                vmem(tile, F32),
                vmem((LAYERS,) + tile, BF16),
                vmem((LAYERS,) + tile, BF16),
                vmem((3, pixels, half), BF16),
                vmem((3, pixels, half), F32),
                vmem((2, 2, maps_here, PAD // 2, half), F32),
                vmem((4, 2, maps_here, PAD // 2, half), F32),
                vmem((half // 128, PAD, 128), F32),
                vmem((2, maps_here, PAD // 2, half), BF16),
                vmem((2, maps_here, rows_here, PAD, half), F32),
                vmem((rounds, chips, 8, half), F32),
                vmem((rounds, PLANE, 8, half), F32),
                vmem((maps_here, PLANE, 8, half), F32),
                vmem((PLANE, 8, half), F32),
                vmem((2, 8, half), F32),
                vmem((8, half), F32),
                vmem((LAYERS, 8, half), F32),
                vmem((LAYERS, 8, half), F32),
                vmem((1, 8, half), F32),
                vmem((1, 8, half), F32),
                vmem((8, half), F32),
                dma((LAYERS, 3)),
                dma((6,)),
                dma((6,)),
                dma((3,)),
                dma((3,)),
                dma((rounds, chips)),
                dma((rounds, chips)),
                dma((rounds, PLANE)),
                dma((rounds, PLANE)),
                dma((LAYERS, 2)),
                dma((LAYERS, 2)),
                dma((LAYERS, 2)),
                dma((LAYERS, 2)),
                dma((LAYERS,)),
                dma((LAYERS,)),
                dma((LAYERS,)),
                dma((LAYERS,)),
                dma((3,)),
                dma((3,)),
                dma((3,)),
            ],
            compiler_params=pltpu.CompilerParams(
                collective_id=0,
                has_side_effects=True,
                vmem_limit_bytes=63 * 1024 * 1024,
            ),
        )(
            block_input,
            conv_weights,
            norm_gains,
            norm_shifts,
            map_width,
            map_group,
            pool_index,
            task_mask,
            task_weights,
            task_grads,
        )
        kg = pl.pallas_call(
            functools.partial(reduce_kernel, chips),
            out_shape=jax.ShapeDtypeStruct((UNITS, channels, channels), BF16),
            in_specs=[whole],
            out_specs=anywhere,
            scratch_shapes=[
                vmem((UNITS, half, half), BF16),
                vmem((UNITS, half // 2, half), BF16),
                vmem((UNITS, chips - 1, piece, half), BF16),
                vmem((UNITS, piece, half), BF16),
                dma((UNITS,)),
                dma((UNITS,)),
                dma((UNITS,)),
                dma((UNITS,)),
                dma((UNITS, owners)),
                dma((UNITS, chips - 1)),
                dma((UNITS, chips)),
                dma((UNITS, owners)),
                dma((UNITS,)),
                dma((UNITS,)),
                dma((UNITS,)),
                dma((UNITS,)),
                dma((UNITS,)),
                dma((UNITS,)),
                dma((UNITS,)),
            ],
            compiler_params=pltpu.CompilerParams(
                collective_id=1,
                has_side_effects=True,
                vmem_limit_bytes=63 * 1024 * 1024,
            ),
        )(terms)
        pooled = jnp.concatenate([pooled[0], pooled[1]], -1)[:, None, :pooled_columns]
        input_grad = jnp.concatenate([ig[0], ig[1]], -1)[:, :, :columns]
        sums = jnp.concatenate([sums[0], sums[1]], -1)
        return (
            pooled,
            input_grad,
            kg.astype(F32).reshape(conv_weights.shape),
            sums[:LAYERS],
            sums[LAYERS : 2 * LAYERS],
        )

    return jax.shard_map(
        per_device,
        mesh=mesh,
        in_specs=(
            P("maps", "rows", None, None),
            P(),
            P(),
            P(),
            P(),
            P(),
            P("maps", "rows", None, None),
            P("maps", None),
            P(),
            P(None, "maps", "rows", None, None),
        ),
        out_specs=(P("maps", "rows", None, None), P("maps", "rows", None, None), P(), P(), P()),
        check_vma=False,
    )
```

```python
import functools

import jax
import jax.numpy as jnp
from jax import lax
from jax.experimental import pallas as pl
from jax.experimental.pallas import tpu as pltpu
from jax.sharding import PartitionSpec as P

MESH = pl.DeviceIdType.MESH
epsilon = 1e-05
PAD = 64
LAYERS = 3
TAPS = 9
UNITS = LAYERS * TAPS
PLANE = 4
LAG = 2
F32 = jnp.float32
BF16 = jnp.bfloat16


def each(first, last, body):
    if last - first <= 8:
        for k in range(first, last):
            body(k)
    else:
        lax.fori_loop(first, last, lambda k, s: (body(k), s)[1], 0)


def block_kernel(
    chips,
    height,
    x_ref,
    w_ref,
    gain_ref,
    shift_ref,
    width_ref,
    group_ref,
    index_ref,
    tmask_ref,
    tweight_ref,
    tgrad_ref,
    pooled_ref,
    ig_ref,
    kg_ref,
    sums_ref,
    wa,
    wb,
    wc,
    act_own,
    act_oth,
    act_t,
    zbuf,
    dh,
    dyb,
    dz_own,
    dz_oth,
    dz_t,
    prod,
    gsrc,
    gbuf,
    hrow,
    pbuf,
    igbuf,
    st1,
    st2,
    coef,
    nall,
    inv_t,
    cnt_t,
    avg_t,
    scl_t,
    tb_t,
    ta_t,
    sums_own,
    terms,
    r1,
    r2,
    r3,
    fin,
    w_sem,
    x_s,
    x_r,
    g_s,
    g_r,
    st1_s,
    st1_r,
    st2_s,
    st2_r,
    zh_s,
    zh_r,
    dh_s,
    dh_r,
    act_s,
    act_r,
    dz_s,
    dz_r,
    out_s,
    out_r,
    out_l,
    r1_s,
    r1_r,
    r2_s,
    r2_r,
    r3_s,
    r3_r,
    az_s,
    az_r,
    ab_s,
    ab_r,
    aa_s,
    aa_r,
    ap_s,
    ap_r,
    loc_s,
):
    maps_here = x_ref.shape[0]
    columns = x_ref.shape[2]
    half = x_ref.shape[3] // 2
    tasks = tgrad_ref.shape[0]
    pooled_columns = tgrad_ref.shape[3]
    lanes = half // 128
    band = 4
    pixels = maps_here * band * PAD
    owners = min(chips, 8)
    piece = (half // 2) // owners
    m = lax.axis_index("maps")
    r = lax.axis_index("rows")
    c = lax.rem(r, 2)
    z = lax.div(r, 2)
    other = 1 - c
    first_map = m * maps_here
    x_bit = lax.rem(m, 2)
    y_bit = lax.div(m, 2)
    x_peer = m + 1 - 2 * x_bit
    y_peer = m + 2 - 4 * y_bit
    up_there = z > 0
    down_there = z < chips - 1
    row8 = lax.broadcasted_iota(jnp.int32, (8, half), 0)
    column = lax.broadcasted_iota(jnp.int32, (PAD, half), 0)

    def remote(src, dst, send, recv, mm, zz, cc):
        return pltpu.make_async_remote_copy(
            src_ref=src,
            dst_ref=dst,
            send_sem=send,
            recv_sem=recv,
            device_id=(mm, zz * 2 + cc),
            device_id_type=MESH,
        )

    def own_half(v):
        return jnp.where(c == 0, v[..., :half], v[..., half:])

    def width_of(a):
        return width_ref[first_map + a]

    own_at = pl.ds(pl.multiple_of(c * half, half), half)
    oth_at = pl.ds(pl.multiple_of(other * half, half), half)

    def weight_copy(l, n):
        dst = (wa, wb, wc)[n]
        k_at, o_at = ((own_at, own_at), (oth_at, own_at), (own_at, oth_at))[n]
        return pltpu.make_async_copy(w_ref.at[l, :, :, k_at, o_at], dst.at[l], w_sem.at[l, n])

    for l in range(LAYERS):
        weight_copy(l, 0).start()
        weight_copy(l, 1).start()
    for l in range(LAYERS):
        weight_copy(LAYERS - 1 - l, 2).start()

    barrier = pltpu.get_barrier_semaphore()

    def greet(k):
        rr = lax.rem(r + k, 2 * chips)
        pl.semaphore_signal(barrier, inc=1, device_id=(m, rr), device_id_type=MESH)

    each(1, 2 * chips, greet)
    for k in range(1, PLANE):
        pl.semaphore_signal(
            barrier, inc=1, device_id=(lax.rem(m + k, PLANE), r), device_id_type=MESH
        )

    mine = pl.ds(1 + 2 * c, 2)
    for a in range(maps_here):
        inside = lax.broadcasted_iota(jnp.int32, (columns, 2 * half), 0) < width_of(a)
        for rr in range(2):
            v = jnp.where(inside, x_ref[a, rr].astype(F32), 0.0).astype(BF16)
            at = 1 + 2 * c + rr
            act_own[0, a, at, pl.ds(48, 16), :] = jnp.zeros((16, half), BF16)
            act_oth[0, a, at, pl.ds(48, 16), :] = jnp.zeros((16, half), BF16)
            act_own[0, a, at, pl.ds(0, columns), :] = own_half(v)
            act_oth[0, a, at, pl.ds(0, columns), :] = jnp.where(
                c == 0, v[:, half:], v[:, :half]
            )

    @pl.when(z == 0)
    def _():
        act_own[0, :, 0] = jnp.zeros((maps_here, PAD, half), BF16)
        act_oth[0, :, 0] = jnp.zeros((maps_here, PAD, half), BF16)

    @pl.when(z == chips - 1)
    def _():
        act_own[0, :, 5] = jnp.zeros((maps_here, PAD, half), BF16)
        act_oth[0, :, 5] = jnp.zeros((maps_here, PAD, half), BF16)

    gsrc[...] = jnp.zeros(gsrc.shape, F32)
    for a in range(maps_here):
        total = None
        for t in range(tasks):
            scale = tweight_ref[t] * tmask_ref[a, t].astype(F32)
            term = tgrad_ref[t, a, 0].astype(F32) * scale
            total = term if total is None else total + term
        position = index_ref[a, 0].astype(F32)
        for h in range(2):
            gsrc[h, 0, a, pl.ds(0, pooled_columns), :] = total[:, h * half : (h + 1) * half]
            gsrc[h, 1, a, pl.ds(0, pooled_columns), :] = position[:, h * half : (h + 1) * half]
    gbuf[1 + c] = gsrc[c]

    pl.semaphore_wait(barrier, 2 * chips - 1 + PLANE - 1)

    x_partner = (
        remote(act_own.at[0, :, mine], act_oth.at[0, :, mine], x_s.at[0], x_r.at[0], m, z, other),
        remote(act_oth.at[0, :, mine], act_own.at[0, :, mine], x_s.at[1], x_r.at[1], m, z, other),
    )
    g_partner = remote(gsrc.at[other], gbuf.at[1 + c], g_s.at[0], g_r.at[0], m, z, other)

    def x_halo(n, src_row, dst_row, zz):
        cc = (c, c, other, other, c, other)[n]
        low = dst_row == band + 1
        if n >= 4:
            src, dst = gsrc.at[cc], gbuf.at[3 if low else 0]
            return remote(src, dst, g_s.at[n - 3], g_r.at[1 if low else 2], m, zz, cc)
        src = (act_own, act_oth, act_own, act_oth)[n].at[0, :, src_row]
        dst = (act_own, act_oth, act_oth, act_own)[n].at[0, :, dst_row]
        return remote(src, dst, x_s.at[2 + n], x_r.at[(2 if low else 4) + n % 2], m, zz, cc)

    for copy in x_partner:
        copy.start()

    @pl.when(jnp.logical_and(c == 0, up_there))
    def _():
        for n in range(6):
            x_halo(n, 1, 5, z - 1).start()

    @pl.when(jnp.logical_and(c == 1, down_there))
    def _():
        for n in range(6):
            x_halo(n, 4, 0, z + 1).start()

    g_partner.start()

    for mm in range(PLANE):
        sizes = jnp.zeros((8, half), F32)
        for b in range(maps_here):
            sizes = jnp.where(
                row8 == b, (width_ref[mm * maps_here + b] * height).astype(F32), sizes
            )
        nall[mm] = sizes
    inside_sizes = jnp.zeros((8, half), F32)
    for b in range(maps_here):
        inside_sizes = jnp.where(row8 == b, (width_of(b) * band).astype(F32), inside_sizes)
    inv_t[0] = inside_sizes
    inv_t[1] = jnp.where(row8 < maps_here, 1.0 / jnp.maximum(inside_sizes, 1.0), 0.0)
    counts = jnp.ones((8, half), F32)
    for a in range(maps_here):
        total = jnp.zeros((1, half), F32)
        for mm in range(PLANE):
            same = jnp.zeros((8, half), F32)
            for b in range(maps_here):
                alike = group_ref[first_map + a] == group_ref[mm * maps_here + b]
                same = jnp.where(row8 == b, jnp.where(alike, 1.0, 0.0), same)
            coef[a, mm] = same
            total = total + jnp.sum(same * nall[mm], 0, keepdims=True)
        counts = jnp.where(row8 == a, total, counts)
    cnt_t[...] = counts

    def z_copy(e, k):
        zz = lax.rem(z + k, chips)
        return remote(st1.at[e, z], st1.at[e, z], st1_s.at[e, k], st1_r.at[e, z], m, zz, c)

    def z_arrival(e, k):
        zz = lax.rem(z + k, chips)
        return remote(st1.at[e, zz], st1.at[e, zz], st1_s.at[e, k], st1_r.at[e, zz], m, zz, c)

    def m_copy(e, k):
        mm = lax.rem(m + k, PLANE)
        return remote(st2.at[e, m], st2.at[e, m], st2_s.at[e, k], st2_r.at[e, m], mm, z, c)

    def m_arrival(e, k):
        mm = lax.rem(m + k, PLANE)
        return remote(st2.at[e, mm], st2.at[e, mm], st2_s.at[e, k], st2_r.at[e, mm], mm, z, c)

    def send_z(e, tile):
        st1[e, z] = tile
        each(1, chips, lambda k: z_copy(e, k).start())

    def wait_z(e):
        each(1, chips, lambda k: z_arrival(e, k).wait_recv())
        each(1, chips, lambda k: z_copy(e, k).wait_send())

    def send_m(e, tile):
        st2[e, m] = tile
        each(1, PLANE, lambda k: m_copy(e, k).start())

    def wait_m(e):
        each(1, PLANE, lambda k: m_arrival(e, k).wait_recv())
        each(1, PLANE, lambda k: m_copy(e, k).wait_send())

    def products(source, l, starts, kernel, transposed, fresh):
        parts = [
            source[l, :, s : s + band].reshape(pixels, half) for s in starts
        ]
        lhs = jnp.concatenate(parts, 1)
        for j in range(3):
            if transposed:
                rhs = jnp.concatenate([kernel[l, i, j] for i in range(3)], 1)
                got = lax.dot_general(
                    lhs, rhs, (((1,), (1,)), ((), ())), preferred_element_type=F32
                )
            else:
                rhs = kernel[l, :, j].reshape(3 * half, half)
                got = jnp.dot(lhs, rhs, preferred_element_type=F32)
            if fresh:
                prod[j] = got
            else:
                prod[j] = prod[j] + got

    def shifted(a, rr, before, behind):
        at = pl.ds(pl.multiple_of((a * band + rr) * PAD, PAD), PAD)
        return (
            prod[1, at, :]
            + pltpu.roll(prod[before, at, :], 1, 0)
            + pltpu.roll(prod[behind, at, :], PAD - 1, 0)
        )

    def row_of(table, l, a):
        return table[l, pl.ds(a, 1), :]

    def gain_of(l):
        return own_half(gain_ref[pl.ds(l, 1), :])

    def shift_of(l):
        return own_half(shift_ref[pl.ds(l, 1), :])

    def limit(a, rr):
        w = width_of(a)
        if rr == 0:
            return jnp.where(up_there, w, 0)
        if rr == band + 1:
            return jnp.where(down_there, w, 0)
        return w

    def z_halo(l, way):
        if way == 0:
            return remote(zbuf.at[l, :, 1], zbuf.at[l, :, 5], zh_s.at[l, 0], zh_r.at[l, 0], m, z - 1, c)
        return remote(zbuf.at[l, :, 4], zbuf.at[l, :, 0], zh_s.at[l, 1], zh_r.at[l, 1], m, z + 1, c)

    def dh_halo(l, way):
        if way == 0:
            return remote(dh.at[l, :, 1], dh.at[l, :, 5], dh_s.at[l, 0], dh_r.at[l, 0], m, z - 1, c)
        return remote(dh.at[l, :, 4], dh.at[l, :, 0], dh_s.at[l, 1], dh_r.at[l, 1], m, z + 1, c)

    def start_halo(halo, l):
        @pl.when(up_there)
        def _():
            halo(l, 0).start()

        @pl.when(down_there)
        def _():
            halo(l, 1).start()

    def wait_halo(halo, l):
        @pl.when(up_there)
        def _():
            halo(l, 1).wait_recv()
            halo(l, 0).wait_send()

        @pl.when(down_there)
        def _():
            halo(l, 0).wait_recv()
            halo(l, 1).wait_send()

    def act_copy(l):
        return remote(act_own.at[l], act_oth.at[l], act_s.at[l], act_r.at[l], m, z, other)

    def dz_copy(l):
        return remote(dz_own.at[l], dz_oth.at[l], dz_s.at[l], dz_r.at[l], m, z, other)

    for copy in x_partner:
        copy.wait()

    @pl.when(up_there)
    def _():
        for n in (0, 1, 4):
            x_halo(n, 4, 0, z - 1).wait_recv()

    @pl.when(down_there)
    def _():
        for n in (0, 1, 4):
            x_halo(n, 1, 5, z + 1).wait_recv()

    @pl.when(jnp.logical_and(c == 0, up_there))
    def _():
        for n in range(6):
            x_halo(n, 1, 5, z - 1).wait_send()

    @pl.when(jnp.logical_and(c == 1, down_there))
    def _():
        for n in range(6):
            x_halo(n, 4, 0, z + 1).wait_send()

    g_partner.wait()

    def forward(l, carry):
        weight_copy(l, 0).wait()
        products(act_own, l, (0, 1, 2), wa, False, True)
        weight_copy(l, 1).wait()

        @pl.when(l > 0)
        def _():
            act_copy(l).wait_recv()

        products(act_oth, l, (0, 1, 2), wb, False, False)

        def collect(a, tile):
            inside = column < width_of(a)
            total = jnp.zeros((PAD, half), F32)
            for rr in range(band):
                v = shifted(a, rr, 0, 2)
                zbuf[l, a, 1 + rr] = v
                total = total + jnp.where(inside, v, 0.0)
            total = jnp.sum(total, 0, keepdims=True)
            mean = total / (width_of(a) * band).astype(F32)
            square = jnp.zeros((PAD, half), F32)
            for rr in range(band):
                v = jnp.where(inside, zbuf[l, a, 1 + rr] - mean, 0.0)
                square = square + v * v
            square = jnp.sum(square, 0, keepdims=True)
            tile = jnp.where(row8 == a, total, tile)
            return jnp.where(row8 == a + maps_here, square, tile)

        tile = lax.fori_loop(0, maps_here, collect, jnp.zeros((8, half), F32))
        send_z(l, tile)
        start_halo(z_halo, l)
        for i in range(3):
            act_t[l, i, 0] = act_own[l, :, i : i + band].reshape(pixels, half).T
        wait_z(l)
        sizes, inverse = inv_t[0], inv_t[1]
        total = st1[l, 0]
        for zz in range(1, chips):
            total = total + st1[l, zz]
        mean = total * inverse * (1.0 / chips)
        square = jnp.zeros((8, half), F32)
        for zz in range(chips):
            v = st1[l, zz]
            gap = v * inverse - mean
            square = square + pltpu.roll(v, 8 - maps_here, 0) + sizes * gap * gap
        tile = jnp.where(row8 < maps_here, mean, pltpu.roll(square, maps_here, 0))
        send_m(l, jnp.where(row8 < 2 * maps_here, tile, 0.0))
        for i in range(3):
            act_t[l, i, 1] = act_oth[l, :, i : i + band].reshape(pixels, half).T
        wait_m(l)
        averages = jnp.zeros((8, half), F32)
        scalings = jnp.zeros((8, half), F32)
        for a in range(maps_here):
            count = cnt_t[a : a + 1, :]
            average = jnp.zeros((8, half), F32)
            for mm in range(PLANE):
                average = average + coef[a, mm] * nall[mm] * st2[l, mm]
            average = jnp.sum(average, 0, keepdims=True) / count
            variance = jnp.zeros((8, half), F32)
            for mm in range(PLANE):
                v = st2[l, mm]
                gap = v - average
                variance = variance + coef[a, mm] * (
                    pltpu.roll(v, 8 - maps_here, 0) + nall[mm] * gap * gap
                )
            variance = jnp.sum(variance, 0, keepdims=True) / count
            averages = jnp.where(row8 == a, average, averages)
            scalings = jnp.where(row8 == a, lax.rsqrt(variance + epsilon), scalings)
        avg_t[l] = averages
        scl_t[l] = scalings
        wait_halo(z_halo, l)

        def activate(a, s):
            average = row_of(avg_t, l, a)
            factor = row_of(scl_t, l, a) * gain_of(l)
            shift = shift_of(l)
            for rr in range(band + 2):
                y = (zbuf[l, a, rr] - average) * factor + shift
                h = jnp.where(column < limit(a, rr), y * jax.nn.sigmoid(y), 0.0)
                act_own[l + 1, a, rr] = h.astype(BF16)
            return s

        lax.fori_loop(0, maps_here, activate, 0)

        @pl.when(l < LAYERS - 1)
        def _():
            act_copy(l + 1).start()

        return carry

    lax.fori_loop(0, LAYERS, forward, 0)

    def unpool(a, s):
        for rr in range(band + 2):
            slot, lower = (rr + 1) // 2, (rr + 1) % 2
            g = gbuf[slot, 0, a]
            position = gbuf[slot, 1, a]
            for b in range(2):
                v = jnp.where(position == float(2 * lower + b), g, 0.0)
                for n in range(lanes):
                    hrow[n, pl.ds(b, PAD // 2, stride=2), :] = v[:, n * 128 : (n + 1) * 128]
            dh[LAYERS, a, rr] = jnp.concatenate([hrow[n] for n in range(lanes)], 1)
        return s

    lax.fori_loop(0, maps_here, unpool, 0)

    def pool():
        def one(a, s):
            for pr in range(2):
                total = jnp.zeros((PAD // 2, half), F32)
                position = gbuf[1 + pr, 1, a]
                for lower in range(2):
                    v = act_own[LAYERS, a, 1 + 2 * pr + lower].astype(F32)
                    for n in range(lanes):
                        hrow[n] = v[:, n * 128 : (n + 1) * 128]
                    for b in range(2):
                        v = jnp.concatenate(
                            [hrow[n, pl.ds(b, PAD // 2, stride=2), :] for n in range(lanes)], 1
                        )
                        total = total + jnp.where(position == float(2 * lower + b), v, 0.0)
                pbuf[pr, a] = total.astype(BF16)
            return s

        lax.fori_loop(0, maps_here, one, 0)

    def order(q):
        swap = lax.rem(q, 2)
        keep = 1 - swap
        return (
            keep * x_peer + swap * y_peer,
            keep * x_bit + swap * y_bit,
            keep * y_peer + swap * x_peer,
            keep * y_bit + swap * x_bit,
        )

    def c1(q):
        peer, bit, _, _ = order(q)
        return remote(terms.at[q, 1 - bit], r1.at[q], r1_s.at[q], r1_r.at[q], peer, z, c)

    def second_rows(bit):
        return pl.ds(pl.multiple_of(bit * (half // 2), half // 2), half // 2)

    def c2(q):
        _, _, peer, bit = order(q)
        return remote(r1.at[q, second_rows(1 - bit)], r2.at[q], r2_s.at[q], r2_r.at[q], peer, z, c)

    def piece_rows(p):
        return pl.ds(pl.multiple_of(p * piece, piece), piece)

    def c3(q, p):
        slot = lax.rem(z - p + chips - 1, chips)
        return remote(
            r2.at[q, piece_rows(p)], r3.at[q, slot], r3_s.at[q, p], r3_r.at[q, slot], m, p, c
        )

    def unit_of(q):
        k = lax.div(q, TAPS)
        return (LAYERS - 1 - k) * TAPS + (q - k * TAPS)

    def region(q, start, size):
        start = pl.multiple_of(start, piece)
        return kg_ref.at[unit_of(q), pl.ds(start, size), own_at]

    def base(q):
        _, first_bit, _, second_bit = order(q)
        return first_bit * half + second_bit * (half // 2)

    def cz(q, p, zz):
        return remote(
            fin.at[q],
            region(q, base(q) + p * piece, piece),
            az_s.at[q, zz],
            az_r.at[q, p],
            m,
            zz,
            c,
        )

    def cl(q):
        return pltpu.make_async_copy(
            fin.at[q], region(q, base(q) + z * piece, piece), loc_s.at[q]
        )

    def cb(q):
        _, _, peer, _ = order(q)
        part = region(q, base(q), half // 2)
        return remote(part, part, ab_s.at[q], ab_r.at[q], peer, z, c)

    def ca(q):
        peer, bit, _, _ = order(q)
        part = region(q, bit * half, half)
        return remote(part, part, aa_s.at[q], aa_r.at[q], peer, z, c)

    def cp(q):
        part = region(q, 0, 2 * half)
        return remote(part, part, ap_s.at[q], ap_r.at[q], m, z, other)

    def weight_terms(l, first, last):
        def one(t, s):
            i = lax.div(t, 3)
            j = t - 3 * i
            got = jnp.dot(
                act_t[l, i].reshape(2 * half, pixels), dz_t[j], preferred_element_type=F32
            ).astype(BF16)
            q = (LAYERS - 1 - l) * TAPS + t
            terms[q, c] = got[:half]
            terms[q, other] = got[half:]
            c1(q).start()
            return s

        lax.fori_loop(first, last, one, 0)

    def backward(k, carry):
        l = LAYERS - 1 - k
        gain, shift = gain_of(l), shift_of(l)

        def gradient(a, rr):
            zhat = (zbuf[l, a, rr] - row_of(avg_t, l, a)) * row_of(scl_t, l, a)
            y = zhat * gain + shift
            s = jax.nn.sigmoid(y)
            dy = dh[l + 1, a, rr] * (s * (1.0 + y * (1.0 - s)))
            dy = jnp.where(column < limit(a, rr), dy, 0.0)
            dyb[a, rr] = dy
            return dy, zhat

        def collect(a, tile):
            plain = jnp.zeros((PAD, half), F32)
            crossed = jnp.zeros((PAD, half), F32)
            for rr in range(1, band + 1):
                dy, zhat = gradient(a, rr)
                plain = plain + dy
                crossed = crossed + dy * zhat
            plain = jnp.sum(plain, 0, keepdims=True)
            crossed = jnp.sum(crossed, 0, keepdims=True)
            tile = jnp.where(row8 == a, plain, tile)
            return jnp.where(row8 == a + maps_here, crossed, tile)

        e = LAYERS + l
        tile = lax.fori_loop(0, maps_here, collect, jnp.zeros((8, half), F32))
        send_z(e, tile)

        @pl.when(k > 0)
        def _():
            weight_terms(l + 1, 0, 5)

        wait_z(e)
        total = st1[e, 0]
        for zz in range(1, chips):
            total = total + st1[e, zz]
        send_m(e, total)

        @pl.when(k > 0)
        def _():
            weight_terms(l + 1, 5, TAPS)
            wait_halo(dh_halo, l + 1)

        @pl.when(k == 0)
        def _():
            pool()

        def edges(a, s):
            gradient(a, 0)
            gradient(a, band + 1)
            return s

        lax.fori_loop(0, maps_here, edges, 0)
        wait_m(e)
        total = st2[e, 0]
        for mm in range(1, PLANE):
            total = total + st2[e, mm]
        sums_own[pl.ds(l, 1), :] = jnp.sum(
            jnp.where(row8 >= maps_here, total, 0.0), 0, keepdims=True
        )
        sums_own[pl.ds(LAYERS + l, 1), :] = jnp.sum(
            jnp.where(row8 < maps_here, total, 0.0), 0, keepdims=True
        )
        plains = jnp.zeros((8, half), F32)
        crosses = jnp.zeros((8, half), F32)
        for a in range(maps_here):
            plain = jnp.zeros((8, half), F32)
            crossed = jnp.zeros((8, half), F32)
            for mm in range(PLANE):
                v = st2[e, mm]
                plain = plain + coef[a, mm] * v
                crossed = crossed + coef[a, mm] * pltpu.roll(v, 8 - maps_here, 0)
            count = cnt_t[a : a + 1, :]
            plain = gain * (jnp.sum(plain, 0, keepdims=True) / count)
            crossed = gain * (jnp.sum(crossed, 0, keepdims=True) / count)
            plains = jnp.where(row8 == a, plain, plains)
            crosses = jnp.where(row8 == a, crossed, crosses)
        tb_t[0] = plains
        ta_t[0] = crosses

        def settle(a, s):
            average, scaling = row_of(avg_t, l, a), row_of(scl_t, l, a)
            plain, crossed = row_of(tb_t, 0, a), row_of(ta_t, 0, a)
            for rr in range(band + 2):
                zhat = (zbuf[l, a, rr] - average) * scaling
                v = scaling * (dyb[a, rr] * gain - plain - zhat * crossed)
                v = jnp.where(column < limit(a, rr), v, 0.0)
                rounded = v.astype(BF16)
                dz_own[l, a, rr] = rounded
                if 0 < rr <= band:
                    at = pl.ds(pl.multiple_of((a * band + rr - 1) * PAD, PAD), PAD)
                    dz_t[1, at, :] = rounded
                    dz_t[0, at, :] = pltpu.roll(v, PAD - 1, 0).astype(BF16)
                    dz_t[2, at, :] = pltpu.roll(v, 1, 0).astype(BF16)
            return s

        lax.fori_loop(0, maps_here, settle, 0)
        dz_copy(l).start()
        products(dz_own, l, (2, 1, 0), wa, True, True)
        weight_copy(l, 2).wait()
        dz_copy(l).wait_recv()
        products(dz_oth, l, (2, 1, 0), wc, True, False)

        def gather(a, s):
            for rr in range(band):
                dh[l, a, 1 + rr] = shifted(a, rr, 2, 0)
            return s

        lax.fori_loop(0, maps_here, gather, 0)

        @pl.when(l > 0)
        def _():
            start_halo(dh_halo, l)

        return carry

    lax.fori_loop(0, LAYERS, backward, 0)
    weight_terms(0, 0, TAPS)

    def input_rows(a, s):
        for rr in range(band):
            igbuf[rr // 2, a, rr % 2] = jnp.where(
                column < width_of(a), dh[0, a, 1 + rr], 0.0
            )
        return s

    lax.fori_loop(0, maps_here, input_rows, 0)

    outs = (
        (
            remote(igbuf.at[other], ig_ref.at[c], out_s.at[0], out_r.at[0], m, z, other),
            pltpu.make_async_copy(igbuf.at[c], ig_ref.at[c], out_l.at[0]),
        ),
        (
            remote(pbuf.at[other], pooled_ref.at[c], out_s.at[1], out_r.at[1], m, z, other),
            pltpu.make_async_copy(pbuf.at[c], pooled_ref.at[c], out_l.at[1]),
        ),
        (
            remote(sums_own, sums_ref.at[c], out_s.at[2], out_r.at[2], m, z, other),
            pltpu.make_async_copy(sums_own, sums_ref.at[c], out_l.at[2]),
        ),
    )
    for there, here in outs:
        there.start()
        here.start()

    def within(q):
        return jnp.logical_and(q >= 0, q < UNITS)

    def drain(s, carry):
        @pl.when(within(s - 5 * LAG))
        def _():
            q = s - 5 * LAG
            ca(q).wait_recv()
            cp(q).start()

        @pl.when(within(s - 4 * LAG))
        def _():
            q = s - 4 * LAG
            cb(q).wait_recv()
            ca(q).start()

        @pl.when(within(s - 3 * LAG))
        def _():
            q = s - 3 * LAG

            def arrived(k):
                p = lax.rem(z + k, chips)

                @pl.when(p < owners)
                def _():
                    cz(q, p, p).wait_recv()

            each(1, chips, arrived)

            @pl.when(z < owners)
            def _():
                cl(q).wait()

            cb(q).start()

        @pl.when(within(s - 2 * LAG))
        def _():
            q = s - 2 * LAG

            @pl.when(z < owners)
            def _():
                total = r2[q, piece_rows(z)].astype(F32)
                for k in range(chips - 1):
                    remote(
                        r2.at[q, piece_rows(0)],
                        r3.at[q, k],
                        r3_s.at[q, 0],
                        r3_r.at[q, k],
                        m,
                        z,
                        c,
                    ).wait_recv()
                for k in range(chips - 1):
                    total = total + r3[q, k].astype(F32)
                fin[q] = total.astype(BF16)
                each(1, chips, lambda k: cz(q, z, lax.rem(z + k, chips)).start())
                cl(q).start()

        @pl.when(within(s - 1 * LAG))
        def _():
            q = s - 1 * LAG
            _, _, _, bit = order(q)
            c2(q).wait_recv()
            r2[q] = (r2[q].astype(F32) + r1[q, second_rows(bit)].astype(F32)).astype(BF16)

            def give(k):
                p = lax.rem(z + k, chips)

                @pl.when(p < owners)
                def _():
                    c3(q, p).start()

            each(1, chips, give)

        @pl.when(within(s))
        def _():
            q = s
            _, bit, _, _ = order(q)
            c1(q).wait_recv()
            r1[q] = (r1[q].astype(F32) + terms[q, bit].astype(F32)).astype(BF16)
            c2(q).start()

        return carry

    lax.fori_loop(0, UNITS + 5 * LAG, drain, 0)

    def finish(q, carry):
        cp(q).wait()
        ca(q).wait_send()
        cb(q).wait_send()
        c1(q).wait_send()
        c2(q).wait_send()

        def given(k):
            p = lax.rem(z + k, chips)

            @pl.when(p < owners)
            def _():
                c3(q, p).wait_send()

        each(1, chips, given)

        @pl.when(z < owners)
        def _():
            each(1, chips, lambda k: cz(q, z, lax.rem(z + k, chips)).wait_send())

        return carry

    lax.fori_loop(0, UNITS, finish, 0)
    for l in range(1, LAYERS):
        act_copy(l).wait_send()
    for l in range(LAYERS):
        dz_copy(l).wait_send()
    for there, here in outs:
        there.wait()
        here.wait()


def solution(mesh):
    chips = mesh.shape["rows"] // 2

    def per_device(
        block_input,
        conv_weights,
        norm_gains,
        norm_shifts,
        map_width,
        map_group,
        pool_index,
        task_mask,
        task_weights,
        task_grads,
    ):
        maps_here, rows_here, columns, channels = block_input.shape
        pooled_columns = pool_index.shape[2]
        height = rows_here * mesh.shape["rows"]
        half = channels // 2
        band = 2 * rows_here
        pixels = maps_here * band * PAD
        owners = min(chips, 8)
        piece = half // 2 // owners
        rounds = 2 * LAYERS
        vmem, dma = pltpu.VMEM, pltpu.SemaphoreType.DMA
        tile = (maps_here, band + 2, PAD, half)
        whole = pl.BlockSpec(memory_space=pltpu.VMEM)
        scalars = pl.BlockSpec(memory_space=pltpu.SMEM)
        anywhere = pl.BlockSpec(memory_space=pl.ANY)
        pooled, ig, kg, sums = pl.pallas_call(
            functools.partial(block_kernel, chips, height),
            out_shape=(
                jax.ShapeDtypeStruct((2, maps_here, PAD // 2, half), BF16),
                jax.ShapeDtypeStruct((2, maps_here, rows_here, PAD, half), F32),
                jax.ShapeDtypeStruct((UNITS, channels, channels), BF16),
                jax.ShapeDtypeStruct((2, 8, half), F32),
            ),
            in_specs=[whole, anywhere, whole, whole, scalars, scalars, whole, scalars, scalars, whole],
            out_specs=[anywhere] * 4,
            scratch_shapes=[
                vmem((LAYERS, 3, 3, half, half), BF16),
                vmem((LAYERS, 3, 3, half, half), BF16),
                vmem((LAYERS, 3, 3, half, half), BF16),
                vmem((LAYERS + 1,) + tile, BF16),
                vmem((LAYERS,) + tile, BF16),
                vmem((LAYERS, 3, 2, half, pixels), BF16),
                vmem((LAYERS,) + tile, F32),
                vmem((LAYERS + 1,) + tile, F32),
                vmem(tile, F32),
                vmem((LAYERS,) + tile, BF16),
                vmem((LAYERS,) + tile, BF16),
                vmem((3, pixels, half), BF16),
                vmem((3, pixels, half), F32),
                vmem((2, 2, maps_here, PAD // 2, half), F32),
                vmem((4, 2, maps_here, PAD // 2, half), F32),
                vmem((half // 128, PAD, 128), F32),
                vmem((2, maps_here, PAD // 2, half), BF16),
                vmem((2, maps_here, rows_here, PAD, half), F32),
                vmem((rounds, chips, 8, half), F32),
                vmem((rounds, PLANE, 8, half), F32),
                vmem((maps_here, PLANE, 8, half), F32),
                vmem((PLANE, 8, half), F32),
                vmem((2, 8, half), F32),
                vmem((8, half), F32),
                vmem((LAYERS, 8, half), F32),
                vmem((LAYERS, 8, half), F32),
                vmem((1, 8, half), F32),
                vmem((1, 8, half), F32),
                vmem((8, half), F32),
                vmem((UNITS, 2, half, half), BF16),
                vmem((UNITS, half, half), BF16),
                vmem((UNITS, half // 2, half), BF16),
                vmem((UNITS, chips - 1, piece, half), BF16),
                vmem((UNITS, piece, half), BF16),
                dma((LAYERS, 3)),
                dma((6,)),
                dma((6,)),
                dma((3,)),
                dma((3,)),
                dma((rounds, chips)),
                dma((rounds, chips)),
                dma((rounds, PLANE)),
                dma((rounds, PLANE)),
                dma((LAYERS, 2)),
                dma((LAYERS, 2)),
                dma((LAYERS, 2)),
                dma((LAYERS, 2)),
                dma((LAYERS,)),
                dma((LAYERS,)),
                dma((LAYERS,)),
                dma((LAYERS,)),
                dma((3,)),
                dma((3,)),
                dma((3,)),
                dma((UNITS,)),
                dma((UNITS,)),
                dma((UNITS,)),
                dma((UNITS,)),
                dma((UNITS, owners)),
                dma((UNITS, chips - 1)),
                dma((UNITS, chips)),
                dma((UNITS, owners)),
                dma((UNITS,)),
                dma((UNITS,)),
                dma((UNITS,)),
                dma((UNITS,)),
                dma((UNITS,)),
                dma((UNITS,)),
                dma((UNITS,)),
            ],
            compiler_params=pltpu.CompilerParams(
                collective_id=0,
                has_side_effects=True,
                vmem_limit_bytes=63 * 1024 * 1024,
            ),
        )(
            block_input,
            conv_weights,
            norm_gains,
            norm_shifts,
            map_width,
            map_group,
            pool_index,
            task_mask,
            task_weights,
            task_grads,
        )
        pooled = jnp.concatenate([pooled[0], pooled[1]], -1)[:, None, :pooled_columns]
        input_grad = jnp.concatenate([ig[0], ig[1]], -1)[:, :, :columns]
        sums = jnp.concatenate([sums[0], sums[1]], -1)
        return (
            pooled,
            input_grad,
            kg.astype(F32).reshape(conv_weights.shape),
            sums[:LAYERS],
            sums[LAYERS : 2 * LAYERS],
        )

    return jax.shard_map(
        per_device,
        mesh=mesh,
        in_specs=(
            P("maps", "rows", None, None),
            P(),
            P(),
            P(),
            P(),
            P(),
            P("maps", "rows", None, None),
            P("maps", None),
            P(),
            P(None, "maps", "rows", None, None),
        ),
        out_specs=(P("maps", "rows", None, None), P("maps", "rows", None, None), P(), P(), P()),
        check_vma=False,
    )
```

```python
import functools

import jax
import jax.numpy as jnp
from jax import lax
from jax.experimental import pallas as pl
from jax.experimental.pallas import tpu as pltpu
from jax.sharding import PartitionSpec as P

MESH = pl.DeviceIdType.MESH
epsilon = 1e-05
PAD = 64
LAYERS = 3
TAPS = 9
UNITS = LAYERS * TAPS
PLANE = 4
LAG = 2
F32 = jnp.float32
BF16 = jnp.bfloat16


def each(first, last, body):
    if last - first <= 8:
        for k in range(first, last):
            body(k)
    else:
        lax.fori_loop(first, last, lambda k, s: (body(k), s)[1], 0)


def block_kernel(
    chips,
    height,
    x_ref,
    w_ref,
    gain_ref,
    shift_ref,
    width_ref,
    group_ref,
    index_ref,
    tmask_ref,
    tweight_ref,
    tgrad_ref,
    pooled_ref,
    ig_ref,
    kg_ref,
    sums_ref,
    wa,
    wb,
    wc,
    act_own,
    act_oth,
    at,
    zbuf,
    dh,
    dyb,
    dz_own,
    dz_oth,
    dzs,
    dzv,
    prod,
    gsrc,
    gbuf,
    hrow,
    pbuf,
    igbuf,
    st1,
    st2,
    coef,
    nall,
    inv_t,
    cnt_t,
    avg_t,
    scl_t,
    tb_t,
    ta_t,
    sums_own,
    terms,
    r3,
    fin,
    w_sem,
    x_s,
    x_r,
    g_s,
    g_r,
    st1_s,
    st1_r,
    st2_s,
    st2_r,
    zh_s,
    zh_r,
    dh_s,
    dh_r,
    act_s,
    act_r,
    dz_s,
    dz_r,
    out_s,
    out_r,
    out_l,
    at_s,
    at_r,
    dzs_s,
    dzs_r,
    r3_s,
    r3_r,
    az_s,
    az_r,
    ab_s,
    ab_r,
    aa_s,
    aa_r,
    ap_s,
    ap_r,
    loc_s,
):
    maps_here = x_ref.shape[0]
    columns = x_ref.shape[2]
    half = x_ref.shape[3] // 2
    tasks = tgrad_ref.shape[0]
    pooled_columns = tgrad_ref.shape[3]
    lanes = half // 128
    tiles = [slice(n * 128, (n + 1) * 128) for n in range(lanes)]
    band = 4
    pixels = maps_here * band * PAD
    owners = min(chips, 8)
    piece = half // owners
    slice_lanes = 2 * half // PLANE
    m = lax.axis_index("maps")
    r = lax.axis_index("rows")
    c = lax.rem(r, 2)
    z = lax.div(r, 2)
    other = 1 - c
    first_map = m * maps_here
    x_peer = m + 1 - 2 * lax.rem(m, 2)
    y_peer = m + 2 - 4 * lax.div(m, 2)
    up_there = z > 0
    down_there = z < chips - 1
    row8 = lax.broadcasted_iota(jnp.int32, (8, half), 0)
    column = lax.broadcasted_iota(jnp.int32, (PAD, half), 0)

    def remote(src, dst, send, recv, mm, zz, cc):
        return pltpu.make_async_remote_copy(
            src_ref=src,
            dst_ref=dst,
            send_sem=send,
            recv_sem=recv,
            device_id=(mm, zz * 2 + cc),
            device_id_type=MESH,
        )

    def own_half(v):
        return jnp.where(c == 0, v[..., :half], v[..., half:])

    def width_of(a):
        return width_ref[first_map + a]

    own_at = pl.ds(pl.multiple_of(c * half, half), half)
    oth_at = pl.ds(pl.multiple_of(other * half, half), half)

    def weight_copy(l, n):
        dst = (wa, wb, wc)[n]
        k_at, o_at = ((own_at, own_at), (oth_at, own_at), (own_at, oth_at))[n]
        return pltpu.make_async_copy(w_ref.at[l, :, :, k_at, o_at], dst.at[l], w_sem.at[l, n])

    for l in range(LAYERS):
        weight_copy(l, 0).start()
        weight_copy(l, 1).start()
    for l in range(LAYERS):
        weight_copy(LAYERS - 1 - l, 2).start()

    barrier = pltpu.get_barrier_semaphore()

    def greet(k):
        rr = lax.rem(r + k, 2 * chips)
        pl.semaphore_signal(barrier, inc=1, device_id=(m, rr), device_id_type=MESH)

    each(1, 2 * chips, greet)
    for k in range(1, PLANE):
        pl.semaphore_signal(
            barrier, inc=1, device_id=(lax.rem(m + k, PLANE), r), device_id_type=MESH
        )

    mine = pl.ds(1 + 2 * c, 2)
    for a in range(maps_here):
        inside = lax.broadcasted_iota(jnp.int32, (columns, 2 * half), 0) < width_of(a)
        for rr in range(2):
            v = jnp.where(inside, x_ref[a, rr].astype(F32), 0.0).astype(BF16)
            spot = 1 + 2 * c + rr
            act_own[0, a, spot, pl.ds(48, 16), :] = jnp.zeros((16, half), BF16)
            act_oth[0, a, spot, pl.ds(48, 16), :] = jnp.zeros((16, half), BF16)
            act_own[0, a, spot, pl.ds(0, columns), :] = own_half(v)
            act_oth[0, a, spot, pl.ds(0, columns), :] = jnp.where(
                c == 0, v[:, half:], v[:, :half]
            )

    @pl.when(z == 0)
    def _():
        act_own[0, :, 0] = jnp.zeros((maps_here, PAD, half), BF16)
        act_oth[0, :, 0] = jnp.zeros((maps_here, PAD, half), BF16)

    @pl.when(z == chips - 1)
    def _():
        act_own[0, :, 5] = jnp.zeros((maps_here, PAD, half), BF16)
        act_oth[0, :, 5] = jnp.zeros((maps_here, PAD, half), BF16)

    gsrc[...] = jnp.zeros(gsrc.shape, F32)
    for a in range(maps_here):
        total = None
        for t in range(tasks):
            scale = tweight_ref[t] * tmask_ref[a, t].astype(F32)
            term = tgrad_ref[t, a, 0].astype(F32) * scale
            total = term if total is None else total + term
        position = index_ref[a, 0].astype(F32)
        for h in range(2):
            gsrc[h, 0, a, pl.ds(0, pooled_columns), :] = total[:, h * half : (h + 1) * half]
            gsrc[h, 1, a, pl.ds(0, pooled_columns), :] = position[:, h * half : (h + 1) * half]
    gbuf[1 + c] = gsrc[c]

    pl.semaphore_wait(barrier, 2 * chips - 1 + PLANE - 1)

    x_partner = (
        remote(act_own.at[0, :, mine], act_oth.at[0, :, mine], x_s.at[0], x_r.at[0], m, z, other),
        remote(act_oth.at[0, :, mine], act_own.at[0, :, mine], x_s.at[1], x_r.at[1], m, z, other),
    )
    g_partner = remote(gsrc.at[other], gbuf.at[1 + c], g_s.at[0], g_r.at[0], m, z, other)

    def x_halo(n, src_row, dst_row, zz):
        cc = (c, c, other, other, c, other)[n]
        low = dst_row == band + 1
        if n >= 4:
            src, dst = gsrc.at[cc], gbuf.at[3 if low else 0]
            return remote(src, dst, g_s.at[n - 3], g_r.at[1 if low else 2], m, zz, cc)
        src = (act_own, act_oth, act_own, act_oth)[n].at[0, :, src_row]
        dst = (act_own, act_oth, act_oth, act_own)[n].at[0, :, dst_row]
        return remote(src, dst, x_s.at[2 + n], x_r.at[(2 if low else 4) + n % 2], m, zz, cc)

    for copy in x_partner:
        copy.start()

    @pl.when(jnp.logical_and(c == 0, up_there))
    def _():
        for n in range(6):
            x_halo(n, 1, 5, z - 1).start()

    @pl.when(jnp.logical_and(c == 1, down_there))
    def _():
        for n in range(6):
            x_halo(n, 4, 0, z + 1).start()

    g_partner.start()

    for mm in range(PLANE):
        sizes = jnp.zeros((8, half), F32)
        for b in range(maps_here):
            sizes = jnp.where(
                row8 == b, (width_ref[mm * maps_here + b] * height).astype(F32), sizes
            )
        nall[mm] = sizes
    inside_sizes = jnp.zeros((8, half), F32)
    for b in range(maps_here):
        inside_sizes = jnp.where(row8 == b, (width_of(b) * band).astype(F32), inside_sizes)
    inv_t[0] = inside_sizes
    inv_t[1] = jnp.where(row8 < maps_here, 1.0 / jnp.maximum(inside_sizes, 1.0), 0.0)
    counts = jnp.ones((8, half), F32)
    for a in range(maps_here):
        total = jnp.zeros((1, half), F32)
        for mm in range(PLANE):
            same = jnp.zeros((8, half), F32)
            for b in range(maps_here):
                alike = group_ref[first_map + a] == group_ref[mm * maps_here + b]
                same = jnp.where(row8 == b, jnp.where(alike, 1.0, 0.0), same)
            coef[a, mm] = same
            total = total + jnp.sum(same * nall[mm], 0, keepdims=True)
        counts = jnp.where(row8 == a, total, counts)
    cnt_t[...] = counts

    def z_copy(e, k):
        zz = lax.rem(z + k, chips)
        return remote(st1.at[e, z], st1.at[e, z], st1_s.at[e, k], st1_r.at[e, z], m, zz, c)

    def z_arrival(e, k):
        zz = lax.rem(z + k, chips)
        return remote(st1.at[e, zz], st1.at[e, zz], st1_s.at[e, k], st1_r.at[e, zz], m, zz, c)

    def m_copy(e, k):
        mm = lax.rem(m + k, PLANE)
        return remote(st2.at[e, m], st2.at[e, m], st2_s.at[e, k], st2_r.at[e, m], mm, z, c)

    def m_arrival(e, k):
        mm = lax.rem(m + k, PLANE)
        return remote(st2.at[e, mm], st2.at[e, mm], st2_s.at[e, k], st2_r.at[e, mm], mm, z, c)

    def send_z(e, tile):
        st1[e, z] = tile
        each(1, chips, lambda k: z_copy(e, k).start())

    def wait_z(e):
        each(1, chips, lambda k: z_arrival(e, k).wait_recv())
        each(1, chips, lambda k: z_copy(e, k).wait_send())

    def send_m(e, tile):
        st2[e, m] = tile
        each(1, PLANE, lambda k: m_copy(e, k).start())

    def wait_m(e):
        each(1, PLANE, lambda k: m_arrival(e, k).wait_recv())
        each(1, PLANE, lambda k: m_copy(e, k).wait_send())

    def products(source, l, starts, kernel, transposed, fresh):
        parts = [
            source[l, :, s : s + band].reshape(pixels, half) for s in starts
        ]
        lhs = jnp.concatenate(parts, 1)
        for j in range(3):
            if transposed:
                rhs = jnp.concatenate([kernel[l, i, j] for i in range(3)], 1)
                got = lax.dot_general(
                    lhs, rhs, (((1,), (1,)), ((), ())), preferred_element_type=F32
                )
            else:
                rhs = kernel[l, :, j].reshape(3 * half, half)
                got = jnp.dot(lhs, rhs, preferred_element_type=F32)
            if fresh:
                prod[j] = got
            else:
                prod[j] = prod[j] + got

    def shifted(a, rr, before, behind, n):
        rows = pl.ds(pl.multiple_of((a * band + rr) * PAD, PAD), PAD)
        return (
            prod[1, rows, n]
            + pltpu.roll(prod[before, rows, n], 1, 0)
            + pltpu.roll(prod[behind, rows, n], PAD - 1, 0)
        )

    def row_of(table, l, a):
        return table[l, pl.ds(a, 1), :]

    def gain_of(l):
        return own_half(gain_ref[pl.ds(l, 1), :])

    def shift_of(l):
        return own_half(shift_ref[pl.ds(l, 1), :])

    def limit(a, rr):
        w = width_of(a)
        if rr == 0:
            return jnp.where(up_there, w, 0)
        if rr == band + 1:
            return jnp.where(down_there, w, 0)
        return w

    def z_halo(l, way):
        if way == 0:
            return remote(zbuf.at[l, :, 1], zbuf.at[l, :, 5], zh_s.at[l, 0], zh_r.at[l, 0], m, z - 1, c)
        return remote(zbuf.at[l, :, 4], zbuf.at[l, :, 0], zh_s.at[l, 1], zh_r.at[l, 1], m, z + 1, c)

    def dh_halo(l, way):
        if way == 0:
            return remote(dh.at[l, :, 1], dh.at[l, :, 5], dh_s.at[l, 0], dh_r.at[l, 0], m, z - 1, c)
        return remote(dh.at[l, :, 4], dh.at[l, :, 0], dh_s.at[l, 1], dh_r.at[l, 1], m, z + 1, c)

    def start_halo(halo, l):
        @pl.when(up_there)
        def _():
            halo(l, 0).start()

        @pl.when(down_there)
        def _():
            halo(l, 1).start()

    def wait_halo(halo, l):
        @pl.when(up_there)
        def _():
            halo(l, 1).wait_recv()
            halo(l, 0).wait_send()

        @pl.when(down_there)
        def _():
            halo(l, 0).wait_recv()
            halo(l, 1).wait_send()

    def act_copy(l):
        return remote(act_own.at[l], act_oth.at[l], act_s.at[l], act_r.at[l], m, z, other)

    def at_copy(l, k):
        mm = lax.rem(m + k, PLANE)
        return remote(at.at[l, m], at.at[l, m], at_s.at[l, k], at_r.at[l, m], mm, z, c)

    def at_arrival(l, k):
        mm = lax.rem(m + k, PLANE)
        return remote(at.at[l, mm], at.at[l, mm], at_s.at[l, k], at_r.at[l, mm], mm, z, c)

    per_half = half // slice_lanes

    def slice_at(mm):
        first = lax.rem(mm, per_half) * slice_lanes
        return pl.ds(pl.multiple_of(first, slice_lanes), slice_lanes)

    def dzs_copy(l, k, source):
        mm = lax.rem(m + k, PLANE)
        src = source.at[l, :, :, :, slice_at(mm)]
        return remote(src, dzs.at[l, m], dzs_s.at[l, k], dzs_r.at[l, m], mm, z, c)

    def dzs_arrival(l, k):
        mm = lax.rem(m + k, PLANE)
        return remote(dzs.at[l, mm], dzs.at[l, mm], dzs_s.at[l, k], dzs_r.at[l, mm], mm, z, c)

    def send_slices(l, source, core):
        for k in range(PLANE):
            mm = lax.rem(m + k, PLANE)

            @pl.when(lax.div(mm, per_half) == core)
            def _(k=k, mm=mm):
                if k:
                    dzs_copy(l, k, source).start()
                else:
                    for a in range(maps_here):
                        dzs[l, m, a] = source[l, a, :, :, slice_at(mm)]

    def dz_copy(l):
        return remote(dz_own.at[l], dz_oth.at[l], dz_s.at[l], dz_r.at[l], m, z, other)

    for copy in x_partner:
        copy.wait()

    @pl.when(up_there)
    def _():
        for n in (0, 1, 4):
            x_halo(n, 4, 0, z - 1).wait_recv()

    @pl.when(down_there)
    def _():
        for n in (0, 1, 4):
            x_halo(n, 1, 5, z + 1).wait_recv()

    @pl.when(jnp.logical_and(c == 0, up_there))
    def _():
        for n in range(6):
            x_halo(n, 1, 5, z - 1).wait_send()

    @pl.when(jnp.logical_and(c == 1, down_there))
    def _():
        for n in range(6):
            x_halo(n, 4, 0, z + 1).wait_send()

    g_partner.wait()

    def forward(l, carry):
        weight_copy(l, 0).wait()
        products(act_own, l, (0, 1, 2), wa, False, True)
        weight_copy(l, 1).wait()

        @pl.when(l > 0)
        def _():
            act_copy(l).wait_recv()

        products(act_oth, l, (0, 1, 2), wb, False, False)

        def collect(a, tile):
            inside = column[:, :128] < width_of(a)
            pixels_inside = (width_of(a) * band).astype(F32)
            totals, squares = [], []
            for n in tiles:
                total = jnp.zeros((PAD, 128), F32)
                for rr in range(band):
                    v = shifted(a, rr, 0, 2, n)
                    zbuf[l, a, 1 + rr, :, n] = v
                    total = total + jnp.where(inside, v, 0.0)
                total = jnp.sum(total, 0, keepdims=True)
                mean = total / pixels_inside
                square = jnp.zeros((PAD, 128), F32)
                for rr in range(band):
                    v = jnp.where(inside, zbuf[l, a, 1 + rr, :, n] - mean, 0.0)
                    square = square + v * v
                totals.append(total)
                squares.append(jnp.sum(square, 0, keepdims=True))
            tile = jnp.where(row8 == a, jnp.concatenate(totals, 1), tile)
            return jnp.where(row8 == a + maps_here, jnp.concatenate(squares, 1), tile)

        tile = lax.fori_loop(0, maps_here, collect, jnp.zeros((8, half), F32))
        send_z(l, tile)
        start_halo(z_halo, l)
        at[l, m] = act_own[l, :, 1 : 1 + band].reshape(pixels, half).T
        wait_z(l)
        sizes, inverse = inv_t[0], inv_t[1]
        total = st1[l, 0]
        for zz in range(1, chips):
            total = total + st1[l, zz]
        mean = total * inverse * (1.0 / chips)
        square = jnp.zeros((8, half), F32)
        for zz in range(chips):
            v = st1[l, zz]
            gap = v * inverse - mean
            square = square + pltpu.roll(v, 8 - maps_here, 0) + sizes * gap * gap
        tile = jnp.where(row8 < maps_here, mean, pltpu.roll(square, maps_here, 0))
        send_m(l, jnp.where(row8 < 2 * maps_here, tile, 0.0))
        wait_m(l)
        each(1, PLANE, lambda k: at_copy(l, k).start())
        averages = jnp.zeros((8, half), F32)
        scalings = jnp.zeros((8, half), F32)
        for a in range(maps_here):
            count = cnt_t[a : a + 1, :]
            average = jnp.zeros((8, half), F32)
            for mm in range(PLANE):
                average = average + coef[a, mm] * nall[mm] * st2[l, mm]
            average = jnp.sum(average, 0, keepdims=True) / count
            variance = jnp.zeros((8, half), F32)
            for mm in range(PLANE):
                v = st2[l, mm]
                gap = v - average
                variance = variance + coef[a, mm] * (
                    pltpu.roll(v, 8 - maps_here, 0) + nall[mm] * gap * gap
                )
            variance = jnp.sum(variance, 0, keepdims=True) / count
            averages = jnp.where(row8 == a, average, averages)
            scalings = jnp.where(row8 == a, lax.rsqrt(variance + epsilon), scalings)
        avg_t[l] = averages
        scl_t[l] = scalings
        wait_halo(z_halo, l)

        def activate(a, s):
            gain, shift = gain_of(l), shift_of(l)
            for n in tiles:
                average = row_of(avg_t, l, a)[:, n]
                factor = row_of(scl_t, l, a)[:, n] * gain[:, n]
                for rr in range(band + 2):
                    y = (zbuf[l, a, rr, :, n] - average) * factor + shift[:, n]
                    h = jnp.where(column[:, n] < limit(a, rr), y * jax.nn.sigmoid(y), 0.0)
                    act_own[l + 1, a, rr, :, n] = h.astype(BF16)
            return s

        lax.fori_loop(0, maps_here, activate, 0)

        @pl.when(l < LAYERS - 1)
        def _():
            act_copy(l + 1).start()

        return carry

    lax.fori_loop(0, LAYERS, forward, 0)

    def unpool(a, s):
        for rr in range(band + 2):
            slot, lower = (rr + 1) // 2, (rr + 1) % 2
            g = gbuf[slot, 0, a]
            position = gbuf[slot, 1, a]
            for b in range(2):
                v = jnp.where(position == float(2 * lower + b), g, 0.0)
                for n in range(lanes):
                    hrow[n, pl.ds(b, PAD // 2, stride=2), :] = v[:, n * 128 : (n + 1) * 128]
            dh[LAYERS, a, rr] = jnp.concatenate([hrow[n] for n in range(lanes)], 1)
        return s

    lax.fori_loop(0, maps_here, unpool, 0)

    def pool():
        def one(a, s):
            for pr in range(2):
                total = jnp.zeros((PAD // 2, half), F32)
                position = gbuf[1 + pr, 1, a]
                for lower in range(2):
                    v = act_own[LAYERS, a, 1 + 2 * pr + lower].astype(F32)
                    for n in range(lanes):
                        hrow[n] = v[:, n * 128 : (n + 1) * 128]
                    for b in range(2):
                        v = jnp.concatenate(
                            [hrow[n, pl.ds(b, PAD // 2, stride=2), :] for n in range(lanes)], 1
                        )
                        total = total + jnp.where(position == float(2 * lower + b), v, 0.0)
                pbuf[pr, a] = total.astype(BF16)
            return s

        lax.fori_loop(0, maps_here, one, 0)

    def piece_rows(p):
        return pl.ds(pl.multiple_of(p * piece, piece), piece)

    def c3(q, p):
        slot = lax.rem(z - p + chips - 1, chips)
        return remote(
            terms.at[q, piece_rows(p)], r3.at[q, slot], r3_s.at[q, p], r3_r.at[q, slot], m, p, c
        )

    def unit_of(q):
        k = lax.div(q, TAPS)
        return (LAYERS - 1 - k) * TAPS + (q - k * TAPS)

    def region(q, start, size, mm, lanes=slice_lanes):
        start = pl.multiple_of(c * half + start, piece)
        first = pl.multiple_of(mm * slice_lanes, slice_lanes)
        return kg_ref.at[unit_of(q), pl.ds(start, size), pl.ds(first, lanes)]

    def order(q):
        swap = lax.rem(q, 2)
        keep = 1 - swap
        return keep * x_peer + swap * y_peer, keep * y_peer + swap * x_peer

    def cz(q, p, zz):
        part = region(q, p * piece, piece, m)
        return remote(fin.at[q], part, az_s.at[q, zz], az_r.at[q, p], m, zz, c)

    def cl(q):
        return pltpu.make_async_copy(fin.at[q], region(q, z * piece, piece, m), loc_s.at[q])

    def ca(q):
        part = region(q, 0, half, m)
        return remote(part, part, aa_s.at[q], aa_r.at[q], order(q)[0], z, c)

    def cb(q, n):
        first, second = order(q)
        part = region(q, 0, half, first if n else m)
        return remote(part, part, ab_s.at[q, n], ab_r.at[q, n], second, z, c)

    def cp(q):
        part = region(q, 0, half, 0, 2 * half)
        return remote(part, part, ap_s.at[q], ap_r.at[q], m, z, other)

    def variants(l):
        def one(n, s):
            chip = lax.div(n, maps_here)
            a = n - chip * maps_here
            for rr in range(band + 2):
                v = dzs[l, chip, a, rr]
                dzv[1, chip, a, rr] = v
                v = v.astype(F32)
                dzv[0, chip, a, rr] = pltpu.roll(v, PAD - 1, 0).astype(BF16)
                dzv[2, chip, a, rr] = pltpu.roll(v, 1, 0).astype(BF16)
            return s

        lax.fori_loop(0, PLANE * maps_here, one, 0)

    def weight_terms(l):
        each(1, PLANE, lambda k: at_arrival(l, k).wait_recv())
        each(1, PLANE, lambda k: dzs_arrival(l, k).wait_recv())
        variants(l)
        first = (LAYERS - 1 - l) * TAPS

        def shifted_slices(t):
            i = lax.div(t, 3)
            j = t - 3 * i
            return dzv[j, :, :, pl.ds(2 - i, band)].reshape(PLANE * pixels, slice_lanes)

        def times(rhs):
            lhs = jnp.concatenate([at[l, chip] for chip in range(PLANE)], 1)
            return jnp.dot(lhs, rhs, preferred_element_type=F32).astype(BF16)

        def give(q):
            def to(k):
                p = lax.rem(z + k, chips)

                @pl.when(p < owners)
                def _():
                    c3(q, p).start()

            each(1, chips, to)

        def pair(g, s):
            t = 2 * g
            got = times(jnp.concatenate([shifted_slices(t), shifted_slices(t + 1)], 1))
            terms[first + t] = got[:, :slice_lanes]
            terms[first + t + 1] = got[:, slice_lanes:]
            give(first + t)
            give(first + t + 1)
            return s

        lax.fori_loop(0, TAPS // 2, pair, 0)
        terms[first + TAPS - 1] = times(shifted_slices(TAPS - 1))
        give(first + TAPS - 1)

    def stage_sum(q):
        @pl.when(z < owners)
        def _():
            for k in range(chips - 1):
                remote(
                    r3.at[q, k], r3.at[q, k], r3_s.at[q, 0], r3_r.at[q, k], m, z, c
                ).wait_recv()
            total = terms[q, piece_rows(z)].astype(F32)
            for k in range(chips - 1):
                total = total + r3[q, k].astype(F32)
            fin[q] = total.astype(BF16)
            each(1, chips, lambda k: cz(q, z, lax.rem(z + k, chips)).start())
            cl(q).start()

    def stage_plane(q):
        def arrived(k):
            p = lax.rem(z + k, chips)

            @pl.when(p < owners)
            def _():
                cz(q, p, p).wait_recv()

        each(1, chips, arrived)

        @pl.when(z < owners)
        def _():
            cl(q).wait()

        ca(q).start()
        cb(q, 0).start()

    def stage_second(q):
        ca(q).wait_recv()
        cb(q, 1).start()

    def stage_chip(q):
        cb(q, 0).wait_recv()
        cb(q, 1).wait_recv()
        cp(q).start()

    def run(stage, first, last):
        lax.fori_loop(first, last, lambda q, s: (stage(q), s)[1], 0)

    def backward(k, carry):
        l = LAYERS - 1 - k
        gain, shift = gain_of(l), shift_of(l)

        def gradient(a, rr, n):
            zhat = (zbuf[l, a, rr, :, n] - row_of(avg_t, l, a)[:, n]) * row_of(scl_t, l, a)[:, n]
            y = zhat * gain[:, n] + shift[:, n]
            s = jax.nn.sigmoid(y)
            dy = dh[l + 1, a, rr, :, n] * (s * (1.0 + y * (1.0 - s)))
            dy = jnp.where(column[:, n] < limit(a, rr), dy, 0.0)
            dyb[a, rr, :, n] = dy
            return dy, zhat

        def collect(a, tile):
            plains, crosses = [], []
            for n in tiles:
                plain = jnp.zeros((PAD, 128), F32)
                crossed = jnp.zeros((PAD, 128), F32)
                for rr in range(1, band + 1):
                    dy, zhat = gradient(a, rr, n)
                    plain = plain + dy
                    crossed = crossed + dy * zhat
                plains.append(jnp.sum(plain, 0, keepdims=True))
                crosses.append(jnp.sum(crossed, 0, keepdims=True))
            tile = jnp.where(row8 == a, jnp.concatenate(plains, 1), tile)
            return jnp.where(row8 == a + maps_here, jnp.concatenate(crosses, 1), tile)

        e = LAYERS + l
        tile = lax.fori_loop(0, maps_here, collect, jnp.zeros((8, half), F32))
        send_z(e, tile)

        @pl.when(k == LAYERS - 1)
        def _():
            run(stage_sum, 0, TAPS)

        wait_z(e)
        total = st1[e, 0]
        for zz in range(1, chips):
            total = total + st1[e, zz]
        send_m(e, total)

        @pl.when(k > 0)
        def _():
            weight_terms(l + 1)
            wait_halo(dh_halo, l + 1)

        @pl.when(k == 0)
        def _():
            pool()

        def edges(a, s):
            for n in tiles:
                gradient(a, 0, n)
                gradient(a, band + 1, n)
            return s

        lax.fori_loop(0, maps_here, edges, 0)
        wait_m(e)
        total = st2[e, 0]
        for mm in range(1, PLANE):
            total = total + st2[e, mm]
        sums_own[pl.ds(l, 1), :] = jnp.sum(
            jnp.where(row8 >= maps_here, total, 0.0), 0, keepdims=True
        )
        sums_own[pl.ds(LAYERS + l, 1), :] = jnp.sum(
            jnp.where(row8 < maps_here, total, 0.0), 0, keepdims=True
        )
        plains = jnp.zeros((8, half), F32)
        crosses = jnp.zeros((8, half), F32)
        for a in range(maps_here):
            plain = jnp.zeros((8, half), F32)
            crossed = jnp.zeros((8, half), F32)
            for mm in range(PLANE):
                v = st2[e, mm]
                plain = plain + coef[a, mm] * v
                crossed = crossed + coef[a, mm] * pltpu.roll(v, 8 - maps_here, 0)
            count = cnt_t[a : a + 1, :]
            plain = gain * (jnp.sum(plain, 0, keepdims=True) / count)
            crossed = gain * (jnp.sum(crossed, 0, keepdims=True) / count)
            plains = jnp.where(row8 == a, plain, plains)
            crosses = jnp.where(row8 == a, crossed, crosses)
        tb_t[0] = plains
        ta_t[0] = crosses

        def settle(a, s):
            for n in tiles:
                average, scaling = row_of(avg_t, l, a)[:, n], row_of(scl_t, l, a)[:, n]
                plain, crossed = row_of(tb_t, 0, a)[:, n], row_of(ta_t, 0, a)[:, n]
                for rr in range(band + 2):
                    zhat = (zbuf[l, a, rr, :, n] - average) * scaling
                    v = scaling * (dyb[a, rr, :, n] * gain[:, n] - plain - zhat * crossed)
                    v = jnp.where(column[:, n] < limit(a, rr), v, 0.0)
                    dz_own[l, a, rr, :, n] = v.astype(BF16)
            return s

        lax.fori_loop(0, maps_here, settle, 0)
        dz_copy(l).start()
        send_slices(l, dz_own, c)
        products(dz_own, l, (2, 1, 0), wa, True, True)
        weight_copy(l, 2).wait()
        dz_copy(l).wait_recv()
        send_slices(l, dz_oth, other)
        products(dz_oth, l, (2, 1, 0), wc, True, False)

        def gather(a, s):
            for n in tiles:
                for rr in range(band):
                    dh[l, a, 1 + rr, :, n] = shifted(a, rr, 2, 0, n)
            return s

        lax.fori_loop(0, maps_here, gather, 0)

        @pl.when(l > 0)
        def _():
            start_halo(dh_halo, l)

        return carry

    lax.fori_loop(0, LAYERS, backward, 0)
    run(stage_plane, 0, TAPS)

    def input_rows(a, s):
        for rr in range(band):
            igbuf[rr // 2, a, rr % 2] = jnp.where(
                column < width_of(a), dh[0, a, 1 + rr], 0.0
            )
        return s

    lax.fori_loop(0, maps_here, input_rows, 0)

    outs = (
        (
            remote(igbuf.at[other], ig_ref.at[c], out_s.at[0], out_r.at[0], m, z, other),
            pltpu.make_async_copy(igbuf.at[c], ig_ref.at[c], out_l.at[0]),
        ),
        (
            remote(pbuf.at[other], pooled_ref.at[c], out_s.at[1], out_r.at[1], m, z, other),
            pltpu.make_async_copy(pbuf.at[c], pooled_ref.at[c], out_l.at[1]),
        ),
        (
            remote(sums_own, sums_ref.at[c], out_s.at[2], out_r.at[2], m, z, other),
            pltpu.make_async_copy(sums_own, sums_ref.at[c], out_l.at[2]),
        ),
    )
    for there, here in outs:
        there.start()
        here.start()

    run(stage_sum, TAPS, 2 * TAPS)
    run(stage_second, 0, TAPS)
    weight_terms(0)
    run(stage_chip, 0, TAPS)

    def drain(s, carry):
        for stage, first, lag in (
            (stage_chip, TAPS, 2 * LAG),
            (stage_second, TAPS, LAG),
            (stage_plane, TAPS, 0),
            (stage_sum, 2 * TAPS, 0),
        ):
            q = first + s - lag

            @pl.when(jnp.logical_and(q >= first, q < UNITS))
            def _(stage=stage, q=q):
                stage(q)

        return carry

    lax.fori_loop(0, UNITS - TAPS + 2 * LAG, drain, 0)

    def finish(q, carry):
        cp(q).wait()
        ca(q).wait_send()
        cb(q, 0).wait_send()
        cb(q, 1).wait_send()

        def given(k):
            p = lax.rem(z + k, chips)

            @pl.when(p < owners)
            def _():
                c3(q, p).wait_send()

        each(1, chips, given)

        @pl.when(z < owners)
        def _():
            each(1, chips, lambda k: cz(q, z, lax.rem(z + k, chips)).wait_send())

        return carry

    lax.fori_loop(0, UNITS, finish, 0)
    for l in range(LAYERS):
        each(1, PLANE, lambda k: at_copy(l, k).wait_send())
        each(1, PLANE, lambda k: dzs_copy(l, k, dz_own).wait_send())
    for l in range(1, LAYERS):
        act_copy(l).wait_send()
    for l in range(LAYERS):
        dz_copy(l).wait_send()
    for there, here in outs:
        there.wait()
        here.wait()


def solution(mesh):
    chips = mesh.shape["rows"] // 2

    def per_device(
        block_input,
        conv_weights,
        norm_gains,
        norm_shifts,
        map_width,
        map_group,
        pool_index,
        task_mask,
        task_weights,
        task_grads,
    ):
        maps_here, rows_here, columns, channels = block_input.shape
        pooled_columns = pool_index.shape[2]
        height = rows_here * mesh.shape["rows"]
        half = channels // 2
        band = 2 * rows_here
        pixels = maps_here * band * PAD
        owners = min(chips, 8)
        piece = half // owners
        slice_lanes = channels // PLANE
        rounds = 2 * LAYERS
        vmem, dma = pltpu.VMEM, pltpu.SemaphoreType.DMA
        tile = (maps_here, band + 2, PAD, half)
        whole = pl.BlockSpec(memory_space=pltpu.VMEM)
        scalars = pl.BlockSpec(memory_space=pltpu.SMEM)
        anywhere = pl.BlockSpec(memory_space=pl.ANY)
        pooled, ig, kg, sums = pl.pallas_call(
            functools.partial(block_kernel, chips, height),
            out_shape=(
                jax.ShapeDtypeStruct((2, maps_here, PAD // 2, half), BF16),
                jax.ShapeDtypeStruct((2, maps_here, rows_here, PAD, half), F32),
                jax.ShapeDtypeStruct((UNITS, channels, channels), BF16),
                jax.ShapeDtypeStruct((2, 8, half), F32),
            ),
            in_specs=[whole, anywhere, whole, whole, scalars, scalars, whole, scalars, scalars, whole],
            out_specs=[anywhere] * 4,
            scratch_shapes=[
                vmem((LAYERS, 3, 3, half, half), BF16),
                vmem((LAYERS, 3, 3, half, half), BF16),
                vmem((LAYERS, 3, 3, half, half), BF16),
                vmem((LAYERS + 1,) + tile, BF16),
                vmem((LAYERS,) + tile, BF16),
                vmem((LAYERS, PLANE, half, pixels), BF16),
                vmem((LAYERS,) + tile, F32),
                vmem((LAYERS + 1,) + tile, F32),
                vmem(tile, F32),
                vmem((LAYERS,) + tile, BF16),
                vmem((LAYERS,) + tile, BF16),
                vmem((LAYERS, PLANE, maps_here, band + 2, PAD, slice_lanes), BF16),
                vmem((3, PLANE, maps_here, band + 2, PAD, slice_lanes), BF16),
                vmem((3, pixels, half), F32),
                vmem((2, 2, maps_here, PAD // 2, half), F32),
                vmem((4, 2, maps_here, PAD // 2, half), F32),
                vmem((half // 128, PAD, 128), F32),
                vmem((2, maps_here, PAD // 2, half), BF16),
                vmem((2, maps_here, rows_here, PAD, half), F32),
                vmem((rounds, chips, 8, half), F32),
                vmem((rounds, PLANE, 8, half), F32),
                vmem((maps_here, PLANE, 8, half), F32),
                vmem((PLANE, 8, half), F32),
                vmem((2, 8, half), F32),
                vmem((8, half), F32),
                vmem((LAYERS, 8, half), F32),
                vmem((LAYERS, 8, half), F32),
                vmem((1, 8, half), F32),
                vmem((1, 8, half), F32),
                vmem((8, half), F32),
                vmem((UNITS, half, slice_lanes), BF16),
                vmem((UNITS, chips - 1, piece, slice_lanes), BF16),
                vmem((UNITS, piece, slice_lanes), BF16),
                dma((LAYERS, 3)),
                dma((6,)),
                dma((6,)),
                dma((3,)),
                dma((3,)),
                dma((rounds, chips)),
                dma((rounds, chips)),
                dma((rounds, PLANE)),
                dma((rounds, PLANE)),
                dma((LAYERS, 2)),
                dma((LAYERS, 2)),
                dma((LAYERS, 2)),
                dma((LAYERS, 2)),
                dma((LAYERS,)),
                dma((LAYERS,)),
                dma((LAYERS,)),
                dma((LAYERS,)),
                dma((3,)),
                dma((3,)),
                dma((3,)),
                dma((LAYERS, PLANE)),
                dma((LAYERS, PLANE)),
                dma((LAYERS, PLANE)),
                dma((LAYERS, PLANE)),
                dma((UNITS, owners)),
                dma((UNITS, chips - 1)),
                dma((UNITS, chips)),
                dma((UNITS, owners)),
                dma((UNITS, 2)),
                dma((UNITS, 2)),
                dma((UNITS,)),
                dma((UNITS,)),
                dma((UNITS,)),
                dma((UNITS,)),
                dma((UNITS,)),
            ],
            compiler_params=pltpu.CompilerParams(
                collective_id=0,
                has_side_effects=True,
                vmem_limit_bytes=63 * 1024 * 1024,
            ),
        )(
            block_input,
            conv_weights,
            norm_gains,
            norm_shifts,
            map_width,
            map_group,
            pool_index,
            task_mask,
            task_weights,
            task_grads,
        )
        pooled = jnp.concatenate([pooled[0], pooled[1]], -1)[:, None, :pooled_columns]
        input_grad = jnp.concatenate([ig[0], ig[1]], -1)[:, :, :columns]
        sums = jnp.concatenate([sums[0], sums[1]], -1)
        return (
            pooled,
            input_grad,
            kg.astype(F32).reshape(conv_weights.shape),
            sums[:LAYERS],
            sums[LAYERS : 2 * LAYERS],
        )

    return jax.shard_map(
        per_device,
        mesh=mesh,
        in_specs=(
            P("maps", "rows", None, None),
            P(),
            P(),
            P(),
            P(),
            P(),
            P("maps", "rows", None, None),
            P("maps", None),
            P(),
            P(None, "maps", "rows", None, None),
        ),
        out_specs=(P("maps", "rows", None, None), P("maps", "rows", None, None), P(), P(), P()),
        check_vma=False,
    )
```

```python
import functools

import jax
import jax.numpy as jnp
from jax import lax
from jax.experimental import pallas as pl
from jax.experimental.pallas import tpu as pltpu
from jax.sharding import PartitionSpec as P

MESH = pl.DeviceIdType.MESH
epsilon = 1e-05
PAD = 64
LAYERS = 3
TAPS = 9
UNITS = LAYERS * TAPS
PLANE = 4
LAG = 2
F32 = jnp.float32
BF16 = jnp.bfloat16


def each(first, last, body):
    if last - first <= 8:
        for k in range(first, last):
            body(k)
    else:
        lax.fori_loop(first, last, lambda k, s: (body(k), s)[1], 0)


def block_kernel(
    chips,
    height,
    x_ref,
    w_ref,
    gain_ref,
    shift_ref,
    width_ref,
    group_ref,
    index_ref,
    tmask_ref,
    tweight_ref,
    tgrad_ref,
    pooled_ref,
    ig_ref,
    terms,
    sums_ref,
    wa,
    wb,
    wc,
    act_own,
    act_oth,
    at,
    zbuf,
    dh,
    dyb,
    dz_own,
    dz_oth,
    dzs,
    dzv,
    prod,
    gsrc,
    gbuf,
    hrow,
    pbuf,
    igbuf,
    st1,
    st2,
    coef,
    nall,
    inv_t,
    cnt_t,
    avg_t,
    scl_t,
    tb_t,
    ta_t,
    sums_own,
    w_sem,
    x_s,
    x_r,
    g_s,
    g_r,
    st1_s,
    st1_r,
    st2_s,
    st2_r,
    zh_s,
    zh_r,
    dh_s,
    dh_r,
    act_s,
    act_r,
    dz_s,
    dz_r,
    out_s,
    out_r,
    out_l,
    at_s,
    at_r,
    dzs_s,
    dzs_r,
):
    maps_here = x_ref.shape[0]
    columns = x_ref.shape[2]
    half = x_ref.shape[3] // 2
    tasks = tgrad_ref.shape[0]
    pooled_columns = tgrad_ref.shape[3]
    lanes = half // 128
    tiles = [slice(n * 128, (n + 1) * 128) for n in range(lanes)]
    band = 4
    pixels = maps_here * band * PAD
    slice_lanes = 2 * half // PLANE
    m = lax.axis_index("maps")
    r = lax.axis_index("rows")
    c = lax.rem(r, 2)
    z = lax.div(r, 2)
    other = 1 - c
    first_map = m * maps_here
    up_there = z > 0
    down_there = z < chips - 1
    row8 = lax.broadcasted_iota(jnp.int32, (8, half), 0)
    column = lax.broadcasted_iota(jnp.int32, (PAD, half), 0)

    def remote(src, dst, send, recv, mm, zz, cc):
        return pltpu.make_async_remote_copy(
            src_ref=src,
            dst_ref=dst,
            send_sem=send,
            recv_sem=recv,
            device_id=(mm, zz * 2 + cc),
            device_id_type=MESH,
        )

    def own_half(v):
        return jnp.where(c == 0, v[..., :half], v[..., half:])

    def width_of(a):
        return width_ref[first_map + a]

    own_at = pl.ds(pl.multiple_of(c * half, half), half)
    oth_at = pl.ds(pl.multiple_of(other * half, half), half)

    def weight_copy(l, n):
        dst = (wa, wb, wc)[n]
        k_at, o_at = ((own_at, own_at), (oth_at, own_at), (own_at, oth_at))[n]
        return pltpu.make_async_copy(w_ref.at[l, :, :, k_at, o_at], dst.at[l], w_sem.at[l, n])

    for l in range(LAYERS):
        weight_copy(l, 0).start()
        weight_copy(l, 1).start()
    for l in range(LAYERS):
        weight_copy(LAYERS - 1 - l, 2).start()

    barrier = pltpu.get_barrier_semaphore()

    def greet(k):
        rr = lax.rem(r + k, 2 * chips)
        pl.semaphore_signal(barrier, inc=1, device_id=(m, rr), device_id_type=MESH)

    each(1, 2 * chips, greet)
    for k in range(1, PLANE):
        pl.semaphore_signal(
            barrier, inc=1, device_id=(lax.rem(m + k, PLANE), r), device_id_type=MESH
        )

    mine = pl.ds(1 + 2 * c, 2)
    for a in range(maps_here):
        inside = lax.broadcasted_iota(jnp.int32, (columns, 2 * half), 0) < width_of(a)
        for rr in range(2):
            v = jnp.where(inside, x_ref[a, rr].astype(F32), 0.0).astype(BF16)
            spot = 1 + 2 * c + rr
            act_own[0, a, spot, pl.ds(48, 16), :] = jnp.zeros((16, half), BF16)
            act_oth[0, a, spot, pl.ds(48, 16), :] = jnp.zeros((16, half), BF16)
            act_own[0, a, spot, pl.ds(0, columns), :] = own_half(v)
            act_oth[0, a, spot, pl.ds(0, columns), :] = jnp.where(
                c == 0, v[:, half:], v[:, :half]
            )

    @pl.when(z == 0)
    def _():
        act_own[0, :, 0] = jnp.zeros((maps_here, PAD, half), BF16)
        act_oth[0, :, 0] = jnp.zeros((maps_here, PAD, half), BF16)

    @pl.when(z == chips - 1)
    def _():
        act_own[0, :, 5] = jnp.zeros((maps_here, PAD, half), BF16)
        act_oth[0, :, 5] = jnp.zeros((maps_here, PAD, half), BF16)

    gsrc[...] = jnp.zeros(gsrc.shape, F32)
    for a in range(maps_here):
        total = None
        for t in range(tasks):
            scale = tweight_ref[t] * tmask_ref[a, t].astype(F32)
            term = tgrad_ref[t, a, 0].astype(F32) * scale
            total = term if total is None else total + term
        position = index_ref[a, 0].astype(F32)
        for h in range(2):
            gsrc[h, 0, a, pl.ds(0, pooled_columns), :] = total[:, h * half : (h + 1) * half]
            gsrc[h, 1, a, pl.ds(0, pooled_columns), :] = position[:, h * half : (h + 1) * half]
    gbuf[1 + c] = gsrc[c]

    pl.semaphore_wait(barrier, 2 * chips - 1 + PLANE - 1)

    x_partner = (
        remote(act_own.at[0, :, mine], act_oth.at[0, :, mine], x_s.at[0], x_r.at[0], m, z, other),
        remote(act_oth.at[0, :, mine], act_own.at[0, :, mine], x_s.at[1], x_r.at[1], m, z, other),
    )
    g_partner = remote(gsrc.at[other], gbuf.at[1 + c], g_s.at[0], g_r.at[0], m, z, other)

    def x_halo(n, src_row, dst_row, zz):
        cc = (c, c, other, other, c, other)[n]
        low = dst_row == band + 1
        if n >= 4:
            src, dst = gsrc.at[cc], gbuf.at[3 if low else 0]
            return remote(src, dst, g_s.at[n - 3], g_r.at[1 if low else 2], m, zz, cc)
        src = (act_own, act_oth, act_own, act_oth)[n].at[0, :, src_row]
        dst = (act_own, act_oth, act_oth, act_own)[n].at[0, :, dst_row]
        return remote(src, dst, x_s.at[2 + n], x_r.at[(2 if low else 4) + n % 2], m, zz, cc)

    for copy in x_partner:
        copy.start()

    @pl.when(jnp.logical_and(c == 0, up_there))
    def _():
        for n in range(6):
            x_halo(n, 1, 5, z - 1).start()

    @pl.when(jnp.logical_and(c == 1, down_there))
    def _():
        for n in range(6):
            x_halo(n, 4, 0, z + 1).start()

    g_partner.start()

    for mm in range(PLANE):
        sizes = jnp.zeros((8, half), F32)
        for b in range(maps_here):
            sizes = jnp.where(
                row8 == b, (width_ref[mm * maps_here + b] * height).astype(F32), sizes
            )
        nall[mm] = sizes
    inside_sizes = jnp.zeros((8, half), F32)
    for b in range(maps_here):
        inside_sizes = jnp.where(row8 == b, (width_of(b) * band).astype(F32), inside_sizes)
    inv_t[0] = inside_sizes
    inv_t[1] = jnp.where(row8 < maps_here, 1.0 / jnp.maximum(inside_sizes, 1.0), 0.0)
    counts = jnp.ones((8, half), F32)
    for a in range(maps_here):
        total = jnp.zeros((1, half), F32)
        for mm in range(PLANE):
            same = jnp.zeros((8, half), F32)
            for b in range(maps_here):
                alike = group_ref[first_map + a] == group_ref[mm * maps_here + b]
                same = jnp.where(row8 == b, jnp.where(alike, 1.0, 0.0), same)
            coef[a, mm] = same
            total = total + jnp.sum(same * nall[mm], 0, keepdims=True)
        counts = jnp.where(row8 == a, total, counts)
    cnt_t[...] = counts

    def z_copy(e, k):
        zz = lax.rem(z + k, chips)
        return remote(st1.at[e, z], st1.at[e, z], st1_s.at[e, k], st1_r.at[e, z], m, zz, c)

    def z_arrival(e, k):
        zz = lax.rem(z + k, chips)
        return remote(st1.at[e, zz], st1.at[e, zz], st1_s.at[e, k], st1_r.at[e, zz], m, zz, c)

    def m_copy(e, k):
        mm = lax.rem(m + k, PLANE)
        return remote(st2.at[e, m], st2.at[e, m], st2_s.at[e, k], st2_r.at[e, m], mm, z, c)

    def m_arrival(e, k):
        mm = lax.rem(m + k, PLANE)
        return remote(st2.at[e, mm], st2.at[e, mm], st2_s.at[e, k], st2_r.at[e, mm], mm, z, c)

    def send_z(e, tile):
        st1[e, z] = tile
        each(1, chips, lambda k: z_copy(e, k).start())

    def wait_z(e):
        each(1, chips, lambda k: z_arrival(e, k).wait_recv())
        each(1, chips, lambda k: z_copy(e, k).wait_send())

    def send_m(e, tile):
        st2[e, m] = tile
        each(1, PLANE, lambda k: m_copy(e, k).start())

    def wait_m(e):
        each(1, PLANE, lambda k: m_arrival(e, k).wait_recv())
        each(1, PLANE, lambda k: m_copy(e, k).wait_send())

    def products(source, l, starts, kernel, transposed, fresh):
        parts = [
            source[l, :, s : s + band].reshape(pixels, half) for s in starts
        ]
        lhs = jnp.concatenate(parts, 1)
        for j in range(3):
            if transposed:
                rhs = jnp.concatenate([kernel[l, i, j] for i in range(3)], 1)
                got = lax.dot_general(
                    lhs, rhs, (((1,), (1,)), ((), ())), preferred_element_type=F32
                )
            else:
                rhs = kernel[l, :, j].reshape(3 * half, half)
                got = jnp.dot(lhs, rhs, preferred_element_type=F32)
            if fresh:
                prod[j] = got
            else:
                prod[j] = prod[j] + got

    def shifted(a, rr, before, behind, n):
        rows = pl.ds(pl.multiple_of((a * band + rr) * PAD, PAD), PAD)
        return (
            prod[1, rows, n]
            + pltpu.roll(prod[before, rows, n], 1, 0)
            + pltpu.roll(prod[behind, rows, n], PAD - 1, 0)
        )

    def row_of(table, l, a):
        return table[l, pl.ds(a, 1), :]

    def gain_of(l):
        return own_half(gain_ref[pl.ds(l, 1), :])

    def shift_of(l):
        return own_half(shift_ref[pl.ds(l, 1), :])

    def limit(a, rr):
        w = width_of(a)
        if rr == 0:
            return jnp.where(up_there, w, 0)
        if rr == band + 1:
            return jnp.where(down_there, w, 0)
        return w

    def z_halo(l, way):
        if way == 0:
            return remote(zbuf.at[l, :, 1], zbuf.at[l, :, 5], zh_s.at[l, 0], zh_r.at[l, 0], m, z - 1, c)
        return remote(zbuf.at[l, :, 4], zbuf.at[l, :, 0], zh_s.at[l, 1], zh_r.at[l, 1], m, z + 1, c)

    def dh_halo(l, way):
        if way == 0:
            return remote(dh.at[l, :, 1], dh.at[l, :, 5], dh_s.at[l, 0], dh_r.at[l, 0], m, z - 1, c)
        return remote(dh.at[l, :, 4], dh.at[l, :, 0], dh_s.at[l, 1], dh_r.at[l, 1], m, z + 1, c)

    def start_halo(halo, l):
        @pl.when(up_there)
        def _():
            halo(l, 0).start()

        @pl.when(down_there)
        def _():
            halo(l, 1).start()

    def wait_halo(halo, l):
        @pl.when(up_there)
        def _():
            halo(l, 1).wait_recv()
            halo(l, 0).wait_send()

        @pl.when(down_there)
        def _():
            halo(l, 0).wait_recv()
            halo(l, 1).wait_send()

    def act_copy(l):
        return remote(act_own.at[l], act_oth.at[l], act_s.at[l], act_r.at[l], m, z, other)

    def at_copy(l, k):
        mm = lax.rem(m + k, PLANE)
        return remote(at.at[l, m], at.at[l, m], at_s.at[l, k], at_r.at[l, m], mm, z, c)

    def at_arrival(l, k):
        mm = lax.rem(m + k, PLANE)
        return remote(at.at[l, mm], at.at[l, mm], at_s.at[l, k], at_r.at[l, mm], mm, z, c)

    per_half = half // slice_lanes

    def slice_at(mm):
        first = lax.rem(mm, per_half) * slice_lanes
        return pl.ds(pl.multiple_of(first, slice_lanes), slice_lanes)

    def dzs_copy(l, k, source):
        mm = lax.rem(m + k, PLANE)
        src = source.at[l, :, :, :, slice_at(mm)]
        return remote(src, dzs.at[l, m], dzs_s.at[l, k], dzs_r.at[l, m], mm, z, c)

    def dzs_arrival(l, k):
        mm = lax.rem(m + k, PLANE)
        return remote(dzs.at[l, mm], dzs.at[l, mm], dzs_s.at[l, k], dzs_r.at[l, mm], mm, z, c)

    def send_slices(l, source, core):
        for k in range(PLANE):
            mm = lax.rem(m + k, PLANE)

            @pl.when(lax.div(mm, per_half) == core)
            def _(k=k, mm=mm):
                if k:
                    dzs_copy(l, k, source).start()
                else:
                    for a in range(maps_here):
                        dzs[l, m, a] = source[l, a, :, :, slice_at(mm)]

    def dz_copy(l):
        return remote(dz_own.at[l], dz_oth.at[l], dz_s.at[l], dz_r.at[l], m, z, other)

    for copy in x_partner:
        copy.wait()

    @pl.when(up_there)
    def _():
        for n in (0, 1, 4):
            x_halo(n, 4, 0, z - 1).wait_recv()

    @pl.when(down_there)
    def _():
        for n in (0, 1, 4):
            x_halo(n, 1, 5, z + 1).wait_recv()

    @pl.when(jnp.logical_and(c == 0, up_there))
    def _():
        for n in range(6):
            x_halo(n, 1, 5, z - 1).wait_send()

    @pl.when(jnp.logical_and(c == 1, down_there))
    def _():
        for n in range(6):
            x_halo(n, 4, 0, z + 1).wait_send()

    g_partner.wait()

    def forward(l, carry):
        weight_copy(l, 0).wait()
        products(act_own, l, (0, 1, 2), wa, False, True)
        weight_copy(l, 1).wait()

        @pl.when(l > 0)
        def _():
            act_copy(l).wait_recv()

        products(act_oth, l, (0, 1, 2), wb, False, False)

        def collect(a, tile):
            inside = column[:, :128] < width_of(a)
            pixels_inside = (width_of(a) * band).astype(F32)
            totals, squares = [], []
            for n in tiles:
                total = jnp.zeros((PAD, 128), F32)
                for rr in range(band):
                    v = shifted(a, rr, 0, 2, n)
                    zbuf[l, a, 1 + rr, :, n] = v
                    total = total + jnp.where(inside, v, 0.0)
                total = jnp.sum(total, 0, keepdims=True)
                mean = total / pixels_inside
                square = jnp.zeros((PAD, 128), F32)
                for rr in range(band):
                    v = jnp.where(inside, zbuf[l, a, 1 + rr, :, n] - mean, 0.0)
                    square = square + v * v
                totals.append(total)
                squares.append(jnp.sum(square, 0, keepdims=True))
            tile = jnp.where(row8 == a, jnp.concatenate(totals, 1), tile)
            return jnp.where(row8 == a + maps_here, jnp.concatenate(squares, 1), tile)

        tile = lax.fori_loop(0, maps_here, collect, jnp.zeros((8, half), F32))
        send_z(l, tile)
        start_halo(z_halo, l)
        at[l, m] = act_own[l, :, 1 : 1 + band].reshape(pixels, half).T
        wait_z(l)
        sizes, inverse = inv_t[0], inv_t[1]
        total = st1[l, 0]
        for zz in range(1, chips):
            total = total + st1[l, zz]
        mean = total * inverse * (1.0 / chips)
        square = jnp.zeros((8, half), F32)
        for zz in range(chips):
            v = st1[l, zz]
            gap = v * inverse - mean
            square = square + pltpu.roll(v, 8 - maps_here, 0) + sizes * gap * gap
        tile = jnp.where(row8 < maps_here, mean, pltpu.roll(square, maps_here, 0))
        send_m(l, jnp.where(row8 < 2 * maps_here, tile, 0.0))
        wait_m(l)
        each(1, PLANE, lambda k: at_copy(l, k).start())
        averages = jnp.zeros((8, half), F32)
        scalings = jnp.zeros((8, half), F32)
        for a in range(maps_here):
            count = cnt_t[a : a + 1, :]
            average = jnp.zeros((8, half), F32)
            for mm in range(PLANE):
                average = average + coef[a, mm] * nall[mm] * st2[l, mm]
            average = jnp.sum(average, 0, keepdims=True) / count
            variance = jnp.zeros((8, half), F32)
            for mm in range(PLANE):
                v = st2[l, mm]
                gap = v - average
                variance = variance + coef[a, mm] * (
                    pltpu.roll(v, 8 - maps_here, 0) + nall[mm] * gap * gap
                )
            variance = jnp.sum(variance, 0, keepdims=True) / count
            averages = jnp.where(row8 == a, average, averages)
            scalings = jnp.where(row8 == a, lax.rsqrt(variance + epsilon), scalings)
        avg_t[l] = averages
        scl_t[l] = scalings
        wait_halo(z_halo, l)

        def activate(a, s):
            gain, shift = gain_of(l), shift_of(l)
            for n in tiles:
                average = row_of(avg_t, l, a)[:, n]
                factor = row_of(scl_t, l, a)[:, n] * gain[:, n]
                for rr in range(band + 2):
                    y = (zbuf[l, a, rr, :, n] - average) * factor + shift[:, n]
                    h = jnp.where(column[:, n] < limit(a, rr), y * jax.nn.sigmoid(y), 0.0)
                    act_own[l + 1, a, rr, :, n] = h.astype(BF16)
            return s

        lax.fori_loop(0, maps_here, activate, 0)

        @pl.when(l < LAYERS - 1)
        def _():
            act_copy(l + 1).start()

        return carry

    lax.fori_loop(0, LAYERS, forward, 0)

    def unpool(a, s):
        for rr in range(band + 2):
            slot, lower = (rr + 1) // 2, (rr + 1) % 2
            g = gbuf[slot, 0, a]
            position = gbuf[slot, 1, a]
            for b in range(2):
                v = jnp.where(position == float(2 * lower + b), g, 0.0)
                for n in range(lanes):
                    hrow[n, pl.ds(b, PAD // 2, stride=2), :] = v[:, n * 128 : (n + 1) * 128]
            dh[LAYERS, a, rr] = jnp.concatenate([hrow[n] for n in range(lanes)], 1)
        return s

    lax.fori_loop(0, maps_here, unpool, 0)

    def pool():
        def one(a, s):
            for pr in range(2):
                total = jnp.zeros((PAD // 2, half), F32)
                position = gbuf[1 + pr, 1, a]
                for lower in range(2):
                    v = act_own[LAYERS, a, 1 + 2 * pr + lower].astype(F32)
                    for n in range(lanes):
                        hrow[n] = v[:, n * 128 : (n + 1) * 128]
                    for b in range(2):
                        v = jnp.concatenate(
                            [hrow[n, pl.ds(b, PAD // 2, stride=2), :] for n in range(lanes)], 1
                        )
                        total = total + jnp.where(position == float(2 * lower + b), v, 0.0)
                pbuf[pr, a] = total.astype(BF16)
            return s

        lax.fori_loop(0, maps_here, one, 0)

    def variants(l):
        def one(n, s):
            chip = lax.div(n, maps_here)
            a = n - chip * maps_here
            for rr in range(band + 2):
                v = dzs[l, chip, a, rr]
                dzv[1, chip, a, rr] = v
                v = v.astype(F32)
                dzv[0, chip, a, rr] = pltpu.roll(v, PAD - 1, 0).astype(BF16)
                dzv[2, chip, a, rr] = pltpu.roll(v, 1, 0).astype(BF16)
            return s

        lax.fori_loop(0, PLANE * maps_here, one, 0)

    def weight_terms(l):
        each(1, PLANE, lambda k: at_arrival(l, k).wait_recv())
        each(1, PLANE, lambda k: dzs_arrival(l, k).wait_recv())
        variants(l)
        first = (LAYERS - 1 - l) * TAPS

        def shifted_slices(t):
            i = lax.div(t, 3)
            j = t - 3 * i
            return dzv[j, :, :, pl.ds(2 - i, band)].reshape(PLANE * pixels, slice_lanes)

        def times(rhs):
            lhs = jnp.concatenate([at[l, chip] for chip in range(PLANE)], 1)
            return jnp.dot(lhs, rhs, preferred_element_type=F32).astype(BF16)

        def pair(g, s):
            t = 2 * g
            got = times(jnp.concatenate([shifted_slices(t), shifted_slices(t + 1)], 1))
            terms[first + t] = got[:, :slice_lanes]
            terms[first + t + 1] = got[:, slice_lanes:]
            return s

        lax.fori_loop(0, TAPS // 2, pair, 0)
        terms[first + TAPS - 1] = times(shifted_slices(TAPS - 1))

    def backward(k, carry):
        l = LAYERS - 1 - k
        gain, shift = gain_of(l), shift_of(l)

        def gradient(a, rr, n):
            zhat = (zbuf[l, a, rr, :, n] - row_of(avg_t, l, a)[:, n]) * row_of(scl_t, l, a)[:, n]
            y = zhat * gain[:, n] + shift[:, n]
            s = jax.nn.sigmoid(y)
            dy = dh[l + 1, a, rr, :, n] * (s * (1.0 + y * (1.0 - s)))
            dy = jnp.where(column[:, n] < limit(a, rr), dy, 0.0)
            dyb[a, rr, :, n] = dy
            return dy, zhat

        def collect(a, tile):
            plains, crosses = [], []
            for n in tiles:
                plain = jnp.zeros((PAD, 128), F32)
                crossed = jnp.zeros((PAD, 128), F32)
                for rr in range(1, band + 1):
                    dy, zhat = gradient(a, rr, n)
                    plain = plain + dy
                    crossed = crossed + dy * zhat
                plains.append(jnp.sum(plain, 0, keepdims=True))
                crosses.append(jnp.sum(crossed, 0, keepdims=True))
            tile = jnp.where(row8 == a, jnp.concatenate(plains, 1), tile)
            return jnp.where(row8 == a + maps_here, jnp.concatenate(crosses, 1), tile)

        e = LAYERS + l
        tile = lax.fori_loop(0, maps_here, collect, jnp.zeros((8, half), F32))
        send_z(e, tile)

        wait_z(e)
        total = st1[e, 0]
        for zz in range(1, chips):
            total = total + st1[e, zz]
        send_m(e, total)

        @pl.when(k > 0)
        def _():
            weight_terms(l + 1)
            wait_halo(dh_halo, l + 1)

        @pl.when(k == 0)
        def _():
            pool()

        def edges(a, s):
            for n in tiles:
                gradient(a, 0, n)
                gradient(a, band + 1, n)
            return s

        lax.fori_loop(0, maps_here, edges, 0)
        wait_m(e)
        total = st2[e, 0]
        for mm in range(1, PLANE):
            total = total + st2[e, mm]
        sums_own[pl.ds(l, 1), :] = jnp.sum(
            jnp.where(row8 >= maps_here, total, 0.0), 0, keepdims=True
        )
        sums_own[pl.ds(LAYERS + l, 1), :] = jnp.sum(
            jnp.where(row8 < maps_here, total, 0.0), 0, keepdims=True
        )
        plains = jnp.zeros((8, half), F32)
        crosses = jnp.zeros((8, half), F32)
        for a in range(maps_here):
            plain = jnp.zeros((8, half), F32)
            crossed = jnp.zeros((8, half), F32)
            for mm in range(PLANE):
                v = st2[e, mm]
                plain = plain + coef[a, mm] * v
                crossed = crossed + coef[a, mm] * pltpu.roll(v, 8 - maps_here, 0)
            count = cnt_t[a : a + 1, :]
            plain = gain * (jnp.sum(plain, 0, keepdims=True) / count)
            crossed = gain * (jnp.sum(crossed, 0, keepdims=True) / count)
            plains = jnp.where(row8 == a, plain, plains)
            crosses = jnp.where(row8 == a, crossed, crosses)
        tb_t[0] = plains
        ta_t[0] = crosses

        def settle(a, s):
            for n in tiles:
                average, scaling = row_of(avg_t, l, a)[:, n], row_of(scl_t, l, a)[:, n]
                plain, crossed = row_of(tb_t, 0, a)[:, n], row_of(ta_t, 0, a)[:, n]
                for rr in range(band + 2):
                    zhat = (zbuf[l, a, rr, :, n] - average) * scaling
                    v = scaling * (dyb[a, rr, :, n] * gain[:, n] - plain - zhat * crossed)
                    v = jnp.where(column[:, n] < limit(a, rr), v, 0.0)
                    dz_own[l, a, rr, :, n] = v.astype(BF16)
            return s

        lax.fori_loop(0, maps_here, settle, 0)
        dz_copy(l).start()
        send_slices(l, dz_own, c)
        products(dz_own, l, (2, 1, 0), wa, True, True)
        weight_copy(l, 2).wait()
        dz_copy(l).wait_recv()
        send_slices(l, dz_oth, other)
        products(dz_oth, l, (2, 1, 0), wc, True, False)

        def gather(a, s):
            for n in tiles:
                for rr in range(band):
                    dh[l, a, 1 + rr, :, n] = shifted(a, rr, 2, 0, n)
            return s

        lax.fori_loop(0, maps_here, gather, 0)

        @pl.when(l > 0)
        def _():
            start_halo(dh_halo, l)

        return carry

    lax.fori_loop(0, LAYERS, backward, 0)
    weight_terms(0)

    def input_rows(a, s):
        for rr in range(band):
            igbuf[rr // 2, a, rr % 2] = jnp.where(
                column < width_of(a), dh[0, a, 1 + rr], 0.0
            )
        return s

    lax.fori_loop(0, maps_here, input_rows, 0)

    outs = (
        (
            remote(igbuf.at[other], ig_ref.at[c], out_s.at[0], out_r.at[0], m, z, other),
            pltpu.make_async_copy(igbuf.at[c], ig_ref.at[c], out_l.at[0]),
        ),
        (
            remote(pbuf.at[other], pooled_ref.at[c], out_s.at[1], out_r.at[1], m, z, other),
            pltpu.make_async_copy(pbuf.at[c], pooled_ref.at[c], out_l.at[1]),
        ),
        (
            remote(sums_own, sums_ref.at[c], out_s.at[2], out_r.at[2], m, z, other),
            pltpu.make_async_copy(sums_own, sums_ref.at[c], out_l.at[2]),
        ),
    )
    for there, here in outs:
        there.start()
        here.start()

    for l in range(LAYERS):
        each(1, PLANE, lambda k: at_copy(l, k).wait_send())
        each(1, PLANE, lambda k: dzs_copy(l, k, dz_own).wait_send())
    for l in range(1, LAYERS):
        act_copy(l).wait_send()
    for l in range(LAYERS):
        dz_copy(l).wait_send()
    for there, here in outs:
        there.wait()
        here.wait()


def reduce_kernel(
    chips,
    terms,
    kg_ref,
    r3,
    fin,
    r3_s,
    r3_r,
    az_s,
    az_r,
    ab_s,
    ab_r,
    aa_s,
    aa_r,
    ap_s,
    ap_r,
    loc_s,
):
    half, slice_lanes = terms.shape[1:]
    owners = min(chips, 8)
    piece = half // owners
    m = lax.axis_index("maps")
    r = lax.axis_index("rows")
    c = lax.rem(r, 2)
    z = lax.div(r, 2)
    other = 1 - c
    x_peer = m + 1 - 2 * lax.rem(m, 2)
    y_peer = m + 2 - 4 * lax.div(m, 2)

    def remote(src, dst, send, recv, mm, zz, cc):
        return pltpu.make_async_remote_copy(
            src_ref=src,
            dst_ref=dst,
            send_sem=send,
            recv_sem=recv,
            device_id=(mm, zz * 2 + cc),
            device_id_type=MESH,
        )

    barrier = pltpu.get_barrier_semaphore()

    def greet(k):
        rr = lax.rem(r + k, 2 * chips)
        pl.semaphore_signal(barrier, inc=1, device_id=(m, rr), device_id_type=MESH)

    each(1, 2 * chips, greet)
    for k in range(1, PLANE):
        pl.semaphore_signal(
            barrier, inc=1, device_id=(lax.rem(m + k, PLANE), r), device_id_type=MESH
        )
    pl.semaphore_wait(barrier, 2 * chips - 1 + PLANE - 1)

    def piece_rows(p):
        return pl.ds(pl.multiple_of(p * piece, piece), piece)

    def c3(q, p):
        slot = lax.rem(z - p + chips - 1, chips)
        return remote(
            terms.at[q, piece_rows(p)], r3.at[q, slot], r3_s.at[q, p], r3_r.at[q, slot], m, p, c
        )

    def unit_of(q):
        k = lax.div(q, TAPS)
        return (LAYERS - 1 - k) * TAPS + (q - k * TAPS)

    def region(q, start, size, mm, lanes=slice_lanes):
        start = pl.multiple_of(c * half + start, piece)
        first = pl.multiple_of(mm * slice_lanes, slice_lanes)
        return kg_ref.at[unit_of(q), pl.ds(start, size), pl.ds(first, lanes)]

    def order(q):
        swap = lax.rem(q, 2)
        keep = 1 - swap
        return keep * x_peer + swap * y_peer, keep * y_peer + swap * x_peer

    def cz(q, p, zz):
        part = region(q, p * piece, piece, m)
        return remote(fin.at[q], part, az_s.at[q, zz], az_r.at[q, p], m, zz, c)

    def cl(q):
        return pltpu.make_async_copy(fin.at[q], region(q, z * piece, piece, m), loc_s.at[q])

    def ca(q):
        part = region(q, 0, half, m)
        return remote(part, part, aa_s.at[q], aa_r.at[q], order(q)[0], z, c)

    def cb(q, n):
        first, second = order(q)
        part = region(q, 0, half, first if n else m)
        return remote(part, part, ab_s.at[q, n], ab_r.at[q, n], second, z, c)

    def cp(q):
        part = region(q, 0, half, 0, 2 * half)
        return remote(part, part, ap_s.at[q], ap_r.at[q], m, z, other)

    def give(q):
        def to(k):
            p = lax.rem(z + k, chips)

            @pl.when(p < owners)
            def _():
                c3(q, p).start()

        each(1, chips, to)

    def stage_sum(q):
        @pl.when(z < owners)
        def _():
            for k in range(chips - 1):
                remote(
                    r3.at[q, k], r3.at[q, k], r3_s.at[q, 0], r3_r.at[q, k], m, z, c
                ).wait_recv()
            total = terms[q, piece_rows(z)].astype(F32)
            for k in range(chips - 1):
                total = total + r3[q, k].astype(F32)
            fin[q] = total.astype(BF16)
            each(1, chips, lambda k: cz(q, z, lax.rem(z + k, chips)).start())
            cl(q).start()

    def stage_plane(q):
        def arrived(k):
            p = lax.rem(z + k, chips)

            @pl.when(p < owners)
            def _():
                cz(q, p, p).wait_recv()

        each(1, chips, arrived)

        @pl.when(z < owners)
        def _():
            cl(q).wait()

        ca(q).start()
        cb(q, 0).start()

    def stage_second(q):
        ca(q).wait_recv()
        cb(q, 1).start()

    def stage_chip(q):
        cb(q, 0).wait_recv()
        cb(q, 1).wait_recv()
        cp(q).start()

    def run(stage, first, last):
        lax.fori_loop(first, last, lambda q, s: (stage(q), s)[1], 0)

    run(give, 0, UNITS)

    def drain(s, carry):
        for stage, lag in (
            (stage_chip, 3 * LAG),
            (stage_second, 2 * LAG),
            (stage_plane, LAG),
            (stage_sum, 0),
        ):
            q = s - lag

            @pl.when(jnp.logical_and(q >= 0, q < UNITS))
            def _(stage=stage, q=q):
                stage(q)

        return carry

    lax.fori_loop(0, UNITS + 3 * LAG, drain, 0)

    def finish(q, carry):
        cp(q).wait()
        ca(q).wait_send()
        cb(q, 0).wait_send()
        cb(q, 1).wait_send()

        def given(k):
            p = lax.rem(z + k, chips)

            @pl.when(p < owners)
            def _():
                c3(q, p).wait_send()

        each(1, chips, given)

        @pl.when(z < owners)
        def _():
            each(1, chips, lambda k: cz(q, z, lax.rem(z + k, chips)).wait_send())

        return carry

    lax.fori_loop(0, UNITS, finish, 0)


def solution(mesh):
    chips = mesh.shape["rows"] // 2

    def per_device(
        block_input,
        conv_weights,
        norm_gains,
        norm_shifts,
        map_width,
        map_group,
        pool_index,
        task_mask,
        task_weights,
        task_grads,
    ):
        maps_here, rows_here, columns, channels = block_input.shape
        pooled_columns = pool_index.shape[2]
        height = rows_here * mesh.shape["rows"]
        half = channels // 2
        band = 2 * rows_here
        pixels = maps_here * band * PAD
        owners = min(chips, 8)
        piece = half // owners
        slice_lanes = channels // PLANE
        rounds = 2 * LAYERS
        vmem, dma = pltpu.VMEM, pltpu.SemaphoreType.DMA
        tile = (maps_here, band + 2, PAD, half)
        whole = pl.BlockSpec(memory_space=pltpu.VMEM)
        scalars = pl.BlockSpec(memory_space=pltpu.SMEM)
        anywhere = pl.BlockSpec(memory_space=pl.ANY)
        pooled, ig, terms, sums = pl.pallas_call(
            functools.partial(block_kernel, chips, height),
            out_shape=(
                jax.ShapeDtypeStruct((2, maps_here, PAD // 2, half), BF16),
                jax.ShapeDtypeStruct((2, maps_here, rows_here, PAD, half), F32),
                jax.ShapeDtypeStruct((UNITS, half, slice_lanes), BF16),
                jax.ShapeDtypeStruct((2, 8, half), F32),
            ),
            in_specs=[whole, anywhere, whole, whole, scalars, scalars, whole, scalars, scalars, whole],
            out_specs=[anywhere, anywhere, whole, anywhere],
            scratch_shapes=[
                vmem((LAYERS, 3, 3, half, half), BF16),
                vmem((LAYERS, 3, 3, half, half), BF16),
                vmem((LAYERS, 3, 3, half, half), BF16),
                vmem((LAYERS + 1,) + tile, BF16),
                vmem((LAYERS,) + tile, BF16),
                vmem((LAYERS, PLANE, half, pixels), BF16),
                vmem((LAYERS,) + tile, F32),
                vmem((LAYERS + 1,) + tile, F32),
                vmem(tile, F32),
                vmem((LAYERS,) + tile, BF16),
                vmem((LAYERS,) + tile, BF16),
                vmem((LAYERS, PLANE, maps_here, band + 2, PAD, slice_lanes), BF16),
                vmem((3, PLANE, maps_here, band + 2, PAD, slice_lanes), BF16),
                vmem((3, pixels, half), F32),
                vmem((2, 2, maps_here, PAD // 2, half), F32),
                vmem((4, 2, maps_here, PAD // 2, half), F32),
                vmem((half // 128, PAD, 128), F32),
                vmem((2, maps_here, PAD // 2, half), BF16),
                vmem((2, maps_here, rows_here, PAD, half), F32),
                vmem((rounds, chips, 8, half), F32),
                vmem((rounds, PLANE, 8, half), F32),
                vmem((maps_here, PLANE, 8, half), F32),
                vmem((PLANE, 8, half), F32),
                vmem((2, 8, half), F32),
                vmem((8, half), F32),
                vmem((LAYERS, 8, half), F32),
                vmem((LAYERS, 8, half), F32),
                vmem((1, 8, half), F32),
                vmem((1, 8, half), F32),
                vmem((8, half), F32),
                dma((LAYERS, 3)),
                dma((6,)),
                dma((6,)),
                dma((3,)),
                dma((3,)),
                dma((rounds, chips)),
                dma((rounds, chips)),
                dma((rounds, PLANE)),
                dma((rounds, PLANE)),
                dma((LAYERS, 2)),
                dma((LAYERS, 2)),
                dma((LAYERS, 2)),
                dma((LAYERS, 2)),
                dma((LAYERS,)),
                dma((LAYERS,)),
                dma((LAYERS,)),
                dma((LAYERS,)),
                dma((3,)),
                dma((3,)),
                dma((3,)),
                dma((LAYERS, PLANE)),
                dma((LAYERS, PLANE)),
                dma((LAYERS, PLANE)),
                dma((LAYERS, PLANE)),
            ],
            compiler_params=pltpu.CompilerParams(
                collective_id=0,
                has_side_effects=True,
                vmem_limit_bytes=63 * 1024 * 1024,
            ),
        )(
            block_input,
            conv_weights,
            norm_gains,
            norm_shifts,
            map_width,
            map_group,
            pool_index,
            task_mask,
            task_weights,
            task_grads,
        )
        kg = pl.pallas_call(
            functools.partial(reduce_kernel, chips),
            out_shape=jax.ShapeDtypeStruct((UNITS, channels, channels), BF16),
            in_specs=[whole],
            out_specs=anywhere,
            scratch_shapes=[
                vmem((UNITS, chips - 1, piece, slice_lanes), BF16),
                vmem((UNITS, piece, slice_lanes), BF16),
                dma((UNITS, owners)),
                dma((UNITS, chips - 1)),
                dma((UNITS, chips)),
                dma((UNITS, owners)),
                dma((UNITS, 2)),
                dma((UNITS, 2)),
                dma((UNITS,)),
                dma((UNITS,)),
                dma((UNITS,)),
                dma((UNITS,)),
                dma((UNITS,)),
            ],
            compiler_params=pltpu.CompilerParams(
                collective_id=1,
                has_side_effects=True,
                vmem_limit_bytes=32 * 1024 * 1024,
            ),
        )(terms)
        pooled = jnp.concatenate([pooled[0], pooled[1]], -1)[:, None, :pooled_columns]
        input_grad = jnp.concatenate([ig[0], ig[1]], -1)[:, :, :columns]
        sums = jnp.concatenate([sums[0], sums[1]], -1)
        return (
            pooled,
            input_grad,
            kg.astype(F32).reshape(conv_weights.shape),
            sums[:LAYERS],
            sums[LAYERS : 2 * LAYERS],
        )

    return jax.shard_map(
        per_device,
        mesh=mesh,
        in_specs=(
            P("maps", "rows", None, None),
            P(),
            P(),
            P(),
            P(),
            P(),
            P("maps", "rows", None, None),
            P("maps", None),
            P(),
            P(None, "maps", "rows", None, None),
        ),
        out_specs=(P("maps", "rows", None, None), P("maps", "rows", None, None), P(), P(), P()),
        check_vma=False,
    )
```

```python
import functools

import jax
import jax.numpy as jnp
from jax import lax
from jax.experimental import pallas as pl
from jax.experimental.pallas import tpu as pltpu
from jax.sharding import PartitionSpec as P

MESH = pl.DeviceIdType.MESH
epsilon = 1e-05
PAD = 64
LAYERS = 3
TAPS = 9
UNITS = LAYERS * TAPS
PLANE = 4
LAG = 2
F32 = jnp.float32
BF16 = jnp.bfloat16


def each(first, last, body):
    if last - first <= 8:
        for k in range(first, last):
            body(k)
    else:
        lax.fori_loop(first, last, lambda k, s: (body(k), s)[1], 0)


def block_kernel(
    chips,
    height,
    x_ref,
    w_ref,
    gain_ref,
    shift_ref,
    width_ref,
    group_ref,
    index_ref,
    tmask_ref,
    tweight_ref,
    tgrad_ref,
    pooled_ref,
    ig_ref,
    kg_ref,
    sums_ref,
    wa,
    wb,
    act_own,
    act_oth,
    act_t,
    zbuf,
    zs,
    zh,
    dh,
    dhs,
    dhh,
    dyb,
    dz_own,
    dz_oth,
    dzr,
    dzv,
    prod,
    gsrc,
    gbuf,
    hrow,
    pbuf,
    igbuf,
    st1,
    st2,
    coef,
    nall,
    inv_t,
    cnt_t,
    avg_t,
    scl_t,
    mean_t,
    tb_t,
    ta_t,
    sums_own,
    terms,
    r2,
    r3,
    fin,
    w_sem,
    x_s,
    x_r,
    g_s,
    g_r,
    st1_s,
    st1_r,
    st2_s,
    st2_r,
    zh_s,
    zh_r,
    dh_s,
    dh_r,
    act_s,
    act_r,
    dz_s,
    dz_r,
    out_s,
    out_r,
    out_l,
    at_s,
    at_r,
    dzr_s,
    dzr_r,
    r2_s,
    r2_r,
    r3_s,
    r3_r,
    az_s,
    az_r,
    ab_s,
    ab_r,
    aa_s,
    aa_r,
    ap_s,
    ap_r,
    loc_s,
):
    maps_here = x_ref.shape[0]
    columns = x_ref.shape[2]
    half = x_ref.shape[3] // 2
    tasks = tgrad_ref.shape[0]
    pooled_columns = tgrad_ref.shape[3]
    lanes = half // 128
    tiles = [slice(n * 128, (n + 1) * 128) for n in range(lanes)]
    band = 4
    pixels = maps_here * band * PAD
    owners = min(chips, 8)
    piece = (half // 2) // owners
    m = lax.axis_index("maps")
    r = lax.axis_index("rows")
    c = lax.rem(r, 2)
    z = lax.div(r, 2)
    other = 1 - c
    first_map = m * maps_here
    x_bit = lax.rem(m, 2)
    y_bit = lax.div(m, 2)
    x_peer = m + 1 - 2 * x_bit
    y_peer = m + 2 - 4 * y_bit
    g_bit = (1 - c) * x_bit + c * y_bit
    h_bit = (1 - c) * y_bit + c * x_bit
    g_peer = (1 - c) * x_peer + c * y_peer
    h_peer = (1 - c) * y_peer + c * x_peer
    up_there = z > 0
    down_there = z < chips - 1
    row8 = lax.broadcasted_iota(jnp.int32, (8, half), 0)
    column = lax.broadcasted_iota(jnp.int32, (PAD, half), 0)

    def remote(src, dst, send, recv, mm, zz, cc):
        return pltpu.make_async_remote_copy(
            src_ref=src,
            dst_ref=dst,
            send_sem=send,
            recv_sem=recv,
            device_id=(mm, zz * 2 + cc),
            device_id_type=MESH,
        )

    def own_half(v):
        return jnp.where(c == 0, v[..., :half], v[..., half:])

    def width_of(a):
        return width_ref[first_map + a]

    own_at = pl.ds(pl.multiple_of(c * half, half), half)
    oth_at = pl.ds(pl.multiple_of(other * half, half), half)

    def weight_copy(l, n):
        dst = (wa, wb, wb)[n]
        k_at, o_at = ((own_at, own_at), (oth_at, own_at), (own_at, oth_at))[n]
        return pltpu.make_async_copy(w_ref.at[l, :, :, k_at, o_at], dst.at[l], w_sem.at[l, n])

    for l in range(LAYERS):
        weight_copy(l, 0).start()
        weight_copy(l, 1).start()

    barrier = pltpu.get_barrier_semaphore()

    def greet(k):
        rr = lax.rem(r + k, 2 * chips)
        pl.semaphore_signal(barrier, inc=1, device_id=(m, rr), device_id_type=MESH)

    each(1, 2 * chips, greet)
    for k in range(1, PLANE):
        pl.semaphore_signal(
            barrier, inc=1, device_id=(lax.rem(m + k, PLANE), r), device_id_type=MESH
        )

    mine = pl.ds(1 + 2 * c, 2)
    for a in range(maps_here):
        inside = lax.broadcasted_iota(jnp.int32, (columns, 2 * half), 0) < width_of(a)
        for rr in range(2):
            v = jnp.where(inside, x_ref[a, rr].astype(F32), 0.0).astype(BF16)
            spot = 1 + 2 * c + rr
            act_own[0, a, spot, pl.ds(48, 16), :] = jnp.zeros((16, half), BF16)
            act_oth[0, a, spot, pl.ds(48, 16), :] = jnp.zeros((16, half), BF16)
            act_own[0, a, spot, pl.ds(0, columns), :] = own_half(v)
            act_oth[0, a, spot, pl.ds(0, columns), :] = jnp.where(
                c == 0, v[:, half:], v[:, :half]
            )

    @pl.when(z == 0)
    def _():
        act_own[0, :, 0] = jnp.zeros((maps_here, PAD, half), BF16)
        act_oth[0, :, 0] = jnp.zeros((maps_here, PAD, half), BF16)

    @pl.when(z == chips - 1)
    def _():
        act_own[0, :, 5] = jnp.zeros((maps_here, PAD, half), BF16)
        act_oth[0, :, 5] = jnp.zeros((maps_here, PAD, half), BF16)

    gsrc[...] = jnp.zeros(gsrc.shape, F32)
    for a in range(maps_here):
        total = None
        for t in range(tasks):
            scale = tweight_ref[t] * tmask_ref[a, t].astype(F32)
            term = tgrad_ref[t, a, 0].astype(F32) * scale
            total = term if total is None else total + term
        position = index_ref[a, 0].astype(F32)
        for h in range(2):
            gsrc[h, 0, a, pl.ds(0, pooled_columns), :] = total[:, h * half : (h + 1) * half]
            gsrc[h, 1, a, pl.ds(0, pooled_columns), :] = position[:, h * half : (h + 1) * half]
    gbuf[1 + c] = gsrc[c]

    pl.semaphore_wait(barrier, 2 * chips - 1 + PLANE - 1)

    x_partner = (
        remote(act_own.at[0, :, mine], act_oth.at[0, :, mine], x_s.at[0], x_r.at[0], m, z, other),
        remote(act_oth.at[0, :, mine], act_own.at[0, :, mine], x_s.at[1], x_r.at[1], m, z, other),
    )
    g_partner = remote(gsrc.at[other], gbuf.at[1 + c], g_s.at[0], g_r.at[0], m, z, other)

    def x_halo(n, src_row, dst_row, zz):
        cc = (c, c, other, other, c, other)[n]
        low = dst_row == band + 1
        if n >= 4:
            src, dst = gsrc.at[cc], gbuf.at[3 if low else 0]
            return remote(src, dst, g_s.at[n - 3], g_r.at[1 if low else 2], m, zz, cc)
        src = (act_own, act_oth, act_own, act_oth)[n].at[0, :, src_row]
        dst = (act_own, act_oth, act_oth, act_own)[n].at[0, :, dst_row]
        return remote(src, dst, x_s.at[2 + n], x_r.at[(2 if low else 4) + n % 2], m, zz, cc)

    for copy in x_partner:
        copy.start()

    @pl.when(jnp.logical_and(c == 0, up_there))
    def _():
        for n in range(4):
            x_halo(n, 1, 5, z - 1).start()

    @pl.when(jnp.logical_and(c == 1, down_there))
    def _():
        for n in range(4):
            x_halo(n, 4, 0, z + 1).start()

    g_partner.start()

    @pl.when(jnp.logical_and(c == 0, up_there))
    def _():
        for n in range(4, 6):
            x_halo(n, 1, 5, z - 1).start()

    @pl.when(jnp.logical_and(c == 1, down_there))
    def _():
        for n in range(4, 6):
            x_halo(n, 4, 0, z + 1).start()

    for mm in range(PLANE):
        sizes = jnp.zeros((8, half), F32)
        for b in range(maps_here):
            sizes = jnp.where(
                row8 == b, (width_ref[mm * maps_here + b] * height).astype(F32), sizes
            )
        nall[mm] = sizes
    inside_sizes = jnp.zeros((8, half), F32)
    for b in range(maps_here):
        inside_sizes = jnp.where(row8 == b, (width_of(b) * band).astype(F32), inside_sizes)
    inv_t[0] = inside_sizes
    inv_t[1] = jnp.where(row8 < maps_here, 1.0 / jnp.maximum(inside_sizes, 1.0), 0.0)
    counts = jnp.ones((8, half), F32)
    for a in range(maps_here):
        total = jnp.zeros((1, half), F32)
        for mm in range(PLANE):
            same = jnp.zeros((8, half), F32)
            for b in range(maps_here):
                alike = group_ref[first_map + a] == group_ref[mm * maps_here + b]
                same = jnp.where(row8 == b, jnp.where(alike, 1.0, 0.0), same)
            coef[a, mm] = same
            total = total + jnp.sum(same * nall[mm], 0, keepdims=True)
        counts = jnp.where(row8 == a, total, counts)
    cnt_t[...] = counts

    def z_copy(e, k):
        zz = lax.rem(z + k, chips)
        return remote(st1.at[e, z], st1.at[e, z], st1_s.at[e, k], st1_r.at[e, z], m, zz, c)

    def z_arrival(e, k):
        zz = lax.rem(z + k, chips)
        return remote(st1.at[e, zz], st1.at[e, zz], st1_s.at[e, k], st1_r.at[e, zz], m, zz, c)

    def m_copy(e, k):
        mm = lax.rem(m + k, PLANE)
        return remote(st2.at[e, m], st2.at[e, m], st2_s.at[e, k], st2_r.at[e, m], mm, z, c)

    def m_arrival(e, k):
        mm = lax.rem(m + k, PLANE)
        return remote(st2.at[e, mm], st2.at[e, mm], st2_s.at[e, k], st2_r.at[e, mm], mm, z, c)

    def send_z(e, tile):
        st1[e, z] = tile
        each(1, chips, lambda k: z_copy(e, k).start())

    def wait_z(e):
        each(1, chips, lambda k: z_arrival(e, k).wait_recv())

    def send_m(e, tile):
        st2[e, m] = tile
        each(1, PLANE, lambda k: m_copy(e, k).start())

    def wait_m(e):
        each(1, PLANE, lambda k: m_arrival(e, k).wait_recv())

    def products(source, l, taps, kernel, transposed, fresh):
        starts = [2 - i if transposed else i for i in taps]
        lhs = jnp.concatenate(
            [source[l, :, s : s + band].reshape(pixels, half) for s in starts], 1
        )
        for j in range(3):
            rhs = jnp.concatenate([kernel[l, i, j] for i in taps], 1 if transposed else 0)
            got = lax.dot_general(
                lhs,
                rhs,
                (((1,), (1 if transposed else 0,)), ((), ())),
                preferred_element_type=F32,
            )
            if fresh:
                prod[j] = got
            else:
                prod[j] = prod[j] + got

    def shifted(a, rr, before, behind, n):
        rows = pl.ds(pl.multiple_of((a * band + rr) * PAD, PAD), PAD)
        return (
            prod[1, rows, n]
            + pltpu.roll(prod[before, rows, n], 1, 0)
            + pltpu.roll(prod[behind, rows, n], PAD - 1, 0)
        )

    def row_of(table, l, a):
        return table[l, pl.ds(a, 1), :]

    def gain_of(l):
        return own_half(gain_ref[pl.ds(l, 1), :])

    def shift_of(l):
        return own_half(shift_ref[pl.ds(l, 1), :])

    def limit(a, rr):
        w = width_of(a)
        if rr == 0:
            return jnp.where(up_there, w, 0)
        if rr == band + 1:
            return jnp.where(down_there, w, 0)
        return w

    def z_halo(l, way):
        there = z - 1 + 2 * way
        return remote(zs.at[way], zh.at[l, 1 - way], zh_s.at[l, way], zh_r.at[l, way], m, there, c)

    def dh_halo(l, way):
        there = z - 1 + 2 * way
        return remote(dhs.at[way], dhh.at[l, 1 - way], dh_s.at[l, way], dh_r.at[l, way], m, there, c)

    def start_halo(halo, l):
        @pl.when(up_there)
        def _():
            halo(l, 0).start()

        @pl.when(down_there)
        def _():
            halo(l, 1).start()

    def wait_halo(halo, l):
        @pl.when(up_there)
        def _():
            halo(l, 1).wait_recv()
            halo(l, 0).wait_send()

        @pl.when(down_there)
        def _():
            halo(l, 0).wait_recv()
            halo(l, 1).wait_send()

    def act_copy(l):
        return remote(act_own.at[l], act_oth.at[l], act_s.at[l], act_r.at[l], m, z, other)

    def at_copy(l):
        return remote(act_t.at[l, 0], act_t.at[l, 1], at_s.at[l], at_r.at[l], g_peer, z, c)

    def dzr_copy(l, source):
        return remote(source.at[l], dzr.at[l], dzr_s.at[l], dzr_r.at[l], g_peer, z, c)

    def dz_copy(l):
        return remote(dz_own.at[l], dz_oth.at[l], dz_s.at[l], dz_r.at[l], m, z, other)

    def wait_x_halo(first, last):
        @pl.when(up_there)
        def _():
            for n in (0, 1, 4)[first:last]:
                x_halo(n, 4, 0, z - 1).wait_recv()

        @pl.when(down_there)
        def _():
            for n in (0, 1, 4)[first:last]:
                x_halo(n, 1, 5, z + 1).wait_recv()

    def sent_x_halo():
        @pl.when(jnp.logical_and(c == 0, up_there))
        def _():
            for n in range(6):
                x_halo(n, 1, 5, z - 1).wait_send()

        @pl.when(jnp.logical_and(c == 1, down_there))
        def _():
            for n in range(6):
                x_halo(n, 4, 0, z + 1).wait_send()

    def forward(l, first):
        weight_copy(l, 0).wait()
        weight_copy(l, 1).wait()
        if first:
            for copy in x_partner:
                copy.wait_recv()
            products(act_own, l, (1,), wa, False, True)
            products(act_oth, l, (1,), wb, False, False)
            wait_x_halo(0, 2)
            products(act_own, l, (0, 2), wa, False, False)
            products(act_oth, l, (0, 2), wb, False, False)
        else:
            products(act_own, l, (0, 1, 2), wa, False, True)
            act_copy(l).wait_recv()
            products(act_oth, l, (0, 1, 2), wb, False, False)
        weight_copy(l, 2).start()

        def collect(a, tile):
            inside = column[:, :128] < width_of(a)
            pixels_inside = (width_of(a) * band).astype(F32)
            totals, squares = [], []
            for n in tiles:
                total = jnp.zeros((PAD, 128), F32)
                for rr in range(band):
                    v = shifted(a, rr, 0, 2, n)
                    zbuf[l, a, 1 + rr, :, n] = v
                    total = total + jnp.where(inside, v, 0.0)
                total = jnp.sum(total, 0, keepdims=True)
                mean = total / pixels_inside
                square = jnp.zeros((PAD, 128), F32)
                for rr in range(band):
                    v = jnp.where(inside, zbuf[l, a, 1 + rr, :, n] - mean, 0.0)
                    square = square + v * v
                    if rr in (0, band - 1):
                        zs[rr // (band - 1), a, :, n] = v.astype(BF16)
                totals.append(total)
                squares.append(jnp.sum(square, 0, keepdims=True))
            tile = jnp.where(row8 == a, jnp.concatenate(totals, 1), tile)
            return jnp.where(row8 == a + maps_here, jnp.concatenate(squares, 1), tile)

        tile = lax.fori_loop(0, maps_here, collect, jnp.zeros((8, half), F32))
        send_z(l, tile)
        start_halo(z_halo, l)
        act_t[l, 0] = act_own[l, :, 1 : 1 + band].reshape(pixels, half).T
        wait_z(l)
        sizes, inverse = inv_t[0], inv_t[1]
        mean_t[0] = st1[l, jnp.maximum(z - 1, 0)] * inverse
        mean_t[1] = st1[l, jnp.minimum(z + 1, chips - 1)] * inverse
        total = st1[l, 0]
        for zz in range(1, chips):
            total = total + st1[l, zz]
        mean = total * inverse * (1.0 / chips)
        square = jnp.zeros((8, half), F32)
        for zz in range(chips):
            v = st1[l, zz]
            gap = v * inverse - mean
            square = square + pltpu.roll(v, 8 - maps_here, 0) + sizes * gap * gap
        tile = jnp.where(row8 < maps_here, mean, pltpu.roll(square, maps_here, 0))
        send_m(l, jnp.where(row8 < 2 * maps_here, tile, 0.0))
        wait_m(l)
        at_copy(l).start()
        averages = jnp.zeros((8, half), F32)
        scalings = jnp.zeros((8, half), F32)
        for a in range(maps_here):
            count = cnt_t[a : a + 1, :]
            average = jnp.zeros((8, half), F32)
            for mm in range(PLANE):
                average = average + coef[a, mm] * nall[mm] * st2[l, mm]
            average = jnp.sum(average, 0, keepdims=True) / count
            variance = jnp.zeros((8, half), F32)
            for mm in range(PLANE):
                v = st2[l, mm]
                gap = v - average
                variance = variance + coef[a, mm] * (
                    pltpu.roll(v, 8 - maps_here, 0) + nall[mm] * gap * gap
                )
            variance = jnp.sum(variance, 0, keepdims=True) / count
            averages = jnp.where(row8 == a, average, averages)
            scalings = jnp.where(row8 == a, lax.rsqrt(variance + epsilon), scalings)
        avg_t[l] = averages
        scl_t[l] = scalings
        wait_halo(z_halo, l)

        def activate(a, s):
            gain, shift = gain_of(l), shift_of(l)
            for n in tiles:
                average = row_of(avg_t, l, a)[:, n]
                factor = row_of(scl_t, l, a)[:, n] * gain[:, n]
                for rr in range(band + 2):
                    if rr in (0, band + 1):
                        way = rr // (band + 1)
                        v = zh[l, way, a, :, n].astype(F32) + row_of(mean_t, way, a)[:, n]
                        zbuf[l, a, rr, :, n] = v
                    else:
                        v = zbuf[l, a, rr, :, n]
                    y = (v - average) * factor + shift[:, n]
                    h = jnp.where(column[:, n] < limit(a, rr), y * jax.nn.sigmoid(y), 0.0)
                    act_own[l + 1, a, rr, :, n] = h.astype(BF16)
            return s

        lax.fori_loop(0, maps_here, activate, 0)

        if first:
            act_copy(l + 1).start()
        else:

            @pl.when(l < LAYERS - 1)
            def _():
                act_copy(l + 1).start()

    forward(0, True)
    lax.fori_loop(1, LAYERS, lambda l, s: (forward(l, False), s)[1], 0)
    g_partner.wait_recv()
    wait_x_halo(2, 3)

    def unpool(a, s):
        for rr in range(band + 2):
            slot, lower = (rr + 1) // 2, (rr + 1) % 2
            g = gbuf[slot, 0, a]
            position = gbuf[slot, 1, a]
            for b in range(2):
                v = jnp.where(position == float(2 * lower + b), g, 0.0)
                for n in range(lanes):
                    hrow[n, pl.ds(b, PAD // 2, stride=2), :] = v[:, n * 128 : (n + 1) * 128]
            v = jnp.concatenate([hrow[n] for n in range(lanes)], 1)
            if rr in (0, band + 1):
                dhh[LAYERS - 1, rr // (band + 1), a] = v.astype(BF16)
            else:
                dh[a, rr - 1] = v
        return s

    lax.fori_loop(0, maps_here, unpool, 0)

    def pool():
        def one(a, s):
            for pr in range(2):
                total = jnp.zeros((PAD // 2, half), F32)
                position = gbuf[1 + pr, 1, a]
                for lower in range(2):
                    v = act_own[LAYERS, a, 1 + 2 * pr + lower].astype(F32)
                    for n in range(lanes):
                        hrow[n] = v[:, n * 128 : (n + 1) * 128]
                    for b in range(2):
                        v = jnp.concatenate(
                            [hrow[n, pl.ds(b, PAD // 2, stride=2), :] for n in range(lanes)], 1
                        )
                        total = total + jnp.where(position == float(2 * lower + b), v, 0.0)
                pbuf[pr, a] = total.astype(BF16)
            return s

        lax.fori_loop(0, maps_here, one, 0)

    def second_rows(bit):
        return pl.ds(pl.multiple_of(bit * (half // 2), half // 2), half // 2)

    def piece_rows(p):
        return pl.ds(pl.multiple_of(p * piece, piece), piece)

    def c2(q):
        return remote(
            terms.at[q, second_rows(1 - h_bit)], r2.at[q], r2_s.at[q], r2_r.at[q], h_peer, z, c
        )

    def c3(q, p):
        slot = lax.rem(z - p + chips - 1, chips)
        return remote(
            r2.at[q, piece_rows(p)], r3.at[q, slot], r3_s.at[q, p], r3_r.at[q, slot], m, p, c
        )

    def unit_of(q):
        k = lax.div(q, TAPS)
        return (LAYERS - 1 - k) * TAPS + (q - k * TAPS)

    def region(q, start, size, lane, lanes):
        start = pl.multiple_of(c * half + start, piece)
        lane = pl.multiple_of(lane, half)
        return kg_ref.at[unit_of(q), pl.ds(start, size), pl.ds(lane, lanes)]

    def cz(q, p, zz):
        part = region(q, h_bit * (half // 2) + p * piece, piece, g_bit * half, half)
        return remote(fin.at[q], part, az_s.at[q, zz], az_r.at[q, p], m, zz, c)

    def cl(q):
        part = region(q, h_bit * (half // 2) + z * piece, piece, g_bit * half, half)
        return pltpu.make_async_copy(fin.at[q], part, loc_s.at[q])

    def cb(q):
        part = region(q, h_bit * (half // 2), half // 2, g_bit * half, half)
        return remote(part, part, ab_s.at[q], ab_r.at[q], h_peer, z, c)

    def ca(q):
        part = region(q, 0, half, g_bit * half, half)
        return remote(part, part, aa_s.at[q], aa_r.at[q], g_peer, z, c)

    def cp(q):
        part = region(q, 0, half, 0, 2 * half)
        return remote(part, part, ap_s.at[q], ap_r.at[q], m, z, other)

    def variants(l):
        def one(a, s):
            for chip in range(2):
                for rr in range(band + 2):
                    for n in tiles:
                        if chip == 0:
                            v = jnp.where(g_bit == c, dz_own[l, a, rr, :, n], dz_oth[l, a, rr, :, n])
                        else:
                            v = dzr[l, a, rr, :, n]
                        dzv[1, chip, a, rr, :, n] = v
                        v = v.astype(F32)
                        dzv[0, chip, a, rr, :, n] = pltpu.roll(v, PAD - 1, 0).astype(BF16)
                        dzv[2, chip, a, rr, :, n] = pltpu.roll(v, 1, 0).astype(BF16)
            return s

        lax.fori_loop(0, maps_here, one, 0)

    def ready_terms(l):
        at_copy(l).wait_recv()
        dzr_copy(l, dz_own).wait_recv()
        variants(l)

    def weight_terms(l, first, last):
        def one(t, s):
            i = lax.div(t, 3)
            j = t - 3 * i
            lhs = jnp.concatenate([act_t[l, 0], act_t[l, 1]], 1)
            rhs = dzv[j, :, :, pl.ds(2 - i, band)].reshape(2 * pixels, half)
            q = (LAYERS - 1 - l) * TAPS + t
            terms[q] = jnp.dot(lhs, rhs, preferred_element_type=F32).astype(BF16)
            c2(q).start()
            return s

        lax.fori_loop(first, last, one, 0)

    def stage_second(q):
        c2(q).wait_recv()
        r2[q] = (r2[q].astype(F32) + terms[q, second_rows(h_bit)].astype(F32)).astype(BF16)

        def give(k):
            p = lax.rem(z + k, chips)

            @pl.when(p < owners)
            def _():
                c3(q, p).start()

        each(1, chips, give)

    def stage_sum(q):
        @pl.when(z < owners)
        def _():
            for k in range(chips - 1):
                remote(
                    r3.at[q, k], r3.at[q, k], r3_s.at[q, 0], r3_r.at[q, k], m, z, c
                ).wait_recv()
            total = r2[q, piece_rows(z)].astype(F32)
            for k in range(chips - 1):
                total = total + r3[q, k].astype(F32)
            fin[q] = total.astype(BF16)
            each(1, chips, lambda k: cz(q, z, lax.rem(z + k, chips)).start())
            cl(q).start()

    def stage_back(q):
        def arrived(k):
            p = lax.rem(z + k, chips)

            @pl.when(p < owners)
            def _():
                cz(q, p, p).wait_recv()

        each(1, chips, arrived)

        @pl.when(z < owners)
        def _():
            cl(q).wait()

        cb(q).start()

    def stage_first(q):
        cb(q).wait_recv()
        ca(q).start()

    def stage_chip(q):
        ca(q).wait_recv()
        cp(q).start()

    def run(stage, first, last):
        lax.fori_loop(first, last, lambda q, s: (stage(q), s)[1], 0)

    def backward(k, carry):
        l = LAYERS - 1 - k
        gain, shift = gain_of(l), shift_of(l)

        def gradient(a, rr, n):
            zhat = (zbuf[l, a, rr, :, n] - row_of(avg_t, l, a)[:, n]) * row_of(scl_t, l, a)[:, n]
            y = zhat * gain[:, n] + shift[:, n]
            s = jax.nn.sigmoid(y)
            if rr in (0, band + 1):
                upstream = dhh[l, rr // (band + 1), a, :, n].astype(F32)
            else:
                upstream = dh[a, rr - 1, :, n]
            dy = upstream * (s * (1.0 + y * (1.0 - s)))
            dy = jnp.where(column[:, n] < limit(a, rr), dy, 0.0)
            dyb[a, rr, :, n] = dy
            return dy, zhat

        def collect(a, tile):
            plains, crosses = [], []
            for n in tiles:
                plain = jnp.zeros((PAD, 128), F32)
                crossed = jnp.zeros((PAD, 128), F32)
                for rr in range(1, band + 1):
                    dy, zhat = gradient(a, rr, n)
                    plain = plain + dy
                    crossed = crossed + dy * zhat
                plains.append(jnp.sum(plain, 0, keepdims=True))
                crosses.append(jnp.sum(crossed, 0, keepdims=True))
            tile = jnp.where(row8 == a, jnp.concatenate(plains, 1), tile)
            return jnp.where(row8 == a + maps_here, jnp.concatenate(crosses, 1), tile)

        e = LAYERS + l
        tile = lax.fori_loop(0, maps_here, collect, jnp.zeros((8, half), F32))
        send_z(e, tile)

        @pl.when(k == LAYERS - 1)
        def _():
            run(stage_second, 0, TAPS)

        @pl.when(k > 0)
        def _():
            ready_terms(l + 1)
            weight_terms(l + 1, 0, 4)

        wait_z(e)
        total = st1[e, 0]
        for zz in range(1, chips):
            total = total + st1[e, zz]
        send_m(e, total)

        @pl.when(k > 0)
        def _():
            weight_terms(l + 1, 4, TAPS)
            wait_halo(dh_halo, l)

        @pl.when(k == 0)
        def _():
            pool()

        def edges(a, s):
            for n in tiles:
                gradient(a, 0, n)
                gradient(a, band + 1, n)
            return s

        lax.fori_loop(0, maps_here, edges, 0)
        wait_m(e)
        total = st2[e, 0]
        for mm in range(1, PLANE):
            total = total + st2[e, mm]
        sums_own[pl.ds(l, 1), :] = jnp.sum(
            jnp.where(row8 >= maps_here, total, 0.0), 0, keepdims=True
        )
        sums_own[pl.ds(LAYERS + l, 1), :] = jnp.sum(
            jnp.where(row8 < maps_here, total, 0.0), 0, keepdims=True
        )
        plains = jnp.zeros((8, half), F32)
        crosses = jnp.zeros((8, half), F32)
        for a in range(maps_here):
            plain = jnp.zeros((8, half), F32)
            crossed = jnp.zeros((8, half), F32)
            for mm in range(PLANE):
                v = st2[e, mm]
                plain = plain + coef[a, mm] * v
                crossed = crossed + coef[a, mm] * pltpu.roll(v, 8 - maps_here, 0)
            count = cnt_t[a : a + 1, :]
            plain = gain * (jnp.sum(plain, 0, keepdims=True) / count)
            crossed = gain * (jnp.sum(crossed, 0, keepdims=True) / count)
            plains = jnp.where(row8 == a, plain, plains)
            crosses = jnp.where(row8 == a, crossed, crosses)
        tb_t[0] = plains
        ta_t[0] = crosses

        def settle(a, s):
            for n in tiles:
                average, scaling = row_of(avg_t, l, a)[:, n], row_of(scl_t, l, a)[:, n]
                plain, crossed = row_of(tb_t, 0, a)[:, n], row_of(ta_t, 0, a)[:, n]
                for rr in range(band + 2):
                    zhat = (zbuf[l, a, rr, :, n] - average) * scaling
                    v = scaling * (dyb[a, rr, :, n] * gain[:, n] - plain - zhat * crossed)
                    v = jnp.where(column[:, n] < limit(a, rr), v, 0.0)
                    dz_own[l, a, rr, :, n] = v.astype(BF16)
            return s

        lax.fori_loop(0, maps_here, settle, 0)
        dz_copy(l).start()

        @pl.when(g_bit != c)
        def _():
            dzr_copy(l, dz_own).start()

        products(dz_own, l, (0, 1, 2), wa, True, True)
        weight_copy(l, 2).wait()
        dz_copy(l).wait_recv()

        @pl.when(g_bit == c)
        def _():
            dzr_copy(l, dz_oth).start()

        products(dz_oth, l, (0, 1, 2), wb, True, False)

        def gather(a, s):
            for n in tiles:
                for rr in range(band):
                    v = shifted(a, rr, 2, 0, n)
                    dh[a, rr, :, n] = v
                    if rr in (0, band - 1):
                        dhs[rr // (band - 1), a, :, n] = v.astype(BF16)
            return s

        lax.fori_loop(0, maps_here, gather, 0)

        @pl.when(l > 0)
        def _():
            start_halo(dh_halo, l - 1)

        return carry

    lax.fori_loop(0, LAYERS, backward, 0)
    run(stage_sum, 0, TAPS)
    ready_terms(0)
    weight_terms(0, 0, TAPS)

    def input_rows(a, s):
        for rr in range(band):
            igbuf[rr // 2, a, rr % 2] = jnp.where(
                column < width_of(a), dh[a, rr], 0.0
            )
        return s

    lax.fori_loop(0, maps_here, input_rows, 0)

    outs = (
        (
            remote(igbuf.at[other], ig_ref.at[c], out_s.at[0], out_r.at[0], m, z, other),
            pltpu.make_async_copy(igbuf.at[c], ig_ref.at[c], out_l.at[0]),
        ),
        (
            remote(pbuf.at[other], pooled_ref.at[c], out_s.at[1], out_r.at[1], m, z, other),
            pltpu.make_async_copy(pbuf.at[c], pooled_ref.at[c], out_l.at[1]),
        ),
        (
            remote(sums_own, sums_ref.at[c], out_s.at[2], out_r.at[2], m, z, other),
            pltpu.make_async_copy(sums_own, sums_ref.at[c], out_l.at[2]),
        ),
    )
    for there, here in outs:
        there.start()
        here.start()

    def drain(s, carry):
        for stage, first, lag in (
            (stage_chip, 0, 2 * LAG),
            (stage_first, 0, LAG),
            (stage_back, 0, 0),
            (stage_sum, TAPS, LAG),
            (stage_second, TAPS, 0),
        ):
            q = first + s - lag

            @pl.when(jnp.logical_and(q >= first, q < UNITS))
            def _(stage=stage, q=q):
                stage(q)

        return carry

    lax.fori_loop(0, UNITS + 2 * LAG, drain, 0)

    def finish(q, carry):
        cp(q).wait()
        ca(q).wait_send()
        cb(q).wait_send()
        c2(q).wait_send()

        def given(k):
            p = lax.rem(z + k, chips)

            @pl.when(p < owners)
            def _():
                c3(q, p).wait_send()

        each(1, chips, given)

        @pl.when(z < owners)
        def _():
            each(1, chips, lambda k: cz(q, z, lax.rem(z + k, chips)).wait_send())

        return carry

    lax.fori_loop(0, UNITS, finish, 0)
    for copy in x_partner:
        copy.wait_send()
    g_partner.wait_send()
    sent_x_halo()

    def sent(e, carry):
        each(1, chips, lambda k: z_copy(e, k).wait_send())
        each(1, PLANE, lambda k: m_copy(e, k).wait_send())
        return carry

    lax.fori_loop(0, 2 * LAYERS, sent, 0)
    for l in range(LAYERS):
        at_copy(l).wait_send()
        dzr_copy(l, dz_own).wait_send()
    for l in range(1, LAYERS):
        act_copy(l).wait_send()
    for l in range(LAYERS):
        dz_copy(l).wait_send()
    for there, here in outs:
        there.wait()
        here.wait()


def solution(mesh):
    chips = mesh.shape["rows"] // 2

    def per_device(
        block_input,
        conv_weights,
        norm_gains,
        norm_shifts,
        map_width,
        map_group,
        pool_index,
        task_mask,
        task_weights,
        task_grads,
    ):
        maps_here, rows_here, columns, channels = block_input.shape
        pooled_columns = pool_index.shape[2]
        height = rows_here * mesh.shape["rows"]
        half = channels // 2
        band = 2 * rows_here
        pixels = maps_here * band * PAD
        owners = min(chips, 8)
        piece = half // 2 // owners
        rounds = 2 * LAYERS
        slots = 2 * UNITS * (chips - 1) * piece * half + 4 * rounds * chips * 8 * half
        grant = 41 * 1024 * 1024 + slots
        vmem, dma = pltpu.VMEM, pltpu.SemaphoreType.DMA
        tile = (maps_here, band + 2, PAD, half)
        edge = (2, maps_here, PAD, half)
        whole = pl.BlockSpec(memory_space=pltpu.VMEM)
        scalars = pl.BlockSpec(memory_space=pltpu.SMEM)
        anywhere = pl.BlockSpec(memory_space=pl.ANY)
        pooled, ig, kg, sums = pl.pallas_call(
            functools.partial(block_kernel, chips, height),
            out_shape=(
                jax.ShapeDtypeStruct((2, maps_here, PAD // 2, half), BF16),
                jax.ShapeDtypeStruct((2, maps_here, rows_here, PAD, half), F32),
                jax.ShapeDtypeStruct((UNITS, channels, channels), BF16),
                jax.ShapeDtypeStruct((2, 8, half), F32),
            ),
            in_specs=[whole, anywhere, whole, whole, scalars, scalars, whole, scalars, scalars, whole],
            out_specs=[anywhere] * 4,
            scratch_shapes=[
                vmem((LAYERS, 3, 3, half, half), BF16),
                vmem((LAYERS, 3, 3, half, half), BF16),
                vmem((LAYERS + 1,) + tile, BF16),
                vmem((LAYERS,) + tile, BF16),
                vmem((LAYERS, 2, half, pixels), BF16),
                vmem((LAYERS,) + tile, F32),
                vmem(edge, BF16),
                vmem((LAYERS,) + edge, BF16),
                vmem((maps_here, band, PAD, half), F32),
                vmem(edge, BF16),
                vmem((LAYERS,) + edge, BF16),
                vmem(tile, F32),
                vmem((LAYERS,) + tile, BF16),
                vmem((LAYERS,) + tile, BF16),
                vmem((LAYERS,) + tile, BF16),
                vmem((3, 2) + tile, BF16),
                vmem((3, pixels, half), F32),
                vmem((2, 2, maps_here, PAD // 2, half), F32),
                vmem((4, 2, maps_here, PAD // 2, half), F32),
                vmem((half // 128, PAD, 128), F32),
                vmem((2, maps_here, PAD // 2, half), BF16),
                vmem((2, maps_here, rows_here, PAD, half), F32),
                vmem((rounds, chips, 8, half), F32),
                vmem((rounds, PLANE, 8, half), F32),
                vmem((maps_here, PLANE, 8, half), F32),
                vmem((PLANE, 8, half), F32),
                vmem((2, 8, half), F32),
                vmem((8, half), F32),
                vmem((LAYERS, 8, half), F32),
                vmem((LAYERS, 8, half), F32),
                vmem((2, 8, half), F32),
                vmem((1, 8, half), F32),
                vmem((1, 8, half), F32),
                vmem((8, half), F32),
                vmem((UNITS, half, half), BF16),
                vmem((UNITS, half // 2, half), BF16),
                vmem((UNITS, chips - 1, piece, half), BF16),
                vmem((UNITS, piece, half), BF16),
                dma((LAYERS, 3)),
                dma((6,)),
                dma((6,)),
                dma((3,)),
                dma((3,)),
                dma((rounds, chips)),
                dma((rounds, chips)),
                dma((rounds, PLANE)),
                dma((rounds, PLANE)),
                dma((LAYERS, 2)),
                dma((LAYERS, 2)),
                dma((LAYERS, 2)),
                dma((LAYERS, 2)),
                dma((LAYERS,)),
                dma((LAYERS,)),
                dma((LAYERS,)),
                dma((LAYERS,)),
                dma((3,)),
                dma((3,)),
                dma((3,)),
                dma((LAYERS,)),
                dma((LAYERS,)),
                dma((LAYERS,)),
                dma((LAYERS,)),
                dma((UNITS,)),
                dma((UNITS,)),
                dma((UNITS, owners)),
                dma((UNITS, chips - 1)),
                dma((UNITS, chips)),
                dma((UNITS, owners)),
                dma((UNITS,)),
                dma((UNITS,)),
                dma((UNITS,)),
                dma((UNITS,)),
                dma((UNITS,)),
                dma((UNITS,)),
                dma((UNITS,)),
            ],
            compiler_params=pltpu.CompilerParams(
                collective_id=0,
                has_side_effects=True,
                vmem_limit_bytes=grant,
            ),
        )(
            block_input,
            conv_weights,
            norm_gains,
            norm_shifts,
            map_width,
            map_group,
            pool_index,
            task_mask,
            task_weights,
            task_grads,
        )
        pooled = jnp.concatenate([pooled[0], pooled[1]], -1)[:, None, :pooled_columns]
        input_grad = jnp.concatenate([ig[0], ig[1]], -1)[:, :, :columns]
        sums = jnp.concatenate([sums[0], sums[1]], -1)
        return (
            pooled,
            input_grad,
            kg.astype(F32).reshape(conv_weights.shape),
            sums[:LAYERS],
            sums[LAYERS : 2 * LAYERS],
        )

    return jax.shard_map(
        per_device,
        mesh=mesh,
        in_specs=(
            P("maps", "rows", None, None),
            P(),
            P(),
            P(),
            P(),
            P(),
            P("maps", "rows", None, None),
            P("maps", None),
            P(),
            P(None, "maps", "rows", None, None),
        ),
        out_specs=(P("maps", "rows", None, None), P("maps", "rows", None, None), P(), P(), P()),
        check_vma=False,
    )
```

```python
import functools

import jax
import jax.numpy as jnp
from jax import lax
from jax.experimental import pallas as pl
from jax.experimental.pallas import tpu as pltpu
from jax.sharding import PartitionSpec as P

MESH = pl.DeviceIdType.MESH
epsilon = 1e-05
PAD = 64
LAYERS = 3
TAPS = 9
UNITS = LAYERS * TAPS
PLANE = 4
LAG = 4
F32 = jnp.float32
BF16 = jnp.bfloat16


def each(first, last, body):
    if last - first <= 8:
        for k in range(first, last):
            body(k)
    else:
        lax.fori_loop(first, last, lambda k, s: (body(k), s)[1], 0)


def block_kernel(
    chips,
    height,
    x_ref,
    w_ref,
    gain_ref,
    shift_ref,
    width_ref,
    group_ref,
    index_ref,
    tmask_ref,
    tweight_ref,
    tgrad_ref,
    pooled_ref,
    ig_ref,
    kg_ref,
    sums_ref,
    wa,
    wb,
    act_own,
    act_oth,
    act_t,
    zbuf,
    zs,
    zh,
    dh,
    dhs,
    dhh,
    dyb,
    dz_own,
    dz_oth,
    dzr,
    dzv,
    prod,
    gsrc,
    gbuf,
    hrow,
    pbuf,
    igbuf,
    st1,
    st2,
    coef,
    nall,
    inv_t,
    cnt_t,
    avg_t,
    scl_t,
    mean_t,
    tb_t,
    ta_t,
    sums_own,
    terms,
    r2,
    r3,
    fin,
    w_sem,
    x_s,
    x_r,
    g_s,
    g_r,
    st1_s,
    st1_r,
    st2_s,
    st2_r,
    zh_s,
    zh_r,
    dh_s,
    dh_r,
    act_s,
    act_r,
    dz_s,
    dz_r,
    out_s,
    out_r,
    out_l,
    at_s,
    at_r,
    dzr_s,
    dzr_r,
    r2_s,
    r2_r,
    r3_s,
    r3_r,
    az_s,
    az_r,
    ab_s,
    ab_r,
    aa_s,
    aa_r,
    ap_s,
    ap_r,
    loc_s,
):
    maps_here = x_ref.shape[0]
    columns = x_ref.shape[2]
    half = x_ref.shape[3] // 2
    tasks = tgrad_ref.shape[0]
    pooled_columns = tgrad_ref.shape[3]
    lanes = half // 128
    tiles = [slice(n * 128, (n + 1) * 128) for n in range(lanes)]
    band = 4
    pixels = maps_here * band * PAD
    owners = min(chips, 8)
    piece = (half // 2) // owners
    m = lax.axis_index("maps")
    r = lax.axis_index("rows")
    c = lax.rem(r, 2)
    z = lax.div(r, 2)
    other = 1 - c
    first_map = m * maps_here
    x_bit = lax.rem(m, 2)
    y_bit = lax.div(m, 2)
    x_peer = m + 1 - 2 * x_bit
    y_peer = m + 2 - 4 * y_bit
    g_bit = (1 - c) * x_bit + c * y_bit
    h_bit = (1 - c) * y_bit + c * x_bit
    g_peer = (1 - c) * x_peer + c * y_peer
    h_peer = (1 - c) * y_peer + c * x_peer
    up_there = z > 0
    down_there = z < chips - 1
    row8 = lax.broadcasted_iota(jnp.int32, (8, half), 0)
    column = lax.broadcasted_iota(jnp.int32, (PAD, half), 0)

    def remote(src, dst, send, recv, mm, zz, cc):
        return pltpu.make_async_remote_copy(
            src_ref=src,
            dst_ref=dst,
            send_sem=send,
            recv_sem=recv,
            device_id=(mm, zz * 2 + cc),
            device_id_type=MESH,
        )

    def own_half(v):
        return jnp.where(c == 0, v[..., :half], v[..., half:])

    def width_of(a):
        return width_ref[first_map + a]

    own_at = pl.ds(pl.multiple_of(c * half, half), half)
    oth_at = pl.ds(pl.multiple_of(other * half, half), half)

    def weight_copy(l, n):
        dst = (wa, wb, wb)[n]
        k_at, o_at = ((own_at, own_at), (oth_at, own_at), (own_at, oth_at))[n]
        return pltpu.make_async_copy(w_ref.at[l, :, :, k_at, o_at], dst.at[l], w_sem.at[l, n])

    for l in range(LAYERS):
        weight_copy(l, 0).start()
        weight_copy(l, 1).start()

    barrier = pltpu.get_barrier_semaphore()

    def greet(k):
        rr = lax.rem(r + k, 2 * chips)
        pl.semaphore_signal(barrier, inc=1, device_id=(m, rr), device_id_type=MESH)

    each(1, 2 * chips, greet)
    for k in range(1, PLANE):
        pl.semaphore_signal(
            barrier, inc=1, device_id=(lax.rem(m + k, PLANE), r), device_id_type=MESH
        )

    mine = pl.ds(1 + 2 * c, 2)
    for a in range(maps_here):
        inside = lax.broadcasted_iota(jnp.int32, (columns, 2 * half), 0) < width_of(a)
        for rr in range(2):
            v = jnp.where(inside, x_ref[a, rr].astype(F32), 0.0).astype(BF16)
            spot = 1 + 2 * c + rr
            act_own[0, a, spot, pl.ds(48, 16), :] = jnp.zeros((16, half), BF16)
            act_oth[0, a, spot, pl.ds(48, 16), :] = jnp.zeros((16, half), BF16)
            act_own[0, a, spot, pl.ds(0, columns), :] = own_half(v)
            act_oth[0, a, spot, pl.ds(0, columns), :] = jnp.where(
                c == 0, v[:, half:], v[:, :half]
            )

    @pl.when(z == 0)
    def _():
        act_own[0, :, 0] = jnp.zeros((maps_here, PAD, half), BF16)
        act_oth[0, :, 0] = jnp.zeros((maps_here, PAD, half), BF16)

    @pl.when(z == chips - 1)
    def _():
        act_own[0, :, 5] = jnp.zeros((maps_here, PAD, half), BF16)
        act_oth[0, :, 5] = jnp.zeros((maps_here, PAD, half), BF16)

    gsrc[...] = jnp.zeros(gsrc.shape, F32)
    for a in range(maps_here):
        total = None
        for t in range(tasks):
            scale = tweight_ref[t] * tmask_ref[a, t].astype(F32)
            term = tgrad_ref[t, a, 0].astype(F32) * scale
            total = term if total is None else total + term
        position = index_ref[a, 0].astype(F32)
        for h in range(2):
            gsrc[h, 0, a, pl.ds(0, pooled_columns), :] = total[:, h * half : (h + 1) * half]
            gsrc[h, 1, a, pl.ds(0, pooled_columns), :] = position[:, h * half : (h + 1) * half]
    gbuf[1 + c] = gsrc[c]

    pl.semaphore_wait(barrier, 2 * chips - 1 + PLANE - 1)

    x_partner = (
        remote(act_own.at[0, :, mine], act_oth.at[0, :, mine], x_s.at[0], x_r.at[0], m, z, other),
        remote(act_oth.at[0, :, mine], act_own.at[0, :, mine], x_s.at[1], x_r.at[1], m, z, other),
    )
    g_partner = remote(gsrc.at[other], gbuf.at[1 + c], g_s.at[0], g_r.at[0], m, z, other)

    def x_halo(n, src_row, dst_row, zz):
        cc = (c, c, other, other, c, other)[n]
        low = dst_row == band + 1
        if n >= 4:
            src, dst = gsrc.at[cc], gbuf.at[3 if low else 0]
            return remote(src, dst, g_s.at[n - 3], g_r.at[1 if low else 2], m, zz, cc)
        src = (act_own, act_oth, act_own, act_oth)[n].at[0, :, src_row]
        dst = (act_own, act_oth, act_oth, act_own)[n].at[0, :, dst_row]
        return remote(src, dst, x_s.at[2 + n], x_r.at[(2 if low else 4) + n % 2], m, zz, cc)

    for copy in x_partner:
        copy.start()

    @pl.when(jnp.logical_and(c == 0, up_there))
    def _():
        for n in range(4):
            x_halo(n, 1, 5, z - 1).start()

    @pl.when(jnp.logical_and(c == 1, down_there))
    def _():
        for n in range(4):
            x_halo(n, 4, 0, z + 1).start()

    g_partner.start()

    @pl.when(jnp.logical_and(c == 0, up_there))
    def _():
        for n in range(4, 6):
            x_halo(n, 1, 5, z - 1).start()

    @pl.when(jnp.logical_and(c == 1, down_there))
    def _():
        for n in range(4, 6):
            x_halo(n, 4, 0, z + 1).start()

    for mm in range(PLANE):
        sizes = jnp.zeros((8, half), F32)
        for b in range(maps_here):
            sizes = jnp.where(
                row8 == b, (width_ref[mm * maps_here + b] * height).astype(F32), sizes
            )
        nall[mm] = sizes
    inside_sizes = jnp.zeros((8, half), F32)
    for b in range(maps_here):
        inside_sizes = jnp.where(row8 == b, (width_of(b) * band).astype(F32), inside_sizes)
    inv_t[0] = inside_sizes
    inv_t[1] = jnp.where(row8 < maps_here, 1.0 / jnp.maximum(inside_sizes, 1.0), 0.0)
    counts = jnp.ones((8, half), F32)
    for a in range(maps_here):
        total = jnp.zeros((1, half), F32)
        for mm in range(PLANE):
            same = jnp.zeros((8, half), F32)
            for b in range(maps_here):
                alike = group_ref[first_map + a] == group_ref[mm * maps_here + b]
                same = jnp.where(row8 == b, jnp.where(alike, 1.0, 0.0), same)
            coef[a, mm] = same
            total = total + jnp.sum(same * nall[mm], 0, keepdims=True)
        counts = jnp.where(row8 == a, total, counts)
    cnt_t[...] = counts

    def z_copy(e, k):
        zz = lax.rem(z + k, chips)
        return remote(st1.at[e, z], st1.at[e, z], st1_s.at[e, k], st1_r.at[e, z], m, zz, c)

    def z_arrival(e, k):
        zz = lax.rem(z + k, chips)
        return remote(st1.at[e, zz], st1.at[e, zz], st1_s.at[e, k], st1_r.at[e, zz], m, zz, c)

    def m_copy(e, k):
        mm = lax.rem(m + k, PLANE)
        return remote(st2.at[e, m], st2.at[e, m], st2_s.at[e, k], st2_r.at[e, m], mm, z, c)

    def m_arrival(e, k):
        mm = lax.rem(m + k, PLANE)
        return remote(st2.at[e, mm], st2.at[e, mm], st2_s.at[e, k], st2_r.at[e, mm], mm, z, c)

    def send_z(e, tile):
        st1[e, z] = tile
        each(1, chips, lambda k: z_copy(e, k).start())

    def wait_z(e):
        each(1, chips, lambda k: z_arrival(e, k).wait_recv())

    def send_m(e, tile):
        st2[e, m] = tile
        each(1, PLANE, lambda k: m_copy(e, k).start())

    def wait_m(e):
        each(1, PLANE, lambda k: m_arrival(e, k).wait_recv())

    def products(source, l, taps, kernel, transposed, fresh):
        starts = [2 - i if transposed else i for i in taps]
        lhs = jnp.concatenate(
            [source[l, :, s : s + band].reshape(pixels, half) for s in starts], 1
        )
        for j in range(3):
            rhs = jnp.concatenate([kernel[l, i, j] for i in taps], 1 if transposed else 0)
            got = lax.dot_general(
                lhs,
                rhs,
                (((1,), (1 if transposed else 0,)), ((), ())),
                preferred_element_type=F32,
            )
            if fresh:
                prod[j] = got
            else:
                prod[j] = prod[j] + got

    def shifted(a, rr, before, behind, n):
        rows = pl.ds(pl.multiple_of((a * band + rr) * PAD, PAD), PAD)
        return (
            prod[1, rows, n]
            + pltpu.roll(prod[before, rows, n], 1, 0)
            + pltpu.roll(prod[behind, rows, n], PAD - 1, 0)
        )

    def row_of(table, l, a):
        return table[l, pl.ds(a, 1), :]

    def gain_of(l):
        return own_half(gain_ref[pl.ds(l, 1), :])

    def shift_of(l):
        return own_half(shift_ref[pl.ds(l, 1), :])

    def limit(a, rr):
        w = width_of(a)
        if rr == 0:
            return jnp.where(up_there, w, 0)
        if rr == band + 1:
            return jnp.where(down_there, w, 0)
        return w

    def z_halo(l, way):
        there = z - 1 + 2 * way
        return remote(zs.at[way], zh.at[l, 1 - way], zh_s.at[l, way], zh_r.at[l, way], m, there, c)

    def dh_halo(l, way):
        there = z - 1 + 2 * way
        return remote(dhs.at[way], dhh.at[l, 1 - way], dh_s.at[l, way], dh_r.at[l, way], m, there, c)

    def start_halo(halo, l):
        @pl.when(up_there)
        def _():
            halo(l, 0).start()

        @pl.when(down_there)
        def _():
            halo(l, 1).start()

    def wait_halo(halo, l):
        @pl.when(up_there)
        def _():
            halo(l, 1).wait_recv()
            halo(l, 0).wait_send()

        @pl.when(down_there)
        def _():
            halo(l, 0).wait_recv()
            halo(l, 1).wait_send()

    def act_copy(l):
        return remote(act_own.at[l], act_oth.at[l], act_s.at[l], act_r.at[l], m, z, other)

    def at_copy(l):
        return remote(act_t.at[l, 0], act_t.at[l, 1], at_s.at[l], at_r.at[l], g_peer, z, c)

    def dzr_copy(l, source):
        return remote(source.at[l], dzr.at[l], dzr_s.at[l], dzr_r.at[l], g_peer, z, c)

    def dz_copy(l):
        return remote(dz_own.at[l], dz_oth.at[l], dz_s.at[l], dz_r.at[l], m, z, other)

    def wait_x_halo(first, last):
        @pl.when(up_there)
        def _():
            for n in (0, 1, 4)[first:last]:
                x_halo(n, 4, 0, z - 1).wait_recv()

        @pl.when(down_there)
        def _():
            for n in (0, 1, 4)[first:last]:
                x_halo(n, 1, 5, z + 1).wait_recv()

    def sent_x_halo():
        @pl.when(jnp.logical_and(c == 0, up_there))
        def _():
            for n in range(6):
                x_halo(n, 1, 5, z - 1).wait_send()

        @pl.when(jnp.logical_and(c == 1, down_there))
        def _():
            for n in range(6):
                x_halo(n, 4, 0, z + 1).wait_send()

    def forward(l, first):
        weight_copy(l, 0).wait()
        weight_copy(l, 1).wait()
        if first:
            for copy in x_partner:
                copy.wait_recv()
            products(act_own, l, (1,), wa, False, True)
            products(act_oth, l, (1,), wb, False, False)
            wait_x_halo(0, 2)
            products(act_own, l, (0, 2), wa, False, False)
            products(act_oth, l, (0, 2), wb, False, False)
        else:
            products(act_own, l, (0, 1, 2), wa, False, True)
            act_copy(l).wait_recv()
            products(act_oth, l, (0, 1, 2), wb, False, False)
        weight_copy(l, 2).start()

        def collect(a, tile):
            inside = column[:, :128] < width_of(a)
            pixels_inside = (width_of(a) * band).astype(F32)
            totals, squares = [], []
            for n in tiles:
                total = jnp.zeros((PAD, 128), F32)
                for rr in range(band):
                    v = shifted(a, rr, 0, 2, n)
                    zbuf[l, a, 1 + rr, :, n] = v
                    total = total + jnp.where(inside, v, 0.0)
                total = jnp.sum(total, 0, keepdims=True)
                mean = total / pixels_inside
                square = jnp.zeros((PAD, 128), F32)
                for rr in range(band):
                    v = jnp.where(inside, zbuf[l, a, 1 + rr, :, n] - mean, 0.0)
                    square = square + v * v
                    if rr in (0, band - 1):
                        zs[rr // (band - 1), a, :, n] = v.astype(BF16)
                totals.append(total)
                squares.append(jnp.sum(square, 0, keepdims=True))
            tile = jnp.where(row8 == a, jnp.concatenate(totals, 1), tile)
            return jnp.where(row8 == a + maps_here, jnp.concatenate(squares, 1), tile)

        tile = lax.fori_loop(0, maps_here, collect, jnp.zeros((8, half), F32))
        send_z(l, tile)
        start_halo(z_halo, l)
        act_t[l, 0] = act_own[l, :, 1 : 1 + band].reshape(pixels, half).T
        wait_z(l)
        sizes, inverse = inv_t[0], inv_t[1]
        mean_t[0] = st1[l, jnp.maximum(z - 1, 0)] * inverse
        mean_t[1] = st1[l, jnp.minimum(z + 1, chips - 1)] * inverse
        total = st1[l, 0]
        for zz in range(1, chips):
            total = total + st1[l, zz]
        mean = total * inverse * (1.0 / chips)
        square = jnp.zeros((8, half), F32)
        for zz in range(chips):
            v = st1[l, zz]
            gap = v * inverse - mean
            square = square + pltpu.roll(v, 8 - maps_here, 0) + sizes * gap * gap
        tile = jnp.where(row8 < maps_here, mean, pltpu.roll(square, maps_here, 0))
        send_m(l, jnp.where(row8 < 2 * maps_here, tile, 0.0))
        wait_m(l)
        at_copy(l).start()
        averages = jnp.zeros((8, half), F32)
        scalings = jnp.zeros((8, half), F32)
        for a in range(maps_here):
            count = cnt_t[a : a + 1, :]
            average = jnp.zeros((8, half), F32)
            for mm in range(PLANE):
                average = average + coef[a, mm] * nall[mm] * st2[l, mm]
            average = jnp.sum(average, 0, keepdims=True) / count
            variance = jnp.zeros((8, half), F32)
            for mm in range(PLANE):
                v = st2[l, mm]
                gap = v - average
                variance = variance + coef[a, mm] * (
                    pltpu.roll(v, 8 - maps_here, 0) + nall[mm] * gap * gap
                )
            variance = jnp.sum(variance, 0, keepdims=True) / count
            averages = jnp.where(row8 == a, average, averages)
            scalings = jnp.where(row8 == a, lax.rsqrt(variance + epsilon), scalings)
        avg_t[l] = averages
        scl_t[l] = scalings
        wait_halo(z_halo, l)

        def activate(a, s):
            gain, shift = gain_of(l), shift_of(l)
            for n in tiles:
                average = row_of(avg_t, l, a)[:, n]
                factor = row_of(scl_t, l, a)[:, n] * gain[:, n]
                for rr in range(band + 2):
                    if rr in (0, band + 1):
                        way = rr // (band + 1)
                        v = zh[l, way, a, :, n].astype(F32) + row_of(mean_t, way, a)[:, n]
                        zbuf[l, a, rr, :, n] = v
                    else:
                        v = zbuf[l, a, rr, :, n]
                    y = (v - average) * factor + shift[:, n]
                    h = jnp.where(column[:, n] < limit(a, rr), y * jax.nn.sigmoid(y), 0.0)
                    act_own[l + 1, a, rr, :, n] = h.astype(BF16)
            return s

        lax.fori_loop(0, maps_here, activate, 0)

        if first:
            act_copy(l + 1).start()
        else:

            @pl.when(l < LAYERS - 1)
            def _():
                act_copy(l + 1).start()

    forward(0, True)
    lax.fori_loop(1, LAYERS, lambda l, s: (forward(l, False), s)[1], 0)
    g_partner.wait_recv()
    wait_x_halo(2, 3)

    def unpool(a, s):
        for rr in range(band + 2):
            slot, lower = (rr + 1) // 2, (rr + 1) % 2
            g = gbuf[slot, 0, a]
            position = gbuf[slot, 1, a]
            for b in range(2):
                v = jnp.where(position == float(2 * lower + b), g, 0.0)
                for n in range(lanes):
                    hrow[n, pl.ds(b, PAD // 2, stride=2), :] = v[:, n * 128 : (n + 1) * 128]
            v = jnp.concatenate([hrow[n] for n in range(lanes)], 1)
            if rr in (0, band + 1):
                dhh[LAYERS - 1, rr // (band + 1), a] = v.astype(BF16)
            else:
                dh[a, rr - 1] = v
        return s

    lax.fori_loop(0, maps_here, unpool, 0)

    def pool():
        def one(a, s):
            for pr in range(2):
                total = jnp.zeros((PAD // 2, half), F32)
                position = gbuf[1 + pr, 1, a]
                for lower in range(2):
                    v = act_own[LAYERS, a, 1 + 2 * pr + lower].astype(F32)
                    for n in range(lanes):
                        hrow[n] = v[:, n * 128 : (n + 1) * 128]
                    for b in range(2):
                        v = jnp.concatenate(
                            [hrow[n, pl.ds(b, PAD // 2, stride=2), :] for n in range(lanes)], 1
                        )
                        total = total + jnp.where(position == float(2 * lower + b), v, 0.0)
                pbuf[pr, a] = total.astype(BF16)
            return s

        lax.fori_loop(0, maps_here, one, 0)

    def second_rows(bit):
        return pl.ds(pl.multiple_of(bit * (half // 2), half // 2), half // 2)

    def piece_rows(p):
        return pl.ds(pl.multiple_of(p * piece, piece), piece)

    def c2(q):
        return remote(
            terms.at[q, second_rows(1 - h_bit)], r2.at[q], r2_s.at[q], r2_r.at[q], h_peer, z, c
        )

    def c3(q, p):
        slot = lax.rem(z - p + chips - 1, chips)
        return remote(
            r2.at[q, piece_rows(p)], r3.at[q, slot], r3_s.at[q, p], r3_r.at[q, slot], m, p, c
        )

    def unit_of(q):
        k = lax.div(q, TAPS)
        return (LAYERS - 1 - k) * TAPS + (q - k * TAPS)

    def region(q, start, size, lane, lanes):
        start = pl.multiple_of(c * half + start, piece)
        lane = pl.multiple_of(lane, half)
        return kg_ref.at[unit_of(q), pl.ds(start, size), pl.ds(lane, lanes)]

    def cz(q, p, zz):
        part = region(q, h_bit * (half // 2) + p * piece, piece, g_bit * half, half)
        return remote(fin.at[q], part, az_s.at[q, zz], az_r.at[q, p], m, zz, c)

    def cl(q):
        part = region(q, h_bit * (half // 2) + z * piece, piece, g_bit * half, half)
        return pltpu.make_async_copy(fin.at[q], part, loc_s.at[q])

    def cb(q):
        part = region(q, h_bit * (half // 2), half // 2, g_bit * half, half)
        return remote(part, part, ab_s.at[q], ab_r.at[q], h_peer, z, c)

    def ca(q):
        part = region(q, 0, half, g_bit * half, half)
        return remote(part, part, aa_s.at[q], aa_r.at[q], g_peer, z, c)

    def cp(q):
        part = region(q, 0, half, 0, 2 * half)
        return remote(part, part, ap_s.at[q], ap_r.at[q], m, z, other)

    def variants(l):
        def one(a, s):
            for chip in range(2):
                for rr in range(band + 2):
                    for n in tiles:
                        if chip == 0:
                            v = jnp.where(g_bit == c, dz_own[l, a, rr, :, n], dz_oth[l, a, rr, :, n])
                        else:
                            v = dzr[l, a, rr, :, n]
                        dzv[1, chip, a, rr, :, n] = v
                        v = v.astype(F32)
                        dzv[0, chip, a, rr, :, n] = pltpu.roll(v, PAD - 1, 0).astype(BF16)
                        dzv[2, chip, a, rr, :, n] = pltpu.roll(v, 1, 0).astype(BF16)
            return s

        lax.fori_loop(0, maps_here, one, 0)

    def ready_terms(l):
        at_copy(l).wait_recv()
        dzr_copy(l, dz_own).wait_recv()
        variants(l)

    def weight_terms(l, first, last):
        def one(t, s):
            i = lax.div(t, 3)
            j = t - 3 * i
            lhs = jnp.concatenate([act_t[l, 0], act_t[l, 1]], 1)
            rhs = dzv[j, :, :, pl.ds(2 - i, band)].reshape(2 * pixels, half)
            q = (LAYERS - 1 - l) * TAPS + t
            terms[q] = jnp.dot(lhs, rhs, preferred_element_type=F32).astype(BF16)
            c2(q).start()
            return s

        lax.fori_loop(first, last, one, 0)

    def stage_second(q):
        c2(q).wait_recv()
        r2[q] = (r2[q].astype(F32) + terms[q, second_rows(h_bit)].astype(F32)).astype(BF16)

        def give(k):
            p = lax.rem(z + k, chips)

            @pl.when(p < owners)
            def _():
                c3(q, p).start()

        each(1, chips, give)

    def stage_sum(q):
        @pl.when(z < owners)
        def _():
            for k in range(chips - 1):
                remote(
                    r3.at[q, k], r3.at[q, k], r3_s.at[q, 0], r3_r.at[q, k], m, z, c
                ).wait_recv()
            total = r2[q, piece_rows(z)].astype(F32)
            for k in range(chips - 1):
                total = total + r3[q, k].astype(F32)
            fin[q] = total.astype(BF16)
            each(1, chips, lambda k: cz(q, z, lax.rem(z + k, chips)).start())
            cl(q).start()

    def stage_back(q):
        def arrived(k):
            p = lax.rem(z + k, chips)

            @pl.when(p < owners)
            def _():
                cz(q, p, p).wait_recv()

        each(1, chips, arrived)

        @pl.when(z < owners)
        def _():
            cl(q).wait()

        cb(q).start()

    def stage_first(q):
        cb(q).wait_recv()
        ca(q).start()

    def stage_chip(q):
        ca(q).wait_recv()
        cp(q).start()

    def run(stage, first, last):
        lax.fori_loop(first, last, lambda q, s: (stage(q), s)[1], 0)

    def backward(k, carry):
        l = LAYERS - 1 - k
        gain, shift = gain_of(l), shift_of(l)

        def gradient(a, rr, n):
            zhat = (zbuf[l, a, rr, :, n] - row_of(avg_t, l, a)[:, n]) * row_of(scl_t, l, a)[:, n]
            y = zhat * gain[:, n] + shift[:, n]
            s = jax.nn.sigmoid(y)
            if rr in (0, band + 1):
                upstream = dhh[l, rr // (band + 1), a, :, n].astype(F32)
            else:
                upstream = dh[a, rr - 1, :, n]
            dy = upstream * (s * (1.0 + y * (1.0 - s)))
            dy = jnp.where(column[:, n] < limit(a, rr), dy, 0.0)
            dyb[a, rr, :, n] = dy
            return dy, zhat

        def collect(a, tile):
            plains, crosses = [], []
            for n in tiles:
                plain = jnp.zeros((PAD, 128), F32)
                crossed = jnp.zeros((PAD, 128), F32)
                for rr in range(1, band + 1):
                    dy, zhat = gradient(a, rr, n)
                    plain = plain + dy
                    crossed = crossed + dy * zhat
                plains.append(jnp.sum(plain, 0, keepdims=True))
                crosses.append(jnp.sum(crossed, 0, keepdims=True))
            tile = jnp.where(row8 == a, jnp.concatenate(plains, 1), tile)
            return jnp.where(row8 == a + maps_here, jnp.concatenate(crosses, 1), tile)

        e = LAYERS + l
        tile = lax.fori_loop(0, maps_here, collect, jnp.zeros((8, half), F32))
        send_z(e, tile)

        @pl.when(k == LAYERS - 1)
        def _():
            run(stage_second, 0, TAPS)

        @pl.when(k > 0)
        def _():
            ready_terms(l + 1)
            weight_terms(l + 1, 0, 4)

        wait_z(e)
        total = st1[e, 0]
        for zz in range(1, chips):
            total = total + st1[e, zz]
        send_m(e, total)

        @pl.when(k > 0)
        def _():
            weight_terms(l + 1, 4, TAPS)
            wait_halo(dh_halo, l)

        @pl.when(k == 0)
        def _():
            pool()

        def edges(a, s):
            for n in tiles:
                gradient(a, 0, n)
                gradient(a, band + 1, n)
            return s

        lax.fori_loop(0, maps_here, edges, 0)
        wait_m(e)
        total = st2[e, 0]
        for mm in range(1, PLANE):
            total = total + st2[e, mm]
        sums_own[pl.ds(l, 1), :] = jnp.sum(
            jnp.where(row8 >= maps_here, total, 0.0), 0, keepdims=True
        )
        sums_own[pl.ds(LAYERS + l, 1), :] = jnp.sum(
            jnp.where(row8 < maps_here, total, 0.0), 0, keepdims=True
        )
        plains = jnp.zeros((8, half), F32)
        crosses = jnp.zeros((8, half), F32)
        for a in range(maps_here):
            plain = jnp.zeros((8, half), F32)
            crossed = jnp.zeros((8, half), F32)
            for mm in range(PLANE):
                v = st2[e, mm]
                plain = plain + coef[a, mm] * v
                crossed = crossed + coef[a, mm] * pltpu.roll(v, 8 - maps_here, 0)
            count = cnt_t[a : a + 1, :]
            plain = gain * (jnp.sum(plain, 0, keepdims=True) / count)
            crossed = gain * (jnp.sum(crossed, 0, keepdims=True) / count)
            plains = jnp.where(row8 == a, plain, plains)
            crosses = jnp.where(row8 == a, crossed, crosses)
        tb_t[0] = plains
        ta_t[0] = crosses

        def settle(a, s):
            for n in tiles:
                average, scaling = row_of(avg_t, l, a)[:, n], row_of(scl_t, l, a)[:, n]
                plain, crossed = row_of(tb_t, 0, a)[:, n], row_of(ta_t, 0, a)[:, n]
                for rr in range(band + 2):
                    zhat = (zbuf[l, a, rr, :, n] - average) * scaling
                    v = scaling * (dyb[a, rr, :, n] * gain[:, n] - plain - zhat * crossed)
                    v = jnp.where(column[:, n] < limit(a, rr), v, 0.0)
                    dz_own[l, a, rr, :, n] = v.astype(BF16)
            return s

        lax.fori_loop(0, maps_here, settle, 0)
        dz_copy(l).start()

        @pl.when(g_bit != c)
        def _():
            dzr_copy(l, dz_own).start()

        products(dz_own, l, (0, 1, 2), wa, True, True)
        weight_copy(l, 2).wait()
        dz_copy(l).wait_recv()

        @pl.when(g_bit == c)
        def _():
            dzr_copy(l, dz_oth).start()

        products(dz_oth, l, (0, 1, 2), wb, True, False)

        def gather(a, s):
            for n in tiles:
                for rr in range(band):
                    v = shifted(a, rr, 2, 0, n)
                    dh[a, rr, :, n] = v
                    if rr in (0, band - 1):
                        dhs[rr // (band - 1), a, :, n] = v.astype(BF16)
            return s

        lax.fori_loop(0, maps_here, gather, 0)

        @pl.when(l > 0)
        def _():
            start_halo(dh_halo, l - 1)

        return carry

    lax.fori_loop(0, LAYERS, backward, 0)
    run(stage_sum, 0, TAPS)
    ready_terms(0)
    weight_terms(0, 0, TAPS)

    def input_rows(a, s):
        for rr in range(band):
            igbuf[rr // 2, a, rr % 2] = jnp.where(
                column < width_of(a), dh[a, rr], 0.0
            )
        return s

    lax.fori_loop(0, maps_here, input_rows, 0)

    outs = (
        (
            remote(igbuf.at[other], ig_ref.at[c], out_s.at[0], out_r.at[0], m, z, other),
            pltpu.make_async_copy(igbuf.at[c], ig_ref.at[c], out_l.at[0]),
        ),
        (
            remote(pbuf.at[other], pooled_ref.at[c], out_s.at[1], out_r.at[1], m, z, other),
            pltpu.make_async_copy(pbuf.at[c], pooled_ref.at[c], out_l.at[1]),
        ),
        (
            remote(sums_own, sums_ref.at[c], out_s.at[2], out_r.at[2], m, z, other),
            pltpu.make_async_copy(sums_own, sums_ref.at[c], out_l.at[2]),
        ),
    )
    for there, here in outs:
        there.start()
        here.start()

    def drain(s, carry):
        for stage, first, lag in (
            (stage_chip, 0, 2 * LAG),
            (stage_first, 0, LAG),
            (stage_back, 0, 0),
            (stage_sum, TAPS, LAG),
            (stage_second, TAPS, 0),
        ):
            q = first + s - lag

            @pl.when(jnp.logical_and(q >= first, q < UNITS))
            def _(stage=stage, q=q):
                stage(q)

        return carry

    lax.fori_loop(0, UNITS + 2 * LAG, drain, 0)

    def finish(q, carry):
        cp(q).wait()
        ca(q).wait_send()
        cb(q).wait_send()
        c2(q).wait_send()

        def given(k):
            p = lax.rem(z + k, chips)

            @pl.when(p < owners)
            def _():
                c3(q, p).wait_send()

        each(1, chips, given)

        @pl.when(z < owners)
        def _():
            each(1, chips, lambda k: cz(q, z, lax.rem(z + k, chips)).wait_send())

        return carry

    lax.fori_loop(0, UNITS, finish, 0)
    for copy in x_partner:
        copy.wait_send()
    g_partner.wait_send()
    sent_x_halo()

    def sent(e, carry):
        each(1, chips, lambda k: z_copy(e, k).wait_send())
        each(1, PLANE, lambda k: m_copy(e, k).wait_send())
        return carry

    lax.fori_loop(0, 2 * LAYERS, sent, 0)
    for l in range(LAYERS):
        at_copy(l).wait_send()
        dzr_copy(l, dz_own).wait_send()
    for l in range(1, LAYERS):
        act_copy(l).wait_send()
    for l in range(LAYERS):
        dz_copy(l).wait_send()
    for there, here in outs:
        there.wait()
        here.wait()


def solution(mesh):
    chips = mesh.shape["rows"] // 2

    def per_device(
        block_input,
        conv_weights,
        norm_gains,
        norm_shifts,
        map_width,
        map_group,
        pool_index,
        task_mask,
        task_weights,
        task_grads,
    ):
        maps_here, rows_here, columns, channels = block_input.shape
        pooled_columns = pool_index.shape[2]
        height = rows_here * mesh.shape["rows"]
        half = channels // 2
        band = 2 * rows_here
        pixels = maps_here * band * PAD
        owners = min(chips, 8)
        piece = half // 2 // owners
        rounds = 2 * LAYERS
        slots = 2 * UNITS * (chips - 1) * piece * half + 4 * rounds * chips * 8 * half
        grant = 41 * 1024 * 1024 + slots
        vmem, dma = pltpu.VMEM, pltpu.SemaphoreType.DMA
        tile = (maps_here, band + 2, PAD, half)
        edge = (2, maps_here, PAD, half)
        whole = pl.BlockSpec(memory_space=pltpu.VMEM)
        scalars = pl.BlockSpec(memory_space=pltpu.SMEM)
        anywhere = pl.BlockSpec(memory_space=pl.ANY)
        pooled, ig, kg, sums = pl.pallas_call(
            functools.partial(block_kernel, chips, height),
            out_shape=(
                jax.ShapeDtypeStruct((2, maps_here, PAD // 2, half), BF16),
                jax.ShapeDtypeStruct((2, maps_here, rows_here, PAD, half), F32),
                jax.ShapeDtypeStruct((UNITS, channels, channels), BF16),
                jax.ShapeDtypeStruct((2, 8, half), F32),
            ),
            in_specs=[whole, anywhere, whole, whole, scalars, scalars, whole, scalars, scalars, whole],
            out_specs=[anywhere] * 4,
            scratch_shapes=[
                vmem((LAYERS, 3, 3, half, half), BF16),
                vmem((LAYERS, 3, 3, half, half), BF16),
                vmem((LAYERS + 1,) + tile, BF16),
                vmem((LAYERS,) + tile, BF16),
                vmem((LAYERS, 2, half, pixels), BF16),
                vmem((LAYERS,) + tile, F32),
                vmem(edge, BF16),
                vmem((LAYERS,) + edge, BF16),
                vmem((maps_here, band, PAD, half), F32),
                vmem(edge, BF16),
                vmem((LAYERS,) + edge, BF16),
                vmem(tile, F32),
                vmem((LAYERS,) + tile, BF16),
                vmem((LAYERS,) + tile, BF16),
                vmem((LAYERS,) + tile, BF16),
                vmem((3, 2) + tile, BF16),
                vmem((3, pixels, half), F32),
                vmem((2, 2, maps_here, PAD // 2, half), F32),
                vmem((4, 2, maps_here, PAD // 2, half), F32),
                vmem((half // 128, PAD, 128), F32),
                vmem((2, maps_here, PAD // 2, half), BF16),
                vmem((2, maps_here, rows_here, PAD, half), F32),
                vmem((rounds, chips, 8, half), F32),
                vmem((rounds, PLANE, 8, half), F32),
                vmem((maps_here, PLANE, 8, half), F32),
                vmem((PLANE, 8, half), F32),
                vmem((2, 8, half), F32),
                vmem((8, half), F32),
                vmem((LAYERS, 8, half), F32),
                vmem((LAYERS, 8, half), F32),
                vmem((2, 8, half), F32),
                vmem((1, 8, half), F32),
                vmem((1, 8, half), F32),
                vmem((8, half), F32),
                vmem((UNITS, half, half), BF16),
                vmem((UNITS, half // 2, half), BF16),
                vmem((UNITS, chips - 1, piece, half), BF16),
                vmem((UNITS, piece, half), BF16),
                dma((LAYERS, 3)),
                dma((6,)),
                dma((6,)),
                dma((3,)),
                dma((3,)),
                dma((rounds, chips)),
                dma((rounds, chips)),
                dma((rounds, PLANE)),
                dma((rounds, PLANE)),
                dma((LAYERS, 2)),
                dma((LAYERS, 2)),
                dma((LAYERS, 2)),
                dma((LAYERS, 2)),
                dma((LAYERS,)),
                dma((LAYERS,)),
                dma((LAYERS,)),
                dma((LAYERS,)),
                dma((3,)),
                dma((3,)),
                dma((3,)),
                dma((LAYERS,)),
                dma((LAYERS,)),
                dma((LAYERS,)),
                dma((LAYERS,)),
                dma((UNITS,)),
                dma((UNITS,)),
                dma((UNITS, owners)),
                dma((UNITS, chips - 1)),
                dma((UNITS, chips)),
                dma((UNITS, owners)),
                dma((UNITS,)),
                dma((UNITS,)),
                dma((UNITS,)),
                dma((UNITS,)),
                dma((UNITS,)),
                dma((UNITS,)),
                dma((UNITS,)),
            ],
            compiler_params=pltpu.CompilerParams(
                collective_id=0,
                has_side_effects=True,
                vmem_limit_bytes=grant,
            ),
        )(
            block_input,
            conv_weights,
            norm_gains,
            norm_shifts,
            map_width,
            map_group,
            pool_index,
            task_mask,
            task_weights,
            task_grads,
        )
        pooled = jnp.concatenate([pooled[0], pooled[1]], -1)[:, None, :pooled_columns]
        input_grad = jnp.concatenate([ig[0], ig[1]], -1)[:, :, :columns]
        sums = jnp.concatenate([sums[0], sums[1]], -1)
        return (
            pooled,
            input_grad,
            kg.astype(F32).reshape(conv_weights.shape),
            sums[:LAYERS],
            sums[LAYERS : 2 * LAYERS],
        )

    return jax.shard_map(
        per_device,
        mesh=mesh,
        in_specs=(
            P("maps", "rows", None, None),
            P(),
            P(),
            P(),
            P(),
            P(),
            P("maps", "rows", None, None),
            P("maps", None),
            P(),
            P(None, "maps", "rows", None, None),
        ),
        out_specs=(P("maps", "rows", None, None), P("maps", "rows", None, None), P(), P(), P()),
        check_vma=False,
    )
```

```python
import functools

import jax
import jax.numpy as jnp
from jax import lax
from jax.experimental import pallas as pl
from jax.experimental.pallas import tpu as pltpu
from jax.sharding import PartitionSpec as P

MESH = pl.DeviceIdType.MESH
epsilon = 1e-05
PAD = 64
LAYERS = 3
TAPS = 9
UNITS = LAYERS * TAPS
PLANE = 4
LAG = 4
EARLY = 2
F32 = jnp.float32
BF16 = jnp.bfloat16


def each(first, last, body):
    if last - first <= 8:
        for k in range(first, last):
            body(k)
    else:
        lax.fori_loop(first, last, lambda k, s: (body(k), s)[1], 0)


def block_kernel(
    chips,
    height,
    x_ref,
    w_ref,
    gain_ref,
    shift_ref,
    width_ref,
    group_ref,
    index_ref,
    tmask_ref,
    tweight_ref,
    tgrad_ref,
    pooled_ref,
    ig_ref,
    kg_ref,
    sums_ref,
    wa,
    wb,
    act_own,
    act_oth,
    act_t,
    act_b,
    zbuf,
    zs,
    zh,
    dh,
    dhs,
    dhh,
    dz_own,
    dz_oth,
    dzr,
    dzv,
    prod,
    gsrc,
    gbuf,
    hrow,
    pbuf,
    igbuf,
    st1,
    st2,
    coef,
    nall,
    inv_t,
    cnt_t,
    avg_t,
    scl_t,
    mean_t,
    tb_t,
    ta_t,
    sums_own,
    terms,
    r2,
    r3,
    fin,
    w_sem,
    x_s,
    x_r,
    g_s,
    g_r,
    st1_s,
    st1_r,
    st2_s,
    st2_r,
    zh_s,
    zh_r,
    dh_s,
    dh_r,
    act_s,
    act_r,
    dz_s,
    dz_r,
    out_s,
    out_r,
    out_l,
    at_s,
    at_r,
    dzr_s,
    dzr_r,
    r2_s,
    r2_r,
    r3_s,
    r3_r,
    az_s,
    az_r,
    ab_s,
    ab_r,
    aa_s,
    aa_r,
    ap_s,
    ap_r,
    loc_s,
):
    maps_here = x_ref.shape[0]
    columns = x_ref.shape[2]
    half = x_ref.shape[3] // 2
    tasks = tgrad_ref.shape[0]
    pooled_columns = tgrad_ref.shape[3]
    lanes = half // 128
    tiles = [slice(n * 128, (n + 1) * 128) for n in range(lanes)]
    band = 4
    pixels = maps_here * band * PAD
    owners = min(chips, 8)
    piece = (half // 2) // owners
    m = lax.axis_index("maps")
    r = lax.axis_index("rows")
    c = lax.rem(r, 2)
    z = lax.div(r, 2)
    other = 1 - c
    first_map = m * maps_here
    x_bit = lax.rem(m, 2)
    y_bit = lax.div(m, 2)
    x_peer = m + 1 - 2 * x_bit
    y_peer = m + 2 - 4 * y_bit
    g_bit = (1 - c) * x_bit + c * y_bit
    h_bit = (1 - c) * y_bit + c * x_bit
    g_peer = (1 - c) * x_peer + c * y_peer
    h_peer = (1 - c) * y_peer + c * x_peer
    up_there = z > 0
    down_there = z < chips - 1
    row8 = lax.broadcasted_iota(jnp.int32, (8, half), 0)
    column = lax.broadcasted_iota(jnp.int32, (PAD, half), 0)

    def remote(src, dst, send, recv, mm, zz, cc):
        return pltpu.make_async_remote_copy(
            src_ref=src,
            dst_ref=dst,
            send_sem=send,
            recv_sem=recv,
            device_id=(mm, zz * 2 + cc),
            device_id_type=MESH,
        )

    def own_half(v):
        return jnp.where(c == 0, v[..., :half], v[..., half:])

    def width_of(a):
        return width_ref[first_map + a]

    own_at = pl.ds(pl.multiple_of(c * half, half), half)
    oth_at = pl.ds(pl.multiple_of(other * half, half), half)

    def weight_copy(l, n):
        dst = (wa, wb, wb)[n]
        k_at, o_at = ((own_at, own_at), (oth_at, own_at), (own_at, oth_at))[n]
        return pltpu.make_async_copy(w_ref.at[l, :, :, k_at, o_at], dst.at[l], w_sem.at[l, n])

    for l in range(LAYERS):
        weight_copy(l, 0).start()
        weight_copy(l, 1).start()

    barrier = pltpu.get_barrier_semaphore()

    def greet(k):
        rr = lax.rem(r + k, 2 * chips)
        pl.semaphore_signal(barrier, inc=1, device_id=(m, rr), device_id_type=MESH)

    each(1, 2 * chips, greet)
    for k in range(1, PLANE):
        for core in (c, other):
            there = (lax.rem(m + k, PLANE), z * 2 + core)
            pl.semaphore_signal(barrier, inc=1, device_id=there, device_id_type=MESH)

    mine = pl.ds(1 + 2 * c, 2)
    for a in range(maps_here):
        inside = lax.broadcasted_iota(jnp.int32, (columns, 2 * half), 0) < width_of(a)
        for rr in range(2):
            v = jnp.where(inside, x_ref[a, rr].astype(F32), 0.0).astype(BF16)
            spot = 1 + 2 * c + rr
            act_own[0, a, spot, pl.ds(48, 16), :] = jnp.zeros((16, half), BF16)
            act_oth[0, a, spot, pl.ds(48, 16), :] = jnp.zeros((16, half), BF16)
            act_own[0, a, spot, pl.ds(0, columns), :] = own_half(v)
            act_oth[0, a, spot, pl.ds(0, columns), :] = jnp.where(
                c == 0, v[:, half:], v[:, :half]
            )

    @pl.when(z == 0)
    def _():
        act_own[0, :, 0] = jnp.zeros((maps_here, PAD, half), BF16)
        act_oth[0, :, 0] = jnp.zeros((maps_here, PAD, half), BF16)

    @pl.when(z == chips - 1)
    def _():
        act_own[0, :, 5] = jnp.zeros((maps_here, PAD, half), BF16)
        act_oth[0, :, 5] = jnp.zeros((maps_here, PAD, half), BF16)

    gsrc[...] = jnp.zeros(gsrc.shape, F32)
    for a in range(maps_here):
        total = None
        for t in range(tasks):
            scale = tweight_ref[t] * tmask_ref[a, t].astype(F32)
            term = tgrad_ref[t, a, 0].astype(F32) * scale
            total = term if total is None else total + term
        position = index_ref[a, 0].astype(F32)
        for h in range(2):
            gsrc[h, 0, a, pl.ds(0, pooled_columns), :] = total[:, h * half : (h + 1) * half]
            gsrc[h, 1, a, pl.ds(0, pooled_columns), :] = position[:, h * half : (h + 1) * half]
    gbuf[1 + c] = gsrc[c]

    pl.semaphore_wait(barrier, 2 * chips - 1 + 2 * (PLANE - 1))

    x_partner = (
        remote(act_own.at[0, :, mine], act_oth.at[0, :, mine], x_s.at[0], x_r.at[0], m, z, other),
        remote(act_oth.at[0, :, mine], act_own.at[0, :, mine], x_s.at[1], x_r.at[1], m, z, other),
    )
    g_partner = remote(gsrc.at[other], gbuf.at[1 + c], g_s.at[0], g_r.at[0], m, z, other)

    def x_halo(n, src_row, dst_row, zz):
        cc = (c, c, other, other, c, other)[n]
        low = dst_row == band + 1
        if n >= 4:
            src, dst = gsrc.at[cc], gbuf.at[3 if low else 0]
            return remote(src, dst, g_s.at[n - 3], g_r.at[1 if low else 2], m, zz, cc)
        src = (act_own, act_oth, act_own, act_oth)[n].at[0, :, src_row]
        dst = (act_own, act_oth, act_oth, act_own)[n].at[0, :, dst_row]
        return remote(src, dst, x_s.at[2 + n], x_r.at[(2 if low else 4) + n % 2], m, zz, cc)

    for copy in x_partner:
        copy.start()

    @pl.when(jnp.logical_and(c == 0, up_there))
    def _():
        for n in range(4):
            x_halo(n, 1, 5, z - 1).start()

    @pl.when(jnp.logical_and(c == 1, down_there))
    def _():
        for n in range(4):
            x_halo(n, 4, 0, z + 1).start()

    g_partner.start()

    @pl.when(jnp.logical_and(c == 0, up_there))
    def _():
        for n in range(4, 6):
            x_halo(n, 1, 5, z - 1).start()

    @pl.when(jnp.logical_and(c == 1, down_there))
    def _():
        for n in range(4, 6):
            x_halo(n, 4, 0, z + 1).start()

    for mm in range(PLANE):
        sizes = jnp.zeros((8, half), F32)
        for b in range(maps_here):
            sizes = jnp.where(
                row8 == b, (width_ref[mm * maps_here + b] * height).astype(F32), sizes
            )
        nall[mm] = sizes
    inside_sizes = jnp.zeros((8, half), F32)
    for b in range(maps_here):
        inside_sizes = jnp.where(row8 == b, (width_of(b) * band).astype(F32), inside_sizes)
    inv_t[0] = inside_sizes
    inv_t[1] = jnp.where(row8 < maps_here, 1.0 / jnp.maximum(inside_sizes, 1.0), 0.0)
    counts = jnp.ones((8, half), F32)
    for a in range(maps_here):
        total = jnp.zeros((1, half), F32)
        for mm in range(PLANE):
            same = jnp.zeros((8, half), F32)
            for b in range(maps_here):
                alike = group_ref[first_map + a] == group_ref[mm * maps_here + b]
                same = jnp.where(row8 == b, jnp.where(alike, 1.0, 0.0), same)
            coef[a, mm] = same
            total = total + jnp.sum(same * nall[mm], 0, keepdims=True)
        counts = jnp.where(row8 == a, total, counts)
    cnt_t[...] = counts

    def z_copy(e, k):
        zz = lax.rem(z + k, chips)
        return remote(st1.at[e, z], st1.at[e, z], st1_s.at[e, k], st1_r.at[e, z], m, zz, c)

    def z_arrival(e, k):
        zz = lax.rem(z + k, chips)
        return remote(st1.at[e, zz], st1.at[e, zz], st1_s.at[e, k], st1_r.at[e, zz], m, zz, c)

    def m_copy(e, k):
        mm = lax.rem(m + k, PLANE)
        return remote(st2.at[e, m], st2.at[e, m], st2_s.at[e, k], st2_r.at[e, m], mm, z, c)

    def m_arrival(e, k):
        mm = lax.rem(m + k, PLANE)
        return remote(st2.at[e, mm], st2.at[e, mm], st2_s.at[e, k], st2_r.at[e, mm], mm, z, c)

    def send_z(e, tile):
        st1[e, z] = tile
        each(1, chips, lambda k: z_copy(e, k).start())

    def wait_z(e):
        each(1, chips, lambda k: z_arrival(e, k).wait_recv())

    def send_m(e, tile):
        st2[e, m] = tile
        each(1, PLANE, lambda k: m_copy(e, k).start())

    def wait_m(e):
        each(1, PLANE, lambda k: m_arrival(e, k).wait_recv())

    def products(source, l, taps, kernel, transposed, fresh):
        starts = [2 - i if transposed else i for i in taps]
        lhs = jnp.concatenate(
            [source[lax.rem(l, 2), :, s : s + band].reshape(pixels, half) for s in starts], 1
        )
        for j in range(3):
            rhs = jnp.concatenate([kernel[l, i, j] for i in taps], 1 if transposed else 0)
            got = lax.dot_general(
                lhs,
                rhs,
                (((1,), (1 if transposed else 0,)), ((), ())),
                preferred_element_type=F32,
            )
            if fresh:
                prod[j] = got
            else:
                prod[j] = prod[j] + got

    def shifted(a, rr, before, behind, n):
        rows = pl.ds(pl.multiple_of((a * band + rr) * PAD, PAD), PAD)
        return (
            prod[1, rows, n]
            + pltpu.roll(prod[before, rows, n], 1, 0)
            + pltpu.roll(prod[behind, rows, n], PAD - 1, 0)
        )

    def row_of(table, l, a):
        return table[l, pl.ds(a, 1), :]

    def gain_of(l):
        return own_half(gain_ref[pl.ds(l, 1), :])

    def shift_of(l):
        return own_half(shift_ref[pl.ds(l, 1), :])

    def limit(a, rr):
        w = width_of(a)
        if rr == 0:
            return jnp.where(up_there, w, 0)
        if rr == band + 1:
            return jnp.where(down_there, w, 0)
        return w

    def z_halo(l, way):
        there = z - 1 + 2 * way
        return remote(zs.at[way], zh.at[l, 1 - way], zh_s.at[l, way], zh_r.at[l, way], m, there, c)

    def dh_halo(l, way):
        there = z - 1 + 2 * way
        return remote(dhs.at[way], dhh.at[l, 1 - way], dh_s.at[l, way], dh_r.at[l, way], m, there, c)

    def start_halo(halo, l):
        @pl.when(up_there)
        def _():
            halo(l, 0).start()

        @pl.when(down_there)
        def _():
            halo(l, 1).start()

    def wait_halo(halo, l):
        @pl.when(up_there)
        def _():
            halo(l, 1).wait_recv()
            halo(l, 0).wait_send()

        @pl.when(down_there)
        def _():
            halo(l, 0).wait_recv()
            halo(l, 1).wait_send()

    def act_copy(l, a):
        slot = lax.rem(l, 2)
        src, dst = act_own.at[slot, a], act_oth.at[slot, a]
        return remote(src, dst, act_s.at[l, a], act_r.at[l, a], m, z, other)

    def at_copy(l):
        return remote(act_t.at[l, 0], act_t.at[l, 1], at_s.at[l], at_r.at[l], g_peer, z, c)

    def dzr_copy(l, a, way):
        src, dst = dz_own.at[lax.rem(l, 2), a, pl.ds(1, band)], dzr.at[l, a]
        peer = (x_peer, y_peer)[way]
        return remote(src, dst, dzr_s.at[l, way, a], dzr_r.at[l, a], peer, z, way)

    def if_wanted(way, body):
        @pl.when((x_bit, y_bit)[way] + c == 1)
        def _():
            body()

    def dz_copy(l, a):
        slot = lax.rem(l, 2)
        src, dst = dz_own.at[slot, a], dz_oth.at[slot, a]
        return remote(src, dst, dz_s.at[l, a], dz_r.at[l, a], m, z, other)

    def wait_x_halo(first, last):
        @pl.when(up_there)
        def _():
            for n in (0, 1, 4)[first:last]:
                x_halo(n, 4, 0, z - 1).wait_recv()

        @pl.when(down_there)
        def _():
            for n in (0, 1, 4)[first:last]:
                x_halo(n, 1, 5, z + 1).wait_recv()

    def sent_x_halo(first, last):
        @pl.when(jnp.logical_and(c == 0, up_there))
        def _():
            for n in range(first, last):
                x_halo(n, 1, 5, z - 1).wait_send()

        @pl.when(jnp.logical_and(c == 1, down_there))
        def _():
            for n in range(first, last):
                x_halo(n, 4, 0, z + 1).wait_send()

    def forward(l, first):
        weight_copy(l, 0).wait()
        weight_copy(l, 1).wait()
        if first:
            for copy in x_partner:
                copy.wait_recv()
            products(act_own, l, (1,), wa, False, True)
            products(act_oth, l, (1,), wb, False, False)
            wait_x_halo(0, 2)
            products(act_own, l, (0, 2), wa, False, False)
            products(act_oth, l, (0, 2), wb, False, False)
        else:
            products(act_own, l, (0, 1, 2), wa, False, True)
            for a in range(maps_here):
                act_copy(l, a).wait_recv()
            products(act_oth, l, (0, 1, 2), wb, False, False)
        weight_copy(l, 2).start()

        def collect(a, tile):
            inside = column[:, :128] < width_of(a)
            pixels_inside = (width_of(a) * band).astype(F32)
            totals, squares = [], []
            for n in tiles:
                total = jnp.zeros((PAD, 128), F32)
                for rr in range(band):
                    v = shifted(a, rr, 0, 2, n)
                    zbuf[l, a, 1 + rr, :, n] = v
                    total = total + jnp.where(inside, v, 0.0)
                total = jnp.sum(total, 0, keepdims=True)
                mean = total / pixels_inside
                square = jnp.zeros((PAD, 128), F32)
                for rr in range(band):
                    v = jnp.where(inside, zbuf[l, a, 1 + rr, :, n] - mean, 0.0)
                    square = square + v * v
                    if rr in (0, band - 1):
                        zs[rr // (band - 1), a, :, n] = v.astype(BF16)
                totals.append(total)
                squares.append(jnp.sum(square, 0, keepdims=True))
            tile = jnp.where(row8 == a, jnp.concatenate(totals, 1), tile)
            return jnp.where(row8 == a + maps_here, jnp.concatenate(squares, 1), tile)

        tile = lax.fori_loop(0, maps_here, collect, jnp.zeros((8, half), F32))
        send_z(l, tile)
        start_halo(z_halo, l)
        act_t[l, 0] = act_own[lax.rem(l, 2)].reshape(maps_here * (band + 2) * PAD, half).T
        wait_z(l)
        sizes, inverse = inv_t[0], inv_t[1]
        mean_t[0] = st1[l, jnp.maximum(z - 1, 0)] * inverse
        mean_t[1] = st1[l, jnp.minimum(z + 1, chips - 1)] * inverse
        total = st1[l, 0]
        for zz in range(1, chips):
            total = total + st1[l, zz]
        mean = total * inverse * (1.0 / chips)
        square = jnp.zeros((8, half), F32)
        for zz in range(chips):
            v = st1[l, zz]
            gap = v * inverse - mean
            square = square + pltpu.roll(v, 8 - maps_here, 0) + sizes * gap * gap
        tile = jnp.where(row8 < maps_here, mean, pltpu.roll(square, maps_here, 0))
        send_m(l, jnp.where(row8 < 2 * maps_here, tile, 0.0))
        wait_m(l)
        at_copy(l).start()
        averages = jnp.zeros((8, half), F32)
        scalings = jnp.zeros((8, half), F32)
        for a in range(maps_here):
            count = cnt_t[a : a + 1, :]
            average = jnp.zeros((8, half), F32)
            for mm in range(PLANE):
                average = average + coef[a, mm] * nall[mm] * st2[l, mm]
            average = jnp.sum(average, 0, keepdims=True) / count
            variance = jnp.zeros((8, half), F32)
            for mm in range(PLANE):
                v = st2[l, mm]
                gap = v - average
                variance = variance + coef[a, mm] * (
                    pltpu.roll(v, 8 - maps_here, 0) + nall[mm] * gap * gap
                )
            variance = jnp.sum(variance, 0, keepdims=True) / count
            averages = jnp.where(row8 == a, average, averages)
            scalings = jnp.where(row8 == a, lax.rsqrt(variance + epsilon), scalings)
        avg_t[l] = averages
        scl_t[l] = scalings
        wait_halo(z_halo, l)

        def activate(a, s):
            gain, shift = gain_of(l), shift_of(l)
            for n in tiles:
                average = row_of(avg_t, l, a)[:, n]
                factor = row_of(scl_t, l, a)[:, n] * gain[:, n]
                for rr in range(band + 2):
                    if rr in (0, band + 1):
                        way = rr // (band + 1)
                        v = zh[l, way, a, :, n].astype(F32) + row_of(mean_t, way, a)[:, n]
                        zbuf[l, a, rr, :, n] = v
                    else:
                        v = zbuf[l, a, rr, :, n]
                    y = (v - average) * factor + shift[:, n]
                    h = jnp.where(column[:, n] < limit(a, rr), y * jax.nn.sigmoid(y), 0.0)
                    act_own[lax.rem(l + 1, 2), a, rr, :, n] = h.astype(BF16)

            @pl.when(l < LAYERS - 1)
            def _():
                act_copy(l + 1, a).start()

            return s

        if first:
            for copy in x_partner:
                copy.wait_send()
            sent_x_halo(0, 4)
        else:

            @pl.when(l == 2)
            def _():
                for a in range(maps_here):
                    act_copy(1, a).wait_send()

        lax.fori_loop(0, maps_here, activate, 0)

    forward(0, True)
    lax.fori_loop(1, LAYERS, lambda l, s: (forward(l, False), s)[1], 0)
    g_partner.wait_recv()
    wait_x_halo(2, 3)

    def unpool(a, s):
        for rr in range(band + 2):
            slot, lower = (rr + 1) // 2, (rr + 1) % 2
            g = gbuf[slot, 0, a]
            position = gbuf[slot, 1, a]
            for b in range(2):
                v = jnp.where(position == float(2 * lower + b), g, 0.0)
                for n in range(lanes):
                    hrow[n, pl.ds(b, PAD // 2, stride=2), :] = v[:, n * 128 : (n + 1) * 128]
            v = jnp.concatenate([hrow[n] for n in range(lanes)], 1)
            if rr in (0, band + 1):
                dhh[LAYERS - 1, rr // (band + 1), a] = v.astype(BF16)
            else:
                dh[a, rr - 1] = v
        return s

    lax.fori_loop(0, maps_here, unpool, 0)

    def pool():
        def one(a, s):
            for pr in range(2):
                total = jnp.zeros((PAD // 2, half), F32)
                position = gbuf[1 + pr, 1, a]
                for lower in range(2):
                    v = act_own[LAYERS % 2, a, 1 + 2 * pr + lower].astype(F32)
                    for n in range(lanes):
                        hrow[n] = v[:, n * 128 : (n + 1) * 128]
                    for b in range(2):
                        v = jnp.concatenate(
                            [hrow[n, pl.ds(b, PAD // 2, stride=2), :] for n in range(lanes)], 1
                        )
                        total = total + jnp.where(position == float(2 * lower + b), v, 0.0)
                pbuf[pr, a] = total.astype(BF16)
            return s

        lax.fori_loop(0, maps_here, one, 0)

    def second_rows(bit):
        return pl.ds(pl.multiple_of(bit * (half // 2), half // 2), half // 2)

    def piece_rows(p):
        return pl.ds(pl.multiple_of(p * piece, piece), piece)

    def term_slot(q):
        return lax.rem(q, 2 * TAPS)

    def c2(q):
        src = terms.at[term_slot(q), second_rows(1 - h_bit)]
        return remote(src, r2.at[q], r2_s.at[q], r2_r.at[q], h_peer, z, c)

    def c3(q, p):
        slot = lax.rem(z - p + chips - 1, chips)
        return remote(
            r2.at[q, piece_rows(p)], r3.at[q, slot], r3_s.at[q, p], r3_r.at[q, slot], m, p, c
        )

    def unit_of(q):
        k = lax.div(q, TAPS)
        return (LAYERS - 1 - k) * TAPS + (q - k * TAPS)

    def region(q, start, size, lane, lanes):
        start = pl.multiple_of(c * half + start, piece)
        lane = pl.multiple_of(lane, half)
        return kg_ref.at[unit_of(q), pl.ds(start, size), pl.ds(lane, lanes)]

    def cz(q, p, zz):
        part = region(q, h_bit * (half // 2) + p * piece, piece, g_bit * half, half)
        return remote(fin.at[q], part, az_s.at[q, zz], az_r.at[q, p], m, zz, c)

    def cl(q):
        part = region(q, h_bit * (half // 2) + z * piece, piece, g_bit * half, half)
        return pltpu.make_async_copy(fin.at[q], part, loc_s.at[q])

    def cb(q):
        part = region(q, h_bit * (half // 2), half // 2, g_bit * half, half)
        return remote(part, part, ab_s.at[q], ab_r.at[q], h_peer, z, c)

    def ca(q):
        part = region(q, 0, half, g_bit * half, half)
        return remote(part, part, aa_s.at[q], aa_r.at[q], g_peer, z, c)

    def cp(q):
        part = region(q, 0, half, 0, 2 * half)
        return remote(part, part, ap_s.at[q], ap_r.at[q], m, z, other)

    def ready_terms(l):
        at_copy(l).wait_recv()
        for chip in range(2):
            for a in range(maps_here):
                first = a * (band + 2) * PAD
                rows = act_t[l, chip, :, first : first + (band + 2) * PAD]
                act_b[chip, :, a * band * PAD : (a + 1) * band * PAD] = rows[:, PAD : PAD + band * PAD]
        slot = lax.rem(l, 2)

        def variants(a, s):
            dzr_copy(l, a, 0).wait_recv()
            for chip in range(2):
                for rr in range(band):
                    for n in tiles:
                        if chip == 0:
                            mine, theirs = dz_own[slot, a, 1 + rr, :, n], dz_oth[slot, a, 1 + rr, :, n]
                            v = jnp.where(g_bit == c, mine, theirs)
                        else:
                            v = dzr[l, a, rr, :, n]
                        dzv[1, chip, a, rr, :, n] = v
                        v = v.astype(F32)
                        dzv[0, chip, a, rr, :, n] = pltpu.roll(v, PAD - 1, 0).astype(BF16)
                        dzv[2, chip, a, rr, :, n] = pltpu.roll(v, 1, 0).astype(BF16)
            return s

        lax.fori_loop(0, maps_here, variants, 0)

    def tap_terms(l, i, j):
        if i == 1:
            lhs = [act_b[0], act_b[1]]
        else:
            lhs = []
            for chip in range(2):
                for a in range(maps_here):
                    first = (a * (band + 2) + i) * PAD
                    lhs.append(act_t[l, chip, :, first : first + band * PAD])
        rhs = dzv[j].reshape(2 * pixels, half)
        q = (LAYERS - 1 - l) * TAPS + 3 * i + j
        got = jnp.dot(jnp.concatenate(lhs, 1), rhs, preferred_element_type=F32)
        terms[term_slot(q)] = got.astype(BF16)
        c2(q).start()

    def weight_terms(l, i):
        lax.fori_loop(0, 3, lambda j, s: (tap_terms(l, i, j), s)[1], 0)

    def stage_second(q):
        c2(q).wait()
        kept = terms[term_slot(q), second_rows(h_bit)].astype(F32)
        r2[q] = (r2[q].astype(F32) + kept).astype(BF16)

        def give(k):
            p = lax.rem(z + k, chips)

            @pl.when(p < owners)
            def _():
                c3(q, p).start()

        each(1, chips, give)

    def stage_sum(q):
        @pl.when(z < owners)
        def _():
            for k in range(chips - 1):
                remote(
                    r3.at[q, k], r3.at[q, k], r3_s.at[q, 0], r3_r.at[q, k], m, z, c
                ).wait_recv()
            total = r2[q, piece_rows(z)].astype(F32)
            for k in range(chips - 1):
                total = total + r3[q, k].astype(F32)
            fin[q] = total.astype(BF16)
            each(1, chips, lambda k: cz(q, z, lax.rem(z + k, chips)).start())
            cl(q).start()

    def stage_back(q):
        def arrived(k):
            p = lax.rem(z + k, chips)

            @pl.when(p < owners)
            def _():
                cz(q, p, p).wait_recv()

        each(1, chips, arrived)

        @pl.when(z < owners)
        def _():
            cl(q).wait()

        cb(q).start()

    def stage_first(q):
        cb(q).wait_recv()
        ca(q).start()

        def given(k):
            p = lax.rem(z + k, chips)

            @pl.when(p < owners)
            def _():
                c3(q, p).wait_send()

        each(1, chips, given)

    def stage_chip(q):
        ca(q).wait_recv()
        cp(q).start()

        @pl.when(z < owners)
        def _():
            each(1, chips, lambda k: cz(q, z, lax.rem(z + k, chips)).wait_send())

    def stage_done(q):
        cb(q).wait_send()
        ca(q).wait_send()
        cp(q).wait()

    def run(stage, first, last):
        lax.fori_loop(first, last, lambda q, s: (stage(q), s)[1], 0)

    def sent_dz(l):
        for a in range(maps_here):
            dz_copy(l, a).wait_send()
            for way in range(2):
                if_wanted(way, dzr_copy(l, a, way).wait_send)

    def backward(k, carry):
        l = LAYERS - 1 - k
        gain, shift = gain_of(l), shift_of(l)

        def gradient(a, rr, n):
            zhat = (zbuf[l, a, rr, :, n] - row_of(avg_t, l, a)[:, n]) * row_of(scl_t, l, a)[:, n]
            y = zhat * gain[:, n] + shift[:, n]
            s = jax.nn.sigmoid(y)
            if rr in (0, band + 1):
                upstream = dhh[l, rr // (band + 1), a, :, n].astype(F32)
            else:
                upstream = dh[a, rr - 1, :, n]
            dy = upstream * (s * (1.0 + y * (1.0 - s)))
            dy = jnp.where(column[:, n] < limit(a, rr), dy, 0.0)
            return dy, zhat

        def collect(a, tile):
            plains, crosses = [], []
            for n in tiles:
                plain = jnp.zeros((PAD, 128), F32)
                crossed = jnp.zeros((PAD, 128), F32)
                for rr in range(1, band + 1):
                    dy, zhat = gradient(a, rr, n)
                    dh[a, rr - 1, :, n] = dy
                    plain = plain + dy
                    crossed = crossed + dy * zhat
                plains.append(jnp.sum(plain, 0, keepdims=True))
                crosses.append(jnp.sum(crossed, 0, keepdims=True))
            tile = jnp.where(row8 == a, jnp.concatenate(plains, 1), tile)
            return jnp.where(row8 == a + maps_here, jnp.concatenate(crosses, 1), tile)

        e = LAYERS + l
        tile = lax.fori_loop(0, maps_here, collect, jnp.zeros((8, half), F32))
        send_z(e, tile)

        @pl.when(k == LAYERS - 1)
        def _():
            run(stage_second, 0, TAPS)

        @pl.when(k > 0)
        def _():
            ready_terms(l + 1)
            weight_terms(l + 1, 0)

        wait_z(e)
        total = st1[e, 0]
        for zz in range(1, chips):
            total = total + st1[e, zz]
        send_m(e, total)

        @pl.when(k > 0)
        def _():
            weight_terms(l + 1, 1)
            weight_terms(l + 1, 2)
            wait_halo(dh_halo, l)

        @pl.when(k == 0)
        def _():
            pool()

        wait_m(e)
        total = st2[e, 0]
        for mm in range(1, PLANE):
            total = total + st2[e, mm]
        sums_own[pl.ds(l, 1), :] = jnp.sum(
            jnp.where(row8 >= maps_here, total, 0.0), 0, keepdims=True
        )
        sums_own[pl.ds(LAYERS + l, 1), :] = jnp.sum(
            jnp.where(row8 < maps_here, total, 0.0), 0, keepdims=True
        )
        plains = jnp.zeros((8, half), F32)
        crosses = jnp.zeros((8, half), F32)
        for a in range(maps_here):
            plain = jnp.zeros((8, half), F32)
            crossed = jnp.zeros((8, half), F32)
            for mm in range(PLANE):
                v = st2[e, mm]
                plain = plain + coef[a, mm] * v
                crossed = crossed + coef[a, mm] * pltpu.roll(v, 8 - maps_here, 0)
            count = cnt_t[a : a + 1, :]
            plain = gain * (jnp.sum(plain, 0, keepdims=True) / count)
            crossed = gain * (jnp.sum(crossed, 0, keepdims=True) / count)
            plains = jnp.where(row8 == a, plain, plains)
            crosses = jnp.where(row8 == a, crossed, crosses)
        tb_t[0] = plains
        ta_t[0] = crosses

        def settle(a, s):
            for n in tiles:
                average, scaling = row_of(avg_t, l, a)[:, n], row_of(scl_t, l, a)[:, n]
                plain, crossed = row_of(tb_t, 0, a)[:, n], row_of(ta_t, 0, a)[:, n]
                for rr in range(band + 2):
                    if rr in (0, band + 1):
                        dy, zhat = gradient(a, rr, n)
                    else:
                        dy = dh[a, rr - 1, :, n]
                        zhat = (zbuf[l, a, rr, :, n] - average) * scaling
                    v = scaling * (dy * gain[:, n] - plain - zhat * crossed)
                    v = jnp.where(column[:, n] < limit(a, rr), v, 0.0)
                    dz_own[lax.rem(l, 2), a, rr, :, n] = v.astype(BF16)
            dz_copy(l, a).start()
            for way in range(2):
                if_wanted(way, dzr_copy(l, a, way).start)
            return s

        @pl.when(k == 2)
        def _():
            sent_dz(LAYERS - 1)

        lax.fori_loop(0, maps_here, settle, 0)
        products(dz_own, l, (0, 1, 2), wa, True, True)
        weight_copy(l, 2).wait()
        for a in range(maps_here):
            dz_copy(l, a).wait_recv()
        products(dz_oth, l, (0, 1, 2), wb, True, False)

        def gather(a, s):
            for n in tiles:
                for rr in range(band):
                    v = shifted(a, rr, 2, 0, n)
                    dh[a, rr, :, n] = v
                    if rr in (0, band - 1):
                        dhs[rr // (band - 1), a, :, n] = v.astype(BF16)
            return s

        lax.fori_loop(0, maps_here, gather, 0)

        @pl.when(l > 0)
        def _():
            start_halo(dh_halo, l - 1)

        return carry

    lax.fori_loop(0, LAYERS, backward, 0)
    run(stage_sum, 0, TAPS)

    def input_rows(a, s):
        for rr in range(band):
            igbuf[rr // 2, a, rr % 2] = jnp.where(
                column < width_of(a), dh[a, rr], 0.0
            )
        return s

    lax.fori_loop(0, maps_here, input_rows, 0)

    outs = (
        (
            remote(igbuf.at[other], ig_ref.at[c], out_s.at[0], out_r.at[0], m, z, other),
            pltpu.make_async_copy(igbuf.at[c], ig_ref.at[c], out_l.at[0]),
        ),
        (
            remote(pbuf.at[other], pooled_ref.at[c], out_s.at[1], out_r.at[1], m, z, other),
            pltpu.make_async_copy(pbuf.at[c], pooled_ref.at[c], out_l.at[1]),
        ),
        (
            remote(sums_own, sums_ref.at[c], out_s.at[2], out_r.at[2], m, z, other),
            pltpu.make_async_copy(sums_own, sums_ref.at[c], out_l.at[2]),
        ),
    )
    for there, here in outs:
        there.start()
        here.start()

    g_partner.wait_send()
    sent_x_halo(4, 6)

    def sent(e, carry):
        each(1, chips, lambda k: z_copy(e, k).wait_send())
        each(1, PLANE, lambda k: m_copy(e, k).wait_send())
        return carry

    lax.fori_loop(0, 2 * LAYERS, sent, 0)
    for l in range(LAYERS):
        at_copy(l).wait_send()
    for l in range(LAYERS - 1):
        sent_dz(l)

    def drain(s, carry):
        @pl.when(s == EARLY)
        def _():
            ready_terms(0)

        for i in range(3):
            j = s - EARLY - 3 * i

            @pl.when(jnp.logical_and(j >= 0, j < 3))
            def _(i=i, j=j):
                tap_terms(0, i, j)

        for stage, first, lag in (
            (stage_done, 0, 3 * LAG),
            (stage_chip, 0, 2 * LAG),
            (stage_first, 0, LAG),
            (stage_back, 0, 0),
            (stage_sum, TAPS, LAG),
            (stage_second, TAPS, 0),
        ):
            q = first + s - lag

            @pl.when(jnp.logical_and(q >= first, q < UNITS))
            def _(stage=stage, q=q):
                stage(q)

        return carry

    lax.fori_loop(0, UNITS + 3 * LAG, drain, 0)
    for a in range(maps_here):
        act_copy(2, a).wait_send()
    for there, here in outs:
        there.wait()
        here.wait()


def solution(mesh):
    chips = mesh.shape["rows"] // 2

    def per_device(
        block_input,
        conv_weights,
        norm_gains,
        norm_shifts,
        map_width,
        map_group,
        pool_index,
        task_mask,
        task_weights,
        task_grads,
    ):
        maps_here, rows_here, columns, channels = block_input.shape
        pooled_columns = pool_index.shape[2]
        height = rows_here * mesh.shape["rows"]
        half = channels // 2
        band = 2 * rows_here
        pixels = maps_here * band * PAD
        owners = min(chips, 8)
        piece = half // 2 // owners
        rounds = 2 * LAYERS
        slots = 2 * UNITS * (chips - 1) * piece * half + 4 * rounds * chips * 8 * half
        grant = 35 * 1024 * 1024 + slots
        vmem, dma = pltpu.VMEM, pltpu.SemaphoreType.DMA
        tile = (maps_here, band + 2, PAD, half)
        edge = (2, maps_here, PAD, half)
        whole = pl.BlockSpec(memory_space=pltpu.VMEM)
        scalars = pl.BlockSpec(memory_space=pltpu.SMEM)
        anywhere = pl.BlockSpec(memory_space=pl.ANY)
        pooled, ig, kg, sums = pl.pallas_call(
            functools.partial(block_kernel, chips, height),
            out_shape=(
                jax.ShapeDtypeStruct((2, maps_here, PAD // 2, half), BF16),
                jax.ShapeDtypeStruct((2, maps_here, rows_here, PAD, half), F32),
                jax.ShapeDtypeStruct((UNITS, channels, channels), BF16),
                jax.ShapeDtypeStruct((2, 8, half), F32),
            ),
            in_specs=[whole, anywhere, whole, whole, scalars, scalars, whole, scalars, scalars, whole],
            out_specs=[anywhere] * 4,
            scratch_shapes=[
                vmem((LAYERS, 3, 3, half, half), BF16),
                vmem((LAYERS, 3, 3, half, half), BF16),
                vmem((2,) + tile, BF16),
                vmem((2,) + tile, BF16),
                vmem((LAYERS, 2, half, maps_here * (band + 2) * PAD), BF16),
                vmem((2, half, pixels), BF16),
                vmem((LAYERS,) + tile, F32),
                vmem(edge, BF16),
                vmem((LAYERS,) + edge, BF16),
                vmem((maps_here, band, PAD, half), F32),
                vmem(edge, BF16),
                vmem((LAYERS,) + edge, BF16),
                vmem((2,) + tile, BF16),
                vmem((2,) + tile, BF16),
                vmem((LAYERS, maps_here, band, PAD, half), BF16),
                vmem((3, 2, maps_here, band, PAD, half), BF16),
                vmem((3, pixels, half), F32),
                vmem((2, 2, maps_here, PAD // 2, half), F32),
                vmem((4, 2, maps_here, PAD // 2, half), F32),
                vmem((half // 128, PAD, 128), F32),
                vmem((2, maps_here, PAD // 2, half), BF16),
                vmem((2, maps_here, rows_here, PAD, half), F32),
                vmem((rounds, chips, 8, half), F32),
                vmem((rounds, PLANE, 8, half), F32),
                vmem((maps_here, PLANE, 8, half), F32),
                vmem((PLANE, 8, half), F32),
                vmem((2, 8, half), F32),
                vmem((8, half), F32),
                vmem((LAYERS, 8, half), F32),
                vmem((LAYERS, 8, half), F32),
                vmem((2, 8, half), F32),
                vmem((1, 8, half), F32),
                vmem((1, 8, half), F32),
                vmem((8, half), F32),
                vmem((2 * TAPS, half, half), BF16),
                vmem((UNITS, half // 2, half), BF16),
                vmem((UNITS, chips - 1, piece, half), BF16),
                vmem((UNITS, piece, half), BF16),
                dma((LAYERS, 3)),
                dma((6,)),
                dma((6,)),
                dma((3,)),
                dma((3,)),
                dma((rounds, chips)),
                dma((rounds, chips)),
                dma((rounds, PLANE)),
                dma((rounds, PLANE)),
                dma((LAYERS, 2)),
                dma((LAYERS, 2)),
                dma((LAYERS, 2)),
                dma((LAYERS, 2)),
                dma((LAYERS, maps_here)),
                dma((LAYERS, maps_here)),
                dma((LAYERS, maps_here)),
                dma((LAYERS, maps_here)),
                dma((3,)),
                dma((3,)),
                dma((3,)),
                dma((LAYERS,)),
                dma((LAYERS,)),
                dma((LAYERS, 2, maps_here)),
                dma((LAYERS, maps_here)),
                dma((UNITS,)),
                dma((UNITS,)),
                dma((UNITS, owners)),
                dma((UNITS, chips - 1)),
                dma((UNITS, chips)),
                dma((UNITS, owners)),
                dma((UNITS,)),
                dma((UNITS,)),
                dma((UNITS,)),
                dma((UNITS,)),
                dma((UNITS,)),
                dma((UNITS,)),
                dma((UNITS,)),
            ],
            compiler_params=pltpu.CompilerParams(
                collective_id=0,
                has_side_effects=True,
                vmem_limit_bytes=grant,
            ),
        )(
            block_input,
            conv_weights,
            norm_gains,
            norm_shifts,
            map_width,
            map_group,
            pool_index,
            task_mask,
            task_weights,
            task_grads,
        )
        pooled = jnp.concatenate([pooled[0], pooled[1]], -1)[:, None, :pooled_columns]
        input_grad = jnp.concatenate([ig[0], ig[1]], -1)[:, :, :columns]
        sums = jnp.concatenate([sums[0], sums[1]], -1)
        return (
            pooled,
            input_grad,
            kg.astype(F32).reshape(conv_weights.shape),
            sums[:LAYERS],
            sums[LAYERS : 2 * LAYERS],
        )

    return jax.shard_map(
        per_device,
        mesh=mesh,
        in_specs=(
            P("maps", "rows", None, None),
            P(),
            P(),
            P(),
            P(),
            P(),
            P("maps", "rows", None, None),
            P("maps", None),
            P(),
            P(None, "maps", "rows", None, None),
        ),
        out_specs=(P("maps", "rows", None, None), P("maps", "rows", None, None), P(), P(), P()),
        check_vma=False,
    )
```

```python
import functools

import jax
import jax.numpy as jnp
from jax import lax
from jax.experimental import pallas as pl
from jax.experimental.pallas import tpu as pltpu
from jax.sharding import PartitionSpec as P

MESH = pl.DeviceIdType.MESH
epsilon = 1e-05
PAD = 64
LAYERS = 3
TAPS = 9
UNITS = LAYERS * TAPS
PLANE = 4
LAG = 4
EARLY = 2
FOLD = 3
F32 = jnp.float32
BF16 = jnp.bfloat16


def each(first, last, body):
    if last - first <= 8:
        for k in range(first, last):
            body(k)
    else:
        lax.fori_loop(first, last, lambda k, s: (body(k), s)[1], 0)


def block_kernel(
    chips,
    height,
    x_ref,
    w_ref,
    gain_hbm,
    shift_hbm,
    width_hbm,
    group_hbm,
    index_hbm,
    tmask_hbm,
    tweight_hbm,
    tgrad_hbm,
    pooled_ref,
    ig_ref,
    kg_ref,
    sums_ref,
    gain_ref,
    shift_ref,
    width_ref,
    group_ref,
    index_ref,
    tmask_ref,
    tweight_ref,
    tgrad_ref,
    wa,
    wb,
    act_own,
    act_oth,
    act_t,
    act_b,
    zbuf,
    zs,
    zh,
    dh,
    dhs,
    dhh,
    dz_own,
    dz_oth,
    dzr,
    dzv,
    prod,
    gsrc,
    gbuf,
    hrow,
    pbuf,
    st1,
    st2,
    coef,
    nall,
    inv_t,
    cnt_t,
    avg_t,
    scl_t,
    mean_t,
    tb_t,
    ta_t,
    sums_own,
    terms,
    r2,
    rf,
    r3,
    fin,
    in_sem,
    w_sem,
    x_s,
    x_r,
    g_s,
    g_r,
    st1_s,
    st1_r,
    st2_s,
    st2_r,
    zh_s,
    zh_r,
    dh_s,
    dh_r,
    act_s,
    act_r,
    dz_s,
    dz_r,
    out_s,
    out_r,
    out_l,
    at_s,
    at_r,
    dzr_s,
    dzr_r,
    r2_s,
    r2_r,
    rf_s,
    rf_r,
    r3_s,
    r3_r,
    az_s,
    az_r,
    af_s,
    af_r,
    ab_s,
    ab_r,
    aa_s,
    aa_r,
    ap_s,
    ap_r,
    loc_s,
):
    maps_here = x_ref.shape[0]
    columns = x_ref.shape[2]
    half = x_ref.shape[3] // 2
    tasks = tgrad_ref.shape[0]
    pooled_columns = tgrad_ref.shape[3]
    lanes = half // 128
    tiles = [slice(n * 128, (n + 1) * 128) for n in range(lanes)]
    band = 4
    pixels = maps_here * band * PAD
    actives = chips // 2
    owners = min(actives, 8)
    piece = (half // 2) // owners
    m = lax.axis_index("maps")
    r = lax.axis_index("rows")
    c = lax.rem(r, 2)
    z = lax.div(r, 2)
    other = 1 - c
    first_map = m * maps_here
    x_bit = lax.rem(m, 2)
    y_bit = lax.div(m, 2)
    x_peer = m + 1 - 2 * x_bit
    y_peer = m + 2 - 4 * y_bit
    g_bit = (1 - c) * x_bit + c * y_bit
    h_bit = (1 - c) * y_bit + c * x_bit
    g_peer = (1 - c) * x_peer + c * y_peer
    h_peer = (1 - c) * y_peer + c * x_peer
    pair = lax.div(z, 2)
    turn = lax.rem(pair, 2)
    active_z = 2 * pair + 1 - turn
    is_active = z == active_z
    is_passive = z != active_z
    is_owner = jnp.logical_and(is_active, pair < owners)
    up_there = z > 0
    down_there = z < chips - 1
    row8 = lax.broadcasted_iota(jnp.int32, (8, half), 0)
    column = lax.broadcasted_iota(jnp.int32, (PAD, half), 0)

    def remote(src, dst, send, recv, mm, zz, cc):
        return pltpu.make_async_remote_copy(
            src_ref=src,
            dst_ref=dst,
            send_sem=send,
            recv_sem=recv,
            device_id=(mm, zz * 2 + cc),
            device_id_type=MESH,
        )

    def own_half(v):
        return jnp.where(c == 0, v[..., :half], v[..., half:])

    def width_of(a):
        return width_ref[first_map + a]

    own_at = pl.ds(pl.multiple_of(c * half, half), half)
    oth_at = pl.ds(pl.multiple_of(other * half, half), half)

    def weight_copy(l, n):
        dst = (wa, wb, wb)[n]
        k_at, o_at = ((own_at, own_at), (oth_at, own_at), (own_at, oth_at))[n]
        return pltpu.make_async_copy(w_ref.at[l, :, :, k_at, o_at], dst.at[l], w_sem.at[l, n])

    fetches = [
        pltpu.make_async_copy(src, dst, in_sem.at[n])
        for n, (src, dst) in enumerate(
            (
                (width_hbm, width_ref),
                (group_hbm, group_ref),
                (tmask_hbm, tmask_ref),
                (tweight_hbm, tweight_ref),
                (gain_hbm, gain_ref),
                (shift_hbm, shift_ref),
                (index_hbm.at[:, :, 0, :], index_ref),
                (tgrad_hbm, tgrad_ref),
            )
        )
    ]
    for fetch in fetches:
        fetch.start()
    for l in range(LAYERS):
        weight_copy(l, 0).start()
        weight_copy(l, 1).start()

    barrier = pltpu.get_barrier_semaphore()

    def greet(k):
        rr = lax.rem(r + k, 2 * chips)
        pl.semaphore_signal(barrier, inc=1, device_id=(m, rr), device_id_type=MESH)

    each(1, 2 * chips, greet)
    for k in range(1, PLANE):
        for core in (c, other):
            there = (lax.rem(m + k, PLANE), z * 2 + core)
            pl.semaphore_signal(barrier, inc=1, device_id=there, device_id_type=MESH)

    for fetch in fetches:
        fetch.wait()

    mine = pl.ds(1 + 2 * c, 2)
    for a in range(maps_here):
        inside = lax.broadcasted_iota(jnp.int32, (columns, 2 * half), 0) < width_of(a)
        for rr in range(2):
            v = jnp.where(inside, x_ref[a, rr].astype(F32), 0.0).astype(BF16)
            spot = 1 + 2 * c + rr
            act_own[0, a, spot, pl.ds(48, 16), :] = jnp.zeros((16, half), BF16)
            act_oth[0, a, spot, pl.ds(48, 16), :] = jnp.zeros((16, half), BF16)
            act_own[0, a, spot, pl.ds(0, columns), :] = own_half(v)
            act_oth[0, a, spot, pl.ds(0, columns), :] = jnp.where(
                c == 0, v[:, half:], v[:, :half]
            )

    @pl.when(z == 0)
    def _():
        act_own[0, :, 0] = jnp.zeros((maps_here, PAD, half), BF16)
        act_oth[0, :, 0] = jnp.zeros((maps_here, PAD, half), BF16)

    @pl.when(z == chips - 1)
    def _():
        act_own[0, :, 5] = jnp.zeros((maps_here, PAD, half), BF16)
        act_oth[0, :, 5] = jnp.zeros((maps_here, PAD, half), BF16)

    gsrc[...] = jnp.zeros(gsrc.shape, F32)
    for a in range(maps_here):
        total = None
        for t in range(tasks):
            scale = tweight_ref[t] * tmask_ref[a, t].astype(F32)
            term = tgrad_ref[t, a, 0].astype(F32) * scale
            total = term if total is None else total + term
        position = index_ref[a].astype(F32)
        for h in range(2):
            gsrc[h, 0, a, pl.ds(0, pooled_columns), :] = total[:, h * half : (h + 1) * half]
            gsrc[h, 1, a, pl.ds(0, pooled_columns), :] = position[:, h * half : (h + 1) * half]
    gbuf[1 + c] = gsrc[c]

    pl.semaphore_wait(barrier, 2 * chips - 1 + 2 * (PLANE - 1))

    x_partner = (
        remote(act_own.at[0, :, mine], act_oth.at[0, :, mine], x_s.at[0], x_r.at[0], m, z, other),
        remote(act_oth.at[0, :, mine], act_own.at[0, :, mine], x_s.at[1], x_r.at[1], m, z, other),
    )
    g_partner = remote(gsrc.at[other], gbuf.at[1 + c], g_s.at[0], g_r.at[0], m, z, other)

    def x_halo(n, src_row, dst_row, zz):
        cc = (c, c, other, other, c, other)[n]
        low = dst_row == band + 1
        if n >= 4:
            src, dst = gsrc.at[cc], gbuf.at[3 if low else 0]
            return remote(src, dst, g_s.at[n - 3], g_r.at[1 if low else 2], m, zz, cc)
        src = (act_own, act_oth, act_own, act_oth)[n].at[0, :, src_row]
        dst = (act_own, act_oth, act_oth, act_own)[n].at[0, :, dst_row]
        return remote(src, dst, x_s.at[2 + n], x_r.at[(2 if low else 4) + n % 2], m, zz, cc)

    for copy in x_partner:
        copy.start()

    @pl.when(jnp.logical_and(c == 0, up_there))
    def _():
        for n in range(4):
            x_halo(n, 1, 5, z - 1).start()

    @pl.when(jnp.logical_and(c == 1, down_there))
    def _():
        for n in range(4):
            x_halo(n, 4, 0, z + 1).start()

    g_partner.start()

    @pl.when(jnp.logical_and(c == 0, up_there))
    def _():
        for n in range(4, 6):
            x_halo(n, 1, 5, z - 1).start()

    @pl.when(jnp.logical_and(c == 1, down_there))
    def _():
        for n in range(4, 6):
            x_halo(n, 4, 0, z + 1).start()

    for mm in range(PLANE):
        sizes = jnp.zeros((8, half), F32)
        for b in range(maps_here):
            sizes = jnp.where(
                row8 == b, (width_ref[mm * maps_here + b] * height).astype(F32), sizes
            )
        nall[mm] = sizes
    inside_sizes = jnp.zeros((8, half), F32)
    for b in range(maps_here):
        inside_sizes = jnp.where(row8 == b, (width_of(b) * band).astype(F32), inside_sizes)
    inv_t[0] = inside_sizes
    inv_t[1] = jnp.where(row8 < maps_here, 1.0 / jnp.maximum(inside_sizes, 1.0), 0.0)
    counts = jnp.ones((8, half), F32)
    for a in range(maps_here):
        total = jnp.zeros((1, half), F32)
        for mm in range(PLANE):
            same = jnp.zeros((8, half), F32)
            for b in range(maps_here):
                alike = group_ref[first_map + a] == group_ref[mm * maps_here + b]
                same = jnp.where(row8 == b, jnp.where(alike, 1.0, 0.0), same)
            coef[a, mm] = same
            total = total + jnp.sum(same * nall[mm], 0, keepdims=True)
        counts = jnp.where(row8 == a, total, counts)
    cnt_t[...] = counts

    def z_copy(e, k):
        zz = lax.rem(z + k, chips)
        return remote(st1.at[e, z], st1.at[e, z], st1_s.at[e, k], st1_r.at[e, z], m, zz, c)

    def z_arrival(e, k):
        zz = lax.rem(z + k, chips)
        return remote(st1.at[e, zz], st1.at[e, zz], st1_s.at[e, k], st1_r.at[e, zz], m, zz, c)

    def m_copy(e, k):
        mm = lax.rem(m + k, PLANE)
        return remote(st2.at[e, m], st2.at[e, m], st2_s.at[e, k], st2_r.at[e, m], mm, z, c)

    def m_arrival(e, k):
        mm = lax.rem(m + k, PLANE)
        return remote(st2.at[e, mm], st2.at[e, mm], st2_s.at[e, k], st2_r.at[e, mm], mm, z, c)

    def send_z(e, tile):
        st1[e, z] = tile
        each(1, chips, lambda k: z_copy(e, k).start())

    def wait_z(e):
        each(1, chips, lambda k: z_arrival(e, k).wait_recv())

    def send_m(e, tile):
        st2[e, m] = tile
        each(1, PLANE, lambda k: m_copy(e, k).start())

    def wait_m(e):
        each(1, PLANE, lambda k: m_arrival(e, k).wait_recv())

    def products(source, l, taps, kernel, transposed, fresh):
        starts = [2 - i if transposed else i for i in taps]
        lhs = jnp.concatenate(
            [source[lax.rem(l, 2), :, s : s + band].reshape(pixels, half) for s in starts], 1
        )
        for j in range(3):
            rhs = jnp.concatenate([kernel[l, i, j] for i in taps], 1 if transposed else 0)
            got = lax.dot_general(
                lhs,
                rhs,
                (((1,), (1 if transposed else 0,)), ((), ())),
                preferred_element_type=F32,
            )
            if fresh:
                prod[j] = got
            else:
                prod[j] = prod[j] + got

    def shifted(a, rr, before, behind, n):
        rows = pl.ds(pl.multiple_of((a * band + rr) * PAD, PAD), PAD)
        return (
            prod[1, rows, n]
            + pltpu.roll(prod[before, rows, n], 1, 0)
            + pltpu.roll(prod[behind, rows, n], PAD - 1, 0)
        )

    def row_of(table, l, a):
        return table[l, pl.ds(a, 1), :]

    def gain_of(l):
        return own_half(gain_ref[pl.ds(l, 1), :])

    def shift_of(l):
        return own_half(shift_ref[pl.ds(l, 1), :])

    def limit(a, rr):
        w = width_of(a)
        if rr == 0:
            return jnp.where(up_there, w, 0)
        if rr == band + 1:
            return jnp.where(down_there, w, 0)
        return w

    def z_halo(l, way):
        there = z - 1 + 2 * way
        return remote(zs.at[way], zh.at[l, 1 - way], zh_s.at[l, way], zh_r.at[l, way], m, there, c)

    def dh_halo(l, way):
        there = z - 1 + 2 * way
        return remote(dhs.at[way], dhh.at[l, 1 - way], dh_s.at[l, way], dh_r.at[l, way], m, there, c)

    def start_halo(halo, l):
        @pl.when(up_there)
        def _():
            halo(l, 0).start()

        @pl.when(down_there)
        def _():
            halo(l, 1).start()

    def wait_halo(halo, l):
        @pl.when(up_there)
        def _():
            halo(l, 1).wait_recv()
            halo(l, 0).wait_send()

        @pl.when(down_there)
        def _():
            halo(l, 0).wait_recv()
            halo(l, 1).wait_send()

    def act_copy(l, a):
        slot = lax.rem(l, 2)
        src, dst = act_own.at[slot, a], act_oth.at[slot, a]
        return remote(src, dst, act_s.at[l, a], act_r.at[l, a], m, z, other)

    def at_copy(l):
        return remote(act_t.at[l, 0], act_t.at[l, 1], at_s.at[l], at_r.at[l], g_peer, z, c)

    def dzr_copy(l, a, way):
        src, dst = dz_own.at[lax.rem(l, 2), a, pl.ds(1, band)], dzr.at[l, a]
        peer = (x_peer, y_peer)[way]
        return remote(src, dst, dzr_s.at[l, way, a], dzr_r.at[l, a], peer, z, way)

    def if_wanted(way, body):
        @pl.when((x_bit, y_bit)[way] + c == 1)
        def _():
            body()

    def dz_copy(l, a):
        slot = lax.rem(l, 2)
        src, dst = dz_own.at[slot, a], dz_oth.at[slot, a]
        return remote(src, dst, dz_s.at[l, a], dz_r.at[l, a], m, z, other)

    def wait_x_halo(first, last):
        @pl.when(up_there)
        def _():
            for n in (0, 1, 4)[first:last]:
                x_halo(n, 4, 0, z - 1).wait_recv()

        @pl.when(down_there)
        def _():
            for n in (0, 1, 4)[first:last]:
                x_halo(n, 1, 5, z + 1).wait_recv()

    def sent_x_halo(first, last):
        @pl.when(jnp.logical_and(c == 0, up_there))
        def _():
            for n in range(first, last):
                x_halo(n, 1, 5, z - 1).wait_send()

        @pl.when(jnp.logical_and(c == 1, down_there))
        def _():
            for n in range(first, last):
                x_halo(n, 4, 0, z + 1).wait_send()

    def forward(l, first):
        weight_copy(l, 0).wait()
        weight_copy(l, 1).wait()
        if first:
            for copy in x_partner:
                copy.wait_recv()
            products(act_own, l, (1,), wa, False, True)
            products(act_oth, l, (1,), wb, False, False)
            wait_x_halo(0, 2)
            products(act_own, l, (0, 2), wa, False, False)
            products(act_oth, l, (0, 2), wb, False, False)
        else:
            products(act_own, l, (0, 1, 2), wa, False, True)
            for a in range(maps_here):
                act_copy(l, a).wait_recv()
            products(act_oth, l, (0, 1, 2), wb, False, False)
        weight_copy(l, 2).start()

        def collect(a, tile):
            inside = column[:, :128] < width_of(a)
            pixels_inside = (width_of(a) * band).astype(F32)
            totals, squares = [], []
            for n in tiles:
                total = jnp.zeros((PAD, 128), F32)
                for rr in range(band):
                    v = shifted(a, rr, 0, 2, n)
                    zbuf[l, a, 1 + rr, :, n] = v
                    total = total + jnp.where(inside, v, 0.0)
                total = jnp.sum(total, 0, keepdims=True)
                mean = total / pixels_inside
                square = jnp.zeros((PAD, 128), F32)
                for rr in range(band):
                    v = jnp.where(inside, zbuf[l, a, 1 + rr, :, n] - mean, 0.0)
                    square = square + v * v
                    if rr in (0, band - 1):
                        zs[rr // (band - 1), a, :, n] = v.astype(BF16)
                totals.append(total)
                squares.append(jnp.sum(square, 0, keepdims=True))
            tile = jnp.where(row8 == a, jnp.concatenate(totals, 1), tile)
            return jnp.where(row8 == a + maps_here, jnp.concatenate(squares, 1), tile)

        tile = lax.fori_loop(0, maps_here, collect, jnp.zeros((8, half), F32))
        send_z(l, tile)
        start_halo(z_halo, l)
        act_t[l, 0] = act_own[lax.rem(l, 2)].reshape(maps_here * (band + 2) * PAD, half).T
        wait_z(l)
        sizes, inverse = inv_t[0], inv_t[1]
        mean_t[0] = st1[l, jnp.maximum(z - 1, 0)] * inverse
        mean_t[1] = st1[l, jnp.minimum(z + 1, chips - 1)] * inverse
        total = st1[l, 0]
        for zz in range(1, chips):
            total = total + st1[l, zz]
        mean = total * inverse * (1.0 / chips)
        square = jnp.zeros((8, half), F32)
        for zz in range(chips):
            v = st1[l, zz]
            gap = v * inverse - mean
            square = square + pltpu.roll(v, 8 - maps_here, 0) + sizes * gap * gap
        tile = jnp.where(row8 < maps_here, mean, pltpu.roll(square, maps_here, 0))
        send_m(l, jnp.where(row8 < 2 * maps_here, tile, 0.0))
        wait_m(l)
        at_copy(l).start()
        averages = jnp.zeros((8, half), F32)
        scalings = jnp.zeros((8, half), F32)
        for a in range(maps_here):
            count = cnt_t[a : a + 1, :]
            average = jnp.zeros((8, half), F32)
            for mm in range(PLANE):
                average = average + coef[a, mm] * nall[mm] * st2[l, mm]
            average = jnp.sum(average, 0, keepdims=True) / count
            variance = jnp.zeros((8, half), F32)
            for mm in range(PLANE):
                v = st2[l, mm]
                gap = v - average
                variance = variance + coef[a, mm] * (
                    pltpu.roll(v, 8 - maps_here, 0) + nall[mm] * gap * gap
                )
            variance = jnp.sum(variance, 0, keepdims=True) / count
            averages = jnp.where(row8 == a, average, averages)
            scalings = jnp.where(row8 == a, lax.rsqrt(variance + epsilon), scalings)
        avg_t[l] = averages
        scl_t[l] = scalings
        wait_halo(z_halo, l)

        def activate(a, s):
            gain, shift = gain_of(l), shift_of(l)
            for n in tiles:
                average = row_of(avg_t, l, a)[:, n]
                factor = row_of(scl_t, l, a)[:, n] * gain[:, n]
                for rr in range(band + 2):
                    if rr in (0, band + 1):
                        way = rr // (band + 1)
                        v = zh[l, way, a, :, n].astype(F32) + row_of(mean_t, way, a)[:, n]
                        zbuf[l, a, rr, :, n] = v
                    else:
                        v = zbuf[l, a, rr, :, n]
                    y = (v - average) * factor + shift[:, n]
                    h = jnp.where(column[:, n] < limit(a, rr), y * jax.nn.sigmoid(y), 0.0)
                    act_own[lax.rem(l + 1, 2), a, rr, :, n] = h.astype(BF16)

            @pl.when(l < LAYERS - 1)
            def _():
                act_copy(l + 1, a).start()

            return s

        if first:
            for copy in x_partner:
                copy.wait_send()
            sent_x_halo(0, 4)
        else:

            @pl.when(l == 2)
            def _():
                for a in range(maps_here):
                    act_copy(1, a).wait_send()

        lax.fori_loop(0, maps_here, activate, 0)

    forward(0, True)
    lax.fori_loop(1, LAYERS, lambda l, s: (forward(l, False), s)[1], 0)
    g_partner.wait_recv()
    wait_x_halo(2, 3)

    def unpool(a, s):
        for rr in range(band + 2):
            slot, lower = (rr + 1) // 2, (rr + 1) % 2
            g = gbuf[slot, 0, a]
            position = gbuf[slot, 1, a]
            for b in range(2):
                v = jnp.where(position == float(2 * lower + b), g, 0.0)
                for n in range(lanes):
                    hrow[n, pl.ds(b, PAD // 2, stride=2), :] = v[:, n * 128 : (n + 1) * 128]
            v = jnp.concatenate([hrow[n] for n in range(lanes)], 1)
            if rr in (0, band + 1):
                dhh[LAYERS - 1, rr // (band + 1), a] = v.astype(BF16)
            else:
                dh[a, rr - 1] = v
        return s

    lax.fori_loop(0, maps_here, unpool, 0)

    def pool():
        def one(a, s):
            for pr in range(2):
                total = jnp.zeros((PAD // 2, half), F32)
                position = gbuf[1 + pr, 1, a]
                for lower in range(2):
                    v = act_own[LAYERS % 2, a, 1 + 2 * pr + lower].astype(F32)
                    for n in range(lanes):
                        hrow[n] = v[:, n * 128 : (n + 1) * 128]
                    for b in range(2):
                        v = jnp.concatenate(
                            [hrow[n, pl.ds(b, PAD // 2, stride=2), :] for n in range(lanes)], 1
                        )
                        total = total + jnp.where(position == float(2 * lower + b), v, 0.0)
                pbuf[pr, a] = total.astype(BF16)
            return s

        lax.fori_loop(0, maps_here, one, 0)

    def second_rows(bit):
        return pl.ds(pl.multiple_of(bit * (half // 2), half // 2), half // 2)

    def piece_rows(p):
        return pl.ds(pl.multiple_of(p * piece, piece), piece)

    def term_slot(q):
        return lax.rem(q, 2 * TAPS)

    def c2(q):
        src = terms.at[term_slot(q), second_rows(1 - h_bit)]
        return remote(src, r2.at[q], r2_s.at[q], r2_r.at[q], h_peer, z, c)

    def z_of(n):
        return 2 * n + 1 - lax.rem(n, 2)

    def cf(q):
        passive_z = 2 * pair + turn
        there = active_z + passive_z - z
        return remote(r2.at[q], rf.at[term_slot(q)], rf_s.at[q], rf_r.at[q], m, there, c)

    def c3(q, p):
        slot = lax.rem(pair - p + actives - 1, actives)
        return remote(
            r2.at[q, piece_rows(p)], r3.at[q, slot], r3_s.at[q, p], r3_r.at[q, slot], m, z_of(p), c
        )

    def others(first, body, limit):
        def one(k):
            n = lax.rem(pair + k, actives)

            @pl.when(n < limit)
            def _():
                body(n)

        each(first, actives, one)

    def unit_of(q):
        k = lax.div(q, TAPS)
        return (LAYERS - 1 - k) * TAPS + (q - k * TAPS)

    def region(q, start, size, lane, lanes):
        start = pl.multiple_of(c * half + start, piece)
        lane = pl.multiple_of(lane, half)
        return kg_ref.at[unit_of(q), pl.ds(start, size), pl.ds(lane, lanes)]

    def cz(q, p, n):
        part = region(q, h_bit * (half // 2) + p * piece, piece, g_bit * half, half)
        return remote(fin.at[q], part, az_s.at[q, n], az_r.at[q, p], m, z_of(n), c)

    def cl(q):
        part = region(q, h_bit * (half // 2) + pair * piece, piece, g_bit * half, half)
        return pltpu.make_async_copy(fin.at[q], part, loc_s.at[q])

    def cu(q):
        passive_z = 2 * pair + turn
        there = active_z + passive_z - z
        part = region(q, h_bit * (half // 2), half // 2, g_bit * half, half)
        return remote(part, part, af_s.at[q], af_r.at[q], m, there, c)

    def cb(q):
        part = region(q, h_bit * (half // 2), half // 2, g_bit * half, half)
        return remote(part, part, ab_s.at[q], ab_r.at[q], h_peer, z, c)

    def ca(q):
        part = region(q, 0, half, g_bit * half, half)
        return remote(part, part, aa_s.at[q], aa_r.at[q], g_peer, z, c)

    def cp(q):
        part = region(q, 0, half, 0, 2 * half)
        return remote(part, part, ap_s.at[q], ap_r.at[q], m, z, other)

    def ready_terms(l):
        at_copy(l).wait_recv()
        for chip in range(2):
            for a in range(maps_here):
                first = a * (band + 2) * PAD
                rows = act_t[l, chip, :, first : first + (band + 2) * PAD]
                act_b[chip, :, a * band * PAD : (a + 1) * band * PAD] = rows[:, PAD : PAD + band * PAD]
        slot = lax.rem(l, 2)

        def variants(a, s):
            dzr_copy(l, a, 0).wait_recv()
            for chip in range(2):
                for rr in range(band):
                    for n in tiles:
                        if chip == 0:
                            mine, theirs = dz_own[slot, a, 1 + rr, :, n], dz_oth[slot, a, 1 + rr, :, n]
                            v = jnp.where(g_bit == c, mine, theirs)
                        else:
                            v = dzr[l, a, rr, :, n]
                        dzv[1, chip, a, rr, :, n] = v
                        v = v.astype(F32)
                        dzv[0, chip, a, rr, :, n] = pltpu.roll(v, PAD - 1, 0).astype(BF16)
                        dzv[2, chip, a, rr, :, n] = pltpu.roll(v, 1, 0).astype(BF16)
            return s

        lax.fori_loop(0, maps_here, variants, 0)

    def tap_terms(l, i, j):
        if i == 1:
            lhs = [act_b[0], act_b[1]]
        else:
            lhs = []
            for chip in range(2):
                for a in range(maps_here):
                    first = (a * (band + 2) + i) * PAD
                    lhs.append(act_t[l, chip, :, first : first + band * PAD])
        rhs = dzv[j].reshape(2 * pixels, half)
        q = (LAYERS - 1 - l) * TAPS + 3 * i + j
        got = jnp.dot(jnp.concatenate(lhs, 1), rhs, preferred_element_type=F32)
        terms[term_slot(q)] = got.astype(BF16)
        c2(q).start()

    def weight_terms(l, i):
        lax.fori_loop(0, 3, lambda j, s: (tap_terms(l, i, j), s)[1], 0)

    def stage_second(q):
        c2(q).wait()
        kept = terms[term_slot(q), second_rows(h_bit)].astype(F32)
        r2[q] = (r2[q].astype(F32) + kept).astype(BF16)

        @pl.when(is_passive)
        def _():
            cf(q).start()

    def stage_fold(q):
        @pl.when(is_active)
        def _():
            cf(q).wait_recv()
            r2[q] = (r2[q].astype(F32) + rf[term_slot(q)].astype(F32)).astype(BF16)
            others(1, lambda n: c3(q, n).start(), owners)

    def stage_sum(q):
        @pl.when(is_owner)
        def _():
            for k in range(actives - 1):
                remote(
                    r3.at[q, k], r3.at[q, k], r3_s.at[q, 0], r3_r.at[q, k], m, z, c
                ).wait_recv()
            total = r2[q, piece_rows(pair)].astype(F32)
            for k in range(actives - 1):
                total = total + r3[q, k].astype(F32)
            fin[q] = total.astype(BF16)
            others(1, lambda n: cz(q, pair, n).start(), actives)
            cl(q).start()

    def stage_back(q):
        @pl.when(is_active)
        def _():
            others(1, lambda n: cz(q, n, n).wait_recv(), owners)

        @pl.when(is_owner)
        def _():
            cl(q).wait()

        @pl.when(is_active)
        def _():
            cu(q).start()

        @pl.when(is_passive)
        def _():
            cu(q).wait_recv()

        cb(q).start()

    def stage_first(q):
        cb(q).wait_recv()
        ca(q).start()

        @pl.when(is_active)
        def _():
            others(1, lambda n: c3(q, n).wait_send(), owners)

        @pl.when(is_passive)
        def _():
            cf(q).wait_send()

    def stage_chip(q):
        ca(q).wait_recv()
        cp(q).start()

        @pl.when(is_owner)
        def _():
            others(1, lambda n: cz(q, pair, n).wait_send(), actives)

        @pl.when(is_active)
        def _():
            cu(q).wait_send()

    def stage_done(q):
        cb(q).wait_send()
        ca(q).wait_send()
        cp(q).wait()

    def run(stage, first, last):
        lax.fori_loop(first, last, lambda q, s: (stage(q), s)[1], 0)

    def sent_dz(l):
        for a in range(maps_here):
            dz_copy(l, a).wait_send()
            for way in range(2):
                if_wanted(way, dzr_copy(l, a, way).wait_send)

    def backward(k, carry):
        l = LAYERS - 1 - k
        gain, shift = gain_of(l), shift_of(l)

        def gradient(a, rr, n):
            zhat = (zbuf[l, a, rr, :, n] - row_of(avg_t, l, a)[:, n]) * row_of(scl_t, l, a)[:, n]
            y = zhat * gain[:, n] + shift[:, n]
            s = jax.nn.sigmoid(y)
            if rr in (0, band + 1):
                upstream = dhh[l, rr // (band + 1), a, :, n].astype(F32)
            else:
                upstream = dh[a, rr - 1, :, n]
            dy = upstream * (s * (1.0 + y * (1.0 - s)))
            dy = jnp.where(column[:, n] < limit(a, rr), dy, 0.0)
            return dy, zhat

        def collect(a, tile):
            plains, crosses = [], []
            for n in tiles:
                plain = jnp.zeros((PAD, 128), F32)
                crossed = jnp.zeros((PAD, 128), F32)
                for rr in range(1, band + 1):
                    dy, zhat = gradient(a, rr, n)
                    dh[a, rr - 1, :, n] = dy
                    plain = plain + dy
                    crossed = crossed + dy * zhat
                plains.append(jnp.sum(plain, 0, keepdims=True))
                crosses.append(jnp.sum(crossed, 0, keepdims=True))
            tile = jnp.where(row8 == a, jnp.concatenate(plains, 1), tile)
            return jnp.where(row8 == a + maps_here, jnp.concatenate(crosses, 1), tile)

        e = LAYERS + l
        tile = lax.fori_loop(0, maps_here, collect, jnp.zeros((8, half), F32))
        send_z(e, tile)

        @pl.when(k == LAYERS - 1)
        def _():
            run(stage_second, 0, TAPS)

        @pl.when(k > 0)
        def _():
            ready_terms(l + 1)
            weight_terms(l + 1, 0)

        wait_z(e)
        total = st1[e, 0]
        for zz in range(1, chips):
            total = total + st1[e, zz]
        send_m(e, total)

        @pl.when(k > 0)
        def _():
            weight_terms(l + 1, 1)
            weight_terms(l + 1, 2)
            wait_halo(dh_halo, l)

        @pl.when(k == 0)
        def _():
            pool()

        wait_m(e)
        total = st2[e, 0]
        for mm in range(1, PLANE):
            total = total + st2[e, mm]
        sums_own[pl.ds(l, 1), :] = jnp.sum(
            jnp.where(row8 >= maps_here, total, 0.0), 0, keepdims=True
        )
        sums_own[pl.ds(LAYERS + l, 1), :] = jnp.sum(
            jnp.where(row8 < maps_here, total, 0.0), 0, keepdims=True
        )
        plains = jnp.zeros((8, half), F32)
        crosses = jnp.zeros((8, half), F32)
        for a in range(maps_here):
            plain = jnp.zeros((8, half), F32)
            crossed = jnp.zeros((8, half), F32)
            for mm in range(PLANE):
                v = st2[e, mm]
                plain = plain + coef[a, mm] * v
                crossed = crossed + coef[a, mm] * pltpu.roll(v, 8 - maps_here, 0)
            count = cnt_t[a : a + 1, :]
            plain = gain * (jnp.sum(plain, 0, keepdims=True) / count)
            crossed = gain * (jnp.sum(crossed, 0, keepdims=True) / count)
            plains = jnp.where(row8 == a, plain, plains)
            crosses = jnp.where(row8 == a, crossed, crosses)
        tb_t[0] = plains
        ta_t[0] = crosses

        def settle(a, s):
            for n in tiles:
                average, scaling = row_of(avg_t, l, a)[:, n], row_of(scl_t, l, a)[:, n]
                plain, crossed = row_of(tb_t, 0, a)[:, n], row_of(ta_t, 0, a)[:, n]
                for rr in range(band + 2):
                    if rr in (0, band + 1):
                        dy, zhat = gradient(a, rr, n)
                    else:
                        dy = dh[a, rr - 1, :, n]
                        zhat = (zbuf[l, a, rr, :, n] - average) * scaling
                    v = scaling * (dy * gain[:, n] - plain - zhat * crossed)
                    v = jnp.where(column[:, n] < limit(a, rr), v, 0.0)
                    dz_own[lax.rem(l, 2), a, rr, :, n] = v.astype(BF16)
            dz_copy(l, a).start()
            for way in range(2):
                if_wanted(way, dzr_copy(l, a, way).start)
            return s

        @pl.when(k == 2)
        def _():
            sent_dz(LAYERS - 1)

        lax.fori_loop(0, maps_here, settle, 0)
        products(dz_own, l, (0, 1, 2), wa, True, True)
        weight_copy(l, 2).wait()
        for a in range(maps_here):
            dz_copy(l, a).wait_recv()
        products(dz_oth, l, (0, 1, 2), wb, True, False)

        def gather(a, s):
            for n in tiles:
                for rr in range(band):
                    v = shifted(a, rr, 2, 0, n)
                    dh[a, rr, :, n] = v
                    if rr in (0, band - 1):
                        dhs[rr // (band - 1), a, :, n] = v.astype(BF16)
            return s

        lax.fori_loop(0, maps_here, gather, 0)

        @pl.when(l > 0)
        def _():
            start_halo(dh_halo, l - 1)

        return carry

    lax.fori_loop(0, LAYERS, backward, 0)
    run(stage_fold, 0, TAPS)
    run(stage_sum, 0, TAPS)

    def input_rows(a, s):
        for rr in range(band):
            dh[a, rr] = jnp.where(column < width_of(a), dh[a, rr], 0.0)
        return s

    lax.fori_loop(0, maps_here, input_rows, 0)

    outs = (
        (
            remote(dh.at[:, pl.ds(2 * other, 2)], ig_ref.at[c], out_s.at[0], out_r.at[0], m, z, other),
            pltpu.make_async_copy(dh.at[:, pl.ds(2 * c, 2)], ig_ref.at[c], out_l.at[0]),
        ),
        (
            remote(pbuf.at[other], pooled_ref.at[c], out_s.at[1], out_r.at[1], m, z, other),
            pltpu.make_async_copy(pbuf.at[c], pooled_ref.at[c], out_l.at[1]),
        ),
        (
            remote(sums_own, sums_ref.at[c], out_s.at[2], out_r.at[2], m, z, other),
            pltpu.make_async_copy(sums_own, sums_ref.at[c], out_l.at[2]),
        ),
    )
    for there, here in outs:
        there.start()
        here.start()

    g_partner.wait_send()
    sent_x_halo(4, 6)

    def sent(e, carry):
        each(1, chips, lambda k: z_copy(e, k).wait_send())
        each(1, PLANE, lambda k: m_copy(e, k).wait_send())
        return carry

    lax.fori_loop(0, 2 * LAYERS, sent, 0)
    for l in range(LAYERS):
        at_copy(l).wait_send()
    for l in range(LAYERS - 1):
        sent_dz(l)

    def drain(s, carry):
        @pl.when(s == EARLY)
        def _():
            ready_terms(0)

        for i in range(3):
            j = s - EARLY - 3 * i

            @pl.when(jnp.logical_and(j >= 0, j < 3))
            def _(i=i, j=j):
                tap_terms(0, i, j)

        for stage, first, lag in (
            (stage_done, 0, 3 * LAG),
            (stage_chip, 0, 2 * LAG),
            (stage_first, 0, LAG),
            (stage_back, 0, 0),
            (stage_sum, TAPS, 2 * FOLD),
            (stage_fold, TAPS, FOLD),
            (stage_second, TAPS, 0),
        ):
            q = first + s - lag

            @pl.when(jnp.logical_and(q >= first, q < UNITS))
            def _(stage=stage, q=q):
                stage(q)

        return carry

    lax.fori_loop(0, UNITS + 3 * LAG, drain, 0)
    for a in range(maps_here):
        act_copy(2, a).wait_send()
    for there, here in outs:
        there.wait()
        here.wait()


def solution(mesh):
    chips = mesh.shape["rows"] // 2

    def per_device(
        block_input,
        conv_weights,
        norm_gains,
        norm_shifts,
        map_width,
        map_group,
        pool_index,
        task_mask,
        task_weights,
        task_grads,
    ):
        maps_here, rows_here, columns, channels = block_input.shape
        pooled_columns = pool_index.shape[2]
        height = rows_here * mesh.shape["rows"]
        half = channels // 2
        band = 2 * rows_here
        pixels = maps_here * band * PAD
        actives = chips // 2
        owners = min(actives, 8)
        piece = half // 2 // owners
        rounds = 2 * LAYERS
        slots = 2 * UNITS * (actives - 1) * piece * half + 4 * rounds * chips * 8 * half
        grant = (36 * 1024 + 256) * 1024 + slots
        vmem, dma = pltpu.VMEM, pltpu.SemaphoreType.DMA
        tile = (maps_here, band + 2, PAD, half)
        edge = (2, maps_here, PAD, half)
        whole = pl.BlockSpec(memory_space=pltpu.VMEM)
        outside = pl.BlockSpec(memory_space=pltpu.HBM)
        index_rows = jnp.transpose(pool_index, (0, 2, 1, 3))
        anywhere = pl.BlockSpec(memory_space=pl.ANY)
        pooled, ig, kg, sums = pl.pallas_call(
            functools.partial(block_kernel, chips, height),
            out_shape=(
                jax.ShapeDtypeStruct((2, maps_here, PAD // 2, half), BF16),
                jax.ShapeDtypeStruct((2, maps_here, rows_here, PAD, half), F32),
                jax.ShapeDtypeStruct((UNITS, channels, channels), BF16),
                jax.ShapeDtypeStruct((2, 8, half), F32),
            ),
            in_specs=[whole, anywhere] + [outside] * 8,
            out_specs=[anywhere] * 4,
            scratch_shapes=[
                vmem(norm_gains.shape, F32),
                vmem(norm_shifts.shape, F32),
                pltpu.SMEM(map_width.shape, jnp.int32),
                pltpu.SMEM(map_group.shape, jnp.int32),
                vmem((maps_here, pooled_columns, channels), jnp.int32),
                pltpu.SMEM(task_mask.shape, jnp.int32),
                pltpu.SMEM(task_weights.shape, F32),
                vmem(task_grads.shape, BF16),
                vmem((LAYERS, 3, 3, half, half), BF16),
                vmem((LAYERS, 3, 3, half, half), BF16),
                vmem((2,) + tile, BF16),
                vmem((2,) + tile, BF16),
                vmem((LAYERS, 2, half, maps_here * (band + 2) * PAD), BF16),
                vmem((2, half, pixels), BF16),
                vmem((LAYERS,) + tile, F32),
                vmem(edge, BF16),
                vmem((LAYERS,) + edge, BF16),
                vmem((maps_here, band, PAD, half), F32),
                vmem(edge, BF16),
                vmem((LAYERS,) + edge, BF16),
                vmem((2,) + tile, BF16),
                vmem((2,) + tile, BF16),
                vmem((LAYERS, maps_here, band, PAD, half), BF16),
                vmem((3, 2, maps_here, band, PAD, half), BF16),
                vmem((3, pixels, half), F32),
                vmem((2, 2, maps_here, PAD // 2, half), F32),
                vmem((4, 2, maps_here, PAD // 2, half), F32),
                vmem((half // 128, PAD, 128), F32),
                vmem((2, maps_here, PAD // 2, half), BF16),
                vmem((rounds, chips, 8, half), F32),
                vmem((rounds, PLANE, 8, half), F32),
                vmem((maps_here, PLANE, 8, half), F32),
                vmem((PLANE, 8, half), F32),
                vmem((2, 8, half), F32),
                vmem((8, half), F32),
                vmem((LAYERS, 8, half), F32),
                vmem((LAYERS, 8, half), F32),
                vmem((2, 8, half), F32),
                vmem((1, 8, half), F32),
                vmem((1, 8, half), F32),
                vmem((8, half), F32),
                vmem((2 * TAPS, half, half), BF16),
                vmem((UNITS, half // 2, half), BF16),
                vmem((2 * TAPS, half // 2, half), BF16),
                vmem((UNITS, actives - 1, piece, half), BF16),
                vmem((UNITS, piece, half), BF16),
                dma((8,)),
                dma((LAYERS, 3)),
                dma((6,)),
                dma((6,)),
                dma((3,)),
                dma((3,)),
                dma((rounds, chips)),
                dma((rounds, chips)),
                dma((rounds, PLANE)),
                dma((rounds, PLANE)),
                dma((LAYERS, 2)),
                dma((LAYERS, 2)),
                dma((LAYERS, 2)),
                dma((LAYERS, 2)),
                dma((LAYERS, maps_here)),
                dma((LAYERS, maps_here)),
                dma((LAYERS, maps_here)),
                dma((LAYERS, maps_here)),
                dma((3,)),
                dma((3,)),
                dma((3,)),
                dma((LAYERS,)),
                dma((LAYERS,)),
                dma((LAYERS, 2, maps_here)),
                dma((LAYERS, maps_here)),
                dma((UNITS,)),
                dma((UNITS,)),
                dma((UNITS,)),
                dma((UNITS,)),
                dma((UNITS, owners)),
                dma((UNITS, actives - 1)),
                dma((UNITS, actives)),
                dma((UNITS, owners)),
                dma((UNITS,)),
                dma((UNITS,)),
                dma((UNITS,)),
                dma((UNITS,)),
                dma((UNITS,)),
                dma((UNITS,)),
                dma((UNITS,)),
                dma((UNITS,)),
                dma((UNITS,)),
            ],
            compiler_params=pltpu.CompilerParams(
                collective_id=0,
                has_side_effects=True,
                vmem_limit_bytes=grant,
            ),
        )(
            block_input,
            conv_weights,
            *(
                pltpu.with_memory_space_constraint(v, pltpu.HBM)
                for v in (
                    norm_gains,
                    norm_shifts,
                    map_width,
                    map_group,
                    index_rows,
                    task_mask,
                    task_weights,
                    task_grads,
                )
            ),
        )
        pooled = jnp.concatenate([pooled[0], pooled[1]], -1)[:, None, :pooled_columns]
        input_grad = jnp.concatenate([ig[0], ig[1]], -1)[:, :, :columns]
        sums = jnp.concatenate([sums[0], sums[1]], -1)
        return (
            pooled,
            input_grad,
            kg.astype(F32).reshape(conv_weights.shape),
            sums[:LAYERS],
            sums[LAYERS : 2 * LAYERS],
        )

    return jax.shard_map(
        per_device,
        mesh=mesh,
        in_specs=(
            P("maps", "rows", None, None),
            P(),
            P(),
            P(),
            P(),
            P(),
            P("maps", "rows", None, None),
            P("maps", None),
            P(),
            P(None, "maps", "rows", None, None),
        ),
        out_specs=(P("maps", "rows", None, None), P("maps", "rows", None, None), P(), P(), P()),
        check_vma=False,
    )
```

```python
import functools

import jax
import jax.numpy as jnp
from jax import lax
from jax.experimental import pallas as pl
from jax.experimental.pallas import tpu as pltpu
from jax.sharding import PartitionSpec as P

MESH = pl.DeviceIdType.MESH
epsilon = 1e-05
PAD = 64
LAYERS = 3
TAPS = 9
UNITS = LAYERS * TAPS
PLANE = 4
LAG = 4
EARLY = 1
FOLD = 2
F32 = jnp.float32
BF16 = jnp.bfloat16


def each(first, last, body):
    if last - first <= 8:
        for k in range(first, last):
            body(k)
    else:
        lax.fori_loop(first, last, lambda k, s: (body(k), s)[1], 0)


def block_kernel(
    chips,
    height,
    x_ref,
    w_ref,
    gain_hbm,
    shift_hbm,
    width_hbm,
    group_hbm,
    index_hbm,
    tmask_hbm,
    tweight_hbm,
    tgrad_hbm,
    pooled_ref,
    ig_ref,
    kg_ref,
    sums_ref,
    gain_ref,
    shift_ref,
    width_ref,
    group_ref,
    index_ref,
    tmask_ref,
    tweight_ref,
    tgrad_ref,
    wa,
    wb,
    act_own,
    act_oth,
    act_t,
    act_b,
    zbuf,
    zs,
    zh,
    dh,
    dhs,
    dhh,
    dz_own,
    dz_oth,
    dzr,
    dzv,
    prod,
    gsrc,
    gbuf,
    hrow,
    pbuf,
    st1,
    st2,
    coef,
    nall,
    inv_t,
    cnt_t,
    avg_t,
    scl_t,
    mean_t,
    tb_t,
    ta_t,
    sums_own,
    terms,
    r2,
    rf,
    r3,
    fin,
    in_sem,
    w_sem,
    x_s,
    x_r,
    g_s,
    g_r,
    st1_s,
    st1_r,
    st2_s,
    st2_r,
    zh_s,
    zh_r,
    dh_s,
    dh_r,
    act_s,
    act_r,
    dz_s,
    dz_r,
    out_s,
    out_r,
    out_l,
    at_s,
    at_r,
    dzr_s,
    dzr_r,
    r2_s,
    r2_r,
    rf_s,
    rf_r,
    r3_s,
    r3_r,
    az_s,
    az_r,
    af_s,
    af_r,
    ab_s,
    ab_r,
    aa_s,
    aa_r,
    ap_s,
    ap_r,
    loc_s,
):
    maps_here = x_ref.shape[0]
    columns = x_ref.shape[2]
    half = x_ref.shape[3] // 2
    tasks = tgrad_ref.shape[0]
    pooled_columns = tgrad_ref.shape[3]
    lanes = half // 128
    tiles = [slice(n * 128, (n + 1) * 128) for n in range(lanes)]
    band = 4
    pixels = maps_here * band * PAD
    actives = chips // 2
    owners = min(actives, 8)
    piece = (half // 2) // owners
    m = lax.axis_index("maps")
    r = lax.axis_index("rows")
    c = lax.rem(r, 2)
    z = lax.div(r, 2)
    other = 1 - c
    first_map = m * maps_here
    x_bit = lax.rem(m, 2)
    y_bit = lax.div(m, 2)
    x_peer = m + 1 - 2 * x_bit
    y_peer = m + 2 - 4 * y_bit
    g_bit = (1 - c) * x_bit + c * y_bit
    h_bit = (1 - c) * y_bit + c * x_bit
    g_peer = (1 - c) * x_peer + c * y_peer
    h_peer = (1 - c) * y_peer + c * x_peer
    pair = lax.div(z, 2)
    turn = lax.rem(pair, 2)
    active_z = 2 * pair + 1 - turn
    is_active = z == active_z
    is_passive = z != active_z
    is_owner = jnp.logical_and(is_active, pair < owners)
    up_there = z > 0
    down_there = z < chips - 1
    row8 = lax.broadcasted_iota(jnp.int32, (8, half), 0)
    column = lax.broadcasted_iota(jnp.int32, (PAD, half), 0)

    def remote(src, dst, send, recv, mm, zz, cc):
        return pltpu.make_async_remote_copy(
            src_ref=src,
            dst_ref=dst,
            send_sem=send,
            recv_sem=recv,
            device_id=(mm, zz * 2 + cc),
            device_id_type=MESH,
        )

    def own_half(v):
        return jnp.where(c == 0, v[..., :half], v[..., half:])

    def width_of(a):
        return width_ref[first_map + a]

    own_at = pl.ds(pl.multiple_of(c * half, half), half)
    oth_at = pl.ds(pl.multiple_of(other * half, half), half)

    def weight_copy(l, n):
        dst = (wa, wb, wb)[n]
        k_at, o_at = ((own_at, own_at), (oth_at, own_at), (own_at, oth_at))[n]
        return pltpu.make_async_copy(w_ref.at[l, :, :, k_at, o_at], dst.at[l], w_sem.at[l, n])

    fetches = [
        pltpu.make_async_copy(src, dst, in_sem.at[n])
        for n, (src, dst) in enumerate(
            (
                (width_hbm, width_ref),
                (group_hbm, group_ref),
                (tmask_hbm, tmask_ref),
                (tweight_hbm, tweight_ref),
                (gain_hbm, gain_ref),
                (shift_hbm, shift_ref),
                (index_hbm.at[:, :, 0, :], index_ref),
                (tgrad_hbm, tgrad_ref),
            )
        )
    ]
    for fetch in fetches:
        fetch.start()
    for l in range(LAYERS):
        weight_copy(l, 0).start()
        weight_copy(l, 1).start()

    barrier = pltpu.get_barrier_semaphore()

    def greet(k):
        rr = lax.rem(r + k, 2 * chips)
        pl.semaphore_signal(barrier, inc=1, device_id=(m, rr), device_id_type=MESH)

    each(1, 2 * chips, greet)
    for k in range(1, PLANE):
        for core in (c, other):
            there = (lax.rem(m + k, PLANE), z * 2 + core)
            pl.semaphore_signal(barrier, inc=1, device_id=there, device_id_type=MESH)

    for fetch in fetches:
        fetch.wait()

    mine = pl.ds(1 + 2 * c, 2)
    for a in range(maps_here):
        inside = lax.broadcasted_iota(jnp.int32, (columns, 2 * half), 0) < width_of(a)
        for rr in range(2):
            v = jnp.where(inside, x_ref[a, rr].astype(F32), 0.0).astype(BF16)
            spot = 1 + 2 * c + rr
            act_own[0, a, spot, pl.ds(48, 16), :] = jnp.zeros((16, half), BF16)
            act_oth[0, a, spot, pl.ds(48, 16), :] = jnp.zeros((16, half), BF16)
            act_own[0, a, spot, pl.ds(0, columns), :] = own_half(v)
            act_oth[0, a, spot, pl.ds(0, columns), :] = jnp.where(
                c == 0, v[:, half:], v[:, :half]
            )

    @pl.when(z == 0)
    def _():
        act_own[0, :, 0] = jnp.zeros((maps_here, PAD, half), BF16)
        act_oth[0, :, 0] = jnp.zeros((maps_here, PAD, half), BF16)

    @pl.when(z == chips - 1)
    def _():
        act_own[0, :, 5] = jnp.zeros((maps_here, PAD, half), BF16)
        act_oth[0, :, 5] = jnp.zeros((maps_here, PAD, half), BF16)

    pl.semaphore_wait(barrier, 2 * chips - 1 + 2 * (PLANE - 1))

    x_partner = (
        remote(act_own.at[0, :, mine], act_oth.at[0, :, mine], x_s.at[0], x_r.at[0], m, z, other),
        remote(act_oth.at[0, :, mine], act_own.at[0, :, mine], x_s.at[1], x_r.at[1], m, z, other),
    )
    g_partner = remote(gsrc.at[other], gbuf.at[1 + c], g_s.at[0], g_r.at[0], m, z, other)

    def x_halo(n, src_row, dst_row, zz):
        cc = (c, c, other, other, c, other)[n]
        low = dst_row == band + 1
        if n >= 4:
            src, dst = gsrc.at[cc], gbuf.at[3 if low else 0]
            return remote(src, dst, g_s.at[n - 3], g_r.at[1 if low else 2], m, zz, cc)
        src = (act_own, act_oth, act_own, act_oth)[n].at[0, :, src_row]
        dst = (act_own, act_oth, act_oth, act_own)[n].at[0, :, dst_row]
        return remote(src, dst, x_s.at[2 + n], x_r.at[(2 if low else 4) + n % 2], m, zz, cc)

    for copy in x_partner:
        copy.start()

    @pl.when(jnp.logical_and(c == 0, up_there))
    def _():
        for n in range(4):
            x_halo(n, 1, 5, z - 1).start()

    @pl.when(jnp.logical_and(c == 1, down_there))
    def _():
        for n in range(4):
            x_halo(n, 4, 0, z + 1).start()

    gsrc[...] = jnp.zeros(gsrc.shape, F32)
    for a in range(maps_here):
        total = None
        for t in range(tasks):
            scale = tweight_ref[t] * tmask_ref[a, t].astype(F32)
            term = tgrad_ref[t, a, 0].astype(F32) * scale
            total = term if total is None else total + term
        position = index_ref[a].astype(F32)
        for h in range(2):
            gsrc[h, 0, a, pl.ds(0, pooled_columns), :] = total[:, h * half : (h + 1) * half]
            gsrc[h, 1, a, pl.ds(0, pooled_columns), :] = position[:, h * half : (h + 1) * half]
    gbuf[1 + c] = gsrc[c]

    for mm in range(PLANE):
        sizes = jnp.zeros((8, half), F32)
        for b in range(maps_here):
            sizes = jnp.where(
                row8 == b, (width_ref[mm * maps_here + b] * height).astype(F32), sizes
            )
        nall[mm] = sizes
    inside_sizes = jnp.zeros((8, half), F32)
    for b in range(maps_here):
        inside_sizes = jnp.where(row8 == b, (width_of(b) * band).astype(F32), inside_sizes)
    inv_t[0] = inside_sizes
    inv_t[1] = jnp.where(row8 < maps_here, 1.0 / jnp.maximum(inside_sizes, 1.0), 0.0)
    counts = jnp.ones((8, half), F32)
    for a in range(maps_here):
        total = jnp.zeros((1, half), F32)
        for mm in range(PLANE):
            same = jnp.zeros((8, half), F32)
            for b in range(maps_here):
                alike = group_ref[first_map + a] == group_ref[mm * maps_here + b]
                same = jnp.where(row8 == b, jnp.where(alike, 1.0, 0.0), same)
            coef[a, mm] = same
            total = total + jnp.sum(same * nall[mm], 0, keepdims=True)
        counts = jnp.where(row8 == a, total, counts)
    cnt_t[...] = counts

    def z_copy(e, k):
        zz = lax.rem(z + k, chips)
        return remote(st1.at[e, z], st1.at[e, z], st1_s.at[e, k], st1_r.at[e, z], m, zz, c)

    def z_arrival(e, k):
        zz = lax.rem(z + k, chips)
        return remote(st1.at[e, zz], st1.at[e, zz], st1_s.at[e, k], st1_r.at[e, zz], m, zz, c)

    def m_copy(e, k):
        mm = lax.rem(m + k, PLANE)
        return remote(st2.at[e, m], st2.at[e, m], st2_s.at[e, k], st2_r.at[e, m], mm, z, c)

    def m_arrival(e, k):
        mm = lax.rem(m + k, PLANE)
        return remote(st2.at[e, mm], st2.at[e, mm], st2_s.at[e, k], st2_r.at[e, mm], mm, z, c)

    def send_z(e, tile):
        st1[e, z] = tile
        each(1, chips, lambda k: z_copy(e, k).start())

    def wait_z(e):
        each(1, chips, lambda k: z_arrival(e, k).wait_recv())

    def send_m(e, tile):
        st2[e, m] = tile
        each(1, PLANE, lambda k: m_copy(e, k).start())

    def wait_m(e):
        each(1, PLANE, lambda k: m_arrival(e, k).wait_recv())

    def products(source, l, taps, kernel, transposed, fresh):
        starts = [2 - i if transposed else i for i in taps]
        lhs = jnp.concatenate(
            [source[lax.rem(l, 2), :, s : s + band].reshape(pixels, half) for s in starts], 1
        )
        for j in range(3):
            rhs = jnp.concatenate([kernel[l, i, j] for i in taps], 1 if transposed else 0)
            got = lax.dot_general(
                lhs,
                rhs,
                (((1,), (1 if transposed else 0,)), ((), ())),
                preferred_element_type=F32,
            )
            if fresh:
                prod[j] = got
            else:
                prod[j] = prod[j] + got

    def shifted(a, rr, before, behind, n):
        rows = pl.ds(pl.multiple_of((a * band + rr) * PAD, PAD), PAD)
        return (
            prod[1, rows, n]
            + pltpu.roll(prod[before, rows, n], 1, 0)
            + pltpu.roll(prod[behind, rows, n], PAD - 1, 0)
        )

    def row_of(table, l, a):
        return table[l, pl.ds(a, 1), :]

    def gain_of(l):
        return own_half(gain_ref[pl.ds(l, 1), :])

    def shift_of(l):
        return own_half(shift_ref[pl.ds(l, 1), :])

    def limit(a, rr):
        w = width_of(a)
        if rr == 0:
            return jnp.where(up_there, w, 0)
        if rr == band + 1:
            return jnp.where(down_there, w, 0)
        return w

    def z_halo(l, way):
        there = z - 1 + 2 * way
        return remote(zs.at[way], zh.at[l, 1 - way], zh_s.at[l, way], zh_r.at[l, way], m, there, c)

    def dh_halo(l, way):
        there = z - 1 + 2 * way
        return remote(dhs.at[way], dhh.at[l, 1 - way], dh_s.at[l, way], dh_r.at[l, way], m, there, c)

    def start_halo(halo, l):
        @pl.when(up_there)
        def _():
            halo(l, 0).start()

        @pl.when(down_there)
        def _():
            halo(l, 1).start()

    def wait_halo(halo, l):
        @pl.when(up_there)
        def _():
            halo(l, 1).wait_recv()
            halo(l, 0).wait_send()

        @pl.when(down_there)
        def _():
            halo(l, 0).wait_recv()
            halo(l, 1).wait_send()

    def act_copy(l, a):
        slot = lax.rem(l, 2)
        src, dst = act_own.at[slot, a], act_oth.at[slot, a]
        return remote(src, dst, act_s.at[l, a], act_r.at[l, a], m, z, other)

    def at_copy(l):
        return remote(act_t.at[l, 0], act_t.at[l, 1], at_s.at[l], at_r.at[l], g_peer, z, c)

    def dzr_copy(l, a, way):
        src, dst = dz_own.at[lax.rem(l, 2), a, pl.ds(1, band)], dzr.at[l, a]
        peer = (x_peer, y_peer)[way]
        return remote(src, dst, dzr_s.at[l, way, a], dzr_r.at[l, a], peer, z, way)

    def if_wanted(way, body):
        @pl.when((x_bit, y_bit)[way] + c == 1)
        def _():
            body()

    def dz_copy(l, a):
        slot = lax.rem(l, 2)
        src, dst = dz_own.at[slot, a], dz_oth.at[slot, a]
        return remote(src, dst, dz_s.at[l, a], dz_r.at[l, a], m, z, other)

    def send_gradients():
        g_partner.start()

        @pl.when(jnp.logical_and(c == 0, up_there))
        def _():
            for n in range(4, 6):
                x_halo(n, 1, 5, z - 1).start()

        @pl.when(jnp.logical_and(c == 1, down_there))
        def _():
            for n in range(4, 6):
                x_halo(n, 4, 0, z + 1).start()

    def wait_x_halo(first, last):
        @pl.when(up_there)
        def _():
            for n in (0, 1, 4)[first:last]:
                x_halo(n, 4, 0, z - 1).wait_recv()

        @pl.when(down_there)
        def _():
            for n in (0, 1, 4)[first:last]:
                x_halo(n, 1, 5, z + 1).wait_recv()

    def sent_x_halo(first, last):
        @pl.when(jnp.logical_and(c == 0, up_there))
        def _():
            for n in range(first, last):
                x_halo(n, 1, 5, z - 1).wait_send()

        @pl.when(jnp.logical_and(c == 1, down_there))
        def _():
            for n in range(first, last):
                x_halo(n, 4, 0, z + 1).wait_send()

    def forward(l, first):
        weight_copy(l, 0).wait()
        weight_copy(l, 1).wait()
        if first:
            for copy in x_partner:
                copy.wait_recv()
            products(act_own, l, (1,), wa, False, True)
            products(act_oth, l, (1,), wb, False, False)
            wait_x_halo(0, 2)
            products(act_own, l, (0, 2), wa, False, False)
            products(act_oth, l, (0, 2), wb, False, False)
        else:
            products(act_own, l, (0, 1, 2), wa, False, True)
            for a in range(maps_here):
                act_copy(l, a).wait_recv()
            products(act_oth, l, (0, 1, 2), wb, False, False)
        weight_copy(l, 2).start()

        def collect(a, tile):
            inside = column[:, :128] < width_of(a)
            pixels_inside = (width_of(a) * band).astype(F32)
            totals, squares = [], []
            for n in tiles:
                total = jnp.zeros((PAD, 128), F32)
                for rr in range(band):
                    v = shifted(a, rr, 0, 2, n)
                    zbuf[l, a, 1 + rr, :, n] = v
                    total = total + jnp.where(inside, v, 0.0)
                total = jnp.sum(total, 0, keepdims=True)
                mean = total / pixels_inside
                square = jnp.zeros((PAD, 128), F32)
                for rr in range(band):
                    v = jnp.where(inside, zbuf[l, a, 1 + rr, :, n] - mean, 0.0)
                    square = square + v * v
                    if rr in (0, band - 1):
                        zs[rr // (band - 1), a, :, n] = v.astype(BF16)
                totals.append(total)
                squares.append(jnp.sum(square, 0, keepdims=True))
            tile = jnp.where(row8 == a, jnp.concatenate(totals, 1), tile)
            return jnp.where(row8 == a + maps_here, jnp.concatenate(squares, 1), tile)

        tile = lax.fori_loop(0, maps_here, collect, jnp.zeros((8, half), F32))
        send_z(l, tile)
        start_halo(z_halo, l)
        act_t[l, 0] = act_own[lax.rem(l, 2)].reshape(maps_here * (band + 2) * PAD, half).T
        wait_z(l)
        sizes, inverse = inv_t[0], inv_t[1]
        mean_t[0] = st1[l, jnp.maximum(z - 1, 0)] * inverse
        mean_t[1] = st1[l, jnp.minimum(z + 1, chips - 1)] * inverse
        total = st1[l, 0]
        for zz in range(1, chips):
            total = total + st1[l, zz]
        mean = total * inverse * (1.0 / chips)
        square = jnp.zeros((8, half), F32)
        for zz in range(chips):
            v = st1[l, zz]
            gap = v * inverse - mean
            square = square + pltpu.roll(v, 8 - maps_here, 0) + sizes * gap * gap
        tile = jnp.where(row8 < maps_here, mean, pltpu.roll(square, maps_here, 0))
        send_m(l, jnp.where(row8 < 2 * maps_here, tile, 0.0))
        wait_m(l)
        at_copy(l).start()
        if first:
            send_gradients()
        averages = jnp.zeros((8, half), F32)
        scalings = jnp.zeros((8, half), F32)
        for a in range(maps_here):
            count = cnt_t[a : a + 1, :]
            average = jnp.zeros((8, half), F32)
            for mm in range(PLANE):
                average = average + coef[a, mm] * nall[mm] * st2[l, mm]
            average = jnp.sum(average, 0, keepdims=True) / count
            variance = jnp.zeros((8, half), F32)
            for mm in range(PLANE):
                v = st2[l, mm]
                gap = v - average
                variance = variance + coef[a, mm] * (
                    pltpu.roll(v, 8 - maps_here, 0) + nall[mm] * gap * gap
                )
            variance = jnp.sum(variance, 0, keepdims=True) / count
            averages = jnp.where(row8 == a, average, averages)
            scalings = jnp.where(row8 == a, lax.rsqrt(variance + epsilon), scalings)
        avg_t[l] = averages
        scl_t[l] = scalings
        wait_halo(z_halo, l)

        def activate(a, s):
            gain, shift = gain_of(l), shift_of(l)
            for n in tiles:
                average = row_of(avg_t, l, a)[:, n]
                factor = row_of(scl_t, l, a)[:, n] * gain[:, n]
                for rr in range(band + 2):
                    if rr in (0, band + 1):
                        way = rr // (band + 1)
                        v = zh[l, way, a, :, n].astype(F32) + row_of(mean_t, way, a)[:, n]
                        zbuf[l, a, rr, :, n] = v
                    else:
                        v = zbuf[l, a, rr, :, n]
                    y = (v - average) * factor + shift[:, n]
                    h = jnp.where(column[:, n] < limit(a, rr), y * jax.nn.sigmoid(y), 0.0)
                    act_own[lax.rem(l + 1, 2), a, rr, :, n] = h.astype(BF16)

            @pl.when(l < LAYERS - 1)
            def _():
                act_copy(l + 1, a).start()

            return s

        if first:
            for copy in x_partner:
                copy.wait_send()
            sent_x_halo(0, 4)
        else:

            @pl.when(l == 2)
            def _():
                for a in range(maps_here):
                    act_copy(1, a).wait_send()

        lax.fori_loop(0, maps_here, activate, 0)

    forward(0, True)
    lax.fori_loop(1, LAYERS, lambda l, s: (forward(l, False), s)[1], 0)
    g_partner.wait_recv()
    wait_x_halo(2, 3)

    def unpool(a, s):
        for rr in range(band + 2):
            slot, lower = (rr + 1) // 2, (rr + 1) % 2
            g = gbuf[slot, 0, a]
            position = gbuf[slot, 1, a]
            for b in range(2):
                v = jnp.where(position == float(2 * lower + b), g, 0.0)
                for n in range(lanes):
                    hrow[n, pl.ds(b, PAD // 2, stride=2), :] = v[:, n * 128 : (n + 1) * 128]
            v = jnp.concatenate([hrow[n] for n in range(lanes)], 1)
            if rr in (0, band + 1):
                dhh[LAYERS - 1, rr // (band + 1), a] = v.astype(BF16)
            else:
                dh[a, rr - 1] = v
        return s

    lax.fori_loop(0, maps_here, unpool, 0)

    def pool():
        def one(a, s):
            for pr in range(2):
                total = jnp.zeros((PAD // 2, half), F32)
                position = gbuf[1 + pr, 1, a]
                for lower in range(2):
                    v = act_own[LAYERS % 2, a, 1 + 2 * pr + lower].astype(F32)
                    for n in range(lanes):
                        hrow[n] = v[:, n * 128 : (n + 1) * 128]
                    for b in range(2):
                        v = jnp.concatenate(
                            [hrow[n, pl.ds(b, PAD // 2, stride=2), :] for n in range(lanes)], 1
                        )
                        total = total + jnp.where(position == float(2 * lower + b), v, 0.0)
                pbuf[pr, a] = total.astype(BF16)
            return s

        lax.fori_loop(0, maps_here, one, 0)

    def second_rows(bit):
        return pl.ds(pl.multiple_of(bit * (half // 2), half // 2), half // 2)

    def piece_rows(p):
        return pl.ds(pl.multiple_of(p * piece, piece), piece)

    def term_slot(q):
        return lax.rem(q, 2 * TAPS)

    def c2(q):
        src = terms.at[term_slot(q), second_rows(1 - h_bit)]
        return remote(src, r2.at[q], r2_s.at[q], r2_r.at[q], h_peer, z, c)

    def z_of(n):
        return 2 * n + 1 - lax.rem(n, 2)

    def cf(q):
        passive_z = 2 * pair + turn
        there = active_z + passive_z - z
        return remote(r2.at[q], rf.at[term_slot(q)], rf_s.at[q], rf_r.at[q], m, there, c)

    def c3(q, p):
        slot = lax.rem(pair - p + actives - 1, actives)
        return remote(
            r2.at[q, piece_rows(p)], r3.at[q, slot], r3_s.at[q, p], r3_r.at[q, slot], m, z_of(p), c
        )

    def others(first, body, limit):
        def one(k):
            n = lax.rem(pair + k, actives)

            @pl.when(n < limit)
            def _():
                body(n)

        each(first, actives, one)

    def unit_of(q):
        k = lax.div(q, TAPS)
        return (LAYERS - 1 - k) * TAPS + (q - k * TAPS)

    def region(q, start, size, lane, lanes):
        start = pl.multiple_of(c * half + start, piece)
        lane = pl.multiple_of(lane, half)
        return kg_ref.at[unit_of(q), pl.ds(start, size), pl.ds(lane, lanes)]

    def cz(q, p, n):
        part = region(q, h_bit * (half // 2) + p * piece, piece, g_bit * half, half)
        return remote(fin.at[q], part, az_s.at[q, n], az_r.at[q, p], m, z_of(n), c)

    def cl(q):
        part = region(q, h_bit * (half // 2) + pair * piece, piece, g_bit * half, half)
        return pltpu.make_async_copy(fin.at[q], part, loc_s.at[q])

    def cu(q):
        passive_z = 2 * pair + turn
        there = active_z + passive_z - z
        part = region(q, h_bit * (half // 2), half // 2, g_bit * half, half)
        return remote(part, part, af_s.at[q], af_r.at[q], m, there, c)

    def cb(q):
        part = region(q, h_bit * (half // 2), half // 2, g_bit * half, half)
        return remote(part, part, ab_s.at[q], ab_r.at[q], h_peer, z, c)

    def ca(q):
        part = region(q, 0, half, g_bit * half, half)
        return remote(part, part, aa_s.at[q], aa_r.at[q], g_peer, z, c)

    def cp(q):
        part = region(q, 0, half, 0, 2 * half)
        return remote(part, part, ap_s.at[q], ap_r.at[q], m, z, other)

    def ready_terms(l):
        at_copy(l).wait_recv()
        for chip in range(2):
            for a in range(maps_here):
                first = a * (band + 2) * PAD
                rows = act_t[l, chip, :, first : first + (band + 2) * PAD]
                act_b[chip, :, a * band * PAD : (a + 1) * band * PAD] = rows[:, PAD : PAD + band * PAD]
        slot = lax.rem(l, 2)

        def variants(a, s):
            dzr_copy(l, a, 0).wait_recv()
            for chip in range(2):
                for rr in range(band):
                    for n in tiles:
                        if chip == 0:
                            mine, theirs = dz_own[slot, a, 1 + rr, :, n], dz_oth[slot, a, 1 + rr, :, n]
                            v = jnp.where(g_bit == c, mine, theirs)
                        else:
                            v = dzr[l, a, rr, :, n]
                        dzv[1, chip, a, rr, :, n] = v
                        v = v.astype(F32)
                        dzv[0, chip, a, rr, :, n] = pltpu.roll(v, PAD - 1, 0).astype(BF16)
                        dzv[2, chip, a, rr, :, n] = pltpu.roll(v, 1, 0).astype(BF16)
            return s

        lax.fori_loop(0, maps_here, variants, 0)

    def tap_terms(l, i, j):
        if i == 1:
            lhs = [act_b[0], act_b[1]]
        else:
            lhs = []
            for chip in range(2):
                for a in range(maps_here):
                    first = (a * (band + 2) + i) * PAD
                    lhs.append(act_t[l, chip, :, first : first + band * PAD])
        rhs = dzv[j].reshape(2 * pixels, half)
        q = (LAYERS - 1 - l) * TAPS + 3 * i + j
        got = jnp.dot(jnp.concatenate(lhs, 1), rhs, preferred_element_type=F32)
        terms[term_slot(q)] = got.astype(BF16)

    def weight_terms(l, i):
        lax.fori_loop(0, 3, lambda j, s: (tap_terms(l, i, j), s)[1], 0)

    def stage_second(q):
        c2(q).wait()
        kept = terms[term_slot(q), second_rows(h_bit)].astype(F32)
        r2[q] = (r2[q].astype(F32) + kept).astype(BF16)

        @pl.when(is_passive)
        def _():
            cf(q).start()

    def stage_fold(q):
        @pl.when(is_active)
        def _():
            cf(q).wait_recv()
            r2[q] = (r2[q].astype(F32) + rf[term_slot(q)].astype(F32)).astype(BF16)
            others(1, lambda n: c3(q, n).start(), owners)

    def stage_sum(q):
        @pl.when(is_owner)
        def _():
            for k in range(actives - 1):
                remote(
                    r3.at[q, k], r3.at[q, k], r3_s.at[q, 0], r3_r.at[q, k], m, z, c
                ).wait_recv()
            total = r2[q, piece_rows(pair)].astype(F32)
            for k in range(actives - 1):
                total = total + r3[q, k].astype(F32)
            fin[q] = total.astype(BF16)
            others(1, lambda n: cz(q, pair, n).start(), actives)
            cl(q).start()

    def stage_back(q):
        @pl.when(is_active)
        def _():
            others(1, lambda n: cz(q, n, n).wait_recv(), owners)

        @pl.when(is_owner)
        def _():
            cl(q).wait()

        @pl.when(is_active)
        def _():
            cu(q).start()

        @pl.when(is_passive)
        def _():
            cu(q).wait_recv()

        cb(q).start()

    def stage_first(q):
        cb(q).wait_recv()
        ca(q).start()

        @pl.when(is_active)
        def _():
            others(1, lambda n: c3(q, n).wait_send(), owners)

        @pl.when(is_passive)
        def _():
            cf(q).wait_send()

    def stage_chip(q):
        ca(q).wait_recv()
        cp(q).start()

        @pl.when(is_owner)
        def _():
            others(1, lambda n: cz(q, pair, n).wait_send(), actives)

        @pl.when(is_active)
        def _():
            cu(q).wait_send()

    def stage_done(q):
        cb(q).wait_send()
        ca(q).wait_send()
        cp(q).wait()

    def run(stage, first, last):
        lax.fori_loop(first, last, lambda q, s: (stage(q), s)[1], 0)

    def sent_dz(l):
        for a in range(maps_here):
            dz_copy(l, a).wait_send()
            for way in range(2):
                if_wanted(way, dzr_copy(l, a, way).wait_send)

    def backward(k, carry):
        l = LAYERS - 1 - k
        gain, shift = gain_of(l), shift_of(l)

        def gradient(a, rr, n):
            zhat = (zbuf[l, a, rr, :, n] - row_of(avg_t, l, a)[:, n]) * row_of(scl_t, l, a)[:, n]
            y = zhat * gain[:, n] + shift[:, n]
            s = jax.nn.sigmoid(y)
            if rr in (0, band + 1):
                upstream = dhh[l, rr // (band + 1), a, :, n].astype(F32)
            else:
                upstream = dh[a, rr - 1, :, n]
            dy = upstream * (s * (1.0 + y * (1.0 - s)))
            dy = jnp.where(column[:, n] < limit(a, rr), dy, 0.0)
            return dy, zhat

        def collect(a, tile):
            plains, crosses = [], []
            for n in tiles:
                plain = jnp.zeros((PAD, 128), F32)
                crossed = jnp.zeros((PAD, 128), F32)
                for rr in range(1, band + 1):
                    dy, zhat = gradient(a, rr, n)
                    dh[a, rr - 1, :, n] = dy
                    plain = plain + dy
                    crossed = crossed + dy * zhat
                plains.append(jnp.sum(plain, 0, keepdims=True))
                crosses.append(jnp.sum(crossed, 0, keepdims=True))
            tile = jnp.where(row8 == a, jnp.concatenate(plains, 1), tile)
            return jnp.where(row8 == a + maps_here, jnp.concatenate(crosses, 1), tile)

        e = LAYERS + l
        tile = lax.fori_loop(0, maps_here, collect, jnp.zeros((8, half), F32))
        send_z(e, tile)

        @pl.when(k == LAYERS - 1)
        def _():
            run(stage_second, 0, TAPS)

        @pl.when(k > 0)
        def _():
            ready_terms(l + 1)
            weight_terms(l + 1, 0)

        wait_z(e)
        total = st1[e, 0]
        for zz in range(1, chips):
            total = total + st1[e, zz]
        send_m(e, total)

        @pl.when(k > 0)
        def _():
            first = (LAYERS - 2 - l) * TAPS
            run(lambda q: c2(q).start(), first, first + 3)
            weight_terms(l + 1, 1)
            run(lambda q: c2(q).start(), first + 3, first + 6)
            weight_terms(l + 1, 2)
            run(lambda q: c2(q).start(), first + 6, first + 9)
            wait_halo(dh_halo, l)

        @pl.when(k == 0)
        def _():
            pool()

        wait_m(e)
        total = st2[e, 0]
        for mm in range(1, PLANE):
            total = total + st2[e, mm]
        sums_own[pl.ds(l, 1), :] = jnp.sum(
            jnp.where(row8 >= maps_here, total, 0.0), 0, keepdims=True
        )
        sums_own[pl.ds(LAYERS + l, 1), :] = jnp.sum(
            jnp.where(row8 < maps_here, total, 0.0), 0, keepdims=True
        )
        plains = jnp.zeros((8, half), F32)
        crosses = jnp.zeros((8, half), F32)
        for a in range(maps_here):
            plain = jnp.zeros((8, half), F32)
            crossed = jnp.zeros((8, half), F32)
            for mm in range(PLANE):
                v = st2[e, mm]
                plain = plain + coef[a, mm] * v
                crossed = crossed + coef[a, mm] * pltpu.roll(v, 8 - maps_here, 0)
            count = cnt_t[a : a + 1, :]
            plain = gain * (jnp.sum(plain, 0, keepdims=True) / count)
            crossed = gain * (jnp.sum(crossed, 0, keepdims=True) / count)
            plains = jnp.where(row8 == a, plain, plains)
            crosses = jnp.where(row8 == a, crossed, crosses)
        tb_t[0] = plains
        ta_t[0] = crosses

        def settle(a, s):
            for n in tiles:
                average, scaling = row_of(avg_t, l, a)[:, n], row_of(scl_t, l, a)[:, n]
                plain, crossed = row_of(tb_t, 0, a)[:, n], row_of(ta_t, 0, a)[:, n]
                for rr in range(band + 2):
                    if rr in (0, band + 1):
                        dy, zhat = gradient(a, rr, n)
                    else:
                        dy = dh[a, rr - 1, :, n]
                        zhat = (zbuf[l, a, rr, :, n] - average) * scaling
                    v = scaling * (dy * gain[:, n] - plain - zhat * crossed)
                    v = jnp.where(column[:, n] < limit(a, rr), v, 0.0)
                    dz_own[lax.rem(l, 2), a, rr, :, n] = v.astype(BF16)
            dz_copy(l, a).start()
            for way in range(2):
                if_wanted(way, dzr_copy(l, a, way).start)
            return s

        @pl.when(k == 2)
        def _():
            sent_dz(LAYERS - 1)

        lax.fori_loop(0, maps_here, settle, 0)
        products(dz_own, l, (0, 1, 2), wa, True, True)
        weight_copy(l, 2).wait()
        for a in range(maps_here):
            dz_copy(l, a).wait_recv()
        products(dz_oth, l, (0, 1, 2), wb, True, False)

        def gather(a, s):
            for n in tiles:
                for rr in range(band):
                    v = shifted(a, rr, 2, 0, n)
                    dh[a, rr, :, n] = v
                    if rr in (0, band - 1):
                        dhs[rr // (band - 1), a, :, n] = v.astype(BF16)
            return s

        lax.fori_loop(0, maps_here, gather, 0)

        @pl.when(l > 0)
        def _():
            start_halo(dh_halo, l - 1)

        return carry

    lax.fori_loop(0, LAYERS, backward, 0)
    def input_rows(a, s):
        for rr in range(band):
            dh[a, rr] = jnp.where(column < width_of(a), dh[a, rr], 0.0)
        return s

    lax.fori_loop(0, maps_here, input_rows, 0)

    outs = (
        (
            remote(dh.at[:, pl.ds(2 * other, 2)], ig_ref.at[c], out_s.at[0], out_r.at[0], m, z, other),
            pltpu.make_async_copy(dh.at[:, pl.ds(2 * c, 2)], ig_ref.at[c], out_l.at[0]),
        ),
        (
            remote(pbuf.at[other], pooled_ref.at[c], out_s.at[1], out_r.at[1], m, z, other),
            pltpu.make_async_copy(pbuf.at[c], pooled_ref.at[c], out_l.at[1]),
        ),
        (
            remote(sums_own, sums_ref.at[c], out_s.at[2], out_r.at[2], m, z, other),
            pltpu.make_async_copy(sums_own, sums_ref.at[c], out_l.at[2]),
        ),
    )
    for there, here in outs:
        there.start()
        here.start()

    g_partner.wait_send()
    sent_x_halo(4, 6)

    def sent(e, carry):
        each(1, chips, lambda k: z_copy(e, k).wait_send())
        each(1, PLANE, lambda k: m_copy(e, k).wait_send())
        return carry

    lax.fori_loop(0, 2 * LAYERS, sent, 0)
    for l in range(LAYERS):
        at_copy(l).wait_send()
    for l in range(LAYERS - 1):
        sent_dz(l)

    def drain(s, carry):
        @pl.when(s == EARLY)
        def _():
            ready_terms(0)

        for i in range(3):
            j = s - EARLY - 3 * i

            @pl.when(jnp.logical_and(j >= 0, j < 3))
            def _(i=i, j=j):
                tap_terms(0, i, j)
                c2(2 * TAPS + 3 * i + j).start()

        for stage, first, lag in (
            (stage_done, 0, 2 * FOLD + 3 * LAG),
            (stage_chip, 0, 2 * FOLD + 2 * LAG),
            (stage_first, 0, 2 * FOLD + LAG),
            (stage_back, 0, 2 * FOLD),
            (stage_sum, 0, FOLD),
            (stage_fold, 0, 0),
            (stage_second, TAPS, 0),
        ):
            q = first + s - lag

            @pl.when(jnp.logical_and(q >= first, q < UNITS))
            def _(stage=stage, q=q):
                stage(q)

        return carry

    lax.fori_loop(0, UNITS + 2 * FOLD + 3 * LAG, drain, 0)
    for a in range(maps_here):
        act_copy(2, a).wait_send()
    for there, here in outs:
        there.wait()
        here.wait()


def solution(mesh):
    chips = mesh.shape["rows"] // 2

    def per_device(
        block_input,
        conv_weights,
        norm_gains,
        norm_shifts,
        map_width,
        map_group,
        pool_index,
        task_mask,
        task_weights,
        task_grads,
    ):
        maps_here, rows_here, columns, channels = block_input.shape
        pooled_columns = pool_index.shape[2]
        height = rows_here * mesh.shape["rows"]
        half = channels // 2
        band = 2 * rows_here
        pixels = maps_here * band * PAD
        actives = chips // 2
        owners = min(actives, 8)
        piece = half // 2 // owners
        rounds = 2 * LAYERS
        slots = 2 * UNITS * (actives - 1) * piece * half + 4 * rounds * chips * 8 * half
        grant = (36 * 1024 + 256) * 1024 + slots
        vmem, dma = pltpu.VMEM, pltpu.SemaphoreType.DMA
        tile = (maps_here, band + 2, PAD, half)
        edge = (2, maps_here, PAD, half)
        whole = pl.BlockSpec(memory_space=pltpu.VMEM)
        outside = pl.BlockSpec(memory_space=pltpu.HBM)
        index_rows = jnp.transpose(pool_index, (0, 2, 1, 3))
        anywhere = pl.BlockSpec(memory_space=pl.ANY)
        pooled, ig, kg, sums = pl.pallas_call(
            functools.partial(block_kernel, chips, height),
            out_shape=(
                jax.ShapeDtypeStruct((2, maps_here, PAD // 2, half), BF16),
                jax.ShapeDtypeStruct((2, maps_here, rows_here, PAD, half), F32),
                jax.ShapeDtypeStruct((UNITS, channels, channels), BF16),
                jax.ShapeDtypeStruct((2, 8, half), F32),
            ),
            in_specs=[whole, anywhere] + [outside] * 8,
            out_specs=[anywhere] * 4,
            scratch_shapes=[
                vmem(norm_gains.shape, F32),
                vmem(norm_shifts.shape, F32),
                pltpu.SMEM(map_width.shape, jnp.int32),
                pltpu.SMEM(map_group.shape, jnp.int32),
                vmem((maps_here, pooled_columns, channels), jnp.int32),
                pltpu.SMEM(task_mask.shape, jnp.int32),
                pltpu.SMEM(task_weights.shape, F32),
                vmem(task_grads.shape, BF16),
                vmem((LAYERS, 3, 3, half, half), BF16),
                vmem((LAYERS, 3, 3, half, half), BF16),
                vmem((2,) + tile, BF16),
                vmem((2,) + tile, BF16),
                vmem((LAYERS, 2, half, maps_here * (band + 2) * PAD), BF16),
                vmem((2, half, pixels), BF16),
                vmem((LAYERS,) + tile, F32),
                vmem(edge, BF16),
                vmem((LAYERS,) + edge, BF16),
                vmem((maps_here, band, PAD, half), F32),
                vmem(edge, BF16),
                vmem((LAYERS,) + edge, BF16),
                vmem((2,) + tile, BF16),
                vmem((2,) + tile, BF16),
                vmem((LAYERS, maps_here, band, PAD, half), BF16),
                vmem((3, 2, maps_here, band, PAD, half), BF16),
                vmem((3, pixels, half), F32),
                vmem((2, 2, maps_here, PAD // 2, half), F32),
                vmem((4, 2, maps_here, PAD // 2, half), F32),
                vmem((half // 128, PAD, 128), F32),
                vmem((2, maps_here, PAD // 2, half), BF16),
                vmem((rounds, chips, 8, half), F32),
                vmem((rounds, PLANE, 8, half), F32),
                vmem((maps_here, PLANE, 8, half), F32),
                vmem((PLANE, 8, half), F32),
                vmem((2, 8, half), F32),
                vmem((8, half), F32),
                vmem((LAYERS, 8, half), F32),
                vmem((LAYERS, 8, half), F32),
                vmem((2, 8, half), F32),
                vmem((1, 8, half), F32),
                vmem((1, 8, half), F32),
                vmem((8, half), F32),
                vmem((2 * TAPS, half, half), BF16),
                vmem((UNITS, half // 2, half), BF16),
                vmem((2 * TAPS, half // 2, half), BF16),
                vmem((UNITS, actives - 1, piece, half), BF16),
                vmem((UNITS, piece, half), BF16),
                dma((8,)),
                dma((LAYERS, 3)),
                dma((6,)),
                dma((6,)),
                dma((3,)),
                dma((3,)),
                dma((rounds, chips)),
                dma((rounds, chips)),
                dma((rounds, PLANE)),
                dma((rounds, PLANE)),
                dma((LAYERS, 2)),
                dma((LAYERS, 2)),
                dma((LAYERS, 2)),
                dma((LAYERS, 2)),
                dma((LAYERS, maps_here)),
                dma((LAYERS, maps_here)),
                dma((LAYERS, maps_here)),
                dma((LAYERS, maps_here)),
                dma((3,)),
                dma((3,)),
                dma((3,)),
                dma((LAYERS,)),
                dma((LAYERS,)),
                dma((LAYERS, 2, maps_here)),
                dma((LAYERS, maps_here)),
                dma((UNITS,)),
                dma((UNITS,)),
                dma((UNITS,)),
                dma((UNITS,)),
                dma((UNITS, owners)),
                dma((UNITS, actives - 1)),
                dma((UNITS, actives)),
                dma((UNITS, owners)),
                dma((UNITS,)),
                dma((UNITS,)),
                dma((UNITS,)),
                dma((UNITS,)),
                dma((UNITS,)),
                dma((UNITS,)),
                dma((UNITS,)),
                dma((UNITS,)),
                dma((UNITS,)),
            ],
            compiler_params=pltpu.CompilerParams(
                collective_id=0,
                has_side_effects=True,
                vmem_limit_bytes=grant,
            ),
        )(
            block_input,
            conv_weights,
            *(
                pltpu.with_memory_space_constraint(v, pltpu.HBM)
                for v in (
                    norm_gains,
                    norm_shifts,
                    map_width,
                    map_group,
                    index_rows,
                    task_mask,
                    task_weights,
                    task_grads,
                )
            ),
        )
        pooled = jnp.concatenate([pooled[0], pooled[1]], -1)[:, None, :pooled_columns]
        input_grad = jnp.concatenate([ig[0], ig[1]], -1)[:, :, :columns]
        sums = jnp.concatenate([sums[0], sums[1]], -1)
        return (
            pooled,
            input_grad,
            kg.astype(F32).reshape(conv_weights.shape),
            sums[:LAYERS],
            sums[LAYERS : 2 * LAYERS],
        )

    return jax.shard_map(
        per_device,
        mesh=mesh,
        in_specs=(
            P("maps", "rows", None, None),
            P(),
            P(),
            P(),
            P(),
            P(),
            P("maps", "rows", None, None),
            P("maps", None),
            P(),
            P(None, "maps", "rows", None, None),
        ),
        out_specs=(P("maps", "rows", None, None), P("maps", "rows", None, None), P(), P(), P()),
        check_vma=False,
    )
```

```python
import functools

import jax
import jax.numpy as jnp
from jax import lax
from jax.experimental import pallas as pl
from jax.experimental.pallas import tpu as pltpu
from jax.sharding import PartitionSpec as P

MESH = pl.DeviceIdType.MESH
epsilon = 1e-05
PAD = 64
LAYERS = 3
TAPS = 9
UNITS = LAYERS * TAPS
PLANE = 4
LAG = 4
EARLY = 1
FOLD = 2
F32 = jnp.float32
BF16 = jnp.bfloat16


def each(first, last, body):
    if last - first <= 8:
        for k in range(first, last):
            body(k)
    else:
        lax.fori_loop(first, last, lambda k, s: (body(k), s)[1], 0)


def block_kernel(
    chips,
    height,
    x_ref,
    w_ref,
    gain_hbm,
    shift_hbm,
    width_hbm,
    group_hbm,
    index_hbm,
    tmask_hbm,
    tweight_hbm,
    tgrad_hbm,
    pooled_ref,
    ig_ref,
    kg_ref,
    sums_ref,
    gain_ref,
    shift_ref,
    width_ref,
    group_ref,
    index_ref,
    tmask_ref,
    tweight_ref,
    tgrad_ref,
    wa,
    wb,
    act_own,
    act_oth,
    act_t,
    act_b,
    zbuf,
    zs,
    zh,
    dh,
    dhs,
    dhh,
    dz_own,
    dz_oth,
    dzr,
    dzv,
    prod,
    gsrc,
    gbuf,
    hrow,
    pbuf,
    st1,
    st2,
    coef,
    nall,
    inv_t,
    cnt_t,
    avg_t,
    scl_t,
    mean_t,
    tb_t,
    ta_t,
    sums_own,
    terms,
    r2,
    rf,
    r3,
    fin,
    in_sem,
    w_sem,
    x_s,
    x_r,
    g_s,
    g_r,
    st1_s,
    st1_r,
    st2_s,
    st2_r,
    zh_s,
    zh_r,
    dh_s,
    dh_r,
    act_s,
    act_r,
    dz_s,
    dz_r,
    out_s,
    out_r,
    out_l,
    at_s,
    at_r,
    dzr_s,
    dzr_r,
    r2_s,
    r2_r,
    rf_s,
    rf_r,
    r3_s,
    r3_r,
    az_s,
    az_r,
    af_s,
    af_r,
    ab_s,
    ab_r,
    aa_s,
    aa_r,
    ap_s,
    ap_r,
    loc_s,
):
    maps_here = x_ref.shape[0]
    columns = x_ref.shape[2]
    half = x_ref.shape[3] // 2
    tasks = tgrad_ref.shape[0]
    pooled_columns = tgrad_ref.shape[3]
    lanes = half // 128
    tiles = [slice(n * 128, (n + 1) * 128) for n in range(lanes)]
    band = 4
    pixels = maps_here * band * PAD
    actives = chips // 2
    owners = min(actives, 8)
    piece = (half // 2) // owners
    m = lax.axis_index("maps")
    r = lax.axis_index("rows")
    c = lax.rem(r, 2)
    z = lax.div(r, 2)
    other = 1 - c
    first_map = m * maps_here
    x_bit = lax.rem(m, 2)
    y_bit = lax.div(m, 2)
    x_peer = m + 1 - 2 * x_bit
    y_peer = m + 2 - 4 * y_bit
    g_bit = (1 - c) * x_bit + c * y_bit
    h_bit = (1 - c) * y_bit + c * x_bit
    g_peer = (1 - c) * x_peer + c * y_peer
    h_peer = (1 - c) * y_peer + c * x_peer
    pair = lax.div(z, 2)
    turn = lax.rem(pair, 2)
    active_z = 2 * pair + 1 - turn
    is_active = z == active_z
    is_passive = z != active_z
    is_owner = jnp.logical_and(is_active, pair < owners)
    up_there = z > 0
    down_there = z < chips - 1
    row8 = lax.broadcasted_iota(jnp.int32, (8, half), 0)
    column = lax.broadcasted_iota(jnp.int32, (PAD, half), 0)

    def remote(src, dst, send, recv, mm, zz, cc):
        return pltpu.make_async_remote_copy(
            src_ref=src,
            dst_ref=dst,
            send_sem=send,
            recv_sem=recv,
            device_id=(mm, zz * 2 + cc),
            device_id_type=MESH,
        )

    def own_half(v):
        return jnp.where(c == 0, v[..., :half], v[..., half:])

    def width_of(a):
        return width_ref[first_map + a]

    own_at = pl.ds(pl.multiple_of(c * half, half), half)
    oth_at = pl.ds(pl.multiple_of(other * half, half), half)

    def weight_copy(l, n):
        dst = (wa, wb, wb)[n]
        k_at, o_at = ((own_at, own_at), (oth_at, own_at), (own_at, oth_at))[n]
        return pltpu.make_async_copy(w_ref.at[l, :, :, k_at, o_at], dst.at[l], w_sem.at[l, n])

    fetches = [
        pltpu.make_async_copy(src, dst, in_sem.at[n])
        for n, (src, dst) in enumerate(
            (
                (width_hbm, width_ref),
                (group_hbm, group_ref),
                (tmask_hbm, tmask_ref),
                (tweight_hbm, tweight_ref),
                (gain_hbm, gain_ref),
                (shift_hbm, shift_ref),
                (index_hbm.at[:, :, 0, :], index_ref),
                (tgrad_hbm, tgrad_ref),
            )
        )
    ]
    for fetch in fetches:
        fetch.start()
    for l in range(LAYERS):
        weight_copy(l, 0).start()
        weight_copy(l, 1).start()

    barrier = pltpu.get_barrier_semaphore()

    def greet(k):
        rr = lax.rem(r + k, 2 * chips)
        pl.semaphore_signal(barrier, inc=1, device_id=(m, rr), device_id_type=MESH)

    each(1, 2 * chips, greet)
    for k in range(1, PLANE):
        for core in (c, other):
            there = (lax.rem(m + k, PLANE), z * 2 + core)
            pl.semaphore_signal(barrier, inc=1, device_id=there, device_id_type=MESH)

    for fetch in fetches:
        fetch.wait()

    mine = pl.ds(1 + 2 * c, 2)
    for a in range(maps_here):
        inside = lax.broadcasted_iota(jnp.int32, (columns, 2 * half), 0) < width_of(a)
        for rr in range(2):
            v = jnp.where(inside, x_ref[a, rr].astype(F32), 0.0).astype(BF16)
            spot = 1 + 2 * c + rr
            act_own[0, a, spot, pl.ds(48, 16), :] = jnp.zeros((16, half), BF16)
            act_oth[0, a, spot, pl.ds(48, 16), :] = jnp.zeros((16, half), BF16)
            act_own[0, a, spot, pl.ds(0, columns), :] = own_half(v)
            act_oth[0, a, spot, pl.ds(0, columns), :] = jnp.where(
                c == 0, v[:, half:], v[:, :half]
            )

    @pl.when(z == 0)
    def _():
        act_own[0, :, 0] = jnp.zeros((maps_here, PAD, half), BF16)
        act_oth[0, :, 0] = jnp.zeros((maps_here, PAD, half), BF16)

    @pl.when(z == chips - 1)
    def _():
        act_own[0, :, 5] = jnp.zeros((maps_here, PAD, half), BF16)
        act_oth[0, :, 5] = jnp.zeros((maps_here, PAD, half), BF16)

    pl.semaphore_wait(barrier, 2 * chips - 1 + 2 * (PLANE - 1))

    x_partner = (
        remote(act_own.at[0, :, mine], act_oth.at[0, :, mine], x_s.at[0], x_r.at[0], m, z, other),
        remote(act_oth.at[0, :, mine], act_own.at[0, :, mine], x_s.at[1], x_r.at[1], m, z, other),
    )
    g_partner = remote(gsrc.at[other], gbuf.at[1 + c], g_s.at[0], g_r.at[0], m, z, other)

    def x_halo(n, src_row, dst_row, zz):
        cc = (c, c, other, other, c, other)[n]
        low = dst_row == band + 1
        if n >= 4:
            src, dst = gsrc.at[cc], gbuf.at[3 if low else 0]
            return remote(src, dst, g_s.at[n - 3], g_r.at[1 if low else 2], m, zz, cc)
        src = (act_own, act_oth, act_own, act_oth)[n].at[0, :, src_row]
        dst = (act_own, act_oth, act_oth, act_own)[n].at[0, :, dst_row]
        return remote(src, dst, x_s.at[2 + n], x_r.at[(2 if low else 4) + n % 2], m, zz, cc)

    for copy in x_partner:
        copy.start()

    @pl.when(jnp.logical_and(c == 0, up_there))
    def _():
        for n in range(4):
            x_halo(n, 1, 5, z - 1).start()

    @pl.when(jnp.logical_and(c == 1, down_there))
    def _():
        for n in range(4):
            x_halo(n, 4, 0, z + 1).start()

    gsrc[...] = jnp.zeros(gsrc.shape, F32)
    for a in range(maps_here):
        total = None
        for t in range(tasks):
            scale = tweight_ref[t] * tmask_ref[a, t].astype(F32)
            term = tgrad_ref[t, a, 0].astype(F32) * scale
            total = term if total is None else total + term
        position = index_ref[a].astype(F32)
        for h in range(2):
            gsrc[h, 0, a, pl.ds(0, pooled_columns), :] = total[:, h * half : (h + 1) * half]
            gsrc[h, 1, a, pl.ds(0, pooled_columns), :] = position[:, h * half : (h + 1) * half]
    gbuf[1 + c] = gsrc[c]

    for mm in range(PLANE):
        sizes = jnp.zeros((8, half), F32)
        for b in range(maps_here):
            sizes = jnp.where(
                row8 == b, (width_ref[mm * maps_here + b] * height).astype(F32), sizes
            )
        nall[mm] = sizes
    inside_sizes = jnp.zeros((8, half), F32)
    for b in range(maps_here):
        inside_sizes = jnp.where(row8 == b, (width_of(b) * band).astype(F32), inside_sizes)
    inv_t[0] = inside_sizes
    inv_t[1] = jnp.where(row8 < maps_here, 1.0 / jnp.maximum(inside_sizes, 1.0), 0.0)
    counts = jnp.ones((8, half), F32)
    for a in range(maps_here):
        total = jnp.zeros((1, half), F32)
        for mm in range(PLANE):
            same = jnp.zeros((8, half), F32)
            for b in range(maps_here):
                alike = group_ref[first_map + a] == group_ref[mm * maps_here + b]
                same = jnp.where(row8 == b, jnp.where(alike, 1.0, 0.0), same)
            coef[a, mm] = same
            total = total + jnp.sum(same * nall[mm], 0, keepdims=True)
        counts = jnp.where(row8 == a, total, counts)
    cnt_t[...] = counts

    def z_copy(e, k):
        zz = lax.rem(z + k, chips)
        return remote(st1.at[e, z], st1.at[e, z], st1_s.at[e, k], st1_r.at[e, z], m, zz, c)

    def z_arrival(e, k):
        zz = lax.rem(z + k, chips)
        return remote(st1.at[e, zz], st1.at[e, zz], st1_s.at[e, k], st1_r.at[e, zz], m, zz, c)

    def m_copy(e, k):
        mm = lax.rem(m + k, PLANE)
        return remote(st2.at[e, m], st2.at[e, m], st2_s.at[e, k], st2_r.at[e, m], mm, z, c)

    def m_arrival(e, k):
        mm = lax.rem(m + k, PLANE)
        return remote(st2.at[e, mm], st2.at[e, mm], st2_s.at[e, k], st2_r.at[e, mm], mm, z, c)

    def send_z(e, tile):
        st1[e, z] = tile
        each(1, chips, lambda k: z_copy(e, k).start())

    def wait_z(e):
        each(1, chips, lambda k: z_arrival(e, k).wait_recv())

    def send_m(e, tile):
        st2[e, m] = tile
        each(1, PLANE, lambda k: m_copy(e, k).start())

    def wait_m(e):
        each(1, PLANE, lambda k: m_arrival(e, k).wait_recv())

    def products(source, l, taps, kernel, transposed, fresh):
        starts = [2 - i if transposed else i for i in taps]
        lhs = jnp.concatenate(
            [source[lax.rem(l, 2), :, s : s + band].reshape(pixels, half) for s in starts], 1
        )
        for j in range(3):
            rhs = jnp.concatenate([kernel[l, i, j] for i in taps], 1 if transposed else 0)
            got = lax.dot_general(
                lhs,
                rhs,
                (((1,), (1 if transposed else 0,)), ((), ())),
                preferred_element_type=F32,
            )
            if fresh:
                prod[j] = got
            else:
                prod[j] = prod[j] + got

    def shifted(a, rr, before, behind, n):
        rows = pl.ds(pl.multiple_of((a * band + rr) * PAD, PAD), PAD)
        return (
            prod[1, rows, n]
            + pltpu.roll(prod[before, rows, n], 1, 0)
            + pltpu.roll(prod[behind, rows, n], PAD - 1, 0)
        )

    def row_of(table, l, a):
        return table[l, pl.ds(a, 1), :]

    def gain_of(l):
        return own_half(gain_ref[pl.ds(l, 1), :])

    def shift_of(l):
        return own_half(shift_ref[pl.ds(l, 1), :])

    def limit(a, rr):
        w = width_of(a)
        if rr == 0:
            return jnp.where(up_there, w, 0)
        if rr == band + 1:
            return jnp.where(down_there, w, 0)
        return w

    def z_halo(l, way):
        there = z - 1 + 2 * way
        return remote(zs.at[way], zh.at[l, 1 - way], zh_s.at[l, way], zh_r.at[l, way], m, there, c)

    def dh_halo(l, way):
        there = z - 1 + 2 * way
        return remote(dhs.at[way], dhh.at[l, 1 - way], dh_s.at[l, way], dh_r.at[l, way], m, there, c)

    def start_halo(halo, l):
        @pl.when(up_there)
        def _():
            halo(l, 0).start()

        @pl.when(down_there)
        def _():
            halo(l, 1).start()

    def wait_halo(halo, l):
        @pl.when(up_there)
        def _():
            halo(l, 1).wait_recv()
            halo(l, 0).wait_send()

        @pl.when(down_there)
        def _():
            halo(l, 0).wait_recv()
            halo(l, 1).wait_send()

    def act_copy(l, a, first=0, rows=band + 2):
        at = (lax.rem(l, 2), a, pl.ds(first, rows))
        src, dst = act_own.at[at], act_oth.at[at]
        return remote(src, dst, act_s.at[l, a], act_r.at[l, a], m, z, other)

    def at_copy(l):
        return remote(act_t.at[l, 0], act_t.at[l, 1], at_s.at[l], at_r.at[l], g_peer, z, c)

    def dzr_copy(l, a, way):
        src, dst = dz_own.at[lax.rem(l, 2), a, pl.ds(1, band)], dzr.at[l, a]
        peer = (x_peer, y_peer)[way]
        return remote(src, dst, dzr_s.at[l, way, a], dzr_r.at[l, a], peer, z, way)

    def if_wanted(way, body):
        @pl.when((x_bit, y_bit)[way] + c == 1)
        def _():
            body()

    def dz_copy(l, a, first=0, rows=band + 2):
        at = (lax.rem(l, 2), a, pl.ds(first, rows))
        src, dst = dz_own.at[at], dz_oth.at[at]
        return remote(src, dst, dz_s.at[l, a], dz_r.at[l, a], m, z, other)

    def send_gradients():
        g_partner.start()

        @pl.when(jnp.logical_and(c == 0, up_there))
        def _():
            for n in range(4, 6):
                x_halo(n, 1, 5, z - 1).start()

        @pl.when(jnp.logical_and(c == 1, down_there))
        def _():
            for n in range(4, 6):
                x_halo(n, 4, 0, z + 1).start()

    def wait_x_halo(first, last):
        @pl.when(up_there)
        def _():
            for n in (0, 1, 4)[first:last]:
                x_halo(n, 4, 0, z - 1).wait_recv()

        @pl.when(down_there)
        def _():
            for n in (0, 1, 4)[first:last]:
                x_halo(n, 1, 5, z + 1).wait_recv()

    def sent_x_halo(first, last):
        @pl.when(jnp.logical_and(c == 0, up_there))
        def _():
            for n in range(first, last):
                x_halo(n, 1, 5, z - 1).wait_send()

        @pl.when(jnp.logical_and(c == 1, down_there))
        def _():
            for n in range(first, last):
                x_halo(n, 4, 0, z + 1).wait_send()

    def forward(l, first):
        weight_copy(l, 0).wait()
        weight_copy(l, 1).wait()
        if first:
            for copy in x_partner:
                copy.wait_recv()
            products(act_own, l, (1,), wa, False, True)
            products(act_oth, l, (1,), wb, False, False)
            wait_x_halo(0, 2)
            products(act_own, l, (0, 2), wa, False, False)
            products(act_oth, l, (0, 2), wb, False, False)
        else:
            products(act_own, l, (0, 1, 2), wa, False, True)
            for a in range(maps_here):
                act_copy(l, a).wait_recv()
            products(act_oth, l, (0, 1, 2), wb, False, False)
        weight_copy(l, 2).start()

        def collect(a, tile):
            inside = column[:, :128] < width_of(a)
            pixels_inside = (width_of(a) * band).astype(F32)
            totals, squares = [], []
            for n in tiles:
                total = jnp.zeros((PAD, 128), F32)
                for rr in range(band):
                    v = shifted(a, rr, 0, 2, n)
                    zbuf[l, a, 1 + rr, :, n] = v
                    total = total + jnp.where(inside, v, 0.0)
                total = jnp.sum(total, 0, keepdims=True)
                mean = total / pixels_inside
                square = jnp.zeros((PAD, 128), F32)
                for rr in range(band):
                    v = jnp.where(inside, zbuf[l, a, 1 + rr, :, n] - mean, 0.0)
                    square = square + v * v
                    if rr in (0, band - 1):
                        zs[rr // (band - 1), a, :, n] = v.astype(BF16)
                totals.append(total)
                squares.append(jnp.sum(square, 0, keepdims=True))
            tile = jnp.where(row8 == a, jnp.concatenate(totals, 1), tile)
            return jnp.where(row8 == a + maps_here, jnp.concatenate(squares, 1), tile)

        tile = lax.fori_loop(0, maps_here, collect, jnp.zeros((8, half), F32))
        send_z(l, tile)
        start_halo(z_halo, l)
        act_t[l, 0] = act_own[lax.rem(l, 2)].reshape(maps_here * (band + 2) * PAD, half).T
        wait_z(l)
        sizes, inverse = inv_t[0], inv_t[1]
        mean_t[0] = st1[l, jnp.maximum(z - 1, 0)] * inverse
        mean_t[1] = st1[l, jnp.minimum(z + 1, chips - 1)] * inverse
        total = st1[l, 0]
        for zz in range(1, chips):
            total = total + st1[l, zz]
        mean = total * inverse * (1.0 / chips)
        square = jnp.zeros((8, half), F32)
        for zz in range(chips):
            v = st1[l, zz]
            gap = v * inverse - mean
            square = square + pltpu.roll(v, 8 - maps_here, 0) + sizes * gap * gap
        tile = jnp.where(row8 < maps_here, mean, pltpu.roll(square, maps_here, 0))
        send_m(l, jnp.where(row8 < 2 * maps_here, tile, 0.0))
        wait_m(l)
        at_copy(l).start()
        if first:
            send_gradients()
        averages = jnp.zeros((8, half), F32)
        scalings = jnp.zeros((8, half), F32)
        for a in range(maps_here):
            count = cnt_t[a : a + 1, :]
            average = jnp.zeros((8, half), F32)
            for mm in range(PLANE):
                average = average + coef[a, mm] * nall[mm] * st2[l, mm]
            average = jnp.sum(average, 0, keepdims=True) / count
            variance = jnp.zeros((8, half), F32)
            for mm in range(PLANE):
                v = st2[l, mm]
                gap = v - average
                variance = variance + coef[a, mm] * (
                    pltpu.roll(v, 8 - maps_here, 0) + nall[mm] * gap * gap
                )
            variance = jnp.sum(variance, 0, keepdims=True) / count
            averages = jnp.where(row8 == a, average, averages)
            scalings = jnp.where(row8 == a, lax.rsqrt(variance + epsilon), scalings)
        avg_t[l] = averages
        scl_t[l] = scalings
        wait_halo(z_halo, l)

        def activate(a, s):
            gain, shift = gain_of(l), shift_of(l)
            for n in tiles:
                average = row_of(avg_t, l, a)[:, n]
                factor = row_of(scl_t, l, a)[:, n] * gain[:, n]
                for rr in range(band + 2):
                    if rr in (0, band + 1):
                        way = rr // (band + 1)
                        v = zh[l, way, a, :, n].astype(F32) + row_of(mean_t, way, a)[:, n]
                        zbuf[l, a, rr, :, n] = v
                    else:
                        v = zbuf[l, a, rr, :, n]
                    y = (v - average) * factor + shift[:, n]
                    h = jnp.where(column[:, n] < limit(a, rr), y * jax.nn.sigmoid(y), 0.0)
                    act_own[lax.rem(l + 1, 2), a, rr, :, n] = h.astype(BF16)

            @pl.when(l < LAYERS - 1)
            def _():
                for n in range(0, band + 2, 2):
                    act_copy(l + 1, a, n, 2).start()

            return s

        if first:
            for copy in x_partner:
                copy.wait_send()
            sent_x_halo(0, 4)
        else:

            @pl.when(l == 2)
            def _():
                for a in range(maps_here):
                    act_copy(1, a).wait_send()

        lax.fori_loop(0, maps_here, activate, 0)

    forward(0, True)
    lax.fori_loop(1, LAYERS, lambda l, s: (forward(l, False), s)[1], 0)
    g_partner.wait_recv()
    wait_x_halo(2, 3)

    def unpool(a, s):
        for rr in range(band + 2):
            slot, lower = (rr + 1) // 2, (rr + 1) % 2
            g = gbuf[slot, 0, a]
            position = gbuf[slot, 1, a]
            for b in range(2):
                v = jnp.where(position == float(2 * lower + b), g, 0.0)
                for n in range(lanes):
                    hrow[n, pl.ds(b, PAD // 2, stride=2), :] = v[:, n * 128 : (n + 1) * 128]
            v = jnp.concatenate([hrow[n] for n in range(lanes)], 1)
            if rr in (0, band + 1):
                dhh[LAYERS - 1, rr // (band + 1), a] = v.astype(BF16)
            else:
                dh[a, rr - 1] = v
        return s

    lax.fori_loop(0, maps_here, unpool, 0)

    def pool():
        def one(a, s):
            for pr in range(2):
                total = jnp.zeros((PAD // 2, half), F32)
                position = gbuf[1 + pr, 1, a]
                for lower in range(2):
                    v = act_own[LAYERS % 2, a, 1 + 2 * pr + lower].astype(F32)
                    for n in range(lanes):
                        hrow[n] = v[:, n * 128 : (n + 1) * 128]
                    for b in range(2):
                        v = jnp.concatenate(
                            [hrow[n, pl.ds(b, PAD // 2, stride=2), :] for n in range(lanes)], 1
                        )
                        total = total + jnp.where(position == float(2 * lower + b), v, 0.0)
                pbuf[pr, a] = total.astype(BF16)
            return s

        lax.fori_loop(0, maps_here, one, 0)

    def second_rows(bit):
        return pl.ds(pl.multiple_of(bit * (half // 2), half // 2), half // 2)

    def piece_rows(p):
        return pl.ds(pl.multiple_of(p * piece, piece), piece)

    def term_slot(q):
        return lax.rem(q, 2 * TAPS)

    def c2(q):
        src = terms.at[term_slot(q), second_rows(1 - h_bit)]
        return remote(src, r2.at[q], r2_s.at[q], r2_r.at[q], h_peer, z, c)

    def z_of(n):
        return 2 * n + 1 - lax.rem(n, 2)

    def cf(q):
        passive_z = 2 * pair + turn
        there = active_z + passive_z - z
        return remote(r2.at[q], rf.at[term_slot(q)], rf_s.at[q], rf_r.at[q], m, there, c)

    def c3(q, p):
        slot = lax.rem(pair - p + actives - 1, actives)
        return remote(
            r2.at[q, piece_rows(p)], r3.at[q, slot], r3_s.at[q, p], r3_r.at[q, slot], m, z_of(p), c
        )

    def others(first, body, limit):
        def one(k):
            n = lax.rem(pair + k, actives)

            @pl.when(n < limit)
            def _():
                body(n)

        each(first, actives, one)

    def unit_of(q):
        k = lax.div(q, TAPS)
        return (LAYERS - 1 - k) * TAPS + (q - k * TAPS)

    def region(q, start, size, lane, lanes):
        start = pl.multiple_of(c * half + start, piece)
        lane = pl.multiple_of(lane, half)
        return kg_ref.at[unit_of(q), pl.ds(start, size), pl.ds(lane, lanes)]

    def cz(q, p, n):
        part = region(q, h_bit * (half // 2) + p * piece, piece, g_bit * half, half)
        return remote(fin.at[q], part, az_s.at[q, n], az_r.at[q, p], m, z_of(n), c)

    def cl(q):
        part = region(q, h_bit * (half // 2) + pair * piece, piece, g_bit * half, half)
        return pltpu.make_async_copy(fin.at[q], part, loc_s.at[q])

    def cu(q):
        passive_z = 2 * pair + turn
        there = active_z + passive_z - z
        part = region(q, h_bit * (half // 2), half // 2, g_bit * half, half)
        return remote(part, part, af_s.at[q], af_r.at[q], m, there, c)

    def cb(q):
        part = region(q, h_bit * (half // 2), half // 2, g_bit * half, half)
        return remote(part, part, ab_s.at[q], ab_r.at[q], h_peer, z, c)

    def ca(q, first=0, rows=half):
        part = region(q, first, rows, g_bit * half, half)
        return remote(part, part, aa_s.at[q], aa_r.at[q], g_peer, z, c)

    def cp(q, first=0, rows=half):
        part = region(q, first, rows, 0, 2 * half)
        return remote(part, part, ap_s.at[q], ap_r.at[q], m, z, other)

    def ready_terms(l):
        at_copy(l).wait_recv()
        for chip in range(2):
            for a in range(maps_here):
                first = a * (band + 2) * PAD
                rows = act_t[l, chip, :, first : first + (band + 2) * PAD]
                act_b[chip, :, a * band * PAD : (a + 1) * band * PAD] = rows[:, PAD : PAD + band * PAD]
        slot = lax.rem(l, 2)

        def variants(a, s):
            dzr_copy(l, a, 0).wait_recv()
            for chip in range(2):
                for rr in range(band):
                    for n in tiles:
                        if chip == 0:
                            mine, theirs = dz_own[slot, a, 1 + rr, :, n], dz_oth[slot, a, 1 + rr, :, n]
                            v = jnp.where(g_bit == c, mine, theirs)
                        else:
                            v = dzr[l, a, rr, :, n]
                        dzv[1, chip, a, rr, :, n] = v
                        v = v.astype(F32)
                        dzv[0, chip, a, rr, :, n] = pltpu.roll(v, PAD - 1, 0).astype(BF16)
                        dzv[2, chip, a, rr, :, n] = pltpu.roll(v, 1, 0).astype(BF16)
            return s

        lax.fori_loop(0, maps_here, variants, 0)

    def tap_terms(l, i, j):
        if i == 1:
            lhs = [act_b[0], act_b[1]]
        else:
            lhs = []
            for chip in range(2):
                for a in range(maps_here):
                    first = (a * (band + 2) + i) * PAD
                    lhs.append(act_t[l, chip, :, first : first + band * PAD])
        rhs = dzv[j].reshape(2 * pixels, half)
        q = (LAYERS - 1 - l) * TAPS + 3 * i + j
        got = jnp.dot(jnp.concatenate(lhs, 1), rhs, preferred_element_type=F32)
        terms[term_slot(q)] = got.astype(BF16)

    def weight_terms(l, i):
        lax.fori_loop(0, 3, lambda j, s: (tap_terms(l, i, j), s)[1], 0)

    def stage_second(q):
        c2(q).wait()
        kept = terms[term_slot(q), second_rows(h_bit)].astype(F32)
        r2[q] = (r2[q].astype(F32) + kept).astype(BF16)

        @pl.when(is_passive)
        def _():
            cf(q).start()

    def stage_fold(q):
        @pl.when(is_active)
        def _():
            cf(q).wait_recv()
            r2[q] = (r2[q].astype(F32) + rf[term_slot(q)].astype(F32)).astype(BF16)
            others(1, lambda n: c3(q, n).start(), owners)

    def stage_sum(q):
        @pl.when(is_owner)
        def _():
            for k in range(actives - 1):
                remote(
                    r3.at[q, k], r3.at[q, k], r3_s.at[q, 0], r3_r.at[q, k], m, z, c
                ).wait_recv()
            total = r2[q, piece_rows(pair)].astype(F32)
            for k in range(actives - 1):
                total = total + r3[q, k].astype(F32)
            fin[q] = total.astype(BF16)
            others(1, lambda n: cz(q, pair, n).start(), actives)
            cl(q).start()

    def stage_back(q):
        @pl.when(is_active)
        def _():
            others(1, lambda n: cz(q, n, n).wait_recv(), owners)

        @pl.when(is_owner)
        def _():
            cl(q).wait()

        @pl.when(is_active)
        def _():
            cu(q).start()

        @pl.when(is_passive)
        def _():
            cu(q).wait_recv()

        cb(q).start()

    def stage_first(q):
        cb(q).wait_recv()
        for n in range(2):
            ca(q, n * (half // 2), half // 2).start()

        @pl.when(is_active)
        def _():
            others(1, lambda n: c3(q, n).wait_send(), owners)

        @pl.when(is_passive)
        def _():
            cf(q).wait_send()

    def stage_chip(q):
        ca(q).wait_recv()
        for n in range(4):
            cp(q, n * (half // 4), half // 4).start()

        @pl.when(is_owner)
        def _():
            others(1, lambda n: cz(q, pair, n).wait_send(), actives)

        @pl.when(is_active)
        def _():
            cu(q).wait_send()

    def stage_done(q):
        cb(q).wait_send()
        ca(q).wait_send()
        cp(q).wait()

    def run(stage, first, last):
        lax.fori_loop(first, last, lambda q, s: (stage(q), s)[1], 0)

    def sent_dz(l):
        for a in range(maps_here):
            dz_copy(l, a).wait_send()
            for way in range(2):
                if_wanted(way, dzr_copy(l, a, way).wait_send)

    def backward(k, carry):
        l = LAYERS - 1 - k
        gain, shift = gain_of(l), shift_of(l)

        def gradient(a, rr, n):
            zhat = (zbuf[l, a, rr, :, n] - row_of(avg_t, l, a)[:, n]) * row_of(scl_t, l, a)[:, n]
            y = zhat * gain[:, n] + shift[:, n]
            s = jax.nn.sigmoid(y)
            if rr in (0, band + 1):
                upstream = dhh[l, rr // (band + 1), a, :, n].astype(F32)
            else:
                upstream = dh[a, rr - 1, :, n]
            dy = upstream * (s * (1.0 + y * (1.0 - s)))
            dy = jnp.where(column[:, n] < limit(a, rr), dy, 0.0)
            return dy, zhat

        def collect(a, tile):
            plains, crosses = [], []
            for n in tiles:
                plain = jnp.zeros((PAD, 128), F32)
                crossed = jnp.zeros((PAD, 128), F32)
                for rr in range(1, band + 1):
                    dy, zhat = gradient(a, rr, n)
                    dh[a, rr - 1, :, n] = dy
                    plain = plain + dy
                    crossed = crossed + dy * zhat
                plains.append(jnp.sum(plain, 0, keepdims=True))
                crosses.append(jnp.sum(crossed, 0, keepdims=True))
            tile = jnp.where(row8 == a, jnp.concatenate(plains, 1), tile)
            return jnp.where(row8 == a + maps_here, jnp.concatenate(crosses, 1), tile)

        e = LAYERS + l
        tile = lax.fori_loop(0, maps_here, collect, jnp.zeros((8, half), F32))
        send_z(e, tile)

        @pl.when(k == LAYERS - 1)
        def _():
            run(stage_second, 0, TAPS)

        @pl.when(k > 0)
        def _():
            ready_terms(l + 1)
            weight_terms(l + 1, 0)

        wait_z(e)
        total = st1[e, 0]
        for zz in range(1, chips):
            total = total + st1[e, zz]
        send_m(e, total)

        @pl.when(k > 0)
        def _():
            first = (LAYERS - 2 - l) * TAPS
            run(lambda q: c2(q).start(), first, first + 3)
            weight_terms(l + 1, 1)
            run(lambda q: c2(q).start(), first + 3, first + 6)
            weight_terms(l + 1, 2)
            run(lambda q: c2(q).start(), first + 6, first + 9)
            wait_halo(dh_halo, l)

        @pl.when(k == 0)
        def _():
            pool()

        wait_m(e)
        total = st2[e, 0]
        for mm in range(1, PLANE):
            total = total + st2[e, mm]
        sums_own[pl.ds(l, 1), :] = jnp.sum(
            jnp.where(row8 >= maps_here, total, 0.0), 0, keepdims=True
        )
        sums_own[pl.ds(LAYERS + l, 1), :] = jnp.sum(
            jnp.where(row8 < maps_here, total, 0.0), 0, keepdims=True
        )
        plains = jnp.zeros((8, half), F32)
        crosses = jnp.zeros((8, half), F32)
        for a in range(maps_here):
            plain = jnp.zeros((8, half), F32)
            crossed = jnp.zeros((8, half), F32)
            for mm in range(PLANE):
                v = st2[e, mm]
                plain = plain + coef[a, mm] * v
                crossed = crossed + coef[a, mm] * pltpu.roll(v, 8 - maps_here, 0)
            count = cnt_t[a : a + 1, :]
            plain = gain * (jnp.sum(plain, 0, keepdims=True) / count)
            crossed = gain * (jnp.sum(crossed, 0, keepdims=True) / count)
            plains = jnp.where(row8 == a, plain, plains)
            crosses = jnp.where(row8 == a, crossed, crosses)
        tb_t[0] = plains
        ta_t[0] = crosses

        def settle(a, s):
            for n in tiles:
                average, scaling = row_of(avg_t, l, a)[:, n], row_of(scl_t, l, a)[:, n]
                plain, crossed = row_of(tb_t, 0, a)[:, n], row_of(ta_t, 0, a)[:, n]
                for rr in range(band + 2):
                    if rr in (0, band + 1):
                        dy, zhat = gradient(a, rr, n)
                    else:
                        dy = dh[a, rr - 1, :, n]
                        zhat = (zbuf[l, a, rr, :, n] - average) * scaling
                    v = scaling * (dy * gain[:, n] - plain - zhat * crossed)
                    v = jnp.where(column[:, n] < limit(a, rr), v, 0.0)
                    dz_own[lax.rem(l, 2), a, rr, :, n] = v.astype(BF16)
            for n in range(0, band + 2, 2):
                dz_copy(l, a, n, 2).start()
            for way in range(2):
                if_wanted(way, dzr_copy(l, a, way).start)
            return s

        @pl.when(k == 2)
        def _():
            sent_dz(LAYERS - 1)

        lax.fori_loop(0, maps_here, settle, 0)
        products(dz_own, l, (0, 1, 2), wa, True, True)
        weight_copy(l, 2).wait()
        for a in range(maps_here):
            dz_copy(l, a).wait_recv()
        products(dz_oth, l, (0, 1, 2), wb, True, False)

        def gather(a, s):
            for n in tiles:
                for rr in range(band):
                    v = shifted(a, rr, 2, 0, n)
                    dh[a, rr, :, n] = v
                    if rr in (0, band - 1):
                        dhs[rr // (band - 1), a, :, n] = v.astype(BF16)
            return s

        lax.fori_loop(0, maps_here, gather, 0)

        @pl.when(l > 0)
        def _():
            start_halo(dh_halo, l - 1)

        return carry

    lax.fori_loop(0, LAYERS, backward, 0)
    def input_rows(a, s):
        for rr in range(band):
            dh[a, rr] = jnp.where(column < width_of(a), dh[a, rr], 0.0)
        return s

    lax.fori_loop(0, maps_here, input_rows, 0)

    outs = (
        (
            remote(dh.at[:, pl.ds(2 * other, 2)], ig_ref.at[c], out_s.at[0], out_r.at[0], m, z, other),
            pltpu.make_async_copy(dh.at[:, pl.ds(2 * c, 2)], ig_ref.at[c], out_l.at[0]),
        ),
        (
            remote(pbuf.at[other], pooled_ref.at[c], out_s.at[1], out_r.at[1], m, z, other),
            pltpu.make_async_copy(pbuf.at[c], pooled_ref.at[c], out_l.at[1]),
        ),
        (
            remote(sums_own, sums_ref.at[c], out_s.at[2], out_r.at[2], m, z, other),
            pltpu.make_async_copy(sums_own, sums_ref.at[c], out_l.at[2]),
        ),
    )
    for there, here in outs:
        there.start()
        here.start()

    g_partner.wait_send()
    sent_x_halo(4, 6)

    def sent(e, carry):
        each(1, chips, lambda k: z_copy(e, k).wait_send())
        each(1, PLANE, lambda k: m_copy(e, k).wait_send())
        return carry

    lax.fori_loop(0, 2 * LAYERS, sent, 0)
    for l in range(LAYERS):
        at_copy(l).wait_send()
    for l in range(LAYERS - 1):
        sent_dz(l)

    def drain(s, carry):
        @pl.when(s == EARLY)
        def _():
            ready_terms(0)

        for i in range(3):
            j = s - EARLY - 3 * i

            @pl.when(jnp.logical_and(j >= 0, j < 3))
            def _(i=i, j=j):
                tap_terms(0, i, j)
                c2(2 * TAPS + 3 * i + j).start()

        for stage, first, lag in (
            (stage_done, 0, 2 * FOLD + 3 * LAG),
            (stage_chip, 0, 2 * FOLD + 2 * LAG),
            (stage_first, 0, 2 * FOLD + LAG),
            (stage_back, 0, 2 * FOLD),
            (stage_sum, 0, FOLD),
            (stage_fold, 0, 0),
            (stage_second, TAPS, 0),
        ):
            q = first + s - lag

            @pl.when(jnp.logical_and(q >= first, q < UNITS))
            def _(stage=stage, q=q):
                stage(q)

        return carry

    lax.fori_loop(0, UNITS + 2 * FOLD + 3 * LAG, drain, 0)
    for a in range(maps_here):
        act_copy(2, a).wait_send()
    for there, here in outs:
        there.wait()
        here.wait()


def solution(mesh):
    chips = mesh.shape["rows"] // 2

    def per_device(
        block_input,
        conv_weights,
        norm_gains,
        norm_shifts,
        map_width,
        map_group,
        pool_index,
        task_mask,
        task_weights,
        task_grads,
    ):
        maps_here, rows_here, columns, channels = block_input.shape
        pooled_columns = pool_index.shape[2]
        height = rows_here * mesh.shape["rows"]
        half = channels // 2
        band = 2 * rows_here
        pixels = maps_here * band * PAD
        actives = chips // 2
        owners = min(actives, 8)
        piece = half // 2 // owners
        rounds = 2 * LAYERS
        slots = 2 * UNITS * (actives - 1) * piece * half + 4 * rounds * chips * 8 * half
        grant = (36 * 1024 + 256) * 1024 + slots
        vmem, dma = pltpu.VMEM, pltpu.SemaphoreType.DMA
        tile = (maps_here, band + 2, PAD, half)
        edge = (2, maps_here, PAD, half)
        whole = pl.BlockSpec(memory_space=pltpu.VMEM)
        outside = pl.BlockSpec(memory_space=pltpu.HBM)
        index_rows = jnp.transpose(pool_index, (0, 2, 1, 3))
        anywhere = pl.BlockSpec(memory_space=pl.ANY)
        pooled, ig, kg, sums = pl.pallas_call(
            functools.partial(block_kernel, chips, height),
            out_shape=(
                jax.ShapeDtypeStruct((2, maps_here, PAD // 2, half), BF16),
                jax.ShapeDtypeStruct((2, maps_here, rows_here, PAD, half), F32),
                jax.ShapeDtypeStruct((UNITS, channels, channels), BF16),
                jax.ShapeDtypeStruct((2, 8, half), F32),
            ),
            in_specs=[whole, anywhere] + [outside] * 8,
            out_specs=[anywhere] * 4,
            scratch_shapes=[
                vmem(norm_gains.shape, F32),
                vmem(norm_shifts.shape, F32),
                pltpu.SMEM(map_width.shape, jnp.int32),
                pltpu.SMEM(map_group.shape, jnp.int32),
                vmem((maps_here, pooled_columns, channels), jnp.int32),
                pltpu.SMEM(task_mask.shape, jnp.int32),
                pltpu.SMEM(task_weights.shape, F32),
                vmem(task_grads.shape, BF16),
                vmem((LAYERS, 3, 3, half, half), BF16),
                vmem((LAYERS, 3, 3, half, half), BF16),
                vmem((2,) + tile, BF16),
                vmem((2,) + tile, BF16),
                vmem((LAYERS, 2, half, maps_here * (band + 2) * PAD), BF16),
                vmem((2, half, pixels), BF16),
                vmem((LAYERS,) + tile, F32),
                vmem(edge, BF16),
                vmem((LAYERS,) + edge, BF16),
                vmem((maps_here, band, PAD, half), F32),
                vmem(edge, BF16),
                vmem((LAYERS,) + edge, BF16),
                vmem((2,) + tile, BF16),
                vmem((2,) + tile, BF16),
                vmem((LAYERS, maps_here, band, PAD, half), BF16),
                vmem((3, 2, maps_here, band, PAD, half), BF16),
                vmem((3, pixels, half), F32),
                vmem((2, 2, maps_here, PAD // 2, half), F32),
                vmem((4, 2, maps_here, PAD // 2, half), F32),
                vmem((half // 128, PAD, 128), F32),
                vmem((2, maps_here, PAD // 2, half), BF16),
                vmem((rounds, chips, 8, half), F32),
                vmem((rounds, PLANE, 8, half), F32),
                vmem((maps_here, PLANE, 8, half), F32),
                vmem((PLANE, 8, half), F32),
                vmem((2, 8, half), F32),
                vmem((8, half), F32),
                vmem((LAYERS, 8, half), F32),
                vmem((LAYERS, 8, half), F32),
                vmem((2, 8, half), F32),
                vmem((1, 8, half), F32),
                vmem((1, 8, half), F32),
                vmem((8, half), F32),
                vmem((2 * TAPS, half, half), BF16),
                vmem((UNITS, half // 2, half), BF16),
                vmem((2 * TAPS, half // 2, half), BF16),
                vmem((UNITS, actives - 1, piece, half), BF16),
                vmem((UNITS, piece, half), BF16),
                dma((8,)),
                dma((LAYERS, 3)),
                dma((6,)),
                dma((6,)),
                dma((3,)),
                dma((3,)),
                dma((rounds, chips)),
                dma((rounds, chips)),
                dma((rounds, PLANE)),
                dma((rounds, PLANE)),
                dma((LAYERS, 2)),
                dma((LAYERS, 2)),
                dma((LAYERS, 2)),
                dma((LAYERS, 2)),
                dma((LAYERS, maps_here)),
                dma((LAYERS, maps_here)),
                dma((LAYERS, maps_here)),
                dma((LAYERS, maps_here)),
                dma((3,)),
                dma((3,)),
                dma((3,)),
                dma((LAYERS,)),
                dma((LAYERS,)),
                dma((LAYERS, 2, maps_here)),
                dma((LAYERS, maps_here)),
                dma((UNITS,)),
                dma((UNITS,)),
                dma((UNITS,)),
                dma((UNITS,)),
                dma((UNITS, owners)),
                dma((UNITS, actives - 1)),
                dma((UNITS, actives)),
                dma((UNITS, owners)),
                dma((UNITS,)),
                dma((UNITS,)),
                dma((UNITS,)),
                dma((UNITS,)),
                dma((UNITS,)),
                dma((UNITS,)),
                dma((UNITS,)),
                dma((UNITS,)),
                dma((UNITS,)),
            ],
            compiler_params=pltpu.CompilerParams(
                collective_id=0,
                has_side_effects=True,
                vmem_limit_bytes=grant,
            ),
        )(
            block_input,
            conv_weights,
            *(
                pltpu.with_memory_space_constraint(v, pltpu.HBM)
                for v in (
                    norm_gains,
                    norm_shifts,
                    map_width,
                    map_group,
                    index_rows,
                    task_mask,
                    task_weights,
                    task_grads,
                )
            ),
        )
        pooled = jnp.concatenate([pooled[0], pooled[1]], -1)[:, None, :pooled_columns]
        input_grad = jnp.concatenate([ig[0], ig[1]], -1)[:, :, :columns]
        sums = jnp.concatenate([sums[0], sums[1]], -1)
        return (
            pooled,
            input_grad,
            kg.astype(F32).reshape(conv_weights.shape),
            sums[:LAYERS],
            sums[LAYERS : 2 * LAYERS],
        )

    return jax.shard_map(
        per_device,
        mesh=mesh,
        in_specs=(
            P("maps", "rows", None, None),
            P(),
            P(),
            P(),
            P(),
            P(),
            P("maps", "rows", None, None),
            P("maps", None),
            P(),
            P(None, "maps", "rows", None, None),
        ),
        out_specs=(P("maps", "rows", None, None), P("maps", "rows", None, None), P(), P(), P()),
        check_vma=False,
    )
```

```python
import functools

import jax
import jax.numpy as jnp
from jax import lax
from jax.experimental import pallas as pl
from jax.experimental.pallas import tpu as pltpu
from jax.sharding import PartitionSpec as P

MESH = pl.DeviceIdType.MESH
epsilon = 1e-05
PAD = 64
LAYERS = 3
TAPS = 9
UNITS = LAYERS * TAPS
PLANE = 4
LAG = 4
EARLY = 1
FOLD = 2
F32 = jnp.float32
BF16 = jnp.bfloat16


def each(first, last, body):
    if last - first <= 8:
        for k in range(first, last):
            body(k)
    else:
        lax.fori_loop(first, last, lambda k, s: (body(k), s)[1], 0)


def block_kernel(
    chips,
    height,
    x_ref,
    w_ref,
    gain_hbm,
    shift_hbm,
    width_hbm,
    group_hbm,
    index_hbm,
    tmask_hbm,
    tweight_hbm,
    tgrad_hbm,
    pooled_ref,
    ig_ref,
    kg_ref,
    sums_ref,
    gain_ref,
    shift_ref,
    width_ref,
    group_ref,
    index_ref,
    tmask_ref,
    tweight_ref,
    tgrad_ref,
    wa,
    wb,
    act_own,
    act_oth,
    act_t,
    act_b,
    zbuf,
    zs,
    zh,
    dh,
    dhs,
    dhh,
    dz_own,
    dz_oth,
    dzr,
    dzv,
    prod,
    gsrc,
    gbuf,
    hrow,
    pbuf,
    st1,
    st2,
    coef,
    nall,
    inv_t,
    cnt_t,
    avg_t,
    scl_t,
    mean_t,
    tb_t,
    ta_t,
    sums_own,
    terms,
    r2,
    rf,
    r3,
    fin,
    in_sem,
    w_sem,
    x_s,
    x_r,
    g_s,
    g_r,
    st1_s,
    st1_r,
    st2_s,
    st2_r,
    zh_s,
    zh_r,
    dh_s,
    dh_r,
    act_s,
    act_r,
    dz_s,
    dz_r,
    out_s,
    out_r,
    out_l,
    at_s,
    at_r,
    dzr_s,
    dzr_r,
    r2_s,
    r2_r,
    rf_s,
    rf_r,
    r3_s,
    r3_r,
    az_s,
    az_r,
    af_s,
    af_r,
    ab_s,
    ab_r,
    aa_s,
    aa_r,
    ae_s,
    ae_r,
    ap_s,
    ap_r,
    loc_s,
):
    maps_here = x_ref.shape[0]
    columns = x_ref.shape[2]
    half = x_ref.shape[3] // 2
    tasks = tgrad_ref.shape[0]
    pooled_columns = tgrad_ref.shape[3]
    lanes = half // 128
    tiles = [slice(n * 128, (n + 1) * 128) for n in range(lanes)]
    band = 4
    pixels = maps_here * band * PAD
    actives = chips // 2
    owners = min(actives, 8)
    piece = (half // 2) // owners
    m = lax.axis_index("maps")
    r = lax.axis_index("rows")
    c = lax.rem(r, 2)
    z = lax.div(r, 2)
    other = 1 - c
    first_map = m * maps_here
    x_bit = lax.rem(m, 2)
    y_bit = lax.div(m, 2)
    x_peer = m + 1 - 2 * x_bit
    y_peer = m + 2 - 4 * y_bit
    g_bit = (1 - c) * x_bit + c * y_bit
    h_bit = (1 - c) * y_bit + c * x_bit
    g_peer = (1 - c) * x_peer + c * y_peer
    h_peer = (1 - c) * y_peer + c * x_peer
    pair = lax.div(z, 2)
    turn = lax.rem(pair, 2)
    active_z = 2 * pair + 1 - turn
    is_active = z == active_z
    is_passive = z != active_z
    is_owner = jnp.logical_and(is_active, pair < owners)
    role = jnp.where(is_active, 0, 1)
    up_there = z > 0
    down_there = z < chips - 1
    row8 = lax.broadcasted_iota(jnp.int32, (8, half), 0)
    column = lax.broadcasted_iota(jnp.int32, (PAD, half), 0)

    def remote(src, dst, send, recv, mm, zz, cc):
        return pltpu.make_async_remote_copy(
            src_ref=src,
            dst_ref=dst,
            send_sem=send,
            recv_sem=recv,
            device_id=(mm, zz * 2 + cc),
            device_id_type=MESH,
        )

    def own_half(v):
        return jnp.where(c == 0, v[..., :half], v[..., half:])

    def width_of(a):
        return width_ref[first_map + a]

    own_at = pl.ds(pl.multiple_of(c * half, half), half)
    oth_at = pl.ds(pl.multiple_of(other * half, half), half)

    def weight_copy(l, n):
        dst = (wa, wb, wb)[n]
        k_at, o_at = ((own_at, own_at), (oth_at, own_at), (own_at, oth_at))[n]
        return pltpu.make_async_copy(w_ref.at[l, :, :, k_at, o_at], dst.at[l], w_sem.at[l, n])

    fetches = [
        pltpu.make_async_copy(src, dst, in_sem.at[n])
        for n, (src, dst) in enumerate(
            (
                (width_hbm, width_ref),
                (group_hbm, group_ref),
                (tmask_hbm, tmask_ref),
                (tweight_hbm, tweight_ref),
                (gain_hbm, gain_ref),
                (shift_hbm, shift_ref),
                (index_hbm.at[:, :, 0, :], index_ref),
                (tgrad_hbm, tgrad_ref),
            )
        )
    ]
    for fetch in fetches:
        fetch.start()
    for l in range(LAYERS):
        weight_copy(l, 0).start()
        weight_copy(l, 1).start()

    barrier = pltpu.get_barrier_semaphore()

    def greet(k):
        rr = lax.rem(r + k, 2 * chips)
        pl.semaphore_signal(barrier, inc=1, device_id=(m, rr), device_id_type=MESH)

    each(1, 2 * chips, greet)
    for k in range(1, PLANE):
        for core in (c, other):
            there = (lax.rem(m + k, PLANE), z * 2 + core)
            pl.semaphore_signal(barrier, inc=1, device_id=there, device_id_type=MESH)

    for fetch in fetches:
        fetch.wait()

    mine = pl.ds(1 + 2 * c, 2)
    for a in range(maps_here):
        inside = lax.broadcasted_iota(jnp.int32, (columns, 2 * half), 0) < width_of(a)
        for rr in range(2):
            v = jnp.where(inside, x_ref[a, rr].astype(F32), 0.0).astype(BF16)
            spot = 1 + 2 * c + rr
            act_own[0, a, spot, pl.ds(48, 16), :] = jnp.zeros((16, half), BF16)
            act_oth[0, a, spot, pl.ds(48, 16), :] = jnp.zeros((16, half), BF16)
            act_own[0, a, spot, pl.ds(0, columns), :] = own_half(v)
            act_oth[0, a, spot, pl.ds(0, columns), :] = jnp.where(
                c == 0, v[:, half:], v[:, :half]
            )

    @pl.when(z == 0)
    def _():
        act_own[0, :, 0] = jnp.zeros((maps_here, PAD, half), BF16)
        act_oth[0, :, 0] = jnp.zeros((maps_here, PAD, half), BF16)

    @pl.when(z == chips - 1)
    def _():
        act_own[0, :, 5] = jnp.zeros((maps_here, PAD, half), BF16)
        act_oth[0, :, 5] = jnp.zeros((maps_here, PAD, half), BF16)

    pl.semaphore_wait(barrier, 2 * chips - 1 + 2 * (PLANE - 1))

    x_partner = (
        remote(act_own.at[0, :, mine], act_oth.at[0, :, mine], x_s.at[0], x_r.at[0], m, z, other),
        remote(act_oth.at[0, :, mine], act_own.at[0, :, mine], x_s.at[1], x_r.at[1], m, z, other),
    )
    g_partner = remote(gsrc.at[other], gbuf.at[1 + c], g_s.at[0], g_r.at[0], m, z, other)

    def x_halo(n, src_row, dst_row, zz):
        cc = (c, c, other, other, c, other)[n]
        low = dst_row == band + 1
        if n >= 4:
            src, dst = gsrc.at[cc], gbuf.at[3 if low else 0]
            return remote(src, dst, g_s.at[n - 3], g_r.at[1 if low else 2], m, zz, cc)
        src = (act_own, act_oth, act_own, act_oth)[n].at[0, :, src_row]
        dst = (act_own, act_oth, act_oth, act_own)[n].at[0, :, dst_row]
        return remote(src, dst, x_s.at[2 + n], x_r.at[(2 if low else 4) + n % 2], m, zz, cc)

    for copy in x_partner:
        copy.start()

    @pl.when(jnp.logical_and(c == 0, up_there))
    def _():
        for n in range(4):
            x_halo(n, 1, 5, z - 1).start()

    @pl.when(jnp.logical_and(c == 1, down_there))
    def _():
        for n in range(4):
            x_halo(n, 4, 0, z + 1).start()

    gsrc[...] = jnp.zeros(gsrc.shape, F32)
    for a in range(maps_here):
        total = None
        for t in range(tasks):
            scale = tweight_ref[t] * tmask_ref[a, t].astype(F32)
            term = tgrad_ref[t, a, 0].astype(F32) * scale
            total = term if total is None else total + term
        position = index_ref[a].astype(F32)
        for h in range(2):
            gsrc[h, 0, a, pl.ds(0, pooled_columns), :] = total[:, h * half : (h + 1) * half]
            gsrc[h, 1, a, pl.ds(0, pooled_columns), :] = position[:, h * half : (h + 1) * half]
    gbuf[1 + c] = gsrc[c]

    for mm in range(PLANE):
        sizes = jnp.zeros((8, half), F32)
        for b in range(maps_here):
            sizes = jnp.where(
                row8 == b, (width_ref[mm * maps_here + b] * height).astype(F32), sizes
            )
        nall[mm] = sizes
    inside_sizes = jnp.zeros((8, half), F32)
    for b in range(maps_here):
        inside_sizes = jnp.where(row8 == b, (width_of(b) * band).astype(F32), inside_sizes)
    inv_t[0] = inside_sizes
    inv_t[1] = jnp.where(row8 < maps_here, 1.0 / jnp.maximum(inside_sizes, 1.0), 0.0)
    counts = jnp.ones((8, half), F32)
    for a in range(maps_here):
        total = jnp.zeros((1, half), F32)
        for mm in range(PLANE):
            same = jnp.zeros((8, half), F32)
            for b in range(maps_here):
                alike = group_ref[first_map + a] == group_ref[mm * maps_here + b]
                same = jnp.where(row8 == b, jnp.where(alike, 1.0, 0.0), same)
            coef[a, mm] = same
            total = total + jnp.sum(same * nall[mm], 0, keepdims=True)
        counts = jnp.where(row8 == a, total, counts)
    cnt_t[...] = counts

    def z_copy(e, k):
        zz = lax.rem(z + k, chips)
        return remote(st1.at[e, z], st1.at[e, z], st1_s.at[e, k], st1_r.at[e, z], m, zz, c)

    def z_arrival(e, k):
        zz = lax.rem(z + k, chips)
        return remote(st1.at[e, zz], st1.at[e, zz], st1_s.at[e, k], st1_r.at[e, zz], m, zz, c)

    def m_copy(e, k):
        mm = lax.rem(m + k, PLANE)
        return remote(st2.at[e, m], st2.at[e, m], st2_s.at[e, k], st2_r.at[e, m], mm, z, c)

    def m_arrival(e, k):
        mm = lax.rem(m + k, PLANE)
        return remote(st2.at[e, mm], st2.at[e, mm], st2_s.at[e, k], st2_r.at[e, mm], mm, z, c)

    def send_z(e, tile):
        st1[e, z] = tile
        each(1, chips, lambda k: z_copy(e, k).start())

    def wait_z(e):
        each(1, chips, lambda k: z_arrival(e, k).wait_recv())

    def send_m(e, tile):
        st2[e, m] = tile
        each(1, PLANE, lambda k: m_copy(e, k).start())

    def wait_m(e):
        each(1, PLANE, lambda k: m_arrival(e, k).wait_recv())

    def products(source, l, taps, kernel, transposed, fresh):
        starts = [2 - i if transposed else i for i in taps]
        lhs = jnp.concatenate(
            [source[lax.rem(l, 2), :, s : s + band].reshape(pixels, half) for s in starts], 1
        )
        for j in range(3):
            rhs = jnp.concatenate([kernel[l, i, j] for i in taps], 1 if transposed else 0)
            got = lax.dot_general(
                lhs,
                rhs,
                (((1,), (1 if transposed else 0,)), ((), ())),
                preferred_element_type=F32,
            )
            if fresh:
                prod[j] = got
            else:
                prod[j] = prod[j] + got

    def shifted(a, rr, before, behind, n):
        rows = pl.ds(pl.multiple_of((a * band + rr) * PAD, PAD), PAD)
        return (
            prod[1, rows, n]
            + pltpu.roll(prod[before, rows, n], 1, 0)
            + pltpu.roll(prod[behind, rows, n], PAD - 1, 0)
        )

    def row_of(table, l, a):
        return table[l, pl.ds(a, 1), :]

    def gain_of(l):
        return own_half(gain_ref[pl.ds(l, 1), :])

    def shift_of(l):
        return own_half(shift_ref[pl.ds(l, 1), :])

    def limit(a, rr):
        w = width_of(a)
        if rr == 0:
            return jnp.where(up_there, w, 0)
        if rr == band + 1:
            return jnp.where(down_there, w, 0)
        return w

    def z_halo(l, way):
        there = z - 1 + 2 * way
        return remote(zs.at[way], zh.at[l, 1 - way], zh_s.at[l, way], zh_r.at[l, way], m, there, c)

    def dh_halo(l, way):
        there = z - 1 + 2 * way
        return remote(dhs.at[way], dhh.at[l, 1 - way], dh_s.at[l, way], dh_r.at[l, way], m, there, c)

    def start_halo(halo, l):
        @pl.when(up_there)
        def _():
            halo(l, 0).start()

        @pl.when(down_there)
        def _():
            halo(l, 1).start()

    def wait_halo(halo, l):
        @pl.when(up_there)
        def _():
            halo(l, 1).wait_recv()
            halo(l, 0).wait_send()

        @pl.when(down_there)
        def _():
            halo(l, 0).wait_recv()
            halo(l, 1).wait_send()

    def act_copy(l, a):
        slot = lax.rem(l, 2)
        src, dst = act_own.at[slot, a], act_oth.at[slot, a]
        return remote(src, dst, act_s.at[l, a], act_r.at[l, a], m, z, other)

    def at_copy(l):
        return remote(act_t.at[l, 0], act_t.at[l, 1], at_s.at[l], at_r.at[l], g_peer, z, c)

    def dzr_copy(l, a, way):
        src, dst = dz_own.at[lax.rem(l, 2), a, pl.ds(1, band)], dzr.at[l, a]
        peer = (x_peer, y_peer)[way]
        return remote(src, dst, dzr_s.at[l, way, a], dzr_r.at[l, a], peer, z, way)

    def if_wanted(way, body):
        @pl.when((x_bit, y_bit)[way] + c == 1)
        def _():
            body()

    def dz_copy(l, a):
        slot = lax.rem(l, 2)
        src, dst = dz_own.at[slot, a], dz_oth.at[slot, a]
        return remote(src, dst, dz_s.at[l, a], dz_r.at[l, a], m, z, other)

    def send_gradients():
        g_partner.start()

        @pl.when(jnp.logical_and(c == 0, up_there))
        def _():
            for n in range(4, 6):
                x_halo(n, 1, 5, z - 1).start()

        @pl.when(jnp.logical_and(c == 1, down_there))
        def _():
            for n in range(4, 6):
                x_halo(n, 4, 0, z + 1).start()

    def wait_x_halo(first, last):
        @pl.when(up_there)
        def _():
            for n in (0, 1, 4)[first:last]:
                x_halo(n, 4, 0, z - 1).wait_recv()

        @pl.when(down_there)
        def _():
            for n in (0, 1, 4)[first:last]:
                x_halo(n, 1, 5, z + 1).wait_recv()

    def sent_x_halo(first, last):
        @pl.when(jnp.logical_and(c == 0, up_there))
        def _():
            for n in range(first, last):
                x_halo(n, 1, 5, z - 1).wait_send()

        @pl.when(jnp.logical_and(c == 1, down_there))
        def _():
            for n in range(first, last):
                x_halo(n, 4, 0, z + 1).wait_send()

    def forward(l, first):
        weight_copy(l, 0).wait()
        weight_copy(l, 1).wait()
        if first:
            for copy in x_partner:
                copy.wait_recv()
            products(act_own, l, (1,), wa, False, True)
            products(act_oth, l, (1,), wb, False, False)
            wait_x_halo(0, 2)
            products(act_own, l, (0, 2), wa, False, False)
            products(act_oth, l, (0, 2), wb, False, False)
        else:
            products(act_own, l, (0, 1, 2), wa, False, True)
            for a in range(maps_here):
                act_copy(l, a).wait_recv()
            products(act_oth, l, (0, 1, 2), wb, False, False)
        weight_copy(l, 2).start()

        def collect(a, tile):
            inside = column[:, :128] < width_of(a)
            pixels_inside = (width_of(a) * band).astype(F32)
            totals, squares = [], []
            for n in tiles:
                total = jnp.zeros((PAD, 128), F32)
                for rr in range(band):
                    v = shifted(a, rr, 0, 2, n)
                    zbuf[l, a, 1 + rr, :, n] = v
                    total = total + jnp.where(inside, v, 0.0)
                total = jnp.sum(total, 0, keepdims=True)
                mean = total / pixels_inside
                square = jnp.zeros((PAD, 128), F32)
                for rr in range(band):
                    v = jnp.where(inside, zbuf[l, a, 1 + rr, :, n] - mean, 0.0)
                    square = square + v * v
                    if rr in (0, band - 1):
                        zs[rr // (band - 1), a, :, n] = v.astype(BF16)
                totals.append(total)
                squares.append(jnp.sum(square, 0, keepdims=True))
            tile = jnp.where(row8 == a, jnp.concatenate(totals, 1), tile)
            return jnp.where(row8 == a + maps_here, jnp.concatenate(squares, 1), tile)

        tile = lax.fori_loop(0, maps_here, collect, jnp.zeros((8, half), F32))
        send_z(l, tile)
        start_halo(z_halo, l)
        act_t[l, 0] = act_own[lax.rem(l, 2)].reshape(maps_here * (band + 2) * PAD, half).T
        wait_z(l)
        sizes, inverse = inv_t[0], inv_t[1]
        mean_t[0] = st1[l, jnp.maximum(z - 1, 0)] * inverse
        mean_t[1] = st1[l, jnp.minimum(z + 1, chips - 1)] * inverse
        total = st1[l, 0]
        for zz in range(1, chips):
            total = total + st1[l, zz]
        mean = total * inverse * (1.0 / chips)
        square = jnp.zeros((8, half), F32)
        for zz in range(chips):
            v = st1[l, zz]
            gap = v * inverse - mean
            square = square + pltpu.roll(v, 8 - maps_here, 0) + sizes * gap * gap
        tile = jnp.where(row8 < maps_here, mean, pltpu.roll(square, maps_here, 0))
        send_m(l, jnp.where(row8 < 2 * maps_here, tile, 0.0))
        wait_m(l)
        at_copy(l).start()
        if first:
            send_gradients()
        averages = jnp.zeros((8, half), F32)
        scalings = jnp.zeros((8, half), F32)
        for a in range(maps_here):
            count = cnt_t[a : a + 1, :]
            average = jnp.zeros((8, half), F32)
            for mm in range(PLANE):
                average = average + coef[a, mm] * nall[mm] * st2[l, mm]
            average = jnp.sum(average, 0, keepdims=True) / count
            variance = jnp.zeros((8, half), F32)
            for mm in range(PLANE):
                v = st2[l, mm]
                gap = v - average
                variance = variance + coef[a, mm] * (
                    pltpu.roll(v, 8 - maps_here, 0) + nall[mm] * gap * gap
                )
            variance = jnp.sum(variance, 0, keepdims=True) / count
            averages = jnp.where(row8 == a, average, averages)
            scalings = jnp.where(row8 == a, lax.rsqrt(variance + epsilon), scalings)
        avg_t[l] = averages
        scl_t[l] = scalings
        wait_halo(z_halo, l)

        def activate(a, s):
            gain, shift = gain_of(l), shift_of(l)
            for n in tiles:
                average = row_of(avg_t, l, a)[:, n]
                factor = row_of(scl_t, l, a)[:, n] * gain[:, n]
                for rr in range(band + 2):
                    if rr in (0, band + 1):
                        way = rr // (band + 1)
                        v = zh[l, way, a, :, n].astype(F32) + row_of(mean_t, way, a)[:, n]
                        zbuf[l, a, rr, :, n] = v
                    else:
                        v = zbuf[l, a, rr, :, n]
                    y = (v - average) * factor + shift[:, n]
                    h = jnp.where(column[:, n] < limit(a, rr), y * jax.nn.sigmoid(y), 0.0)
                    act_own[lax.rem(l + 1, 2), a, rr, :, n] = h.astype(BF16)

            @pl.when(l < LAYERS - 1)
            def _():
                act_copy(l + 1, a).start()

            return s

        if first:
            for copy in x_partner:
                copy.wait_send()
            sent_x_halo(0, 4)
        else:

            @pl.when(l == 2)
            def _():
                for a in range(maps_here):
                    act_copy(1, a).wait_send()

        lax.fori_loop(0, maps_here, activate, 0)

    forward(0, True)
    lax.fori_loop(1, LAYERS, lambda l, s: (forward(l, False), s)[1], 0)
    g_partner.wait_recv()
    wait_x_halo(2, 3)

    def unpool(a, s):
        for rr in range(band + 2):
            slot, lower = (rr + 1) // 2, (rr + 1) % 2
            g = gbuf[slot, 0, a]
            position = gbuf[slot, 1, a]
            for b in range(2):
                v = jnp.where(position == float(2 * lower + b), g, 0.0)
                for n in range(lanes):
                    hrow[n, pl.ds(b, PAD // 2, stride=2), :] = v[:, n * 128 : (n + 1) * 128]
            v = jnp.concatenate([hrow[n] for n in range(lanes)], 1)
            if rr in (0, band + 1):
                dhh[LAYERS - 1, rr // (band + 1), a] = v.astype(BF16)
            else:
                dh[a, rr - 1] = v
        return s

    lax.fori_loop(0, maps_here, unpool, 0)

    def pool():
        def one(a, s):
            for pr in range(2):
                total = jnp.zeros((PAD // 2, half), F32)
                position = gbuf[1 + pr, 1, a]
                for lower in range(2):
                    v = act_own[LAYERS % 2, a, 1 + 2 * pr + lower].astype(F32)
                    for n in range(lanes):
                        hrow[n] = v[:, n * 128 : (n + 1) * 128]
                    for b in range(2):
                        v = jnp.concatenate(
                            [hrow[n, pl.ds(b, PAD // 2, stride=2), :] for n in range(lanes)], 1
                        )
                        total = total + jnp.where(position == float(2 * lower + b), v, 0.0)
                pbuf[pr, a] = total.astype(BF16)
            return s

        lax.fori_loop(0, maps_here, one, 0)

    def second_rows(bit):
        return pl.ds(pl.multiple_of(bit * (half // 2), half // 2), half // 2)

    def piece_rows(p):
        return pl.ds(pl.multiple_of(p * piece, piece), piece)

    def term_slot(q):
        return lax.rem(q, 2 * TAPS)

    def c2(q):
        src = terms.at[term_slot(q), second_rows(1 - h_bit)]
        return remote(src, r2.at[q], r2_s.at[q], r2_r.at[q], h_peer, z, c)

    def z_of(n):
        return 2 * n + 1 - lax.rem(n, 2)

    def cf(q):
        passive_z = 2 * pair + turn
        there = active_z + passive_z - z
        return remote(r2.at[q], rf.at[term_slot(q)], rf_s.at[q], rf_r.at[q], m, there, c)

    def c3(q, p):
        slot = lax.rem(pair - p + actives - 1, actives)
        return remote(
            r2.at[q, piece_rows(p)], r3.at[q, slot], r3_s.at[q, p], r3_r.at[q, slot], m, z_of(p), c
        )

    def others(first, body, limit):
        def one(k):
            n = lax.rem(pair + k, actives)

            @pl.when(n < limit)
            def _():
                body(n)

        each(first, actives, one)

    def unit_of(q):
        k = lax.div(q, TAPS)
        return (LAYERS - 1 - k) * TAPS + (q - k * TAPS)

    def region(q, start, size, lane, lanes):
        start = pl.multiple_of(c * half + start, piece)
        lane = pl.multiple_of(lane, half)
        return kg_ref.at[unit_of(q), pl.ds(start, size), pl.ds(lane, lanes)]

    def cz(q, p, n):
        part = region(q, h_bit * (half // 2) + p * piece, piece, g_bit * half, half)
        return remote(fin.at[q], part, az_s.at[q, n], az_r.at[q, p], m, z_of(n), c)

    def cl(q):
        part = region(q, h_bit * (half // 2) + pair * piece, piece, g_bit * half, half)
        return pltpu.make_async_copy(fin.at[q], part, loc_s.at[q])

    def cu(q):
        passive_z = 2 * pair + turn
        there = active_z + passive_z - z
        part = region(q, h_bit * (half // 2), half // 2, g_bit * half, half)
        return remote(part, part, af_s.at[q], af_r.at[q], m, there, c)

    def cb(q):
        part = region(q, h_bit * (half // 2), half // 2, g_bit * half, half)
        return remote(part, part, ab_s.at[q], ab_r.at[q], h_peer, z, c)

    def ca(q):
        part = region(q, 0, half, g_bit * half, half)
        return remote(part, part, aa_s.at[q], aa_r.at[q], g_peer, z, c)

    def plan(q):
        k = lax.rem(q, 5)
        both = jnp.logical_or(k == 4, q >= UNITS - 2)
        mine = jnp.logical_or(both, lax.rem(k, 2) == role)
        return mine, jnp.logical_and(mine, jnp.logical_not(both)), jnp.logical_not(mine)

    def ce(q):
        passive_z = 2 * pair + turn
        there = active_z + passive_z - z
        part = region(q, 0, half, (1 - g_bit) * half, half)
        return remote(part, part, ae_s.at[q], ae_r.at[q], m, there, c)

    def cp(q):
        part = region(q, 0, half, 0, 2 * half)
        return remote(part, part, ap_s.at[q], ap_r.at[q], m, z, other)

    def ready_terms(l):
        at_copy(l).wait_recv()
        for chip in range(2):
            for a in range(maps_here):
                first = a * (band + 2) * PAD
                rows = act_t[l, chip, :, first : first + (band + 2) * PAD]
                act_b[chip, :, a * band * PAD : (a + 1) * band * PAD] = rows[:, PAD : PAD + band * PAD]
        slot = lax.rem(l, 2)

        def variants(a, s):
            dzr_copy(l, a, 0).wait_recv()
            for chip in range(2):
                for rr in range(band):
                    for n in tiles:
                        if chip == 0:
                            mine, theirs = dz_own[slot, a, 1 + rr, :, n], dz_oth[slot, a, 1 + rr, :, n]
                            v = jnp.where(g_bit == c, mine, theirs)
                        else:
                            v = dzr[l, a, rr, :, n]
                        dzv[1, chip, a, rr, :, n] = v
                        v = v.astype(F32)
                        dzv[0, chip, a, rr, :, n] = pltpu.roll(v, PAD - 1, 0).astype(BF16)
                        dzv[2, chip, a, rr, :, n] = pltpu.roll(v, 1, 0).astype(BF16)
            return s

        lax.fori_loop(0, maps_here, variants, 0)

    def tap_terms(l, i, j):
        if i == 1:
            lhs = [act_b[0], act_b[1]]
        else:
            lhs = []
            for chip in range(2):
                for a in range(maps_here):
                    first = (a * (band + 2) + i) * PAD
                    lhs.append(act_t[l, chip, :, first : first + band * PAD])
        rhs = dzv[j].reshape(2 * pixels, half)
        q = (LAYERS - 1 - l) * TAPS + 3 * i + j
        got = jnp.dot(jnp.concatenate(lhs, 1), rhs, preferred_element_type=F32)
        terms[term_slot(q)] = got.astype(BF16)

    def weight_terms(l, i):
        lax.fori_loop(0, 3, lambda j, s: (tap_terms(l, i, j), s)[1], 0)

    def stage_second(q):
        c2(q).wait()
        kept = terms[term_slot(q), second_rows(h_bit)].astype(F32)
        r2[q] = (r2[q].astype(F32) + kept).astype(BF16)

        @pl.when(is_passive)
        def _():
            cf(q).start()

    def stage_fold(q):
        @pl.when(is_active)
        def _():
            cf(q).wait_recv()
            r2[q] = (r2[q].astype(F32) + rf[term_slot(q)].astype(F32)).astype(BF16)
            others(1, lambda n: c3(q, n).start(), owners)

    def stage_sum(q):
        @pl.when(is_owner)
        def _():
            for k in range(actives - 1):
                remote(
                    r3.at[q, k], r3.at[q, k], r3_s.at[q, 0], r3_r.at[q, k], m, z, c
                ).wait_recv()
            total = r2[q, piece_rows(pair)].astype(F32)
            for k in range(actives - 1):
                total = total + r3[q, k].astype(F32)
            fin[q] = total.astype(BF16)
            others(1, lambda n: cz(q, pair, n).start(), actives)
            cl(q).start()

    def stage_back(q):
        @pl.when(is_active)
        def _():
            others(1, lambda n: cz(q, n, n).wait_recv(), owners)

        @pl.when(is_owner)
        def _():
            cl(q).wait()

        @pl.when(is_active)
        def _():
            cu(q).start()

        @pl.when(is_passive)
        def _():
            cu(q).wait_recv()

        cb(q).start()

    def stage_first(q):
        cb(q).wait_recv()
        mine, _, _ = plan(q)

        @pl.when(mine)
        def _():
            ca(q).start()

        @pl.when(is_active)
        def _():
            others(1, lambda n: c3(q, n).wait_send(), owners)

        @pl.when(is_passive)
        def _():
            cf(q).wait_send()

    def stage_chip(q):
        mine, for_both, _ = plan(q)

        @pl.when(mine)
        def _():
            ca(q).wait_recv()

        @pl.when(for_both)
        def _():
            ce(q).start()

        @pl.when(mine)
        def _():
            cp(q).start()

        @pl.when(is_owner)
        def _():
            others(1, lambda n: cz(q, pair, n).wait_send(), actives)

        @pl.when(is_active)
        def _():
            cu(q).wait_send()

    def stage_late(q):
        _, _, not_mine = plan(q)

        @pl.when(not_mine)
        def _():
            ce(q).wait_recv()
            cp(q).start()

    def stage_done(q):
        mine, for_both, _ = plan(q)
        cb(q).wait_send()

        @pl.when(mine)
        def _():
            ca(q).wait_send()

        @pl.when(for_both)
        def _():
            ce(q).wait_send()

        cp(q).wait()

    def run(stage, first, last):
        lax.fori_loop(first, last, lambda q, s: (stage(q), s)[1], 0)

    def sent_dz(l):
        for a in range(maps_here):
            dz_copy(l, a).wait_send()
            for way in range(2):
                if_wanted(way, dzr_copy(l, a, way).wait_send)

    def backward(k, carry):
        l = LAYERS - 1 - k
        gain, shift = gain_of(l), shift_of(l)

        def gradient(a, rr, n):
            zhat = (zbuf[l, a, rr, :, n] - row_of(avg_t, l, a)[:, n]) * row_of(scl_t, l, a)[:, n]
            y = zhat * gain[:, n] + shift[:, n]
            s = jax.nn.sigmoid(y)
            if rr in (0, band + 1):
                upstream = dhh[l, rr // (band + 1), a, :, n].astype(F32)
            else:
                upstream = dh[a, rr - 1, :, n]
            dy = upstream * (s * (1.0 + y * (1.0 - s)))
            dy = jnp.where(column[:, n] < limit(a, rr), dy, 0.0)
            return dy, zhat

        def collect(a, tile):
            plains, crosses = [], []
            for n in tiles:
                plain = jnp.zeros((PAD, 128), F32)
                crossed = jnp.zeros((PAD, 128), F32)
                for rr in range(1, band + 1):
                    dy, zhat = gradient(a, rr, n)
                    dh[a, rr - 1, :, n] = dy
                    plain = plain + dy
                    crossed = crossed + dy * zhat
                plains.append(jnp.sum(plain, 0, keepdims=True))
                crosses.append(jnp.sum(crossed, 0, keepdims=True))
            tile = jnp.where(row8 == a, jnp.concatenate(plains, 1), tile)
            return jnp.where(row8 == a + maps_here, jnp.concatenate(crosses, 1), tile)

        e = LAYERS + l
        tile = lax.fori_loop(0, maps_here, collect, jnp.zeros((8, half), F32))
        send_z(e, tile)

        @pl.when(k == LAYERS - 1)
        def _():
            run(stage_second, 0, TAPS)

        @pl.when(k > 0)
        def _():
            ready_terms(l + 1)
            weight_terms(l + 1, 0)

        wait_z(e)
        total = st1[e, 0]
        for zz in range(1, chips):
            total = total + st1[e, zz]
        send_m(e, total)

        @pl.when(k > 0)
        def _():
            first = (LAYERS - 2 - l) * TAPS
            run(lambda q: c2(q).start(), first, first + 3)
            weight_terms(l + 1, 1)
            run(lambda q: c2(q).start(), first + 3, first + 6)
            weight_terms(l + 1, 2)
            run(lambda q: c2(q).start(), first + 6, first + 9)
            wait_halo(dh_halo, l)

        @pl.when(k == 0)
        def _():
            pool()

        wait_m(e)
        total = st2[e, 0]
        for mm in range(1, PLANE):
            total = total + st2[e, mm]
        sums_own[pl.ds(l, 1), :] = jnp.sum(
            jnp.where(row8 >= maps_here, total, 0.0), 0, keepdims=True
        )
        sums_own[pl.ds(LAYERS + l, 1), :] = jnp.sum(
            jnp.where(row8 < maps_here, total, 0.0), 0, keepdims=True
        )
        plains = jnp.zeros((8, half), F32)
        crosses = jnp.zeros((8, half), F32)
        for a in range(maps_here):
            plain = jnp.zeros((8, half), F32)
            crossed = jnp.zeros((8, half), F32)
            for mm in range(PLANE):
                v = st2[e, mm]
                plain = plain + coef[a, mm] * v
                crossed = crossed + coef[a, mm] * pltpu.roll(v, 8 - maps_here, 0)
            count = cnt_t[a : a + 1, :]
            plain = gain * (jnp.sum(plain, 0, keepdims=True) / count)
            crossed = gain * (jnp.sum(crossed, 0, keepdims=True) / count)
            plains = jnp.where(row8 == a, plain, plains)
            crosses = jnp.where(row8 == a, crossed, crosses)
        tb_t[0] = plains
        ta_t[0] = crosses

        def settle(a, s):
            for n in tiles:
                average, scaling = row_of(avg_t, l, a)[:, n], row_of(scl_t, l, a)[:, n]
                plain, crossed = row_of(tb_t, 0, a)[:, n], row_of(ta_t, 0, a)[:, n]
                for rr in range(band + 2):
                    if rr in (0, band + 1):
                        dy, zhat = gradient(a, rr, n)
                    else:
                        dy = dh[a, rr - 1, :, n]
                        zhat = (zbuf[l, a, rr, :, n] - average) * scaling
                    v = scaling * (dy * gain[:, n] - plain - zhat * crossed)
                    v = jnp.where(column[:, n] < limit(a, rr), v, 0.0)
                    dz_own[lax.rem(l, 2), a, rr, :, n] = v.astype(BF16)
            dz_copy(l, a).start()
            for way in range(2):
                if_wanted(way, dzr_copy(l, a, way).start)
            return s

        @pl.when(k == 2)
        def _():
            sent_dz(LAYERS - 1)

        lax.fori_loop(0, maps_here, settle, 0)
        products(dz_own, l, (0, 1, 2), wa, True, True)
        weight_copy(l, 2).wait()
        for a in range(maps_here):
            dz_copy(l, a).wait_recv()
        products(dz_oth, l, (0, 1, 2), wb, True, False)

        def gather(a, s):
            for n in tiles:
                for rr in range(band):
                    v = shifted(a, rr, 2, 0, n)
                    dh[a, rr, :, n] = v
                    if rr in (0, band - 1):
                        dhs[rr // (band - 1), a, :, n] = v.astype(BF16)
            return s

        lax.fori_loop(0, maps_here, gather, 0)

        @pl.when(l > 0)
        def _():
            start_halo(dh_halo, l - 1)

        return carry

    lax.fori_loop(0, LAYERS, backward, 0)
    def input_rows(a, s):
        for rr in range(band):
            dh[a, rr] = jnp.where(column < width_of(a), dh[a, rr], 0.0)
        return s

    lax.fori_loop(0, maps_here, input_rows, 0)

    outs = (
        (
            remote(dh.at[:, pl.ds(2 * other, 2)], ig_ref.at[c], out_s.at[0], out_r.at[0], m, z, other),
            pltpu.make_async_copy(dh.at[:, pl.ds(2 * c, 2)], ig_ref.at[c], out_l.at[0]),
        ),
        (
            remote(pbuf.at[other], pooled_ref.at[c], out_s.at[1], out_r.at[1], m, z, other),
            pltpu.make_async_copy(pbuf.at[c], pooled_ref.at[c], out_l.at[1]),
        ),
        (
            remote(sums_own, sums_ref.at[c], out_s.at[2], out_r.at[2], m, z, other),
            pltpu.make_async_copy(sums_own, sums_ref.at[c], out_l.at[2]),
        ),
    )
    for there, here in outs:
        there.start()
        here.start()

    g_partner.wait_send()
    sent_x_halo(4, 6)

    def sent(e, carry):
        each(1, chips, lambda k: z_copy(e, k).wait_send())
        each(1, PLANE, lambda k: m_copy(e, k).wait_send())
        return carry

    lax.fori_loop(0, 2 * LAYERS, sent, 0)
    for l in range(LAYERS):
        at_copy(l).wait_send()
    for l in range(LAYERS - 1):
        sent_dz(l)

    def drain(s, carry):
        @pl.when(s == EARLY)
        def _():
            ready_terms(0)

        for i in range(3):
            j = s - EARLY - 3 * i

            @pl.when(jnp.logical_and(j >= 0, j < 3))
            def _(i=i, j=j):
                tap_terms(0, i, j)
                c2(2 * TAPS + 3 * i + j).start()

        for stage, first, lag in (
            (stage_done, 0, 2 * FOLD + 4 * LAG),
            (stage_late, 0, 2 * FOLD + 3 * LAG),
            (stage_chip, 0, 2 * FOLD + 2 * LAG),
            (stage_first, 0, 2 * FOLD + LAG),
            (stage_back, 0, 2 * FOLD),
            (stage_sum, 0, FOLD),
            (stage_fold, 0, 0),
            (stage_second, TAPS, 0),
        ):
            q = first + s - lag

            @pl.when(jnp.logical_and(q >= first, q < UNITS))
            def _(stage=stage, q=q):
                stage(q)

        return carry

    lax.fori_loop(0, UNITS + 2 * FOLD + 4 * LAG, drain, 0)
    for a in range(maps_here):
        act_copy(2, a).wait_send()
    for there, here in outs:
        there.wait()
        here.wait()


def solution(mesh):
    chips = mesh.shape["rows"] // 2

    def per_device(
        block_input,
        conv_weights,
        norm_gains,
        norm_shifts,
        map_width,
        map_group,
        pool_index,
        task_mask,
        task_weights,
        task_grads,
    ):
        maps_here, rows_here, columns, channels = block_input.shape
        pooled_columns = pool_index.shape[2]
        height = rows_here * mesh.shape["rows"]
        half = channels // 2
        band = 2 * rows_here
        pixels = maps_here * band * PAD
        actives = chips // 2
        owners = min(actives, 8)
        piece = half // 2 // owners
        rounds = 2 * LAYERS
        slots = 2 * UNITS * (actives - 1) * piece * half + 4 * rounds * chips * 8 * half
        grant = (36 * 1024 + 256) * 1024 + slots
        vmem, dma = pltpu.VMEM, pltpu.SemaphoreType.DMA
        tile = (maps_here, band + 2, PAD, half)
        edge = (2, maps_here, PAD, half)
        whole = pl.BlockSpec(memory_space=pltpu.VMEM)
        outside = pl.BlockSpec(memory_space=pltpu.HBM)
        index_rows = jnp.transpose(pool_index, (0, 2, 1, 3))
        anywhere = pl.BlockSpec(memory_space=pl.ANY)
        pooled, ig, kg, sums = pl.pallas_call(
            functools.partial(block_kernel, chips, height),
            out_shape=(
                jax.ShapeDtypeStruct((2, maps_here, PAD // 2, half), BF16),
                jax.ShapeDtypeStruct((2, maps_here, rows_here, PAD, half), F32),
                jax.ShapeDtypeStruct((UNITS, channels, channels), BF16),
                jax.ShapeDtypeStruct((2, 8, half), F32),
            ),
            in_specs=[whole, anywhere] + [outside] * 8,
            out_specs=[anywhere] * 4,
            scratch_shapes=[
                vmem(norm_gains.shape, F32),
                vmem(norm_shifts.shape, F32),
                pltpu.SMEM(map_width.shape, jnp.int32),
                pltpu.SMEM(map_group.shape, jnp.int32),
                vmem((maps_here, pooled_columns, channels), jnp.int32),
                pltpu.SMEM(task_mask.shape, jnp.int32),
                pltpu.SMEM(task_weights.shape, F32),
                vmem(task_grads.shape, BF16),
                vmem((LAYERS, 3, 3, half, half), BF16),
                vmem((LAYERS, 3, 3, half, half), BF16),
                vmem((2,) + tile, BF16),
                vmem((2,) + tile, BF16),
                vmem((LAYERS, 2, half, maps_here * (band + 2) * PAD), BF16),
                vmem((2, half, pixels), BF16),
                vmem((LAYERS,) + tile, F32),
                vmem(edge, BF16),
                vmem((LAYERS,) + edge, BF16),
                vmem((maps_here, band, PAD, half), F32),
                vmem(edge, BF16),
                vmem((LAYERS,) + edge, BF16),
                vmem((2,) + tile, BF16),
                vmem((2,) + tile, BF16),
                vmem((LAYERS, maps_here, band, PAD, half), BF16),
                vmem((3, 2, maps_here, band, PAD, half), BF16),
                vmem((3, pixels, half), F32),
                vmem((2, 2, maps_here, PAD // 2, half), F32),
                vmem((4, 2, maps_here, PAD // 2, half), F32),
                vmem((half // 128, PAD, 128), F32),
                vmem((2, maps_here, PAD // 2, half), BF16),
                vmem((rounds, chips, 8, half), F32),
                vmem((rounds, PLANE, 8, half), F32),
                vmem((maps_here, PLANE, 8, half), F32),
                vmem((PLANE, 8, half), F32),
                vmem((2, 8, half), F32),
                vmem((8, half), F32),
                vmem((LAYERS, 8, half), F32),
                vmem((LAYERS, 8, half), F32),
                vmem((2, 8, half), F32),
                vmem((1, 8, half), F32),
                vmem((1, 8, half), F32),
                vmem((8, half), F32),
                vmem((2 * TAPS, half, half), BF16),
                vmem((UNITS, half // 2, half), BF16),
                vmem((2 * TAPS, half // 2, half), BF16),
                vmem((UNITS, actives - 1, piece, half), BF16),
                vmem((UNITS, piece, half), BF16),
                dma((8,)),
                dma((LAYERS, 3)),
                dma((6,)),
                dma((6,)),
                dma((3,)),
                dma((3,)),
                dma((rounds, chips)),
                dma((rounds, chips)),
                dma((rounds, PLANE)),
                dma((rounds, PLANE)),
                dma((LAYERS, 2)),
                dma((LAYERS, 2)),
                dma((LAYERS, 2)),
                dma((LAYERS, 2)),
                dma((LAYERS, maps_here)),
                dma((LAYERS, maps_here)),
                dma((LAYERS, maps_here)),
                dma((LAYERS, maps_here)),
                dma((3,)),
                dma((3,)),
                dma((3,)),
                dma((LAYERS,)),
                dma((LAYERS,)),
                dma((LAYERS, 2, maps_here)),
                dma((LAYERS, maps_here)),
                dma((UNITS,)),
                dma((UNITS,)),
                dma((UNITS,)),
                dma((UNITS,)),
                dma((UNITS, owners)),
                dma((UNITS, actives - 1)),
                dma((UNITS, actives)),
                dma((UNITS, owners)),
                dma((UNITS,)),
                dma((UNITS,)),
                dma((UNITS,)),
                dma((UNITS,)),
                dma((UNITS,)),
                dma((UNITS,)),
                dma((UNITS,)),
                dma((UNITS,)),
                dma((UNITS,)),
                dma((UNITS,)),
                dma((UNITS,)),
            ],
            compiler_params=pltpu.CompilerParams(
                collective_id=0,
                has_side_effects=True,
                vmem_limit_bytes=grant,
            ),
        )(
            block_input,
            conv_weights,
            *(
                pltpu.with_memory_space_constraint(v, pltpu.HBM)
                for v in (
                    norm_gains,
                    norm_shifts,
                    map_width,
                    map_group,
                    index_rows,
                    task_mask,
                    task_weights,
                    task_grads,
                )
            ),
        )
        pooled = jnp.concatenate([pooled[0], pooled[1]], -1)[:, None, :pooled_columns]
        input_grad = jnp.concatenate([ig[0], ig[1]], -1)[:, :, :columns]
        sums = jnp.concatenate([sums[0], sums[1]], -1)
        return (
            pooled,
            input_grad,
            kg.astype(F32).reshape(conv_weights.shape),
            sums[:LAYERS],
            sums[LAYERS : 2 * LAYERS],
        )

    return jax.shard_map(
        per_device,
        mesh=mesh,
        in_specs=(
            P("maps", "rows", None, None),
            P(),
            P(),
            P(),
            P(),
            P(),
            P("maps", "rows", None, None),
            P("maps", None),
            P(),
            P(None, "maps", "rows", None, None),
        ),
        out_specs=(P("maps", "rows", None, None), P("maps", "rows", None, None), P(), P(), P()),
        check_vma=False,
    )
```

```python
import functools

import jax
import jax.numpy as jnp
from jax import lax
from jax.experimental import pallas as pl
from jax.experimental.pallas import tpu as pltpu
from jax.sharding import PartitionSpec as P

MESH = pl.DeviceIdType.MESH
epsilon = 1e-05
PAD = 64
LAYERS = 3
TAPS = 9
UNITS = LAYERS * TAPS
PLANE = 4
LAG = 4
EARLY = 1
FOLD = 2
F32 = jnp.float32
BF16 = jnp.bfloat16


def each(first, last, body):
    if last - first <= 8:
        for k in range(first, last):
            body(k)
    else:
        lax.fori_loop(first, last, lambda k, s: (body(k), s)[1], 0)


def block_kernel(
    chips,
    height,
    x_ref,
    w_ref,
    gain_hbm,
    shift_hbm,
    width_hbm,
    group_hbm,
    index_hbm,
    tmask_hbm,
    tweight_hbm,
    tgrad_hbm,
    pooled_ref,
    ig_ref,
    kg_ref,
    sums_ref,
    gain_ref,
    shift_ref,
    width_ref,
    group_ref,
    index_ref,
    tmask_ref,
    tweight_ref,
    tgrad_ref,
    wa,
    wb,
    act_own,
    act_oth,
    act_t,
    act_b,
    zbuf,
    zs,
    zh,
    dh,
    dhs,
    dhh,
    dz_own,
    dz_oth,
    dzr,
    dzv,
    prod,
    gsrc,
    gbuf,
    hrow,
    pbuf,
    st1,
    st2,
    coef,
    nall,
    inv_t,
    cnt_t,
    avg_t,
    scl_t,
    mean_t,
    tb_t,
    ta_t,
    sums_own,
    terms,
    r2,
    rf,
    r3,
    fin,
    in_sem,
    w_sem,
    x_s,
    x_r,
    g_s,
    g_r,
    st1_s,
    st1_r,
    st2_s,
    st2_r,
    zh_s,
    zh_r,
    dh_s,
    dh_r,
    act_s,
    act_r,
    dz_s,
    dz_r,
    out_s,
    out_r,
    out_l,
    at_s,
    at_r,
    dzr_s,
    dzr_r,
    r2_s,
    r2_r,
    rf_s,
    rf_r,
    r3_s,
    r3_r,
    az_s,
    az_r,
    af_s,
    af_r,
    ab_s,
    ab_r,
    aa_s,
    aa_r,
    ae_s,
    ae_r,
    ap_s,
    ap_r,
    loc_s,
):
    maps_here = x_ref.shape[0]
    columns = x_ref.shape[2]
    half = x_ref.shape[3] // 2
    tasks = tgrad_ref.shape[0]
    pooled_columns = tgrad_ref.shape[3]
    lanes = half // 128
    tiles = [slice(n * 128, (n + 1) * 128) for n in range(lanes)]
    band = 4
    pixels = maps_here * band * PAD
    actives = chips // 2
    owners = min(actives, 8)
    piece = (half // 2) // owners
    m = lax.axis_index("maps")
    r = lax.axis_index("rows")
    c = lax.rem(r, 2)
    z = lax.div(r, 2)
    other = 1 - c
    first_map = m * maps_here
    x_bit = lax.rem(m, 2)
    y_bit = lax.div(m, 2)
    x_peer = m + 1 - 2 * x_bit
    y_peer = m + 2 - 4 * y_bit
    g_bit = (1 - c) * x_bit + c * y_bit
    h_bit = (1 - c) * y_bit + c * x_bit
    g_peer = (1 - c) * x_peer + c * y_peer
    h_peer = (1 - c) * y_peer + c * x_peer
    pair = lax.div(z, 2)
    turn = lax.rem(pair, 2)
    active_z = 2 * pair + 1 - turn
    is_active = z == active_z
    is_passive = z != active_z
    is_owner = jnp.logical_and(is_active, pair < owners)
    role = jnp.where(is_active, 0, 1)
    up_there = z > 0
    down_there = z < chips - 1
    row8 = lax.broadcasted_iota(jnp.int32, (8, half), 0)
    column = lax.broadcasted_iota(jnp.int32, (PAD, half), 0)

    def remote(src, dst, send, recv, mm, zz, cc):
        return pltpu.make_async_remote_copy(
            src_ref=src,
            dst_ref=dst,
            send_sem=send,
            recv_sem=recv,
            device_id=(mm, zz * 2 + cc),
            device_id_type=MESH,
        )

    def own_half(v):
        return jnp.where(c == 0, v[..., :half], v[..., half:])

    def width_of(a):
        return width_ref[first_map + a]

    own_at = pl.ds(pl.multiple_of(c * half, half), half)
    oth_at = pl.ds(pl.multiple_of(other * half, half), half)

    def weight_copy(l, n):
        dst = (wa, wb, wb)[n]
        k_at, o_at = ((own_at, own_at), (oth_at, own_at), (own_at, oth_at))[n]
        return pltpu.make_async_copy(w_ref.at[l, :, :, k_at, o_at], dst.at[l], w_sem.at[l, n])

    fetches = [
        pltpu.make_async_copy(src, dst, in_sem.at[n])
        for n, (src, dst) in enumerate(
            (
                (width_hbm, width_ref),
                (group_hbm, group_ref),
                (tmask_hbm, tmask_ref),
                (tweight_hbm, tweight_ref),
                (gain_hbm, gain_ref),
                (shift_hbm, shift_ref),
                (index_hbm.at[:, :, 0, :], index_ref),
                (tgrad_hbm, tgrad_ref),
            )
        )
    ]
    for fetch in fetches:
        fetch.start()
    for l in range(LAYERS):
        weight_copy(l, 0).start()
        weight_copy(l, 1).start()

    barrier = pltpu.get_barrier_semaphore()

    def greet(k):
        rr = lax.rem(r + k, 2 * chips)
        pl.semaphore_signal(barrier, inc=1, device_id=(m, rr), device_id_type=MESH)

    each(1, 2 * chips, greet)
    for k in range(1, PLANE):
        for core in (c, other):
            there = (lax.rem(m + k, PLANE), z * 2 + core)
            pl.semaphore_signal(barrier, inc=1, device_id=there, device_id_type=MESH)

    for fetch in fetches:
        fetch.wait()

    mine = pl.ds(1 + 2 * c, 2)
    for a in range(maps_here):
        inside = lax.broadcasted_iota(jnp.int32, (columns, 2 * half), 0) < width_of(a)
        for rr in range(2):
            v = jnp.where(inside, x_ref[a, rr].astype(F32), 0.0).astype(BF16)
            spot = 1 + 2 * c + rr
            act_own[0, a, spot, pl.ds(48, 16), :] = jnp.zeros((16, half), BF16)
            act_oth[0, a, spot, pl.ds(48, 16), :] = jnp.zeros((16, half), BF16)
            act_own[0, a, spot, pl.ds(0, columns), :] = own_half(v)
            act_oth[0, a, spot, pl.ds(0, columns), :] = jnp.where(
                c == 0, v[:, half:], v[:, :half]
            )

    @pl.when(z == 0)
    def _():
        act_own[0, :, 0] = jnp.zeros((maps_here, PAD, half), BF16)
        act_oth[0, :, 0] = jnp.zeros((maps_here, PAD, half), BF16)

    @pl.when(z == chips - 1)
    def _():
        act_own[0, :, 5] = jnp.zeros((maps_here, PAD, half), BF16)
        act_oth[0, :, 5] = jnp.zeros((maps_here, PAD, half), BF16)

    pl.semaphore_wait(barrier, 2 * chips - 1 + 2 * (PLANE - 1))

    x_partner = (
        remote(act_own.at[0, :, mine], act_oth.at[0, :, mine], x_s.at[0], x_r.at[0], m, z, other),
        remote(act_oth.at[0, :, mine], act_own.at[0, :, mine], x_s.at[1], x_r.at[1], m, z, other),
    )
    g_partner = remote(gsrc.at[other], gbuf.at[1 + c], g_s.at[0], g_r.at[0], m, z, other)

    def x_halo(n, src_row, dst_row, zz):
        cc = (c, c, other, other, c, other)[n]
        low = dst_row == band + 1
        if n >= 4:
            src, dst = gsrc.at[cc], gbuf.at[3 if low else 0]
            return remote(src, dst, g_s.at[n - 3], g_r.at[1 if low else 2], m, zz, cc)
        src = (act_own, act_oth, act_own, act_oth)[n].at[0, :, src_row]
        dst = (act_own, act_oth, act_oth, act_own)[n].at[0, :, dst_row]
        return remote(src, dst, x_s.at[2 + n], x_r.at[(2 if low else 4) + n % 2], m, zz, cc)

    for copy in x_partner:
        copy.start()

    @pl.when(jnp.logical_and(c == 0, up_there))
    def _():
        for n in range(4):
            x_halo(n, 1, 5, z - 1).start()

    @pl.when(jnp.logical_and(c == 1, down_there))
    def _():
        for n in range(4):
            x_halo(n, 4, 0, z + 1).start()

    gsrc[...] = jnp.zeros(gsrc.shape, F32)
    for a in range(maps_here):
        total = None
        for t in range(tasks):
            scale = tweight_ref[t] * tmask_ref[a, t].astype(F32)
            term = tgrad_ref[t, a, 0].astype(F32) * scale
            total = term if total is None else total + term
        position = index_ref[a].astype(F32)
        for h in range(2):
            gsrc[h, 0, a, pl.ds(0, pooled_columns), :] = total[:, h * half : (h + 1) * half]
            gsrc[h, 1, a, pl.ds(0, pooled_columns), :] = position[:, h * half : (h + 1) * half]
    gbuf[1 + c] = gsrc[c]

    for mm in range(PLANE):
        sizes = jnp.zeros((8, half), F32)
        for b in range(maps_here):
            sizes = jnp.where(
                row8 == b, (width_ref[mm * maps_here + b] * height).astype(F32), sizes
            )
        nall[mm] = sizes
    inside_sizes = jnp.zeros((8, half), F32)
    for b in range(maps_here):
        inside_sizes = jnp.where(row8 == b, (width_of(b) * band).astype(F32), inside_sizes)
    inv_t[0] = inside_sizes
    inv_t[1] = jnp.where(row8 < maps_here, 1.0 / jnp.maximum(inside_sizes, 1.0), 0.0)
    counts = jnp.ones((8, half), F32)
    for a in range(maps_here):
        total = jnp.zeros((1, half), F32)
        for mm in range(PLANE):
            same = jnp.zeros((8, half), F32)
            for b in range(maps_here):
                alike = group_ref[first_map + a] == group_ref[mm * maps_here + b]
                same = jnp.where(row8 == b, jnp.where(alike, 1.0, 0.0), same)
            coef[a, mm] = same
            total = total + jnp.sum(same * nall[mm], 0, keepdims=True)
        counts = jnp.where(row8 == a, total, counts)
    cnt_t[...] = counts

    def z_copy(e, k):
        zz = lax.rem(z + k, chips)
        return remote(st1.at[e, z], st1.at[e, z], st1_s.at[e, k], st1_r.at[e, z], m, zz, c)

    def z_arrival(e, k):
        zz = lax.rem(z + k, chips)
        return remote(st1.at[e, zz], st1.at[e, zz], st1_s.at[e, k], st1_r.at[e, zz], m, zz, c)

    def m_copy(e, k):
        mm = lax.rem(m + k, PLANE)
        return remote(st2.at[e, m], st2.at[e, m], st2_s.at[e, k], st2_r.at[e, m], mm, z, c)

    def m_arrival(e, k):
        mm = lax.rem(m + k, PLANE)
        return remote(st2.at[e, mm], st2.at[e, mm], st2_s.at[e, k], st2_r.at[e, mm], mm, z, c)

    def send_z(e, tile):
        st1[e, z] = tile
        each(1, chips, lambda k: z_copy(e, k).start())

    def wait_z(e):
        each(1, chips, lambda k: z_arrival(e, k).wait_recv())

    def send_m(e, tile):
        st2[e, m] = tile
        each(1, PLANE, lambda k: m_copy(e, k).start())

    def wait_m(e):
        each(1, PLANE, lambda k: m_arrival(e, k).wait_recv())

    def products(source, l, taps, kernel, transposed, fresh):
        starts = [2 - i if transposed else i for i in taps]
        lhs = jnp.concatenate(
            [source[lax.rem(l, 2), :, s : s + band].reshape(pixels, half) for s in starts], 1
        )
        for j in range(3):
            rhs = jnp.concatenate([kernel[l, i, j] for i in taps], 1 if transposed else 0)
            got = lax.dot_general(
                lhs,
                rhs,
                (((1,), (1 if transposed else 0,)), ((), ())),
                preferred_element_type=F32,
            )
            if fresh:
                prod[j] = got
            else:
                prod[j] = prod[j] + got

    def shifted(a, rr, before, behind, n):
        rows = pl.ds(pl.multiple_of((a * band + rr) * PAD, PAD), PAD)
        return (
            prod[1, rows, n]
            + pltpu.roll(prod[before, rows, n], 1, 0)
            + pltpu.roll(prod[behind, rows, n], PAD - 1, 0)
        )

    def row_of(table, l, a):
        return table[l, pl.ds(a, 1), :]

    def gain_of(l):
        return own_half(gain_ref[pl.ds(l, 1), :])

    def shift_of(l):
        return own_half(shift_ref[pl.ds(l, 1), :])

    def limit(a, rr):
        w = width_of(a)
        if rr == 0:
            return jnp.where(up_there, w, 0)
        if rr == band + 1:
            return jnp.where(down_there, w, 0)
        return w

    def z_halo(l, way):
        there = z - 1 + 2 * way
        return remote(zs.at[way], zh.at[l, 1 - way], zh_s.at[l, way], zh_r.at[l, way], m, there, c)

    def dh_halo(l, way):
        there = z - 1 + 2 * way
        return remote(dhs.at[way], dhh.at[l, 1 - way], dh_s.at[l, way], dh_r.at[l, way], m, there, c)

    def start_halo(halo, l):
        @pl.when(up_there)
        def _():
            halo(l, 0).start()

        @pl.when(down_there)
        def _():
            halo(l, 1).start()

    def wait_halo(halo, l):
        @pl.when(up_there)
        def _():
            halo(l, 1).wait_recv()
            halo(l, 0).wait_send()

        @pl.when(down_there)
        def _():
            halo(l, 0).wait_recv()
            halo(l, 1).wait_send()

    def act_copy(l, a):
        slot = lax.rem(l, 2)
        src, dst = act_own.at[slot, a], act_oth.at[slot, a]
        return remote(src, dst, act_s.at[l, a], act_r.at[l, a], m, z, other)

    def at_copy(l):
        return remote(act_t.at[l, 0], act_t.at[l, 1], at_s.at[l], at_r.at[l], g_peer, z, c)

    def dzr_copy(l, a, way):
        src, dst = dz_own.at[lax.rem(l, 2), a, pl.ds(1, band)], dzr.at[l, a]
        peer = (x_peer, y_peer)[way]
        return remote(src, dst, dzr_s.at[l, way, a], dzr_r.at[l, a], peer, z, way)

    def if_wanted(way, body):
        @pl.when((x_bit, y_bit)[way] + c == 1)
        def _():
            body()

    def dz_copy(l, a):
        slot = lax.rem(l, 2)
        src, dst = dz_own.at[slot, a], dz_oth.at[slot, a]
        return remote(src, dst, dz_s.at[l, a], dz_r.at[l, a], m, z, other)

    def send_gradients():
        g_partner.start()

        @pl.when(jnp.logical_and(c == 0, up_there))
        def _():
            for n in range(4, 6):
                x_halo(n, 1, 5, z - 1).start()

        @pl.when(jnp.logical_and(c == 1, down_there))
        def _():
            for n in range(4, 6):
                x_halo(n, 4, 0, z + 1).start()

    def wait_x_halo(first, last):
        @pl.when(up_there)
        def _():
            for n in (0, 1, 4)[first:last]:
                x_halo(n, 4, 0, z - 1).wait_recv()

        @pl.when(down_there)
        def _():
            for n in (0, 1, 4)[first:last]:
                x_halo(n, 1, 5, z + 1).wait_recv()

    def sent_x_halo(first, last):
        @pl.when(jnp.logical_and(c == 0, up_there))
        def _():
            for n in range(first, last):
                x_halo(n, 1, 5, z - 1).wait_send()

        @pl.when(jnp.logical_and(c == 1, down_there))
        def _():
            for n in range(first, last):
                x_halo(n, 4, 0, z + 1).wait_send()

    def forward(l, first):
        weight_copy(l, 0).wait()
        weight_copy(l, 1).wait()
        if first:
            for copy in x_partner:
                copy.wait_recv()
            products(act_own, l, (1,), wa, False, True)
            products(act_oth, l, (1,), wb, False, False)
            wait_x_halo(0, 2)
            products(act_own, l, (0, 2), wa, False, False)
            products(act_oth, l, (0, 2), wb, False, False)
        else:
            products(act_own, l, (0, 1, 2), wa, False, True)
            for a in range(maps_here):
                act_copy(l, a).wait_recv()
            products(act_oth, l, (0, 1, 2), wb, False, False)
        weight_copy(l, 2).start()

        def collect(a, tile):
            inside = column[:, :128] < width_of(a)
            pixels_inside = (width_of(a) * band).astype(F32)
            totals, squares = [], []
            for n in tiles:
                total = jnp.zeros((PAD, 128), F32)
                for rr in range(band):
                    v = shifted(a, rr, 0, 2, n)
                    zbuf[l, a, 1 + rr, :, n] = v
                    total = total + jnp.where(inside, v, 0.0)
                total = jnp.sum(total, 0, keepdims=True)
                mean = total / pixels_inside
                square = jnp.zeros((PAD, 128), F32)
                for rr in range(band):
                    v = jnp.where(inside, zbuf[l, a, 1 + rr, :, n] - mean, 0.0)
                    square = square + v * v
                    if rr in (0, band - 1):
                        zs[rr // (band - 1), a, :, n] = v.astype(BF16)
                totals.append(total)
                squares.append(jnp.sum(square, 0, keepdims=True))
            tile = jnp.where(row8 == a, jnp.concatenate(totals, 1), tile)
            return jnp.where(row8 == a + maps_here, jnp.concatenate(squares, 1), tile)

        tile = lax.fori_loop(0, maps_here, collect, jnp.zeros((8, half), F32))
        send_z(l, tile)
        start_halo(z_halo, l)
        act_t[l, 0] = act_own[lax.rem(l, 2)].reshape(maps_here * (band + 2) * PAD, half).T
        wait_z(l)
        sizes, inverse = inv_t[0], inv_t[1]
        mean_t[0] = st1[l, jnp.maximum(z - 1, 0)] * inverse
        mean_t[1] = st1[l, jnp.minimum(z + 1, chips - 1)] * inverse
        total = st1[l, 0]
        for zz in range(1, chips):
            total = total + st1[l, zz]
        mean = total * inverse * (1.0 / chips)
        square = jnp.zeros((8, half), F32)
        for zz in range(chips):
            v = st1[l, zz]
            gap = v * inverse - mean
            square = square + pltpu.roll(v, 8 - maps_here, 0) + sizes * gap * gap
        tile = jnp.where(row8 < maps_here, mean, pltpu.roll(square, maps_here, 0))
        send_m(l, jnp.where(row8 < 2 * maps_here, tile, 0.0))
        wait_m(l)
        at_copy(l).start()
        if first:
            send_gradients()
        averages = jnp.zeros((8, half), F32)
        scalings = jnp.zeros((8, half), F32)
        for a in range(maps_here):
            count = cnt_t[a : a + 1, :]
            average = jnp.zeros((8, half), F32)
            for mm in range(PLANE):
                average = average + coef[a, mm] * nall[mm] * st2[l, mm]
            average = jnp.sum(average, 0, keepdims=True) / count
            variance = jnp.zeros((8, half), F32)
            for mm in range(PLANE):
                v = st2[l, mm]
                gap = v - average
                variance = variance + coef[a, mm] * (
                    pltpu.roll(v, 8 - maps_here, 0) + nall[mm] * gap * gap
                )
            variance = jnp.sum(variance, 0, keepdims=True) / count
            averages = jnp.where(row8 == a, average, averages)
            scalings = jnp.where(row8 == a, lax.rsqrt(variance + epsilon), scalings)
        avg_t[l] = averages
        scl_t[l] = scalings
        wait_halo(z_halo, l)

        def activate(a, s):
            gain, shift = gain_of(l), shift_of(l)
            for n in tiles:
                average = row_of(avg_t, l, a)[:, n]
                factor = row_of(scl_t, l, a)[:, n] * gain[:, n]
                for rr in range(band + 2):
                    if rr in (0, band + 1):
                        way = rr // (band + 1)
                        v = zh[l, way, a, :, n].astype(F32) + row_of(mean_t, way, a)[:, n]
                        zbuf[l, a, rr, :, n] = v
                    else:
                        v = zbuf[l, a, rr, :, n]
                    y = (v - average) * factor + shift[:, n]
                    h = jnp.where(column[:, n] < limit(a, rr), y * jax.nn.sigmoid(y), 0.0)
                    act_own[lax.rem(l + 1, 2), a, rr, :, n] = h.astype(BF16)

            @pl.when(l < LAYERS - 1)
            def _():
                act_copy(l + 1, a).start()

            return s

        if first:
            for copy in x_partner:
                copy.wait_send()
            sent_x_halo(0, 4)
        else:

            @pl.when(l == 2)
            def _():
                for a in range(maps_here):
                    act_copy(1, a).wait_send()

        lax.fori_loop(0, maps_here, activate, 0)

    forward(0, True)
    lax.fori_loop(1, LAYERS, lambda l, s: (forward(l, False), s)[1], 0)
    g_partner.wait_recv()
    wait_x_halo(2, 3)

    def unpool(a, s):
        for rr in range(band + 2):
            slot, lower = (rr + 1) // 2, (rr + 1) % 2
            g = gbuf[slot, 0, a]
            position = gbuf[slot, 1, a]
            for b in range(2):
                v = jnp.where(position == float(2 * lower + b), g, 0.0)
                for n in range(lanes):
                    hrow[n, pl.ds(b, PAD // 2, stride=2), :] = v[:, n * 128 : (n + 1) * 128]
            v = jnp.concatenate([hrow[n] for n in range(lanes)], 1)
            if rr in (0, band + 1):
                dhh[LAYERS - 1, rr // (band + 1), a] = v.astype(BF16)
            else:
                dh[a, rr - 1] = v
        return s

    lax.fori_loop(0, maps_here, unpool, 0)

    def pool():
        def one(a, s):
            for pr in range(2):
                total = jnp.zeros((PAD // 2, half), F32)
                position = gbuf[1 + pr, 1, a]
                for lower in range(2):
                    v = act_own[LAYERS % 2, a, 1 + 2 * pr + lower].astype(F32)
                    for n in range(lanes):
                        hrow[n] = v[:, n * 128 : (n + 1) * 128]
                    for b in range(2):
                        v = jnp.concatenate(
                            [hrow[n, pl.ds(b, PAD // 2, stride=2), :] for n in range(lanes)], 1
                        )
                        total = total + jnp.where(position == float(2 * lower + b), v, 0.0)
                pbuf[pr, a] = total.astype(BF16)
            return s

        lax.fori_loop(0, maps_here, one, 0)

    def second_rows(bit):
        return pl.ds(pl.multiple_of(bit * (half // 2), half // 2), half // 2)

    def piece_rows(p):
        return pl.ds(pl.multiple_of(p * piece, piece), piece)

    def term_slot(q):
        return lax.rem(q, 2 * TAPS)

    def c2(q):
        src = terms.at[term_slot(q), second_rows(1 - h_bit)]
        return remote(src, r2.at[q], r2_s.at[q], r2_r.at[q], h_peer, z, c)

    def z_of(n):
        return 2 * n + 1 - lax.rem(n, 2)

    def cf(q):
        passive_z = 2 * pair + turn
        there = active_z + passive_z - z
        return remote(r2.at[q], rf.at[term_slot(q)], rf_s.at[q], rf_r.at[q], m, there, c)

    def c3(q, p):
        slot = lax.rem(pair - p + actives - 1, actives)
        return remote(
            r2.at[q, piece_rows(p)], r3.at[q, slot], r3_s.at[q, p], r3_r.at[q, slot], m, z_of(p), c
        )

    def others(first, body, limit):
        def one(k):
            n = lax.rem(pair + k, actives)

            @pl.when(n < limit)
            def _():
                body(n)

        each(first, actives, one)

    def unit_of(q):
        k = lax.div(q, TAPS)
        return (LAYERS - 1 - k) * TAPS + (q - k * TAPS)

    def region(q, start, size, lane, lanes):
        start = pl.multiple_of(c * half + start, piece)
        lane = pl.multiple_of(lane, half)
        return kg_ref.at[unit_of(q), pl.ds(start, size), pl.ds(lane, lanes)]

    def cz(q, p, n):
        part = region(q, h_bit * (half // 2) + p * piece, piece, g_bit * half, half)
        return remote(fin.at[q], part, az_s.at[q, n], az_r.at[q, p], m, z_of(n), c)

    def cl(q):
        part = region(q, h_bit * (half // 2) + pair * piece, piece, g_bit * half, half)
        return pltpu.make_async_copy(fin.at[q], part, loc_s.at[q])

    def cu(q):
        passive_z = 2 * pair + turn
        there = active_z + passive_z - z
        part = region(q, h_bit * (half // 2), half // 2, g_bit * half, half)
        return remote(part, part, af_s.at[q], af_r.at[q], m, there, c)

    def cb(q):
        part = region(q, h_bit * (half // 2), half // 2, g_bit * half, half)
        return remote(part, part, ab_s.at[q], ab_r.at[q], h_peer, z, c)

    def ca(q):
        part = region(q, 0, half, g_bit * half, half)
        return remote(part, part, aa_s.at[q], aa_r.at[q], g_peer, z, c)

    def plan(q):
        k = lax.rem(q, 5)
        both = jnp.logical_or(lax.rem(k, 2) == 0, q >= UNITS - 5)
        mine = jnp.logical_or(both, lax.div(k, 2) == role)
        return mine, jnp.logical_and(mine, jnp.logical_not(both)), jnp.logical_not(mine)

    def ce(q):
        passive_z = 2 * pair + turn
        there = active_z + passive_z - z
        part = region(q, 0, half, (1 - g_bit) * half, half)
        return remote(part, part, ae_s.at[q], ae_r.at[q], m, there, c)

    def cp_part(q, start, size, lane, lanes):
        part = region(q, start, size, lane, lanes)
        return remote(part, part, ap_s.at[q], ap_r.at[q], m, z, other)

    def cp(q):
        return cp_part(q, 0, half, 0, 2 * half)

    def cp_rows(q, bit):
        return cp_part(q, bit * (half // 2), half // 2, g_bit * half, half)

    def cp_lanes(q):
        return cp_part(q, 0, half, (1 - g_bit) * half, half)

    def ready_terms(l):
        at_copy(l).wait_recv()
        for chip in range(2):
            for a in range(maps_here):
                first = a * (band + 2) * PAD
                rows = act_t[l, chip, :, first : first + (band + 2) * PAD]
                act_b[chip, :, a * band * PAD : (a + 1) * band * PAD] = rows[:, PAD : PAD + band * PAD]
        slot = lax.rem(l, 2)

        def variants(a, s):
            dzr_copy(l, a, 0).wait_recv()
            for chip in range(2):
                for rr in range(band):
                    for n in tiles:
                        if chip == 0:
                            mine, theirs = dz_own[slot, a, 1 + rr, :, n], dz_oth[slot, a, 1 + rr, :, n]
                            v = jnp.where(g_bit == c, mine, theirs)
                        else:
                            v = dzr[l, a, rr, :, n]
                        dzv[1, chip, a, rr, :, n] = v
                        v = v.astype(F32)
                        dzv[0, chip, a, rr, :, n] = pltpu.roll(v, PAD - 1, 0).astype(BF16)
                        dzv[2, chip, a, rr, :, n] = pltpu.roll(v, 1, 0).astype(BF16)
            return s

        lax.fori_loop(0, maps_here, variants, 0)

    def tap_terms(l, i, j):
        if i == 1:
            lhs = [act_b[0], act_b[1]]
        else:
            lhs = []
            for chip in range(2):
                for a in range(maps_here):
                    first = (a * (band + 2) + i) * PAD
                    lhs.append(act_t[l, chip, :, first : first + band * PAD])
        rhs = dzv[j].reshape(2 * pixels, half)
        q = (LAYERS - 1 - l) * TAPS + 3 * i + j
        got = jnp.dot(jnp.concatenate(lhs, 1), rhs, preferred_element_type=F32)
        terms[term_slot(q)] = got.astype(BF16)

    def weight_terms(l, i):
        lax.fori_loop(0, 3, lambda j, s: (tap_terms(l, i, j), s)[1], 0)

    def stage_second(q):
        c2(q).wait()
        kept = terms[term_slot(q), second_rows(h_bit)].astype(F32)
        r2[q] = (r2[q].astype(F32) + kept).astype(BF16)

        @pl.when(is_passive)
        def _():
            cf(q).start()

    def stage_fold(q):
        @pl.when(is_active)
        def _():
            cf(q).wait_recv()
            r2[q] = (r2[q].astype(F32) + rf[term_slot(q)].astype(F32)).astype(BF16)
            others(1, lambda n: c3(q, n).start(), owners)

    def stage_sum(q):
        @pl.when(is_owner)
        def _():
            for k in range(actives - 1):
                remote(
                    r3.at[q, k], r3.at[q, k], r3_s.at[q, 0], r3_r.at[q, k], m, z, c
                ).wait_recv()
            total = r2[q, piece_rows(pair)].astype(F32)
            for k in range(actives - 1):
                total = total + r3[q, k].astype(F32)
            fin[q] = total.astype(BF16)
            others(1, lambda n: cz(q, pair, n).start(), actives)
            cl(q).start()

    def stage_back(q):
        @pl.when(is_active)
        def _():
            others(1, lambda n: cz(q, n, n).wait_recv(), owners)

        @pl.when(is_owner)
        def _():
            cl(q).wait()

        @pl.when(is_active)
        def _():
            cu(q).start()

        @pl.when(is_passive)
        def _():
            cu(q).wait_recv()

        cb(q).start()
        cp_rows(q, h_bit).start()

    def stage_first(q):
        cb(q).wait_recv()
        mine, _, _ = plan(q)

        @pl.when(mine)
        def _():
            ca(q).start()

        cp_rows(q, 1 - h_bit).start()

        @pl.when(is_active)
        def _():
            others(1, lambda n: c3(q, n).wait_send(), owners)

        @pl.when(is_passive)
        def _():
            cf(q).wait_send()

    def stage_chip(q):
        mine, for_both, _ = plan(q)

        @pl.when(mine)
        def _():
            ca(q).wait_recv()

        @pl.when(for_both)
        def _():
            ce(q).start()

        @pl.when(mine)
        def _():
            cp_lanes(q).start()

        @pl.when(is_owner)
        def _():
            others(1, lambda n: cz(q, pair, n).wait_send(), actives)

        @pl.when(is_active)
        def _():
            cu(q).wait_send()

    def stage_late(q):
        _, _, not_mine = plan(q)

        @pl.when(not_mine)
        def _():
            ce(q).wait_recv()
            cp_lanes(q).start()

    def stage_done(q):
        mine, for_both, _ = plan(q)
        cb(q).wait_send()

        @pl.when(mine)
        def _():
            ca(q).wait_send()

        @pl.when(for_both)
        def _():
            ce(q).wait_send()

        cp(q).wait()

    def run(stage, first, last):
        lax.fori_loop(first, last, lambda q, s: (stage(q), s)[1], 0)

    def sent_dz(l):
        for a in range(maps_here):
            dz_copy(l, a).wait_send()
            for way in range(2):
                if_wanted(way, dzr_copy(l, a, way).wait_send)

    def backward(k, carry):
        l = LAYERS - 1 - k
        gain, shift = gain_of(l), shift_of(l)

        def gradient(a, rr, n):
            zhat = (zbuf[l, a, rr, :, n] - row_of(avg_t, l, a)[:, n]) * row_of(scl_t, l, a)[:, n]
            y = zhat * gain[:, n] + shift[:, n]
            s = jax.nn.sigmoid(y)
            if rr in (0, band + 1):
                upstream = dhh[l, rr // (band + 1), a, :, n].astype(F32)
            else:
                upstream = dh[a, rr - 1, :, n]
            dy = upstream * (s * (1.0 + y * (1.0 - s)))
            dy = jnp.where(column[:, n] < limit(a, rr), dy, 0.0)
            return dy, zhat

        def collect(a, tile):
            plains, crosses = [], []
            for n in tiles:
                plain = jnp.zeros((PAD, 128), F32)
                crossed = jnp.zeros((PAD, 128), F32)
                for rr in range(1, band + 1):
                    dy, zhat = gradient(a, rr, n)
                    dh[a, rr - 1, :, n] = dy
                    plain = plain + dy
                    crossed = crossed + dy * zhat
                plains.append(jnp.sum(plain, 0, keepdims=True))
                crosses.append(jnp.sum(crossed, 0, keepdims=True))
            tile = jnp.where(row8 == a, jnp.concatenate(plains, 1), tile)
            return jnp.where(row8 == a + maps_here, jnp.concatenate(crosses, 1), tile)

        e = LAYERS + l
        tile = lax.fori_loop(0, maps_here, collect, jnp.zeros((8, half), F32))
        send_z(e, tile)

        @pl.when(k == LAYERS - 1)
        def _():
            run(stage_second, 0, TAPS)

        @pl.when(k > 0)
        def _():
            ready_terms(l + 1)
            weight_terms(l + 1, 0)

        wait_z(e)
        total = st1[e, 0]
        for zz in range(1, chips):
            total = total + st1[e, zz]
        send_m(e, total)

        @pl.when(k > 0)
        def _():
            first = (LAYERS - 2 - l) * TAPS
            run(lambda q: c2(q).start(), first, first + 3)
            weight_terms(l + 1, 1)
            run(lambda q: c2(q).start(), first + 3, first + 6)
            weight_terms(l + 1, 2)
            run(lambda q: c2(q).start(), first + 6, first + 9)
            wait_halo(dh_halo, l)

        @pl.when(k == 0)
        def _():
            pool()

        wait_m(e)
        total = st2[e, 0]
        for mm in range(1, PLANE):
            total = total + st2[e, mm]
        sums_own[pl.ds(l, 1), :] = jnp.sum(
            jnp.where(row8 >= maps_here, total, 0.0), 0, keepdims=True
        )
        sums_own[pl.ds(LAYERS + l, 1), :] = jnp.sum(
            jnp.where(row8 < maps_here, total, 0.0), 0, keepdims=True
        )
        plains = jnp.zeros((8, half), F32)
        crosses = jnp.zeros((8, half), F32)
        for a in range(maps_here):
            plain = jnp.zeros((8, half), F32)
            crossed = jnp.zeros((8, half), F32)
            for mm in range(PLANE):
                v = st2[e, mm]
                plain = plain + coef[a, mm] * v
                crossed = crossed + coef[a, mm] * pltpu.roll(v, 8 - maps_here, 0)
            count = cnt_t[a : a + 1, :]
            plain = gain * (jnp.sum(plain, 0, keepdims=True) / count)
            crossed = gain * (jnp.sum(crossed, 0, keepdims=True) / count)
            plains = jnp.where(row8 == a, plain, plains)
            crosses = jnp.where(row8 == a, crossed, crosses)
        tb_t[0] = plains
        ta_t[0] = crosses

        def settle(a, s):
            for n in tiles:
                average, scaling = row_of(avg_t, l, a)[:, n], row_of(scl_t, l, a)[:, n]
                plain, crossed = row_of(tb_t, 0, a)[:, n], row_of(ta_t, 0, a)[:, n]
                for rr in range(band + 2):
                    if rr in (0, band + 1):
                        dy, zhat = gradient(a, rr, n)
                    else:
                        dy = dh[a, rr - 1, :, n]
                        zhat = (zbuf[l, a, rr, :, n] - average) * scaling
                    v = scaling * (dy * gain[:, n] - plain - zhat * crossed)
                    v = jnp.where(column[:, n] < limit(a, rr), v, 0.0)
                    dz_own[lax.rem(l, 2), a, rr, :, n] = v.astype(BF16)
            dz_copy(l, a).start()
            for way in range(2):
                if_wanted(way, dzr_copy(l, a, way).start)
            return s

        @pl.when(k == 2)
        def _():
            sent_dz(LAYERS - 1)

        lax.fori_loop(0, maps_here, settle, 0)
        products(dz_own, l, (0, 1, 2), wa, True, True)
        weight_copy(l, 2).wait()
        for a in range(maps_here):
            dz_copy(l, a).wait_recv()
        products(dz_oth, l, (0, 1, 2), wb, True, False)

        def gather(a, s):
            for n in tiles:
                for rr in range(band):
                    v = shifted(a, rr, 2, 0, n)
                    dh[a, rr, :, n] = v
                    if rr in (0, band - 1):
                        dhs[rr // (band - 1), a, :, n] = v.astype(BF16)
            return s

        lax.fori_loop(0, maps_here, gather, 0)

        @pl.when(l > 0)
        def _():
            start_halo(dh_halo, l - 1)

        return carry

    lax.fori_loop(0, LAYERS, backward, 0)
    def input_rows(a, s):
        for rr in range(band):
            dh[a, rr] = jnp.where(column < width_of(a), dh[a, rr], 0.0)
        return s

    lax.fori_loop(0, maps_here, input_rows, 0)

    outs = (
        (
            remote(dh.at[:, pl.ds(2 * other, 2)], ig_ref.at[c], out_s.at[0], out_r.at[0], m, z, other),
            pltpu.make_async_copy(dh.at[:, pl.ds(2 * c, 2)], ig_ref.at[c], out_l.at[0]),
        ),
        (
            remote(pbuf.at[other], pooled_ref.at[c], out_s.at[1], out_r.at[1], m, z, other),
            pltpu.make_async_copy(pbuf.at[c], pooled_ref.at[c], out_l.at[1]),
        ),
        (
            remote(sums_own, sums_ref.at[c], out_s.at[2], out_r.at[2], m, z, other),
            pltpu.make_async_copy(sums_own, sums_ref.at[c], out_l.at[2]),
        ),
    )
    for there, here in outs:
        there.start()
        here.start()

    g_partner.wait_send()
    sent_x_halo(4, 6)

    def sent(e, carry):
        each(1, chips, lambda k: z_copy(e, k).wait_send())
        each(1, PLANE, lambda k: m_copy(e, k).wait_send())
        return carry

    lax.fori_loop(0, 2 * LAYERS, sent, 0)
    for l in range(LAYERS):
        at_copy(l).wait_send()
    for l in range(LAYERS - 1):
        sent_dz(l)

    def drain(s, carry):
        @pl.when(s == EARLY)
        def _():
            ready_terms(0)

        for i in range(3):
            j = s - EARLY - 3 * i

            @pl.when(jnp.logical_and(j >= 0, j < 3))
            def _(i=i, j=j):
                tap_terms(0, i, j)
                c2(2 * TAPS + 3 * i + j).start()

        for stage, first, lag in (
            (stage_done, 0, 2 * FOLD + 4 * LAG),
            (stage_late, 0, 2 * FOLD + 3 * LAG),
            (stage_chip, 0, 2 * FOLD + 2 * LAG),
            (stage_first, 0, 2 * FOLD + LAG),
            (stage_back, 0, 2 * FOLD),
            (stage_sum, 0, FOLD),
            (stage_fold, 0, 0),
            (stage_second, TAPS, 0),
        ):
            q = first + s - lag

            @pl.when(jnp.logical_and(q >= first, q < UNITS))
            def _(stage=stage, q=q):
                stage(q)

        return carry

    lax.fori_loop(0, UNITS + 2 * FOLD + 4 * LAG, drain, 0)
    for a in range(maps_here):
        act_copy(2, a).wait_send()
    for there, here in outs:
        there.wait()
        here.wait()


def solution(mesh):
    chips = mesh.shape["rows"] // 2

    def per_device(
        block_input,
        conv_weights,
        norm_gains,
        norm_shifts,
        map_width,
        map_group,
        pool_index,
        task_mask,
        task_weights,
        task_grads,
    ):
        maps_here, rows_here, columns, channels = block_input.shape
        pooled_columns = pool_index.shape[2]
        height = rows_here * mesh.shape["rows"]
        half = channels // 2
        band = 2 * rows_here
        pixels = maps_here * band * PAD
        actives = chips // 2
        owners = min(actives, 8)
        piece = half // 2 // owners
        rounds = 2 * LAYERS
        slots = 2 * UNITS * (actives - 1) * piece * half + 4 * rounds * chips * 8 * half
        grant = (36 * 1024 + 256) * 1024 + slots
        vmem, dma = pltpu.VMEM, pltpu.SemaphoreType.DMA
        tile = (maps_here, band + 2, PAD, half)
        edge = (2, maps_here, PAD, half)
        whole = pl.BlockSpec(memory_space=pltpu.VMEM)
        outside = pl.BlockSpec(memory_space=pltpu.HBM)
        index_rows = jnp.transpose(pool_index, (0, 2, 1, 3))
        anywhere = pl.BlockSpec(memory_space=pl.ANY)
        pooled, ig, kg, sums = pl.pallas_call(
            functools.partial(block_kernel, chips, height),
            out_shape=(
                jax.ShapeDtypeStruct((2, maps_here, PAD // 2, half), BF16),
                jax.ShapeDtypeStruct((2, maps_here, rows_here, PAD, half), F32),
                jax.ShapeDtypeStruct((UNITS, channels, channels), BF16),
                jax.ShapeDtypeStruct((2, 8, half), F32),
            ),
            in_specs=[whole, anywhere] + [outside] * 8,
            out_specs=[anywhere] * 4,
            scratch_shapes=[
                vmem(norm_gains.shape, F32),
                vmem(norm_shifts.shape, F32),
                pltpu.SMEM(map_width.shape, jnp.int32),
                pltpu.SMEM(map_group.shape, jnp.int32),
                vmem((maps_here, pooled_columns, channels), jnp.int32),
                pltpu.SMEM(task_mask.shape, jnp.int32),
                pltpu.SMEM(task_weights.shape, F32),
                vmem(task_grads.shape, BF16),
                vmem((LAYERS, 3, 3, half, half), BF16),
                vmem((LAYERS, 3, 3, half, half), BF16),
                vmem((2,) + tile, BF16),
                vmem((2,) + tile, BF16),
                vmem((LAYERS, 2, half, maps_here * (band + 2) * PAD), BF16),
                vmem((2, half, pixels), BF16),
                vmem((LAYERS,) + tile, F32),
                vmem(edge, BF16),
                vmem((LAYERS,) + edge, BF16),
                vmem((maps_here, band, PAD, half), F32),
                vmem(edge, BF16),
                vmem((LAYERS,) + edge, BF16),
                vmem((2,) + tile, BF16),
                vmem((2,) + tile, BF16),
                vmem((LAYERS, maps_here, band, PAD, half), BF16),
                vmem((3, 2, maps_here, band, PAD, half), BF16),
                vmem((3, pixels, half), F32),
                vmem((2, 2, maps_here, PAD // 2, half), F32),
                vmem((4, 2, maps_here, PAD // 2, half), F32),
                vmem((half // 128, PAD, 128), F32),
                vmem((2, maps_here, PAD // 2, half), BF16),
                vmem((rounds, chips, 8, half), F32),
                vmem((rounds, PLANE, 8, half), F32),
                vmem((maps_here, PLANE, 8, half), F32),
                vmem((PLANE, 8, half), F32),
                vmem((2, 8, half), F32),
                vmem((8, half), F32),
                vmem((LAYERS, 8, half), F32),
                vmem((LAYERS, 8, half), F32),
                vmem((2, 8, half), F32),
                vmem((1, 8, half), F32),
                vmem((1, 8, half), F32),
                vmem((8, half), F32),
                vmem((2 * TAPS, half, half), BF16),
                vmem((UNITS, half // 2, half), BF16),
                vmem((2 * TAPS, half // 2, half), BF16),
                vmem((UNITS, actives - 1, piece, half), BF16),
                vmem((UNITS, piece, half), BF16),
                dma((8,)),
                dma((LAYERS, 3)),
                dma((6,)),
                dma((6,)),
                dma((3,)),
                dma((3,)),
                dma((rounds, chips)),
                dma((rounds, chips)),
                dma((rounds, PLANE)),
                dma((rounds, PLANE)),
                dma((LAYERS, 2)),
                dma((LAYERS, 2)),
                dma((LAYERS, 2)),
                dma((LAYERS, 2)),
                dma((LAYERS, maps_here)),
                dma((LAYERS, maps_here)),
                dma((LAYERS, maps_here)),
                dma((LAYERS, maps_here)),
                dma((3,)),
                dma((3,)),
                dma((3,)),
                dma((LAYERS,)),
                dma((LAYERS,)),
                dma((LAYERS, 2, maps_here)),
                dma((LAYERS, maps_here)),
                dma((UNITS,)),
                dma((UNITS,)),
                dma((UNITS,)),
                dma((UNITS,)),
                dma((UNITS, owners)),
                dma((UNITS, actives - 1)),
                dma((UNITS, actives)),
                dma((UNITS, owners)),
                dma((UNITS,)),
                dma((UNITS,)),
                dma((UNITS,)),
                dma((UNITS,)),
                dma((UNITS,)),
                dma((UNITS,)),
                dma((UNITS,)),
                dma((UNITS,)),
                dma((UNITS,)),
                dma((UNITS,)),
                dma((UNITS,)),
            ],
            compiler_params=pltpu.CompilerParams(
                collective_id=0,
                has_side_effects=True,
                vmem_limit_bytes=grant,
            ),
        )(
            block_input,
            conv_weights,
            *(
                pltpu.with_memory_space_constraint(v, pltpu.HBM)
                for v in (
                    norm_gains,
                    norm_shifts,
                    map_width,
                    map_group,
                    index_rows,
                    task_mask,
                    task_weights,
                    task_grads,
                )
            ),
        )
        pooled = jnp.concatenate([pooled[0], pooled[1]], -1)[:, None, :pooled_columns]
        input_grad = jnp.concatenate([ig[0], ig[1]], -1)[:, :, :columns]
        sums = jnp.concatenate([sums[0], sums[1]], -1)
        return (
            pooled,
            input_grad,
            kg.astype(F32).reshape(conv_weights.shape),
            sums[:LAYERS],
            sums[LAYERS : 2 * LAYERS],
        )

    return jax.shard_map(
        per_device,
        mesh=mesh,
        in_specs=(
            P("maps", "rows", None, None),
            P(),
            P(),
            P(),
            P(),
            P(),
            P("maps", "rows", None, None),
            P("maps", None),
            P(),
            P(None, "maps", "rows", None, None),
        ),
        out_specs=(P("maps", "rows", None, None), P("maps", "rows", None, None), P(), P(), P()),
        check_vma=False,
    )
```

```python
import functools

import jax
import jax.numpy as jnp
from jax import lax
from jax.experimental import pallas as pl
from jax.experimental.pallas import tpu as pltpu
from jax.sharding import PartitionSpec as P

MESH = pl.DeviceIdType.MESH
epsilon = 1e-05
PAD = 64
LAYERS = 3
TAPS = 9
UNITS = LAYERS * TAPS
PLANE = 4
LAG = 4
EARLY = 1
FOLD = 2
F32 = jnp.float32
BF16 = jnp.bfloat16


def each(first, last, body):
    if last - first <= 8:
        for k in range(first, last):
            body(k)
    else:
        lax.fori_loop(first, last, lambda k, s: (body(k), s)[1], 0)


def block_kernel(
    chips,
    height,
    x_ref,
    w_ref,
    gain_hbm,
    shift_hbm,
    width_hbm,
    group_hbm,
    index_hbm,
    tmask_hbm,
    tweight_hbm,
    tgrad_hbm,
    pooled_ref,
    ig_ref,
    kg_ref,
    sums_ref,
    gain_ref,
    shift_ref,
    width_ref,
    group_ref,
    index_ref,
    tmask_ref,
    tweight_ref,
    tgrad_ref,
    wa,
    wb,
    act_own,
    act_oth,
    act_t,
    act_b,
    zbuf,
    zs,
    zh,
    dh,
    dhs,
    dhh,
    dz_own,
    dz_oth,
    dzr,
    dzv,
    prod,
    gsrc,
    gbuf,
    hrow,
    pbuf,
    st1,
    st2,
    coef,
    nall,
    inv_t,
    cnt_t,
    avg_t,
    scl_t,
    mean_t,
    tb_t,
    ta_t,
    sums_own,
    terms,
    r2,
    rf,
    r3,
    fin,
    in_sem,
    w_sem,
    x_s,
    x_r,
    g_s,
    g_r,
    st1_s,
    st1_r,
    st2_s,
    st2_r,
    zh_s,
    zh_r,
    dh_s,
    dh_r,
    act_s,
    act_r,
    dz_s,
    dz_r,
    out_s,
    out_r,
    out_l,
    at_s,
    at_r,
    dzr_s,
    dzr_r,
    r2_s,
    r2_r,
    rf_s,
    rf_r,
    r3_s,
    r3_r,
    az_s,
    az_r,
    af_s,
    af_r,
    ab_s,
    ab_r,
    aa_s,
    aa_r,
    ae_s,
    ae_r,
    ap_s,
    ap_r,
    loc_s,
):
    maps_here = x_ref.shape[0]
    columns = x_ref.shape[2]
    half = x_ref.shape[3] // 2
    tasks = tgrad_ref.shape[0]
    pooled_columns = tgrad_ref.shape[3]
    lanes = half // 128
    tiles = [slice(n * 128, (n + 1) * 128) for n in range(lanes)]
    band = 4
    pixels = maps_here * band * PAD
    actives = chips // 2
    owners = min(actives, 8)
    piece = (half // 2) // owners
    m = lax.axis_index("maps")
    r = lax.axis_index("rows")
    c = lax.rem(r, 2)
    z = lax.div(r, 2)
    other = 1 - c
    first_map = m * maps_here
    x_bit = lax.rem(m, 2)
    y_bit = lax.div(m, 2)
    x_peer = m + 1 - 2 * x_bit
    y_peer = m + 2 - 4 * y_bit
    g_bit = (1 - c) * x_bit + c * y_bit
    h_bit = (1 - c) * y_bit + c * x_bit
    g_peer = (1 - c) * x_peer + c * y_peer
    h_peer = (1 - c) * y_peer + c * x_peer
    pair = lax.div(z, 2)
    turn = lax.rem(pair, 2)
    active_z = 2 * pair + 1 - turn
    is_active = z == active_z
    is_passive = z != active_z
    is_owner = jnp.logical_and(is_active, pair < owners)
    role = jnp.where(is_active, 0, 1)
    up_there = z > 0
    down_there = z < chips - 1
    row8 = lax.broadcasted_iota(jnp.int32, (8, half), 0)
    column = lax.broadcasted_iota(jnp.int32, (PAD, half), 0)

    def remote(src, dst, send, recv, mm, zz, cc):
        return pltpu.make_async_remote_copy(
            src_ref=src,
            dst_ref=dst,
            send_sem=send,
            recv_sem=recv,
            device_id=(mm, zz * 2 + cc),
            device_id_type=MESH,
        )

    def own_half(v):
        return jnp.where(c == 0, v[..., :half], v[..., half:])

    def width_of(a):
        return width_ref[first_map + a]

    own_at = pl.ds(pl.multiple_of(c * half, half), half)
    oth_at = pl.ds(pl.multiple_of(other * half, half), half)

    def weight_copy(l, n):
        dst = (wa, wb, wb)[n]
        k_at, o_at = ((own_at, own_at), (oth_at, own_at), (own_at, oth_at))[n]
        return pltpu.make_async_copy(w_ref.at[l, :, :, k_at, o_at], dst.at[l], w_sem.at[l, n])

    fetches = [
        pltpu.make_async_copy(src, dst, in_sem.at[n])
        for n, (src, dst) in enumerate(
            (
                (width_hbm, width_ref),
                (group_hbm, group_ref),
                (tmask_hbm, tmask_ref),
                (tweight_hbm, tweight_ref),
                (gain_hbm, gain_ref),
                (shift_hbm, shift_ref),
                (index_hbm.at[:, :, 0, :], index_ref),
                (tgrad_hbm, tgrad_ref),
            )
        )
    ]
    for fetch in fetches:
        fetch.start()
    for l in range(LAYERS):
        weight_copy(l, 0).start()
        weight_copy(l, 1).start()

    barrier = pltpu.get_barrier_semaphore()

    def greet(k):
        rr = lax.rem(r + k, 2 * chips)
        pl.semaphore_signal(barrier, inc=1, device_id=(m, rr), device_id_type=MESH)

    each(1, 2 * chips, greet)
    for k in range(1, PLANE):
        for core in (c, other):
            there = (lax.rem(m + k, PLANE), z * 2 + core)
            pl.semaphore_signal(barrier, inc=1, device_id=there, device_id_type=MESH)

    for fetch in fetches:
        fetch.wait()

    mine = pl.ds(1 + 2 * c, 2)
    for a in range(maps_here):
        inside = lax.broadcasted_iota(jnp.int32, (columns, 2 * half), 0) < width_of(a)
        for rr in range(2):
            v = jnp.where(inside, x_ref[a, rr].astype(F32), 0.0).astype(BF16)
            spot = 1 + 2 * c + rr
            act_own[0, a, spot, pl.ds(48, 16), :] = jnp.zeros((16, half), BF16)
            act_oth[0, a, spot, pl.ds(48, 16), :] = jnp.zeros((16, half), BF16)
            act_own[0, a, spot, pl.ds(0, columns), :] = own_half(v)
            act_oth[0, a, spot, pl.ds(0, columns), :] = jnp.where(
                c == 0, v[:, half:], v[:, :half]
            )

    @pl.when(z == 0)
    def _():
        act_own[0, :, 0] = jnp.zeros((maps_here, PAD, half), BF16)
        act_oth[0, :, 0] = jnp.zeros((maps_here, PAD, half), BF16)

    @pl.when(z == chips - 1)
    def _():
        act_own[0, :, 5] = jnp.zeros((maps_here, PAD, half), BF16)
        act_oth[0, :, 5] = jnp.zeros((maps_here, PAD, half), BF16)

    pl.semaphore_wait(barrier, 2 * chips - 1 + 2 * (PLANE - 1))

    x_partner = (
        remote(act_own.at[0, :, mine], act_oth.at[0, :, mine], x_s.at[0], x_r.at[0], m, z, other),
        remote(act_oth.at[0, :, mine], act_own.at[0, :, mine], x_s.at[1], x_r.at[1], m, z, other),
    )
    g_partner = remote(gsrc.at[other], gbuf.at[1 + c], g_s.at[0], g_r.at[0], m, z, other)

    def x_halo(n, src_row, dst_row, zz):
        cc = (c, other)[n % 2]
        low = dst_row == band + 1
        if n >= 2:
            src, dst = gsrc.at[cc], gbuf.at[3 if low else 0]
            return remote(src, dst, g_s.at[n - 1], g_r.at[1 if low else 2], m, zz, cc)
        src, dst = (act_own, act_oth)[n].at[0, :, src_row], act_own.at[0, :, dst_row]
        return remote(src, dst, x_s.at[2 + n], x_r.at[2 if low else 3], m, zz, cc)

    def x_pass(row):
        n = 4 if row == 0 else 5
        src, dst = act_own.at[0, :, row], act_oth.at[0, :, row]
        return remote(src, dst, x_s.at[n], x_r.at[n], m, z, other)

    for copy in x_partner:
        copy.start()

    @pl.when(jnp.logical_and(c == 0, up_there))
    def _():
        for n in range(2):
            x_halo(n, 1, 5, z - 1).start()

    @pl.when(jnp.logical_and(c == 1, down_there))
    def _():
        for n in range(2):
            x_halo(n, 4, 0, z + 1).start()

    gsrc[...] = jnp.zeros(gsrc.shape, F32)
    for a in range(maps_here):
        total = None
        for t in range(tasks):
            scale = tweight_ref[t] * tmask_ref[a, t].astype(F32)
            term = tgrad_ref[t, a, 0].astype(F32) * scale
            total = term if total is None else total + term
        position = index_ref[a].astype(F32)
        for h in range(2):
            gsrc[h, 0, a, pl.ds(0, pooled_columns), :] = total[:, h * half : (h + 1) * half]
            gsrc[h, 1, a, pl.ds(0, pooled_columns), :] = position[:, h * half : (h + 1) * half]
    gbuf[1 + c] = gsrc[c]

    for mm in range(PLANE):
        sizes = jnp.zeros((8, half), F32)
        for b in range(maps_here):
            sizes = jnp.where(
                row8 == b, (width_ref[mm * maps_here + b] * height).astype(F32), sizes
            )
        nall[mm] = sizes
    inside_sizes = jnp.zeros((8, half), F32)
    for b in range(maps_here):
        inside_sizes = jnp.where(row8 == b, (width_of(b) * band).astype(F32), inside_sizes)
    inv_t[0] = inside_sizes
    inv_t[1] = jnp.where(row8 < maps_here, 1.0 / jnp.maximum(inside_sizes, 1.0), 0.0)
    counts = jnp.ones((8, half), F32)
    for a in range(maps_here):
        total = jnp.zeros((1, half), F32)
        for mm in range(PLANE):
            same = jnp.zeros((8, half), F32)
            for b in range(maps_here):
                alike = group_ref[first_map + a] == group_ref[mm * maps_here + b]
                same = jnp.where(row8 == b, jnp.where(alike, 1.0, 0.0), same)
            coef[a, mm] = same
            total = total + jnp.sum(same * nall[mm], 0, keepdims=True)
        counts = jnp.where(row8 == a, total, counts)
    cnt_t[...] = counts

    def z_copy(e, k):
        zz = lax.rem(z + k, chips)
        return remote(st1.at[e, z], st1.at[e, z], st1_s.at[e, k], st1_r.at[e, z], m, zz, c)

    def z_arrival(e, k):
        zz = lax.rem(z + k, chips)
        return remote(st1.at[e, zz], st1.at[e, zz], st1_s.at[e, k], st1_r.at[e, zz], m, zz, c)

    def m_copy(e, k):
        mm = lax.rem(m + k, PLANE)
        return remote(st2.at[e, m], st2.at[e, m], st2_s.at[e, k], st2_r.at[e, m], mm, z, c)

    def m_arrival(e, k):
        mm = lax.rem(m + k, PLANE)
        return remote(st2.at[e, mm], st2.at[e, mm], st2_s.at[e, k], st2_r.at[e, mm], mm, z, c)

    def send_z(e, tile):
        st1[e, z] = tile
        each(1, chips, lambda k: z_copy(e, k).start())

    def wait_z(e):
        each(1, chips, lambda k: z_arrival(e, k).wait_recv())

    def send_m(e, tile):
        st2[e, m] = tile
        each(1, PLANE, lambda k: m_copy(e, k).start())

    def wait_m(e):
        each(1, PLANE, lambda k: m_arrival(e, k).wait_recv())

    def products(source, l, taps, kernel, transposed, fresh):
        starts = [2 - i if transposed else i for i in taps]
        lhs = jnp.concatenate(
            [source[lax.rem(l, 2), :, s : s + band].reshape(pixels, half) for s in starts], 1
        )
        for j in range(3):
            rhs = jnp.concatenate([kernel[l, i, j] for i in taps], 1 if transposed else 0)
            got = lax.dot_general(
                lhs,
                rhs,
                (((1,), (1 if transposed else 0,)), ((), ())),
                preferred_element_type=F32,
            )
            if fresh:
                prod[j] = got
            else:
                prod[j] = prod[j] + got

    def shifted(a, rr, before, behind, n):
        rows = pl.ds(pl.multiple_of((a * band + rr) * PAD, PAD), PAD)
        return (
            prod[1, rows, n]
            + pltpu.roll(prod[before, rows, n], 1, 0)
            + pltpu.roll(prod[behind, rows, n], PAD - 1, 0)
        )

    def row_of(table, l, a):
        return table[l, pl.ds(a, 1), :]

    def gain_of(l):
        return own_half(gain_ref[pl.ds(l, 1), :])

    def shift_of(l):
        return own_half(shift_ref[pl.ds(l, 1), :])

    def limit(a, rr):
        w = width_of(a)
        if rr == 0:
            return jnp.where(up_there, w, 0)
        if rr == band + 1:
            return jnp.where(down_there, w, 0)
        return w

    def z_halo(l, way):
        there = z - 1 + 2 * way
        return remote(zs.at[way], zh.at[l, 1 - way], zh_s.at[l, way], zh_r.at[l, way], m, there, c)

    def dh_halo(l, way):
        there = z - 1 + 2 * way
        return remote(dhs.at[way], dhh.at[l, 1 - way], dh_s.at[l, way], dh_r.at[l, way], m, there, c)

    def start_halo(halo, l):
        @pl.when(up_there)
        def _():
            halo(l, 0).start()

        @pl.when(down_there)
        def _():
            halo(l, 1).start()

    def wait_halo(halo, l):
        @pl.when(up_there)
        def _():
            halo(l, 1).wait_recv()
            halo(l, 0).wait_send()

        @pl.when(down_there)
        def _():
            halo(l, 0).wait_recv()
            halo(l, 1).wait_send()

    def act_copy(l, a):
        slot = lax.rem(l, 2)
        src, dst = act_own.at[slot, a], act_oth.at[slot, a]
        return remote(src, dst, act_s.at[l, a], act_r.at[l, a], m, z, other)

    def at_copy(l):
        return remote(act_t.at[l, 0], act_t.at[l, 1], at_s.at[l], at_r.at[l], g_peer, z, c)

    def dzr_copy(l, a, way):
        src, dst = dz_own.at[lax.rem(l, 2), a, pl.ds(1, band)], dzr.at[l, a]
        peer = (x_peer, y_peer)[way]
        return remote(src, dst, dzr_s.at[l, way, a], dzr_r.at[l, a], peer, z, way)

    def if_wanted(way, body):
        @pl.when((x_bit, y_bit)[way] + c == 1)
        def _():
            body()

    def dz_copy(l, a):
        slot = lax.rem(l, 2)
        src, dst = dz_own.at[slot, a], dz_oth.at[slot, a]
        return remote(src, dst, dz_s.at[l, a], dz_r.at[l, a], m, z, other)

    def send_gradients():
        g_partner.start()

        @pl.when(jnp.logical_and(c == 0, up_there))
        def _():
            for n in range(2, 4):
                x_halo(n, 1, 5, z - 1).start()

        @pl.when(jnp.logical_and(c == 1, down_there))
        def _():
            for n in range(2, 4):
                x_halo(n, 4, 0, z + 1).start()

    def if_there(way, body):
        @pl.when((up_there, down_there)[way])
        def _():
            body()

    def wait_x_halo(n):
        if_there(0, lambda: x_halo(n, 4, 0, z - 1).wait_recv())
        if_there(1, lambda: x_halo(n, 1, 5, z + 1).wait_recv())

    def each_x_pass(act):
        if_there(0, lambda: act(x_pass(0)))
        if_there(1, lambda: act(x_pass(band + 1)))

    def sent_x_halo(first, last):
        @pl.when(jnp.logical_and(c == 0, up_there))
        def _():
            for n in range(first, last):
                x_halo(n, 1, 5, z - 1).wait_send()

        @pl.when(jnp.logical_and(c == 1, down_there))
        def _():
            for n in range(first, last):
                x_halo(n, 4, 0, z + 1).wait_send()

    def unpool(a, s):
        for rr in range(band + 2):
            slot, lower = (rr + 1) // 2, (rr + 1) % 2
            g = gbuf[slot, 0, a]
            position = gbuf[slot, 1, a]
            for b in range(2):
                v = jnp.where(position == float(2 * lower + b), g, 0.0)
                for n in range(lanes):
                    hrow[n, pl.ds(b, PAD // 2, stride=2), :] = v[:, n * 128 : (n + 1) * 128]
            v = jnp.concatenate([hrow[n] for n in range(lanes)], 1)
            if rr in (0, band + 1):
                dhh[LAYERS - 1, rr // (band + 1), a] = v.astype(BF16)
            else:
                dh[a, rr - 1] = v
        return s

    def forward(l, first):
        weight_copy(l, 0).wait()
        weight_copy(l, 1).wait()
        if first:
            for copy in x_partner:
                copy.wait_recv()
            products(act_own, l, (1,), wa, False, True)
            products(act_oth, l, (1,), wb, False, False)
            wait_x_halo(0)
            each_x_pass(lambda copy: copy.start())
            products(act_own, l, (0, 2), wa, False, False)
            each_x_pass(lambda copy: copy.wait_recv())
            products(act_oth, l, (0, 2), wb, False, False)
        else:
            products(act_own, l, (0, 1, 2), wa, False, True)
            for a in range(maps_here):
                act_copy(l, a).wait_recv()
            products(act_oth, l, (0, 1, 2), wb, False, False)
        weight_copy(l, 2).start()

        def collect(a, tile):
            inside = column[:, :128] < width_of(a)
            pixels_inside = (width_of(a) * band).astype(F32)
            totals, squares = [], []
            for n in tiles:
                total = jnp.zeros((PAD, 128), F32)
                for rr in range(band):
                    v = shifted(a, rr, 0, 2, n)
                    zbuf[l, a, 1 + rr, :, n] = v
                    total = total + jnp.where(inside, v, 0.0)
                total = jnp.sum(total, 0, keepdims=True)
                mean = total / pixels_inside
                square = jnp.zeros((PAD, 128), F32)
                for rr in range(band):
                    v = jnp.where(inside, zbuf[l, a, 1 + rr, :, n] - mean, 0.0)
                    square = square + v * v
                    if rr in (0, band - 1):
                        zs[rr // (band - 1), a, :, n] = v.astype(BF16)
                totals.append(total)
                squares.append(jnp.sum(square, 0, keepdims=True))
            tile = jnp.where(row8 == a, jnp.concatenate(totals, 1), tile)
            return jnp.where(row8 == a + maps_here, jnp.concatenate(squares, 1), tile)

        tile = lax.fori_loop(0, maps_here, collect, jnp.zeros((8, half), F32))
        send_z(l, tile)
        start_halo(z_halo, l)
        act_t[l, 0] = act_own[lax.rem(l, 2)].reshape(maps_here * (band + 2) * PAD, half).T
        wait_z(l)
        sizes, inverse = inv_t[0], inv_t[1]
        mean_t[0] = st1[l, jnp.maximum(z - 1, 0)] * inverse
        mean_t[1] = st1[l, jnp.minimum(z + 1, chips - 1)] * inverse
        total = st1[l, 0]
        for zz in range(1, chips):
            total = total + st1[l, zz]
        mean = total * inverse * (1.0 / chips)
        square = jnp.zeros((8, half), F32)
        for zz in range(chips):
            v = st1[l, zz]
            gap = v * inverse - mean
            square = square + pltpu.roll(v, 8 - maps_here, 0) + sizes * gap * gap
        tile = jnp.where(row8 < maps_here, mean, pltpu.roll(square, maps_here, 0))
        send_m(l, jnp.where(row8 < 2 * maps_here, tile, 0.0))
        if not first:

            @pl.when(l == LAYERS - 1)
            def _():
                g_partner.wait_recv()
                wait_x_halo(2)
                lax.fori_loop(0, maps_here, unpool, 0)

        wait_m(l)
        at_copy(l).start()
        if first:
            send_gradients()
        averages = jnp.zeros((8, half), F32)
        scalings = jnp.zeros((8, half), F32)
        for a in range(maps_here):
            count = cnt_t[a : a + 1, :]
            average = jnp.zeros((8, half), F32)
            for mm in range(PLANE):
                average = average + coef[a, mm] * nall[mm] * st2[l, mm]
            average = jnp.sum(average, 0, keepdims=True) / count
            variance = jnp.zeros((8, half), F32)
            for mm in range(PLANE):
                v = st2[l, mm]
                gap = v - average
                variance = variance + coef[a, mm] * (
                    pltpu.roll(v, 8 - maps_here, 0) + nall[mm] * gap * gap
                )
            variance = jnp.sum(variance, 0, keepdims=True) / count
            averages = jnp.where(row8 == a, average, averages)
            scalings = jnp.where(row8 == a, lax.rsqrt(variance + epsilon), scalings)
        avg_t[l] = averages
        scl_t[l] = scalings
        wait_halo(z_halo, l)

        def activate(a, s):
            gain, shift = gain_of(l), shift_of(l)
            for n in tiles:
                average = row_of(avg_t, l, a)[:, n]
                factor = row_of(scl_t, l, a)[:, n] * gain[:, n]
                for rr in range(band + 2):
                    if rr in (0, band + 1):
                        way = rr // (band + 1)
                        v = zh[l, way, a, :, n].astype(F32) + row_of(mean_t, way, a)[:, n]
                        zbuf[l, a, rr, :, n] = v
                    else:
                        v = zbuf[l, a, rr, :, n]
                    y = (v - average) * factor + shift[:, n]
                    h = jnp.where(column[:, n] < limit(a, rr), y * jax.nn.sigmoid(y), 0.0)
                    act_own[lax.rem(l + 1, 2), a, rr, :, n] = h.astype(BF16)

            @pl.when(l < LAYERS - 1)
            def _():
                act_copy(l + 1, a).start()

            return s

        if first:
            for copy in x_partner:
                copy.wait_send()
            sent_x_halo(0, 2)
            each_x_pass(lambda copy: copy.wait_send())
        else:

            @pl.when(l == 2)
            def _():
                for a in range(maps_here):
                    act_copy(1, a).wait_send()

        lax.fori_loop(0, maps_here, activate, 0)

    forward(0, True)
    lax.fori_loop(1, LAYERS, lambda l, s: (forward(l, False), s)[1], 0)


    def pool():
        def one(a, s):
            for pr in range(2):
                total = jnp.zeros((PAD // 2, half), F32)
                position = gbuf[1 + pr, 1, a]
                for lower in range(2):
                    v = act_own[LAYERS % 2, a, 1 + 2 * pr + lower].astype(F32)
                    for n in range(lanes):
                        hrow[n] = v[:, n * 128 : (n + 1) * 128]
                    for b in range(2):
                        v = jnp.concatenate(
                            [hrow[n, pl.ds(b, PAD // 2, stride=2), :] for n in range(lanes)], 1
                        )
                        total = total + jnp.where(position == float(2 * lower + b), v, 0.0)
                pbuf[pr, a] = total.astype(BF16)
            return s

        lax.fori_loop(0, maps_here, one, 0)

    def second_rows(bit):
        return pl.ds(pl.multiple_of(bit * (half // 2), half // 2), half // 2)

    def piece_rows(p):
        return pl.ds(pl.multiple_of(p * piece, piece), piece)

    def term_slot(q):
        return lax.rem(q, 2 * TAPS)

    def c2(q):
        src = terms.at[term_slot(q), second_rows(1 - h_bit)]
        return remote(src, r2.at[q], r2_s.at[q], r2_r.at[q], h_peer, z, c)

    def z_of(n):
        return 2 * n + 1 - lax.rem(n, 2)

    def cf(q):
        passive_z = 2 * pair + turn
        there = active_z + passive_z - z
        return remote(r2.at[q], rf.at[term_slot(q)], rf_s.at[q], rf_r.at[q], m, there, c)

    def c3(q, p):
        slot = lax.rem(pair - p + actives - 1, actives)
        return remote(
            r2.at[q, piece_rows(p)], r3.at[q, slot], r3_s.at[q, p], r3_r.at[q, slot], m, z_of(p), c
        )

    def others(first, body, limit):
        def one(k):
            n = lax.rem(pair + k, actives)

            @pl.when(n < limit)
            def _():
                body(n)

        each(first, actives, one)

    def unit_of(q):
        k = lax.div(q, TAPS)
        return (LAYERS - 1 - k) * TAPS + (q - k * TAPS)

    def region(q, start, size, lane, lanes):
        start = pl.multiple_of(c * half + start, piece)
        lane = pl.multiple_of(lane, half)
        return kg_ref.at[unit_of(q), pl.ds(start, size), pl.ds(lane, lanes)]

    def cz(q, p, n):
        part = region(q, h_bit * (half // 2) + p * piece, piece, g_bit * half, half)
        return remote(fin.at[q], part, az_s.at[q, n], az_r.at[q, p], m, z_of(n), c)

    def cl(q):
        part = region(q, h_bit * (half // 2) + pair * piece, piece, g_bit * half, half)
        return pltpu.make_async_copy(fin.at[q], part, loc_s.at[q])

    def cu(q):
        passive_z = 2 * pair + turn
        there = active_z + passive_z - z
        part = region(q, h_bit * (half // 2), half // 2, g_bit * half, half)
        return remote(part, part, af_s.at[q], af_r.at[q], m, there, c)

    def cb(q):
        part = region(q, h_bit * (half // 2), half // 2, g_bit * half, half)
        return remote(part, part, ab_s.at[q], ab_r.at[q], h_peer, z, c)

    def ca(q):
        part = region(q, 0, half, g_bit * half, half)
        return remote(part, part, aa_s.at[q], aa_r.at[q], g_peer, z, c)

    def plan(q):
        k = lax.rem(q, 5)
        both = jnp.logical_or(lax.rem(k, 2) == 0, q >= UNITS - 5)
        mine = jnp.logical_or(both, lax.div(k, 2) == role)
        return mine, jnp.logical_and(mine, jnp.logical_not(both)), jnp.logical_not(mine)

    def ce(q):
        passive_z = 2 * pair + turn
        there = active_z + passive_z - z
        part = region(q, 0, half, (1 - g_bit) * half, half)
        return remote(part, part, ae_s.at[q], ae_r.at[q], m, there, c)

    def cp_part(q, start, size, lane, lanes):
        part = region(q, start, size, lane, lanes)
        return remote(part, part, ap_s.at[q], ap_r.at[q], m, z, other)

    def cp(q):
        return cp_part(q, 0, half, 0, 2 * half)

    def cp_rows(q, bit):
        return cp_part(q, bit * (half // 2), half // 2, g_bit * half, half)

    def cp_lanes(q):
        return cp_part(q, 0, half, (1 - g_bit) * half, half)

    def ready_terms(l):
        at_copy(l).wait_recv()
        for chip in range(2):
            for a in range(maps_here):
                first = a * (band + 2) * PAD
                rows = act_t[l, chip, :, first : first + (band + 2) * PAD]
                act_b[chip, :, a * band * PAD : (a + 1) * band * PAD] = rows[:, PAD : PAD + band * PAD]
        slot = lax.rem(l, 2)

        def variants(a, s):
            dzr_copy(l, a, 0).wait_recv()
            for chip in range(2):
                for rr in range(band):
                    for n in tiles:
                        if chip == 0:
                            mine, theirs = dz_own[slot, a, 1 + rr, :, n], dz_oth[slot, a, 1 + rr, :, n]
                            v = jnp.where(g_bit == c, mine, theirs)
                        else:
                            v = dzr[l, a, rr, :, n]
                        dzv[1, chip, a, rr, :, n] = v
                        v = v.astype(F32)
                        dzv[0, chip, a, rr, :, n] = pltpu.roll(v, PAD - 1, 0).astype(BF16)
                        dzv[2, chip, a, rr, :, n] = pltpu.roll(v, 1, 0).astype(BF16)
            return s

        lax.fori_loop(0, maps_here, variants, 0)

    def tap_terms(l, i, j):
        if i == 1:
            lhs = [act_b[0], act_b[1]]
        else:
            lhs = []
            for chip in range(2):
                for a in range(maps_here):
                    first = (a * (band + 2) + i) * PAD
                    lhs.append(act_t[l, chip, :, first : first + band * PAD])
        rhs = dzv[j].reshape(2 * pixels, half)
        q = (LAYERS - 1 - l) * TAPS + 3 * i + j
        got = jnp.dot(jnp.concatenate(lhs, 1), rhs, preferred_element_type=F32)
        terms[term_slot(q)] = got.astype(BF16)

    def weight_terms(l, i):
        lax.fori_loop(0, 3, lambda j, s: (tap_terms(l, i, j), s)[1], 0)

    def stage_second(q):
        c2(q).wait()
        kept = terms[term_slot(q), second_rows(h_bit)].astype(F32)
        r2[q] = (r2[q].astype(F32) + kept).astype(BF16)

        @pl.when(is_passive)
        def _():
            cf(q).start()

    def stage_fold(q):
        @pl.when(is_active)
        def _():
            cf(q).wait_recv()
            r2[q] = (r2[q].astype(F32) + rf[term_slot(q)].astype(F32)).astype(BF16)
            others(1, lambda n: c3(q, n).start(), owners)

    def stage_sum(q):
        @pl.when(is_owner)
        def _():
            for k in range(actives - 1):
                remote(
                    r3.at[q, k], r3.at[q, k], r3_s.at[q, 0], r3_r.at[q, k], m, z, c
                ).wait_recv()
            total = r2[q, piece_rows(pair)].astype(F32)
            for k in range(actives - 1):
                total = total + r3[q, k].astype(F32)
            fin[q] = total.astype(BF16)
            others(1, lambda n: cz(q, pair, n).start(), actives)
            cl(q).start()

    def stage_back(q):
        @pl.when(is_active)
        def _():
            others(1, lambda n: cz(q, n, n).wait_recv(), owners)

        @pl.when(is_owner)
        def _():
            cl(q).wait()

        @pl.when(is_active)
        def _():
            cu(q).start()

        @pl.when(is_passive)
        def _():
            cu(q).wait_recv()

        cb(q).start()
        cp_rows(q, h_bit).start()

    def stage_first(q):
        cb(q).wait_recv()
        mine, _, _ = plan(q)

        @pl.when(mine)
        def _():
            ca(q).start()

        cp_rows(q, 1 - h_bit).start()

        @pl.when(is_active)
        def _():
            others(1, lambda n: c3(q, n).wait_send(), owners)

        @pl.when(is_passive)
        def _():
            cf(q).wait_send()

    def stage_chip(q):
        mine, for_both, _ = plan(q)

        @pl.when(mine)
        def _():
            ca(q).wait_recv()

        @pl.when(for_both)
        def _():
            ce(q).start()

        @pl.when(mine)
        def _():
            cp_lanes(q).start()

        @pl.when(is_owner)
        def _():
            others(1, lambda n: cz(q, pair, n).wait_send(), actives)

        @pl.when(is_active)
        def _():
            cu(q).wait_send()

    def stage_late(q):
        _, _, not_mine = plan(q)

        @pl.when(not_mine)
        def _():
            ce(q).wait_recv()
            cp_lanes(q).start()

    def stage_done(q):
        mine, for_both, _ = plan(q)
        cb(q).wait_send()

        @pl.when(mine)
        def _():
            ca(q).wait_send()

        @pl.when(for_both)
        def _():
            ce(q).wait_send()

        cp(q).wait()

    def run(stage, first, last):
        lax.fori_loop(first, last, lambda q, s: (stage(q), s)[1], 0)

    def sent_dz(l):
        for a in range(maps_here):
            dz_copy(l, a).wait_send()
            for way in range(2):
                if_wanted(way, dzr_copy(l, a, way).wait_send)

    def backward(k, carry):
        l = LAYERS - 1 - k
        gain, shift = gain_of(l), shift_of(l)

        def gradient(a, rr, n):
            zhat = (zbuf[l, a, rr, :, n] - row_of(avg_t, l, a)[:, n]) * row_of(scl_t, l, a)[:, n]
            y = zhat * gain[:, n] + shift[:, n]
            s = jax.nn.sigmoid(y)
            if rr in (0, band + 1):
                upstream = dhh[l, rr // (band + 1), a, :, n].astype(F32)
            else:
                upstream = dh[a, rr - 1, :, n]
            dy = upstream * (s * (1.0 + y * (1.0 - s)))
            dy = jnp.where(column[:, n] < limit(a, rr), dy, 0.0)
            return dy, zhat

        def collect(a, tile):
            plains, crosses = [], []
            for n in tiles:
                plain = jnp.zeros((PAD, 128), F32)
                crossed = jnp.zeros((PAD, 128), F32)
                for rr in range(1, band + 1):
                    dy, zhat = gradient(a, rr, n)
                    dh[a, rr - 1, :, n] = dy
                    plain = plain + dy
                    crossed = crossed + dy * zhat
                plains.append(jnp.sum(plain, 0, keepdims=True))
                crosses.append(jnp.sum(crossed, 0, keepdims=True))
            tile = jnp.where(row8 == a, jnp.concatenate(plains, 1), tile)
            return jnp.where(row8 == a + maps_here, jnp.concatenate(crosses, 1), tile)

        e = LAYERS + l
        tile = lax.fori_loop(0, maps_here, collect, jnp.zeros((8, half), F32))
        send_z(e, tile)

        @pl.when(k == LAYERS - 1)
        def _():
            run(stage_second, 0, TAPS)

        @pl.when(k > 0)
        def _():
            ready_terms(l + 1)
            weight_terms(l + 1, 0)

        wait_z(e)
        total = st1[e, 0]
        for zz in range(1, chips):
            total = total + st1[e, zz]
        send_m(e, total)

        @pl.when(k > 0)
        def _():
            first = (LAYERS - 2 - l) * TAPS
            run(lambda q: c2(q).start(), first, first + 3)
            weight_terms(l + 1, 1)
            run(lambda q: c2(q).start(), first + 3, first + 6)
            weight_terms(l + 1, 2)
            run(lambda q: c2(q).start(), first + 6, first + 9)
            wait_halo(dh_halo, l)

        @pl.when(k == 0)
        def _():
            pool()

        wait_m(e)
        total = st2[e, 0]
        for mm in range(1, PLANE):
            total = total + st2[e, mm]
        sums_own[pl.ds(l, 1), :] = jnp.sum(
            jnp.where(row8 >= maps_here, total, 0.0), 0, keepdims=True
        )
        sums_own[pl.ds(LAYERS + l, 1), :] = jnp.sum(
            jnp.where(row8 < maps_here, total, 0.0), 0, keepdims=True
        )
        plains = jnp.zeros((8, half), F32)
        crosses = jnp.zeros((8, half), F32)
        for a in range(maps_here):
            plain = jnp.zeros((8, half), F32)
            crossed = jnp.zeros((8, half), F32)
            for mm in range(PLANE):
                v = st2[e, mm]
                plain = plain + coef[a, mm] * v
                crossed = crossed + coef[a, mm] * pltpu.roll(v, 8 - maps_here, 0)
            count = cnt_t[a : a + 1, :]
            plain = gain * (jnp.sum(plain, 0, keepdims=True) / count)
            crossed = gain * (jnp.sum(crossed, 0, keepdims=True) / count)
            plains = jnp.where(row8 == a, plain, plains)
            crosses = jnp.where(row8 == a, crossed, crosses)
        tb_t[0] = plains
        ta_t[0] = crosses

        def settle(a, s):
            for n in tiles:
                average, scaling = row_of(avg_t, l, a)[:, n], row_of(scl_t, l, a)[:, n]
                plain, crossed = row_of(tb_t, 0, a)[:, n], row_of(ta_t, 0, a)[:, n]
                for rr in range(band + 2):
                    if rr in (0, band + 1):
                        dy, zhat = gradient(a, rr, n)
                    else:
                        dy = dh[a, rr - 1, :, n]
                        zhat = (zbuf[l, a, rr, :, n] - average) * scaling
                    v = scaling * (dy * gain[:, n] - plain - zhat * crossed)
                    v = jnp.where(column[:, n] < limit(a, rr), v, 0.0)
                    dz_own[lax.rem(l, 2), a, rr, :, n] = v.astype(BF16)
            dz_copy(l, a).start()
            for way in range(2):
                if_wanted(way, dzr_copy(l, a, way).start)
            return s

        @pl.when(k == 2)
        def _():
            sent_dz(LAYERS - 1)

        lax.fori_loop(0, maps_here, settle, 0)
        products(dz_own, l, (0, 1, 2), wa, True, True)
        weight_copy(l, 2).wait()
        for a in range(maps_here):
            dz_copy(l, a).wait_recv()
        products(dz_oth, l, (0, 1, 2), wb, True, False)

        def gather(a, s):
            for n in tiles:
                for rr in range(band):
                    v = shifted(a, rr, 2, 0, n)
                    dh[a, rr, :, n] = v
                    if rr in (0, band - 1):
                        dhs[rr // (band - 1), a, :, n] = v.astype(BF16)
            return s

        lax.fori_loop(0, maps_here, gather, 0)

        @pl.when(l > 0)
        def _():
            start_halo(dh_halo, l - 1)

        return carry

    lax.fori_loop(0, LAYERS, backward, 0)
    def input_rows(a, s):
        for rr in range(band):
            dh[a, rr] = jnp.where(column < width_of(a), dh[a, rr], 0.0)
        return s

    lax.fori_loop(0, maps_here, input_rows, 0)

    outs = (
        (
            remote(dh.at[:, pl.ds(2 * other, 2)], ig_ref.at[c], out_s.at[0], out_r.at[0], m, z, other),
            pltpu.make_async_copy(dh.at[:, pl.ds(2 * c, 2)], ig_ref.at[c], out_l.at[0]),
        ),
        (
            remote(pbuf.at[other], pooled_ref.at[c], out_s.at[1], out_r.at[1], m, z, other),
            pltpu.make_async_copy(pbuf.at[c], pooled_ref.at[c], out_l.at[1]),
        ),
        (
            remote(sums_own, sums_ref.at[c], out_s.at[2], out_r.at[2], m, z, other),
            pltpu.make_async_copy(sums_own, sums_ref.at[c], out_l.at[2]),
        ),
    )
    for there, here in outs:
        there.start()
        here.start()

    g_partner.wait_send()
    sent_x_halo(2, 4)

    def sent(e, carry):
        each(1, chips, lambda k: z_copy(e, k).wait_send())
        each(1, PLANE, lambda k: m_copy(e, k).wait_send())
        return carry

    lax.fori_loop(0, 2 * LAYERS, sent, 0)
    for l in range(LAYERS):
        at_copy(l).wait_send()
    for l in range(LAYERS - 1):
        sent_dz(l)

    def drain(s, carry):
        @pl.when(s == EARLY)
        def _():
            ready_terms(0)

        for i in range(3):
            j = s - EARLY - 3 * i

            @pl.when(jnp.logical_and(j >= 0, j < 3))
            def _(i=i, j=j):
                tap_terms(0, i, j)
                c2(2 * TAPS + 3 * i + j).start()

        for stage, first, lag in (
            (stage_done, 0, 2 * FOLD + 4 * LAG),
            (stage_late, 0, 2 * FOLD + 3 * LAG),
            (stage_chip, 0, 2 * FOLD + 2 * LAG),
            (stage_first, 0, 2 * FOLD + LAG),
            (stage_back, 0, 2 * FOLD),
            (stage_sum, 0, FOLD),
            (stage_fold, 0, 0),
            (stage_second, TAPS, 0),
        ):
            q = first + s - lag

            @pl.when(jnp.logical_and(q >= first, q < UNITS))
            def _(stage=stage, q=q):
                stage(q)

        return carry

    lax.fori_loop(0, UNITS + 2 * FOLD + 4 * LAG, drain, 0)
    for a in range(maps_here):
        act_copy(2, a).wait_send()
    for there, here in outs:
        there.wait()
        here.wait()


def solution(mesh):
    chips = mesh.shape["rows"] // 2

    def per_device(
        block_input,
        conv_weights,
        norm_gains,
        norm_shifts,
        map_width,
        map_group,
        pool_index,
        task_mask,
        task_weights,
        task_grads,
    ):
        maps_here, rows_here, columns, channels = block_input.shape
        pooled_columns = pool_index.shape[2]
        height = rows_here * mesh.shape["rows"]
        half = channels // 2
        band = 2 * rows_here
        pixels = maps_here * band * PAD
        actives = chips // 2
        owners = min(actives, 8)
        piece = half // 2 // owners
        rounds = 2 * LAYERS
        slots = 2 * UNITS * (actives - 1) * piece * half + 4 * rounds * chips * 8 * half
        grant = (36 * 1024 + 256) * 1024 + slots
        vmem, dma = pltpu.VMEM, pltpu.SemaphoreType.DMA
        tile = (maps_here, band + 2, PAD, half)
        edge = (2, maps_here, PAD, half)
        whole = pl.BlockSpec(memory_space=pltpu.VMEM)
        outside = pl.BlockSpec(memory_space=pltpu.HBM)
        index_rows = jnp.transpose(pool_index, (0, 2, 1, 3))
        anywhere = pl.BlockSpec(memory_space=pl.ANY)
        pooled, ig, kg, sums = pl.pallas_call(
            functools.partial(block_kernel, chips, height),
            out_shape=(
                jax.ShapeDtypeStruct((2, maps_here, PAD // 2, half), BF16),
                jax.ShapeDtypeStruct((2, maps_here, rows_here, PAD, half), F32),
                jax.ShapeDtypeStruct((UNITS, channels, channels), BF16),
                jax.ShapeDtypeStruct((2, 8, half), F32),
            ),
            in_specs=[whole, anywhere] + [outside] * 8,
            out_specs=[anywhere] * 4,
            scratch_shapes=[
                vmem(norm_gains.shape, F32),
                vmem(norm_shifts.shape, F32),
                pltpu.SMEM(map_width.shape, jnp.int32),
                pltpu.SMEM(map_group.shape, jnp.int32),
                vmem((maps_here, pooled_columns, channels), jnp.int32),
                pltpu.SMEM(task_mask.shape, jnp.int32),
                pltpu.SMEM(task_weights.shape, F32),
                vmem(task_grads.shape, BF16),
                vmem((LAYERS, 3, 3, half, half), BF16),
                vmem((LAYERS, 3, 3, half, half), BF16),
                vmem((2,) + tile, BF16),
                vmem((2,) + tile, BF16),
                vmem((LAYERS, 2, half, maps_here * (band + 2) * PAD), BF16),
                vmem((2, half, pixels), BF16),
                vmem((LAYERS,) + tile, F32),
                vmem(edge, BF16),
                vmem((LAYERS,) + edge, BF16),
                vmem((maps_here, band, PAD, half), F32),
                vmem(edge, BF16),
                vmem((LAYERS,) + edge, BF16),
                vmem((2,) + tile, BF16),
                vmem((2,) + tile, BF16),
                vmem((LAYERS, maps_here, band, PAD, half), BF16),
                vmem((3, 2, maps_here, band, PAD, half), BF16),
                vmem((3, pixels, half), F32),
                vmem((2, 2, maps_here, PAD // 2, half), F32),
                vmem((4, 2, maps_here, PAD // 2, half), F32),
                vmem((half // 128, PAD, 128), F32),
                vmem((2, maps_here, PAD // 2, half), BF16),
                vmem((rounds, chips, 8, half), F32),
                vmem((rounds, PLANE, 8, half), F32),
                vmem((maps_here, PLANE, 8, half), F32),
                vmem((PLANE, 8, half), F32),
                vmem((2, 8, half), F32),
                vmem((8, half), F32),
                vmem((LAYERS, 8, half), F32),
                vmem((LAYERS, 8, half), F32),
                vmem((2, 8, half), F32),
                vmem((1, 8, half), F32),
                vmem((1, 8, half), F32),
                vmem((8, half), F32),
                vmem((2 * TAPS, half, half), BF16),
                vmem((UNITS, half // 2, half), BF16),
                vmem((2 * TAPS, half // 2, half), BF16),
                vmem((UNITS, actives - 1, piece, half), BF16),
                vmem((UNITS, piece, half), BF16),
                dma((8,)),
                dma((LAYERS, 3)),
                dma((6,)),
                dma((6,)),
                dma((3,)),
                dma((3,)),
                dma((rounds, chips)),
                dma((rounds, chips)),
                dma((rounds, PLANE)),
                dma((rounds, PLANE)),
                dma((LAYERS, 2)),
                dma((LAYERS, 2)),
                dma((LAYERS, 2)),
                dma((LAYERS, 2)),
                dma((LAYERS, maps_here)),
                dma((LAYERS, maps_here)),
                dma((LAYERS, maps_here)),
                dma((LAYERS, maps_here)),
                dma((3,)),
                dma((3,)),
                dma((3,)),
                dma((LAYERS,)),
                dma((LAYERS,)),
                dma((LAYERS, 2, maps_here)),
                dma((LAYERS, maps_here)),
                dma((UNITS,)),
                dma((UNITS,)),
                dma((UNITS,)),
                dma((UNITS,)),
                dma((UNITS, owners)),
                dma((UNITS, actives - 1)),
                dma((UNITS, actives)),
                dma((UNITS, owners)),
                dma((UNITS,)),
                dma((UNITS,)),
                dma((UNITS,)),
                dma((UNITS,)),
                dma((UNITS,)),
                dma((UNITS,)),
                dma((UNITS,)),
                dma((UNITS,)),
                dma((UNITS,)),
                dma((UNITS,)),
                dma((UNITS,)),
            ],
            compiler_params=pltpu.CompilerParams(
                collective_id=0,
                has_side_effects=True,
                vmem_limit_bytes=grant,
            ),
        )(
            block_input,
            conv_weights,
            *(
                pltpu.with_memory_space_constraint(v, pltpu.HBM)
                for v in (
                    norm_gains,
                    norm_shifts,
                    map_width,
                    map_group,
                    index_rows,
                    task_mask,
                    task_weights,
                    task_grads,
                )
            ),
        )
        pooled = jnp.concatenate([pooled[0], pooled[1]], -1)[:, None, :pooled_columns]
        input_grad = jnp.concatenate([ig[0], ig[1]], -1)[:, :, :columns]
        sums = jnp.concatenate([sums[0], sums[1]], -1)
        return (
            pooled,
            input_grad,
            kg.astype(F32).reshape(conv_weights.shape),
            sums[:LAYERS],
            sums[LAYERS : 2 * LAYERS],
        )

    return jax.shard_map(
        per_device,
        mesh=mesh,
        in_specs=(
            P("maps", "rows", None, None),
            P(),
            P(),
            P(),
            P(),
            P(),
            P("maps", "rows", None, None),
            P("maps", None),
            P(),
            P(None, "maps", "rows", None, None),
        ),
        out_specs=(P("maps", "rows", None, None), P("maps", "rows", None, None), P(), P(), P()),
        check_vma=False,
    )
```

```python
import functools

import jax
import jax.numpy as jnp
from jax import lax
from jax.experimental import pallas as pl
from jax.experimental.pallas import tpu as pltpu
from jax.sharding import PartitionSpec as P

MESH = pl.DeviceIdType.MESH
epsilon = 1e-05
PAD = 64
LAYERS = 3
TAPS = 9
UNITS = LAYERS * TAPS
PLANE = 4
LAG = 4
EARLY = 1
FOLD = 2
F32 = jnp.float32
BF16 = jnp.bfloat16


def each(first, last, body):
    if last - first <= 8:
        for k in range(first, last):
            body(k)
    else:
        lax.fori_loop(first, last, lambda k, s: (body(k), s)[1], 0)


def block_kernel(
    chips,
    height,
    x_ref,
    w_ref,
    gain_hbm,
    shift_hbm,
    width_hbm,
    group_hbm,
    index_hbm,
    tmask_hbm,
    tweight_hbm,
    tgrad_hbm,
    pooled_ref,
    ig_ref,
    kg_ref,
    sums_ref,
    gain_ref,
    shift_ref,
    width_ref,
    group_ref,
    index_ref,
    tmask_ref,
    tweight_ref,
    tgrad_ref,
    wa,
    wb,
    act_own,
    act_oth,
    act_t,
    act_b,
    zbuf,
    zs,
    zh,
    dh,
    dhs,
    dhh,
    dz_own,
    dz_oth,
    dzr,
    dzv,
    prod,
    gsrc,
    gbuf,
    hrow,
    pbuf,
    st1,
    st2,
    coef,
    nall,
    inv_t,
    cnt_t,
    avg_t,
    scl_t,
    mean_t,
    tb_t,
    ta_t,
    sums_own,
    terms,
    r2,
    rf,
    r3,
    fin,
    in_sem,
    w_sem,
    x_s,
    x_r,
    g_s,
    g_r,
    st1_s,
    st1_r,
    st2_s,
    st2_r,
    zh_s,
    zh_r,
    dh_s,
    dh_r,
    act_s,
    act_r,
    dz_s,
    dz_r,
    out_s,
    out_r,
    out_l,
    at_s,
    at_r,
    dzr_s,
    dzr_r,
    r2_s,
    r2_r,
    rf_s,
    rf_r,
    r3_s,
    r3_r,
    az_s,
    az_r,
    af_s,
    af_r,
    ab_s,
    ab_r,
    aa_s,
    aa_r,
    ae_s,
    ae_r,
    ap_s,
    ap_r,
    loc_s,
):
    maps_here = x_ref.shape[0]
    columns = x_ref.shape[2]
    half = x_ref.shape[3] // 2
    tasks = tgrad_ref.shape[0]
    pooled_columns = tgrad_ref.shape[3]
    lanes = half // 128
    tiles = [slice(n * 128, (n + 1) * 128) for n in range(lanes)]
    band = 4
    pixels = maps_here * band * PAD
    actives = chips // 2
    owners = min(actives, 8)
    piece = (half // 2) // owners
    m = lax.axis_index("maps")
    r = lax.axis_index("rows")
    c = lax.rem(r, 2)
    z = lax.div(r, 2)
    other = 1 - c
    first_map = m * maps_here
    x_bit = lax.rem(m, 2)
    y_bit = lax.div(m, 2)
    x_peer = m + 1 - 2 * x_bit
    y_peer = m + 2 - 4 * y_bit
    g_bit = (1 - c) * x_bit + c * y_bit
    h_bit = (1 - c) * y_bit + c * x_bit
    g_peer = (1 - c) * x_peer + c * y_peer
    h_peer = (1 - c) * y_peer + c * x_peer
    pair = lax.div(z, 2)
    turn = lax.rem(pair, 2)
    active_z = 2 * pair + 1 - turn
    is_active = z == active_z
    is_passive = z != active_z
    is_owner = jnp.logical_and(is_active, pair < owners)
    role = jnp.where(is_active, 0, 1)
    up_there = z > 0
    down_there = z < chips - 1
    row8 = lax.broadcasted_iota(jnp.int32, (8, half), 0)
    column = lax.broadcasted_iota(jnp.int32, (PAD, half), 0)

    def remote(src, dst, send, recv, mm, zz, cc):
        return pltpu.make_async_remote_copy(
            src_ref=src,
            dst_ref=dst,
            send_sem=send,
            recv_sem=recv,
            device_id=(mm, zz * 2 + cc),
            device_id_type=MESH,
        )

    def own_half(v):
        return jnp.where(c == 0, v[..., :half], v[..., half:])

    def width_of(a):
        return width_ref[first_map + a]

    own_at = pl.ds(pl.multiple_of(c * half, half), half)
    oth_at = pl.ds(pl.multiple_of(other * half, half), half)

    def weight_copy(l, n):
        dst = (wa, wb, wb)[n]
        k_at, o_at = ((own_at, own_at), (oth_at, own_at), (own_at, oth_at))[n]
        return pltpu.make_async_copy(w_ref.at[l, :, :, k_at, o_at], dst.at[l], w_sem.at[l, n])

    fetches = [
        pltpu.make_async_copy(src, dst, in_sem.at[n])
        for n, (src, dst) in enumerate(
            (
                (width_hbm, width_ref),
                (group_hbm, group_ref),
                (tmask_hbm, tmask_ref),
                (tweight_hbm, tweight_ref),
                (gain_hbm, gain_ref),
                (shift_hbm, shift_ref),
                (index_hbm.at[:, :, 0, :], index_ref),
                (tgrad_hbm, tgrad_ref),
            )
        )
    ]
    for fetch in fetches:
        fetch.start()
    for l in range(LAYERS):
        weight_copy(l, 0).start()
        weight_copy(l, 1).start()

    barrier = pltpu.get_barrier_semaphore()

    def greet(k):
        rr = lax.rem(r + k, 2 * chips)
        pl.semaphore_signal(barrier, inc=1, device_id=(m, rr), device_id_type=MESH)

    each(1, 2 * chips, greet)
    for k in range(1, PLANE):
        for core in (c, other):
            there = (lax.rem(m + k, PLANE), z * 2 + core)
            pl.semaphore_signal(barrier, inc=1, device_id=there, device_id_type=MESH)

    for fetch in fetches:
        fetch.wait()

    mine = pl.ds(1 + 2 * c, 2)
    for a in range(maps_here):
        inside = lax.broadcasted_iota(jnp.int32, (columns, 2 * half), 0) < width_of(a)
        for rr in range(2):
            v = jnp.where(inside, x_ref[a, rr].astype(F32), 0.0).astype(BF16)
            spot = 1 + 2 * c + rr
            act_own[0, a, spot, pl.ds(48, 16), :] = jnp.zeros((16, half), BF16)
            act_oth[0, a, spot, pl.ds(48, 16), :] = jnp.zeros((16, half), BF16)
            act_own[0, a, spot, pl.ds(0, columns), :] = own_half(v)
            act_oth[0, a, spot, pl.ds(0, columns), :] = jnp.where(
                c == 0, v[:, half:], v[:, :half]
            )

    @pl.when(z == 0)
    def _():
        act_own[0, :, 0] = jnp.zeros((maps_here, PAD, half), BF16)
        act_oth[0, :, 0] = jnp.zeros((maps_here, PAD, half), BF16)

    @pl.when(z == chips - 1)
    def _():
        act_own[0, :, 5] = jnp.zeros((maps_here, PAD, half), BF16)
        act_oth[0, :, 5] = jnp.zeros((maps_here, PAD, half), BF16)

    pl.semaphore_wait(barrier, 2 * chips - 1 + 2 * (PLANE - 1))

    x_partner = (
        remote(act_own.at[0, :, mine], act_oth.at[0, :, mine], x_s.at[0], x_r.at[0], m, z, other),
        remote(act_oth.at[0, :, mine], act_own.at[0, :, mine], x_s.at[1], x_r.at[1], m, z, other),
    )
    g_partner = remote(gsrc.at[other], gbuf.at[1 + c], g_s.at[0], g_r.at[0], m, z, other)

    def x_halo(n, src_row, dst_row, zz):
        cc = (c, other)[n % 2]
        low = dst_row == band + 1
        if n >= 2:
            src, dst = gsrc.at[cc], gbuf.at[3 if low else 0]
            return remote(src, dst, g_s.at[n - 1], g_r.at[1 if low else 2], m, zz, cc)
        src, dst = (act_own, act_oth)[n].at[0, :, src_row], act_own.at[0, :, dst_row]
        return remote(src, dst, x_s.at[2 + n], x_r.at[2 if low else 3], m, zz, cc)

    def x_pass(row):
        n = 4 if row == 0 else 5
        src, dst = act_own.at[0, :, row], act_oth.at[0, :, row]
        return remote(src, dst, x_s.at[n], x_r.at[n], m, z, other)

    for copy in x_partner:
        copy.start()

    @pl.when(jnp.logical_and(c == 0, up_there))
    def _():
        for n in range(2):
            x_halo(n, 1, 5, z - 1).start()

    @pl.when(jnp.logical_and(c == 1, down_there))
    def _():
        for n in range(2):
            x_halo(n, 4, 0, z + 1).start()

    gsrc[...] = jnp.zeros(gsrc.shape, F32)
    for a in range(maps_here):
        total = None
        for t in range(tasks):
            scale = tweight_ref[t] * tmask_ref[a, t].astype(F32)
            term = tgrad_ref[t, a, 0].astype(F32) * scale
            total = term if total is None else total + term
        position = index_ref[a].astype(F32)
        for h in range(2):
            gsrc[h, 0, a, pl.ds(0, pooled_columns), :] = total[:, h * half : (h + 1) * half]
            gsrc[h, 1, a, pl.ds(0, pooled_columns), :] = position[:, h * half : (h + 1) * half]
    gbuf[1 + c] = gsrc[c]

    for mm in range(PLANE):
        sizes = jnp.zeros((8, half), F32)
        for b in range(maps_here):
            sizes = jnp.where(
                row8 == b, (width_ref[mm * maps_here + b] * height).astype(F32), sizes
            )
        nall[mm] = sizes
    inside_sizes = jnp.zeros((8, half), F32)
    for b in range(maps_here):
        inside_sizes = jnp.where(row8 == b, (width_of(b) * band).astype(F32), inside_sizes)
    inv_t[0] = inside_sizes
    inv_t[1] = jnp.where(row8 < maps_here, 1.0 / jnp.maximum(inside_sizes, 1.0), 0.0)
    counts = jnp.ones((8, half), F32)
    for a in range(maps_here):
        total = jnp.zeros((1, half), F32)
        for mm in range(PLANE):
            same = jnp.zeros((8, half), F32)
            for b in range(maps_here):
                alike = group_ref[first_map + a] == group_ref[mm * maps_here + b]
                same = jnp.where(row8 == b, jnp.where(alike, 1.0, 0.0), same)
            coef[a, mm] = same
            total = total + jnp.sum(same * nall[mm], 0, keepdims=True)
        counts = jnp.where(row8 == a, total, counts)
    cnt_t[...] = counts

    def z_copy(e, k):
        zz = lax.rem(z + k, chips)
        return remote(st1.at[e, z], st1.at[e, z], st1_s.at[e, k], st1_r.at[e, z], m, zz, c)

    def z_arrival(e, k):
        zz = lax.rem(z + k, chips)
        return remote(st1.at[e, zz], st1.at[e, zz], st1_s.at[e, k], st1_r.at[e, zz], m, zz, c)

    def m_copy(e, k):
        mm = lax.rem(m + k, PLANE)
        return remote(st2.at[e, m], st2.at[e, m], st2_s.at[e, k], st2_r.at[e, m], mm, z, c)

    def m_arrival(e, k):
        mm = lax.rem(m + k, PLANE)
        return remote(st2.at[e, mm], st2.at[e, mm], st2_s.at[e, k], st2_r.at[e, mm], mm, z, c)

    def send_z(e, tile):
        st1[e, z] = tile
        each(1, chips, lambda k: z_copy(e, k).start())

    def wait_z(e):
        each(1, chips, lambda k: z_arrival(e, k).wait_recv())

    def send_m(e, tile):
        st2[e, m] = tile
        each(1, PLANE, lambda k: m_copy(e, k).start())

    def wait_m(e):
        each(1, PLANE, lambda k: m_arrival(e, k).wait_recv())

    def products(source, l, taps, kernel, transposed, fresh):
        starts = [2 - i if transposed else i for i in taps]
        lhs = jnp.concatenate(
            [source[lax.rem(l, 2), :, s : s + band].reshape(pixels, half) for s in starts], 1
        )
        for j in range(3):
            rhs = jnp.concatenate([kernel[l, i, j] for i in taps], 1 if transposed else 0)
            got = lax.dot_general(
                lhs,
                rhs,
                (((1,), (1 if transposed else 0,)), ((), ())),
                preferred_element_type=F32,
            )
            if fresh:
                prod[j] = got
            else:
                prod[j] = prod[j] + got

    def shifted(a, rr, before, behind, n):
        rows = pl.ds(pl.multiple_of((a * band + rr) * PAD, PAD), PAD)
        return (
            prod[1, rows, n]
            + pltpu.roll(prod[before, rows, n], 1, 0)
            + pltpu.roll(prod[behind, rows, n], PAD - 1, 0)
        )

    def row_of(table, l, a):
        return table[l, pl.ds(a, 1), :]

    def gain_of(l):
        return own_half(gain_ref[pl.ds(l, 1), :])

    def shift_of(l):
        return own_half(shift_ref[pl.ds(l, 1), :])

    def limit(a, rr):
        w = width_of(a)
        if rr == 0:
            return jnp.where(up_there, w, 0)
        if rr == band + 1:
            return jnp.where(down_there, w, 0)
        return w

    def z_halo(l, way):
        there = z - 1 + 2 * way
        return remote(zs.at[way], zh.at[l, 1 - way], zh_s.at[l, way], zh_r.at[l, way], m, there, c)

    def dh_halo(l, way):
        there = z - 1 + 2 * way
        return remote(dhs.at[way], dhh.at[l, 1 - way], dh_s.at[l, way], dh_r.at[l, way], m, there, c)

    def start_halo(halo, l):
        @pl.when(up_there)
        def _():
            halo(l, 0).start()

        @pl.when(down_there)
        def _():
            halo(l, 1).start()

    def wait_halo(halo, l):
        @pl.when(up_there)
        def _():
            halo(l, 1).wait_recv()
            halo(l, 0).wait_send()

        @pl.when(down_there)
        def _():
            halo(l, 0).wait_recv()
            halo(l, 1).wait_send()

    def act_copy(l, a):
        slot = lax.rem(l, 2)
        src, dst = act_own.at[slot, a], act_oth.at[slot, a]
        return remote(src, dst, act_s.at[l, a], act_r.at[l, a], m, z, other)

    def at_copy(l):
        return remote(act_t.at[l, 0], act_t.at[l, 1], at_s.at[l], at_r.at[l], g_peer, z, c)

    def dzr_copy(l, a, way):
        src, dst = dz_own.at[lax.rem(l, 2), a, pl.ds(1, band)], dzr.at[l, a]
        peer = (x_peer, y_peer)[way]
        return remote(src, dst, dzr_s.at[l, way, a], dzr_r.at[l, a], peer, z, way)

    def if_wanted(way, body):
        @pl.when((x_bit, y_bit)[way] + c == 1)
        def _():
            body()

    def dz_copy(l, a):
        slot = lax.rem(l, 2)
        src, dst = dz_own.at[slot, a], dz_oth.at[slot, a]
        return remote(src, dst, dz_s.at[l, a], dz_r.at[l, a], m, z, other)

    def send_gradients():
        g_partner.start()

        @pl.when(jnp.logical_and(c == 0, up_there))
        def _():
            for n in range(2, 4):
                x_halo(n, 1, 5, z - 1).start()

        @pl.when(jnp.logical_and(c == 1, down_there))
        def _():
            for n in range(2, 4):
                x_halo(n, 4, 0, z + 1).start()

    def if_there(way, body):
        @pl.when((up_there, down_there)[way])
        def _():
            body()

    def wait_x_halo(n):
        if_there(0, lambda: x_halo(n, 4, 0, z - 1).wait_recv())
        if_there(1, lambda: x_halo(n, 1, 5, z + 1).wait_recv())

    def each_x_pass(act):
        if_there(0, lambda: act(x_pass(0)))
        if_there(1, lambda: act(x_pass(band + 1)))

    def sent_x_halo(first, last):
        @pl.when(jnp.logical_and(c == 0, up_there))
        def _():
            for n in range(first, last):
                x_halo(n, 1, 5, z - 1).wait_send()

        @pl.when(jnp.logical_and(c == 1, down_there))
        def _():
            for n in range(first, last):
                x_halo(n, 4, 0, z + 1).wait_send()

    def unpool(a, s):
        for rr in range(band + 2):
            slot, lower = (rr + 1) // 2, (rr + 1) % 2
            g = gbuf[slot, 0, a]
            position = gbuf[slot, 1, a]
            for b in range(2):
                v = jnp.where(position == float(2 * lower + b), g, 0.0)
                for n in range(lanes):
                    hrow[n, pl.ds(b, PAD // 2, stride=2), :] = v[:, n * 128 : (n + 1) * 128]
            v = jnp.concatenate([hrow[n] for n in range(lanes)], 1)
            if rr in (0, band + 1):
                dhh[LAYERS - 1, rr // (band + 1), a] = v.astype(BF16)
            else:
                dh[a, rr - 1] = v
        return s

    def forward(l, first):
        weight_copy(l, 0).wait()
        weight_copy(l, 1).wait()
        if first:
            for copy in x_partner:
                copy.wait_recv()
            products(act_own, l, (1,), wa, False, True)
            products(act_oth, l, (1,), wb, False, False)
            wait_x_halo(0)
            each_x_pass(lambda copy: copy.start())
            products(act_own, l, (0, 2), wa, False, False)
            each_x_pass(lambda copy: copy.wait_recv())
            products(act_oth, l, (0, 2), wb, False, False)
        else:
            products(act_own, l, (0, 1, 2), wa, False, True)
            for a in range(maps_here):
                act_copy(l, a).wait_recv()
            products(act_oth, l, (0, 1, 2), wb, False, False)
        weight_copy(l, 2).start()

        def collect(a, tile):
            inside = column[:, :128] < width_of(a)
            pixels_inside = (width_of(a) * band).astype(F32)
            totals, squares = [], []
            for n in tiles:
                total = jnp.zeros((PAD, 128), F32)
                for rr in range(band):
                    v = shifted(a, rr, 0, 2, n)
                    zbuf[l, a, 1 + rr, :, n] = v
                    total = total + jnp.where(inside, v, 0.0)
                total = jnp.sum(total, 0, keepdims=True)
                mean = total / pixels_inside
                square = jnp.zeros((PAD, 128), F32)
                for rr in range(band):
                    v = jnp.where(inside, zbuf[l, a, 1 + rr, :, n] - mean, 0.0)
                    square = square + v * v
                    if rr in (0, band - 1):
                        zs[rr // (band - 1), a, :, n] = v.astype(BF16)
                totals.append(total)
                squares.append(jnp.sum(square, 0, keepdims=True))
            tile = jnp.where(row8 == a, jnp.concatenate(totals, 1), tile)
            return jnp.where(row8 == a + maps_here, jnp.concatenate(squares, 1), tile)

        tile = lax.fori_loop(0, maps_here, collect, jnp.zeros((8, half), F32))
        send_z(l, tile)
        start_halo(z_halo, l)
        act_t[l, 0] = act_own[lax.rem(l, 2)].reshape(maps_here * (band + 2) * PAD, half).T
        wait_z(l)
        sizes, inverse = inv_t[0], inv_t[1]
        mean_t[0] = st1[l, jnp.maximum(z - 1, 0)] * inverse
        mean_t[1] = st1[l, jnp.minimum(z + 1, chips - 1)] * inverse
        total = st1[l, 0]
        for zz in range(1, chips):
            total = total + st1[l, zz]
        mean = total * inverse * (1.0 / chips)
        square = jnp.zeros((8, half), F32)
        for zz in range(chips):
            v = st1[l, zz]
            gap = v * inverse - mean
            square = square + pltpu.roll(v, 8 - maps_here, 0) + sizes * gap * gap
        tile = jnp.where(row8 < maps_here, mean, pltpu.roll(square, maps_here, 0))
        send_m(l, jnp.where(row8 < 2 * maps_here, tile, 0.0))
        if not first:

            @pl.when(l == LAYERS - 1)
            def _():
                g_partner.wait_recv()
                wait_x_halo(2)
                lax.fori_loop(0, maps_here, unpool, 0)

        wait_m(l)
        at_copy(l).start()
        if first:
            send_gradients()
        averages = jnp.zeros((8, half), F32)
        scalings = jnp.zeros((8, half), F32)
        for a in range(maps_here):
            count = cnt_t[a : a + 1, :]
            average = jnp.zeros((8, half), F32)
            for mm in range(PLANE):
                average = average + coef[a, mm] * nall[mm] * st2[l, mm]
            average = jnp.sum(average, 0, keepdims=True) / count
            variance = jnp.zeros((8, half), F32)
            for mm in range(PLANE):
                v = st2[l, mm]
                gap = v - average
                variance = variance + coef[a, mm] * (
                    pltpu.roll(v, 8 - maps_here, 0) + nall[mm] * gap * gap
                )
            variance = jnp.sum(variance, 0, keepdims=True) / count
            averages = jnp.where(row8 == a, average, averages)
            scalings = jnp.where(row8 == a, lax.rsqrt(variance + epsilon), scalings)
        avg_t[l] = averages
        scl_t[l] = scalings
        wait_halo(z_halo, l)

        def activate(a, s):
            gain, shift = gain_of(l), shift_of(l)
            for n in tiles:
                average = row_of(avg_t, l, a)[:, n]
                factor = row_of(scl_t, l, a)[:, n] * gain[:, n]
                for rr in range(band + 2):
                    if rr in (0, band + 1):
                        way = rr // (band + 1)
                        v = zh[l, way, a, :, n].astype(F32) + row_of(mean_t, way, a)[:, n]
                        zbuf[l, a, rr, :, n] = v
                    else:
                        v = zbuf[l, a, rr, :, n]
                    y = (v - average) * factor + shift[:, n]
                    h = jnp.where(column[:, n] < limit(a, rr), y * jax.nn.sigmoid(y), 0.0)
                    act_own[lax.rem(l + 1, 2), a, rr, :, n] = h.astype(BF16)

            @pl.when(l < LAYERS - 1)
            def _():
                act_copy(l + 1, a).start()

            return s

        if first:
            for copy in x_partner:
                copy.wait_send()
            sent_x_halo(0, 2)
            each_x_pass(lambda copy: copy.wait_send())
        else:

            @pl.when(l == 2)
            def _():
                for a in range(maps_here):
                    act_copy(1, a).wait_send()

        lax.fori_loop(0, maps_here, activate, 0)

    forward(0, True)
    lax.fori_loop(1, LAYERS, lambda l, s: (forward(l, False), s)[1], 0)


    def pool():
        def one(a, s):
            for pr in range(2):
                total = jnp.zeros((PAD // 2, half), F32)
                position = gbuf[1 + pr, 1, a]
                for lower in range(2):
                    v = act_own[LAYERS % 2, a, 1 + 2 * pr + lower].astype(F32)
                    for n in range(lanes):
                        hrow[n] = v[:, n * 128 : (n + 1) * 128]
                    for b in range(2):
                        v = jnp.concatenate(
                            [hrow[n, pl.ds(b, PAD // 2, stride=2), :] for n in range(lanes)], 1
                        )
                        total = total + jnp.where(position == float(2 * lower + b), v, 0.0)
                pbuf[pr, a] = total.astype(BF16)
            return s

        lax.fori_loop(0, maps_here, one, 0)

    def second_rows(bit):
        return pl.ds(pl.multiple_of(bit * (half // 2), half // 2), half // 2)

    def piece_rows(p):
        return pl.ds(pl.multiple_of(p * piece, piece), piece)

    def term_slot(q):
        return lax.rem(q, 2 * TAPS)

    def c2(q):
        src = terms.at[term_slot(q), second_rows(1 - h_bit)]
        return remote(src, r2.at[q], r2_s.at[q], r2_r.at[q], h_peer, z, c)

    def z_of(n):
        return 2 * n + 1 - lax.rem(n, 2)

    def cf(q):
        passive_z = 2 * pair + turn
        there = active_z + passive_z - z
        return remote(r2.at[q], rf.at[term_slot(q)], rf_s.at[q], rf_r.at[q], m, there, c)

    def c3(q, p):
        slot = lax.rem(pair - p + actives - 1, actives)
        return remote(
            r2.at[q, piece_rows(p)], r3.at[q, slot], r3_s.at[q, p], r3_r.at[q, slot], m, z_of(p), c
        )

    def others(first, body, limit):
        def one(k):
            n = lax.rem(pair + k, actives)

            @pl.when(n < limit)
            def _():
                body(n)

        each(first, actives, one)

    def unit_of(q):
        k = lax.div(q, TAPS)
        return (LAYERS - 1 - k) * TAPS + (q - k * TAPS)

    def region(q, start, size, lane, lanes):
        start = pl.multiple_of(c * half + start, piece)
        lane = pl.multiple_of(lane, half)
        return kg_ref.at[unit_of(q), pl.ds(start, size), pl.ds(lane, lanes)]

    def cz(q, p, n):
        part = region(q, h_bit * (half // 2) + p * piece, piece, g_bit * half, half)
        return remote(fin.at[q], part, az_s.at[q, n], az_r.at[q, p], m, z_of(n), c)

    def cl(q):
        part = region(q, h_bit * (half // 2) + pair * piece, piece, g_bit * half, half)
        return pltpu.make_async_copy(fin.at[q], part, loc_s.at[q])

    def cu(q):
        passive_z = 2 * pair + turn
        there = active_z + passive_z - z
        part = region(q, h_bit * (half // 2), half // 2, g_bit * half, half)
        return remote(part, part, af_s.at[q], af_r.at[q], m, there, c)

    def cb(q):
        part = region(q, h_bit * (half // 2), half // 2, g_bit * half, half)
        return remote(part, part, ab_s.at[q], ab_r.at[q], h_peer, z, c)

    def ca(q):
        part = region(q, 0, half, g_bit * half, half)
        return remote(part, part, aa_s.at[q], aa_r.at[q], g_peer, z, c)

    def plan(q):
        k = lax.rem(q, 5)
        both = jnp.logical_or(lax.rem(k, 2) == 0, q >= UNITS - 5)
        mine = jnp.logical_or(both, lax.div(k, 2) == role)
        return mine, jnp.logical_and(mine, jnp.logical_not(both)), jnp.logical_not(mine)

    def ce(q):
        passive_z = 2 * pair + turn
        there = active_z + passive_z - z
        part = region(q, 0, half, (1 - g_bit) * half, half)
        return remote(part, part, ae_s.at[q], ae_r.at[q], m, there, c)

    def cp_part(q, start, size, lane, lanes):
        part = region(q, start, size, lane, lanes)
        return remote(part, part, ap_s.at[q], ap_r.at[q], m, z, other)

    def cp(q):
        return cp_part(q, 0, half, 0, 2 * half)

    def cp_rows(q, bit):
        return cp_part(q, bit * (half // 2), half // 2, g_bit * half, half)

    def cp_lanes(q):
        return cp_part(q, 0, half, (1 - g_bit) * half, half)

    def ready_terms(l):
        at_copy(l).wait_recv()
        for chip in range(2):
            for a in range(maps_here):
                first = a * (band + 2) * PAD
                rows = act_t[l, chip, :, first : first + (band + 2) * PAD]
                act_b[chip, :, a * band * PAD : (a + 1) * band * PAD] = rows[:, PAD : PAD + band * PAD]
        slot = lax.rem(l, 2)

        def variants(a, s):
            dzr_copy(l, a, 0).wait_recv()
            for chip in range(2):
                for rr in range(band):
                    for n in tiles:
                        if chip == 0:
                            mine, theirs = dz_own[slot, a, 1 + rr, :, n], dz_oth[slot, a, 1 + rr, :, n]
                            v = jnp.where(g_bit == c, mine, theirs)
                        else:
                            v = dzr[l, a, rr, :, n]
                        dzv[1, chip, a, rr, :, n] = v
                        v = v.astype(F32)
                        dzv[0, chip, a, rr, :, n] = pltpu.roll(v, PAD - 1, 0).astype(BF16)
                        dzv[2, chip, a, rr, :, n] = pltpu.roll(v, 1, 0).astype(BF16)
            return s

        lax.fori_loop(0, maps_here, variants, 0)

    def tap_terms(l, i, j):
        if i == 1:
            lhs = [act_b[0], act_b[1]]
        else:
            lhs = []
            for chip in range(2):
                for a in range(maps_here):
                    first = (a * (band + 2) + i) * PAD
                    lhs.append(act_t[l, chip, :, first : first + band * PAD])
        rhs = dzv[j].reshape(2 * pixels, half)
        q = (LAYERS - 1 - l) * TAPS + 3 * i + j
        got = jnp.dot(jnp.concatenate(lhs, 1), rhs, preferred_element_type=F32)
        terms[term_slot(q)] = got.astype(BF16)

    def weight_terms(l, i):
        lax.fori_loop(0, 3, lambda j, s: (tap_terms(l, i, j), s)[1], 0)

    def stage_second(q):
        c2(q).wait()
        kept = terms[term_slot(q), second_rows(h_bit)].astype(F32)
        r2[q] = (r2[q].astype(F32) + kept).astype(BF16)

        @pl.when(is_passive)
        def _():
            cf(q).start()

    def stage_fold(q):
        @pl.when(is_active)
        def _():
            cf(q).wait_recv()
            r2[q] = (r2[q].astype(F32) + rf[term_slot(q)].astype(F32)).astype(BF16)
            others(1, lambda n: c3(q, n).start(), owners)

    def stage_sum(q):
        @pl.when(is_owner)
        def _():
            for k in range(actives - 1):
                remote(
                    r3.at[q, k], r3.at[q, k], r3_s.at[q, 0], r3_r.at[q, k], m, z, c
                ).wait_recv()
            total = r2[q, piece_rows(pair)].astype(F32)
            for k in range(actives - 1):
                total = total + r3[q, k].astype(F32)
            fin[q] = total.astype(BF16)
            others(1, lambda n: cz(q, pair, n).start(), actives)
            cl(q).start()

    def stage_back(q):
        @pl.when(is_active)
        def _():
            others(1, lambda n: cz(q, n, n).wait_recv(), owners)

        @pl.when(is_owner)
        def _():
            cl(q).wait()

        @pl.when(is_active)
        def _():
            cu(q).start()

        @pl.when(is_passive)
        def _():
            cu(q).wait_recv()

        cb(q).start()
        cp_rows(q, h_bit).start()

    def stage_first(q):
        cb(q).wait_recv()
        mine, _, _ = plan(q)

        @pl.when(mine)
        def _():
            ca(q).start()

        cp_rows(q, 1 - h_bit).start()

        @pl.when(is_active)
        def _():
            others(1, lambda n: c3(q, n).wait_send(), owners)

        @pl.when(is_passive)
        def _():
            cf(q).wait_send()

    def stage_chip(q):
        mine, for_both, _ = plan(q)

        @pl.when(mine)
        def _():
            ca(q).wait_recv()

        @pl.when(for_both)
        def _():
            ce(q).start()

        @pl.when(mine)
        def _():
            cp_lanes(q).start()

        @pl.when(is_owner)
        def _():
            others(1, lambda n: cz(q, pair, n).wait_send(), actives)

        @pl.when(is_active)
        def _():
            cu(q).wait_send()

    def stage_late(q):
        _, _, not_mine = plan(q)

        @pl.when(not_mine)
        def _():
            ce(q).wait_recv()
            cp_lanes(q).start()

    def stage_done(q):
        mine, for_both, _ = plan(q)
        cb(q).wait_send()

        @pl.when(mine)
        def _():
            ca(q).wait_send()

        @pl.when(for_both)
        def _():
            ce(q).wait_send()

        cp(q).wait()

    def run(stage, first, last):
        lax.fori_loop(first, last, lambda q, s: (stage(q), s)[1], 0)

    def input_side(l, early):
        def arrive():
            weight_copy(l, 2).wait()
            for a in range(maps_here):
                dz_copy(l, a).wait_recv()

        products(dz_own, l, (0, 1, 2), wa, True, True)
        if early:
            arrive()
        products(dz_oth, l, (0, 1, 2), wb, True, False)

        def gather(a, s):
            for n in tiles:
                for rr in range(band):
                    v = shifted(a, rr, 2, 0, n)
                    dh[a, rr, :, n] = v
                    if rr in (0, band - 1):
                        dhs[rr // (band - 1), a, :, n] = v.astype(BF16)
            return s

        lax.fori_loop(0, maps_here, gather, 0)

    def sent_dz(l):
        for a in range(maps_here):
            dz_copy(l, a).wait_send()
            for way in range(2):
                if_wanted(way, dzr_copy(l, a, way).wait_send)

    def backward(k, carry):
        l = LAYERS - 1 - k
        gain, shift = gain_of(l), shift_of(l)

        def gradient(a, rr, n):
            zhat = (zbuf[l, a, rr, :, n] - row_of(avg_t, l, a)[:, n]) * row_of(scl_t, l, a)[:, n]
            y = zhat * gain[:, n] + shift[:, n]
            s = jax.nn.sigmoid(y)
            if rr in (0, band + 1):
                upstream = dhh[l, rr // (band + 1), a, :, n].astype(F32)
            else:
                upstream = dh[a, rr - 1, :, n]
            dy = upstream * (s * (1.0 + y * (1.0 - s)))
            dy = jnp.where(column[:, n] < limit(a, rr), dy, 0.0)
            return dy, zhat

        def collect(a, tile):
            plains, crosses = [], []
            for n in tiles:
                plain = jnp.zeros((PAD, 128), F32)
                crossed = jnp.zeros((PAD, 128), F32)
                for rr in range(1, band + 1):
                    dy, zhat = gradient(a, rr, n)
                    dh[a, rr - 1, :, n] = dy
                    plain = plain + dy
                    crossed = crossed + dy * zhat
                plains.append(jnp.sum(plain, 0, keepdims=True))
                crosses.append(jnp.sum(crossed, 0, keepdims=True))
            tile = jnp.where(row8 == a, jnp.concatenate(plains, 1), tile)
            return jnp.where(row8 == a + maps_here, jnp.concatenate(crosses, 1), tile)

        e = LAYERS + l
        tile = lax.fori_loop(0, maps_here, collect, jnp.zeros((8, half), F32))
        send_z(e, tile)

        @pl.when(k == LAYERS - 1)
        def _():
            run(stage_second, 0, TAPS)

        @pl.when(k > 0)
        def _():
            ready_terms(l + 1)
            weight_terms(l + 1, 0)

        wait_z(e)
        total = st1[e, 0]
        for zz in range(1, chips):
            total = total + st1[e, zz]
        send_m(e, total)

        @pl.when(k > 0)
        def _():
            first = (LAYERS - 2 - l) * TAPS
            run(lambda q: c2(q).start(), first, first + 3)
            weight_terms(l + 1, 1)
            run(lambda q: c2(q).start(), first + 3, first + 6)
            weight_terms(l + 1, 2)
            run(lambda q: c2(q).start(), first + 6, first + 9)
            wait_halo(dh_halo, l)

        @pl.when(k == 0)
        def _():
            pool()

        wait_m(e)
        total = st2[e, 0]
        for mm in range(1, PLANE):
            total = total + st2[e, mm]
        sums_own[pl.ds(l, 1), :] = jnp.sum(
            jnp.where(row8 >= maps_here, total, 0.0), 0, keepdims=True
        )
        sums_own[pl.ds(LAYERS + l, 1), :] = jnp.sum(
            jnp.where(row8 < maps_here, total, 0.0), 0, keepdims=True
        )
        plains = jnp.zeros((8, half), F32)
        crosses = jnp.zeros((8, half), F32)
        for a in range(maps_here):
            plain = jnp.zeros((8, half), F32)
            crossed = jnp.zeros((8, half), F32)
            for mm in range(PLANE):
                v = st2[e, mm]
                plain = plain + coef[a, mm] * v
                crossed = crossed + coef[a, mm] * pltpu.roll(v, 8 - maps_here, 0)
            count = cnt_t[a : a + 1, :]
            plain = gain * (jnp.sum(plain, 0, keepdims=True) / count)
            crossed = gain * (jnp.sum(crossed, 0, keepdims=True) / count)
            plains = jnp.where(row8 == a, plain, plains)
            crosses = jnp.where(row8 == a, crossed, crosses)
        tb_t[0] = plains
        ta_t[0] = crosses

        def settle(a, s):
            for n in tiles:
                average, scaling = row_of(avg_t, l, a)[:, n], row_of(scl_t, l, a)[:, n]
                plain, crossed = row_of(tb_t, 0, a)[:, n], row_of(ta_t, 0, a)[:, n]
                for rr in range(band + 2):
                    if rr in (0, band + 1):
                        dy, zhat = gradient(a, rr, n)
                    else:
                        dy = dh[a, rr - 1, :, n]
                        zhat = (zbuf[l, a, rr, :, n] - average) * scaling
                    v = scaling * (dy * gain[:, n] - plain - zhat * crossed)
                    v = jnp.where(column[:, n] < limit(a, rr), v, 0.0)
                    dz_own[lax.rem(l, 2), a, rr, :, n] = v.astype(BF16)
            dz_copy(l, a).start()
            for way in range(2):
                if_wanted(way, dzr_copy(l, a, way).start)
            return s

        @pl.when(k == 2)
        def _():
            sent_dz(LAYERS - 1)

        lax.fori_loop(0, maps_here, settle, 0)
        @pl.when(l > 0)
        def _():
            input_side(l, True)
            start_halo(dh_halo, l - 1)

        return carry

    lax.fori_loop(0, LAYERS, backward, 0)
    weight_copy(0, 2).wait()
    for a in range(maps_here):
        dz_copy(0, a).wait_recv()

    def input_rows(a, s):
        for rr in range(band):
            dh[a, rr] = jnp.where(column < width_of(a), dh[a, rr], 0.0)
        return s

    outs = (
        (
            remote(dh.at[:, pl.ds(2 * other, 2)], ig_ref.at[c], out_s.at[0], out_r.at[0], m, z, other),
            pltpu.make_async_copy(dh.at[:, pl.ds(2 * c, 2)], ig_ref.at[c], out_l.at[0]),
        ),
        (
            remote(pbuf.at[other], pooled_ref.at[c], out_s.at[1], out_r.at[1], m, z, other),
            pltpu.make_async_copy(pbuf.at[c], pooled_ref.at[c], out_l.at[1]),
        ),
        (
            remote(sums_own, sums_ref.at[c], out_s.at[2], out_r.at[2], m, z, other),
            pltpu.make_async_copy(sums_own, sums_ref.at[c], out_l.at[2]),
        ),
    )

    g_partner.wait_send()
    sent_x_halo(2, 4)

    def sent(e, carry):
        each(1, chips, lambda k: z_copy(e, k).wait_send())
        each(1, PLANE, lambda k: m_copy(e, k).wait_send())
        return carry

    lax.fori_loop(0, 2 * LAYERS, sent, 0)
    for l in range(LAYERS):
        at_copy(l).wait_send()
    for l in range(LAYERS - 1):
        sent_dz(l)

    def drain(s, carry):
        @pl.when(s == EARLY)
        def _():
            ready_terms(0)

        @pl.when(s == EARLY + TAPS + 2)
        def _():
            input_side(0, False)
            lax.fori_loop(0, maps_here, input_rows, 0)
            for there, here in outs:
                there.start()
                here.start()

        for i in range(3):
            j = s - EARLY - 3 * i

            @pl.when(jnp.logical_and(j >= 0, j < 3))
            def _(i=i, j=j):
                tap_terms(0, i, j)
                c2(2 * TAPS + 3 * i + j).start()

        for stage, first, lag in (
            (stage_done, 0, 2 * FOLD + 4 * LAG),
            (stage_late, 0, 2 * FOLD + 3 * LAG),
            (stage_chip, 0, 2 * FOLD + 2 * LAG),
            (stage_first, 0, 2 * FOLD + LAG),
            (stage_back, 0, 2 * FOLD),
            (stage_sum, 0, FOLD),
            (stage_fold, 0, 0),
            (stage_second, TAPS, 0),
        ):
            q = first + s - lag

            @pl.when(jnp.logical_and(q >= first, q < UNITS))
            def _(stage=stage, q=q):
                stage(q)

        return carry

    lax.fori_loop(0, UNITS + 2 * FOLD + 4 * LAG, drain, 0)
    for a in range(maps_here):
        act_copy(2, a).wait_send()
    for there, here in outs:
        there.wait()
        here.wait()


def solution(mesh):
    chips = mesh.shape["rows"] // 2

    def per_device(
        block_input,
        conv_weights,
        norm_gains,
        norm_shifts,
        map_width,
        map_group,
        pool_index,
        task_mask,
        task_weights,
        task_grads,
    ):
        maps_here, rows_here, columns, channels = block_input.shape
        pooled_columns = pool_index.shape[2]
        height = rows_here * mesh.shape["rows"]
        half = channels // 2
        band = 2 * rows_here
        pixels = maps_here * band * PAD
        actives = chips // 2
        owners = min(actives, 8)
        piece = half // 2 // owners
        rounds = 2 * LAYERS
        slots = 2 * UNITS * (actives - 1) * piece * half + 4 * rounds * chips * 8 * half
        grant = (36 * 1024 + 256) * 1024 + slots
        vmem, dma = pltpu.VMEM, pltpu.SemaphoreType.DMA
        tile = (maps_here, band + 2, PAD, half)
        edge = (2, maps_here, PAD, half)
        whole = pl.BlockSpec(memory_space=pltpu.VMEM)
        outside = pl.BlockSpec(memory_space=pltpu.HBM)
        index_rows = jnp.transpose(pool_index, (0, 2, 1, 3))
        anywhere = pl.BlockSpec(memory_space=pl.ANY)
        pooled, ig, kg, sums = pl.pallas_call(
            functools.partial(block_kernel, chips, height),
            out_shape=(
                jax.ShapeDtypeStruct((2, maps_here, PAD // 2, half), BF16),
                jax.ShapeDtypeStruct((2, maps_here, rows_here, PAD, half), F32),
                jax.ShapeDtypeStruct((UNITS, channels, channels), BF16),
                jax.ShapeDtypeStruct((2, 8, half), F32),
            ),
            in_specs=[whole, anywhere] + [outside] * 8,
            out_specs=[anywhere] * 4,
            scratch_shapes=[
                vmem(norm_gains.shape, F32),
                vmem(norm_shifts.shape, F32),
                pltpu.SMEM(map_width.shape, jnp.int32),
                pltpu.SMEM(map_group.shape, jnp.int32),
                vmem((maps_here, pooled_columns, channels), jnp.int32),
                pltpu.SMEM(task_mask.shape, jnp.int32),
                pltpu.SMEM(task_weights.shape, F32),
                vmem(task_grads.shape, BF16),
                vmem((LAYERS, 3, 3, half, half), BF16),
                vmem((LAYERS, 3, 3, half, half), BF16),
                vmem((2,) + tile, BF16),
                vmem((2,) + tile, BF16),
                vmem((LAYERS, 2, half, maps_here * (band + 2) * PAD), BF16),
                vmem((2, half, pixels), BF16),
                vmem((LAYERS,) + tile, F32),
                vmem(edge, BF16),
                vmem((LAYERS,) + edge, BF16),
                vmem((maps_here, band, PAD, half), F32),
                vmem(edge, BF16),
                vmem((LAYERS,) + edge, BF16),
                vmem((2,) + tile, BF16),
                vmem((2,) + tile, BF16),
                vmem((LAYERS, maps_here, band, PAD, half), BF16),
                vmem((3, 2, maps_here, band, PAD, half), BF16),
                vmem((3, pixels, half), F32),
                vmem((2, 2, maps_here, PAD // 2, half), F32),
                vmem((4, 2, maps_here, PAD // 2, half), F32),
                vmem((half // 128, PAD, 128), F32),
                vmem((2, maps_here, PAD // 2, half), BF16),
                vmem((rounds, chips, 8, half), F32),
                vmem((rounds, PLANE, 8, half), F32),
                vmem((maps_here, PLANE, 8, half), F32),
                vmem((PLANE, 8, half), F32),
                vmem((2, 8, half), F32),
                vmem((8, half), F32),
                vmem((LAYERS, 8, half), F32),
                vmem((LAYERS, 8, half), F32),
                vmem((2, 8, half), F32),
                vmem((1, 8, half), F32),
                vmem((1, 8, half), F32),
                vmem((8, half), F32),
                vmem((2 * TAPS, half, half), BF16),
                vmem((UNITS, half // 2, half), BF16),
                vmem((2 * TAPS, half // 2, half), BF16),
                vmem((UNITS, actives - 1, piece, half), BF16),
                vmem((UNITS, piece, half), BF16),
                dma((8,)),
                dma((LAYERS, 3)),
                dma((6,)),
                dma((6,)),
                dma((3,)),
                dma((3,)),
                dma((rounds, chips)),
                dma((rounds, chips)),
                dma((rounds, PLANE)),
                dma((rounds, PLANE)),
                dma((LAYERS, 2)),
                dma((LAYERS, 2)),
                dma((LAYERS, 2)),
                dma((LAYERS, 2)),
                dma((LAYERS, maps_here)),
                dma((LAYERS, maps_here)),
                dma((LAYERS, maps_here)),
                dma((LAYERS, maps_here)),
                dma((3,)),
                dma((3,)),
                dma((3,)),
                dma((LAYERS,)),
                dma((LAYERS,)),
                dma((LAYERS, 2, maps_here)),
                dma((LAYERS, maps_here)),
                dma((UNITS,)),
                dma((UNITS,)),
                dma((UNITS,)),
                dma((UNITS,)),
                dma((UNITS, owners)),
                dma((UNITS, actives - 1)),
                dma((UNITS, actives)),
                dma((UNITS, owners)),
                dma((UNITS,)),
                dma((UNITS,)),
                dma((UNITS,)),
                dma((UNITS,)),
                dma((UNITS,)),
                dma((UNITS,)),
                dma((UNITS,)),
                dma((UNITS,)),
                dma((UNITS,)),
                dma((UNITS,)),
                dma((UNITS,)),
            ],
            compiler_params=pltpu.CompilerParams(
                collective_id=0,
                has_side_effects=True,
                vmem_limit_bytes=grant,
            ),
        )(
            block_input,
            conv_weights,
            *(
                pltpu.with_memory_space_constraint(v, pltpu.HBM)
                for v in (
                    norm_gains,
                    norm_shifts,
                    map_width,
                    map_group,
                    index_rows,
                    task_mask,
                    task_weights,
                    task_grads,
                )
            ),
        )
        pooled = jnp.concatenate([pooled[0], pooled[1]], -1)[:, None, :pooled_columns]
        input_grad = jnp.concatenate([ig[0], ig[1]], -1)[:, :, :columns]
        sums = jnp.concatenate([sums[0], sums[1]], -1)
        return (
            pooled,
            input_grad,
            kg.astype(F32).reshape(conv_weights.shape),
            sums[:LAYERS],
            sums[LAYERS : 2 * LAYERS],
        )

    return jax.shard_map(
        per_device,
        mesh=mesh,
        in_specs=(
            P("maps", "rows", None, None),
            P(),
            P(),
            P(),
            P(),
            P(),
            P("maps", "rows", None, None),
            P("maps", None),
            P(),
            P(None, "maps", "rows", None, None),
        ),
        out_specs=(P("maps", "rows", None, None), P("maps", "rows", None, None), P(), P(), P()),
        check_vma=False,
    )
```

```python
import functools

import jax
import jax.numpy as jnp
from jax import lax
from jax.experimental import pallas as pl
from jax.experimental.pallas import tpu as pltpu
from jax.sharding import PartitionSpec as P

MESH = pl.DeviceIdType.MESH
epsilon = 1e-05
PAD = 64
LAYERS = 3
TAPS = 9
UNITS = LAYERS * TAPS
PLANE = 4
LAG = 4
EARLY = 1
FOLD = 2
F32 = jnp.float32
BF16 = jnp.bfloat16


def each(first, last, body):
    if last - first <= 8:
        for k in range(first, last):
            body(k)
    else:
        lax.fori_loop(first, last, lambda k, s: (body(k), s)[1], 0)


def block_kernel(
    chips,
    height,
    x_ref,
    w_ref,
    gain_hbm,
    shift_hbm,
    width_hbm,
    group_hbm,
    index_hbm,
    tmask_hbm,
    tweight_hbm,
    tgrad_hbm,
    pooled_ref,
    ig_ref,
    kg_ref,
    sums_ref,
    gain_ref,
    shift_ref,
    width_ref,
    group_ref,
    index_ref,
    tmask_ref,
    tweight_ref,
    tgrad_ref,
    wa,
    wb,
    act_own,
    act_oth,
    act_t,
    act_b,
    zbuf,
    zs,
    zh,
    dh,
    dhs,
    dhh,
    dz_own,
    dz_oth,
    dzr,
    dzv,
    prod,
    gsrc,
    gbuf,
    hrow,
    pbuf,
    st1,
    st2,
    coef,
    nall,
    inv_t,
    cnt_t,
    avg_t,
    scl_t,
    mean_t,
    tb_t,
    ta_t,
    sums_own,
    terms,
    r2,
    rf,
    r3,
    fin,
    in_sem,
    w_sem,
    x_s,
    x_r,
    g_s,
    g_r,
    st1_s,
    st1_r,
    st2_s,
    st2_r,
    zh_s,
    zh_r,
    dh_s,
    dh_r,
    act_s,
    act_r,
    dz_s,
    dz_r,
    out_s,
    out_r,
    out_l,
    at_s,
    at_r,
    dzr_s,
    dzr_r,
    r2_s,
    r2_r,
    rf_s,
    rf_r,
    r3_s,
    r3_r,
    az_s,
    az_r,
    af_s,
    af_r,
    ab_s,
    ab_r,
    aa_s,
    aa_r,
    ae_s,
    ae_r,
    ap_s,
    ap_r,
    loc_s,
):
    maps_here = x_ref.shape[0]
    columns = x_ref.shape[2]
    half = x_ref.shape[3] // 2
    tasks = tgrad_ref.shape[0]
    pooled_columns = tgrad_ref.shape[3]
    lanes = half // 128
    tiles = [slice(n * 128, (n + 1) * 128) for n in range(lanes)]
    band = 4
    pixels = maps_here * band * PAD
    actives = chips // 2
    owners = min(actives, 8)
    piece = (half // 2) // owners
    m = lax.axis_index("maps")
    r = lax.axis_index("rows")
    c = lax.rem(r, 2)
    z = lax.div(r, 2)
    other = 1 - c
    first_map = m * maps_here
    x_bit = lax.rem(m, 2)
    y_bit = lax.div(m, 2)
    x_peer = m + 1 - 2 * x_bit
    y_peer = m + 2 - 4 * y_bit
    g_bit = (1 - c) * x_bit + c * y_bit
    h_bit = (1 - c) * y_bit + c * x_bit
    g_peer = (1 - c) * x_peer + c * y_peer
    h_peer = (1 - c) * y_peer + c * x_peer
    pair = lax.div(z, 2)
    turn = lax.rem(pair, 2)
    active_z = 2 * pair + 1 - turn
    is_active = z == active_z
    is_passive = z != active_z
    is_owner = jnp.logical_and(is_active, pair < owners)
    role = jnp.where(is_active, 0, 1)
    up_there = z > 0
    down_there = z < chips - 1
    row8 = lax.broadcasted_iota(jnp.int32, (8, half), 0)
    column = lax.broadcasted_iota(jnp.int32, (PAD, half), 0)

    def remote(src, dst, send, recv, mm, zz, cc):
        return pltpu.make_async_remote_copy(
            src_ref=src,
            dst_ref=dst,
            send_sem=send,
            recv_sem=recv,
            device_id=(mm, zz * 2 + cc),
            device_id_type=MESH,
        )

    def own_half(v):
        return jnp.where(c == 0, v[..., :half], v[..., half:])

    def width_of(a):
        return width_ref[first_map + a]

    own_at = pl.ds(pl.multiple_of(c * half, half), half)
    oth_at = pl.ds(pl.multiple_of(other * half, half), half)

    def weight_copy(l, n):
        dst = (wa, wb, wb)[n]
        k_at, o_at = ((own_at, own_at), (oth_at, own_at), (own_at, oth_at))[n]
        return pltpu.make_async_copy(w_ref.at[l, :, :, k_at, o_at], dst.at[l], w_sem.at[l, n])

    fetches = [
        pltpu.make_async_copy(src, dst, in_sem.at[n])
        for n, (src, dst) in enumerate(
            (
                (width_hbm, width_ref),
                (group_hbm, group_ref),
                (tmask_hbm, tmask_ref),
                (tweight_hbm, tweight_ref),
                (gain_hbm, gain_ref),
                (shift_hbm, shift_ref),
                (index_hbm.at[:, :, 0, :], index_ref),
                (tgrad_hbm, tgrad_ref),
            )
        )
    ]
    for fetch in fetches:
        fetch.start()
    for l in range(LAYERS):
        weight_copy(l, 0).start()
        weight_copy(l, 1).start()

    barrier = pltpu.get_barrier_semaphore()

    def greet(k):
        rr = lax.rem(r + k, 2 * chips)
        pl.semaphore_signal(barrier, inc=1, device_id=(m, rr), device_id_type=MESH)

    each(1, 2 * chips, greet)
    for k in range(1, PLANE):
        for core in (c, other):
            there = (lax.rem(m + k, PLANE), z * 2 + core)
            pl.semaphore_signal(barrier, inc=1, device_id=there, device_id_type=MESH)

    for fetch in fetches:
        fetch.wait()

    mine = pl.ds(1 + 2 * c, 2)
    for a in range(maps_here):
        inside = lax.broadcasted_iota(jnp.int32, (columns, 2 * half), 0) < width_of(a)
        for rr in range(2):
            v = jnp.where(inside, x_ref[a, rr].astype(F32), 0.0).astype(BF16)
            spot = 1 + 2 * c + rr
            act_own[0, a, spot, pl.ds(48, 16), :] = jnp.zeros((16, half), BF16)
            act_oth[0, a, spot, pl.ds(48, 16), :] = jnp.zeros((16, half), BF16)
            act_own[0, a, spot, pl.ds(0, columns), :] = own_half(v)
            act_oth[0, a, spot, pl.ds(0, columns), :] = jnp.where(
                c == 0, v[:, half:], v[:, :half]
            )

    @pl.when(z == 0)
    def _():
        act_own[0, :, 0] = jnp.zeros((maps_here, PAD, half), BF16)
        act_oth[0, :, 0] = jnp.zeros((maps_here, PAD, half), BF16)

    @pl.when(z == chips - 1)
    def _():
        act_own[0, :, 5] = jnp.zeros((maps_here, PAD, half), BF16)
        act_oth[0, :, 5] = jnp.zeros((maps_here, PAD, half), BF16)

    pl.semaphore_wait(barrier, 2 * chips - 1 + 2 * (PLANE - 1))

    x_partner = (
        remote(act_own.at[0, :, mine], act_oth.at[0, :, mine], x_s.at[0], x_r.at[0], m, z, other),
        remote(act_oth.at[0, :, mine], act_own.at[0, :, mine], x_s.at[1], x_r.at[1], m, z, other),
    )
    g_partner = remote(gsrc.at[other], gbuf.at[1 + c], g_s.at[0], g_r.at[0], m, z, other)

    def x_halo(n, src_row, dst_row, zz):
        cc = (c, other)[n % 2]
        low = dst_row == band + 1
        if n >= 2:
            src, dst = gsrc.at[cc], gbuf.at[3 if low else 0]
            return remote(src, dst, g_s.at[n - 1], g_r.at[1 if low else 2], m, zz, cc)
        src, dst = (act_own, act_oth)[n].at[0, :, src_row], act_own.at[0, :, dst_row]
        return remote(src, dst, x_s.at[2 + n], x_r.at[2 if low else 3], m, zz, cc)

    def x_pass(row):
        n = 4 if row == 0 else 5
        src, dst = act_own.at[0, :, row], act_oth.at[0, :, row]
        return remote(src, dst, x_s.at[n], x_r.at[n], m, z, other)

    for copy in x_partner:
        copy.start()

    @pl.when(jnp.logical_and(c == 0, up_there))
    def _():
        for n in range(2):
            x_halo(n, 1, 5, z - 1).start()

    @pl.when(jnp.logical_and(c == 1, down_there))
    def _():
        for n in range(2):
            x_halo(n, 4, 0, z + 1).start()

    gsrc[...] = jnp.zeros(gsrc.shape, F32)
    for a in range(maps_here):
        total = None
        for t in range(tasks):
            scale = tweight_ref[t] * tmask_ref[a, t].astype(F32)
            term = tgrad_ref[t, a, 0].astype(F32) * scale
            total = term if total is None else total + term
        position = index_ref[a].astype(F32)
        for h in range(2):
            gsrc[h, 0, a, pl.ds(0, pooled_columns), :] = total[:, h * half : (h + 1) * half]
            gsrc[h, 1, a, pl.ds(0, pooled_columns), :] = position[:, h * half : (h + 1) * half]
    gbuf[1 + c] = gsrc[c]

    for mm in range(PLANE):
        sizes = jnp.zeros((8, half), F32)
        for b in range(maps_here):
            sizes = jnp.where(
                row8 == b, (width_ref[mm * maps_here + b] * height).astype(F32), sizes
            )
        nall[mm] = sizes
    inside_sizes = jnp.zeros((8, half), F32)
    for b in range(maps_here):
        inside_sizes = jnp.where(row8 == b, (width_of(b) * band).astype(F32), inside_sizes)
    inv_t[0] = inside_sizes
    inv_t[1] = jnp.where(row8 < maps_here, 1.0 / jnp.maximum(inside_sizes, 1.0), 0.0)
    counts = jnp.ones((8, half), F32)
    for a in range(maps_here):
        total = jnp.zeros((1, half), F32)
        for mm in range(PLANE):
            same = jnp.zeros((8, half), F32)
            for b in range(maps_here):
                alike = group_ref[first_map + a] == group_ref[mm * maps_here + b]
                same = jnp.where(row8 == b, jnp.where(alike, 1.0, 0.0), same)
            coef[a, mm] = same
            total = total + jnp.sum(same * nall[mm], 0, keepdims=True)
        counts = jnp.where(row8 == a, total, counts)
    cnt_t[...] = counts

    def z_copy(e, k):
        zz = lax.rem(z + k, chips)
        return remote(st1.at[e, z], st1.at[e, z], st1_s.at[e, k], st1_r.at[e, z], m, zz, c)

    def z_arrival(e, k):
        zz = lax.rem(z + k, chips)
        return remote(st1.at[e, zz], st1.at[e, zz], st1_s.at[e, k], st1_r.at[e, zz], m, zz, c)

    def m_copy(e, k):
        mm = lax.rem(m + k, PLANE)
        return remote(st2.at[e, m], st2.at[e, m], st2_s.at[e, k], st2_r.at[e, m], mm, z, c)

    def m_arrival(e, k):
        mm = lax.rem(m + k, PLANE)
        return remote(st2.at[e, mm], st2.at[e, mm], st2_s.at[e, k], st2_r.at[e, mm], mm, z, c)

    def send_z(e, tile):
        st1[e, z] = tile
        each(1, chips, lambda k: z_copy(e, k).start())

    def wait_z(e):
        each(1, chips, lambda k: z_arrival(e, k).wait_recv())

    def send_m(e, tile):
        st2[e, m] = tile
        each(1, PLANE, lambda k: m_copy(e, k).start())

    def wait_m(e):
        each(1, PLANE, lambda k: m_arrival(e, k).wait_recv())

    def products(source, l, taps, kernel, transposed, fresh):
        starts = [2 - i if transposed else i for i in taps]
        lhs = jnp.concatenate(
            [source[lax.rem(l, 2), :, s : s + band].reshape(pixels, half) for s in starts], 1
        )
        for j in range(3):
            rhs = jnp.concatenate([kernel[l, i, j] for i in taps], 1 if transposed else 0)
            got = lax.dot_general(
                lhs,
                rhs,
                (((1,), (1 if transposed else 0,)), ((), ())),
                preferred_element_type=F32,
            )
            if fresh:
                prod[j] = got
            else:
                prod[j] = prod[j] + got

    def shifted(a, rr, before, behind, n):
        rows = pl.ds(pl.multiple_of((a * band + rr) * PAD, PAD), PAD)
        return (
            prod[1, rows, n]
            + pltpu.roll(prod[before, rows, n], 1, 0)
            + pltpu.roll(prod[behind, rows, n], PAD - 1, 0)
        )

    def row_of(table, l, a):
        return table[l, pl.ds(a, 1), :]

    def gain_of(l):
        return own_half(gain_ref[pl.ds(l, 1), :])

    def shift_of(l):
        return own_half(shift_ref[pl.ds(l, 1), :])

    def limit(a, rr):
        w = width_of(a)
        if rr == 0:
            return jnp.where(up_there, w, 0)
        if rr == band + 1:
            return jnp.where(down_there, w, 0)
        return w

    def z_halo(l, way):
        there = z - 1 + 2 * way
        return remote(zs.at[way], zh.at[l, 1 - way], zh_s.at[l, way], zh_r.at[l, way], m, there, c)

    def dh_halo(l, way):
        there = z - 1 + 2 * way
        return remote(dhs.at[way], dhh.at[l, 1 - way], dh_s.at[l, way], dh_r.at[l, way], m, there, c)

    def start_halo(halo, l):
        @pl.when(up_there)
        def _():
            halo(l, 0).start()

        @pl.when(down_there)
        def _():
            halo(l, 1).start()

    def wait_halo(halo, l):
        @pl.when(up_there)
        def _():
            halo(l, 1).wait_recv()
            halo(l, 0).wait_send()

        @pl.when(down_there)
        def _():
            halo(l, 0).wait_recv()
            halo(l, 1).wait_send()

    def act_copy(l, a):
        slot = lax.rem(l, 2)
        src, dst = act_own.at[slot, a], act_oth.at[slot, a]
        return remote(src, dst, act_s.at[l, a], act_r.at[l, a], m, z, other)

    def at_copy(l):
        return remote(act_t.at[l, 0], act_t.at[l, 1], at_s.at[l], at_r.at[l], g_peer, z, c)

    def dzr_copy(l, a, way):
        src, dst = dz_own.at[lax.rem(l, 2), a, pl.ds(1, band)], dzr.at[l, a]
        peer = (x_peer, y_peer)[way]
        return remote(src, dst, dzr_s.at[l, way, a], dzr_r.at[l, a], peer, z, way)

    def if_wanted(way, body):
        @pl.when((x_bit, y_bit)[way] + c == 1)
        def _():
            body()

    def dz_copy(l, a):
        slot = lax.rem(l, 2)
        src, dst = dz_own.at[slot, a], dz_oth.at[slot, a]
        return remote(src, dst, dz_s.at[l, a], dz_r.at[l, a], m, z, other)

    def send_gradients():
        g_partner.start()

        @pl.when(jnp.logical_and(c == 0, up_there))
        def _():
            for n in range(2, 4):
                x_halo(n, 1, 5, z - 1).start()

        @pl.when(jnp.logical_and(c == 1, down_there))
        def _():
            for n in range(2, 4):
                x_halo(n, 4, 0, z + 1).start()

    def if_there(way, body):
        @pl.when((up_there, down_there)[way])
        def _():
            body()

    def wait_x_halo(n):
        if_there(0, lambda: x_halo(n, 4, 0, z - 1).wait_recv())
        if_there(1, lambda: x_halo(n, 1, 5, z + 1).wait_recv())

    def each_x_pass(act):
        if_there(0, lambda: act(x_pass(0)))
        if_there(1, lambda: act(x_pass(band + 1)))

    def sent_x_halo(first, last):
        @pl.when(jnp.logical_and(c == 0, up_there))
        def _():
            for n in range(first, last):
                x_halo(n, 1, 5, z - 1).wait_send()

        @pl.when(jnp.logical_and(c == 1, down_there))
        def _():
            for n in range(first, last):
                x_halo(n, 4, 0, z + 1).wait_send()

    def unpool(a, s):
        for rr in range(band + 2):
            slot, lower = (rr + 1) // 2, (rr + 1) % 2
            g = gbuf[slot, 0, a]
            position = gbuf[slot, 1, a]
            for b in range(2):
                v = jnp.where(position == float(2 * lower + b), g, 0.0)
                for n in range(lanes):
                    hrow[n, pl.ds(b, PAD // 2, stride=2), :] = v[:, n * 128 : (n + 1) * 128]
            v = jnp.concatenate([hrow[n] for n in range(lanes)], 1)
            if rr in (0, band + 1):
                dhh[LAYERS - 1, rr // (band + 1), a] = v.astype(BF16)
            else:
                dh[a, rr - 1] = v
        return s

    def forward(l, first):
        weight_copy(l, 0).wait()
        weight_copy(l, 1).wait()
        if first:
            for copy in x_partner:
                copy.wait_recv()
            products(act_own, l, (1,), wa, False, True)
            products(act_oth, l, (1,), wb, False, False)
            wait_x_halo(0)
            each_x_pass(lambda copy: copy.start())
            products(act_own, l, (0, 2), wa, False, False)
            each_x_pass(lambda copy: copy.wait_recv())
            products(act_oth, l, (0, 2), wb, False, False)
        else:
            products(act_own, l, (0, 1, 2), wa, False, True)
            for a in range(maps_here):
                act_copy(l, a).wait_recv()
            products(act_oth, l, (0, 1, 2), wb, False, False)
        weight_copy(l, 2).start()

        def collect(a, tile):
            inside = column[:, :128] < width_of(a)
            pixels_inside = (width_of(a) * band).astype(F32)
            totals, squares = [], []
            for n in tiles:
                total = jnp.zeros((PAD, 128), F32)
                for rr in range(band):
                    v = shifted(a, rr, 0, 2, n)
                    zbuf[l, a, 1 + rr, :, n] = v
                    total = total + jnp.where(inside, v, 0.0)
                total = jnp.sum(total, 0, keepdims=True)
                mean = total / pixels_inside
                square = jnp.zeros((PAD, 128), F32)
                for rr in range(band):
                    v = jnp.where(inside, zbuf[l, a, 1 + rr, :, n] - mean, 0.0)
                    square = square + v * v
                    if rr in (0, band - 1):
                        zs[rr // (band - 1), a, :, n] = v.astype(BF16)
                totals.append(total)
                squares.append(jnp.sum(square, 0, keepdims=True))
            tile = jnp.where(row8 == a, jnp.concatenate(totals, 1), tile)
            return jnp.where(row8 == a + maps_here, jnp.concatenate(squares, 1), tile)

        tile = lax.fori_loop(0, maps_here, collect, jnp.zeros((8, half), F32))
        send_z(l, tile)
        start_halo(z_halo, l)
        act_t[l, 0] = act_own[lax.rem(l, 2)].reshape(maps_here * (band + 2) * PAD, half).T
        wait_z(l)
        sizes, inverse = inv_t[0], inv_t[1]
        mean_t[0] = st1[l, jnp.maximum(z - 1, 0)] * inverse
        mean_t[1] = st1[l, jnp.minimum(z + 1, chips - 1)] * inverse
        total = st1[l, 0]
        for zz in range(1, chips):
            total = total + st1[l, zz]
        mean = total * inverse * (1.0 / chips)
        square = jnp.zeros((8, half), F32)
        for zz in range(chips):
            v = st1[l, zz]
            gap = v * inverse - mean
            square = square + pltpu.roll(v, 8 - maps_here, 0) + sizes * gap * gap
        tile = jnp.where(row8 < maps_here, mean, pltpu.roll(square, maps_here, 0))
        send_m(l, jnp.where(row8 < 2 * maps_here, tile, 0.0))
        if not first:

            @pl.when(l == LAYERS - 1)
            def _():
                g_partner.wait_recv()
                wait_x_halo(2)
                lax.fori_loop(0, maps_here, unpool, 0)

        wait_m(l)
        at_copy(l).start()
        if first:
            send_gradients()
        averages = jnp.zeros((8, half), F32)
        scalings = jnp.zeros((8, half), F32)
        for a in range(maps_here):
            count = cnt_t[a : a + 1, :]
            average = jnp.zeros((8, half), F32)
            for mm in range(PLANE):
                average = average + coef[a, mm] * nall[mm] * st2[l, mm]
            average = jnp.sum(average, 0, keepdims=True) / count
            variance = jnp.zeros((8, half), F32)
            for mm in range(PLANE):
                v = st2[l, mm]
                gap = v - average
                variance = variance + coef[a, mm] * (
                    pltpu.roll(v, 8 - maps_here, 0) + nall[mm] * gap * gap
                )
            variance = jnp.sum(variance, 0, keepdims=True) / count
            averages = jnp.where(row8 == a, average, averages)
            scalings = jnp.where(row8 == a, lax.rsqrt(variance + epsilon), scalings)
        avg_t[l] = averages
        scl_t[l] = scalings
        wait_halo(z_halo, l)

        def activate(a, s):
            gain, shift = gain_of(l), shift_of(l)
            for n in tiles:
                average = row_of(avg_t, l, a)[:, n]
                factor = row_of(scl_t, l, a)[:, n] * gain[:, n]
                for rr in range(band + 2):
                    if rr in (0, band + 1):
                        way = rr // (band + 1)
                        v = zh[l, way, a, :, n].astype(F32) + row_of(mean_t, way, a)[:, n]
                        zbuf[l, a, rr, :, n] = v
                    else:
                        v = zbuf[l, a, rr, :, n]
                    y = (v - average) * factor + shift[:, n]
                    h = jnp.where(column[:, n] < limit(a, rr), y * jax.nn.sigmoid(y), 0.0)
                    act_own[lax.rem(l + 1, 2), a, rr, :, n] = h.astype(BF16)

            @pl.when(l < LAYERS - 1)
            def _():
                act_copy(l + 1, a).start()

            return s

        if first:
            for copy in x_partner:
                copy.wait_send()
            sent_x_halo(0, 2)
            each_x_pass(lambda copy: copy.wait_send())
        else:

            @pl.when(l == 2)
            def _():
                for a in range(maps_here):
                    act_copy(1, a).wait_send()

        lax.fori_loop(0, maps_here, activate, 0)

    forward(0, True)
    lax.fori_loop(1, LAYERS, lambda l, s: (forward(l, False), s)[1], 0)


    def pool():
        def one(a, s):
            for pr in range(2):
                total = jnp.zeros((PAD // 2, half), F32)
                position = gbuf[1 + pr, 1, a]
                for lower in range(2):
                    v = act_own[LAYERS % 2, a, 1 + 2 * pr + lower].astype(F32)
                    for n in range(lanes):
                        hrow[n] = v[:, n * 128 : (n + 1) * 128]
                    for b in range(2):
                        v = jnp.concatenate(
                            [hrow[n, pl.ds(b, PAD // 2, stride=2), :] for n in range(lanes)], 1
                        )
                        total = total + jnp.where(position == float(2 * lower + b), v, 0.0)
                pbuf[pr, a] = total.astype(BF16)
            return s

        lax.fori_loop(0, maps_here, one, 0)

    def second_rows(bit):
        return pl.ds(pl.multiple_of(bit * (half // 2), half // 2), half // 2)

    def piece_rows(p):
        return pl.ds(pl.multiple_of(p * piece, piece), piece)

    def term_slot(q):
        return lax.rem(q, 2 * TAPS)

    def c2(q):
        src = terms.at[term_slot(q), second_rows(1 - h_bit)]
        return remote(src, r2.at[q], r2_s.at[q], r2_r.at[q], h_peer, z, c)

    def z_of(n):
        return 2 * n + 1 - lax.rem(n, 2)

    def cf(q):
        passive_z = 2 * pair + turn
        there = active_z + passive_z - z
        return remote(r2.at[q], rf.at[term_slot(q)], rf_s.at[q], rf_r.at[q], m, there, c)

    def c3(q, p):
        slot = lax.rem(pair - p + actives - 1, actives)
        return remote(
            r2.at[q, piece_rows(p)], r3.at[q, slot], r3_s.at[q, p], r3_r.at[q, slot], m, z_of(p), c
        )

    def others(first, body, limit):
        def one(k):
            n = lax.rem(pair + k, actives)

            @pl.when(n < limit)
            def _():
                body(n)

        each(first, actives, one)

    def unit_of(q):
        k = lax.div(q, TAPS)
        return (LAYERS - 1 - k) * TAPS + (q - k * TAPS)

    def region(q, start, size, lane, lanes):
        start = pl.multiple_of(c * half + start, piece)
        lane = pl.multiple_of(lane, half)
        return kg_ref.at[unit_of(q), pl.ds(start, size), pl.ds(lane, lanes)]

    def cz(q, p, n):
        part = region(q, h_bit * (half // 2) + p * piece, piece, g_bit * half, half)
        return remote(fin.at[q], part, az_s.at[q, n], az_r.at[q, p], m, z_of(n), c)

    def cl(q):
        part = region(q, h_bit * (half // 2) + pair * piece, piece, g_bit * half, half)
        return pltpu.make_async_copy(fin.at[q], part, loc_s.at[q])

    def cu(q):
        passive_z = 2 * pair + turn
        there = active_z + passive_z - z
        part = region(q, h_bit * (half // 2), half // 2, g_bit * half, half)
        return remote(part, part, af_s.at[q], af_r.at[q], m, there, c)

    def cb(q):
        part = region(q, h_bit * (half // 2), half // 2, g_bit * half, half)
        return remote(part, part, ab_s.at[q], ab_r.at[q], h_peer, z, c)

    def ca(q):
        part = region(q, 0, half, g_bit * half, half)
        return remote(part, part, aa_s.at[q], aa_r.at[q], g_peer, z, c)

    def plan(q):
        k = lax.rem(q, 4)
        both = jnp.logical_or(lax.rem(k, 2) == 0, q >= UNITS - 3)
        mine = jnp.logical_or(both, lax.div(k, 2) == role)
        return mine, jnp.logical_and(mine, jnp.logical_not(both)), jnp.logical_not(mine)

    def ce(q):
        passive_z = 2 * pair + turn
        there = active_z + passive_z - z
        part = region(q, 0, half, (1 - g_bit) * half, half)
        return remote(part, part, ae_s.at[q], ae_r.at[q], m, there, c)

    def cp_part(q, start, size, lane, lanes):
        part = region(q, start, size, lane, lanes)
        return remote(part, part, ap_s.at[q], ap_r.at[q], m, z, other)

    def cp(q):
        return cp_part(q, 0, half, 0, 2 * half)

    def cp_rows(q, bit):
        return cp_part(q, bit * (half // 2), half // 2, g_bit * half, half)

    def cp_lanes(q):
        return cp_part(q, 0, half, (1 - g_bit) * half, half)

    def ready_terms(l):
        at_copy(l).wait_recv()
        for chip in range(2):
            for a in range(maps_here):
                first = a * (band + 2) * PAD
                rows = act_t[l, chip, :, first : first + (band + 2) * PAD]
                act_b[chip, :, a * band * PAD : (a + 1) * band * PAD] = rows[:, PAD : PAD + band * PAD]
        slot = lax.rem(l, 2)

        def variants(a, s):
            dzr_copy(l, a, 0).wait_recv()
            for chip in range(2):
                for rr in range(band):
                    for n in tiles:
                        if chip == 0:
                            mine, theirs = dz_own[slot, a, 1 + rr, :, n], dz_oth[slot, a, 1 + rr, :, n]
                            v = jnp.where(g_bit == c, mine, theirs)
                        else:
                            v = dzr[l, a, rr, :, n]
                        dzv[1, chip, a, rr, :, n] = v
                        v = v.astype(F32)
                        dzv[0, chip, a, rr, :, n] = pltpu.roll(v, PAD - 1, 0).astype(BF16)
                        dzv[2, chip, a, rr, :, n] = pltpu.roll(v, 1, 0).astype(BF16)
            return s

        lax.fori_loop(0, maps_here, variants, 0)

    def tap_terms(l, i, j):
        if i == 1:
            lhs = [act_b[0], act_b[1]]
        else:
            lhs = []
            for chip in range(2):
                for a in range(maps_here):
                    first = (a * (band + 2) + i) * PAD
                    lhs.append(act_t[l, chip, :, first : first + band * PAD])
        rhs = dzv[j].reshape(2 * pixels, half)
        q = (LAYERS - 1 - l) * TAPS + 3 * i + j
        got = jnp.dot(jnp.concatenate(lhs, 1), rhs, preferred_element_type=F32)
        terms[term_slot(q)] = got.astype(BF16)

    def weight_terms(l, i):
        lax.fori_loop(0, 3, lambda j, s: (tap_terms(l, i, j), s)[1], 0)

    def stage_second(q):
        c2(q).wait()
        kept = terms[term_slot(q), second_rows(h_bit)].astype(F32)
        r2[q] = (r2[q].astype(F32) + kept).astype(BF16)

        @pl.when(is_passive)
        def _():
            cf(q).start()

    def stage_fold(q):
        @pl.when(is_active)
        def _():
            cf(q).wait_recv()
            r2[q] = (r2[q].astype(F32) + rf[term_slot(q)].astype(F32)).astype(BF16)
            others(1, lambda n: c3(q, n).start(), owners)

    def stage_sum(q):
        @pl.when(is_owner)
        def _():
            for k in range(actives - 1):
                remote(
                    r3.at[q, k], r3.at[q, k], r3_s.at[q, 0], r3_r.at[q, k], m, z, c
                ).wait_recv()
            total = r2[q, piece_rows(pair)].astype(F32)
            for k in range(actives - 1):
                total = total + r3[q, k].astype(F32)
            fin[q] = total.astype(BF16)
            others(1, lambda n: cz(q, pair, n).start(), actives)
            cl(q).start()

    def stage_back(q):
        @pl.when(is_active)
        def _():
            others(1, lambda n: cz(q, n, n).wait_recv(), owners)

        @pl.when(is_owner)
        def _():
            cl(q).wait()

        @pl.when(is_active)
        def _():
            cu(q).start()

        @pl.when(is_passive)
        def _():
            cu(q).wait_recv()

        cb(q).start()
        cp_rows(q, h_bit).start()

    def stage_first(q):
        cb(q).wait_recv()
        mine, _, _ = plan(q)

        @pl.when(mine)
        def _():
            ca(q).start()

        cp_rows(q, 1 - h_bit).start()

        @pl.when(is_active)
        def _():
            others(1, lambda n: c3(q, n).wait_send(), owners)

        @pl.when(is_passive)
        def _():
            cf(q).wait_send()

    def stage_chip(q):
        mine, for_both, _ = plan(q)

        @pl.when(mine)
        def _():
            ca(q).wait_recv()

        @pl.when(for_both)
        def _():
            ce(q).start()

        @pl.when(mine)
        def _():
            cp_lanes(q).start()

        @pl.when(is_owner)
        def _():
            others(1, lambda n: cz(q, pair, n).wait_send(), actives)

        @pl.when(is_active)
        def _():
            cu(q).wait_send()

    def stage_late(q):
        _, _, not_mine = plan(q)

        @pl.when(not_mine)
        def _():
            ce(q).wait_recv()
            cp_lanes(q).start()

    def stage_done(q):
        mine, for_both, _ = plan(q)
        cb(q).wait_send()

        @pl.when(mine)
        def _():
            ca(q).wait_send()

        @pl.when(for_both)
        def _():
            ce(q).wait_send()

        cp(q).wait()

    def run(stage, first, last):
        lax.fori_loop(first, last, lambda q, s: (stage(q), s)[1], 0)

    def sent_dz(l):
        for a in range(maps_here):
            dz_copy(l, a).wait_send()
            for way in range(2):
                if_wanted(way, dzr_copy(l, a, way).wait_send)

    def backward(k, carry):
        l = LAYERS - 1 - k
        gain, shift = gain_of(l), shift_of(l)

        def gradient(a, rr, n):
            zhat = (zbuf[l, a, rr, :, n] - row_of(avg_t, l, a)[:, n]) * row_of(scl_t, l, a)[:, n]
            y = zhat * gain[:, n] + shift[:, n]
            s = jax.nn.sigmoid(y)
            if rr in (0, band + 1):
                upstream = dhh[l, rr // (band + 1), a, :, n].astype(F32)
            else:
                upstream = dh[a, rr - 1, :, n]
            dy = upstream * (s * (1.0 + y * (1.0 - s)))
            dy = jnp.where(column[:, n] < limit(a, rr), dy, 0.0)
            return dy, zhat

        def collect(a, tile):
            plains, crosses = [], []
            for n in tiles:
                plain = jnp.zeros((PAD, 128), F32)
                crossed = jnp.zeros((PAD, 128), F32)
                for rr in range(1, band + 1):
                    dy, zhat = gradient(a, rr, n)
                    dh[a, rr - 1, :, n] = dy
                    plain = plain + dy
                    crossed = crossed + dy * zhat
                plains.append(jnp.sum(plain, 0, keepdims=True))
                crosses.append(jnp.sum(crossed, 0, keepdims=True))
            tile = jnp.where(row8 == a, jnp.concatenate(plains, 1), tile)
            return jnp.where(row8 == a + maps_here, jnp.concatenate(crosses, 1), tile)

        e = LAYERS + l
        tile = lax.fori_loop(0, maps_here, collect, jnp.zeros((8, half), F32))
        send_z(e, tile)

        @pl.when(k == LAYERS - 1)
        def _():
            run(stage_second, 0, TAPS)

        @pl.when(k > 0)
        def _():
            ready_terms(l + 1)
            weight_terms(l + 1, 0)

        wait_z(e)
        total = st1[e, 0]
        for zz in range(1, chips):
            total = total + st1[e, zz]
        send_m(e, total)

        @pl.when(k > 0)
        def _():
            first = (LAYERS - 2 - l) * TAPS
            run(lambda q: c2(q).start(), first, first + 3)
            weight_terms(l + 1, 1)
            run(lambda q: c2(q).start(), first + 3, first + 6)
            weight_terms(l + 1, 2)
            run(lambda q: c2(q).start(), first + 6, first + 9)
            wait_halo(dh_halo, l)

        @pl.when(k == 0)
        def _():
            pool()

        wait_m(e)
        total = st2[e, 0]
        for mm in range(1, PLANE):
            total = total + st2[e, mm]
        sums_own[pl.ds(l, 1), :] = jnp.sum(
            jnp.where(row8 >= maps_here, total, 0.0), 0, keepdims=True
        )
        sums_own[pl.ds(LAYERS + l, 1), :] = jnp.sum(
            jnp.where(row8 < maps_here, total, 0.0), 0, keepdims=True
        )
        plains = jnp.zeros((8, half), F32)
        crosses = jnp.zeros((8, half), F32)
        for a in range(maps_here):
            plain = jnp.zeros((8, half), F32)
            crossed = jnp.zeros((8, half), F32)
            for mm in range(PLANE):
                v = st2[e, mm]
                plain = plain + coef[a, mm] * v
                crossed = crossed + coef[a, mm] * pltpu.roll(v, 8 - maps_here, 0)
            count = cnt_t[a : a + 1, :]
            plain = gain * (jnp.sum(plain, 0, keepdims=True) / count)
            crossed = gain * (jnp.sum(crossed, 0, keepdims=True) / count)
            plains = jnp.where(row8 == a, plain, plains)
            crosses = jnp.where(row8 == a, crossed, crosses)
        tb_t[0] = plains
        ta_t[0] = crosses

        def settle(a, s):
            for n in tiles:
                average, scaling = row_of(avg_t, l, a)[:, n], row_of(scl_t, l, a)[:, n]
                plain, crossed = row_of(tb_t, 0, a)[:, n], row_of(ta_t, 0, a)[:, n]
                for rr in range(band + 2):
                    if rr in (0, band + 1):
                        dy, zhat = gradient(a, rr, n)
                    else:
                        dy = dh[a, rr - 1, :, n]
                        zhat = (zbuf[l, a, rr, :, n] - average) * scaling
                    v = scaling * (dy * gain[:, n] - plain - zhat * crossed)
                    v = jnp.where(column[:, n] < limit(a, rr), v, 0.0)
                    dz_own[lax.rem(l, 2), a, rr, :, n] = v.astype(BF16)
            dz_copy(l, a).start()
            for way in range(2):
                if_wanted(way, dzr_copy(l, a, way).start)
            return s

        @pl.when(k == 2)
        def _():
            sent_dz(LAYERS - 1)

        lax.fori_loop(0, maps_here, settle, 0)
        products(dz_own, l, (0, 1, 2), wa, True, True)
        weight_copy(l, 2).wait()
        for a in range(maps_here):
            dz_copy(l, a).wait_recv()
        products(dz_oth, l, (0, 1, 2), wb, True, False)

        def gather(a, s):
            for n in tiles:
                for rr in range(band):
                    v = shifted(a, rr, 2, 0, n)
                    dh[a, rr, :, n] = v
                    if rr in (0, band - 1):
                        dhs[rr // (band - 1), a, :, n] = v.astype(BF16)
            return s

        lax.fori_loop(0, maps_here, gather, 0)

        @pl.when(l > 0)
        def _():
            start_halo(dh_halo, l - 1)

        return carry

    lax.fori_loop(0, LAYERS, backward, 0)
    def input_rows(a, s):
        for rr in range(band):
            dh[a, rr] = jnp.where(column < width_of(a), dh[a, rr], 0.0)
        return s

    lax.fori_loop(0, maps_here, input_rows, 0)

    outs = (
        (
            remote(dh.at[:, pl.ds(2 * other, 2)], ig_ref.at[c], out_s.at[0], out_r.at[0], m, z, other),
            pltpu.make_async_copy(dh.at[:, pl.ds(2 * c, 2)], ig_ref.at[c], out_l.at[0]),
        ),
        (
            remote(pbuf.at[other], pooled_ref.at[c], out_s.at[1], out_r.at[1], m, z, other),
            pltpu.make_async_copy(pbuf.at[c], pooled_ref.at[c], out_l.at[1]),
        ),
        (
            remote(sums_own, sums_ref.at[c], out_s.at[2], out_r.at[2], m, z, other),
            pltpu.make_async_copy(sums_own, sums_ref.at[c], out_l.at[2]),
        ),
    )
    for there, here in outs:
        there.start()
        here.start()

    g_partner.wait_send()
    sent_x_halo(2, 4)

    def sent(e, carry):
        each(1, chips, lambda k: z_copy(e, k).wait_send())
        each(1, PLANE, lambda k: m_copy(e, k).wait_send())
        return carry

    lax.fori_loop(0, 2 * LAYERS, sent, 0)
    for l in range(LAYERS):
        at_copy(l).wait_send()
    for l in range(LAYERS - 1):
        sent_dz(l)

    def drain(s, carry):
        @pl.when(s == EARLY)
        def _():
            ready_terms(0)

        for i in range(3):
            j = s - EARLY - 3 * i

            @pl.when(jnp.logical_and(j >= 0, j < 3))
            def _(i=i, j=j):
                tap_terms(0, i, j)
                c2(2 * TAPS + 3 * i + j).start()

        for stage, first, lag in (
            (stage_done, 0, 2 * FOLD + 4 * LAG),
            (stage_late, 0, 2 * FOLD + 3 * LAG),
            (stage_chip, 0, 2 * FOLD + 2 * LAG),
            (stage_first, 0, 2 * FOLD + LAG),
            (stage_back, 0, 2 * FOLD),
            (stage_sum, 0, FOLD),
            (stage_fold, 0, 0),
            (stage_second, TAPS, 0),
        ):
            q = first + s - lag

            @pl.when(jnp.logical_and(q >= first, q < UNITS))
            def _(stage=stage, q=q):
                stage(q)

        return carry

    lax.fori_loop(0, UNITS + 2 * FOLD + 4 * LAG, drain, 0)
    for a in range(maps_here):
        act_copy(2, a).wait_send()
    for there, here in outs:
        there.wait()
        here.wait()


def solution(mesh):
    chips = mesh.shape["rows"] // 2

    def per_device(
        block_input,
        conv_weights,
        norm_gains,
        norm_shifts,
        map_width,
        map_group,
        pool_index,
        task_mask,
        task_weights,
        task_grads,
    ):
        maps_here, rows_here, columns, channels = block_input.shape
        pooled_columns = pool_index.shape[2]
        height = rows_here * mesh.shape["rows"]
        half = channels // 2
        band = 2 * rows_here
        pixels = maps_here * band * PAD
        actives = chips // 2
        owners = min(actives, 8)
        piece = half // 2 // owners
        rounds = 2 * LAYERS
        slots = 2 * UNITS * (actives - 1) * piece * half + 4 * rounds * chips * 8 * half
        grant = (36 * 1024 + 256) * 1024 + slots
        vmem, dma = pltpu.VMEM, pltpu.SemaphoreType.DMA
        tile = (maps_here, band + 2, PAD, half)
        edge = (2, maps_here, PAD, half)
        whole = pl.BlockSpec(memory_space=pltpu.VMEM)
        outside = pl.BlockSpec(memory_space=pltpu.HBM)
        index_rows = jnp.transpose(pool_index, (0, 2, 1, 3))
        anywhere = pl.BlockSpec(memory_space=pl.ANY)
        pooled, ig, kg, sums = pl.pallas_call(
            functools.partial(block_kernel, chips, height),
            out_shape=(
                jax.ShapeDtypeStruct((2, maps_here, PAD // 2, half), BF16),
                jax.ShapeDtypeStruct((2, maps_here, rows_here, PAD, half), F32),
                jax.ShapeDtypeStruct((UNITS, channels, channels), BF16),
                jax.ShapeDtypeStruct((2, 8, half), F32),
            ),
            in_specs=[whole, anywhere] + [outside] * 8,
            out_specs=[anywhere] * 4,
            scratch_shapes=[
                vmem(norm_gains.shape, F32),
                vmem(norm_shifts.shape, F32),
                pltpu.SMEM(map_width.shape, jnp.int32),
                pltpu.SMEM(map_group.shape, jnp.int32),
                vmem((maps_here, pooled_columns, channels), jnp.int32),
                pltpu.SMEM(task_mask.shape, jnp.int32),
                pltpu.SMEM(task_weights.shape, F32),
                vmem(task_grads.shape, BF16),
                vmem((LAYERS, 3, 3, half, half), BF16),
                vmem((LAYERS, 3, 3, half, half), BF16),
                vmem((2,) + tile, BF16),
                vmem((2,) + tile, BF16),
                vmem((LAYERS, 2, half, maps_here * (band + 2) * PAD), BF16),
                vmem((2, half, pixels), BF16),
                vmem((LAYERS,) + tile, F32),
                vmem(edge, BF16),
                vmem((LAYERS,) + edge, BF16),
                vmem((maps_here, band, PAD, half), F32),
                vmem(edge, BF16),
                vmem((LAYERS,) + edge, BF16),
                vmem((2,) + tile, BF16),
                vmem((2,) + tile, BF16),
                vmem((LAYERS, maps_here, band, PAD, half), BF16),
                vmem((3, 2, maps_here, band, PAD, half), BF16),
                vmem((3, pixels, half), F32),
                vmem((2, 2, maps_here, PAD // 2, half), F32),
                vmem((4, 2, maps_here, PAD // 2, half), F32),
                vmem((half // 128, PAD, 128), F32),
                vmem((2, maps_here, PAD // 2, half), BF16),
                vmem((rounds, chips, 8, half), F32),
                vmem((rounds, PLANE, 8, half), F32),
                vmem((maps_here, PLANE, 8, half), F32),
                vmem((PLANE, 8, half), F32),
                vmem((2, 8, half), F32),
                vmem((8, half), F32),
                vmem((LAYERS, 8, half), F32),
                vmem((LAYERS, 8, half), F32),
                vmem((2, 8, half), F32),
                vmem((1, 8, half), F32),
                vmem((1, 8, half), F32),
                vmem((8, half), F32),
                vmem((2 * TAPS, half, half), BF16),
                vmem((UNITS, half // 2, half), BF16),
                vmem((2 * TAPS, half // 2, half), BF16),
                vmem((UNITS, actives - 1, piece, half), BF16),
                vmem((UNITS, piece, half), BF16),
                dma((8,)),
                dma((LAYERS, 3)),
                dma((6,)),
                dma((6,)),
                dma((3,)),
                dma((3,)),
                dma((rounds, chips)),
                dma((rounds, chips)),
                dma((rounds, PLANE)),
                dma((rounds, PLANE)),
                dma((LAYERS, 2)),
                dma((LAYERS, 2)),
                dma((LAYERS, 2)),
                dma((LAYERS, 2)),
                dma((LAYERS, maps_here)),
                dma((LAYERS, maps_here)),
                dma((LAYERS, maps_here)),
                dma((LAYERS, maps_here)),
                dma((3,)),
                dma((3,)),
                dma((3,)),
                dma((LAYERS,)),
                dma((LAYERS,)),
                dma((LAYERS, 2, maps_here)),
                dma((LAYERS, maps_here)),
                dma((UNITS,)),
                dma((UNITS,)),
                dma((UNITS,)),
                dma((UNITS,)),
                dma((UNITS, owners)),
                dma((UNITS, actives - 1)),
                dma((UNITS, actives)),
                dma((UNITS, owners)),
                dma((UNITS,)),
                dma((UNITS,)),
                dma((UNITS,)),
                dma((UNITS,)),
                dma((UNITS,)),
                dma((UNITS,)),
                dma((UNITS,)),
                dma((UNITS,)),
                dma((UNITS,)),
                dma((UNITS,)),
                dma((UNITS,)),
            ],
            compiler_params=pltpu.CompilerParams(
                collective_id=0,
                has_side_effects=True,
                vmem_limit_bytes=grant,
            ),
        )(
            block_input,
            conv_weights,
            *(
                pltpu.with_memory_space_constraint(v, pltpu.HBM)
                for v in (
                    norm_gains,
                    norm_shifts,
                    map_width,
                    map_group,
                    index_rows,
                    task_mask,
                    task_weights,
                    task_grads,
                )
            ),
        )
        pooled = jnp.concatenate([pooled[0], pooled[1]], -1)[:, None, :pooled_columns]
        input_grad = jnp.concatenate([ig[0], ig[1]], -1)[:, :, :columns]
        sums = jnp.concatenate([sums[0], sums[1]], -1)
        return (
            pooled,
            input_grad,
            kg.astype(F32).reshape(conv_weights.shape),
            sums[:LAYERS],
            sums[LAYERS : 2 * LAYERS],
        )

    return jax.shard_map(
        per_device,
        mesh=mesh,
        in_specs=(
            P("maps", "rows", None, None),
            P(),
            P(),
            P(),
            P(),
            P(),
            P("maps", "rows", None, None),
            P("maps", None),
            P(),
            P(None, "maps", "rows", None, None),
        ),
        out_specs=(P("maps", "rows", None, None), P("maps", "rows", None, None), P(), P(), P()),
        check_vma=False,
    )
```

```python
import functools

import jax
import jax.numpy as jnp
from jax import lax
from jax.experimental import pallas as pl
from jax.experimental.pallas import tpu as pltpu
from jax.sharding import PartitionSpec as P

MESH = pl.DeviceIdType.MESH
epsilon = 1e-05
PAD = 64
LAYERS = 3
TAPS = 9
UNITS = LAYERS * TAPS
PLANE = 4
LAG = 4
EARLY = 1
FOLD = 2
F32 = jnp.float32
BF16 = jnp.bfloat16


def each(first, last, body):
    if last - first <= 8:
        for k in range(first, last):
            body(k)
    else:
        lax.fori_loop(first, last, lambda k, s: (body(k), s)[1], 0)


def block_kernel(
    chips,
    height,
    x_ref,
    w_ref,
    gain_hbm,
    shift_hbm,
    width_hbm,
    group_hbm,
    index_hbm,
    tmask_hbm,
    tweight_hbm,
    tgrad_hbm,
    pooled_ref,
    ig_ref,
    kg_ref,
    sums_ref,
    gain_ref,
    shift_ref,
    width_ref,
    group_ref,
    index_ref,
    tmask_ref,
    tweight_ref,
    tgrad_ref,
    wa,
    wb,
    act_own,
    act_oth,
    act_t,
    act_b,
    zbuf,
    zs,
    zh,
    dh,
    dhs,
    dhh,
    dz_own,
    dz_oth,
    dzr,
    dzv,
    prod,
    gsrc,
    gbuf,
    hrow,
    pbuf,
    st1,
    st2,
    coef,
    nall,
    inv_t,
    cnt_t,
    avg_t,
    scl_t,
    mean_t,
    tb_t,
    ta_t,
    sums_own,
    terms,
    r2,
    rf,
    r3,
    fin,
    in_sem,
    w_sem,
    x_s,
    x_r,
    g_s,
    g_r,
    st1_s,
    st1_r,
    st2_s,
    st2_r,
    zh_s,
    zh_r,
    dh_s,
    dh_r,
    act_s,
    act_r,
    dz_s,
    dz_r,
    out_s,
    out_r,
    out_l,
    at_s,
    at_r,
    dzr_s,
    dzr_r,
    r2_s,
    r2_r,
    rf_s,
    rf_r,
    r3_s,
    r3_r,
    az_s,
    az_r,
    af_s,
    af_r,
    ab_s,
    ab_r,
    aa_s,
    aa_r,
    ap_s,
    ap_r,
    loc_s,
):
    maps_here = x_ref.shape[0]
    columns = x_ref.shape[2]
    half = x_ref.shape[3] // 2
    tasks = tgrad_ref.shape[0]
    pooled_columns = tgrad_ref.shape[3]
    lanes = half // 128
    tiles = [slice(n * 128, (n + 1) * 128) for n in range(lanes)]
    band = 4
    pixels = maps_here * band * PAD
    actives = chips // 2
    owners = min(actives, 8)
    piece = (half // 2) // owners
    m = lax.axis_index("maps")
    r = lax.axis_index("rows")
    c = lax.rem(r, 2)
    z = lax.div(r, 2)
    other = 1 - c
    first_map = m * maps_here
    x_bit = lax.rem(m, 2)
    y_bit = lax.div(m, 2)
    x_peer = m + 1 - 2 * x_bit
    y_peer = m + 2 - 4 * y_bit
    g_bit = (1 - c) * x_bit + c * y_bit
    h_bit = (1 - c) * y_bit + c * x_bit
    g_peer = (1 - c) * x_peer + c * y_peer
    h_peer = (1 - c) * y_peer + c * x_peer
    pair = lax.div(z, 2)
    turn = lax.rem(pair, 2)
    active_z = 2 * pair + 1 - turn
    is_active = z == active_z
    is_passive = z != active_z
    is_owner = jnp.logical_and(is_active, pair < owners)
    up_there = z > 0
    down_there = z < chips - 1
    row8 = lax.broadcasted_iota(jnp.int32, (8, half), 0)
    column = lax.broadcasted_iota(jnp.int32, (PAD, half), 0)

    def remote(src, dst, send, recv, mm, zz, cc):
        return pltpu.make_async_remote_copy(
            src_ref=src,
            dst_ref=dst,
            send_sem=send,
            recv_sem=recv,
            device_id=(mm, zz * 2 + cc),
            device_id_type=MESH,
        )

    def own_half(v):
        return jnp.where(c == 0, v[..., :half], v[..., half:])

    def width_of(a):
        return width_ref[first_map + a]

    own_at = pl.ds(pl.multiple_of(c * half, half), half)
    oth_at = pl.ds(pl.multiple_of(other * half, half), half)

    def weight_copy(l, n):
        dst = (wa, wb, wb)[n]
        k_at, o_at = ((own_at, own_at), (oth_at, own_at), (own_at, oth_at))[n]
        return pltpu.make_async_copy(w_ref.at[l, :, :, k_at, o_at], dst.at[l], w_sem.at[l, n])

    fetches = [
        pltpu.make_async_copy(src, dst, in_sem.at[n])
        for n, (src, dst) in enumerate(
            (
                (width_hbm, width_ref),
                (group_hbm, group_ref),
                (tmask_hbm, tmask_ref),
                (tweight_hbm, tweight_ref),
                (gain_hbm, gain_ref),
                (shift_hbm, shift_ref),
                (index_hbm.at[:, :, 0, :], index_ref),
                (tgrad_hbm, tgrad_ref),
            )
        )
    ]
    for fetch in fetches:
        fetch.start()
    for l in range(LAYERS):
        weight_copy(l, 0).start()
        weight_copy(l, 1).start()

    barrier = pltpu.get_barrier_semaphore()

    def greet(k):
        rr = lax.rem(r + k, 2 * chips)
        pl.semaphore_signal(barrier, inc=1, device_id=(m, rr), device_id_type=MESH)

    each(1, 2 * chips, greet)
    for k in range(1, PLANE):
        for core in (c, other):
            there = (lax.rem(m + k, PLANE), z * 2 + core)
            pl.semaphore_signal(barrier, inc=1, device_id=there, device_id_type=MESH)

    for fetch in fetches:
        fetch.wait()

    mine = pl.ds(1 + 2 * c, 2)
    for a in range(maps_here):
        inside = lax.broadcasted_iota(jnp.int32, (columns, 2 * half), 0) < width_of(a)
        for rr in range(2):
            v = jnp.where(inside, x_ref[a, rr].astype(F32), 0.0).astype(BF16)
            spot = 1 + 2 * c + rr
            act_own[0, a, spot, pl.ds(48, 16), :] = jnp.zeros((16, half), BF16)
            act_oth[0, a, spot, pl.ds(48, 16), :] = jnp.zeros((16, half), BF16)
            act_own[0, a, spot, pl.ds(0, columns), :] = own_half(v)
            act_oth[0, a, spot, pl.ds(0, columns), :] = jnp.where(
                c == 0, v[:, half:], v[:, :half]
            )

    @pl.when(z == 0)
    def _():
        act_own[0, :, 0] = jnp.zeros((maps_here, PAD, half), BF16)
        act_oth[0, :, 0] = jnp.zeros((maps_here, PAD, half), BF16)

    @pl.when(z == chips - 1)
    def _():
        act_own[0, :, 5] = jnp.zeros((maps_here, PAD, half), BF16)
        act_oth[0, :, 5] = jnp.zeros((maps_here, PAD, half), BF16)

    pl.semaphore_wait(barrier, 2 * chips - 1 + 2 * (PLANE - 1))

    x_partner = (
        remote(act_own.at[0, :, mine], act_oth.at[0, :, mine], x_s.at[0], x_r.at[0], m, z, other),
        remote(act_oth.at[0, :, mine], act_own.at[0, :, mine], x_s.at[1], x_r.at[1], m, z, other),
    )
    g_partner = remote(gsrc.at[other], gbuf.at[1 + c], g_s.at[0], g_r.at[0], m, z, other)

    def x_halo(n, src_row, dst_row, zz):
        cc = (c, other)[n % 2]
        low = dst_row == band + 1
        if n >= 2:
            src, dst = gsrc.at[cc], gbuf.at[3 if low else 0]
            return remote(src, dst, g_s.at[n - 1], g_r.at[1 if low else 2], m, zz, cc)
        src, dst = (act_own, act_oth)[n].at[0, :, src_row], act_own.at[0, :, dst_row]
        return remote(src, dst, x_s.at[2 + n], x_r.at[2 if low else 3], m, zz, cc)

    def x_pass(row):
        n = 4 if row == 0 else 5
        src, dst = act_own.at[0, :, row], act_oth.at[0, :, row]
        return remote(src, dst, x_s.at[n], x_r.at[n], m, z, other)

    for copy in x_partner:
        copy.start()

    @pl.when(jnp.logical_and(c == 0, up_there))
    def _():
        for n in range(2):
            x_halo(n, 1, 5, z - 1).start()

    @pl.when(jnp.logical_and(c == 1, down_there))
    def _():
        for n in range(2):
            x_halo(n, 4, 0, z + 1).start()

    gsrc[...] = jnp.zeros(gsrc.shape, F32)
    for a in range(maps_here):
        total = None
        for t in range(tasks):
            scale = tweight_ref[t] * tmask_ref[a, t].astype(F32)
            term = tgrad_ref[t, a, 0].astype(F32) * scale
            total = term if total is None else total + term
        position = index_ref[a].astype(F32)
        for h in range(2):
            gsrc[h, 0, a, pl.ds(0, pooled_columns), :] = total[:, h * half : (h + 1) * half]
            gsrc[h, 1, a, pl.ds(0, pooled_columns), :] = position[:, h * half : (h + 1) * half]
    gbuf[1 + c] = gsrc[c]

    for mm in range(PLANE):
        sizes = jnp.zeros((8, half), F32)
        for b in range(maps_here):
            sizes = jnp.where(
                row8 == b, (width_ref[mm * maps_here + b] * height).astype(F32), sizes
            )
        nall[mm] = sizes
    inside_sizes = jnp.zeros((8, half), F32)
    for b in range(maps_here):
        inside_sizes = jnp.where(row8 == b, (width_of(b) * band).astype(F32), inside_sizes)
    inv_t[0] = inside_sizes
    inv_t[1] = jnp.where(row8 < maps_here, 1.0 / jnp.maximum(inside_sizes, 1.0), 0.0)
    counts = jnp.ones((8, half), F32)
    for a in range(maps_here):
        total = jnp.zeros((1, half), F32)
        for mm in range(PLANE):
            same = jnp.zeros((8, half), F32)
            for b in range(maps_here):
                alike = group_ref[first_map + a] == group_ref[mm * maps_here + b]
                same = jnp.where(row8 == b, jnp.where(alike, 1.0, 0.0), same)
            coef[a, mm] = same
            total = total + jnp.sum(same * nall[mm], 0, keepdims=True)
        counts = jnp.where(row8 == a, total, counts)
    cnt_t[...] = counts

    def z_copy(e, k):
        zz = lax.rem(z + k, chips)
        return remote(st1.at[e, z], st1.at[e, z], st1_s.at[e, k], st1_r.at[e, z], m, zz, c)

    def z_arrival(e, k):
        zz = lax.rem(z + k, chips)
        return remote(st1.at[e, zz], st1.at[e, zz], st1_s.at[e, k], st1_r.at[e, zz], m, zz, c)

    def m_copy(e, k):
        mm = lax.rem(m + k, PLANE)
        return remote(st2.at[e, m], st2.at[e, m], st2_s.at[e, k], st2_r.at[e, m], mm, z, c)

    def m_arrival(e, k):
        mm = lax.rem(m + k, PLANE)
        return remote(st2.at[e, mm], st2.at[e, mm], st2_s.at[e, k], st2_r.at[e, mm], mm, z, c)

    def send_z(e, tile):
        st1[e, z] = tile
        each(1, chips, lambda k: z_copy(e, k).start())

    def wait_z(e):
        each(1, chips, lambda k: z_arrival(e, k).wait_recv())

    def send_m(e, tile):
        st2[e, m] = tile
        each(1, PLANE, lambda k: m_copy(e, k).start())

    def wait_m(e):
        each(1, PLANE, lambda k: m_arrival(e, k).wait_recv())

    def products(source, l, taps, kernel, transposed, fresh):
        starts = [2 - i if transposed else i for i in taps]
        lhs = jnp.concatenate(
            [source[lax.rem(l, 2), :, s : s + band].reshape(pixels, half) for s in starts], 1
        )
        for j in range(3):
            rhs = jnp.concatenate([kernel[l, i, j] for i in taps], 1 if transposed else 0)
            got = lax.dot_general(
                lhs,
                rhs,
                (((1,), (1 if transposed else 0,)), ((), ())),
                preferred_element_type=F32,
            )
            if fresh:
                prod[j] = got
            else:
                prod[j] = prod[j] + got

    def shifted(a, rr, before, behind, n):
        rows = pl.ds(pl.multiple_of((a * band + rr) * PAD, PAD), PAD)
        return (
            prod[1, rows, n]
            + pltpu.roll(prod[before, rows, n], 1, 0)
            + pltpu.roll(prod[behind, rows, n], PAD - 1, 0)
        )

    def row_of(table, l, a):
        return table[l, pl.ds(a, 1), :]

    def gain_of(l):
        return own_half(gain_ref[pl.ds(l, 1), :])

    def shift_of(l):
        return own_half(shift_ref[pl.ds(l, 1), :])

    def limit(a, rr):
        w = width_of(a)
        if rr == 0:
            return jnp.where(up_there, w, 0)
        if rr == band + 1:
            return jnp.where(down_there, w, 0)
        return w

    def z_halo(l, way):
        there = z - 1 + 2 * way
        return remote(zs.at[way], zh.at[l, 1 - way], zh_s.at[l, way], zh_r.at[l, way], m, there, c)

    def dh_halo(l, way):
        there = z - 1 + 2 * way
        return remote(dhs.at[way], dhh.at[l, 1 - way], dh_s.at[l, way], dh_r.at[l, way], m, there, c)

    def start_halo(halo, l):
        @pl.when(up_there)
        def _():
            halo(l, 0).start()

        @pl.when(down_there)
        def _():
            halo(l, 1).start()

    def wait_halo(halo, l):
        @pl.when(up_there)
        def _():
            halo(l, 1).wait_recv()
            halo(l, 0).wait_send()

        @pl.when(down_there)
        def _():
            halo(l, 0).wait_recv()
            halo(l, 1).wait_send()

    def act_copy(l, a):
        slot = lax.rem(l, 2)
        src, dst = act_own.at[slot, a], act_oth.at[slot, a]
        return remote(src, dst, act_s.at[l, a], act_r.at[l, a], m, z, other)

    def at_copy(l):
        return remote(act_t.at[l, 0], act_t.at[l, 1], at_s.at[l], at_r.at[l], g_peer, z, c)

    def dzr_copy(l, a, way):
        src, dst = dz_own.at[lax.rem(l, 2), a, pl.ds(1, band)], dzr.at[l, a]
        peer = (x_peer, y_peer)[way]
        return remote(src, dst, dzr_s.at[l, way, a], dzr_r.at[l, a], peer, z, way)

    def if_wanted(way, body):
        @pl.when((x_bit, y_bit)[way] + c == 1)
        def _():
            body()

    def dz_copy(l, a):
        slot = lax.rem(l, 2)
        src, dst = dz_own.at[slot, a], dz_oth.at[slot, a]
        return remote(src, dst, dz_s.at[l, a], dz_r.at[l, a], m, z, other)

    def send_gradients():
        g_partner.start()

        @pl.when(jnp.logical_and(c == 0, up_there))
        def _():
            for n in range(2, 4):
                x_halo(n, 1, 5, z - 1).start()

        @pl.when(jnp.logical_and(c == 1, down_there))
        def _():
            for n in range(2, 4):
                x_halo(n, 4, 0, z + 1).start()

    def if_there(way, body):
        @pl.when((up_there, down_there)[way])
        def _():
            body()

    def wait_x_halo(n):
        if_there(0, lambda: x_halo(n, 4, 0, z - 1).wait_recv())
        if_there(1, lambda: x_halo(n, 1, 5, z + 1).wait_recv())

    def each_x_pass(act):
        if_there(0, lambda: act(x_pass(0)))
        if_there(1, lambda: act(x_pass(band + 1)))

    def sent_x_halo(first, last):
        @pl.when(jnp.logical_and(c == 0, up_there))
        def _():
            for n in range(first, last):
                x_halo(n, 1, 5, z - 1).wait_send()

        @pl.when(jnp.logical_and(c == 1, down_there))
        def _():
            for n in range(first, last):
                x_halo(n, 4, 0, z + 1).wait_send()

    def unpool(a, s):
        for rr in range(band + 2):
            slot, lower = (rr + 1) // 2, (rr + 1) % 2
            g = gbuf[slot, 0, a]
            position = gbuf[slot, 1, a]
            for b in range(2):
                v = jnp.where(position == float(2 * lower + b), g, 0.0)
                for n in range(lanes):
                    hrow[n, pl.ds(b, PAD // 2, stride=2), :] = v[:, n * 128 : (n + 1) * 128]
            v = jnp.concatenate([hrow[n] for n in range(lanes)], 1)
            if rr in (0, band + 1):
                dhh[LAYERS - 1, rr // (band + 1), a] = v.astype(BF16)
            else:
                dh[a, rr - 1] = v
        return s

    def forward(l, first):
        weight_copy(l, 0).wait()
        weight_copy(l, 1).wait()
        if first:
            for copy in x_partner:
                copy.wait_recv()
            products(act_own, l, (1,), wa, False, True)
            products(act_oth, l, (1,), wb, False, False)
            wait_x_halo(0)
            each_x_pass(lambda copy: copy.start())
            products(act_own, l, (0, 2), wa, False, False)
            each_x_pass(lambda copy: copy.wait_recv())
            products(act_oth, l, (0, 2), wb, False, False)
        else:
            products(act_own, l, (0, 1, 2), wa, False, True)
            for a in range(maps_here):
                act_copy(l, a).wait_recv()
            products(act_oth, l, (0, 1, 2), wb, False, False)
        weight_copy(l, 2).start()

        def collect(a, tile):
            inside = column[:, :128] < width_of(a)
            pixels_inside = (width_of(a) * band).astype(F32)
            totals, squares = [], []
            for n in tiles:
                total = jnp.zeros((PAD, 128), F32)
                for rr in range(band):
                    v = shifted(a, rr, 0, 2, n)
                    zbuf[l, a, 1 + rr, :, n] = v
                    total = total + jnp.where(inside, v, 0.0)
                total = jnp.sum(total, 0, keepdims=True)
                mean = total / pixels_inside
                square = jnp.zeros((PAD, 128), F32)
                for rr in range(band):
                    v = jnp.where(inside, zbuf[l, a, 1 + rr, :, n] - mean, 0.0)
                    square = square + v * v
                    if rr in (0, band - 1):
                        zs[rr // (band - 1), a, :, n] = v.astype(BF16)
                totals.append(total)
                squares.append(jnp.sum(square, 0, keepdims=True))
            tile = jnp.where(row8 == a, jnp.concatenate(totals, 1), tile)
            return jnp.where(row8 == a + maps_here, jnp.concatenate(squares, 1), tile)

        tile = lax.fori_loop(0, maps_here, collect, jnp.zeros((8, half), F32))
        send_z(l, tile)
        start_halo(z_halo, l)
        act_t[l, 0] = act_own[lax.rem(l, 2)].reshape(maps_here * (band + 2) * PAD, half).T
        wait_z(l)
        sizes, inverse = inv_t[0], inv_t[1]
        mean_t[0] = st1[l, jnp.maximum(z - 1, 0)] * inverse
        mean_t[1] = st1[l, jnp.minimum(z + 1, chips - 1)] * inverse
        total = st1[l, 0]
        for zz in range(1, chips):
            total = total + st1[l, zz]
        mean = total * inverse * (1.0 / chips)
        square = jnp.zeros((8, half), F32)
        for zz in range(chips):
            v = st1[l, zz]
            gap = v * inverse - mean
            square = square + pltpu.roll(v, 8 - maps_here, 0) + sizes * gap * gap
        tile = jnp.where(row8 < maps_here, mean, pltpu.roll(square, maps_here, 0))
        send_m(l, jnp.where(row8 < 2 * maps_here, tile, 0.0))
        if not first:

            @pl.when(l == LAYERS - 1)
            def _():
                g_partner.wait_recv()
                wait_x_halo(2)
                lax.fori_loop(0, maps_here, unpool, 0)

        wait_m(l)
        at_copy(l).start()
        if first:
            send_gradients()
        averages = jnp.zeros((8, half), F32)
        scalings = jnp.zeros((8, half), F32)
        for a in range(maps_here):
            count = cnt_t[a : a + 1, :]
            average = jnp.zeros((8, half), F32)
            for mm in range(PLANE):
                average = average + coef[a, mm] * nall[mm] * st2[l, mm]
            average = jnp.sum(average, 0, keepdims=True) / count
            variance = jnp.zeros((8, half), F32)
            for mm in range(PLANE):
                v = st2[l, mm]
                gap = v - average
                variance = variance + coef[a, mm] * (
                    pltpu.roll(v, 8 - maps_here, 0) + nall[mm] * gap * gap
                )
            variance = jnp.sum(variance, 0, keepdims=True) / count
            averages = jnp.where(row8 == a, average, averages)
            scalings = jnp.where(row8 == a, lax.rsqrt(variance + epsilon), scalings)
        avg_t[l] = averages
        scl_t[l] = scalings
        wait_halo(z_halo, l)

        def activate(a, s):
            gain, shift = gain_of(l), shift_of(l)
            for n in tiles:
                average = row_of(avg_t, l, a)[:, n]
                factor = row_of(scl_t, l, a)[:, n] * gain[:, n]
                for rr in range(band + 2):
                    if rr in (0, band + 1):
                        way = rr // (band + 1)
                        v = zh[l, way, a, :, n].astype(F32) + row_of(mean_t, way, a)[:, n]
                        zbuf[l, a, rr, :, n] = v
                    else:
                        v = zbuf[l, a, rr, :, n]
                    y = (v - average) * factor + shift[:, n]
                    h = jnp.where(column[:, n] < limit(a, rr), y * jax.nn.sigmoid(y), 0.0)
                    act_own[lax.rem(l + 1, 2), a, rr, :, n] = h.astype(BF16)

            @pl.when(l < LAYERS - 1)
            def _():
                act_copy(l + 1, a).start()

            return s

        if first:
            for copy in x_partner:
                copy.wait_send()
            sent_x_halo(0, 2)
            each_x_pass(lambda copy: copy.wait_send())
        else:

            @pl.when(l == 2)
            def _():
                for a in range(maps_here):
                    act_copy(1, a).wait_send()

        lax.fori_loop(0, maps_here, activate, 0)

    forward(0, True)
    lax.fori_loop(1, LAYERS, lambda l, s: (forward(l, False), s)[1], 0)


    def pool():
        def one(a, s):
            for pr in range(2):
                total = jnp.zeros((PAD // 2, half), F32)
                position = gbuf[1 + pr, 1, a]
                for lower in range(2):
                    v = act_own[LAYERS % 2, a, 1 + 2 * pr + lower].astype(F32)
                    for n in range(lanes):
                        hrow[n] = v[:, n * 128 : (n + 1) * 128]
                    for b in range(2):
                        v = jnp.concatenate(
                            [hrow[n, pl.ds(b, PAD // 2, stride=2), :] for n in range(lanes)], 1
                        )
                        total = total + jnp.where(position == float(2 * lower + b), v, 0.0)
                pbuf[pr, a] = total.astype(BF16)
            return s

        lax.fori_loop(0, maps_here, one, 0)

    def second_rows(bit):
        return pl.ds(pl.multiple_of(bit * (half // 2), half // 2), half // 2)

    def piece_rows(p):
        return pl.ds(pl.multiple_of(p * piece, piece), piece)

    def term_slot(q):
        return lax.rem(q, 2 * TAPS)

    def c2(q):
        src = terms.at[term_slot(q), second_rows(1 - h_bit)]
        return remote(src, r2.at[q], r2_s.at[q], r2_r.at[q], h_peer, z, c)

    def z_of(n):
        return 2 * n + 1 - lax.rem(n, 2)

    def cf(q):
        passive_z = 2 * pair + turn
        there = active_z + passive_z - z
        return remote(r2.at[q], rf.at[term_slot(q)], rf_s.at[q], rf_r.at[q], m, there, c)

    def c3(q, p):
        slot = lax.rem(pair - p + actives - 1, actives)
        return remote(
            r2.at[q, piece_rows(p)], r3.at[q, slot], r3_s.at[q, p], r3_r.at[q, slot], m, z_of(p), c
        )

    def others(first, body, limit):
        def one(k):
            n = lax.rem(pair + k, actives)

            @pl.when(n < limit)
            def _():
                body(n)

        each(first, actives, one)

    def unit_of(q):
        k = lax.div(q, TAPS)
        return (LAYERS - 1 - k) * TAPS + (q - k * TAPS)

    def region(q, start, size, lane, lanes):
        start = pl.multiple_of(c * half + start, piece)
        lane = pl.multiple_of(lane, half)
        return kg_ref.at[unit_of(q), pl.ds(start, size), pl.ds(lane, lanes)]

    def cz(q, p, n):
        part = region(q, h_bit * (half // 2) + p * piece, piece, g_bit * half, half)
        return remote(fin.at[q], part, az_s.at[q, n], az_r.at[q, p], m, z_of(n), c)

    def cl(q):
        part = region(q, h_bit * (half // 2) + pair * piece, piece, g_bit * half, half)
        return pltpu.make_async_copy(fin.at[q], part, loc_s.at[q])

    def cu(q):
        passive_z = 2 * pair + turn
        there = active_z + passive_z - z
        part = region(q, h_bit * (half // 2), half // 2, g_bit * half, half)
        return remote(part, part, af_s.at[q], af_r.at[q], m, there, c)

    def cb(q):
        part = region(q, h_bit * (half // 2), half // 2, g_bit * half, half)
        return remote(part, part, ab_s.at[q], ab_r.at[q], h_peer, z, c)

    def ca(q):
        part = region(q, 0, half, g_bit * half, half)
        return remote(part, part, aa_s.at[q], aa_r.at[q], g_peer, z, c)

    def cp_part(q, start, size, lane, lanes):
        part = region(q, start, size, lane, lanes)
        return remote(part, part, ap_s.at[q], ap_r.at[q], m, z, other)

    def cp(q):
        return cp_part(q, 0, half, 0, 2 * half)

    def cp_rows(q, bit):
        return cp_part(q, bit * (half // 2), half // 2, g_bit * half, half)

    def cp_lanes(q):
        return cp_part(q, 0, half, (1 - g_bit) * half, half)

    def ready_terms(l):
        at_copy(l).wait_recv()
        for chip in range(2):
            for a in range(maps_here):
                first = a * (band + 2) * PAD
                rows = act_t[l, chip, :, first : first + (band + 2) * PAD]
                act_b[chip, :, a * band * PAD : (a + 1) * band * PAD] = rows[:, PAD : PAD + band * PAD]
        slot = lax.rem(l, 2)

        def variants(a, s):
            dzr_copy(l, a, 0).wait_recv()
            for chip in range(2):
                for rr in range(band):
                    for n in tiles:
                        if chip == 0:
                            mine, theirs = dz_own[slot, a, 1 + rr, :, n], dz_oth[slot, a, 1 + rr, :, n]
                            v = jnp.where(g_bit == c, mine, theirs)
                        else:
                            v = dzr[l, a, rr, :, n]
                        dzv[1, chip, a, rr, :, n] = v
                        v = v.astype(F32)
                        dzv[0, chip, a, rr, :, n] = pltpu.roll(v, PAD - 1, 0).astype(BF16)
                        dzv[2, chip, a, rr, :, n] = pltpu.roll(v, 1, 0).astype(BF16)
            return s

        lax.fori_loop(0, maps_here, variants, 0)

    def tap_terms(l, i, j):
        if i == 1:
            lhs = [act_b[0], act_b[1]]
        else:
            lhs = []
            for chip in range(2):
                for a in range(maps_here):
                    first = (a * (band + 2) + i) * PAD
                    lhs.append(act_t[l, chip, :, first : first + band * PAD])
        rhs = dzv[j].reshape(2 * pixels, half)
        q = (LAYERS - 1 - l) * TAPS + 3 * i + j
        got = jnp.dot(jnp.concatenate(lhs, 1), rhs, preferred_element_type=F32)
        terms[term_slot(q)] = got.astype(BF16)

    def weight_terms(l, i):
        lax.fori_loop(0, 3, lambda j, s: (tap_terms(l, i, j), s)[1], 0)

    def stage_second(q):
        c2(q).wait()
        kept = terms[term_slot(q), second_rows(h_bit)].astype(F32)
        r2[q] = (r2[q].astype(F32) + kept).astype(BF16)

        @pl.when(is_passive)
        def _():
            cf(q).start()

    def stage_fold(q):
        @pl.when(is_active)
        def _():
            cf(q).wait_recv()
            r2[q] = (r2[q].astype(F32) + rf[term_slot(q)].astype(F32)).astype(BF16)
            others(1, lambda n: c3(q, n).start(), owners)

    def stage_sum(q):
        @pl.when(is_owner)
        def _():
            for k in range(actives - 1):
                remote(
                    r3.at[q, k], r3.at[q, k], r3_s.at[q, 0], r3_r.at[q, k], m, z, c
                ).wait_recv()
            total = r2[q, piece_rows(pair)].astype(F32)
            for k in range(actives - 1):
                total = total + r3[q, k].astype(F32)
            fin[q] = total.astype(BF16)
            others(1, lambda n: cz(q, pair, n).start(), actives)
            cl(q).start()

    def stage_back(q):
        @pl.when(is_active)
        def _():
            others(1, lambda n: cz(q, n, n).wait_recv(), owners)

        @pl.when(is_owner)
        def _():
            cl(q).wait()

        @pl.when(is_active)
        def _():
            cu(q).start()

        @pl.when(is_passive)
        def _():
            cu(q).wait_recv()

        cb(q).start()
        cp_rows(q, h_bit).start()

    def stage_first(q):
        cb(q).wait_recv()
        ca(q).start()
        cp_rows(q, 1 - h_bit).start()

        @pl.when(is_active)
        def _():
            others(1, lambda n: c3(q, n).wait_send(), owners)

        @pl.when(is_passive)
        def _():
            cf(q).wait_send()

    def stage_chip(q):
        ca(q).wait_recv()
        cp_lanes(q).start()

        @pl.when(is_owner)
        def _():
            others(1, lambda n: cz(q, pair, n).wait_send(), actives)

        @pl.when(is_active)
        def _():
            cu(q).wait_send()

    def stage_done(q):
        cb(q).wait_send()
        ca(q).wait_send()
        cp(q).wait()

    def run(stage, first, last):
        lax.fori_loop(first, last, lambda q, s: (stage(q), s)[1], 0)

    def sent_dz(l):
        for a in range(maps_here):
            dz_copy(l, a).wait_send()
            for way in range(2):
                if_wanted(way, dzr_copy(l, a, way).wait_send)

    def backward(k, carry):
        l = LAYERS - 1 - k
        gain, shift = gain_of(l), shift_of(l)

        def gradient(a, rr, n):
            zhat = (zbuf[l, a, rr, :, n] - row_of(avg_t, l, a)[:, n]) * row_of(scl_t, l, a)[:, n]
            y = zhat * gain[:, n] + shift[:, n]
            s = jax.nn.sigmoid(y)
            if rr in (0, band + 1):
                upstream = dhh[l, rr // (band + 1), a, :, n].astype(F32)
            else:
                upstream = dh[a, rr - 1, :, n]
            dy = upstream * (s * (1.0 + y * (1.0 - s)))
            dy = jnp.where(column[:, n] < limit(a, rr), dy, 0.0)
            return dy, zhat

        def collect(a, tile):
            plains, crosses = [], []
            for n in tiles:
                plain = jnp.zeros((PAD, 128), F32)
                crossed = jnp.zeros((PAD, 128), F32)
                for rr in range(1, band + 1):
                    dy, zhat = gradient(a, rr, n)
                    dh[a, rr - 1, :, n] = dy
                    plain = plain + dy
                    crossed = crossed + dy * zhat
                plains.append(jnp.sum(plain, 0, keepdims=True))
                crosses.append(jnp.sum(crossed, 0, keepdims=True))
            tile = jnp.where(row8 == a, jnp.concatenate(plains, 1), tile)
            return jnp.where(row8 == a + maps_here, jnp.concatenate(crosses, 1), tile)

        e = LAYERS + l
        tile = lax.fori_loop(0, maps_here, collect, jnp.zeros((8, half), F32))
        send_z(e, tile)

        @pl.when(k == LAYERS - 1)
        def _():
            run(stage_second, 0, TAPS)

        @pl.when(k > 0)
        def _():
            ready_terms(l + 1)
            weight_terms(l + 1, 0)

        wait_z(e)
        total = st1[e, 0]
        for zz in range(1, chips):
            total = total + st1[e, zz]
        send_m(e, total)

        @pl.when(k > 0)
        def _():
            first = (LAYERS - 2 - l) * TAPS
            run(lambda q: c2(q).start(), first, first + 3)
            weight_terms(l + 1, 1)
            run(lambda q: c2(q).start(), first + 3, first + 6)
            weight_terms(l + 1, 2)
            run(lambda q: c2(q).start(), first + 6, first + 9)
            wait_halo(dh_halo, l)

        @pl.when(k == 0)
        def _():
            pool()

        wait_m(e)
        total = st2[e, 0]
        for mm in range(1, PLANE):
            total = total + st2[e, mm]
        sums_own[pl.ds(l, 1), :] = jnp.sum(
            jnp.where(row8 >= maps_here, total, 0.0), 0, keepdims=True
        )
        sums_own[pl.ds(LAYERS + l, 1), :] = jnp.sum(
            jnp.where(row8 < maps_here, total, 0.0), 0, keepdims=True
        )
        plains = jnp.zeros((8, half), F32)
        crosses = jnp.zeros((8, half), F32)
        for a in range(maps_here):
            plain = jnp.zeros((8, half), F32)
            crossed = jnp.zeros((8, half), F32)
            for mm in range(PLANE):
                v = st2[e, mm]
                plain = plain + coef[a, mm] * v
                crossed = crossed + coef[a, mm] * pltpu.roll(v, 8 - maps_here, 0)
            count = cnt_t[a : a + 1, :]
            plain = gain * (jnp.sum(plain, 0, keepdims=True) / count)
            crossed = gain * (jnp.sum(crossed, 0, keepdims=True) / count)
            plains = jnp.where(row8 == a, plain, plains)
            crosses = jnp.where(row8 == a, crossed, crosses)
        tb_t[0] = plains
        ta_t[0] = crosses

        def settle(a, s):
            for n in tiles:
                average, scaling = row_of(avg_t, l, a)[:, n], row_of(scl_t, l, a)[:, n]
                plain, crossed = row_of(tb_t, 0, a)[:, n], row_of(ta_t, 0, a)[:, n]
                for rr in range(band + 2):
                    if rr in (0, band + 1):
                        dy, zhat = gradient(a, rr, n)
                    else:
                        dy = dh[a, rr - 1, :, n]
                        zhat = (zbuf[l, a, rr, :, n] - average) * scaling
                    v = scaling * (dy * gain[:, n] - plain - zhat * crossed)
                    v = jnp.where(column[:, n] < limit(a, rr), v, 0.0)
                    dz_own[lax.rem(l, 2), a, rr, :, n] = v.astype(BF16)
            dz_copy(l, a).start()
            for way in range(2):
                if_wanted(way, dzr_copy(l, a, way).start)
            return s

        @pl.when(k == 2)
        def _():
            sent_dz(LAYERS - 1)

        lax.fori_loop(0, maps_here, settle, 0)
        products(dz_own, l, (0, 1, 2), wa, True, True)
        weight_copy(l, 2).wait()
        for a in range(maps_here):
            dz_copy(l, a).wait_recv()
        products(dz_oth, l, (0, 1, 2), wb, True, False)

        def gather(a, s):
            for n in tiles:
                for rr in range(band):
                    v = shifted(a, rr, 2, 0, n)
                    dh[a, rr, :, n] = v
                    if rr in (0, band - 1):
                        dhs[rr // (band - 1), a, :, n] = v.astype(BF16)
            return s

        lax.fori_loop(0, maps_here, gather, 0)

        @pl.when(l > 0)
        def _():
            start_halo(dh_halo, l - 1)

        return carry

    lax.fori_loop(0, LAYERS, backward, 0)
    def input_rows(a, s):
        for rr in range(band):
            dh[a, rr] = jnp.where(column < width_of(a), dh[a, rr], 0.0)
        return s

    lax.fori_loop(0, maps_here, input_rows, 0)

    outs = (
        (
            remote(dh.at[:, pl.ds(2 * other, 2)], ig_ref.at[c], out_s.at[0], out_r.at[0], m, z, other),
            pltpu.make_async_copy(dh.at[:, pl.ds(2 * c, 2)], ig_ref.at[c], out_l.at[0]),
        ),
        (
            remote(pbuf.at[other], pooled_ref.at[c], out_s.at[1], out_r.at[1], m, z, other),
            pltpu.make_async_copy(pbuf.at[c], pooled_ref.at[c], out_l.at[1]),
        ),
        (
            remote(sums_own, sums_ref.at[c], out_s.at[2], out_r.at[2], m, z, other),
            pltpu.make_async_copy(sums_own, sums_ref.at[c], out_l.at[2]),
        ),
    )
    for there, here in outs:
        there.start()
        here.start()

    g_partner.wait_send()
    sent_x_halo(2, 4)

    def sent(e, carry):
        each(1, chips, lambda k: z_copy(e, k).wait_send())
        each(1, PLANE, lambda k: m_copy(e, k).wait_send())
        return carry

    lax.fori_loop(0, 2 * LAYERS, sent, 0)
    for l in range(LAYERS):
        at_copy(l).wait_send()
    for l in range(LAYERS - 1):
        sent_dz(l)

    def drain(s, carry):
        @pl.when(s == EARLY)
        def _():
            ready_terms(0)

        for i in range(3):
            j = s - EARLY - 3 * i

            @pl.when(jnp.logical_and(j >= 0, j < 3))
            def _(i=i, j=j):
                tap_terms(0, i, j)
                c2(2 * TAPS + 3 * i + j).start()

        for stage, first, lag in (
            (stage_done, 0, 2 * FOLD + 3 * LAG),
            (stage_chip, 0, 2 * FOLD + 2 * LAG),
            (stage_first, 0, 2 * FOLD + LAG),
            (stage_back, 0, 2 * FOLD),
            (stage_sum, 0, FOLD),
            (stage_fold, 0, 0),
            (stage_second, TAPS, 0),
        ):
            q = first + s - lag

            @pl.when(jnp.logical_and(q >= first, q < UNITS))
            def _(stage=stage, q=q):
                stage(q)

        return carry

    lax.fori_loop(0, UNITS + 2 * FOLD + 3 * LAG, drain, 0)
    for a in range(maps_here):
        act_copy(2, a).wait_send()
    for there, here in outs:
        there.wait()
        here.wait()


def solution(mesh):
    chips = mesh.shape["rows"] // 2

    def per_device(
        block_input,
        conv_weights,
        norm_gains,
        norm_shifts,
        map_width,
        map_group,
        pool_index,
        task_mask,
        task_weights,
        task_grads,
    ):
        maps_here, rows_here, columns, channels = block_input.shape
        pooled_columns = pool_index.shape[2]
        height = rows_here * mesh.shape["rows"]
        half = channels // 2
        band = 2 * rows_here
        pixels = maps_here * band * PAD
        actives = chips // 2
        owners = min(actives, 8)
        piece = half // 2 // owners
        rounds = 2 * LAYERS
        slots = 2 * UNITS * (actives - 1) * piece * half + 4 * rounds * chips * 8 * half
        grant = (36 * 1024 + 256) * 1024 + slots
        vmem, dma = pltpu.VMEM, pltpu.SemaphoreType.DMA
        tile = (maps_here, band + 2, PAD, half)
        edge = (2, maps_here, PAD, half)
        whole = pl.BlockSpec(memory_space=pltpu.VMEM)
        outside = pl.BlockSpec(memory_space=pltpu.HBM)
        index_rows = jnp.transpose(pool_index, (0, 2, 1, 3))
        anywhere = pl.BlockSpec(memory_space=pl.ANY)
        pooled, ig, kg, sums = pl.pallas_call(
            functools.partial(block_kernel, chips, height),
            out_shape=(
                jax.ShapeDtypeStruct((2, maps_here, PAD // 2, half), BF16),
                jax.ShapeDtypeStruct((2, maps_here, rows_here, PAD, half), F32),
                jax.ShapeDtypeStruct((UNITS, channels, channels), BF16),
                jax.ShapeDtypeStruct((2, 8, half), F32),
            ),
            in_specs=[whole, anywhere] + [outside] * 8,
            out_specs=[anywhere] * 4,
            scratch_shapes=[
                vmem(norm_gains.shape, F32),
                vmem(norm_shifts.shape, F32),
                pltpu.SMEM(map_width.shape, jnp.int32),
                pltpu.SMEM(map_group.shape, jnp.int32),
                vmem((maps_here, pooled_columns, channels), jnp.int32),
                pltpu.SMEM(task_mask.shape, jnp.int32),
                pltpu.SMEM(task_weights.shape, F32),
                vmem(task_grads.shape, BF16),
                vmem((LAYERS, 3, 3, half, half), BF16),
                vmem((LAYERS, 3, 3, half, half), BF16),
                vmem((2,) + tile, BF16),
                vmem((2,) + tile, BF16),
                vmem((LAYERS, 2, half, maps_here * (band + 2) * PAD), BF16),
                vmem((2, half, pixels), BF16),
                vmem((LAYERS,) + tile, F32),
                vmem(edge, BF16),
                vmem((LAYERS,) + edge, BF16),
                vmem((maps_here, band, PAD, half), F32),
                vmem(edge, BF16),
                vmem((LAYERS,) + edge, BF16),
                vmem((2,) + tile, BF16),
                vmem((2,) + tile, BF16),
                vmem((LAYERS, maps_here, band, PAD, half), BF16),
                vmem((3, 2, maps_here, band, PAD, half), BF16),
                vmem((3, pixels, half), F32),
                vmem((2, 2, maps_here, PAD // 2, half), F32),
                vmem((4, 2, maps_here, PAD // 2, half), F32),
                vmem((half // 128, PAD, 128), F32),
                vmem((2, maps_here, PAD // 2, half), BF16),
                vmem((rounds, chips, 8, half), F32),
                vmem((rounds, PLANE, 8, half), F32),
                vmem((maps_here, PLANE, 8, half), F32),
                vmem((PLANE, 8, half), F32),
                vmem((2, 8, half), F32),
                vmem((8, half), F32),
                vmem((LAYERS, 8, half), F32),
                vmem((LAYERS, 8, half), F32),
                vmem((2, 8, half), F32),
                vmem((1, 8, half), F32),
                vmem((1, 8, half), F32),
                vmem((8, half), F32),
                vmem((2 * TAPS, half, half), BF16),
                vmem((UNITS, half // 2, half), BF16),
                vmem((2 * TAPS, half // 2, half), BF16),
                vmem((UNITS, actives - 1, piece, half), BF16),
                vmem((UNITS, piece, half), BF16),
                dma((8,)),
                dma((LAYERS, 3)),
                dma((6,)),
                dma((6,)),
                dma((3,)),
                dma((3,)),
                dma((rounds, chips)),
                dma((rounds, chips)),
                dma((rounds, PLANE)),
                dma((rounds, PLANE)),
                dma((LAYERS, 2)),
                dma((LAYERS, 2)),
                dma((LAYERS, 2)),
                dma((LAYERS, 2)),
                dma((LAYERS, maps_here)),
                dma((LAYERS, maps_here)),
                dma((LAYERS, maps_here)),
                dma((LAYERS, maps_here)),
                dma((3,)),
                dma((3,)),
                dma((3,)),
                dma((LAYERS,)),
                dma((LAYERS,)),
                dma((LAYERS, 2, maps_here)),
                dma((LAYERS, maps_here)),
                dma((UNITS,)),
                dma((UNITS,)),
                dma((UNITS,)),
                dma((UNITS,)),
                dma((UNITS, owners)),
                dma((UNITS, actives - 1)),
                dma((UNITS, actives)),
                dma((UNITS, owners)),
                dma((UNITS,)),
                dma((UNITS,)),
                dma((UNITS,)),
                dma((UNITS,)),
                dma((UNITS,)),
                dma((UNITS,)),
                dma((UNITS,)),
                dma((UNITS,)),
                dma((UNITS,)),
            ],
            compiler_params=pltpu.CompilerParams(
                collective_id=0,
                has_side_effects=True,
                vmem_limit_bytes=grant,
            ),
        )(
            block_input,
            conv_weights,
            *(
                pltpu.with_memory_space_constraint(v, pltpu.HBM)
                for v in (
                    norm_gains,
                    norm_shifts,
                    map_width,
                    map_group,
                    index_rows,
                    task_mask,
                    task_weights,
                    task_grads,
                )
            ),
        )
        pooled = jnp.concatenate([pooled[0], pooled[1]], -1)[:, None, :pooled_columns]
        input_grad = jnp.concatenate([ig[0], ig[1]], -1)[:, :, :columns]
        sums = jnp.concatenate([sums[0], sums[1]], -1)
        return (
            pooled,
            input_grad,
            kg.astype(F32).reshape(conv_weights.shape),
            sums[:LAYERS],
            sums[LAYERS : 2 * LAYERS],
        )

    return jax.shard_map(
        per_device,
        mesh=mesh,
        in_specs=(
            P("maps", "rows", None, None),
            P(),
            P(),
            P(),
            P(),
            P(),
            P("maps", "rows", None, None),
            P("maps", None),
            P(),
            P(None, "maps", "rows", None, None),
        ),
        out_specs=(P("maps", "rows", None, None), P("maps", "rows", None, None), P(), P(), P()),
        check_vma=False,
    )
```

```python
import functools

import jax
import jax.numpy as jnp
from jax import lax
from jax.experimental import pallas as pl
from jax.experimental.pallas import tpu as pltpu
from jax.sharding import PartitionSpec as P

MESH = pl.DeviceIdType.MESH
epsilon = 1e-05
PAD = 64
LAYERS = 3
TAPS = 9
UNITS = LAYERS * TAPS
PLANE = 4
LAG = 4
EARLY = 1
FOLD = 2
F32 = jnp.float32
BF16 = jnp.bfloat16


def each(first, last, body):
    if last - first <= 8:
        for k in range(first, last):
            body(k)
    else:
        lax.fori_loop(first, last, lambda k, s: (body(k), s)[1], 0)


def block_kernel(
    chips,
    height,
    x_ref,
    w_ref,
    gain_hbm,
    shift_hbm,
    width_hbm,
    group_hbm,
    index_hbm,
    tmask_hbm,
    tweight_hbm,
    tgrad_hbm,
    pooled_ref,
    ig_ref,
    kg_ref,
    sums_ref,
    gain_ref,
    shift_ref,
    width_ref,
    group_ref,
    index_ref,
    tmask_ref,
    tweight_ref,
    tgrad_ref,
    wa,
    wb,
    act_own,
    act_oth,
    act_t,
    act_b,
    zbuf,
    zs,
    zh,
    dh,
    dhs,
    dhh,
    dz_own,
    dz_oth,
    dzr,
    dzv,
    prod,
    gsrc,
    gbuf,
    hrow,
    pbuf,
    st1,
    st2,
    coef,
    nall,
    inv_t,
    cnt_t,
    avg_t,
    scl_t,
    mean_t,
    tb_t,
    ta_t,
    sums_own,
    terms,
    r2,
    rf,
    r3,
    fin,
    in_sem,
    w_sem,
    x_s,
    x_r,
    g_s,
    g_r,
    st1_s,
    st1_r,
    st2_s,
    st2_r,
    zh_s,
    zh_r,
    dh_s,
    dh_r,
    act_s,
    act_r,
    dz_s,
    dz_r,
    out_s,
    out_r,
    out_l,
    at_s,
    at_r,
    dzr_s,
    dzr_r,
    r2_s,
    r2_r,
    rf_s,
    rf_r,
    r3_s,
    r3_r,
    az_s,
    az_r,
    af_s,
    af_r,
    ab_s,
    ab_r,
    aa_s,
    aa_r,
    ae_s,
    ae_r,
    ap_s,
    ap_r,
    loc_s,
):
    maps_here = x_ref.shape[0]
    columns = x_ref.shape[2]
    half = x_ref.shape[3] // 2
    tasks = tgrad_ref.shape[0]
    pooled_columns = tgrad_ref.shape[3]
    lanes = half // 128
    tiles = [slice(n * 128, (n + 1) * 128) for n in range(lanes)]
    band = 4
    pixels = maps_here * band * PAD
    actives = chips // 2
    owners = min(actives, 8)
    piece = (half // 2) // owners
    m = lax.axis_index("maps")
    r = lax.axis_index("rows")
    c = lax.rem(r, 2)
    z = lax.div(r, 2)
    other = 1 - c
    first_map = m * maps_here
    x_bit = lax.rem(m, 2)
    y_bit = lax.div(m, 2)
    x_peer = m + 1 - 2 * x_bit
    y_peer = m + 2 - 4 * y_bit
    g_bit = (1 - c) * x_bit + c * y_bit
    h_bit = (1 - c) * y_bit + c * x_bit
    g_peer = (1 - c) * x_peer + c * y_peer
    h_peer = (1 - c) * y_peer + c * x_peer
    pair = lax.div(z, 2)
    turn = lax.rem(pair, 2)
    active_z = 2 * pair + 1 - turn
    is_active = z == active_z
    is_passive = z != active_z
    is_owner = jnp.logical_and(is_active, pair < owners)
    role = jnp.where(is_active, 0, 1)
    up_there = z > 0
    down_there = z < chips - 1
    row8 = lax.broadcasted_iota(jnp.int32, (8, half), 0)
    column = lax.broadcasted_iota(jnp.int32, (PAD, half), 0)

    def remote(src, dst, send, recv, mm, zz, cc):
        return pltpu.make_async_remote_copy(
            src_ref=src,
            dst_ref=dst,
            send_sem=send,
            recv_sem=recv,
            device_id=(mm, zz * 2 + cc),
            device_id_type=MESH,
        )

    def own_half(v):
        return jnp.where(c == 0, v[..., :half], v[..., half:])

    def width_of(a):
        return width_ref[first_map + a]

    own_at = pl.ds(pl.multiple_of(c * half, half), half)
    oth_at = pl.ds(pl.multiple_of(other * half, half), half)

    def weight_copy(l, n):
        dst = (wa, wb, wb)[n]
        k_at, o_at = ((own_at, own_at), (oth_at, own_at), (own_at, oth_at))[n]
        return pltpu.make_async_copy(w_ref.at[l, :, :, k_at, o_at], dst.at[l], w_sem.at[l, n])

    fetches = [
        pltpu.make_async_copy(src, dst, in_sem.at[n])
        for n, (src, dst) in enumerate(
            (
                (width_hbm, width_ref),
                (group_hbm, group_ref),
                (tmask_hbm, tmask_ref),
                (tweight_hbm, tweight_ref),
                (gain_hbm, gain_ref),
                (shift_hbm, shift_ref),
                (index_hbm.at[:, :, 0, :], index_ref),
                (tgrad_hbm, tgrad_ref),
            )
        )
    ]
    for fetch in fetches:
        fetch.start()
    for l in range(LAYERS):
        weight_copy(l, 0).start()
        weight_copy(l, 1).start()

    barrier = pltpu.get_barrier_semaphore()

    def greet(k):
        rr = lax.rem(r + k, 2 * chips)
        pl.semaphore_signal(barrier, inc=1, device_id=(m, rr), device_id_type=MESH)

    each(1, 2 * chips, greet)
    for k in range(1, PLANE):
        for core in (c, other):
            there = (lax.rem(m + k, PLANE), z * 2 + core)
            pl.semaphore_signal(barrier, inc=1, device_id=there, device_id_type=MESH)

    for fetch in fetches:
        fetch.wait()

    mine = pl.ds(1 + 2 * c, 2)
    for a in range(maps_here):
        inside = lax.broadcasted_iota(jnp.int32, (columns, 2 * half), 0) < width_of(a)
        for rr in range(2):
            v = jnp.where(inside, x_ref[a, rr].astype(F32), 0.0).astype(BF16)
            spot = 1 + 2 * c + rr
            act_own[0, a, spot, pl.ds(48, 16), :] = jnp.zeros((16, half), BF16)
            act_oth[0, a, spot, pl.ds(48, 16), :] = jnp.zeros((16, half), BF16)
            act_own[0, a, spot, pl.ds(0, columns), :] = own_half(v)
            act_oth[0, a, spot, pl.ds(0, columns), :] = jnp.where(
                c == 0, v[:, half:], v[:, :half]
            )

    @pl.when(z == 0)
    def _():
        act_own[0, :, 0] = jnp.zeros((maps_here, PAD, half), BF16)
        act_oth[0, :, 0] = jnp.zeros((maps_here, PAD, half), BF16)

    @pl.when(z == chips - 1)
    def _():
        act_own[0, :, 5] = jnp.zeros((maps_here, PAD, half), BF16)
        act_oth[0, :, 5] = jnp.zeros((maps_here, PAD, half), BF16)

    pl.semaphore_wait(barrier, 2 * chips - 1 + 2 * (PLANE - 1))

    x_partner = (
        remote(act_own.at[0, :, mine], act_oth.at[0, :, mine], x_s.at[0], x_r.at[0], m, z, other),
        remote(act_oth.at[0, :, mine], act_own.at[0, :, mine], x_s.at[1], x_r.at[1], m, z, other),
    )
    g_partner = remote(gsrc.at[other], gbuf.at[1 + c], g_s.at[0], g_r.at[0], m, z, other)

    def x_halo(n, src_row, dst_row, zz):
        cc = (c, other)[n % 2]
        low = dst_row == band + 1
        if n >= 2:
            src, dst = gsrc.at[cc], gbuf.at[3 if low else 0]
            return remote(src, dst, g_s.at[n - 1], g_r.at[1 if low else 2], m, zz, cc)
        src, dst = (act_own, act_oth)[n].at[0, :, src_row], act_own.at[0, :, dst_row]
        return remote(src, dst, x_s.at[2 + n], x_r.at[2 if low else 3], m, zz, cc)

    def x_pass(row):
        n = 4 if row == 0 else 5
        src, dst = act_own.at[0, :, row], act_oth.at[0, :, row]
        return remote(src, dst, x_s.at[n], x_r.at[n], m, z, other)

    for copy in x_partner:
        copy.start()

    @pl.when(jnp.logical_and(c == 0, up_there))
    def _():
        for n in range(2):
            x_halo(n, 1, 5, z - 1).start()

    @pl.when(jnp.logical_and(c == 1, down_there))
    def _():
        for n in range(2):
            x_halo(n, 4, 0, z + 1).start()

    gsrc[...] = jnp.zeros(gsrc.shape, F32)
    for a in range(maps_here):
        total = None
        for t in range(tasks):
            scale = tweight_ref[t] * tmask_ref[a, t].astype(F32)
            term = tgrad_ref[t, a, 0].astype(F32) * scale
            total = term if total is None else total + term
        position = index_ref[a].astype(F32)
        for h in range(2):
            gsrc[h, 0, a, pl.ds(0, pooled_columns), :] = total[:, h * half : (h + 1) * half]
            gsrc[h, 1, a, pl.ds(0, pooled_columns), :] = position[:, h * half : (h + 1) * half]
    gbuf[1 + c] = gsrc[c]

    for mm in range(PLANE):
        sizes = jnp.zeros((8, half), F32)
        for b in range(maps_here):
            sizes = jnp.where(
                row8 == b, (width_ref[mm * maps_here + b] * height).astype(F32), sizes
            )
        nall[mm] = sizes
    inside_sizes = jnp.zeros((8, half), F32)
    for b in range(maps_here):
        inside_sizes = jnp.where(row8 == b, (width_of(b) * band).astype(F32), inside_sizes)
    inv_t[0] = inside_sizes
    inv_t[1] = jnp.where(row8 < maps_here, 1.0 / jnp.maximum(inside_sizes, 1.0), 0.0)
    counts = jnp.ones((8, half), F32)
    for a in range(maps_here):
        total = jnp.zeros((1, half), F32)
        for mm in range(PLANE):
            same = jnp.zeros((8, half), F32)
            for b in range(maps_here):
                alike = group_ref[first_map + a] == group_ref[mm * maps_here + b]
                same = jnp.where(row8 == b, jnp.where(alike, 1.0, 0.0), same)
            coef[a, mm] = same
            total = total + jnp.sum(same * nall[mm], 0, keepdims=True)
        counts = jnp.where(row8 == a, total, counts)
    cnt_t[...] = counts

    def z_copy(e, k):
        zz = lax.rem(z + k, chips)
        return remote(st1.at[e, z], st1.at[e, z], st1_s.at[e, k], st1_r.at[e, z], m, zz, c)

    def z_arrival(e, k):
        zz = lax.rem(z + k, chips)
        return remote(st1.at[e, zz], st1.at[e, zz], st1_s.at[e, k], st1_r.at[e, zz], m, zz, c)

    def m_copy(e, k):
        mm = lax.rem(m + k, PLANE)
        return remote(st2.at[e, m], st2.at[e, m], st2_s.at[e, k], st2_r.at[e, m], mm, z, c)

    def m_arrival(e, k):
        mm = lax.rem(m + k, PLANE)
        return remote(st2.at[e, mm], st2.at[e, mm], st2_s.at[e, k], st2_r.at[e, mm], mm, z, c)

    def send_z(e, tile):
        st1[e, z] = tile
        each(1, chips, lambda k: z_copy(e, k).start())

    def wait_z(e):
        each(1, chips, lambda k: z_arrival(e, k).wait_recv())

    def send_m(e, tile):
        st2[e, m] = tile
        each(1, PLANE, lambda k: m_copy(e, k).start())

    def wait_m(e):
        each(1, PLANE, lambda k: m_arrival(e, k).wait_recv())

    def products(source, l, taps, kernel, transposed, fresh):
        starts = [2 - i if transposed else i for i in taps]
        lhs = jnp.concatenate(
            [source[lax.rem(l, 2), :, s : s + band].reshape(pixels, half) for s in starts], 1
        )
        for j in range(3):
            rhs = jnp.concatenate([kernel[l, i, j] for i in taps], 1 if transposed else 0)
            got = lax.dot_general(
                lhs,
                rhs,
                (((1,), (1 if transposed else 0,)), ((), ())),
                preferred_element_type=F32,
            )
            if fresh:
                prod[j] = got
            else:
                prod[j] = prod[j] + got

    def shifted(a, rr, before, behind, n):
        rows = pl.ds(pl.multiple_of((a * band + rr) * PAD, PAD), PAD)
        return (
            prod[1, rows, n]
            + pltpu.roll(prod[before, rows, n], 1, 0)
            + pltpu.roll(prod[behind, rows, n], PAD - 1, 0)
        )

    def row_of(table, l, a):
        return table[l, pl.ds(a, 1), :]

    def gain_of(l):
        return own_half(gain_ref[pl.ds(l, 1), :])

    def shift_of(l):
        return own_half(shift_ref[pl.ds(l, 1), :])

    def limit(a, rr):
        w = width_of(a)
        if rr == 0:
            return jnp.where(up_there, w, 0)
        if rr == band + 1:
            return jnp.where(down_there, w, 0)
        return w

    def z_halo(l, way):
        there = z - 1 + 2 * way
        return remote(zs.at[way], zh.at[l, 1 - way], zh_s.at[l, way], zh_r.at[l, way], m, there, c)

    def dh_halo(l, way):
        there = z - 1 + 2 * way
        return remote(dhs.at[way], dhh.at[l, 1 - way], dh_s.at[l, way], dh_r.at[l, way], m, there, c)

    def start_halo(halo, l):
        @pl.when(up_there)
        def _():
            halo(l, 0).start()

        @pl.when(down_there)
        def _():
            halo(l, 1).start()

    def wait_halo(halo, l):
        @pl.when(up_there)
        def _():
            halo(l, 1).wait_recv()
            halo(l, 0).wait_send()

        @pl.when(down_there)
        def _():
            halo(l, 0).wait_recv()
            halo(l, 1).wait_send()

    def act_copy(l, a):
        slot = lax.rem(l, 2)
        src, dst = act_own.at[slot, a], act_oth.at[slot, a]
        return remote(src, dst, act_s.at[l, a], act_r.at[l, a], m, z, other)

    def at_copy(l):
        return remote(act_t.at[l, 0], act_t.at[l, 1], at_s.at[l], at_r.at[l], g_peer, z, c)

    def dzr_copy(l, a, way):
        src, dst = dz_own.at[lax.rem(l, 2), a, pl.ds(1, band)], dzr.at[l, a]
        peer = (x_peer, y_peer)[way]
        return remote(src, dst, dzr_s.at[l, way, a], dzr_r.at[l, a], peer, z, way)

    def if_wanted(way, body):
        @pl.when((x_bit, y_bit)[way] + c == 1)
        def _():
            body()

    def dz_copy(l, a):
        slot = lax.rem(l, 2)
        src, dst = dz_own.at[slot, a], dz_oth.at[slot, a]
        return remote(src, dst, dz_s.at[l, a], dz_r.at[l, a], m, z, other)

    def send_gradients():
        g_partner.start()

        @pl.when(jnp.logical_and(c == 0, up_there))
        def _():
            for n in range(2, 4):
                x_halo(n, 1, 5, z - 1).start()

        @pl.when(jnp.logical_and(c == 1, down_there))
        def _():
            for n in range(2, 4):
                x_halo(n, 4, 0, z + 1).start()

    def if_there(way, body):
        @pl.when((up_there, down_there)[way])
        def _():
            body()

    def wait_x_halo(n):
        if_there(0, lambda: x_halo(n, 4, 0, z - 1).wait_recv())
        if_there(1, lambda: x_halo(n, 1, 5, z + 1).wait_recv())

    def each_x_pass(act):
        if_there(0, lambda: act(x_pass(0)))
        if_there(1, lambda: act(x_pass(band + 1)))

    def sent_x_halo(first, last):
        @pl.when(jnp.logical_and(c == 0, up_there))
        def _():
            for n in range(first, last):
                x_halo(n, 1, 5, z - 1).wait_send()

        @pl.when(jnp.logical_and(c == 1, down_there))
        def _():
            for n in range(first, last):
                x_halo(n, 4, 0, z + 1).wait_send()

    def unpool(a, s):
        for rr in range(band + 2):
            slot, lower = (rr + 1) // 2, (rr + 1) % 2
            g = gbuf[slot, 0, a]
            position = gbuf[slot, 1, a]
            for b in range(2):
                v = jnp.where(position == float(2 * lower + b), g, 0.0)
                for n in range(lanes):
                    hrow[n, pl.ds(b, PAD // 2, stride=2), :] = v[:, n * 128 : (n + 1) * 128]
            v = jnp.concatenate([hrow[n] for n in range(lanes)], 1)
            if rr in (0, band + 1):
                dhh[LAYERS - 1, rr // (band + 1), a] = v.astype(BF16)
            else:
                dh[a, rr - 1] = v
        return s

    def forward(l, first):
        weight_copy(l, 0).wait()
        weight_copy(l, 1).wait()
        if first:
            for copy in x_partner:
                copy.wait_recv()
            products(act_own, l, (1,), wa, False, True)
            products(act_oth, l, (1,), wb, False, False)
            wait_x_halo(0)
            each_x_pass(lambda copy: copy.start())
            products(act_own, l, (0, 2), wa, False, False)
            each_x_pass(lambda copy: copy.wait_recv())
            products(act_oth, l, (0, 2), wb, False, False)
        else:
            products(act_own, l, (0, 1, 2), wa, False, True)
            for a in range(maps_here):
                act_copy(l, a).wait_recv()
            products(act_oth, l, (0, 1, 2), wb, False, False)
        weight_copy(l, 2).start()

        def collect(a, tile):
            inside = column[:, :128] < width_of(a)
            pixels_inside = (width_of(a) * band).astype(F32)
            totals, squares = [], []
            for n in tiles:
                total = jnp.zeros((PAD, 128), F32)
                for rr in range(band):
                    v = shifted(a, rr, 0, 2, n)
                    zbuf[l, a, 1 + rr, :, n] = v
                    total = total + jnp.where(inside, v, 0.0)
                total = jnp.sum(total, 0, keepdims=True)
                mean = total / pixels_inside
                square = jnp.zeros((PAD, 128), F32)
                for rr in range(band):
                    v = jnp.where(inside, zbuf[l, a, 1 + rr, :, n] - mean, 0.0)
                    square = square + v * v
                    if rr in (0, band - 1):
                        zs[rr // (band - 1), a, :, n] = v.astype(BF16)
                totals.append(total)
                squares.append(jnp.sum(square, 0, keepdims=True))
            tile = jnp.where(row8 == a, jnp.concatenate(totals, 1), tile)
            return jnp.where(row8 == a + maps_here, jnp.concatenate(squares, 1), tile)

        tile = lax.fori_loop(0, maps_here, collect, jnp.zeros((8, half), F32))
        send_z(l, tile)
        start_halo(z_halo, l)
        act_t[l, 0] = act_own[lax.rem(l, 2)].reshape(maps_here * (band + 2) * PAD, half).T
        wait_z(l)
        sizes, inverse = inv_t[0], inv_t[1]
        mean_t[0] = st1[l, jnp.maximum(z - 1, 0)] * inverse
        mean_t[1] = st1[l, jnp.minimum(z + 1, chips - 1)] * inverse
        total = st1[l, 0]
        for zz in range(1, chips):
            total = total + st1[l, zz]
        mean = total * inverse * (1.0 / chips)
        square = jnp.zeros((8, half), F32)
        for zz in range(chips):
            v = st1[l, zz]
            gap = v * inverse - mean
            square = square + pltpu.roll(v, 8 - maps_here, 0) + sizes * gap * gap
        tile = jnp.where(row8 < maps_here, mean, pltpu.roll(square, maps_here, 0))
        send_m(l, jnp.where(row8 < 2 * maps_here, tile, 0.0))
        if not first:

            @pl.when(l == LAYERS - 1)
            def _():
                g_partner.wait_recv()
                wait_x_halo(2)
                lax.fori_loop(0, maps_here, unpool, 0)

        wait_m(l)
        at_copy(l).start()
        if first:
            send_gradients()
        averages = jnp.zeros((8, half), F32)
        scalings = jnp.zeros((8, half), F32)
        for a in range(maps_here):
            count = cnt_t[a : a + 1, :]
            average = jnp.zeros((8, half), F32)
            for mm in range(PLANE):
                average = average + coef[a, mm] * nall[mm] * st2[l, mm]
            average = jnp.sum(average, 0, keepdims=True) / count
            variance = jnp.zeros((8, half), F32)
            for mm in range(PLANE):
                v = st2[l, mm]
                gap = v - average
                variance = variance + coef[a, mm] * (
                    pltpu.roll(v, 8 - maps_here, 0) + nall[mm] * gap * gap
                )
            variance = jnp.sum(variance, 0, keepdims=True) / count
            averages = jnp.where(row8 == a, average, averages)
            scalings = jnp.where(row8 == a, lax.rsqrt(variance + epsilon), scalings)
        avg_t[l] = averages
        scl_t[l] = scalings
        wait_halo(z_halo, l)

        def activate(a, s):
            gain, shift = gain_of(l), shift_of(l)
            for n in tiles:
                average = row_of(avg_t, l, a)[:, n]
                factor = row_of(scl_t, l, a)[:, n] * gain[:, n]
                for rr in range(band + 2):
                    if rr in (0, band + 1):
                        way = rr // (band + 1)
                        v = zh[l, way, a, :, n].astype(F32) + row_of(mean_t, way, a)[:, n]
                        zbuf[l, a, rr, :, n] = v
                    else:
                        v = zbuf[l, a, rr, :, n]
                    y = (v - average) * factor + shift[:, n]
                    h = jnp.where(column[:, n] < limit(a, rr), y * jax.nn.sigmoid(y), 0.0)
                    act_own[lax.rem(l + 1, 2), a, rr, :, n] = h.astype(BF16)

            @pl.when(l < LAYERS - 1)
            def _():
                act_copy(l + 1, a).start()

            return s

        if first:
            for copy in x_partner:
                copy.wait_send()
            sent_x_halo(0, 2)
            each_x_pass(lambda copy: copy.wait_send())
        else:

            @pl.when(l == 2)
            def _():
                for a in range(maps_here):
                    act_copy(1, a).wait_send()

        lax.fori_loop(0, maps_here, activate, 0)

    forward(0, True)
    lax.fori_loop(1, LAYERS, lambda l, s: (forward(l, False), s)[1], 0)


    def pool():
        def one(a, s):
            for pr in range(2):
                total = jnp.zeros((PAD // 2, half), F32)
                position = gbuf[1 + pr, 1, a]
                for lower in range(2):
                    v = act_own[LAYERS % 2, a, 1 + 2 * pr + lower].astype(F32)
                    for n in range(lanes):
                        hrow[n] = v[:, n * 128 : (n + 1) * 128]
                    for b in range(2):
                        v = jnp.concatenate(
                            [hrow[n, pl.ds(b, PAD // 2, stride=2), :] for n in range(lanes)], 1
                        )
                        total = total + jnp.where(position == float(2 * lower + b), v, 0.0)
                pbuf[pr, a] = total.astype(BF16)
            return s

        lax.fori_loop(0, maps_here, one, 0)

    def second_rows(bit):
        return pl.ds(pl.multiple_of(bit * (half // 2), half // 2), half // 2)

    def piece_rows(p):
        return pl.ds(pl.multiple_of(p * piece, piece), piece)

    def term_slot(q):
        return lax.rem(q, 2 * TAPS)

    def c2(q):
        src = terms.at[term_slot(q), second_rows(1 - h_bit)]
        return remote(src, r2.at[q], r2_s.at[q], r2_r.at[q], h_peer, z, c)

    def z_of(n):
        return 2 * n + 1 - lax.rem(n, 2)

    def cf(q):
        passive_z = 2 * pair + turn
        there = active_z + passive_z - z
        return remote(r2.at[q], rf.at[term_slot(q)], rf_s.at[q], rf_r.at[q], m, there, c)

    def c3(q, p):
        slot = lax.rem(pair - p + actives - 1, actives)
        return remote(
            r2.at[q, piece_rows(p)], r3.at[q, slot], r3_s.at[q, p], r3_r.at[q, slot], m, z_of(p), c
        )

    def others(first, body, limit):
        def one(k):
            n = lax.rem(pair + k, actives)

            @pl.when(n < limit)
            def _():
                body(n)

        each(first, actives, one)

    def unit_of(q):
        k = lax.div(q, TAPS)
        return (LAYERS - 1 - k) * TAPS + (q - k * TAPS)

    def region(q, start, size, lane, lanes):
        start = pl.multiple_of(c * half + start, piece)
        lane = pl.multiple_of(lane, half)
        return kg_ref.at[unit_of(q), pl.ds(start, size), pl.ds(lane, lanes)]

    def cz(q, p, n):
        part = region(q, h_bit * (half // 2) + p * piece, piece, g_bit * half, half)
        return remote(fin.at[q], part, az_s.at[q, n], az_r.at[q, p], m, z_of(n), c)

    def cl(q):
        part = region(q, h_bit * (half // 2) + pair * piece, piece, g_bit * half, half)
        return pltpu.make_async_copy(fin.at[q], part, loc_s.at[q])

    def cu(q):
        passive_z = 2 * pair + turn
        there = active_z + passive_z - z
        part = region(q, h_bit * (half // 2), half // 2, g_bit * half, half)
        return remote(part, part, af_s.at[q], af_r.at[q], m, there, c)

    def cb(q):
        part = region(q, h_bit * (half // 2), half // 2, g_bit * half, half)
        return remote(part, part, ab_s.at[q], ab_r.at[q], h_peer, z, c)

    def ca(q):
        part = region(q, 0, half, g_bit * half, half)
        return remote(part, part, aa_s.at[q], aa_r.at[q], g_peer, z, c)

    def plan(q):
        k = lax.rem(q, 4)
        both = jnp.logical_or(lax.rem(k, 2) == 0, q >= 2 * TAPS)
        mine = jnp.logical_or(both, lax.div(k, 2) == role)
        return mine, jnp.logical_and(mine, jnp.logical_not(both)), jnp.logical_not(mine)

    def ce(q):
        passive_z = 2 * pair + turn
        there = active_z + passive_z - z
        part = region(q, 0, half, (1 - g_bit) * half, half)
        return remote(part, part, ae_s.at[q], ae_r.at[q], m, there, c)

    def cp_part(q, start, size, lane, lanes):
        part = region(q, start, size, lane, lanes)
        return remote(part, part, ap_s.at[q], ap_r.at[q], m, z, other)

    def cp(q):
        return cp_part(q, 0, half, 0, 2 * half)

    def cp_rows(q, bit):
        return cp_part(q, bit * (half // 2), half // 2, g_bit * half, half)

    def cp_lanes(q):
        return cp_part(q, 0, half, (1 - g_bit) * half, half)

    def ready_terms(l):
        at_copy(l).wait_recv()
        for chip in range(2):
            for a in range(maps_here):
                first = a * (band + 2) * PAD
                rows = act_t[l, chip, :, first : first + (band + 2) * PAD]
                act_b[chip, :, a * band * PAD : (a + 1) * band * PAD] = rows[:, PAD : PAD + band * PAD]
        slot = lax.rem(l, 2)

        def variants(a, s):
            dzr_copy(l, a, 0).wait_recv()
            for chip in range(2):
                for rr in range(band):
                    for n in tiles:
                        if chip == 0:
                            mine, theirs = dz_own[slot, a, 1 + rr, :, n], dz_oth[slot, a, 1 + rr, :, n]
                            v = jnp.where(g_bit == c, mine, theirs)
                        else:
                            v = dzr[l, a, rr, :, n]
                        dzv[1, chip, a, rr, :, n] = v
                        v = v.astype(F32)
                        dzv[0, chip, a, rr, :, n] = pltpu.roll(v, PAD - 1, 0).astype(BF16)
                        dzv[2, chip, a, rr, :, n] = pltpu.roll(v, 1, 0).astype(BF16)
            return s

        lax.fori_loop(0, maps_here, variants, 0)

    def tap_terms(l, i, j):
        if i == 1:
            lhs = [act_b[0], act_b[1]]
        else:
            lhs = []
            for chip in range(2):
                for a in range(maps_here):
                    first = (a * (band + 2) + i) * PAD
                    lhs.append(act_t[l, chip, :, first : first + band * PAD])
        rhs = dzv[j].reshape(2 * pixels, half)
        q = (LAYERS - 1 - l) * TAPS + 3 * i + j
        got = jnp.dot(jnp.concatenate(lhs, 1), rhs, preferred_element_type=F32)
        terms[term_slot(q)] = got.astype(BF16)

    def weight_terms(l, i):
        lax.fori_loop(0, 3, lambda j, s: (tap_terms(l, i, j), s)[1], 0)

    def stage_second(q):
        c2(q).wait()
        kept = terms[term_slot(q), second_rows(h_bit)].astype(F32)
        r2[q] = (r2[q].astype(F32) + kept).astype(BF16)

        @pl.when(is_passive)
        def _():
            cf(q).start()

    def stage_fold(q):
        @pl.when(is_active)
        def _():
            cf(q).wait_recv()
            r2[q] = (r2[q].astype(F32) + rf[term_slot(q)].astype(F32)).astype(BF16)
            others(1, lambda n: c3(q, n).start(), owners)

    def stage_sum(q):
        @pl.when(is_owner)
        def _():
            for k in range(actives - 1):
                remote(
                    r3.at[q, k], r3.at[q, k], r3_s.at[q, 0], r3_r.at[q, k], m, z, c
                ).wait_recv()
            total = r2[q, piece_rows(pair)].astype(F32)
            for k in range(actives - 1):
                total = total + r3[q, k].astype(F32)
            fin[q] = total.astype(BF16)
            others(1, lambda n: cz(q, pair, n).start(), actives)
            cl(q).start()

    def stage_back(q):
        @pl.when(is_active)
        def _():
            others(1, lambda n: cz(q, n, n).wait_recv(), owners)

        @pl.when(is_owner)
        def _():
            cl(q).wait()

        @pl.when(is_active)
        def _():
            cu(q).start()

        @pl.when(is_passive)
        def _():
            cu(q).wait_recv()

        cb(q).start()
        cp_rows(q, h_bit).start()

    def stage_first(q):
        cb(q).wait_recv()
        mine, _, _ = plan(q)

        @pl.when(mine)
        def _():
            ca(q).start()

        cp_rows(q, 1 - h_bit).start()

        @pl.when(is_active)
        def _():
            others(1, lambda n: c3(q, n).wait_send(), owners)

        @pl.when(is_passive)
        def _():
            cf(q).wait_send()

    def stage_chip(q):
        mine, for_both, _ = plan(q)

        @pl.when(mine)
        def _():
            ca(q).wait_recv()

        @pl.when(for_both)
        def _():
            ce(q).start()

        @pl.when(mine)
        def _():
            cp_lanes(q).start()

        @pl.when(is_owner)
        def _():
            others(1, lambda n: cz(q, pair, n).wait_send(), actives)

        @pl.when(is_active)
        def _():
            cu(q).wait_send()

    def stage_late(q):
        _, _, not_mine = plan(q)

        @pl.when(not_mine)
        def _():
            ce(q).wait_recv()
            cp_lanes(q).start()

    def stage_done(q):
        mine, for_both, _ = plan(q)
        cb(q).wait_send()

        @pl.when(mine)
        def _():
            ca(q).wait_send()

        @pl.when(for_both)
        def _():
            ce(q).wait_send()

        cp(q).wait()

    def run(stage, first, last):
        lax.fori_loop(first, last, lambda q, s: (stage(q), s)[1], 0)

    def sent_dz(l):
        for a in range(maps_here):
            dz_copy(l, a).wait_send()
            for way in range(2):
                if_wanted(way, dzr_copy(l, a, way).wait_send)

    def backward(k, carry):
        l = LAYERS - 1 - k
        gain, shift = gain_of(l), shift_of(l)

        def gradient(a, rr, n):
            zhat = (zbuf[l, a, rr, :, n] - row_of(avg_t, l, a)[:, n]) * row_of(scl_t, l, a)[:, n]
            y = zhat * gain[:, n] + shift[:, n]
            s = jax.nn.sigmoid(y)
            if rr in (0, band + 1):
                upstream = dhh[l, rr // (band + 1), a, :, n].astype(F32)
            else:
                upstream = dh[a, rr - 1, :, n]
            dy = upstream * (s * (1.0 + y * (1.0 - s)))
            dy = jnp.where(column[:, n] < limit(a, rr), dy, 0.0)
            return dy, zhat

        def collect(a, tile):
            plains, crosses = [], []
            for n in tiles:
                plain = jnp.zeros((PAD, 128), F32)
                crossed = jnp.zeros((PAD, 128), F32)
                for rr in range(1, band + 1):
                    dy, zhat = gradient(a, rr, n)
                    dh[a, rr - 1, :, n] = dy
                    plain = plain + dy
                    crossed = crossed + dy * zhat
                plains.append(jnp.sum(plain, 0, keepdims=True))
                crosses.append(jnp.sum(crossed, 0, keepdims=True))
            tile = jnp.where(row8 == a, jnp.concatenate(plains, 1), tile)
            return jnp.where(row8 == a + maps_here, jnp.concatenate(crosses, 1), tile)

        e = LAYERS + l
        tile = lax.fori_loop(0, maps_here, collect, jnp.zeros((8, half), F32))
        send_z(e, tile)

        @pl.when(k == LAYERS - 1)
        def _():
            run(stage_second, 0, TAPS)

        @pl.when(k > 0)
        def _():
            ready_terms(l + 1)
            weight_terms(l + 1, 0)

        wait_z(e)
        total = st1[e, 0]
        for zz in range(1, chips):
            total = total + st1[e, zz]
        send_m(e, total)

        @pl.when(k > 0)
        def _():
            first = (LAYERS - 2 - l) * TAPS
            run(lambda q: c2(q).start(), first, first + 3)
            weight_terms(l + 1, 1)
            run(lambda q: c2(q).start(), first + 3, first + 6)
            weight_terms(l + 1, 2)
            run(lambda q: c2(q).start(), first + 6, first + 9)
            wait_halo(dh_halo, l)

        @pl.when(k == 0)
        def _():
            pool()

        wait_m(e)
        total = st2[e, 0]
        for mm in range(1, PLANE):
            total = total + st2[e, mm]
        sums_own[pl.ds(l, 1), :] = jnp.sum(
            jnp.where(row8 >= maps_here, total, 0.0), 0, keepdims=True
        )
        sums_own[pl.ds(LAYERS + l, 1), :] = jnp.sum(
            jnp.where(row8 < maps_here, total, 0.0), 0, keepdims=True
        )
        plains = jnp.zeros((8, half), F32)
        crosses = jnp.zeros((8, half), F32)
        for a in range(maps_here):
            plain = jnp.zeros((8, half), F32)
            crossed = jnp.zeros((8, half), F32)
            for mm in range(PLANE):
                v = st2[e, mm]
                plain = plain + coef[a, mm] * v
                crossed = crossed + coef[a, mm] * pltpu.roll(v, 8 - maps_here, 0)
            count = cnt_t[a : a + 1, :]
            plain = gain * (jnp.sum(plain, 0, keepdims=True) / count)
            crossed = gain * (jnp.sum(crossed, 0, keepdims=True) / count)
            plains = jnp.where(row8 == a, plain, plains)
            crosses = jnp.where(row8 == a, crossed, crosses)
        tb_t[0] = plains
        ta_t[0] = crosses

        def settle(a, s):
            for n in tiles:
                average, scaling = row_of(avg_t, l, a)[:, n], row_of(scl_t, l, a)[:, n]
                plain, crossed = row_of(tb_t, 0, a)[:, n], row_of(ta_t, 0, a)[:, n]
                for rr in range(band + 2):
                    if rr in (0, band + 1):
                        dy, zhat = gradient(a, rr, n)
                    else:
                        dy = dh[a, rr - 1, :, n]
                        zhat = (zbuf[l, a, rr, :, n] - average) * scaling
                    v = scaling * (dy * gain[:, n] - plain - zhat * crossed)
                    v = jnp.where(column[:, n] < limit(a, rr), v, 0.0)
                    dz_own[lax.rem(l, 2), a, rr, :, n] = v.astype(BF16)
            dz_copy(l, a).start()
            for way in range(2):
                if_wanted(way, dzr_copy(l, a, way).start)
            return s

        @pl.when(k == 2)
        def _():
            sent_dz(LAYERS - 1)

        lax.fori_loop(0, maps_here, settle, 0)
        products(dz_own, l, (0, 1, 2), wa, True, True)
        weight_copy(l, 2).wait()
        for a in range(maps_here):
            dz_copy(l, a).wait_recv()
        products(dz_oth, l, (0, 1, 2), wb, True, False)

        def gather(a, s):
            for n in tiles:
                for rr in range(band):
                    v = shifted(a, rr, 2, 0, n)
                    dh[a, rr, :, n] = v
                    if rr in (0, band - 1):
                        dhs[rr // (band - 1), a, :, n] = v.astype(BF16)
            return s

        lax.fori_loop(0, maps_here, gather, 0)

        @pl.when(l > 0)
        def _():
            start_halo(dh_halo, l - 1)

        return carry

    lax.fori_loop(0, LAYERS, backward, 0)
    def input_rows(a, s):
        for rr in range(band):
            dh[a, rr] = jnp.where(column < width_of(a), dh[a, rr], 0.0)
        return s

    lax.fori_loop(0, maps_here, input_rows, 0)

    outs = (
        (
            remote(dh.at[:, pl.ds(2 * other, 2)], ig_ref.at[c], out_s.at[0], out_r.at[0], m, z, other),
            pltpu.make_async_copy(dh.at[:, pl.ds(2 * c, 2)], ig_ref.at[c], out_l.at[0]),
        ),
        (
            remote(pbuf.at[other], pooled_ref.at[c], out_s.at[1], out_r.at[1], m, z, other),
            pltpu.make_async_copy(pbuf.at[c], pooled_ref.at[c], out_l.at[1]),
        ),
        (
            remote(sums_own, sums_ref.at[c], out_s.at[2], out_r.at[2], m, z, other),
            pltpu.make_async_copy(sums_own, sums_ref.at[c], out_l.at[2]),
        ),
    )
    for there, here in outs:
        there.start()
        here.start()

    g_partner.wait_send()
    sent_x_halo(2, 4)

    def sent(e, carry):
        each(1, chips, lambda k: z_copy(e, k).wait_send())
        each(1, PLANE, lambda k: m_copy(e, k).wait_send())
        return carry

    lax.fori_loop(0, 2 * LAYERS, sent, 0)
    for l in range(LAYERS):
        at_copy(l).wait_send()
    for l in range(LAYERS - 1):
        sent_dz(l)

    def drain(s, carry):
        @pl.when(s == EARLY)
        def _():
            ready_terms(0)

        for i in range(3):
            j = s - EARLY - 3 * i

            @pl.when(jnp.logical_and(j >= 0, j < 3))
            def _(i=i, j=j):
                tap_terms(0, i, j)
                c2(2 * TAPS + 3 * i + j).start()

        for stage, first, lag in (
            (stage_done, 0, 2 * FOLD + 4 * LAG),
            (stage_late, 0, 2 * FOLD + 3 * LAG),
            (stage_chip, 0, 2 * FOLD + 2 * LAG),
            (stage_first, 0, 2 * FOLD + LAG),
            (stage_back, 0, 2 * FOLD),
            (stage_sum, 0, FOLD),
            (stage_fold, 0, 0),
            (stage_second, TAPS, 0),
        ):
            q = first + s - lag

            @pl.when(jnp.logical_and(q >= first, q < UNITS))
            def _(stage=stage, q=q):
                stage(q)

        return carry

    lax.fori_loop(0, UNITS + 2 * FOLD + 4 * LAG, drain, 0)
    for a in range(maps_here):
        act_copy(2, a).wait_send()
    for there, here in outs:
        there.wait()
        here.wait()


RING = 4


def finish_kernel(kg_ref, pooled_ref, sums_ref, kernel_out, pooled_out, gain_out, shift_out, ring, sem):
    def copy(t):
        slot = lax.rem(t, RING)
        return pltpu.make_async_copy(ring.at[slot], kernel_out.at[t], sem.at[slot])

    def one(t, s):
        @pl.when(t >= RING)
        def _():
            copy(t - RING).wait()

        ring[lax.rem(t, RING)] = kg_ref[t].astype(F32)
        copy(t).start()
        return s

    lax.fori_loop(0, UNITS, one, 0)
    for a in range(pooled_out.shape[0]):
        row = jnp.concatenate([pooled_ref[0, a], pooled_ref[1, a]], 1)
        pooled_out[a, 0] = row[: pooled_out.shape[2]]
    sums = jnp.concatenate([sums_ref[0], sums_ref[1]], 1)
    gain_out[...] = sums[:LAYERS]
    shift_out[...] = sums[LAYERS : 2 * LAYERS]
    for t in range(UNITS - RING, UNITS):
        copy(t).wait()


def solution(mesh):
    chips = mesh.shape["rows"] // 2

    def per_device(
        block_input,
        conv_weights,
        norm_gains,
        norm_shifts,
        map_width,
        map_group,
        pool_index,
        task_mask,
        task_weights,
        task_grads,
    ):
        maps_here, rows_here, columns, channels = block_input.shape
        pooled_columns = pool_index.shape[2]
        height = rows_here * mesh.shape["rows"]
        half = channels // 2
        band = 2 * rows_here
        pixels = maps_here * band * PAD
        actives = chips // 2
        owners = min(actives, 8)
        piece = half // 2 // owners
        rounds = 2 * LAYERS
        slots = 2 * UNITS * (actives - 1) * piece * half + 4 * rounds * chips * 8 * half
        grant = (36 * 1024 + 256) * 1024 + slots
        vmem, dma = pltpu.VMEM, pltpu.SemaphoreType.DMA
        tile = (maps_here, band + 2, PAD, half)
        edge = (2, maps_here, PAD, half)
        whole = pl.BlockSpec(memory_space=pltpu.VMEM)
        outside = pl.BlockSpec(memory_space=pltpu.HBM)
        index_rows = jnp.transpose(pool_index, (0, 2, 1, 3))
        anywhere = pl.BlockSpec(memory_space=pl.ANY)
        pooled, ig, kg, sums = pl.pallas_call(
            functools.partial(block_kernel, chips, height),
            out_shape=(
                jax.ShapeDtypeStruct((2, maps_here, PAD // 2, half), BF16),
                jax.ShapeDtypeStruct((2, maps_here, rows_here, PAD, half), F32),
                jax.ShapeDtypeStruct((UNITS, channels, channels), BF16),
                jax.ShapeDtypeStruct((2, 8, half), F32),
            ),
            in_specs=[whole, anywhere] + [outside] * 8,
            out_specs=[anywhere] * 4,
            scratch_shapes=[
                vmem(norm_gains.shape, F32),
                vmem(norm_shifts.shape, F32),
                pltpu.SMEM(map_width.shape, jnp.int32),
                pltpu.SMEM(map_group.shape, jnp.int32),
                vmem((maps_here, pooled_columns, channels), jnp.int32),
                pltpu.SMEM(task_mask.shape, jnp.int32),
                pltpu.SMEM(task_weights.shape, F32),
                vmem(task_grads.shape, BF16),
                vmem((LAYERS, 3, 3, half, half), BF16),
                vmem((LAYERS, 3, 3, half, half), BF16),
                vmem((2,) + tile, BF16),
                vmem((2,) + tile, BF16),
                vmem((LAYERS, 2, half, maps_here * (band + 2) * PAD), BF16),
                vmem((2, half, pixels), BF16),
                vmem((LAYERS,) + tile, F32),
                vmem(edge, BF16),
                vmem((LAYERS,) + edge, BF16),
                vmem((maps_here, band, PAD, half), F32),
                vmem(edge, BF16),
                vmem((LAYERS,) + edge, BF16),
                vmem((2,) + tile, BF16),
                vmem((2,) + tile, BF16),
                vmem((LAYERS, maps_here, band, PAD, half), BF16),
                vmem((3, 2, maps_here, band, PAD, half), BF16),
                vmem((3, pixels, half), F32),
                vmem((2, 2, maps_here, PAD // 2, half), F32),
                vmem((4, 2, maps_here, PAD // 2, half), F32),
                vmem((half // 128, PAD, 128), F32),
                vmem((2, maps_here, PAD // 2, half), BF16),
                vmem((rounds, chips, 8, half), F32),
                vmem((rounds, PLANE, 8, half), F32),
                vmem((maps_here, PLANE, 8, half), F32),
                vmem((PLANE, 8, half), F32),
                vmem((2, 8, half), F32),
                vmem((8, half), F32),
                vmem((LAYERS, 8, half), F32),
                vmem((LAYERS, 8, half), F32),
                vmem((2, 8, half), F32),
                vmem((1, 8, half), F32),
                vmem((1, 8, half), F32),
                vmem((8, half), F32),
                vmem((2 * TAPS, half, half), BF16),
                vmem((UNITS, half // 2, half), BF16),
                vmem((2 * TAPS, half // 2, half), BF16),
                vmem((UNITS, actives - 1, piece, half), BF16),
                vmem((UNITS, piece, half), BF16),
                dma((8,)),
                dma((LAYERS, 3)),
                dma((6,)),
                dma((6,)),
                dma((3,)),
                dma((3,)),
                dma((rounds, chips)),
                dma((rounds, chips)),
                dma((rounds, PLANE)),
                dma((rounds, PLANE)),
                dma((LAYERS, 2)),
                dma((LAYERS, 2)),
                dma((LAYERS, 2)),
                dma((LAYERS, 2)),
                dma((LAYERS, maps_here)),
                dma((LAYERS, maps_here)),
                dma((LAYERS, maps_here)),
                dma((LAYERS, maps_here)),
                dma((3,)),
                dma((3,)),
                dma((3,)),
                dma((LAYERS,)),
                dma((LAYERS,)),
                dma((LAYERS, 2, maps_here)),
                dma((LAYERS, maps_here)),
                dma((UNITS,)),
                dma((UNITS,)),
                dma((UNITS,)),
                dma((UNITS,)),
                dma((UNITS, owners)),
                dma((UNITS, actives - 1)),
                dma((UNITS, actives)),
                dma((UNITS, owners)),
                dma((UNITS,)),
                dma((UNITS,)),
                dma((UNITS,)),
                dma((UNITS,)),
                dma((UNITS,)),
                dma((UNITS,)),
                dma((UNITS,)),
                dma((UNITS,)),
                dma((UNITS,)),
                dma((UNITS,)),
                dma((UNITS,)),
            ],
            compiler_params=pltpu.CompilerParams(
                collective_id=0,
                has_side_effects=True,
                vmem_limit_bytes=grant,
            ),
        )(
            block_input,
            conv_weights,
            *(
                pltpu.with_memory_space_constraint(v, pltpu.HBM)
                for v in (
                    norm_gains,
                    norm_shifts,
                    map_width,
                    map_group,
                    index_rows,
                    task_mask,
                    task_weights,
                    task_grads,
                )
            ),
        )
        input_grad = jnp.concatenate([ig[0], ig[1]], -1)[:, :, :columns]
        kernel_grads, pooled, gain_grads, shift_grads = pl.pallas_call(
            finish_kernel,
            out_shape=(
                jax.ShapeDtypeStruct(kg.shape, F32),
                jax.ShapeDtypeStruct(pool_index.shape, BF16),
                jax.ShapeDtypeStruct(norm_gains.shape, F32),
                jax.ShapeDtypeStruct(norm_shifts.shape, F32),
            ),
            in_specs=[whole] * 3,
            out_specs=(anywhere, whole, whole, whole),
            scratch_shapes=[vmem((RING,) + kg.shape[1:], F32), dma((RING,))],
            compiler_params=pltpu.CompilerParams(vmem_limit_bytes=24 * 1024 * 1024),
        )(kg, pooled, sums)
        return (
            pooled,
            input_grad,
            kernel_grads.reshape(conv_weights.shape),
            gain_grads,
            shift_grads,
        )

    return jax.shard_map(
        per_device,
        mesh=mesh,
        in_specs=(
            P("maps", "rows", None, None),
            P(),
            P(),
            P(),
            P(),
            P(),
            P("maps", "rows", None, None),
            P("maps", None),
            P(),
            P(None, "maps", "rows", None, None),
        ),
        out_specs=(P("maps", "rows", None, None), P("maps", "rows", None, None), P(), P(), P()),
        check_vma=False,
    )
```

```python
import functools

import jax
import jax.numpy as jnp
from jax import lax
from jax.experimental import pallas as pl
from jax.experimental.pallas import tpu as pltpu
from jax.sharding import PartitionSpec as P

MESH = pl.DeviceIdType.MESH
epsilon = 1e-05
PAD = 64
LAYERS = 3
TAPS = 9
UNITS = LAYERS * TAPS
PLANE = 4
LAG = 4
EARLY = 1
FOLD = 2
F32 = jnp.float32
BF16 = jnp.bfloat16


def each(first, last, body):
    if last - first <= 8:
        for k in range(first, last):
            body(k)
    else:
        lax.fori_loop(first, last, lambda k, s: (body(k), s)[1], 0)


def block_kernel(
    chips,
    height,
    x_ref,
    w_ref,
    gain_hbm,
    shift_hbm,
    width_hbm,
    group_hbm,
    index_hbm,
    tmask_hbm,
    tweight_hbm,
    tgrad_hbm,
    pooled_ref,
    ig_ref,
    kg_ref,
    sums_ref,
    gain_ref,
    shift_ref,
    width_ref,
    group_ref,
    index_ref,
    tmask_ref,
    tweight_ref,
    tgrad_ref,
    wa,
    wb,
    act_own,
    act_oth,
    act_t,
    act_b,
    zbuf,
    zs,
    zh,
    dh,
    dhs,
    dhh,
    dz_own,
    dz_oth,
    dzr,
    dzv,
    prod,
    gsrc,
    gbuf,
    hrow,
    pbuf,
    st1,
    st2,
    coef,
    nall,
    inv_t,
    cnt_t,
    avg_t,
    scl_t,
    mean_t,
    tb_t,
    ta_t,
    sums_own,
    terms,
    r2,
    rf,
    r3,
    fin,
    in_sem,
    w_sem,
    x_s,
    x_r,
    g_s,
    g_r,
    st1_s,
    st1_r,
    st2_s,
    st2_r,
    zh_s,
    zh_r,
    dh_s,
    dh_r,
    act_s,
    act_r,
    dz_s,
    dz_r,
    out_s,
    out_r,
    out_l,
    at_s,
    at_r,
    dzr_s,
    dzr_r,
    r2_s,
    r2_r,
    rf_s,
    rf_r,
    r3_s,
    r3_r,
    az_s,
    az_r,
    af_s,
    af_r,
    ab_s,
    ab_r,
    aa_s,
    aa_r,
    ae_s,
    ae_r,
    ap_s,
    ap_r,
    loc_s,
):
    maps_here = x_ref.shape[0]
    columns = x_ref.shape[2]
    half = x_ref.shape[3] // 2
    tasks = tgrad_ref.shape[0]
    pooled_columns = tgrad_ref.shape[3]
    lanes = half // 128
    tiles = [slice(n * 128, (n + 1) * 128) for n in range(lanes)]
    band = 4
    pixels = maps_here * band * PAD
    actives = chips // 2
    owners = min(actives, 8)
    piece = (half // 2) // owners
    m = lax.axis_index("maps")
    r = lax.axis_index("rows")
    c = lax.rem(r, 2)
    z = lax.div(r, 2)
    other = 1 - c
    first_map = m * maps_here
    x_bit = lax.rem(m, 2)
    y_bit = lax.div(m, 2)
    x_peer = m + 1 - 2 * x_bit
    y_peer = m + 2 - 4 * y_bit
    g_bit = (1 - c) * x_bit + c * y_bit
    h_bit = (1 - c) * y_bit + c * x_bit
    g_peer = (1 - c) * x_peer + c * y_peer
    h_peer = (1 - c) * y_peer + c * x_peer
    pair = lax.div(z, 2)
    turn = lax.rem(pair, 2)
    active_z = 2 * pair + 1 - turn
    is_active = z == active_z
    is_passive = z != active_z
    is_owner = jnp.logical_and(is_active, pair < owners)
    role = jnp.where(is_active, 0, 1)
    up_there = z > 0
    down_there = z < chips - 1
    row8 = lax.broadcasted_iota(jnp.int32, (8, half), 0)
    column = lax.broadcasted_iota(jnp.int32, (PAD, half), 0)

    def remote(src, dst, send, recv, mm, zz, cc):
        return pltpu.make_async_remote_copy(
            src_ref=src,
            dst_ref=dst,
            send_sem=send,
            recv_sem=recv,
            device_id=(mm, zz * 2 + cc),
            device_id_type=MESH,
        )

    def own_half(v):
        return jnp.where(c == 0, v[..., :half], v[..., half:])

    def width_of(a):
        return width_ref[first_map + a]

    own_at = pl.ds(pl.multiple_of(c * half, half), half)
    oth_at = pl.ds(pl.multiple_of(other * half, half), half)

    def weight_copy(l, n):
        dst = (wa, wb, wb)[n]
        k_at, o_at = ((own_at, own_at), (oth_at, own_at), (own_at, oth_at))[n]
        return pltpu.make_async_copy(w_ref.at[l, :, :, k_at, o_at], dst.at[l], w_sem.at[l, n])

    fetches = [
        pltpu.make_async_copy(src, dst, in_sem.at[n])
        for n, (src, dst) in enumerate(
            (
                (width_hbm, width_ref),
                (group_hbm, group_ref),
                (tmask_hbm, tmask_ref),
                (tweight_hbm, tweight_ref),
                (gain_hbm, gain_ref),
                (shift_hbm, shift_ref),
                (index_hbm.at[:, :, 0, :], index_ref),
                (tgrad_hbm, tgrad_ref),
            )
        )
    ]
    for fetch in fetches:
        fetch.start()
    for l in range(LAYERS):
        weight_copy(l, 0).start()
        weight_copy(l, 1).start()

    barrier = pltpu.get_barrier_semaphore()

    def greet(k):
        rr = lax.rem(r + k, 2 * chips)
        pl.semaphore_signal(barrier, inc=1, device_id=(m, rr), device_id_type=MESH)

    each(1, 2 * chips, greet)
    for k in range(1, PLANE):
        for core in (c, other):
            there = (lax.rem(m + k, PLANE), z * 2 + core)
            pl.semaphore_signal(barrier, inc=1, device_id=there, device_id_type=MESH)

    for fetch in fetches:
        fetch.wait()

    mine = pl.ds(1 + 2 * c, 2)
    for a in range(maps_here):
        inside = lax.broadcasted_iota(jnp.int32, (columns, 2 * half), 0) < width_of(a)
        for rr in range(2):
            v = jnp.where(inside, x_ref[a, rr].astype(F32), 0.0).astype(BF16)
            spot = 1 + 2 * c + rr
            act_own[0, a, spot, pl.ds(48, 16), :] = jnp.zeros((16, half), BF16)
            act_oth[0, a, spot, pl.ds(48, 16), :] = jnp.zeros((16, half), BF16)
            act_own[0, a, spot, pl.ds(0, columns), :] = own_half(v)
            act_oth[0, a, spot, pl.ds(0, columns), :] = jnp.where(
                c == 0, v[:, half:], v[:, :half]
            )

    @pl.when(z == 0)
    def _():
        act_own[0, :, 0] = jnp.zeros((maps_here, PAD, half), BF16)
        act_oth[0, :, 0] = jnp.zeros((maps_here, PAD, half), BF16)

    @pl.when(z == chips - 1)
    def _():
        act_own[0, :, 5] = jnp.zeros((maps_here, PAD, half), BF16)
        act_oth[0, :, 5] = jnp.zeros((maps_here, PAD, half), BF16)

    pl.semaphore_wait(barrier, 2 * chips - 1 + 2 * (PLANE - 1))

    x_partner = (
        remote(act_own.at[0, :, mine], act_oth.at[0, :, mine], x_s.at[0], x_r.at[0], m, z, other),
        remote(act_oth.at[0, :, mine], act_own.at[0, :, mine], x_s.at[1], x_r.at[1], m, z, other),
    )
    g_partner = remote(gsrc.at[other], gbuf.at[1 + c], g_s.at[0], g_r.at[0], m, z, other)

    def x_halo(n, src_row, dst_row, zz):
        cc = (c, other)[n % 2]
        low = dst_row == band + 1
        if n >= 2:
            src, dst = gsrc.at[cc], gbuf.at[3 if low else 0]
            return remote(src, dst, g_s.at[n - 1], g_r.at[1 if low else 2], m, zz, cc)
        src, dst = (act_own, act_oth)[n].at[0, :, src_row], act_own.at[0, :, dst_row]
        return remote(src, dst, x_s.at[2 + n], x_r.at[2 if low else 3], m, zz, cc)

    def x_pass(row):
        n = 4 if row == 0 else 5
        src, dst = act_own.at[0, :, row], act_oth.at[0, :, row]
        return remote(src, dst, x_s.at[n], x_r.at[n], m, z, other)

    for copy in x_partner:
        copy.start()

    @pl.when(jnp.logical_and(c == 0, up_there))
    def _():
        for n in range(2):
            x_halo(n, 1, 5, z - 1).start()

    @pl.when(jnp.logical_and(c == 1, down_there))
    def _():
        for n in range(2):
            x_halo(n, 4, 0, z + 1).start()

    gsrc[...] = jnp.zeros(gsrc.shape, F32)
    for a in range(maps_here):
        total = None
        for t in range(tasks):
            scale = tweight_ref[t] * tmask_ref[a, t].astype(F32)
            term = tgrad_ref[t, a, 0].astype(F32) * scale
            total = term if total is None else total + term
        position = index_ref[a].astype(F32)
        for h in range(2):
            gsrc[h, 0, a, pl.ds(0, pooled_columns), :] = total[:, h * half : (h + 1) * half]
            gsrc[h, 1, a, pl.ds(0, pooled_columns), :] = position[:, h * half : (h + 1) * half]
    gbuf[1 + c] = gsrc[c]

    for mm in range(PLANE):
        sizes = jnp.zeros((8, half), F32)
        for b in range(maps_here):
            sizes = jnp.where(
                row8 == b, (width_ref[mm * maps_here + b] * height).astype(F32), sizes
            )
        nall[mm] = sizes
    inside_sizes = jnp.zeros((8, half), F32)
    for b in range(maps_here):
        inside_sizes = jnp.where(row8 == b, (width_of(b) * band).astype(F32), inside_sizes)
    inv_t[0] = inside_sizes
    inv_t[1] = jnp.where(row8 < maps_here, 1.0 / jnp.maximum(inside_sizes, 1.0), 0.0)
    counts = jnp.ones((8, half), F32)
    for a in range(maps_here):
        total = jnp.zeros((1, half), F32)
        for mm in range(PLANE):
            same = jnp.zeros((8, half), F32)
            for b in range(maps_here):
                alike = group_ref[first_map + a] == group_ref[mm * maps_here + b]
                same = jnp.where(row8 == b, jnp.where(alike, 1.0, 0.0), same)
            coef[a, mm] = same
            total = total + jnp.sum(same * nall[mm], 0, keepdims=True)
        counts = jnp.where(row8 == a, total, counts)
    cnt_t[...] = counts

    def z_copy(e, k):
        zz = lax.rem(z + k, chips)
        return remote(st1.at[e, z], st1.at[e, z], st1_s.at[e, k], st1_r.at[e, z], m, zz, c)

    def z_arrival(e, k):
        zz = lax.rem(z + k, chips)
        return remote(st1.at[e, zz], st1.at[e, zz], st1_s.at[e, k], st1_r.at[e, zz], m, zz, c)

    def m_copy(e, k):
        mm = lax.rem(m + k, PLANE)
        return remote(st2.at[e, m], st2.at[e, m], st2_s.at[e, k], st2_r.at[e, m], mm, z, c)

    def m_arrival(e, k):
        mm = lax.rem(m + k, PLANE)
        return remote(st2.at[e, mm], st2.at[e, mm], st2_s.at[e, k], st2_r.at[e, mm], mm, z, c)

    def send_z(e, tile):
        st1[e, z] = tile
        each(1, chips, lambda k: z_copy(e, k).start())

    def wait_z(e):
        each(1, chips, lambda k: z_arrival(e, k).wait_recv())

    def send_m(e, tile):
        st2[e, m] = tile
        each(1, PLANE, lambda k: m_copy(e, k).start())

    def wait_m(e):
        each(1, PLANE, lambda k: m_arrival(e, k).wait_recv())

    def products(source, l, taps, kernel, transposed, fresh):
        starts = [2 - i if transposed else i for i in taps]
        lhs = jnp.concatenate(
            [source[lax.rem(l, 2), :, s : s + band].reshape(pixels, half) for s in starts], 1
        )
        for j in range(3):
            rhs = jnp.concatenate([kernel[l, i, j] for i in taps], 1 if transposed else 0)
            got = lax.dot_general(
                lhs,
                rhs,
                (((1,), (1 if transposed else 0,)), ((), ())),
                preferred_element_type=F32,
            )
            if fresh:
                prod[j] = got
            else:
                prod[j] = prod[j] + got

    def shifted(a, rr, before, behind, n):
        rows = pl.ds(pl.multiple_of((a * band + rr) * PAD, PAD), PAD)
        return (
            prod[1, rows, n]
            + pltpu.roll(prod[before, rows, n], 1, 0)
            + pltpu.roll(prod[behind, rows, n], PAD - 1, 0)
        )

    def row_of(table, l, a):
        return table[l, pl.ds(a, 1), :]

    def gain_of(l):
        return own_half(gain_ref[pl.ds(l, 1), :])

    def shift_of(l):
        return own_half(shift_ref[pl.ds(l, 1), :])

    def limit(a, rr):
        w = width_of(a)
        if rr == 0:
            return jnp.where(up_there, w, 0)
        if rr == band + 1:
            return jnp.where(down_there, w, 0)
        return w

    def z_halo(l, way):
        there = z - 1 + 2 * way
        return remote(zs.at[way], zh.at[l, 1 - way], zh_s.at[l, way], zh_r.at[l, way], m, there, c)

    def dh_halo(l, way):
        there = z - 1 + 2 * way
        return remote(dhs.at[way], dhh.at[l, 1 - way], dh_s.at[l, way], dh_r.at[l, way], m, there, c)

    def start_halo(halo, l):
        @pl.when(up_there)
        def _():
            halo(l, 0).start()

        @pl.when(down_there)
        def _():
            halo(l, 1).start()

    def wait_halo(halo, l):
        @pl.when(up_there)
        def _():
            halo(l, 1).wait_recv()
            halo(l, 0).wait_send()

        @pl.when(down_there)
        def _():
            halo(l, 0).wait_recv()
            halo(l, 1).wait_send()

    def act_copy(l, a):
        slot = lax.rem(l, 2)
        src, dst = act_own.at[slot, a], act_oth.at[slot, a]
        return remote(src, dst, act_s.at[l, a], act_r.at[l, a], m, z, other)

    def at_copy(l):
        return remote(act_t.at[l, 0], act_t.at[l, 1], at_s.at[l], at_r.at[l], g_peer, z, c)

    def dzr_copy(l, a, way):
        src, dst = dz_own.at[lax.rem(l, 2), a, pl.ds(1, band)], dzr.at[l, a]
        peer = (x_peer, y_peer)[way]
        return remote(src, dst, dzr_s.at[l, way, a], dzr_r.at[l, a], peer, z, way)

    def if_wanted(way, body):
        @pl.when((x_bit, y_bit)[way] + c == 1)
        def _():
            body()

    def dz_copy(l, a):
        slot = lax.rem(l, 2)
        src, dst = dz_own.at[slot, a], dz_oth.at[slot, a]
        return remote(src, dst, dz_s.at[l, a], dz_r.at[l, a], m, z, other)

    def send_gradients():
        g_partner.start()

        @pl.when(jnp.logical_and(c == 0, up_there))
        def _():
            for n in range(2, 4):
                x_halo(n, 1, 5, z - 1).start()

        @pl.when(jnp.logical_and(c == 1, down_there))
        def _():
            for n in range(2, 4):
                x_halo(n, 4, 0, z + 1).start()

    def if_there(way, body):
        @pl.when((up_there, down_there)[way])
        def _():
            body()

    def wait_x_halo(n):
        if_there(0, lambda: x_halo(n, 4, 0, z - 1).wait_recv())
        if_there(1, lambda: x_halo(n, 1, 5, z + 1).wait_recv())

    def each_x_pass(act):
        if_there(0, lambda: act(x_pass(0)))
        if_there(1, lambda: act(x_pass(band + 1)))

    def sent_x_halo(first, last):
        @pl.when(jnp.logical_and(c == 0, up_there))
        def _():
            for n in range(first, last):
                x_halo(n, 1, 5, z - 1).wait_send()

        @pl.when(jnp.logical_and(c == 1, down_there))
        def _():
            for n in range(first, last):
                x_halo(n, 4, 0, z + 1).wait_send()

    def unpool(a, s):
        for rr in range(band + 2):
            slot, lower = (rr + 1) // 2, (rr + 1) % 2
            g = gbuf[slot, 0, a]
            position = gbuf[slot, 1, a]
            for b in range(2):
                v = jnp.where(position == float(2 * lower + b), g, 0.0)
                for n in range(lanes):
                    hrow[n, pl.ds(b, PAD // 2, stride=2), :] = v[:, n * 128 : (n + 1) * 128]
            v = jnp.concatenate([hrow[n] for n in range(lanes)], 1)
            if rr in (0, band + 1):
                dhh[LAYERS - 1, rr // (band + 1), a] = v.astype(BF16)
            else:
                dh[a, rr - 1] = v
        return s

    def forward(l, first):
        weight_copy(l, 0).wait()
        weight_copy(l, 1).wait()
        if first:
            for copy in x_partner:
                copy.wait_recv()
            products(act_own, l, (1,), wa, False, True)
            products(act_oth, l, (1,), wb, False, False)
            wait_x_halo(0)
            each_x_pass(lambda copy: copy.start())
            products(act_own, l, (0, 2), wa, False, False)
            each_x_pass(lambda copy: copy.wait_recv())
            products(act_oth, l, (0, 2), wb, False, False)
        else:
            products(act_own, l, (0, 1, 2), wa, False, True)
            for a in range(maps_here):
                act_copy(l, a).wait_recv()
            products(act_oth, l, (0, 1, 2), wb, False, False)
        weight_copy(l, 2).start()

        def collect(a, tile):
            inside = column[:, :128] < width_of(a)
            pixels_inside = (width_of(a) * band).astype(F32)
            totals, squares = [], []
            for n in tiles:
                total = jnp.zeros((PAD, 128), F32)
                for rr in range(band):
                    v = shifted(a, rr, 0, 2, n)
                    zbuf[l, a, 1 + rr, :, n] = v
                    total = total + jnp.where(inside, v, 0.0)
                total = jnp.sum(total, 0, keepdims=True)
                mean = total / pixels_inside
                square = jnp.zeros((PAD, 128), F32)
                for rr in range(band):
                    v = jnp.where(inside, zbuf[l, a, 1 + rr, :, n] - mean, 0.0)
                    square = square + v * v
                    if rr in (0, band - 1):
                        zs[rr // (band - 1), a, :, n] = v.astype(BF16)
                totals.append(total)
                squares.append(jnp.sum(square, 0, keepdims=True))
            tile = jnp.where(row8 == a, jnp.concatenate(totals, 1), tile)
            return jnp.where(row8 == a + maps_here, jnp.concatenate(squares, 1), tile)

        tile = lax.fori_loop(0, maps_here, collect, jnp.zeros((8, half), F32))
        send_z(l, tile)
        start_halo(z_halo, l)
        act_t[l, 0] = act_own[lax.rem(l, 2)].reshape(maps_here * (band + 2) * PAD, half).T
        wait_z(l)
        sizes, inverse = inv_t[0], inv_t[1]
        mean_t[0] = st1[l, jnp.maximum(z - 1, 0)] * inverse
        mean_t[1] = st1[l, jnp.minimum(z + 1, chips - 1)] * inverse
        total = st1[l, 0]
        for zz in range(1, chips):
            total = total + st1[l, zz]
        mean = total * inverse * (1.0 / chips)
        square = jnp.zeros((8, half), F32)
        for zz in range(chips):
            v = st1[l, zz]
            gap = v * inverse - mean
            square = square + pltpu.roll(v, 8 - maps_here, 0) + sizes * gap * gap
        tile = jnp.where(row8 < maps_here, mean, pltpu.roll(square, maps_here, 0))
        send_m(l, jnp.where(row8 < 2 * maps_here, tile, 0.0))
        if not first:

            @pl.when(l == LAYERS - 1)
            def _():
                g_partner.wait_recv()
                wait_x_halo(2)
                lax.fori_loop(0, maps_here, unpool, 0)

        wait_m(l)
        at_copy(l).start()
        if first:
            send_gradients()
        averages = jnp.zeros((8, half), F32)
        scalings = jnp.zeros((8, half), F32)
        for a in range(maps_here):
            count = cnt_t[a : a + 1, :]
            average = jnp.zeros((8, half), F32)
            for mm in range(PLANE):
                average = average + coef[a, mm] * nall[mm] * st2[l, mm]
            average = jnp.sum(average, 0, keepdims=True) / count
            variance = jnp.zeros((8, half), F32)
            for mm in range(PLANE):
                v = st2[l, mm]
                gap = v - average
                variance = variance + coef[a, mm] * (
                    pltpu.roll(v, 8 - maps_here, 0) + nall[mm] * gap * gap
                )
            variance = jnp.sum(variance, 0, keepdims=True) / count
            averages = jnp.where(row8 == a, average, averages)
            scalings = jnp.where(row8 == a, lax.rsqrt(variance + epsilon), scalings)
        avg_t[l] = averages
        scl_t[l] = scalings
        wait_halo(z_halo, l)

        def activate(a, s):
            gain, shift = gain_of(l), shift_of(l)
            for n in tiles:
                average = row_of(avg_t, l, a)[:, n]
                factor = row_of(scl_t, l, a)[:, n] * gain[:, n]
                for rr in range(band + 2):
                    if rr in (0, band + 1):
                        way = rr // (band + 1)
                        v = zh[l, way, a, :, n].astype(F32) + row_of(mean_t, way, a)[:, n]
                        zbuf[l, a, rr, :, n] = v
                    else:
                        v = zbuf[l, a, rr, :, n]
                    y = (v - average) * factor + shift[:, n]
                    h = jnp.where(column[:, n] < limit(a, rr), y * jax.nn.sigmoid(y), 0.0)
                    act_own[lax.rem(l + 1, 2), a, rr, :, n] = h.astype(BF16)

            @pl.when(l < LAYERS - 1)
            def _():
                act_copy(l + 1, a).start()

            return s

        if first:
            for copy in x_partner:
                copy.wait_send()
            sent_x_halo(0, 2)
            each_x_pass(lambda copy: copy.wait_send())
        else:

            @pl.when(l == 2)
            def _():
                for a in range(maps_here):
                    act_copy(1, a).wait_send()

        lax.fori_loop(0, maps_here, activate, 0)

    forward(0, True)
    lax.fori_loop(1, LAYERS, lambda l, s: (forward(l, False), s)[1], 0)


    def pool():
        def one(a, s):
            for pr in range(2):
                total = jnp.zeros((PAD // 2, half), F32)
                position = gbuf[1 + pr, 1, a]
                for lower in range(2):
                    v = act_own[LAYERS % 2, a, 1 + 2 * pr + lower].astype(F32)
                    for n in range(lanes):
                        hrow[n] = v[:, n * 128 : (n + 1) * 128]
                    for b in range(2):
                        v = jnp.concatenate(
                            [hrow[n, pl.ds(b, PAD // 2, stride=2), :] for n in range(lanes)], 1
                        )
                        total = total + jnp.where(position == float(2 * lower + b), v, 0.0)
                pbuf[pr, a] = total.astype(BF16)
            return s

        lax.fori_loop(0, maps_here, one, 0)

    def second_rows(bit):
        return pl.ds(pl.multiple_of(bit * (half // 2), half // 2), half // 2)

    def piece_rows(p):
        return pl.ds(pl.multiple_of(p * piece, piece), piece)

    def term_slot(q):
        return lax.rem(q, 2 * TAPS)

    def c2(q):
        src = terms.at[term_slot(q), second_rows(1 - h_bit)]
        return remote(src, r2.at[q], r2_s.at[q], r2_r.at[q], h_peer, z, c)

    def z_of(n):
        return 2 * n + 1 - lax.rem(n, 2)

    def cf(q):
        passive_z = 2 * pair + turn
        there = active_z + passive_z - z
        return remote(r2.at[q], rf.at[term_slot(q)], rf_s.at[q], rf_r.at[q], m, there, c)

    def c3(q, p):
        slot = lax.rem(pair - p + actives - 1, actives)
        return remote(
            r2.at[q, piece_rows(p)], r3.at[q, slot], r3_s.at[q, p], r3_r.at[q, slot], m, z_of(p), c
        )

    def others(first, body, limit):
        def one(k):
            n = lax.rem(pair + k, actives)

            @pl.when(n < limit)
            def _():
                body(n)

        each(first, actives, one)

    def unit_of(q):
        k = lax.div(q, TAPS)
        return (LAYERS - 1 - k) * TAPS + (q - k * TAPS)

    def region(q, start, size, lane, lanes):
        start = pl.multiple_of(c * half + start, piece)
        lane = pl.multiple_of(lane, half)
        return kg_ref.at[unit_of(q), pl.ds(start, size), pl.ds(lane, lanes)]

    def cz(q, p, n):
        part = region(q, h_bit * (half // 2) + p * piece, piece, g_bit * half, half)
        return remote(fin.at[q], part, az_s.at[q, n], az_r.at[q, p], m, z_of(n), c)

    def cl(q):
        part = region(q, h_bit * (half // 2) + pair * piece, piece, g_bit * half, half)
        return pltpu.make_async_copy(fin.at[q], part, loc_s.at[q])

    def cu(q):
        passive_z = 2 * pair + turn
        there = active_z + passive_z - z
        part = region(q, h_bit * (half // 2), half // 2, g_bit * half, half)
        return remote(part, part, af_s.at[q], af_r.at[q], m, there, c)

    def cb(q):
        part = region(q, h_bit * (half // 2), half // 2, g_bit * half, half)
        return remote(part, part, ab_s.at[q], ab_r.at[q], h_peer, z, c)

    def ca(q):
        part = region(q, 0, half, g_bit * half, half)
        return remote(part, part, aa_s.at[q], aa_r.at[q], g_peer, z, c)

    def plan(q):
        k = lax.rem(q, 5)
        both = jnp.logical_or(lax.rem(k, 2) == 0, q >= UNITS - 5)
        mine = jnp.logical_or(both, lax.div(k, 2) == role)
        return mine, jnp.logical_and(mine, jnp.logical_not(both)), jnp.logical_not(mine)

    def ce(q):
        passive_z = 2 * pair + turn
        there = active_z + passive_z - z
        part = region(q, 0, half, (1 - g_bit) * half, half)
        return remote(part, part, ae_s.at[q], ae_r.at[q], m, there, c)

    def cp_part(q, start, size, lane, lanes):
        part = region(q, start, size, lane, lanes)
        return remote(part, part, ap_s.at[q], ap_r.at[q], m, z, other)

    def cp(q):
        return cp_part(q, 0, half, 0, 2 * half)

    def cp_rows(q, bit):
        return cp_part(q, bit * (half // 2), half // 2, g_bit * half, half)

    def cp_lanes(q):
        return cp_part(q, 0, half, (1 - g_bit) * half, half)

    def ready_terms(l):
        at_copy(l).wait_recv()
        for chip in range(2):
            for a in range(maps_here):
                first = a * (band + 2) * PAD
                rows = act_t[l, chip, :, first : first + (band + 2) * PAD]
                act_b[chip, :, a * band * PAD : (a + 1) * band * PAD] = rows[:, PAD : PAD + band * PAD]
        slot = lax.rem(l, 2)

        def variants(a, s):
            dzr_copy(l, a, 0).wait_recv()
            for chip in range(2):
                for rr in range(band):
                    for n in tiles:
                        if chip == 0:
                            mine, theirs = dz_own[slot, a, 1 + rr, :, n], dz_oth[slot, a, 1 + rr, :, n]
                            v = jnp.where(g_bit == c, mine, theirs)
                        else:
                            v = dzr[l, a, rr, :, n]
                        dzv[1, chip, a, rr, :, n] = v
                        v = v.astype(F32)
                        dzv[0, chip, a, rr, :, n] = pltpu.roll(v, PAD - 1, 0).astype(BF16)
                        dzv[2, chip, a, rr, :, n] = pltpu.roll(v, 1, 0).astype(BF16)
            return s

        lax.fori_loop(0, maps_here, variants, 0)

    def tap_terms(l, i, j):
        if i == 1:
            lhs = [act_b[0], act_b[1]]
        else:
            lhs = []
            for chip in range(2):
                for a in range(maps_here):
                    first = (a * (band + 2) + i) * PAD
                    lhs.append(act_t[l, chip, :, first : first + band * PAD])
        rhs = dzv[j].reshape(2 * pixels, half)
        q = (LAYERS - 1 - l) * TAPS + 3 * i + j
        got = jnp.dot(jnp.concatenate(lhs, 1), rhs, preferred_element_type=F32)
        terms[term_slot(q)] = got.astype(BF16)

    def weight_terms(l, i):
        lax.fori_loop(0, 3, lambda j, s: (tap_terms(l, i, j), s)[1], 0)

    def stage_second(q):
        c2(q).wait()
        kept = terms[term_slot(q), second_rows(h_bit)].astype(F32)
        r2[q] = (r2[q].astype(F32) + kept).astype(BF16)

        @pl.when(is_passive)
        def _():
            cf(q).start()

    def stage_fold(q):
        @pl.when(is_active)
        def _():
            cf(q).wait_recv()
            r2[q] = (r2[q].astype(F32) + rf[term_slot(q)].astype(F32)).astype(BF16)
            others(1, lambda n: c3(q, n).start(), owners)

    def stage_sum(q):
        @pl.when(is_owner)
        def _():
            for k in range(actives - 1):
                remote(
                    r3.at[q, k], r3.at[q, k], r3_s.at[q, 0], r3_r.at[q, k], m, z, c
                ).wait_recv()
            total = r2[q, piece_rows(pair)].astype(F32)
            for k in range(actives - 1):
                total = total + r3[q, k].astype(F32)
            fin[q] = total.astype(BF16)
            others(1, lambda n: cz(q, pair, n).start(), actives)
            cl(q).start()

    def stage_back(q):
        @pl.when(is_active)
        def _():
            others(1, lambda n: cz(q, n, n).wait_recv(), owners)

        @pl.when(is_owner)
        def _():
            cl(q).wait()

        @pl.when(is_active)
        def _():
            cu(q).start()

        @pl.when(is_passive)
        def _():
            cu(q).wait_recv()

        cb(q).start()
        cp_rows(q, h_bit).start()

    def stage_first(q):
        cb(q).wait_recv()
        mine, _, _ = plan(q)

        @pl.when(mine)
        def _():
            ca(q).start()

        cp_rows(q, 1 - h_bit).start()

        @pl.when(is_active)
        def _():
            others(1, lambda n: c3(q, n).wait_send(), owners)

        @pl.when(is_passive)
        def _():
            cf(q).wait_send()

    def stage_chip(q):
        mine, for_both, _ = plan(q)

        @pl.when(mine)
        def _():
            ca(q).wait_recv()

        @pl.when(for_both)
        def _():
            ce(q).start()

        @pl.when(mine)
        def _():
            cp_lanes(q).start()

        @pl.when(is_owner)
        def _():
            others(1, lambda n: cz(q, pair, n).wait_send(), actives)

        @pl.when(is_active)
        def _():
            cu(q).wait_send()

    def stage_late(q):
        _, _, not_mine = plan(q)

        @pl.when(not_mine)
        def _():
            ce(q).wait_recv()
            cp_lanes(q).start()

    def stage_done(q):
        mine, for_both, _ = plan(q)
        cb(q).wait_send()

        @pl.when(mine)
        def _():
            ca(q).wait_send()

        @pl.when(for_both)
        def _():
            ce(q).wait_send()

        cp(q).wait()

    def run(stage, first, last):
        lax.fori_loop(first, last, lambda q, s: (stage(q), s)[1], 0)

    def sent_dz(l):
        for a in range(maps_here):
            dz_copy(l, a).wait_send()
            for way in range(2):
                if_wanted(way, dzr_copy(l, a, way).wait_send)

    def backward(k, carry):
        l = LAYERS - 1 - k
        gain, shift = gain_of(l), shift_of(l)

        def gradient(a, rr, n):
            zhat = (zbuf[l, a, rr, :, n] - row_of(avg_t, l, a)[:, n]) * row_of(scl_t, l, a)[:, n]
            y = zhat * gain[:, n] + shift[:, n]
            s = jax.nn.sigmoid(y)
            if rr in (0, band + 1):
                upstream = dhh[l, rr // (band + 1), a, :, n].astype(F32)
            else:
                upstream = dh[a, rr - 1, :, n]
            dy = upstream * (s * (1.0 + y * (1.0 - s)))
            dy = jnp.where(column[:, n] < limit(a, rr), dy, 0.0)
            return dy, zhat

        def collect(a, tile):
            plains, crosses = [], []
            for n in tiles:
                plain = jnp.zeros((PAD, 128), F32)
                crossed = jnp.zeros((PAD, 128), F32)
                for rr in range(1, band + 1):
                    dy, zhat = gradient(a, rr, n)
                    dh[a, rr - 1, :, n] = dy
                    plain = plain + dy
                    crossed = crossed + dy * zhat
                plains.append(jnp.sum(plain, 0, keepdims=True))
                crosses.append(jnp.sum(crossed, 0, keepdims=True))
            tile = jnp.where(row8 == a, jnp.concatenate(plains, 1), tile)
            return jnp.where(row8 == a + maps_here, jnp.concatenate(crosses, 1), tile)

        e = LAYERS + l
        tile = lax.fori_loop(0, maps_here, collect, jnp.zeros((8, half), F32))
        send_z(e, tile)

        @pl.when(k == LAYERS - 1)
        def _():
            run(stage_second, 0, TAPS)

        @pl.when(k > 0)
        def _():
            ready_terms(l + 1)
            weight_terms(l + 1, 0)

        wait_z(e)
        total = st1[e, 0]
        for zz in range(1, chips):
            total = total + st1[e, zz]
        send_m(e, total)

        @pl.when(k > 0)
        def _():
            first = (LAYERS - 2 - l) * TAPS
            run(lambda q: c2(q).start(), first, first + 3)
            weight_terms(l + 1, 1)
            run(lambda q: c2(q).start(), first + 3, first + 6)
            weight_terms(l + 1, 2)
            run(lambda q: c2(q).start(), first + 6, first + 9)
            wait_halo(dh_halo, l)

        @pl.when(k == 0)
        def _():
            pool()

        wait_m(e)
        total = st2[e, 0]
        for mm in range(1, PLANE):
            total = total + st2[e, mm]
        sums_own[pl.ds(l, 1), :] = jnp.sum(
            jnp.where(row8 >= maps_here, total, 0.0), 0, keepdims=True
        )
        sums_own[pl.ds(LAYERS + l, 1), :] = jnp.sum(
            jnp.where(row8 < maps_here, total, 0.0), 0, keepdims=True
        )
        plains = jnp.zeros((8, half), F32)
        crosses = jnp.zeros((8, half), F32)
        for a in range(maps_here):
            plain = jnp.zeros((8, half), F32)
            crossed = jnp.zeros((8, half), F32)
            for mm in range(PLANE):
                v = st2[e, mm]
                plain = plain + coef[a, mm] * v
                crossed = crossed + coef[a, mm] * pltpu.roll(v, 8 - maps_here, 0)
            count = cnt_t[a : a + 1, :]
            plain = gain * (jnp.sum(plain, 0, keepdims=True) / count)
            crossed = gain * (jnp.sum(crossed, 0, keepdims=True) / count)
            plains = jnp.where(row8 == a, plain, plains)
            crosses = jnp.where(row8 == a, crossed, crosses)
        tb_t[0] = plains
        ta_t[0] = crosses

        def settle(a, s):
            for n in tiles:
                average, scaling = row_of(avg_t, l, a)[:, n], row_of(scl_t, l, a)[:, n]
                plain, crossed = row_of(tb_t, 0, a)[:, n], row_of(ta_t, 0, a)[:, n]
                for rr in range(band + 2):
                    if rr in (0, band + 1):
                        dy, zhat = gradient(a, rr, n)
                    else:
                        dy = dh[a, rr - 1, :, n]
                        zhat = (zbuf[l, a, rr, :, n] - average) * scaling
                    v = scaling * (dy * gain[:, n] - plain - zhat * crossed)
                    v = jnp.where(column[:, n] < limit(a, rr), v, 0.0)
                    dz_own[lax.rem(l, 2), a, rr, :, n] = v.astype(BF16)
            dz_copy(l, a).start()
            for way in range(2):
                if_wanted(way, dzr_copy(l, a, way).start)
            return s

        @pl.when(k == 2)
        def _():
            sent_dz(LAYERS - 1)

        lax.fori_loop(0, maps_here, settle, 0)
        products(dz_own, l, (0, 1, 2), wa, True, True)
        weight_copy(l, 2).wait()
        for a in range(maps_here):
            dz_copy(l, a).wait_recv()
        products(dz_oth, l, (0, 1, 2), wb, True, False)

        def gather(a, s):
            for n in tiles:
                for rr in range(band):
                    v = shifted(a, rr, 2, 0, n)
                    dh[a, rr, :, n] = v
                    if rr in (0, band - 1):
                        dhs[rr // (band - 1), a, :, n] = v.astype(BF16)
            return s

        lax.fori_loop(0, maps_here, gather, 0)

        @pl.when(l > 0)
        def _():
            start_halo(dh_halo, l - 1)

        return carry

    lax.fori_loop(0, LAYERS, backward, 0)
    def input_rows(a, s):
        for rr in range(band):
            dh[a, rr] = jnp.where(column < width_of(a), dh[a, rr], 0.0)
        return s

    lax.fori_loop(0, maps_here, input_rows, 0)

    outs = (
        (
            remote(dh.at[:, pl.ds(2 * other, 2)], ig_ref.at[c], out_s.at[0], out_r.at[0], m, z, other),
            pltpu.make_async_copy(dh.at[:, pl.ds(2 * c, 2)], ig_ref.at[c], out_l.at[0]),
        ),
        (
            remote(pbuf.at[other], pooled_ref.at[c], out_s.at[1], out_r.at[1], m, z, other),
            pltpu.make_async_copy(pbuf.at[c], pooled_ref.at[c], out_l.at[1]),
        ),
        (
            remote(sums_own, sums_ref.at[c], out_s.at[2], out_r.at[2], m, z, other),
            pltpu.make_async_copy(sums_own, sums_ref.at[c], out_l.at[2]),
        ),
    )
    for there, here in outs:
        there.start()
        here.start()

    g_partner.wait_send()
    sent_x_halo(2, 4)

    def sent(e, carry):
        each(1, chips, lambda k: z_copy(e, k).wait_send())
        each(1, PLANE, lambda k: m_copy(e, k).wait_send())
        return carry

    lax.fori_loop(0, 2 * LAYERS, sent, 0)
    for l in range(LAYERS):
        at_copy(l).wait_send()
    for l in range(LAYERS - 1):
        sent_dz(l)

    def drain(s, carry):
        @pl.when(s == EARLY)
        def _():
            ready_terms(0)

        for i in range(3):
            j = s - EARLY - 3 * i

            @pl.when(jnp.logical_and(j >= 0, j < 3))
            def _(i=i, j=j):
                tap_terms(0, i, j)
                c2(2 * TAPS + 3 * i + j).start()

        for stage, first, lag in (
            (stage_done, 0, 2 * FOLD + 4 * LAG),
            (stage_late, 0, 2 * FOLD + 3 * LAG),
            (stage_chip, 0, 2 * FOLD + 2 * LAG),
            (stage_first, 0, 2 * FOLD + LAG),
            (stage_back, 0, 2 * FOLD),
            (stage_sum, 0, FOLD),
            (stage_fold, 0, 0),
            (stage_second, TAPS, 0),
        ):
            q = first + s - lag

            @pl.when(jnp.logical_and(q >= first, q < UNITS))
            def _(stage=stage, q=q):
                stage(q)

        return carry

    lax.fori_loop(0, UNITS + 2 * FOLD + 4 * LAG, drain, 0)
    for a in range(maps_here):
        act_copy(2, a).wait_send()
    for there, here in outs:
        there.wait()
        here.wait()


RING = 4


def finish_kernel(kg_ref, pooled_ref, sums_ref, kernel_out, pooled_out, gain_out, shift_out, ring, sem):
    def copy(t):
        slot = lax.rem(t, RING)
        return pltpu.make_async_copy(ring.at[slot], kernel_out.at[t], sem.at[slot])

    def one(t, s):
        @pl.when(t >= RING)
        def _():
            copy(t - RING).wait()

        ring[lax.rem(t, RING)] = kg_ref[t].astype(F32)
        copy(t).start()
        return s

    lax.fori_loop(0, UNITS, one, 0)
    for a in range(pooled_out.shape[0]):
        row = jnp.concatenate([pooled_ref[0, a], pooled_ref[1, a]], 1)
        pooled_out[a, 0] = row[: pooled_out.shape[2]]
    sums = jnp.concatenate([sums_ref[0], sums_ref[1]], 1)
    gain_out[...] = sums[:LAYERS]
    shift_out[...] = sums[LAYERS : 2 * LAYERS]
    for t in range(UNITS - RING, UNITS):
        copy(t).wait()


def solution(mesh):
    chips = mesh.shape["rows"] // 2

    def per_device(
        block_input,
        conv_weights,
        norm_gains,
        norm_shifts,
        map_width,
        map_group,
        pool_index,
        task_mask,
        task_weights,
        task_grads,
    ):
        maps_here, rows_here, columns, channels = block_input.shape
        pooled_columns = pool_index.shape[2]
        height = rows_here * mesh.shape["rows"]
        half = channels // 2
        band = 2 * rows_here
        pixels = maps_here * band * PAD
        actives = chips // 2
        owners = min(actives, 8)
        piece = half // 2 // owners
        rounds = 2 * LAYERS
        slots = 2 * UNITS * (actives - 1) * piece * half + 4 * rounds * chips * 8 * half
        grant = (36 * 1024 + 256) * 1024 + slots
        vmem, dma = pltpu.VMEM, pltpu.SemaphoreType.DMA
        tile = (maps_here, band + 2, PAD, half)
        edge = (2, maps_here, PAD, half)
        whole = pl.BlockSpec(memory_space=pltpu.VMEM)
        outside = pl.BlockSpec(memory_space=pltpu.HBM)
        index_rows = jnp.transpose(pool_index, (0, 2, 1, 3))
        anywhere = pl.BlockSpec(memory_space=pl.ANY)
        pooled, ig, kg, sums = pl.pallas_call(
            functools.partial(block_kernel, chips, height),
            out_shape=(
                jax.ShapeDtypeStruct((2, maps_here, PAD // 2, half), BF16),
                jax.ShapeDtypeStruct((2, maps_here, rows_here, PAD, half), F32),
                jax.ShapeDtypeStruct((UNITS, channels, channels), BF16),
                jax.ShapeDtypeStruct((2, 8, half), F32),
            ),
            in_specs=[whole, anywhere] + [outside] * 8,
            out_specs=[anywhere] * 4,
            scratch_shapes=[
                vmem(norm_gains.shape, F32),
                vmem(norm_shifts.shape, F32),
                pltpu.SMEM(map_width.shape, jnp.int32),
                pltpu.SMEM(map_group.shape, jnp.int32),
                vmem((maps_here, pooled_columns, channels), jnp.int32),
                pltpu.SMEM(task_mask.shape, jnp.int32),
                pltpu.SMEM(task_weights.shape, F32),
                vmem(task_grads.shape, BF16),
                vmem((LAYERS, 3, 3, half, half), BF16),
                vmem((LAYERS, 3, 3, half, half), BF16),
                vmem((2,) + tile, BF16),
                vmem((2,) + tile, BF16),
                vmem((LAYERS, 2, half, maps_here * (band + 2) * PAD), BF16),
                vmem((2, half, pixels), BF16),
                vmem((LAYERS,) + tile, F32),
                vmem(edge, BF16),
                vmem((LAYERS,) + edge, BF16),
                vmem((maps_here, band, PAD, half), F32),
                vmem(edge, BF16),
                vmem((LAYERS,) + edge, BF16),
                vmem((2,) + tile, BF16),
                vmem((2,) + tile, BF16),
                vmem((LAYERS, maps_here, band, PAD, half), BF16),
                vmem((3, 2, maps_here, band, PAD, half), BF16),
                vmem((3, pixels, half), F32),
                vmem((2, 2, maps_here, PAD // 2, half), F32),
                vmem((4, 2, maps_here, PAD // 2, half), F32),
                vmem((half // 128, PAD, 128), F32),
                vmem((2, maps_here, PAD // 2, half), BF16),
                vmem((rounds, chips, 8, half), F32),
                vmem((rounds, PLANE, 8, half), F32),
                vmem((maps_here, PLANE, 8, half), F32),
                vmem((PLANE, 8, half), F32),
                vmem((2, 8, half), F32),
                vmem((8, half), F32),
                vmem((LAYERS, 8, half), F32),
                vmem((LAYERS, 8, half), F32),
                vmem((2, 8, half), F32),
                vmem((1, 8, half), F32),
                vmem((1, 8, half), F32),
                vmem((8, half), F32),
                vmem((2 * TAPS, half, half), BF16),
                vmem((UNITS, half // 2, half), BF16),
                vmem((2 * TAPS, half // 2, half), BF16),
                vmem((UNITS, actives - 1, piece, half), BF16),
                vmem((UNITS, piece, half), BF16),
                dma((8,)),
                dma((LAYERS, 3)),
                dma((6,)),
                dma((6,)),
                dma((3,)),
                dma((3,)),
                dma((rounds, chips)),
                dma((rounds, chips)),
                dma((rounds, PLANE)),
                dma((rounds, PLANE)),
                dma((LAYERS, 2)),
                dma((LAYERS, 2)),
                dma((LAYERS, 2)),
                dma((LAYERS, 2)),
                dma((LAYERS, maps_here)),
                dma((LAYERS, maps_here)),
                dma((LAYERS, maps_here)),
                dma((LAYERS, maps_here)),
                dma((3,)),
                dma((3,)),
                dma((3,)),
                dma((LAYERS,)),
                dma((LAYERS,)),
                dma((LAYERS, 2, maps_here)),
                dma((LAYERS, maps_here)),
                dma((UNITS,)),
                dma((UNITS,)),
                dma((UNITS,)),
                dma((UNITS,)),
                dma((UNITS, owners)),
                dma((UNITS, actives - 1)),
                dma((UNITS, actives)),
                dma((UNITS, owners)),
                dma((UNITS,)),
                dma((UNITS,)),
                dma((UNITS,)),
                dma((UNITS,)),
                dma((UNITS,)),
                dma((UNITS,)),
                dma((UNITS,)),
                dma((UNITS,)),
                dma((UNITS,)),
                dma((UNITS,)),
                dma((UNITS,)),
            ],
            compiler_params=pltpu.CompilerParams(
                collective_id=0,
                has_side_effects=True,
                vmem_limit_bytes=grant,
            ),
        )(
            block_input,
            conv_weights,
            *(
                pltpu.with_memory_space_constraint(v, pltpu.HBM)
                for v in (
                    norm_gains,
                    norm_shifts,
                    map_width,
                    map_group,
                    index_rows,
                    task_mask,
                    task_weights,
                    task_grads,
                )
            ),
        )
        input_grad = jnp.concatenate([ig[0], ig[1]], -1)[:, :, :columns]
        kernel_grads, pooled, gain_grads, shift_grads = pl.pallas_call(
            finish_kernel,
            out_shape=(
                jax.ShapeDtypeStruct(kg.shape, F32),
                jax.ShapeDtypeStruct(pool_index.shape, BF16),
                jax.ShapeDtypeStruct(norm_gains.shape, F32),
                jax.ShapeDtypeStruct(norm_shifts.shape, F32),
            ),
            in_specs=[whole] * 3,
            out_specs=(anywhere, whole, whole, whole),
            scratch_shapes=[vmem((RING,) + kg.shape[1:], F32), dma((RING,))],
            compiler_params=pltpu.CompilerParams(vmem_limit_bytes=24 * 1024 * 1024),
        )(kg, pooled, sums)
        return (
            pooled,
            input_grad,
            kernel_grads.reshape(conv_weights.shape),
            gain_grads,
            shift_grads,
        )

    return jax.shard_map(
        per_device,
        mesh=mesh,
        in_specs=(
            P("maps", "rows", None, None),
            P(),
            P(),
            P(),
            P(),
            P(),
            P("maps", "rows", None, None),
            P("maps", None),
            P(),
            P(None, "maps", "rows", None, None),
        ),
        out_specs=(P("maps", "rows", None, None), P("maps", "rows", None, None), P(), P(), P()),
        check_vma=False,
    )
```

```python
import functools

import jax
import jax.numpy as jnp
from jax import lax
from jax.experimental import pallas as pl
from jax.experimental.pallas import tpu as pltpu
from jax.sharding import PartitionSpec as P

MESH = pl.DeviceIdType.MESH
epsilon = 1e-05
PAD = 64
LAYERS = 3
TAPS = 9
UNITS = LAYERS * TAPS
PLANE = 4
LAG = 6
EARLY = 1
FOLD = 2
F32 = jnp.float32
BF16 = jnp.bfloat16


def each(first, last, body):
    if last - first <= 8:
        for k in range(first, last):
            body(k)
    else:
        lax.fori_loop(first, last, lambda k, s: (body(k), s)[1], 0)


def block_kernel(
    chips,
    height,
    x_ref,
    w_ref,
    gain_hbm,
    shift_hbm,
    width_hbm,
    group_hbm,
    index_hbm,
    tmask_hbm,
    tweight_hbm,
    tgrad_hbm,
    pooled_ref,
    ig_ref,
    kg_ref,
    sums_ref,
    gain_ref,
    shift_ref,
    width_ref,
    group_ref,
    index_ref,
    tmask_ref,
    tweight_ref,
    tgrad_ref,
    wa,
    wb,
    act_own,
    act_oth,
    act_t,
    act_b,
    zbuf,
    zs,
    zh,
    dh,
    dhs,
    dhh,
    dz_own,
    dz_oth,
    dzr,
    dzv,
    prod,
    gsrc,
    gbuf,
    hrow,
    pbuf,
    st1,
    st2,
    coef,
    nall,
    inv_t,
    cnt_t,
    avg_t,
    scl_t,
    mean_t,
    tb_t,
    ta_t,
    sums_own,
    terms,
    r2,
    rf,
    r3,
    fin,
    in_sem,
    w_sem,
    x_s,
    x_r,
    g_s,
    g_r,
    st1_s,
    st1_r,
    st2_s,
    st2_r,
    zh_s,
    zh_r,
    dh_s,
    dh_r,
    act_s,
    act_r,
    dz_s,
    dz_r,
    out_s,
    out_r,
    out_l,
    at_s,
    at_r,
    dzr_s,
    dzr_r,
    r2_s,
    r2_r,
    rf_s,
    rf_r,
    r3_s,
    r3_r,
    az_s,
    az_r,
    af_s,
    af_r,
    ab_s,
    ab_r,
    aa_s,
    aa_r,
    ae_s,
    ae_r,
    ap_s,
    ap_r,
    loc_s,
):
    maps_here = x_ref.shape[0]
    columns = x_ref.shape[2]
    half = x_ref.shape[3] // 2
    tasks = tgrad_ref.shape[0]
    pooled_columns = tgrad_ref.shape[3]
    lanes = half // 128
    tiles = [slice(n * 128, (n + 1) * 128) for n in range(lanes)]
    band = 4
    pixels = maps_here * band * PAD
    actives = chips // 2
    owners = min(actives, 8)
    piece = (half // 2) // owners
    m = lax.axis_index("maps")
    r = lax.axis_index("rows")
    c = lax.rem(r, 2)
    z = lax.div(r, 2)
    other = 1 - c
    first_map = m * maps_here
    x_bit = lax.rem(m, 2)
    y_bit = lax.div(m, 2)
    x_peer = m + 1 - 2 * x_bit
    y_peer = m + 2 - 4 * y_bit
    g_bit = (1 - c) * x_bit + c * y_bit
    h_bit = (1 - c) * y_bit + c * x_bit
    g_peer = (1 - c) * x_peer + c * y_peer
    h_peer = (1 - c) * y_peer + c * x_peer
    pair = lax.div(z, 2)
    turn = lax.rem(pair, 2)
    active_z = 2 * pair + 1 - turn
    is_active = z == active_z
    is_passive = z != active_z
    is_owner = jnp.logical_and(is_active, pair < owners)
    role = jnp.where(is_active, 0, 1)
    up_there = z > 0
    down_there = z < chips - 1
    row8 = lax.broadcasted_iota(jnp.int32, (8, half), 0)
    column = lax.broadcasted_iota(jnp.int32, (PAD, half), 0)

    def remote(src, dst, send, recv, mm, zz, cc):
        return pltpu.make_async_remote_copy(
            src_ref=src,
            dst_ref=dst,
            send_sem=send,
            recv_sem=recv,
            device_id=(mm, zz * 2 + cc),
            device_id_type=MESH,
        )

    def own_half(v):
        return jnp.where(c == 0, v[..., :half], v[..., half:])

    def width_of(a):
        return width_ref[first_map + a]

    own_at = pl.ds(pl.multiple_of(c * half, half), half)
    oth_at = pl.ds(pl.multiple_of(other * half, half), half)

    def weight_copy(l, n):
        dst = (wa, wb, wb)[n]
        k_at, o_at = ((own_at, own_at), (oth_at, own_at), (own_at, oth_at))[n]
        return pltpu.make_async_copy(w_ref.at[l, :, :, k_at, o_at], dst.at[l], w_sem.at[l, n])

    fetches = [
        pltpu.make_async_copy(src, dst, in_sem.at[n])
        for n, (src, dst) in enumerate(
            (
                (width_hbm, width_ref),
                (group_hbm, group_ref),
                (tmask_hbm, tmask_ref),
                (tweight_hbm, tweight_ref),
                (gain_hbm, gain_ref),
                (shift_hbm, shift_ref),
                (index_hbm.at[:, :, 0, :], index_ref),
                (tgrad_hbm, tgrad_ref),
            )
        )
    ]
    for fetch in fetches:
        fetch.start()
    for l in range(LAYERS):
        weight_copy(l, 0).start()
        weight_copy(l, 1).start()

    barrier = pltpu.get_barrier_semaphore()

    def greet(k):
        rr = lax.rem(r + k, 2 * chips)
        pl.semaphore_signal(barrier, inc=1, device_id=(m, rr), device_id_type=MESH)

    each(1, 2 * chips, greet)
    for k in range(1, PLANE):
        for core in (c, other):
            there = (lax.rem(m + k, PLANE), z * 2 + core)
            pl.semaphore_signal(barrier, inc=1, device_id=there, device_id_type=MESH)

    for fetch in fetches:
        fetch.wait()

    mine = pl.ds(1 + 2 * c, 2)
    for a in range(maps_here):
        inside = lax.broadcasted_iota(jnp.int32, (columns, 2 * half), 0) < width_of(a)
        for rr in range(2):
            v = jnp.where(inside, x_ref[a, rr].astype(F32), 0.0).astype(BF16)
            spot = 1 + 2 * c + rr
            act_own[0, a, spot, pl.ds(48, 16), :] = jnp.zeros((16, half), BF16)
            act_oth[0, a, spot, pl.ds(48, 16), :] = jnp.zeros((16, half), BF16)
            act_own[0, a, spot, pl.ds(0, columns), :] = own_half(v)
            act_oth[0, a, spot, pl.ds(0, columns), :] = jnp.where(
                c == 0, v[:, half:], v[:, :half]
            )

    @pl.when(z == 0)
    def _():
        act_own[0, :, 0] = jnp.zeros((maps_here, PAD, half), BF16)
        act_oth[0, :, 0] = jnp.zeros((maps_here, PAD, half), BF16)

    @pl.when(z == chips - 1)
    def _():
        act_own[0, :, 5] = jnp.zeros((maps_here, PAD, half), BF16)
        act_oth[0, :, 5] = jnp.zeros((maps_here, PAD, half), BF16)

    pl.semaphore_wait(barrier, 2 * chips - 1 + 2 * (PLANE - 1))

    x_partner = (
        remote(act_own.at[0, :, mine], act_oth.at[0, :, mine], x_s.at[0], x_r.at[0], m, z, other),
        remote(act_oth.at[0, :, mine], act_own.at[0, :, mine], x_s.at[1], x_r.at[1], m, z, other),
    )
    g_partner = remote(gsrc.at[other], gbuf.at[1 + c], g_s.at[0], g_r.at[0], m, z, other)

    def x_halo(n, src_row, dst_row, zz):
        cc = (c, other)[n % 2]
        low = dst_row == band + 1
        if n >= 2:
            src, dst = gsrc.at[cc], gbuf.at[3 if low else 0]
            return remote(src, dst, g_s.at[n - 1], g_r.at[1 if low else 2], m, zz, cc)
        src, dst = (act_own, act_oth)[n].at[0, :, src_row], act_own.at[0, :, dst_row]
        return remote(src, dst, x_s.at[2 + n], x_r.at[2 if low else 3], m, zz, cc)

    def x_pass(row):
        n = 4 if row == 0 else 5
        src, dst = act_own.at[0, :, row], act_oth.at[0, :, row]
        return remote(src, dst, x_s.at[n], x_r.at[n], m, z, other)

    for copy in x_partner:
        copy.start()

    @pl.when(jnp.logical_and(c == 0, up_there))
    def _():
        for n in range(2):
            x_halo(n, 1, 5, z - 1).start()

    @pl.when(jnp.logical_and(c == 1, down_there))
    def _():
        for n in range(2):
            x_halo(n, 4, 0, z + 1).start()

    gsrc[...] = jnp.zeros(gsrc.shape, F32)
    for a in range(maps_here):
        total = None
        for t in range(tasks):
            scale = tweight_ref[t] * tmask_ref[a, t].astype(F32)
            term = tgrad_ref[t, a, 0].astype(F32) * scale
            total = term if total is None else total + term
        position = index_ref[a].astype(F32)
        for h in range(2):
            gsrc[h, 0, a, pl.ds(0, pooled_columns), :] = total[:, h * half : (h + 1) * half]
            gsrc[h, 1, a, pl.ds(0, pooled_columns), :] = position[:, h * half : (h + 1) * half]
    gbuf[1 + c] = gsrc[c]

    for mm in range(PLANE):
        sizes = jnp.zeros((8, half), F32)
        for b in range(maps_here):
            sizes = jnp.where(
                row8 == b, (width_ref[mm * maps_here + b] * height).astype(F32), sizes
            )
        nall[mm] = sizes
    inside_sizes = jnp.zeros((8, half), F32)
    for b in range(maps_here):
        inside_sizes = jnp.where(row8 == b, (width_of(b) * band).astype(F32), inside_sizes)
    inv_t[0] = inside_sizes
    inv_t[1] = jnp.where(row8 < maps_here, 1.0 / jnp.maximum(inside_sizes, 1.0), 0.0)
    counts = jnp.ones((8, half), F32)
    for a in range(maps_here):
        total = jnp.zeros((1, half), F32)
        for mm in range(PLANE):
            same = jnp.zeros((8, half), F32)
            for b in range(maps_here):
                alike = group_ref[first_map + a] == group_ref[mm * maps_here + b]
                same = jnp.where(row8 == b, jnp.where(alike, 1.0, 0.0), same)
            coef[a, mm] = same
            total = total + jnp.sum(same * nall[mm], 0, keepdims=True)
        counts = jnp.where(row8 == a, total, counts)
    cnt_t[...] = counts

    def z_copy(e, k):
        zz = lax.rem(z + k, chips)
        return remote(st1.at[e, z], st1.at[e, z], st1_s.at[e, k], st1_r.at[e, z], m, zz, c)

    def z_arrival(e, k):
        zz = lax.rem(z + k, chips)
        return remote(st1.at[e, zz], st1.at[e, zz], st1_s.at[e, k], st1_r.at[e, zz], m, zz, c)

    def m_copy(e, k):
        mm = lax.rem(m + k, PLANE)
        return remote(st2.at[e, m], st2.at[e, m], st2_s.at[e, k], st2_r.at[e, m], mm, z, c)

    def m_arrival(e, k):
        mm = lax.rem(m + k, PLANE)
        return remote(st2.at[e, mm], st2.at[e, mm], st2_s.at[e, k], st2_r.at[e, mm], mm, z, c)

    def send_z(e, tile):
        st1[e, z] = tile
        each(1, chips, lambda k: z_copy(e, k).start())

    def wait_z(e):
        each(1, chips, lambda k: z_arrival(e, k).wait_recv())

    def send_m(e, tile):
        st2[e, m] = tile
        each(1, PLANE, lambda k: m_copy(e, k).start())

    def wait_m(e):
        each(1, PLANE, lambda k: m_arrival(e, k).wait_recv())

    def products(source, l, taps, kernel, transposed, fresh):
        starts = [2 - i if transposed else i for i in taps]
        lhs = jnp.concatenate(
            [source[lax.rem(l, 2), :, s : s + band].reshape(pixels, half) for s in starts], 1
        )
        for j in range(3):
            rhs = jnp.concatenate([kernel[l, i, j] for i in taps], 1 if transposed else 0)
            got = lax.dot_general(
                lhs,
                rhs,
                (((1,), (1 if transposed else 0,)), ((), ())),
                preferred_element_type=F32,
            )
            if fresh:
                prod[j] = got
            else:
                prod[j] = prod[j] + got

    def shifted(a, rr, before, behind, n):
        rows = pl.ds(pl.multiple_of((a * band + rr) * PAD, PAD), PAD)
        return (
            prod[1, rows, n]
            + pltpu.roll(prod[before, rows, n], 1, 0)
            + pltpu.roll(prod[behind, rows, n], PAD - 1, 0)
        )

    def row_of(table, l, a):
        return table[l, pl.ds(a, 1), :]

    def gain_of(l):
        return own_half(gain_ref[pl.ds(l, 1), :])

    def shift_of(l):
        return own_half(shift_ref[pl.ds(l, 1), :])

    def limit(a, rr):
        w = width_of(a)
        if rr == 0:
            return jnp.where(up_there, w, 0)
        if rr == band + 1:
            return jnp.where(down_there, w, 0)
        return w

    def z_halo(l, way):
        there = z - 1 + 2 * way
        return remote(zs.at[way], zh.at[l, 1 - way], zh_s.at[l, way], zh_r.at[l, way], m, there, c)

    def dh_halo(l, way):
        there = z - 1 + 2 * way
        return remote(dhs.at[way], dhh.at[l, 1 - way], dh_s.at[l, way], dh_r.at[l, way], m, there, c)

    def start_halo(halo, l):
        @pl.when(up_there)
        def _():
            halo(l, 0).start()

        @pl.when(down_there)
        def _():
            halo(l, 1).start()

    def wait_halo(halo, l):
        @pl.when(up_there)
        def _():
            halo(l, 1).wait_recv()
            halo(l, 0).wait_send()

        @pl.when(down_there)
        def _():
            halo(l, 0).wait_recv()
            halo(l, 1).wait_send()

    def act_copy(l, a):
        slot = lax.rem(l, 2)
        src, dst = act_own.at[slot, a], act_oth.at[slot, a]
        return remote(src, dst, act_s.at[l, a], act_r.at[l, a], m, z, other)

    def at_copy(l):
        return remote(act_t.at[l, 0], act_t.at[l, 1], at_s.at[l], at_r.at[l], g_peer, z, c)

    def dzr_copy(l, a, way):
        src, dst = dz_own.at[lax.rem(l, 2), a, pl.ds(1, band)], dzr.at[l, a]
        peer = (x_peer, y_peer)[way]
        return remote(src, dst, dzr_s.at[l, way, a], dzr_r.at[l, a], peer, z, way)

    def if_wanted(way, body):
        @pl.when((x_bit, y_bit)[way] + c == 1)
        def _():
            body()

    def dz_copy(l, a):
        slot = lax.rem(l, 2)
        src, dst = dz_own.at[slot, a], dz_oth.at[slot, a]
        return remote(src, dst, dz_s.at[l, a], dz_r.at[l, a], m, z, other)

    def send_gradients():
        g_partner.start()

        @pl.when(jnp.logical_and(c == 0, up_there))
        def _():
            for n in range(2, 4):
                x_halo(n, 1, 5, z - 1).start()

        @pl.when(jnp.logical_and(c == 1, down_there))
        def _():
            for n in range(2, 4):
                x_halo(n, 4, 0, z + 1).start()

    def if_there(way, body):
        @pl.when((up_there, down_there)[way])
        def _():
            body()

    def wait_x_halo(n):
        if_there(0, lambda: x_halo(n, 4, 0, z - 1).wait_recv())
        if_there(1, lambda: x_halo(n, 1, 5, z + 1).wait_recv())

    def each_x_pass(act):
        if_there(0, lambda: act(x_pass(0)))
        if_there(1, lambda: act(x_pass(band + 1)))

    def sent_x_halo(first, last):
        @pl.when(jnp.logical_and(c == 0, up_there))
        def _():
            for n in range(first, last):
                x_halo(n, 1, 5, z - 1).wait_send()

        @pl.when(jnp.logical_and(c == 1, down_there))
        def _():
            for n in range(first, last):
                x_halo(n, 4, 0, z + 1).wait_send()

    def unpool(a, s):
        for rr in range(band + 2):
            slot, lower = (rr + 1) // 2, (rr + 1) % 2
            g = gbuf[slot, 0, a]
            position = gbuf[slot, 1, a]
            for b in range(2):
                v = jnp.where(position == float(2 * lower + b), g, 0.0)
                for n in range(lanes):
                    hrow[n, pl.ds(b, PAD // 2, stride=2), :] = v[:, n * 128 : (n + 1) * 128]
            v = jnp.concatenate([hrow[n] for n in range(lanes)], 1)
            if rr in (0, band + 1):
                dhh[LAYERS - 1, rr // (band + 1), a] = v.astype(BF16)
            else:
                dh[a, rr - 1] = v
        return s

    def forward(l, first):
        weight_copy(l, 0).wait()
        weight_copy(l, 1).wait()
        if first:
            for copy in x_partner:
                copy.wait_recv()
            products(act_own, l, (1,), wa, False, True)
            products(act_oth, l, (1,), wb, False, False)
            wait_x_halo(0)
            each_x_pass(lambda copy: copy.start())
            products(act_own, l, (0, 2), wa, False, False)
            each_x_pass(lambda copy: copy.wait_recv())
            products(act_oth, l, (0, 2), wb, False, False)
        else:
            products(act_own, l, (0, 1, 2), wa, False, True)
            for a in range(maps_here):
                act_copy(l, a).wait_recv()
            products(act_oth, l, (0, 1, 2), wb, False, False)
        weight_copy(l, 2).start()

        def collect(a, tile):
            inside = column[:, :128] < width_of(a)
            pixels_inside = (width_of(a) * band).astype(F32)
            totals, squares = [], []
            for n in tiles:
                total = jnp.zeros((PAD, 128), F32)
                for rr in range(band):
                    v = shifted(a, rr, 0, 2, n)
                    zbuf[l, a, 1 + rr, :, n] = v
                    total = total + jnp.where(inside, v, 0.0)
                total = jnp.sum(total, 0, keepdims=True)
                mean = total / pixels_inside
                square = jnp.zeros((PAD, 128), F32)
                for rr in range(band):
                    v = jnp.where(inside, zbuf[l, a, 1 + rr, :, n] - mean, 0.0)
                    square = square + v * v
                    if rr in (0, band - 1):
                        zs[rr // (band - 1), a, :, n] = v.astype(BF16)
                totals.append(total)
                squares.append(jnp.sum(square, 0, keepdims=True))
            tile = jnp.where(row8 == a, jnp.concatenate(totals, 1), tile)
            return jnp.where(row8 == a + maps_here, jnp.concatenate(squares, 1), tile)

        tile = lax.fori_loop(0, maps_here, collect, jnp.zeros((8, half), F32))
        send_z(l, tile)
        start_halo(z_halo, l)
        act_t[l, 0] = act_own[lax.rem(l, 2)].reshape(maps_here * (band + 2) * PAD, half).T
        wait_z(l)
        sizes, inverse = inv_t[0], inv_t[1]
        mean_t[0] = st1[l, jnp.maximum(z - 1, 0)] * inverse
        mean_t[1] = st1[l, jnp.minimum(z + 1, chips - 1)] * inverse
        total = st1[l, 0]
        for zz in range(1, chips):
            total = total + st1[l, zz]
        mean = total * inverse * (1.0 / chips)
        square = jnp.zeros((8, half), F32)
        for zz in range(chips):
            v = st1[l, zz]
            gap = v * inverse - mean
            square = square + pltpu.roll(v, 8 - maps_here, 0) + sizes * gap * gap
        tile = jnp.where(row8 < maps_here, mean, pltpu.roll(square, maps_here, 0))
        send_m(l, jnp.where(row8 < 2 * maps_here, tile, 0.0))
        if not first:

            @pl.when(l == LAYERS - 1)
            def _():
                g_partner.wait_recv()
                wait_x_halo(2)
                lax.fori_loop(0, maps_here, unpool, 0)

        wait_m(l)
        at_copy(l).start()
        if first:
            send_gradients()
        averages = jnp.zeros((8, half), F32)
        scalings = jnp.zeros((8, half), F32)
        for a in range(maps_here):
            count = cnt_t[a : a + 1, :]
            average = jnp.zeros((8, half), F32)
            for mm in range(PLANE):
                average = average + coef[a, mm] * nall[mm] * st2[l, mm]
            average = jnp.sum(average, 0, keepdims=True) / count
            variance = jnp.zeros((8, half), F32)
            for mm in range(PLANE):
                v = st2[l, mm]
                gap = v - average
                variance = variance + coef[a, mm] * (
                    pltpu.roll(v, 8 - maps_here, 0) + nall[mm] * gap * gap
                )
            variance = jnp.sum(variance, 0, keepdims=True) / count
            averages = jnp.where(row8 == a, average, averages)
            scalings = jnp.where(row8 == a, lax.rsqrt(variance + epsilon), scalings)
        avg_t[l] = averages
        scl_t[l] = scalings
        wait_halo(z_halo, l)

        def activate(a, s):
            gain, shift = gain_of(l), shift_of(l)
            for n in tiles:
                average = row_of(avg_t, l, a)[:, n]
                factor = row_of(scl_t, l, a)[:, n] * gain[:, n]
                for rr in range(band + 2):
                    if rr in (0, band + 1):
                        way = rr // (band + 1)
                        v = zh[l, way, a, :, n].astype(F32) + row_of(mean_t, way, a)[:, n]
                        zbuf[l, a, rr, :, n] = v
                    else:
                        v = zbuf[l, a, rr, :, n]
                    y = (v - average) * factor + shift[:, n]
                    h = jnp.where(column[:, n] < limit(a, rr), y * jax.nn.sigmoid(y), 0.0)
                    act_own[lax.rem(l + 1, 2), a, rr, :, n] = h.astype(BF16)

            @pl.when(l < LAYERS - 1)
            def _():
                act_copy(l + 1, a).start()

            return s

        if first:
            for copy in x_partner:
                copy.wait_send()
            sent_x_halo(0, 2)
            each_x_pass(lambda copy: copy.wait_send())
        else:

            @pl.when(l == 2)
            def _():
                for a in range(maps_here):
                    act_copy(1, a).wait_send()

        lax.fori_loop(0, maps_here, activate, 0)

    forward(0, True)
    lax.fori_loop(1, LAYERS, lambda l, s: (forward(l, False), s)[1], 0)


    def pool():
        def one(a, s):
            for pr in range(2):
                total = jnp.zeros((PAD // 2, half), F32)
                position = gbuf[1 + pr, 1, a]
                for lower in range(2):
                    v = act_own[LAYERS % 2, a, 1 + 2 * pr + lower].astype(F32)
                    for n in range(lanes):
                        hrow[n] = v[:, n * 128 : (n + 1) * 128]
                    for b in range(2):
                        v = jnp.concatenate(
                            [hrow[n, pl.ds(b, PAD // 2, stride=2), :] for n in range(lanes)], 1
                        )
                        total = total + jnp.where(position == float(2 * lower + b), v, 0.0)
                pbuf[pr, a] = total.astype(BF16)
            return s

        lax.fori_loop(0, maps_here, one, 0)

    def second_rows(bit):
        return pl.ds(pl.multiple_of(bit * (half // 2), half // 2), half // 2)

    def piece_rows(p):
        return pl.ds(pl.multiple_of(p * piece, piece), piece)

    def term_slot(q):
        return lax.rem(q, 2 * TAPS)

    def c2(q):
        src = terms.at[term_slot(q), second_rows(1 - h_bit)]
        return remote(src, r2.at[q], r2_s.at[q], r2_r.at[q], h_peer, z, c)

    def z_of(n):
        return 2 * n + 1 - lax.rem(n, 2)

    def cf(q):
        passive_z = 2 * pair + turn
        there = active_z + passive_z - z
        return remote(r2.at[q], rf.at[term_slot(q)], rf_s.at[q], rf_r.at[q], m, there, c)

    def c3(q, p):
        slot = lax.rem(pair - p + actives - 1, actives)
        return remote(
            r2.at[q, piece_rows(p)], r3.at[q, slot], r3_s.at[q, p], r3_r.at[q, slot], m, z_of(p), c
        )

    def others(first, body, limit):
        def one(k):
            n = lax.rem(pair + k, actives)

            @pl.when(n < limit)
            def _():
                body(n)

        each(first, actives, one)

    def unit_of(q):
        k = lax.div(q, TAPS)
        return (LAYERS - 1 - k) * TAPS + (q - k * TAPS)

    def region(q, start, size, lane, lanes):
        start = pl.multiple_of(c * half + start, piece)
        lane = pl.multiple_of(lane, half)
        return kg_ref.at[unit_of(q), pl.ds(start, size), pl.ds(lane, lanes)]

    def cz(q, p, n):
        part = region(q, h_bit * (half // 2) + p * piece, piece, g_bit * half, half)
        return remote(fin.at[q], part, az_s.at[q, n], az_r.at[q, p], m, z_of(n), c)

    def cl(q):
        part = region(q, h_bit * (half // 2) + pair * piece, piece, g_bit * half, half)
        return pltpu.make_async_copy(fin.at[q], part, loc_s.at[q])

    def cu(q):
        passive_z = 2 * pair + turn
        there = active_z + passive_z - z
        part = region(q, h_bit * (half // 2), half // 2, g_bit * half, half)
        return remote(part, part, af_s.at[q], af_r.at[q], m, there, c)

    def cb(q):
        part = region(q, h_bit * (half // 2), half // 2, g_bit * half, half)
        return remote(part, part, ab_s.at[q], ab_r.at[q], h_peer, z, c)

    def ca(q):
        part = region(q, 0, half, g_bit * half, half)
        return remote(part, part, aa_s.at[q], aa_r.at[q], g_peer, z, c)

    def plan(q):
        k = lax.rem(q, 5)
        both = jnp.logical_or(lax.rem(k, 2) == 0, q >= UNITS - 5)
        mine = jnp.logical_or(both, lax.div(k, 2) == role)
        return mine, jnp.logical_and(mine, jnp.logical_not(both)), jnp.logical_not(mine)

    def ce(q):
        passive_z = 2 * pair + turn
        there = active_z + passive_z - z
        part = region(q, 0, half, (1 - g_bit) * half, half)
        return remote(part, part, ae_s.at[q], ae_r.at[q], m, there, c)

    def cp_part(q, start, size, lane, lanes):
        part = region(q, start, size, lane, lanes)
        return remote(part, part, ap_s.at[q], ap_r.at[q], m, z, other)

    def cp(q):
        return cp_part(q, 0, half, 0, 2 * half)

    def cp_rows(q, bit):
        return cp_part(q, bit * (half // 2), half // 2, g_bit * half, half)

    def cp_lanes(q):
        return cp_part(q, 0, half, (1 - g_bit) * half, half)

    def ready_terms(l):
        at_copy(l).wait_recv()
        for chip in range(2):
            for a in range(maps_here):
                first = a * (band + 2) * PAD
                rows = act_t[l, chip, :, first : first + (band + 2) * PAD]
                act_b[chip, :, a * band * PAD : (a + 1) * band * PAD] = rows[:, PAD : PAD + band * PAD]
        slot = lax.rem(l, 2)

        def variants(a, s):
            dzr_copy(l, a, 0).wait_recv()
            for chip in range(2):
                for rr in range(band):
                    for n in tiles:
                        if chip == 0:
                            mine, theirs = dz_own[slot, a, 1 + rr, :, n], dz_oth[slot, a, 1 + rr, :, n]
                            v = jnp.where(g_bit == c, mine, theirs)
                        else:
                            v = dzr[l, a, rr, :, n]
                        dzv[1, chip, a, rr, :, n] = v
                        v = v.astype(F32)
                        dzv[0, chip, a, rr, :, n] = pltpu.roll(v, PAD - 1, 0).astype(BF16)
                        dzv[2, chip, a, rr, :, n] = pltpu.roll(v, 1, 0).astype(BF16)
            return s

        lax.fori_loop(0, maps_here, variants, 0)

    def tap_terms(l, i, j):
        if i == 1:
            lhs = [act_b[0], act_b[1]]
        else:
            lhs = []
            for chip in range(2):
                for a in range(maps_here):
                    first = (a * (band + 2) + i) * PAD
                    lhs.append(act_t[l, chip, :, first : first + band * PAD])
        rhs = dzv[j].reshape(2 * pixels, half)
        q = (LAYERS - 1 - l) * TAPS + 3 * i + j
        got = jnp.dot(jnp.concatenate(lhs, 1), rhs, preferred_element_type=F32)
        terms[term_slot(q)] = got.astype(BF16)

    def weight_terms(l, i):
        lax.fori_loop(0, 3, lambda j, s: (tap_terms(l, i, j), s)[1], 0)

    def stage_second(q):
        c2(q).wait()
        kept = terms[term_slot(q), second_rows(h_bit)].astype(F32)
        r2[q] = (r2[q].astype(F32) + kept).astype(BF16)

        @pl.when(is_passive)
        def _():
            cf(q).start()

    def stage_fold(q):
        @pl.when(is_active)
        def _():
            cf(q).wait_recv()
            r2[q] = (r2[q].astype(F32) + rf[term_slot(q)].astype(F32)).astype(BF16)
            others(1, lambda n: c3(q, n).start(), owners)

    def stage_sum(q):
        @pl.when(is_owner)
        def _():
            for k in range(actives - 1):
                remote(
                    r3.at[q, k], r3.at[q, k], r3_s.at[q, 0], r3_r.at[q, k], m, z, c
                ).wait_recv()
            total = r2[q, piece_rows(pair)].astype(F32)
            for k in range(actives - 1):
                total = total + r3[q, k].astype(F32)
            fin[q] = total.astype(BF16)
            others(1, lambda n: cz(q, pair, n).start(), actives)
            cl(q).start()

    def stage_back(q):
        @pl.when(is_active)
        def _():
            others(1, lambda n: cz(q, n, n).wait_recv(), owners)

        @pl.when(is_owner)
        def _():
            cl(q).wait()

        @pl.when(is_active)
        def _():
            cu(q).start()

        @pl.when(is_passive)
        def _():
            cu(q).wait_recv()

        cb(q).start()
        cp_rows(q, h_bit).start()

    def stage_first(q):
        cb(q).wait_recv()
        mine, _, _ = plan(q)

        @pl.when(mine)
        def _():
            ca(q).start()

        cp_rows(q, 1 - h_bit).start()

        @pl.when(is_active)
        def _():
            others(1, lambda n: c3(q, n).wait_send(), owners)

        @pl.when(is_passive)
        def _():
            cf(q).wait_send()

    def stage_chip(q):
        mine, for_both, _ = plan(q)

        @pl.when(mine)
        def _():
            ca(q).wait_recv()

        @pl.when(for_both)
        def _():
            ce(q).start()

        @pl.when(mine)
        def _():
            cp_lanes(q).start()

        @pl.when(is_owner)
        def _():
            others(1, lambda n: cz(q, pair, n).wait_send(), actives)

        @pl.when(is_active)
        def _():
            cu(q).wait_send()

    def stage_late(q):
        _, _, not_mine = plan(q)

        @pl.when(not_mine)
        def _():
            ce(q).wait_recv()
            cp_lanes(q).start()

    def stage_done(q):
        mine, for_both, _ = plan(q)
        cb(q).wait_send()

        @pl.when(mine)
        def _():
            ca(q).wait_send()

        @pl.when(for_both)
        def _():
            ce(q).wait_send()

        cp(q).wait()

    def run(stage, first, last):
        lax.fori_loop(first, last, lambda q, s: (stage(q), s)[1], 0)

    def sent_dz(l):
        for a in range(maps_here):
            dz_copy(l, a).wait_send()
            for way in range(2):
                if_wanted(way, dzr_copy(l, a, way).wait_send)

    def backward(k, carry):
        l = LAYERS - 1 - k
        gain, shift = gain_of(l), shift_of(l)

        def gradient(a, rr, n):
            zhat = (zbuf[l, a, rr, :, n] - row_of(avg_t, l, a)[:, n]) * row_of(scl_t, l, a)[:, n]
            y = zhat * gain[:, n] + shift[:, n]
            s = jax.nn.sigmoid(y)
            if rr in (0, band + 1):
                upstream = dhh[l, rr // (band + 1), a, :, n].astype(F32)
            else:
                upstream = dh[a, rr - 1, :, n]
            dy = upstream * (s * (1.0 + y * (1.0 - s)))
            dy = jnp.where(column[:, n] < limit(a, rr), dy, 0.0)
            return dy, zhat

        def collect(a, tile):
            plains, crosses = [], []
            for n in tiles:
                plain = jnp.zeros((PAD, 128), F32)
                crossed = jnp.zeros((PAD, 128), F32)
                for rr in range(1, band + 1):
                    dy, zhat = gradient(a, rr, n)
                    dh[a, rr - 1, :, n] = dy
                    plain = plain + dy
                    crossed = crossed + dy * zhat
                plains.append(jnp.sum(plain, 0, keepdims=True))
                crosses.append(jnp.sum(crossed, 0, keepdims=True))
            tile = jnp.where(row8 == a, jnp.concatenate(plains, 1), tile)
            return jnp.where(row8 == a + maps_here, jnp.concatenate(crosses, 1), tile)

        e = LAYERS + l
        tile = lax.fori_loop(0, maps_here, collect, jnp.zeros((8, half), F32))
        send_z(e, tile)

        @pl.when(k == LAYERS - 1)
        def _():
            run(stage_second, 0, TAPS)

        @pl.when(k > 0)
        def _():
            ready_terms(l + 1)
            weight_terms(l + 1, 0)

        wait_z(e)
        total = st1[e, 0]
        for zz in range(1, chips):
            total = total + st1[e, zz]
        send_m(e, total)

        @pl.when(k > 0)
        def _():
            first = (LAYERS - 2 - l) * TAPS
            run(lambda q: c2(q).start(), first, first + 3)
            weight_terms(l + 1, 1)
            run(lambda q: c2(q).start(), first + 3, first + 6)
            weight_terms(l + 1, 2)
            run(lambda q: c2(q).start(), first + 6, first + 9)
            wait_halo(dh_halo, l)

        @pl.when(k == 0)
        def _():
            pool()

        wait_m(e)
        total = st2[e, 0]
        for mm in range(1, PLANE):
            total = total + st2[e, mm]
        sums_own[pl.ds(l, 1), :] = jnp.sum(
            jnp.where(row8 >= maps_here, total, 0.0), 0, keepdims=True
        )
        sums_own[pl.ds(LAYERS + l, 1), :] = jnp.sum(
            jnp.where(row8 < maps_here, total, 0.0), 0, keepdims=True
        )
        plains = jnp.zeros((8, half), F32)
        crosses = jnp.zeros((8, half), F32)
        for a in range(maps_here):
            plain = jnp.zeros((8, half), F32)
            crossed = jnp.zeros((8, half), F32)
            for mm in range(PLANE):
                v = st2[e, mm]
                plain = plain + coef[a, mm] * v
                crossed = crossed + coef[a, mm] * pltpu.roll(v, 8 - maps_here, 0)
            count = cnt_t[a : a + 1, :]
            plain = gain * (jnp.sum(plain, 0, keepdims=True) / count)
            crossed = gain * (jnp.sum(crossed, 0, keepdims=True) / count)
            plains = jnp.where(row8 == a, plain, plains)
            crosses = jnp.where(row8 == a, crossed, crosses)
        tb_t[0] = plains
        ta_t[0] = crosses

        def settle(a, s):
            for n in tiles:
                average, scaling = row_of(avg_t, l, a)[:, n], row_of(scl_t, l, a)[:, n]
                plain, crossed = row_of(tb_t, 0, a)[:, n], row_of(ta_t, 0, a)[:, n]
                for rr in range(band + 2):
                    if rr in (0, band + 1):
                        dy, zhat = gradient(a, rr, n)
                    else:
                        dy = dh[a, rr - 1, :, n]
                        zhat = (zbuf[l, a, rr, :, n] - average) * scaling
                    v = scaling * (dy * gain[:, n] - plain - zhat * crossed)
                    v = jnp.where(column[:, n] < limit(a, rr), v, 0.0)
                    dz_own[lax.rem(l, 2), a, rr, :, n] = v.astype(BF16)
            dz_copy(l, a).start()
            for way in range(2):
                if_wanted(way, dzr_copy(l, a, way).start)
            return s

        @pl.when(k == 2)
        def _():
            sent_dz(LAYERS - 1)

        lax.fori_loop(0, maps_here, settle, 0)
        products(dz_own, l, (0, 1, 2), wa, True, True)
        weight_copy(l, 2).wait()
        for a in range(maps_here):
            dz_copy(l, a).wait_recv()
        products(dz_oth, l, (0, 1, 2), wb, True, False)

        def gather(a, s):
            for n in tiles:
                for rr in range(band):
                    v = shifted(a, rr, 2, 0, n)
                    dh[a, rr, :, n] = v
                    if rr in (0, band - 1):
                        dhs[rr // (band - 1), a, :, n] = v.astype(BF16)
            return s

        lax.fori_loop(0, maps_here, gather, 0)

        @pl.when(l > 0)
        def _():
            start_halo(dh_halo, l - 1)

        return carry

    lax.fori_loop(0, LAYERS, backward, 0)
    def input_rows(a, s):
        for rr in range(band):
            dh[a, rr] = jnp.where(column < width_of(a), dh[a, rr], 0.0)
        return s

    lax.fori_loop(0, maps_here, input_rows, 0)

    outs = (
        (
            remote(dh.at[:, pl.ds(2 * other, 2)], ig_ref.at[c], out_s.at[0], out_r.at[0], m, z, other),
            pltpu.make_async_copy(dh.at[:, pl.ds(2 * c, 2)], ig_ref.at[c], out_l.at[0]),
        ),
        (
            remote(pbuf.at[other], pooled_ref.at[c], out_s.at[1], out_r.at[1], m, z, other),
            pltpu.make_async_copy(pbuf.at[c], pooled_ref.at[c], out_l.at[1]),
        ),
        (
            remote(sums_own, sums_ref.at[c], out_s.at[2], out_r.at[2], m, z, other),
            pltpu.make_async_copy(sums_own, sums_ref.at[c], out_l.at[2]),
        ),
    )
    for there, here in outs:
        there.start()
        here.start()

    g_partner.wait_send()
    sent_x_halo(2, 4)

    def sent(e, carry):
        each(1, chips, lambda k: z_copy(e, k).wait_send())
        each(1, PLANE, lambda k: m_copy(e, k).wait_send())
        return carry

    lax.fori_loop(0, 2 * LAYERS, sent, 0)
    for l in range(LAYERS):
        at_copy(l).wait_send()
    for l in range(LAYERS - 1):
        sent_dz(l)

    def drain(s, carry):
        @pl.when(s == EARLY)
        def _():
            ready_terms(0)

        for i in range(3):
            j = s - EARLY - 3 * i

            @pl.when(jnp.logical_and(j >= 0, j < 3))
            def _(i=i, j=j):
                tap_terms(0, i, j)
                c2(2 * TAPS + 3 * i + j).start()

        for stage, first, lag in (
            (stage_done, 0, 2 * FOLD + 4 * LAG),
            (stage_late, 0, 2 * FOLD + 3 * LAG),
            (stage_chip, 0, 2 * FOLD + 2 * LAG),
            (stage_first, 0, 2 * FOLD + LAG),
            (stage_back, 0, 2 * FOLD),
            (stage_sum, 0, FOLD),
            (stage_fold, 0, 0),
            (stage_second, TAPS, 0),
        ):
            q = first + s - lag

            @pl.when(jnp.logical_and(q >= first, q < UNITS))
            def _(stage=stage, q=q):
                stage(q)

        return carry

    lax.fori_loop(0, UNITS + 2 * FOLD + 4 * LAG, drain, 0)
    for a in range(maps_here):
        act_copy(2, a).wait_send()
    for there, here in outs:
        there.wait()
        here.wait()


RING = 4


def finish_kernel(kg_ref, pooled_ref, sums_ref, kernel_out, pooled_out, gain_out, shift_out, ring, sem):
    def copy(t):
        slot = lax.rem(t, RING)
        return pltpu.make_async_copy(ring.at[slot], kernel_out.at[t], sem.at[slot])

    def one(t, s):
        @pl.when(t >= RING)
        def _():
            copy(t - RING).wait()

        ring[lax.rem(t, RING)] = kg_ref[t].astype(F32)
        copy(t).start()
        return s

    lax.fori_loop(0, UNITS, one, 0)
    for a in range(pooled_out.shape[0]):
        row = jnp.concatenate([pooled_ref[0, a], pooled_ref[1, a]], 1)
        pooled_out[a, 0] = row[: pooled_out.shape[2]]
    sums = jnp.concatenate([sums_ref[0], sums_ref[1]], 1)
    gain_out[...] = sums[:LAYERS]
    shift_out[...] = sums[LAYERS : 2 * LAYERS]
    for t in range(UNITS - RING, UNITS):
        copy(t).wait()


def solution(mesh):
    chips = mesh.shape["rows"] // 2

    def per_device(
        block_input,
        conv_weights,
        norm_gains,
        norm_shifts,
        map_width,
        map_group,
        pool_index,
        task_mask,
        task_weights,
        task_grads,
    ):
        maps_here, rows_here, columns, channels = block_input.shape
        pooled_columns = pool_index.shape[2]
        height = rows_here * mesh.shape["rows"]
        half = channels // 2
        band = 2 * rows_here
        pixels = maps_here * band * PAD
        actives = chips // 2
        owners = min(actives, 8)
        piece = half // 2 // owners
        rounds = 2 * LAYERS
        slots = 2 * UNITS * (actives - 1) * piece * half + 4 * rounds * chips * 8 * half
        grant = (36 * 1024 + 256) * 1024 + slots
        vmem, dma = pltpu.VMEM, pltpu.SemaphoreType.DMA
        tile = (maps_here, band + 2, PAD, half)
        edge = (2, maps_here, PAD, half)
        whole = pl.BlockSpec(memory_space=pltpu.VMEM)
        outside = pl.BlockSpec(memory_space=pltpu.HBM)
        index_rows = jnp.transpose(pool_index, (0, 2, 1, 3))
        anywhere = pl.BlockSpec(memory_space=pl.ANY)
        pooled, ig, kg, sums = pl.pallas_call(
            functools.partial(block_kernel, chips, height),
            out_shape=(
                jax.ShapeDtypeStruct((2, maps_here, PAD // 2, half), BF16),
                jax.ShapeDtypeStruct((2, maps_here, rows_here, PAD, half), F32),
                jax.ShapeDtypeStruct((UNITS, channels, channels), BF16),
                jax.ShapeDtypeStruct((2, 8, half), F32),
            ),
            in_specs=[whole, anywhere] + [outside] * 8,
            out_specs=[anywhere] * 4,
            scratch_shapes=[
                vmem(norm_gains.shape, F32),
                vmem(norm_shifts.shape, F32),
                pltpu.SMEM(map_width.shape, jnp.int32),
                pltpu.SMEM(map_group.shape, jnp.int32),
                vmem((maps_here, pooled_columns, channels), jnp.int32),
                pltpu.SMEM(task_mask.shape, jnp.int32),
                pltpu.SMEM(task_weights.shape, F32),
                vmem(task_grads.shape, BF16),
                vmem((LAYERS, 3, 3, half, half), BF16),
                vmem((LAYERS, 3, 3, half, half), BF16),
                vmem((2,) + tile, BF16),
                vmem((2,) + tile, BF16),
                vmem((LAYERS, 2, half, maps_here * (band + 2) * PAD), BF16),
                vmem((2, half, pixels), BF16),
                vmem((LAYERS,) + tile, F32),
                vmem(edge, BF16),
                vmem((LAYERS,) + edge, BF16),
                vmem((maps_here, band, PAD, half), F32),
                vmem(edge, BF16),
                vmem((LAYERS,) + edge, BF16),
                vmem((2,) + tile, BF16),
                vmem((2,) + tile, BF16),
                vmem((LAYERS, maps_here, band, PAD, half), BF16),
                vmem((3, 2, maps_here, band, PAD, half), BF16),
                vmem((3, pixels, half), F32),
                vmem((2, 2, maps_here, PAD // 2, half), F32),
                vmem((4, 2, maps_here, PAD // 2, half), F32),
                vmem((half // 128, PAD, 128), F32),
                vmem((2, maps_here, PAD // 2, half), BF16),
                vmem((rounds, chips, 8, half), F32),
                vmem((rounds, PLANE, 8, half), F32),
                vmem((maps_here, PLANE, 8, half), F32),
                vmem((PLANE, 8, half), F32),
                vmem((2, 8, half), F32),
                vmem((8, half), F32),
                vmem((LAYERS, 8, half), F32),
                vmem((LAYERS, 8, half), F32),
                vmem((2, 8, half), F32),
                vmem((1, 8, half), F32),
                vmem((1, 8, half), F32),
                vmem((8, half), F32),
                vmem((2 * TAPS, half, half), BF16),
                vmem((UNITS, half // 2, half), BF16),
                vmem((2 * TAPS, half // 2, half), BF16),
                vmem((UNITS, actives - 1, piece, half), BF16),
                vmem((UNITS, piece, half), BF16),
                dma((8,)),
                dma((LAYERS, 3)),
                dma((6,)),
                dma((6,)),
                dma((3,)),
                dma((3,)),
                dma((rounds, chips)),
                dma((rounds, chips)),
                dma((rounds, PLANE)),
                dma((rounds, PLANE)),
                dma((LAYERS, 2)),
                dma((LAYERS, 2)),
                dma((LAYERS, 2)),
                dma((LAYERS, 2)),
                dma((LAYERS, maps_here)),
                dma((LAYERS, maps_here)),
                dma((LAYERS, maps_here)),
                dma((LAYERS, maps_here)),
                dma((3,)),
                dma((3,)),
                dma((3,)),
                dma((LAYERS,)),
                dma((LAYERS,)),
                dma((LAYERS, 2, maps_here)),
                dma((LAYERS, maps_here)),
                dma((UNITS,)),
                dma((UNITS,)),
                dma((UNITS,)),
                dma((UNITS,)),
                dma((UNITS, owners)),
                dma((UNITS, actives - 1)),
                dma((UNITS, actives)),
                dma((UNITS, owners)),
                dma((UNITS,)),
                dma((UNITS,)),
                dma((UNITS,)),
                dma((UNITS,)),
                dma((UNITS,)),
                dma((UNITS,)),
                dma((UNITS,)),
                dma((UNITS,)),
                dma((UNITS,)),
                dma((UNITS,)),
                dma((UNITS,)),
            ],
            compiler_params=pltpu.CompilerParams(
                collective_id=0,
                has_side_effects=True,
                vmem_limit_bytes=grant,
            ),
        )(
            block_input,
            conv_weights,
            *(
                pltpu.with_memory_space_constraint(v, pltpu.HBM)
                for v in (
                    norm_gains,
                    norm_shifts,
                    map_width,
                    map_group,
                    index_rows,
                    task_mask,
                    task_weights,
                    task_grads,
                )
            ),
        )
        input_grad = jnp.concatenate([ig[0], ig[1]], -1)[:, :, :columns]
        kernel_grads, pooled, gain_grads, shift_grads = pl.pallas_call(
            finish_kernel,
            out_shape=(
                jax.ShapeDtypeStruct(kg.shape, F32),
                jax.ShapeDtypeStruct(pool_index.shape, BF16),
                jax.ShapeDtypeStruct(norm_gains.shape, F32),
                jax.ShapeDtypeStruct(norm_shifts.shape, F32),
            ),
            in_specs=[whole] * 3,
            out_specs=(anywhere, whole, whole, whole),
            scratch_shapes=[vmem((RING,) + kg.shape[1:], F32), dma((RING,))],
            compiler_params=pltpu.CompilerParams(vmem_limit_bytes=24 * 1024 * 1024),
        )(kg, pooled, sums)
        return (
            pooled,
            input_grad,
            kernel_grads.reshape(conv_weights.shape),
            gain_grads,
            shift_grads,
        )

    return jax.shard_map(
        per_device,
        mesh=mesh,
        in_specs=(
            P("maps", "rows", None, None),
            P(),
            P(),
            P(),
            P(),
            P(),
            P("maps", "rows", None, None),
            P("maps", None),
            P(),
            P(None, "maps", "rows", None, None),
        ),
        out_specs=(P("maps", "rows", None, None), P("maps", "rows", None, None), P(), P(), P()),
        check_vma=False,
    )
```

```python
import functools

import jax
import jax.numpy as jnp
from jax import lax
from jax.experimental import pallas as pl
from jax.experimental.pallas import tpu as pltpu
from jax.sharding import PartitionSpec as P

MESH = pl.DeviceIdType.MESH
epsilon = 1e-05
PAD = 64
LAYERS = 3
TAPS = 9
UNITS = LAYERS * TAPS
PLANE = 4
LAG = 4
EARLY = 1
FOLD = 2
F32 = jnp.float32
BF16 = jnp.bfloat16


def each(first, last, body):
    if last - first <= 8:
        for k in range(first, last):
            body(k)
    else:
        lax.fori_loop(first, last, lambda k, s: (body(k), s)[1], 0)


def block_kernel(
    chips,
    height,
    x_ref,
    w_ref,
    gain_hbm,
    shift_hbm,
    width_hbm,
    group_hbm,
    index_hbm,
    tmask_hbm,
    tweight_hbm,
    tgrad_hbm,
    pooled_ref,
    ig_ref,
    kg_ref,
    sums_ref,
    gain_ref,
    shift_ref,
    width_ref,
    group_ref,
    index_ref,
    tmask_ref,
    tweight_ref,
    tgrad_ref,
    wa,
    wb,
    act_own,
    act_oth,
    act_t,
    act_b,
    zbuf,
    zs,
    zh,
    dh,
    dhs,
    dhh,
    dz_own,
    dz_oth,
    dzr,
    dzv,
    prod,
    gsrc,
    gbuf,
    hrow,
    pbuf,
    st1,
    st2,
    coef,
    nall,
    inv_t,
    cnt_t,
    avg_t,
    scl_t,
    mean_t,
    tb_t,
    ta_t,
    sums_own,
    terms,
    r2,
    rf,
    r3,
    fin,
    in_sem,
    w_sem,
    x_s,
    x_r,
    g_s,
    g_r,
    st1_s,
    st1_r,
    st2_s,
    st2_r,
    zh_s,
    zh_r,
    dh_s,
    dh_r,
    act_s,
    act_r,
    dz_s,
    dz_r,
    out_s,
    out_r,
    out_l,
    at_s,
    at_r,
    dzr_s,
    dzr_r,
    r2_s,
    r2_r,
    rf_s,
    rf_r,
    r3_s,
    r3_r,
    az_s,
    az_r,
    af_s,
    af_r,
    ab_s,
    ab_r,
    aa_s,
    aa_r,
    ae_s,
    ae_r,
    ap_s,
    ap_r,
    loc_s,
):
    maps_here = x_ref.shape[0]
    columns = x_ref.shape[2]
    half = x_ref.shape[3] // 2
    tasks = tgrad_ref.shape[0]
    pooled_columns = tgrad_ref.shape[3]
    lanes = half // 128
    tiles = [slice(n * 128, (n + 1) * 128) for n in range(lanes)]
    band = 4
    pixels = maps_here * band * PAD
    actives = chips // 2
    owners = min(actives, 8)
    piece = (half // 2) // owners
    m = lax.axis_index("maps")
    r = lax.axis_index("rows")
    c = lax.rem(r, 2)
    z = lax.div(r, 2)
    other = 1 - c
    first_map = m * maps_here
    x_bit = lax.rem(m, 2)
    y_bit = lax.div(m, 2)
    x_peer = m + 1 - 2 * x_bit
    y_peer = m + 2 - 4 * y_bit
    g_bit = (1 - c) * x_bit + c * y_bit
    h_bit = (1 - c) * y_bit + c * x_bit
    g_peer = (1 - c) * x_peer + c * y_peer
    h_peer = (1 - c) * y_peer + c * x_peer
    pair = lax.div(z, 2)
    turn = lax.rem(pair, 2)
    active_z = 2 * pair + 1 - turn
    is_active = z == active_z
    is_passive = z != active_z
    is_owner = jnp.logical_and(is_active, pair < owners)
    role = jnp.where(is_active, 0, 1)
    up_there = z > 0
    down_there = z < chips - 1
    row8 = lax.broadcasted_iota(jnp.int32, (8, half), 0)
    column = lax.broadcasted_iota(jnp.int32, (PAD, half), 0)

    def remote(src, dst, send, recv, mm, zz, cc):
        return pltpu.make_async_remote_copy(
            src_ref=src,
            dst_ref=dst,
            send_sem=send,
            recv_sem=recv,
            device_id=(mm, zz * 2 + cc),
            device_id_type=MESH,
        )

    def own_half(v):
        return jnp.where(c == 0, v[..., :half], v[..., half:])

    def width_of(a):
        return width_ref[first_map + a]

    own_at = pl.ds(pl.multiple_of(c * half, half), half)
    oth_at = pl.ds(pl.multiple_of(other * half, half), half)

    def weight_copy(l, n):
        dst = (wa, wb, wb)[n]
        k_at, o_at = ((own_at, own_at), (oth_at, own_at), (own_at, oth_at))[n]
        return pltpu.make_async_copy(w_ref.at[l, :, :, k_at, o_at], dst.at[l], w_sem.at[l, n])

    fetches = [
        pltpu.make_async_copy(src, dst, in_sem.at[n])
        for n, (src, dst) in enumerate(
            (
                (width_hbm, width_ref),
                (group_hbm, group_ref),
                (tmask_hbm, tmask_ref),
                (tweight_hbm, tweight_ref),
                (gain_hbm, gain_ref),
                (shift_hbm, shift_ref),
                (index_hbm.at[:, :, 0, :], index_ref),
                (tgrad_hbm, tgrad_ref),
            )
        )
    ]
    for fetch in fetches:
        fetch.start()
    for l in range(LAYERS):
        weight_copy(l, 0).start()
        weight_copy(l, 1).start()

    barrier = pltpu.get_barrier_semaphore()

    def greet(k):
        rr = lax.rem(r + k, 2 * chips)
        pl.semaphore_signal(barrier, inc=1, device_id=(m, rr), device_id_type=MESH)

    each(1, 2 * chips, greet)
    for k in range(1, PLANE):
        for core in (c, other):
            there = (lax.rem(m + k, PLANE), z * 2 + core)
            pl.semaphore_signal(barrier, inc=1, device_id=there, device_id_type=MESH)

    for fetch in fetches:
        fetch.wait()

    mine = pl.ds(1 + 2 * c, 2)
    for a in range(maps_here):
        inside = lax.broadcasted_iota(jnp.int32, (columns, 2 * half), 0) < width_of(a)
        for rr in range(2):
            v = jnp.where(inside, x_ref[a, rr].astype(F32), 0.0).astype(BF16)
            spot = 1 + 2 * c + rr
            act_own[0, a, spot, pl.ds(48, 16), :] = jnp.zeros((16, half), BF16)
            act_oth[0, a, spot, pl.ds(48, 16), :] = jnp.zeros((16, half), BF16)
            act_own[0, a, spot, pl.ds(0, columns), :] = own_half(v)
            act_oth[0, a, spot, pl.ds(0, columns), :] = jnp.where(
                c == 0, v[:, half:], v[:, :half]
            )

    @pl.when(z == 0)
    def _():
        act_own[0, :, 0] = jnp.zeros((maps_here, PAD, half), BF16)
        act_oth[0, :, 0] = jnp.zeros((maps_here, PAD, half), BF16)

    @pl.when(z == chips - 1)
    def _():
        act_own[0, :, 5] = jnp.zeros((maps_here, PAD, half), BF16)
        act_oth[0, :, 5] = jnp.zeros((maps_here, PAD, half), BF16)

    pl.semaphore_wait(barrier, 2 * chips - 1 + 2 * (PLANE - 1))

    x_partner = (
        remote(act_own.at[0, :, mine], act_oth.at[0, :, mine], x_s.at[0], x_r.at[0], m, z, other),
        remote(act_oth.at[0, :, mine], act_own.at[0, :, mine], x_s.at[1], x_r.at[1], m, z, other),
    )
    g_partner = remote(gsrc.at[other], gbuf.at[1 + c], g_s.at[0], g_r.at[0], m, z, other)

    def x_halo(n, src_row, dst_row, zz):
        cc = (c, other)[n % 2]
        low = dst_row == band + 1
        if n >= 2:
            src, dst = gsrc.at[cc], gbuf.at[3 if low else 0]
            return remote(src, dst, g_s.at[n - 1], g_r.at[1 if low else 2], m, zz, cc)
        src, dst = (act_own, act_oth)[n].at[0, :, src_row], act_own.at[0, :, dst_row]
        return remote(src, dst, x_s.at[2 + n], x_r.at[2 if low else 3], m, zz, cc)

    def x_pass(row):
        n = 4 if row == 0 else 5
        src, dst = act_own.at[0, :, row], act_oth.at[0, :, row]
        return remote(src, dst, x_s.at[n], x_r.at[n], m, z, other)

    for copy in x_partner:
        copy.start()

    @pl.when(jnp.logical_and(c == 0, up_there))
    def _():
        for n in range(2):
            x_halo(n, 1, 5, z - 1).start()

    @pl.when(jnp.logical_and(c == 1, down_there))
    def _():
        for n in range(2):
            x_halo(n, 4, 0, z + 1).start()

    gsrc[...] = jnp.zeros(gsrc.shape, F32)
    for a in range(maps_here):
        total = None
        for t in range(tasks):
            scale = tweight_ref[t] * tmask_ref[a, t].astype(F32)
            term = tgrad_ref[t, a, 0].astype(F32) * scale
            total = term if total is None else total + term
        position = index_ref[a].astype(F32)
        for h in range(2):
            gsrc[h, 0, a, pl.ds(0, pooled_columns), :] = total[:, h * half : (h + 1) * half]
            gsrc[h, 1, a, pl.ds(0, pooled_columns), :] = position[:, h * half : (h + 1) * half]
    gbuf[1 + c] = gsrc[c]

    for mm in range(PLANE):
        sizes = jnp.zeros((8, half), F32)
        for b in range(maps_here):
            sizes = jnp.where(
                row8 == b, (width_ref[mm * maps_here + b] * height).astype(F32), sizes
            )
        nall[mm] = sizes
    inside_sizes = jnp.zeros((8, half), F32)
    for b in range(maps_here):
        inside_sizes = jnp.where(row8 == b, (width_of(b) * band).astype(F32), inside_sizes)
    inv_t[0] = inside_sizes
    inv_t[1] = jnp.where(row8 < maps_here, 1.0 / jnp.maximum(inside_sizes, 1.0), 0.0)
    counts = jnp.ones((8, half), F32)
    for a in range(maps_here):
        total = jnp.zeros((1, half), F32)
        for mm in range(PLANE):
            same = jnp.zeros((8, half), F32)
            for b in range(maps_here):
                alike = group_ref[first_map + a] == group_ref[mm * maps_here + b]
                same = jnp.where(row8 == b, jnp.where(alike, 1.0, 0.0), same)
            coef[a, mm] = same
            total = total + jnp.sum(same * nall[mm], 0, keepdims=True)
        counts = jnp.where(row8 == a, total, counts)
    cnt_t[...] = counts

    def z_copy(e, k):
        zz = lax.rem(z + k, chips)
        return remote(st1.at[e, z], st1.at[e, z], st1_s.at[e, k], st1_r.at[e, z], m, zz, c)

    def z_arrival(e, k):
        zz = lax.rem(z + k, chips)
        return remote(st1.at[e, zz], st1.at[e, zz], st1_s.at[e, k], st1_r.at[e, zz], m, zz, c)

    def m_copy(e, k):
        mm = lax.rem(m + k, PLANE)
        return remote(st2.at[e, m], st2.at[e, m], st2_s.at[e, k], st2_r.at[e, m], mm, z, c)

    def m_arrival(e, k):
        mm = lax.rem(m + k, PLANE)
        return remote(st2.at[e, mm], st2.at[e, mm], st2_s.at[e, k], st2_r.at[e, mm], mm, z, c)

    def send_z(e, tile):
        st1[e, z] = tile
        each(1, chips, lambda k: z_copy(e, k).start())

    def wait_z(e):
        each(1, chips, lambda k: z_arrival(e, k).wait_recv())

    def send_m(e, tile):
        st2[e, m] = tile
        each(1, PLANE, lambda k: m_copy(e, k).start())

    def wait_m(e):
        each(1, PLANE, lambda k: m_arrival(e, k).wait_recv())

    def products(source, l, taps, kernel, transposed, fresh):
        starts = [2 - i if transposed else i for i in taps]
        lhs = jnp.concatenate(
            [source[lax.rem(l, 2), :, s : s + band].reshape(pixels, half) for s in starts], 1
        )
        for j in range(3):
            rhs = jnp.concatenate([kernel[l, i, j] for i in taps], 1 if transposed else 0)
            got = lax.dot_general(
                lhs,
                rhs,
                (((1,), (1 if transposed else 0,)), ((), ())),
                preferred_element_type=F32,
            )
            if fresh:
                prod[j] = got
            else:
                prod[j] = prod[j] + got

    def shifted(a, rr, before, behind, n):
        rows = pl.ds(pl.multiple_of((a * band + rr) * PAD, PAD), PAD)
        return (
            prod[1, rows, n]
            + pltpu.roll(prod[before, rows, n], 1, 0)
            + pltpu.roll(prod[behind, rows, n], PAD - 1, 0)
        )

    def row_of(table, l, a):
        return table[l, pl.ds(a, 1), :]

    def gain_of(l):
        return own_half(gain_ref[pl.ds(l, 1), :])

    def shift_of(l):
        return own_half(shift_ref[pl.ds(l, 1), :])

    def limit(a, rr):
        w = width_of(a)
        if rr == 0:
            return jnp.where(up_there, w, 0)
        if rr == band + 1:
            return jnp.where(down_there, w, 0)
        return w

    def z_halo(l, way):
        there = z - 1 + 2 * way
        return remote(zs.at[way], zh.at[l, 1 - way], zh_s.at[l, way], zh_r.at[l, way], m, there, c)

    def dh_halo(l, way):
        there = z - 1 + 2 * way
        return remote(dhs.at[way], dhh.at[l, 1 - way], dh_s.at[l, way], dh_r.at[l, way], m, there, c)

    def start_halo(halo, l):
        @pl.when(up_there)
        def _():
            halo(l, 0).start()

        @pl.when(down_there)
        def _():
            halo(l, 1).start()

    def wait_halo(halo, l):
        @pl.when(up_there)
        def _():
            halo(l, 1).wait_recv()
            halo(l, 0).wait_send()

        @pl.when(down_there)
        def _():
            halo(l, 0).wait_recv()
            halo(l, 1).wait_send()

    def act_copy(l, a):
        slot = lax.rem(l, 2)
        src, dst = act_own.at[slot, a], act_oth.at[slot, a]
        return remote(src, dst, act_s.at[l, a], act_r.at[l, a], m, z, other)

    def at_copy(l):
        return remote(act_t.at[l, 0], act_t.at[l, 1], at_s.at[l], at_r.at[l], g_peer, z, c)

    def dzr_copy(l, a, way):
        src, dst = dz_own.at[lax.rem(l, 2), a, pl.ds(1, band)], dzr.at[l, a]
        peer = (x_peer, y_peer)[way]
        return remote(src, dst, dzr_s.at[l, way, a], dzr_r.at[l, a], peer, z, way)

    def if_wanted(way, body):
        @pl.when((x_bit, y_bit)[way] + c == 1)
        def _():
            body()

    def dz_copy(l, a):
        slot = lax.rem(l, 2)
        src, dst = dz_own.at[slot, a], dz_oth.at[slot, a]
        return remote(src, dst, dz_s.at[l, a], dz_r.at[l, a], m, z, other)

    def send_gradients():
        g_partner.start()

        @pl.when(jnp.logical_and(c == 0, up_there))
        def _():
            for n in range(2, 4):
                x_halo(n, 1, 5, z - 1).start()

        @pl.when(jnp.logical_and(c == 1, down_there))
        def _():
            for n in range(2, 4):
                x_halo(n, 4, 0, z + 1).start()

    def if_there(way, body):
        @pl.when((up_there, down_there)[way])
        def _():
            body()

    def wait_x_halo(n):
        if_there(0, lambda: x_halo(n, 4, 0, z - 1).wait_recv())
        if_there(1, lambda: x_halo(n, 1, 5, z + 1).wait_recv())

    def each_x_pass(act):
        if_there(0, lambda: act(x_pass(0)))
        if_there(1, lambda: act(x_pass(band + 1)))

    def sent_x_halo(first, last):
        @pl.when(jnp.logical_and(c == 0, up_there))
        def _():
            for n in range(first, last):
                x_halo(n, 1, 5, z - 1).wait_send()

        @pl.when(jnp.logical_and(c == 1, down_there))
        def _():
            for n in range(first, last):
                x_halo(n, 4, 0, z + 1).wait_send()

    def unpool(a, s):
        for rr in range(band + 2):
            slot, lower = (rr + 1) // 2, (rr + 1) % 2
            g = gbuf[slot, 0, a]
            position = gbuf[slot, 1, a]
            for b in range(2):
                v = jnp.where(position == float(2 * lower + b), g, 0.0)
                for n in range(lanes):
                    hrow[n, pl.ds(b, PAD // 2, stride=2), :] = v[:, n * 128 : (n + 1) * 128]
            v = jnp.concatenate([hrow[n] for n in range(lanes)], 1)
            if rr in (0, band + 1):
                dhh[LAYERS - 1, rr // (band + 1), a] = v.astype(BF16)
            else:
                dh[a, rr - 1] = v
        return s

    def forward(l, first):
        weight_copy(l, 0).wait()
        weight_copy(l, 1).wait()
        if first:
            for copy in x_partner:
                copy.wait_recv()
            products(act_own, l, (1,), wa, False, True)
            products(act_oth, l, (1,), wb, False, False)
            wait_x_halo(0)
            each_x_pass(lambda copy: copy.start())
            products(act_own, l, (0, 2), wa, False, False)
            each_x_pass(lambda copy: copy.wait_recv())
            products(act_oth, l, (0, 2), wb, False, False)
        else:
            products(act_own, l, (0, 1, 2), wa, False, True)
            for a in range(maps_here):
                act_copy(l, a).wait_recv()
            products(act_oth, l, (0, 1, 2), wb, False, False)
        weight_copy(l, 2).start()

        def collect(a, tile):
            inside = column[:, :128] < width_of(a)
            pixels_inside = (width_of(a) * band).astype(F32)
            totals, squares = [], []
            for n in tiles:
                total = jnp.zeros((PAD, 128), F32)
                for rr in range(band):
                    v = shifted(a, rr, 0, 2, n)
                    zbuf[l, a, 1 + rr, :, n] = v
                    total = total + jnp.where(inside, v, 0.0)
                total = jnp.sum(total, 0, keepdims=True)
                mean = total / pixels_inside
                square = jnp.zeros((PAD, 128), F32)
                for rr in range(band):
                    v = jnp.where(inside, zbuf[l, a, 1 + rr, :, n] - mean, 0.0)
                    square = square + v * v
                    if rr in (0, band - 1):
                        zs[rr // (band - 1), a, :, n] = v.astype(BF16)
                totals.append(total)
                squares.append(jnp.sum(square, 0, keepdims=True))
            tile = jnp.where(row8 == a, jnp.concatenate(totals, 1), tile)
            return jnp.where(row8 == a + maps_here, jnp.concatenate(squares, 1), tile)

        tile = lax.fori_loop(0, maps_here, collect, jnp.zeros((8, half), F32))
        send_z(l, tile)
        start_halo(z_halo, l)
        act_t[l, 0] = act_own[lax.rem(l, 2)].reshape(maps_here * (band + 2) * PAD, half).T
        wait_z(l)
        sizes, inverse = inv_t[0], inv_t[1]
        mean_t[0] = st1[l, jnp.maximum(z - 1, 0)] * inverse
        mean_t[1] = st1[l, jnp.minimum(z + 1, chips - 1)] * inverse
        total = st1[l, 0]
        for zz in range(1, chips):
            total = total + st1[l, zz]
        mean = total * inverse * (1.0 / chips)
        square = jnp.zeros((8, half), F32)
        for zz in range(chips):
            v = st1[l, zz]
            gap = v * inverse - mean
            square = square + pltpu.roll(v, 8 - maps_here, 0) + sizes * gap * gap
        tile = jnp.where(row8 < maps_here, mean, pltpu.roll(square, maps_here, 0))
        send_m(l, jnp.where(row8 < 2 * maps_here, tile, 0.0))
        if not first:

            @pl.when(l == LAYERS - 1)
            def _():
                g_partner.wait_recv()
                wait_x_halo(2)
                lax.fori_loop(0, maps_here, unpool, 0)

        wait_m(l)
        at_copy(l).start()
        if first:
            send_gradients()
        averages = jnp.zeros((8, half), F32)
        scalings = jnp.zeros((8, half), F32)
        for a in range(maps_here):
            count = cnt_t[a : a + 1, :]
            average = jnp.zeros((8, half), F32)
            for mm in range(PLANE):
                average = average + coef[a, mm] * nall[mm] * st2[l, mm]
            average = jnp.sum(average, 0, keepdims=True) / count
            variance = jnp.zeros((8, half), F32)
            for mm in range(PLANE):
                v = st2[l, mm]
                gap = v - average
                variance = variance + coef[a, mm] * (
                    pltpu.roll(v, 8 - maps_here, 0) + nall[mm] * gap * gap
                )
            variance = jnp.sum(variance, 0, keepdims=True) / count
            averages = jnp.where(row8 == a, average, averages)
            scalings = jnp.where(row8 == a, lax.rsqrt(variance + epsilon), scalings)
        avg_t[l] = averages
        scl_t[l] = scalings
        wait_halo(z_halo, l)

        def activate(a, s):
            gain, shift = gain_of(l), shift_of(l)
            for n in tiles:
                average = row_of(avg_t, l, a)[:, n]
                factor = row_of(scl_t, l, a)[:, n] * gain[:, n]
                for rr in range(band + 2):
                    if rr in (0, band + 1):
                        way = rr // (band + 1)
                        v = zh[l, way, a, :, n].astype(F32) + row_of(mean_t, way, a)[:, n]
                        zbuf[l, a, rr, :, n] = v
                    else:
                        v = zbuf[l, a, rr, :, n]
                    y = (v - average) * factor + shift[:, n]
                    h = jnp.where(column[:, n] < limit(a, rr), y * jax.nn.sigmoid(y), 0.0)
                    act_own[lax.rem(l + 1, 2), a, rr, :, n] = h.astype(BF16)

            @pl.when(l < LAYERS - 1)
            def _():
                act_copy(l + 1, a).start()

            return s

        if first:
            for copy in x_partner:
                copy.wait_send()
            sent_x_halo(0, 2)
            each_x_pass(lambda copy: copy.wait_send())
        else:

            @pl.when(l == 2)
            def _():
                for a in range(maps_here):
                    act_copy(1, a).wait_send()

        lax.fori_loop(0, maps_here, activate, 0)

    forward(0, True)
    lax.fori_loop(1, LAYERS, lambda l, s: (forward(l, False), s)[1], 0)


    def pool():
        def one(a, s):
            for pr in range(2):
                total = jnp.zeros((PAD // 2, half), F32)
                position = gbuf[1 + pr, 1, a]
                for lower in range(2):
                    v = act_own[LAYERS % 2, a, 1 + 2 * pr + lower].astype(F32)
                    for n in range(lanes):
                        hrow[n] = v[:, n * 128 : (n + 1) * 128]
                    for b in range(2):
                        v = jnp.concatenate(
                            [hrow[n, pl.ds(b, PAD // 2, stride=2), :] for n in range(lanes)], 1
                        )
                        total = total + jnp.where(position == float(2 * lower + b), v, 0.0)
                pbuf[pr, a] = total.astype(BF16)
            return s

        lax.fori_loop(0, maps_here, one, 0)

    def second_rows(bit):
        return pl.ds(pl.multiple_of(bit * (half // 2), half // 2), half // 2)

    def piece_rows(p):
        return pl.ds(pl.multiple_of(p * piece, piece), piece)

    def term_slot(q):
        return lax.rem(q, 2 * TAPS)

    def c2(q):
        src = terms.at[term_slot(q), second_rows(1 - h_bit)]
        return remote(src, r2.at[q], r2_s.at[q], r2_r.at[q], h_peer, z, c)

    def z_of(n):
        return 2 * n + 1 - lax.rem(n, 2)

    def cf(q):
        passive_z = 2 * pair + turn
        there = active_z + passive_z - z
        return remote(r2.at[q], rf.at[term_slot(q)], rf_s.at[q], rf_r.at[q], m, there, c)

    def c3(q, p):
        slot = lax.rem(pair - p + actives - 1, actives)
        return remote(
            r2.at[q, piece_rows(p)], r3.at[q, slot], r3_s.at[q, p], r3_r.at[q, slot], m, z_of(p), c
        )

    def others(first, body, limit):
        def one(k):
            n = lax.rem(pair + k, actives)

            @pl.when(n < limit)
            def _():
                body(n)

        each(first, actives, one)

    def unit_of(q):
        k = lax.div(q, TAPS)
        return (LAYERS - 1 - k) * TAPS + (q - k * TAPS)

    def region(q, start, size, lane, lanes):
        start = pl.multiple_of(c * half + start, piece)
        lane = pl.multiple_of(lane, half)
        return kg_ref.at[unit_of(q), pl.ds(start, size), pl.ds(lane, lanes)]

    def cz(q, p, n):
        part = region(q, h_bit * (half // 2) + p * piece, piece, g_bit * half, half)
        return remote(fin.at[q], part, az_s.at[q, n], az_r.at[q, p], m, z_of(n), c)

    def cl(q):
        part = region(q, h_bit * (half // 2) + pair * piece, piece, g_bit * half, half)
        return pltpu.make_async_copy(fin.at[q], part, loc_s.at[q])

    def cu(q):
        passive_z = 2 * pair + turn
        there = active_z + passive_z - z
        part = region(q, h_bit * (half // 2), half // 2, g_bit * half, half)
        return remote(part, part, af_s.at[q], af_r.at[q], m, there, c)

    def cb(q):
        part = region(q, h_bit * (half // 2), half // 2, g_bit * half, half)
        return remote(part, part, ab_s.at[q], ab_r.at[q], h_peer, z, c)

    def ca(q):
        part = region(q, 0, half, g_bit * half, half)
        return remote(part, part, aa_s.at[q], aa_r.at[q], g_peer, z, c)

    def plan(q):
        k = lax.rem(q, 5)
        both = jnp.logical_or(lax.rem(k, 2) == 0, q >= UNITS - 5)
        mine = jnp.logical_or(both, lax.div(k, 2) == role)
        return mine, jnp.logical_and(mine, jnp.logical_not(both)), jnp.logical_not(mine)

    def ce(q):
        passive_z = 2 * pair + turn
        there = active_z + passive_z - z
        part = region(q, 0, half, (1 - g_bit) * half, half)
        return remote(part, part, ae_s.at[q], ae_r.at[q], m, there, c)

    def cp_part(q, start, size, lane, lanes):
        part = region(q, start, size, lane, lanes)
        return remote(part, part, ap_s.at[q], ap_r.at[q], m, z, other)

    def cp(q):
        return cp_part(q, 0, half, 0, 2 * half)

    def cp_rows(q, bit):
        return cp_part(q, bit * (half // 2), half // 2, g_bit * half, half)

    def cp_lanes(q):
        return cp_part(q, 0, half, (1 - g_bit) * half, half)

    def ready_terms(l):
        at_copy(l).wait_recv()
        for chip in range(2):
            for a in range(maps_here):
                first = a * (band + 2) * PAD
                rows = act_t[l, chip, :, first : first + (band + 2) * PAD]
                act_b[chip, :, a * band * PAD : (a + 1) * band * PAD] = rows[:, PAD : PAD + band * PAD]
        slot = lax.rem(l, 2)

        def variants(a, s):
            dzr_copy(l, a, 0).wait_recv()
            for chip in range(2):
                for rr in range(band):
                    for n in tiles:
                        if chip == 0:
                            mine, theirs = dz_own[slot, a, 1 + rr, :, n], dz_oth[slot, a, 1 + rr, :, n]
                            v = jnp.where(g_bit == c, mine, theirs)
                        else:
                            v = dzr[l, a, rr, :, n]
                        dzv[1, chip, a, rr, :, n] = v
                        v = v.astype(F32)
                        dzv[0, chip, a, rr, :, n] = pltpu.roll(v, PAD - 1, 0).astype(BF16)
                        dzv[2, chip, a, rr, :, n] = pltpu.roll(v, 1, 0).astype(BF16)
            return s

        lax.fori_loop(0, maps_here, variants, 0)

    def tap_terms(l, i, j):
        if i == 1:
            lhs = [act_b[0], act_b[1]]
        else:
            lhs = []
            for chip in range(2):
                for a in range(maps_here):
                    first = (a * (band + 2) + i) * PAD
                    lhs.append(act_t[l, chip, :, first : first + band * PAD])
        rhs = dzv[j].reshape(2 * pixels, half)
        q = (LAYERS - 1 - l) * TAPS + 3 * i + j
        got = jnp.dot(jnp.concatenate(lhs, 1), rhs, preferred_element_type=F32)
        terms[term_slot(q)] = got.astype(BF16)

    def weight_terms(l, i):
        lax.fori_loop(0, 3, lambda j, s: (tap_terms(l, i, j), s)[1], 0)

    def stage_second(q):
        c2(q).wait()
        kept = terms[term_slot(q), second_rows(h_bit)].astype(F32)
        r2[q] = (r2[q].astype(F32) + kept).astype(BF16)

        @pl.when(is_passive)
        def _():
            cf(q).start()

    def stage_fold(q):
        @pl.when(is_active)
        def _():
            cf(q).wait_recv()
            r2[q] = (r2[q].astype(F32) + rf[term_slot(q)].astype(F32)).astype(BF16)
            others(1, lambda n: c3(q, n).start(), owners)

    def stage_sum(q):
        @pl.when(is_owner)
        def _():
            for k in range(actives - 1):
                remote(
                    r3.at[q, k], r3.at[q, k], r3_s.at[q, 0], r3_r.at[q, k], m, z, c
                ).wait_recv()
            total = r2[q, piece_rows(pair)].astype(F32)
            for k in range(actives - 1):
                total = total + r3[q, k].astype(F32)
            fin[q] = total.astype(BF16)
            others(1, lambda n: cz(q, pair, n).start(), actives)
            cl(q).start()

    def stage_back(q):
        @pl.when(is_active)
        def _():
            others(1, lambda n: cz(q, n, n).wait_recv(), owners)

        @pl.when(is_owner)
        def _():
            cl(q).wait()

        @pl.when(is_active)
        def _():
            cu(q).start()

        @pl.when(is_passive)
        def _():
            cu(q).wait_recv()

        cb(q).start()
        cp_rows(q, h_bit).start()

    def stage_first(q):
        cb(q).wait_recv()
        mine, _, _ = plan(q)

        @pl.when(mine)
        def _():
            ca(q).start()

        cp_rows(q, 1 - h_bit).start()

        @pl.when(is_active)
        def _():
            others(1, lambda n: c3(q, n).wait_send(), owners)

        @pl.when(is_passive)
        def _():
            cf(q).wait_send()

    def stage_chip(q):
        mine, for_both, _ = plan(q)

        @pl.when(mine)
        def _():
            ca(q).wait_recv()

        @pl.when(for_both)
        def _():
            ce(q).start()

        @pl.when(mine)
        def _():
            cp_lanes(q).start()

        @pl.when(is_owner)
        def _():
            others(1, lambda n: cz(q, pair, n).wait_send(), actives)

        @pl.when(is_active)
        def _():
            cu(q).wait_send()

    def stage_late(q):
        _, _, not_mine = plan(q)

        @pl.when(not_mine)
        def _():
            ce(q).wait_recv()
            cp_lanes(q).start()

    def stage_done(q):
        mine, for_both, _ = plan(q)
        cb(q).wait_send()

        @pl.when(mine)
        def _():
            ca(q).wait_send()

        @pl.when(for_both)
        def _():
            ce(q).wait_send()

        cp(q).wait()

    def run(stage, first, last):
        lax.fori_loop(first, last, lambda q, s: (stage(q), s)[1], 0)

    def sent_dz(l):
        for a in range(maps_here):
            dz_copy(l, a).wait_send()
            for way in range(2):
                if_wanted(way, dzr_copy(l, a, way).wait_send)

    def backward(k, carry):
        l = LAYERS - 1 - k
        gain, shift = gain_of(l), shift_of(l)

        def gradient(a, rr, n):
            zhat = (zbuf[l, a, rr, :, n] - row_of(avg_t, l, a)[:, n]) * row_of(scl_t, l, a)[:, n]
            y = zhat * gain[:, n] + shift[:, n]
            s = jax.nn.sigmoid(y)
            if rr in (0, band + 1):
                upstream = dhh[l, rr // (band + 1), a, :, n].astype(F32)
            else:
                upstream = dh[a, rr - 1, :, n]
            dy = upstream * (s * (1.0 + y * (1.0 - s)))
            dy = jnp.where(column[:, n] < limit(a, rr), dy, 0.0)
            return dy, zhat

        def collect(a, tile):
            plains, crosses = [], []
            for n in tiles:
                plain = jnp.zeros((PAD, 128), F32)
                crossed = jnp.zeros((PAD, 128), F32)
                for rr in range(1, band + 1):
                    dy, zhat = gradient(a, rr, n)
                    dh[a, rr - 1, :, n] = dy
                    plain = plain + dy
                    crossed = crossed + dy * zhat
                plains.append(jnp.sum(plain, 0, keepdims=True))
                crosses.append(jnp.sum(crossed, 0, keepdims=True))
            tile = jnp.where(row8 == a, jnp.concatenate(plains, 1), tile)
            return jnp.where(row8 == a + maps_here, jnp.concatenate(crosses, 1), tile)

        e = LAYERS + l
        tile = lax.fori_loop(0, maps_here, collect, jnp.zeros((8, half), F32))
        send_z(e, tile)

        @pl.when(k == LAYERS - 1)
        def _():
            run(stage_second, 0, TAPS)

        @pl.when(k > 0)
        def _():
            ready_terms(l + 1)
            weight_terms(l + 1, 0)
            first = (LAYERS - 2 - l) * TAPS
            run(lambda q: c2(q).start(), first, first + 3)

        wait_z(e)
        total = st1[e, 0]
        for zz in range(1, chips):
            total = total + st1[e, zz]
        send_m(e, total)

        @pl.when(k > 0)
        def _():
            first = (LAYERS - 2 - l) * TAPS
            weight_terms(l + 1, 1)
            run(lambda q: c2(q).start(), first + 3, first + 6)
            weight_terms(l + 1, 2)
            run(lambda q: c2(q).start(), first + 6, first + 9)
            wait_halo(dh_halo, l)

        @pl.when(k == 0)
        def _():
            pool()

        wait_m(e)
        total = st2[e, 0]
        for mm in range(1, PLANE):
            total = total + st2[e, mm]
        sums_own[pl.ds(l, 1), :] = jnp.sum(
            jnp.where(row8 >= maps_here, total, 0.0), 0, keepdims=True
        )
        sums_own[pl.ds(LAYERS + l, 1), :] = jnp.sum(
            jnp.where(row8 < maps_here, total, 0.0), 0, keepdims=True
        )
        plains = jnp.zeros((8, half), F32)
        crosses = jnp.zeros((8, half), F32)
        for a in range(maps_here):
            plain = jnp.zeros((8, half), F32)
            crossed = jnp.zeros((8, half), F32)
            for mm in range(PLANE):
                v = st2[e, mm]
                plain = plain + coef[a, mm] * v
                crossed = crossed + coef[a, mm] * pltpu.roll(v, 8 - maps_here, 0)
            count = cnt_t[a : a + 1, :]
            plain = gain * (jnp.sum(plain, 0, keepdims=True) / count)
            crossed = gain * (jnp.sum(crossed, 0, keepdims=True) / count)
            plains = jnp.where(row8 == a, plain, plains)
            crosses = jnp.where(row8 == a, crossed, crosses)
        tb_t[0] = plains
        ta_t[0] = crosses

        def settle(a, s):
            for n in tiles:
                average, scaling = row_of(avg_t, l, a)[:, n], row_of(scl_t, l, a)[:, n]
                plain, crossed = row_of(tb_t, 0, a)[:, n], row_of(ta_t, 0, a)[:, n]
                for rr in range(band + 2):
                    if rr in (0, band + 1):
                        dy, zhat = gradient(a, rr, n)
                    else:
                        dy = dh[a, rr - 1, :, n]
                        zhat = (zbuf[l, a, rr, :, n] - average) * scaling
                    v = scaling * (dy * gain[:, n] - plain - zhat * crossed)
                    v = jnp.where(column[:, n] < limit(a, rr), v, 0.0)
                    dz_own[lax.rem(l, 2), a, rr, :, n] = v.astype(BF16)
            dz_copy(l, a).start()
            for way in range(2):
                if_wanted(way, dzr_copy(l, a, way).start)
            return s

        @pl.when(k == 2)
        def _():
            sent_dz(LAYERS - 1)

        lax.fori_loop(0, maps_here, settle, 0)
        products(dz_own, l, (0, 1, 2), wa, True, True)
        weight_copy(l, 2).wait()
        for a in range(maps_here):
            dz_copy(l, a).wait_recv()
        products(dz_oth, l, (0, 1, 2), wb, True, False)

        def gather(a, s):
            for n in tiles:
                for rr in range(band):
                    v = shifted(a, rr, 2, 0, n)
                    dh[a, rr, :, n] = v
                    if rr in (0, band - 1):
                        dhs[rr // (band - 1), a, :, n] = v.astype(BF16)
            return s

        lax.fori_loop(0, maps_here, gather, 0)

        @pl.when(l > 0)
        def _():
            start_halo(dh_halo, l - 1)

        return carry

    lax.fori_loop(0, LAYERS, backward, 0)
    def input_rows(a, s):
        for rr in range(band):
            dh[a, rr] = jnp.where(column < width_of(a), dh[a, rr], 0.0)
        return s

    lax.fori_loop(0, maps_here, input_rows, 0)

    outs = (
        (
            remote(dh.at[:, pl.ds(2 * other, 2)], ig_ref.at[c], out_s.at[0], out_r.at[0], m, z, other),
            pltpu.make_async_copy(dh.at[:, pl.ds(2 * c, 2)], ig_ref.at[c], out_l.at[0]),
        ),
        (
            remote(pbuf.at[other], pooled_ref.at[c], out_s.at[1], out_r.at[1], m, z, other),
            pltpu.make_async_copy(pbuf.at[c], pooled_ref.at[c], out_l.at[1]),
        ),
        (
            remote(sums_own, sums_ref.at[c], out_s.at[2], out_r.at[2], m, z, other),
            pltpu.make_async_copy(sums_own, sums_ref.at[c], out_l.at[2]),
        ),
    )
    for there, here in outs:
        there.start()
        here.start()

    g_partner.wait_send()
    sent_x_halo(2, 4)

    def sent(e, carry):
        each(1, chips, lambda k: z_copy(e, k).wait_send())
        each(1, PLANE, lambda k: m_copy(e, k).wait_send())
        return carry

    lax.fori_loop(0, 2 * LAYERS, sent, 0)
    for l in range(LAYERS):
        at_copy(l).wait_send()
    for l in range(LAYERS - 1):
        sent_dz(l)

    def drain(s, carry):
        @pl.when(s == EARLY)
        def _():
            ready_terms(0)

        for i in range(3):
            j = s - EARLY - 3 * i

            @pl.when(jnp.logical_and(j >= 0, j < 3))
            def _(i=i, j=j):
                tap_terms(0, i, j)
                c2(2 * TAPS + 3 * i + j).start()

        for stage, first, lag in (
            (stage_done, 0, 2 * FOLD + 4 * LAG),
            (stage_late, 0, 2 * FOLD + 3 * LAG),
            (stage_chip, 0, 2 * FOLD + 2 * LAG),
            (stage_first, 0, 2 * FOLD + LAG),
            (stage_back, 0, 2 * FOLD),
            (stage_sum, 0, FOLD),
            (stage_fold, 0, 0),
            (stage_second, TAPS, 0),
        ):
            q = first + s - lag

            @pl.when(jnp.logical_and(q >= first, q < UNITS))
            def _(stage=stage, q=q):
                stage(q)

        return carry

    lax.fori_loop(0, UNITS + 2 * FOLD + 4 * LAG, drain, 0)
    for a in range(maps_here):
        act_copy(2, a).wait_send()
    for there, here in outs:
        there.wait()
        here.wait()


RING = 4


def finish_kernel(kg_ref, pooled_ref, sums_ref, kernel_out, pooled_out, gain_out, shift_out, ring, sem):
    def copy(t):
        slot = lax.rem(t, RING)
        return pltpu.make_async_copy(ring.at[slot], kernel_out.at[t], sem.at[slot])

    def one(t, s):
        @pl.when(t >= RING)
        def _():
            copy(t - RING).wait()

        ring[lax.rem(t, RING)] = kg_ref[t].astype(F32)
        copy(t).start()
        return s

    lax.fori_loop(0, UNITS, one, 0)
    for a in range(pooled_out.shape[0]):
        row = jnp.concatenate([pooled_ref[0, a], pooled_ref[1, a]], 1)
        pooled_out[a, 0] = row[: pooled_out.shape[2]]
    sums = jnp.concatenate([sums_ref[0], sums_ref[1]], 1)
    gain_out[...] = sums[:LAYERS]
    shift_out[...] = sums[LAYERS : 2 * LAYERS]
    for t in range(UNITS - RING, UNITS):
        copy(t).wait()


def solution(mesh):
    chips = mesh.shape["rows"] // 2

    def per_device(
        block_input,
        conv_weights,
        norm_gains,
        norm_shifts,
        map_width,
        map_group,
        pool_index,
        task_mask,
        task_weights,
        task_grads,
    ):
        maps_here, rows_here, columns, channels = block_input.shape
        pooled_columns = pool_index.shape[2]
        height = rows_here * mesh.shape["rows"]
        half = channels // 2
        band = 2 * rows_here
        pixels = maps_here * band * PAD
        actives = chips // 2
        owners = min(actives, 8)
        piece = half // 2 // owners
        rounds = 2 * LAYERS
        slots = 2 * UNITS * (actives - 1) * piece * half + 4 * rounds * chips * 8 * half
        grant = (36 * 1024 + 256) * 1024 + slots
        vmem, dma = pltpu.VMEM, pltpu.SemaphoreType.DMA
        tile = (maps_here, band + 2, PAD, half)
        edge = (2, maps_here, PAD, half)
        whole = pl.BlockSpec(memory_space=pltpu.VMEM)
        outside = pl.BlockSpec(memory_space=pltpu.HBM)
        index_rows = jnp.transpose(pool_index, (0, 2, 1, 3))
        anywhere = pl.BlockSpec(memory_space=pl.ANY)
        pooled, ig, kg, sums = pl.pallas_call(
            functools.partial(block_kernel, chips, height),
            out_shape=(
                jax.ShapeDtypeStruct((2, maps_here, PAD // 2, half), BF16),
                jax.ShapeDtypeStruct((2, maps_here, rows_here, PAD, half), F32),
                jax.ShapeDtypeStruct((UNITS, channels, channels), BF16),
                jax.ShapeDtypeStruct((2, 8, half), F32),
            ),
            in_specs=[whole, anywhere] + [outside] * 8,
            out_specs=[anywhere] * 4,
            scratch_shapes=[
                vmem(norm_gains.shape, F32),
                vmem(norm_shifts.shape, F32),
                pltpu.SMEM(map_width.shape, jnp.int32),
                pltpu.SMEM(map_group.shape, jnp.int32),
                vmem((maps_here, pooled_columns, channels), jnp.int32),
                pltpu.SMEM(task_mask.shape, jnp.int32),
                pltpu.SMEM(task_weights.shape, F32),
                vmem(task_grads.shape, BF16),
                vmem((LAYERS, 3, 3, half, half), BF16),
                vmem((LAYERS, 3, 3, half, half), BF16),
                vmem((2,) + tile, BF16),
                vmem((2,) + tile, BF16),
                vmem((LAYERS, 2, half, maps_here * (band + 2) * PAD), BF16),
                vmem((2, half, pixels), BF16),
                vmem((LAYERS,) + tile, F32),
                vmem(edge, BF16),
                vmem((LAYERS,) + edge, BF16),
                vmem((maps_here, band, PAD, half), F32),
                vmem(edge, BF16),
                vmem((LAYERS,) + edge, BF16),
                vmem((2,) + tile, BF16),
                vmem((2,) + tile, BF16),
                vmem((LAYERS, maps_here, band, PAD, half), BF16),
                vmem((3, 2, maps_here, band, PAD, half), BF16),
                vmem((3, pixels, half), F32),
                vmem((2, 2, maps_here, PAD // 2, half), F32),
                vmem((4, 2, maps_here, PAD // 2, half), F32),
                vmem((half // 128, PAD, 128), F32),
                vmem((2, maps_here, PAD // 2, half), BF16),
                vmem((rounds, chips, 8, half), F32),
                vmem((rounds, PLANE, 8, half), F32),
                vmem((maps_here, PLANE, 8, half), F32),
                vmem((PLANE, 8, half), F32),
                vmem((2, 8, half), F32),
                vmem((8, half), F32),
                vmem((LAYERS, 8, half), F32),
                vmem((LAYERS, 8, half), F32),
                vmem((2, 8, half), F32),
                vmem((1, 8, half), F32),
                vmem((1, 8, half), F32),
                vmem((8, half), F32),
                vmem((2 * TAPS, half, half), BF16),
                vmem((UNITS, half // 2, half), BF16),
                vmem((2 * TAPS, half // 2, half), BF16),
                vmem((UNITS, actives - 1, piece, half), BF16),
                vmem((UNITS, piece, half), BF16),
                dma((8,)),
                dma((LAYERS, 3)),
                dma((6,)),
                dma((6,)),
                dma((3,)),
                dma((3,)),
                dma((rounds, chips)),
                dma((rounds, chips)),
                dma((rounds, PLANE)),
                dma((rounds, PLANE)),
                dma((LAYERS, 2)),
                dma((LAYERS, 2)),
                dma((LAYERS, 2)),
                dma((LAYERS, 2)),
                dma((LAYERS, maps_here)),
                dma((LAYERS, maps_here)),
                dma((LAYERS, maps_here)),
                dma((LAYERS, maps_here)),
                dma((3,)),
                dma((3,)),
                dma((3,)),
                dma((LAYERS,)),
                dma((LAYERS,)),
                dma((LAYERS, 2, maps_here)),
                dma((LAYERS, maps_here)),
                dma((UNITS,)),
                dma((UNITS,)),
                dma((UNITS,)),
                dma((UNITS,)),
                dma((UNITS, owners)),
                dma((UNITS, actives - 1)),
                dma((UNITS, actives)),
                dma((UNITS, owners)),
                dma((UNITS,)),
                dma((UNITS,)),
                dma((UNITS,)),
                dma((UNITS,)),
                dma((UNITS,)),
                dma((UNITS,)),
                dma((UNITS,)),
                dma((UNITS,)),
                dma((UNITS,)),
                dma((UNITS,)),
                dma((UNITS,)),
            ],
            compiler_params=pltpu.CompilerParams(
                collective_id=0,
                has_side_effects=True,
                vmem_limit_bytes=grant,
            ),
        )(
            block_input,
            conv_weights,
            *(
                pltpu.with_memory_space_constraint(v, pltpu.HBM)
                for v in (
                    norm_gains,
                    norm_shifts,
                    map_width,
                    map_group,
                    index_rows,
                    task_mask,
                    task_weights,
                    task_grads,
                )
            ),
        )
        input_grad = jnp.concatenate([ig[0], ig[1]], -1)[:, :, :columns]
        kernel_grads, pooled, gain_grads, shift_grads = pl.pallas_call(
            finish_kernel,
            out_shape=(
                jax.ShapeDtypeStruct(kg.shape, F32),
                jax.ShapeDtypeStruct(pool_index.shape, BF16),
                jax.ShapeDtypeStruct(norm_gains.shape, F32),
                jax.ShapeDtypeStruct(norm_shifts.shape, F32),
            ),
            in_specs=[whole] * 3,
            out_specs=(anywhere, whole, whole, whole),
            scratch_shapes=[vmem((RING,) + kg.shape[1:], F32), dma((RING,))],
            compiler_params=pltpu.CompilerParams(vmem_limit_bytes=24 * 1024 * 1024),
        )(kg, pooled, sums)
        return (
            pooled,
            input_grad,
            kernel_grads.reshape(conv_weights.shape),
            gain_grads,
            shift_grads,
        )

    return jax.shard_map(
        per_device,
        mesh=mesh,
        in_specs=(
            P("maps", "rows", None, None),
            P(),
            P(),
            P(),
            P(),
            P(),
            P("maps", "rows", None, None),
            P("maps", None),
            P(),
            P(None, "maps", "rows", None, None),
        ),
        out_specs=(P("maps", "rows", None, None), P("maps", "rows", None, None), P(), P(), P()),
        check_vma=False,
    )
```

```python
import functools

import jax
import jax.numpy as jnp
from jax import lax
from jax.experimental import pallas as pl
from jax.experimental.pallas import tpu as pltpu
from jax.sharding import PartitionSpec as P

MESH = pl.DeviceIdType.MESH
epsilon = 1e-05
PAD = 64
LAYERS = 3
TAPS = 9
UNITS = LAYERS * TAPS
PLANE = 4
LAG = 4
EARLY = 1
FOLD = 2
F32 = jnp.float32
BF16 = jnp.bfloat16


def each(first, last, body):
    if last - first <= 8:
        for k in range(first, last):
            body(k)
    else:
        lax.fori_loop(first, last, lambda k, s: (body(k), s)[1], 0)


def block_kernel(
    chips,
    height,
    x_ref,
    w_ref,
    gain_hbm,
    shift_hbm,
    width_hbm,
    group_hbm,
    index_hbm,
    tmask_hbm,
    tweight_hbm,
    tgrad_hbm,
    pooled_ref,
    ig_ref,
    kg_ref,
    sums_ref,
    gain_ref,
    shift_ref,
    width_ref,
    group_ref,
    index_ref,
    tmask_ref,
    tweight_ref,
    tgrad_ref,
    wa,
    wb,
    act_own,
    act_oth,
    act_t,
    act_b,
    zbuf,
    zs,
    zh,
    dh,
    dhs,
    dhh,
    dz_own,
    dz_oth,
    dzr,
    dzv,
    prod,
    gsrc,
    gbuf,
    hrow,
    pbuf,
    st1,
    st2,
    coef,
    nall,
    inv_t,
    cnt_t,
    avg_t,
    scl_t,
    mean_t,
    tb_t,
    ta_t,
    sums_own,
    terms,
    r2,
    rf,
    r3,
    fin,
    in_sem,
    w_sem,
    x_s,
    x_r,
    g_s,
    g_r,
    st1_s,
    st1_r,
    st2_s,
    st2_r,
    zh_s,
    zh_r,
    dh_s,
    dh_r,
    act_s,
    act_r,
    dz_s,
    dz_r,
    out_s,
    out_r,
    out_l,
    at_s,
    at_r,
    dzr_s,
    dzr_r,
    r2_s,
    r2_r,
    rf_s,
    rf_r,
    r3_s,
    r3_r,
    az_s,
    az_r,
    af_s,
    af_r,
    ab_s,
    ab_r,
    aa_s,
    aa_r,
    ae_s,
    ae_r,
    ap_s,
    ap_r,
    loc_s,
):
    maps_here = x_ref.shape[0]
    columns = x_ref.shape[2]
    half = x_ref.shape[3] // 2
    tasks = tgrad_ref.shape[0]
    pooled_columns = tgrad_ref.shape[3]
    lanes = half // 128
    tiles = [slice(n * 128, (n + 1) * 128) for n in range(lanes)]
    band = 4
    pixels = maps_here * band * PAD
    actives = chips // 2
    owners = min(actives, 8)
    piece = (half // 2) // owners
    m = lax.axis_index("maps")
    r = lax.axis_index("rows")
    c = lax.rem(r, 2)
    z = lax.div(r, 2)
    other = 1 - c
    first_map = m * maps_here
    x_bit = lax.rem(m, 2)
    y_bit = lax.div(m, 2)
    x_peer = m + 1 - 2 * x_bit
    y_peer = m + 2 - 4 * y_bit
    g_bit = (1 - c) * x_bit + c * y_bit
    h_bit = (1 - c) * y_bit + c * x_bit
    g_peer = (1 - c) * x_peer + c * y_peer
    h_peer = (1 - c) * y_peer + c * x_peer
    pair = lax.div(z, 2)
    turn = lax.rem(pair, 2)
    active_z = 2 * pair + 1 - turn
    is_active = z == active_z
    is_passive = z != active_z
    is_owner = jnp.logical_and(is_active, pair < owners)
    role = jnp.where(is_active, 0, 1)
    up_there = z > 0
    down_there = z < chips - 1
    row8 = lax.broadcasted_iota(jnp.int32, (8, half), 0)
    column = lax.broadcasted_iota(jnp.int32, (PAD, half), 0)

    def remote(src, dst, send, recv, mm, zz, cc):
        return pltpu.make_async_remote_copy(
            src_ref=src,
            dst_ref=dst,
            send_sem=send,
            recv_sem=recv,
            device_id=(mm, zz * 2 + cc),
            device_id_type=MESH,
        )

    def own_half(v):
        return jnp.where(c == 0, v[..., :half], v[..., half:])

    def width_of(a):
        return width_ref[first_map + a]

    own_at = pl.ds(pl.multiple_of(c * half, half), half)
    oth_at = pl.ds(pl.multiple_of(other * half, half), half)

    def weight_copy(l, n):
        dst = (wa, wb, wb)[n]
        k_at, o_at = ((own_at, own_at), (oth_at, own_at), (own_at, oth_at))[n]
        return pltpu.make_async_copy(w_ref.at[l, :, :, k_at, o_at], dst.at[l], w_sem.at[l, n])

    fetches = [
        pltpu.make_async_copy(src, dst, in_sem.at[n])
        for n, (src, dst) in enumerate(
            (
                (width_hbm, width_ref),
                (group_hbm, group_ref),
                (tmask_hbm, tmask_ref),
                (tweight_hbm, tweight_ref),
                (gain_hbm, gain_ref),
                (shift_hbm, shift_ref),
                (index_hbm.at[:, :, 0, :], index_ref),
                (tgrad_hbm, tgrad_ref),
            )
        )
    ]
    for fetch in fetches:
        fetch.start()
    for l in range(LAYERS):
        weight_copy(l, 0).start()
        weight_copy(l, 1).start()

    barrier = pltpu.get_barrier_semaphore()

    def greet(k):
        rr = lax.rem(r + k, 2 * chips)
        pl.semaphore_signal(barrier, inc=1, device_id=(m, rr), device_id_type=MESH)

    each(1, 2 * chips, greet)
    for k in range(1, PLANE):
        for core in (c, other):
            there = (lax.rem(m + k, PLANE), z * 2 + core)
            pl.semaphore_signal(barrier, inc=1, device_id=there, device_id_type=MESH)

    for fetch in fetches:
        fetch.wait()

    mine = pl.ds(1 + 2 * c, 2)
    for a in range(maps_here):
        inside = lax.broadcasted_iota(jnp.int32, (columns, 2 * half), 0) < width_of(a)
        for rr in range(2):
            v = jnp.where(inside, x_ref[a, rr].astype(F32), 0.0).astype(BF16)
            spot = 1 + 2 * c + rr
            act_own[0, a, spot, pl.ds(48, 16), :] = jnp.zeros((16, half), BF16)
            act_oth[0, a, spot, pl.ds(48, 16), :] = jnp.zeros((16, half), BF16)
            act_own[0, a, spot, pl.ds(0, columns), :] = own_half(v)
            act_oth[0, a, spot, pl.ds(0, columns), :] = jnp.where(
                c == 0, v[:, half:], v[:, :half]
            )

    @pl.when(z == 0)
    def _():
        act_own[0, :, 0] = jnp.zeros((maps_here, PAD, half), BF16)
        act_oth[0, :, 0] = jnp.zeros((maps_here, PAD, half), BF16)

    @pl.when(z == chips - 1)
    def _():
        act_own[0, :, 5] = jnp.zeros((maps_here, PAD, half), BF16)
        act_oth[0, :, 5] = jnp.zeros((maps_here, PAD, half), BF16)

    pl.semaphore_wait(barrier, 2 * chips - 1 + 2 * (PLANE - 1))

    x_partner = (
        remote(act_own.at[0, :, mine], act_oth.at[0, :, mine], x_s.at[0], x_r.at[0], m, z, other),
        remote(act_oth.at[0, :, mine], act_own.at[0, :, mine], x_s.at[1], x_r.at[1], m, z, other),
    )
    g_partner = remote(gsrc.at[other], gbuf.at[1 + c], g_s.at[0], g_r.at[0], m, z, other)

    def x_halo(n, src_row, dst_row, zz):
        cc = (c, other)[n % 2]
        low = dst_row == band + 1
        if n >= 2:
            src, dst = gsrc.at[cc], gbuf.at[3 if low else 0]
            return remote(src, dst, g_s.at[n - 1], g_r.at[1 if low else 2], m, zz, cc)
        src, dst = (act_own, act_oth)[n].at[0, :, src_row], act_own.at[0, :, dst_row]
        return remote(src, dst, x_s.at[2 + n], x_r.at[2 if low else 3], m, zz, cc)

    def x_pass(row):
        n = 4 if row == 0 else 5
        src, dst = act_own.at[0, :, row], act_oth.at[0, :, row]
        return remote(src, dst, x_s.at[n], x_r.at[n], m, z, other)

    for copy in x_partner:
        copy.start()

    @pl.when(jnp.logical_and(c == 0, up_there))
    def _():
        for n in range(2):
            x_halo(n, 1, 5, z - 1).start()

    @pl.when(jnp.logical_and(c == 1, down_there))
    def _():
        for n in range(2):
            x_halo(n, 4, 0, z + 1).start()

    gsrc[...] = jnp.zeros(gsrc.shape, F32)
    for a in range(maps_here):
        total = None
        for t in range(tasks):
            scale = tweight_ref[t] * tmask_ref[a, t].astype(F32)
            term = tgrad_ref[t, a, 0].astype(F32) * scale
            total = term if total is None else total + term
        position = index_ref[a].astype(F32)
        for h in range(2):
            gsrc[h, 0, a, pl.ds(0, pooled_columns), :] = total[:, h * half : (h + 1) * half]
            gsrc[h, 1, a, pl.ds(0, pooled_columns), :] = position[:, h * half : (h + 1) * half]
    gbuf[1 + c] = gsrc[c]

    for mm in range(PLANE):
        sizes = jnp.zeros((8, half), F32)
        for b in range(maps_here):
            sizes = jnp.where(
                row8 == b, (width_ref[mm * maps_here + b] * height).astype(F32), sizes
            )
        nall[mm] = sizes
    inside_sizes = jnp.zeros((8, half), F32)
    for b in range(maps_here):
        inside_sizes = jnp.where(row8 == b, (width_of(b) * band).astype(F32), inside_sizes)
    inv_t[0] = inside_sizes
    inv_t[1] = jnp.where(row8 < maps_here, 1.0 / jnp.maximum(inside_sizes, 1.0), 0.0)
    counts = jnp.ones((8, half), F32)
    for a in range(maps_here):
        total = jnp.zeros((1, half), F32)
        for mm in range(PLANE):
            same = jnp.zeros((8, half), F32)
            for b in range(maps_here):
                alike = group_ref[first_map + a] == group_ref[mm * maps_here + b]
                same = jnp.where(row8 == b, jnp.where(alike, 1.0, 0.0), same)
            coef[a, mm] = same
            total = total + jnp.sum(same * nall[mm], 0, keepdims=True)
        counts = jnp.where(row8 == a, total, counts)
    cnt_t[...] = counts

    def z_copy(e, k):
        zz = lax.rem(z + k, chips)
        return remote(st1.at[e, z], st1.at[e, z], st1_s.at[e, k], st1_r.at[e, z], m, zz, c)

    def z_arrival(e, k):
        zz = lax.rem(z + k, chips)
        return remote(st1.at[e, zz], st1.at[e, zz], st1_s.at[e, k], st1_r.at[e, zz], m, zz, c)

    def m_copy(e, k):
        mm = lax.rem(m + k, PLANE)
        return remote(st2.at[e, m], st2.at[e, m], st2_s.at[e, k], st2_r.at[e, m], mm, z, c)

    def m_arrival(e, k):
        mm = lax.rem(m + k, PLANE)
        return remote(st2.at[e, mm], st2.at[e, mm], st2_s.at[e, k], st2_r.at[e, mm], mm, z, c)

    def send_z(e, tile):
        st1[e, z] = tile
        each(1, chips, lambda k: z_copy(e, k).start())

    def wait_z(e):
        each(1, chips, lambda k: z_arrival(e, k).wait_recv())

    def send_m(e, tile):
        st2[e, m] = tile
        each(1, PLANE, lambda k: m_copy(e, k).start())

    def wait_m(e):
        each(1, PLANE, lambda k: m_arrival(e, k).wait_recv())

    def products(source, l, taps, kernel, transposed, fresh):
        starts = [2 - i if transposed else i for i in taps]
        lhs = jnp.concatenate(
            [source[lax.rem(l, 2), :, s : s + band].reshape(pixels, half) for s in starts], 1
        )
        for j in range(3):
            rhs = jnp.concatenate([kernel[l, i, j] for i in taps], 1 if transposed else 0)
            got = lax.dot_general(
                lhs,
                rhs,
                (((1,), (1 if transposed else 0,)), ((), ())),
                preferred_element_type=F32,
            )
            if fresh:
                prod[j] = got
            else:
                prod[j] = prod[j] + got

    def shifted(a, rr, before, behind, n):
        rows = pl.ds(pl.multiple_of((a * band + rr) * PAD, PAD), PAD)
        return (
            prod[1, rows, n]
            + pltpu.roll(prod[before, rows, n], 1, 0)
            + pltpu.roll(prod[behind, rows, n], PAD - 1, 0)
        )

    def row_of(table, l, a):
        return table[l, pl.ds(a, 1), :]

    def gain_of(l):
        return own_half(gain_ref[pl.ds(l, 1), :])

    def shift_of(l):
        return own_half(shift_ref[pl.ds(l, 1), :])

    def limit(a, rr):
        w = width_of(a)
        if rr == 0:
            return jnp.where(up_there, w, 0)
        if rr == band + 1:
            return jnp.where(down_there, w, 0)
        return w

    def z_halo(l, way):
        there = z - 1 + 2 * way
        return remote(zs.at[way], zh.at[l, 1 - way], zh_s.at[l, way], zh_r.at[l, way], m, there, c)

    def dh_halo(l, way):
        there = z - 1 + 2 * way
        return remote(dhs.at[way], dhh.at[l, 1 - way], dh_s.at[l, way], dh_r.at[l, way], m, there, c)

    def start_halo(halo, l):
        @pl.when(up_there)
        def _():
            halo(l, 0).start()

        @pl.when(down_there)
        def _():
            halo(l, 1).start()

    def wait_halo(halo, l):
        @pl.when(up_there)
        def _():
            halo(l, 1).wait_recv()
            halo(l, 0).wait_send()

        @pl.when(down_there)
        def _():
            halo(l, 0).wait_recv()
            halo(l, 1).wait_send()

    def act_copy(l, a):
        slot = lax.rem(l, 2)
        src, dst = act_own.at[slot, a], act_oth.at[slot, a]
        return remote(src, dst, act_s.at[l, a], act_r.at[l, a], m, z, other)

    def at_copy(l):
        return remote(act_t.at[l, 0], act_t.at[l, 1], at_s.at[l], at_r.at[l], g_peer, z, c)

    def dzr_copy(l, a, way):
        src, dst = dz_own.at[lax.rem(l, 2), a, pl.ds(1, band)], dzr.at[l, a]
        peer = (x_peer, y_peer)[way]
        return remote(src, dst, dzr_s.at[l, way, a], dzr_r.at[l, a], peer, z, way)

    def if_wanted(way, body):
        @pl.when((x_bit, y_bit)[way] + c == 1)
        def _():
            body()

    def dz_copy(l, a):
        slot = lax.rem(l, 2)
        src, dst = dz_own.at[slot, a], dz_oth.at[slot, a]
        return remote(src, dst, dz_s.at[l, a], dz_r.at[l, a], m, z, other)

    def send_gradients():
        g_partner.start()

        @pl.when(jnp.logical_and(c == 0, up_there))
        def _():
            for n in range(2, 4):
                x_halo(n, 1, 5, z - 1).start()

        @pl.when(jnp.logical_and(c == 1, down_there))
        def _():
            for n in range(2, 4):
                x_halo(n, 4, 0, z + 1).start()

    def if_there(way, body):
        @pl.when((up_there, down_there)[way])
        def _():
            body()

    def wait_x_halo(n):
        if_there(0, lambda: x_halo(n, 4, 0, z - 1).wait_recv())
        if_there(1, lambda: x_halo(n, 1, 5, z + 1).wait_recv())

    def each_x_pass(act):
        if_there(0, lambda: act(x_pass(0)))
        if_there(1, lambda: act(x_pass(band + 1)))

    def sent_x_halo(first, last):
        @pl.when(jnp.logical_and(c == 0, up_there))
        def _():
            for n in range(first, last):
                x_halo(n, 1, 5, z - 1).wait_send()

        @pl.when(jnp.logical_and(c == 1, down_there))
        def _():
            for n in range(first, last):
                x_halo(n, 4, 0, z + 1).wait_send()

    def unpool(a, s):
        for rr in range(band + 2):
            slot, lower = (rr + 1) // 2, (rr + 1) % 2
            g = gbuf[slot, 0, a]
            position = gbuf[slot, 1, a]
            for b in range(2):
                v = jnp.where(position == float(2 * lower + b), g, 0.0)
                for n in range(lanes):
                    hrow[n, pl.ds(b, PAD // 2, stride=2), :] = v[:, n * 128 : (n + 1) * 128]
            v = jnp.concatenate([hrow[n] for n in range(lanes)], 1)
            if rr in (0, band + 1):
                dhh[LAYERS - 1, rr // (band + 1), a] = v.astype(BF16)
            else:
                dh[a, rr - 1] = v
        return s

    def forward(l, first):
        weight_copy(l, 0).wait()
        weight_copy(l, 1).wait()
        if first:
            for copy in x_partner:
                copy.wait_recv()
            products(act_own, l, (1,), wa, False, True)
            products(act_oth, l, (1,), wb, False, False)
            wait_x_halo(0)
            each_x_pass(lambda copy: copy.start())
            products(act_own, l, (0, 2), wa, False, False)
            each_x_pass(lambda copy: copy.wait_recv())
            products(act_oth, l, (0, 2), wb, False, False)
        else:
            products(act_own, l, (0, 1, 2), wa, False, True)
            for a in range(maps_here):
                act_copy(l, a).wait_recv()
            products(act_oth, l, (0, 1, 2), wb, False, False)
        weight_copy(l, 2).start()

        def collect(a, tile):
            inside = column[:, :128] < width_of(a)
            pixels_inside = (width_of(a) * band).astype(F32)
            totals, squares = [], []
            for n in tiles:
                total = jnp.zeros((PAD, 128), F32)
                for rr in range(band):
                    v = shifted(a, rr, 0, 2, n)
                    zbuf[l, a, 1 + rr, :, n] = v
                    total = total + jnp.where(inside, v, 0.0)
                total = jnp.sum(total, 0, keepdims=True)
                mean = total / pixels_inside
                square = jnp.zeros((PAD, 128), F32)
                for rr in range(band):
                    v = jnp.where(inside, zbuf[l, a, 1 + rr, :, n] - mean, 0.0)
                    square = square + v * v
                    if rr in (0, band - 1):
                        zs[rr // (band - 1), a, :, n] = v.astype(BF16)
                totals.append(total)
                squares.append(jnp.sum(square, 0, keepdims=True))
            tile = jnp.where(row8 == a, jnp.concatenate(totals, 1), tile)
            return jnp.where(row8 == a + maps_here, jnp.concatenate(squares, 1), tile)

        tile = lax.fori_loop(0, maps_here, collect, jnp.zeros((8, half), F32))
        send_z(l, tile)
        start_halo(z_halo, l)
        act_t[l, 0] = act_own[lax.rem(l, 2)].reshape(maps_here * (band + 2) * PAD, half).T
        wait_z(l)
        sizes, inverse = inv_t[0], inv_t[1]
        mean_t[0] = st1[l, jnp.maximum(z - 1, 0)] * inverse
        mean_t[1] = st1[l, jnp.minimum(z + 1, chips - 1)] * inverse
        total = st1[l, 0]
        for zz in range(1, chips):
            total = total + st1[l, zz]
        mean = total * inverse * (1.0 / chips)
        square = jnp.zeros((8, half), F32)
        for zz in range(chips):
            v = st1[l, zz]
            gap = v * inverse - mean
            square = square + pltpu.roll(v, 8 - maps_here, 0) + sizes * gap * gap
        tile = jnp.where(row8 < maps_here, mean, pltpu.roll(square, maps_here, 0))
        send_m(l, jnp.where(row8 < 2 * maps_here, tile, 0.0))
        if not first:

            @pl.when(l == LAYERS - 1)
            def _():
                g_partner.wait_recv()
                wait_x_halo(2)
                lax.fori_loop(0, maps_here, unpool, 0)

        wait_m(l)
        at_copy(l).start()
        if first:
            send_gradients()
        averages = jnp.zeros((8, half), F32)
        scalings = jnp.zeros((8, half), F32)
        for a in range(maps_here):
            count = cnt_t[a : a + 1, :]
            average = jnp.zeros((8, half), F32)
            for mm in range(PLANE):
                average = average + coef[a, mm] * nall[mm] * st2[l, mm]
            average = jnp.sum(average, 0, keepdims=True) / count
            variance = jnp.zeros((8, half), F32)
            for mm in range(PLANE):
                v = st2[l, mm]
                gap = v - average
                variance = variance + coef[a, mm] * (
                    pltpu.roll(v, 8 - maps_here, 0) + nall[mm] * gap * gap
                )
            variance = jnp.sum(variance, 0, keepdims=True) / count
            averages = jnp.where(row8 == a, average, averages)
            scalings = jnp.where(row8 == a, lax.rsqrt(variance + epsilon), scalings)
        avg_t[l] = averages
        scl_t[l] = scalings
        wait_halo(z_halo, l)

        def activate(a, s):
            gain, shift = gain_of(l), shift_of(l)
            for n in tiles:
                average = row_of(avg_t, l, a)[:, n]
                factor = row_of(scl_t, l, a)[:, n] * gain[:, n]
                for rr in range(band + 2):
                    if rr in (0, band + 1):
                        way = rr // (band + 1)
                        v = zh[l, way, a, :, n].astype(F32) + row_of(mean_t, way, a)[:, n]
                        zbuf[l, a, rr, :, n] = v
                    else:
                        v = zbuf[l, a, rr, :, n]
                    y = (v - average) * factor + shift[:, n]
                    h = jnp.where(column[:, n] < limit(a, rr), y * jax.nn.sigmoid(y), 0.0)
                    act_own[lax.rem(l + 1, 2), a, rr, :, n] = h.astype(BF16)

            @pl.when(l < LAYERS - 1)
            def _():
                act_copy(l + 1, a).start()

            return s

        if first:
            for copy in x_partner:
                copy.wait_send()
            sent_x_halo(0, 2)
            each_x_pass(lambda copy: copy.wait_send())
        else:

            @pl.when(l == 2)
            def _():
                for a in range(maps_here):
                    act_copy(1, a).wait_send()

        lax.fori_loop(0, maps_here, activate, 0)

    forward(0, True)
    lax.fori_loop(1, LAYERS, lambda l, s: (forward(l, False), s)[1], 0)


    def pool():
        def one(a, s):
            for pr in range(2):
                total = jnp.zeros((PAD // 2, half), F32)
                position = gbuf[1 + pr, 1, a]
                for lower in range(2):
                    v = act_own[LAYERS % 2, a, 1 + 2 * pr + lower].astype(F32)
                    for n in range(lanes):
                        hrow[n] = v[:, n * 128 : (n + 1) * 128]
                    for b in range(2):
                        v = jnp.concatenate(
                            [hrow[n, pl.ds(b, PAD // 2, stride=2), :] for n in range(lanes)], 1
                        )
                        total = total + jnp.where(position == float(2 * lower + b), v, 0.0)
                pbuf[pr, a] = total.astype(BF16)
            return s

        lax.fori_loop(0, maps_here, one, 0)

    def second_rows(bit):
        return pl.ds(pl.multiple_of(bit * (half // 2), half // 2), half // 2)

    def piece_rows(p):
        return pl.ds(pl.multiple_of(p * piece, piece), piece)

    def term_slot(q):
        return lax.rem(q, 2 * TAPS)

    def c2(q):
        src = terms.at[term_slot(q), second_rows(1 - h_bit)]
        return remote(src, r2.at[q], r2_s.at[q], r2_r.at[q], h_peer, z, c)

    def z_of(n):
        return 2 * n + 1 - lax.rem(n, 2)

    def cf(q):
        passive_z = 2 * pair + turn
        there = active_z + passive_z - z
        return remote(r2.at[q], rf.at[term_slot(q)], rf_s.at[q], rf_r.at[q], m, there, c)

    def c3(q, p):
        slot = lax.rem(pair - p + actives - 1, actives)
        return remote(
            r2.at[q, piece_rows(p)], r3.at[q, slot], r3_s.at[q, p], r3_r.at[q, slot], m, z_of(p), c
        )

    def others(first, body, limit):
        def one(k):
            n = lax.rem(pair + k, actives)

            @pl.when(n < limit)
            def _():
                body(n)

        each(first, actives, one)

    def unit_of(q):
        k = lax.div(q, TAPS)
        return (LAYERS - 1 - k) * TAPS + (q - k * TAPS)

    def region(q, start, size, lane, lanes):
        start = pl.multiple_of(c * half + start, piece)
        lane = pl.multiple_of(lane, half)
        return kg_ref.at[unit_of(q), pl.ds(start, size), pl.ds(lane, lanes)]

    def cz(q, p, n):
        part = region(q, h_bit * (half // 2) + p * piece, piece, g_bit * half, half)
        return remote(fin.at[q], part, az_s.at[q, n], az_r.at[q, p], m, z_of(n), c)

    def cl(q):
        part = region(q, h_bit * (half // 2) + pair * piece, piece, g_bit * half, half)
        return pltpu.make_async_copy(fin.at[q], part, loc_s.at[q])

    def cu(q):
        passive_z = 2 * pair + turn
        there = active_z + passive_z - z
        part = region(q, h_bit * (half // 2), half // 2, g_bit * half, half)
        return remote(part, part, af_s.at[q], af_r.at[q], m, there, c)

    def cb(q):
        part = region(q, h_bit * (half // 2), half // 2, g_bit * half, half)
        return remote(part, part, ab_s.at[q], ab_r.at[q], h_peer, z, c)

    def ca(q):
        part = region(q, 0, half, g_bit * half, half)
        return remote(part, part, aa_s.at[q], aa_r.at[q], g_peer, z, c)

    def plan(q):
        k = lax.rem(q, 5)
        both = jnp.logical_or(lax.rem(k, 2) == 0, q >= UNITS - 5)
        mine = jnp.logical_or(both, lax.div(k, 2) == role)
        return mine, jnp.logical_and(mine, jnp.logical_not(both)), jnp.logical_not(mine)

    def ce(q):
        passive_z = 2 * pair + turn
        there = active_z + passive_z - z
        part = region(q, 0, half, (1 - g_bit) * half, half)
        return remote(part, part, ae_s.at[q], ae_r.at[q], m, there, c)

    def cp_part(q, start, size, lane, lanes):
        part = region(q, start, size, lane, lanes)
        return remote(part, part, ap_s.at[q], ap_r.at[q], m, z, other)

    def cp(q):
        return cp_part(q, 0, half, 0, 2 * half)

    def cp_rows(q, bit):
        return cp_part(q, bit * (half // 2), half // 2, g_bit * half, half)

    def cp_lanes(q):
        return cp_part(q, 0, half, (1 - g_bit) * half, half)

    def ready_terms(l):
        at_copy(l).wait_recv()
        for chip in range(2):
            for a in range(maps_here):
                first = a * (band + 2) * PAD
                rows = act_t[l, chip, :, first : first + (band + 2) * PAD]
                act_b[chip, :, a * band * PAD : (a + 1) * band * PAD] = rows[:, PAD : PAD + band * PAD]
        slot = lax.rem(l, 2)

        def variants(a, s):
            dzr_copy(l, a, 0).wait_recv()
            for chip in range(2):
                for rr in range(band):
                    for n in tiles:
                        if chip == 0:
                            mine, theirs = dz_own[slot, a, 1 + rr, :, n], dz_oth[slot, a, 1 + rr, :, n]
                            v = jnp.where(g_bit == c, mine, theirs)
                        else:
                            v = dzr[l, a, rr, :, n]
                        dzv[1, chip, a, rr, :, n] = v
                        v = v.astype(F32)
                        dzv[0, chip, a, rr, :, n] = pltpu.roll(v, PAD - 1, 0).astype(BF16)
                        dzv[2, chip, a, rr, :, n] = pltpu.roll(v, 1, 0).astype(BF16)
            return s

        lax.fori_loop(0, maps_here, variants, 0)

    def tap_terms(l, i, j):
        if i == 1:
            lhs = [act_b[0], act_b[1]]
        else:
            lhs = []
            for chip in range(2):
                for a in range(maps_here):
                    first = (a * (band + 2) + i) * PAD
                    lhs.append(act_t[l, chip, :, first : first + band * PAD])
        rhs = dzv[j].reshape(2 * pixels, half)
        q = (LAYERS - 1 - l) * TAPS + 3 * i + j
        got = jnp.dot(jnp.concatenate(lhs, 1), rhs, preferred_element_type=F32)
        terms[term_slot(q)] = got.astype(BF16)
        c2(q).start()

    def weight_terms(l, i):
        lax.fori_loop(0, 3, lambda j, s: (tap_terms(l, i, j), s)[1], 0)

    def stage_second(q):
        c2(q).wait()
        kept = terms[term_slot(q), second_rows(h_bit)].astype(F32)
        r2[q] = (r2[q].astype(F32) + kept).astype(BF16)

        @pl.when(is_passive)
        def _():
            cf(q).start()

    def stage_fold(q):
        @pl.when(is_active)
        def _():
            cf(q).wait_recv()
            r2[q] = (r2[q].astype(F32) + rf[term_slot(q)].astype(F32)).astype(BF16)
            others(1, lambda n: c3(q, n).start(), owners)

    def stage_sum(q):
        @pl.when(is_owner)
        def _():
            for k in range(actives - 1):
                remote(
                    r3.at[q, k], r3.at[q, k], r3_s.at[q, 0], r3_r.at[q, k], m, z, c
                ).wait_recv()
            total = r2[q, piece_rows(pair)].astype(F32)
            for k in range(actives - 1):
                total = total + r3[q, k].astype(F32)
            fin[q] = total.astype(BF16)
            others(1, lambda n: cz(q, pair, n).start(), actives)
            cl(q).start()

    def stage_back(q):
        @pl.when(is_active)
        def _():
            others(1, lambda n: cz(q, n, n).wait_recv(), owners)

        @pl.when(is_owner)
        def _():
            cl(q).wait()

        @pl.when(is_active)
        def _():
            cu(q).start()

        @pl.when(is_passive)
        def _():
            cu(q).wait_recv()

        cb(q).start()
        cp_rows(q, h_bit).start()

    def stage_first(q):
        cb(q).wait_recv()
        mine, _, _ = plan(q)

        @pl.when(mine)
        def _():
            ca(q).start()

        cp_rows(q, 1 - h_bit).start()

        @pl.when(is_active)
        def _():
            others(1, lambda n: c3(q, n).wait_send(), owners)

        @pl.when(is_passive)
        def _():
            cf(q).wait_send()

    def stage_chip(q):
        mine, for_both, _ = plan(q)

        @pl.when(mine)
        def _():
            ca(q).wait_recv()

        @pl.when(for_both)
        def _():
            ce(q).start()

        @pl.when(mine)
        def _():
            cp_lanes(q).start()

        @pl.when(is_owner)
        def _():
            others(1, lambda n: cz(q, pair, n).wait_send(), actives)

        @pl.when(is_active)
        def _():
            cu(q).wait_send()

    def stage_late(q):
        _, _, not_mine = plan(q)

        @pl.when(not_mine)
        def _():
            ce(q).wait_recv()
            cp_lanes(q).start()

    def stage_done(q):
        mine, for_both, _ = plan(q)
        cb(q).wait_send()

        @pl.when(mine)
        def _():
            ca(q).wait_send()

        @pl.when(for_both)
        def _():
            ce(q).wait_send()

        cp(q).wait()

    def run(stage, first, last):
        lax.fori_loop(first, last, lambda q, s: (stage(q), s)[1], 0)

    def sent_dz(l):
        for a in range(maps_here):
            dz_copy(l, a).wait_send()
            for way in range(2):
                if_wanted(way, dzr_copy(l, a, way).wait_send)

    def backward(k, carry):
        l = LAYERS - 1 - k
        gain, shift = gain_of(l), shift_of(l)

        def gradient(a, rr, n):
            zhat = (zbuf[l, a, rr, :, n] - row_of(avg_t, l, a)[:, n]) * row_of(scl_t, l, a)[:, n]
            y = zhat * gain[:, n] + shift[:, n]
            s = jax.nn.sigmoid(y)
            if rr in (0, band + 1):
                upstream = dhh[l, rr // (band + 1), a, :, n].astype(F32)
            else:
                upstream = dh[a, rr - 1, :, n]
            dy = upstream * (s * (1.0 + y * (1.0 - s)))
            dy = jnp.where(column[:, n] < limit(a, rr), dy, 0.0)
            return dy, zhat

        def collect(a, tile):
            plains, crosses = [], []
            for n in tiles:
                plain = jnp.zeros((PAD, 128), F32)
                crossed = jnp.zeros((PAD, 128), F32)
                for rr in range(1, band + 1):
                    dy, zhat = gradient(a, rr, n)
                    dh[a, rr - 1, :, n] = dy
                    plain = plain + dy
                    crossed = crossed + dy * zhat
                plains.append(jnp.sum(plain, 0, keepdims=True))
                crosses.append(jnp.sum(crossed, 0, keepdims=True))
            tile = jnp.where(row8 == a, jnp.concatenate(plains, 1), tile)
            return jnp.where(row8 == a + maps_here, jnp.concatenate(crosses, 1), tile)

        e = LAYERS + l
        tile = lax.fori_loop(0, maps_here, collect, jnp.zeros((8, half), F32))
        send_z(e, tile)

        @pl.when(k == LAYERS - 1)
        def _():
            run(stage_second, 0, TAPS)

        @pl.when(k > 0)
        def _():
            ready_terms(l + 1)
            weight_terms(l + 1, 0)

        wait_z(e)
        total = st1[e, 0]
        for zz in range(1, chips):
            total = total + st1[e, zz]
        send_m(e, total)

        @pl.when(k > 0)
        def _():
            weight_terms(l + 1, 1)
            weight_terms(l + 1, 2)
            wait_halo(dh_halo, l)

        @pl.when(k == 0)
        def _():
            pool()

        wait_m(e)
        total = st2[e, 0]
        for mm in range(1, PLANE):
            total = total + st2[e, mm]
        sums_own[pl.ds(l, 1), :] = jnp.sum(
            jnp.where(row8 >= maps_here, total, 0.0), 0, keepdims=True
        )
        sums_own[pl.ds(LAYERS + l, 1), :] = jnp.sum(
            jnp.where(row8 < maps_here, total, 0.0), 0, keepdims=True
        )
        plains = jnp.zeros((8, half), F32)
        crosses = jnp.zeros((8, half), F32)
        for a in range(maps_here):
            plain = jnp.zeros((8, half), F32)
            crossed = jnp.zeros((8, half), F32)
            for mm in range(PLANE):
                v = st2[e, mm]
                plain = plain + coef[a, mm] * v
                crossed = crossed + coef[a, mm] * pltpu.roll(v, 8 - maps_here, 0)
            count = cnt_t[a : a + 1, :]
            plain = gain * (jnp.sum(plain, 0, keepdims=True) / count)
            crossed = gain * (jnp.sum(crossed, 0, keepdims=True) / count)
            plains = jnp.where(row8 == a, plain, plains)
            crosses = jnp.where(row8 == a, crossed, crosses)
        tb_t[0] = plains
        ta_t[0] = crosses

        def settle(a, s):
            for n in tiles:
                average, scaling = row_of(avg_t, l, a)[:, n], row_of(scl_t, l, a)[:, n]
                plain, crossed = row_of(tb_t, 0, a)[:, n], row_of(ta_t, 0, a)[:, n]
                for rr in range(band + 2):
                    if rr in (0, band + 1):
                        dy, zhat = gradient(a, rr, n)
                    else:
                        dy = dh[a, rr - 1, :, n]
                        zhat = (zbuf[l, a, rr, :, n] - average) * scaling
                    v = scaling * (dy * gain[:, n] - plain - zhat * crossed)
                    v = jnp.where(column[:, n] < limit(a, rr), v, 0.0)
                    dz_own[lax.rem(l, 2), a, rr, :, n] = v.astype(BF16)
            dz_copy(l, a).start()
            for way in range(2):
                if_wanted(way, dzr_copy(l, a, way).start)
            return s

        @pl.when(k == 2)
        def _():
            sent_dz(LAYERS - 1)

        lax.fori_loop(0, maps_here, settle, 0)
        products(dz_own, l, (0, 1, 2), wa, True, True)
        weight_copy(l, 2).wait()
        for a in range(maps_here):
            dz_copy(l, a).wait_recv()
        products(dz_oth, l, (0, 1, 2), wb, True, False)

        def gather(a, s):
            for n in tiles:
                for rr in range(band):
                    v = shifted(a, rr, 2, 0, n)
                    dh[a, rr, :, n] = v
                    if rr in (0, band - 1):
                        dhs[rr // (band - 1), a, :, n] = v.astype(BF16)
            return s

        lax.fori_loop(0, maps_here, gather, 0)

        @pl.when(l > 0)
        def _():
            start_halo(dh_halo, l - 1)

        return carry

    lax.fori_loop(0, LAYERS, backward, 0)
    def input_rows(a, s):
        for rr in range(band):
            dh[a, rr] = jnp.where(column < width_of(a), dh[a, rr], 0.0)
        return s

    lax.fori_loop(0, maps_here, input_rows, 0)

    outs = (
        (
            remote(dh.at[:, pl.ds(2 * other, 2)], ig_ref.at[c], out_s.at[0], out_r.at[0], m, z, other),
            pltpu.make_async_copy(dh.at[:, pl.ds(2 * c, 2)], ig_ref.at[c], out_l.at[0]),
        ),
        (
            remote(pbuf.at[other], pooled_ref.at[c], out_s.at[1], out_r.at[1], m, z, other),
            pltpu.make_async_copy(pbuf.at[c], pooled_ref.at[c], out_l.at[1]),
        ),
        (
            remote(sums_own, sums_ref.at[c], out_s.at[2], out_r.at[2], m, z, other),
            pltpu.make_async_copy(sums_own, sums_ref.at[c], out_l.at[2]),
        ),
    )
    for there, here in outs:
        there.start()
        here.start()

    g_partner.wait_send()
    sent_x_halo(2, 4)

    def sent(e, carry):
        each(1, chips, lambda k: z_copy(e, k).wait_send())
        each(1, PLANE, lambda k: m_copy(e, k).wait_send())
        return carry

    lax.fori_loop(0, 2 * LAYERS, sent, 0)
    for l in range(LAYERS):
        at_copy(l).wait_send()
    for l in range(LAYERS - 1):
        sent_dz(l)

    def drain(s, carry):
        @pl.when(s == EARLY)
        def _():
            ready_terms(0)

        for i in range(3):
            j = s - EARLY - 3 * i

            @pl.when(jnp.logical_and(j >= 0, j < 3))
            def _(i=i, j=j):
                tap_terms(0, i, j)

        for stage, first, lag in (
            (stage_done, 0, 2 * FOLD + 4 * LAG),
            (stage_late, 0, 2 * FOLD + 3 * LAG),
            (stage_chip, 0, 2 * FOLD + 2 * LAG),
            (stage_first, 0, 2 * FOLD + LAG),
            (stage_back, 0, 2 * FOLD),
            (stage_sum, 0, FOLD),
            (stage_fold, 0, 0),
            (stage_second, TAPS, 0),
        ):
            q = first + s - lag

            @pl.when(jnp.logical_and(q >= first, q < UNITS))
            def _(stage=stage, q=q):
                stage(q)

        return carry

    lax.fori_loop(0, UNITS + 2 * FOLD + 4 * LAG, drain, 0)
    for a in range(maps_here):
        act_copy(2, a).wait_send()
    for there, here in outs:
        there.wait()
        here.wait()


RING = 4


def finish_kernel(kg_ref, pooled_ref, sums_ref, kernel_out, pooled_out, gain_out, shift_out, ring, sem):
    def copy(t):
        slot = lax.rem(t, RING)
        return pltpu.make_async_copy(ring.at[slot], kernel_out.at[t], sem.at[slot])

    def one(t, s):
        @pl.when(t >= RING)
        def _():
            copy(t - RING).wait()

        ring[lax.rem(t, RING)] = kg_ref[t].astype(F32)
        copy(t).start()
        return s

    lax.fori_loop(0, UNITS, one, 0)
    for a in range(pooled_out.shape[0]):
        row = jnp.concatenate([pooled_ref[0, a], pooled_ref[1, a]], 1)
        pooled_out[a, 0] = row[: pooled_out.shape[2]]
    sums = jnp.concatenate([sums_ref[0], sums_ref[1]], 1)
    gain_out[...] = sums[:LAYERS]
    shift_out[...] = sums[LAYERS : 2 * LAYERS]
    for t in range(UNITS - RING, UNITS):
        copy(t).wait()


def solution(mesh):
    chips = mesh.shape["rows"] // 2

    def per_device(
        block_input,
        conv_weights,
        norm_gains,
        norm_shifts,
        map_width,
        map_group,
        pool_index,
        task_mask,
        task_weights,
        task_grads,
    ):
        maps_here, rows_here, columns, channels = block_input.shape
        pooled_columns = pool_index.shape[2]
        height = rows_here * mesh.shape["rows"]
        half = channels // 2
        band = 2 * rows_here
        pixels = maps_here * band * PAD
        actives = chips // 2
        owners = min(actives, 8)
        piece = half // 2 // owners
        rounds = 2 * LAYERS
        slots = 2 * UNITS * (actives - 1) * piece * half + 4 * rounds * chips * 8 * half
        grant = (36 * 1024 + 256) * 1024 + slots
        vmem, dma = pltpu.VMEM, pltpu.SemaphoreType.DMA
        tile = (maps_here, band + 2, PAD, half)
        edge = (2, maps_here, PAD, half)
        whole = pl.BlockSpec(memory_space=pltpu.VMEM)
        outside = pl.BlockSpec(memory_space=pltpu.HBM)
        index_rows = jnp.transpose(pool_index, (0, 2, 1, 3))
        anywhere = pl.BlockSpec(memory_space=pl.ANY)
        pooled, ig, kg, sums = pl.pallas_call(
            functools.partial(block_kernel, chips, height),
            out_shape=(
                jax.ShapeDtypeStruct((2, maps_here, PAD // 2, half), BF16),
                jax.ShapeDtypeStruct((2, maps_here, rows_here, PAD, half), F32),
                jax.ShapeDtypeStruct((UNITS, channels, channels), BF16),
                jax.ShapeDtypeStruct((2, 8, half), F32),
            ),
            in_specs=[whole, anywhere] + [outside] * 8,
            out_specs=[anywhere] * 4,
            scratch_shapes=[
                vmem(norm_gains.shape, F32),
                vmem(norm_shifts.shape, F32),
                pltpu.SMEM(map_width.shape, jnp.int32),
                pltpu.SMEM(map_group.shape, jnp.int32),
                vmem((maps_here, pooled_columns, channels), jnp.int32),
                pltpu.SMEM(task_mask.shape, jnp.int32),
                pltpu.SMEM(task_weights.shape, F32),
                vmem(task_grads.shape, BF16),
                vmem((LAYERS, 3, 3, half, half), BF16),
                vmem((LAYERS, 3, 3, half, half), BF16),
                vmem((2,) + tile, BF16),
                vmem((2,) + tile, BF16),
                vmem((LAYERS, 2, half, maps_here * (band + 2) * PAD), BF16),
                vmem((2, half, pixels), BF16),
                vmem((LAYERS,) + tile, F32),
                vmem(edge, BF16),
                vmem((LAYERS,) + edge, BF16),
                vmem((maps_here, band, PAD, half), F32),
                vmem(edge, BF16),
                vmem((LAYERS,) + edge, BF16),
                vmem((2,) + tile, BF16),
                vmem((2,) + tile, BF16),
                vmem((LAYERS, maps_here, band, PAD, half), BF16),
                vmem((3, 2, maps_here, band, PAD, half), BF16),
                vmem((3, pixels, half), F32),
                vmem((2, 2, maps_here, PAD // 2, half), F32),
                vmem((4, 2, maps_here, PAD // 2, half), F32),
                vmem((half // 128, PAD, 128), F32),
                vmem((2, maps_here, PAD // 2, half), BF16),
                vmem((rounds, chips, 8, half), F32),
                vmem((rounds, PLANE, 8, half), F32),
                vmem((maps_here, PLANE, 8, half), F32),
                vmem((PLANE, 8, half), F32),
                vmem((2, 8, half), F32),
                vmem((8, half), F32),
                vmem((LAYERS, 8, half), F32),
                vmem((LAYERS, 8, half), F32),
                vmem((2, 8, half), F32),
                vmem((1, 8, half), F32),
                vmem((1, 8, half), F32),
                vmem((8, half), F32),
                vmem((2 * TAPS, half, half), BF16),
                vmem((UNITS, half // 2, half), BF16),
                vmem((2 * TAPS, half // 2, half), BF16),
                vmem((UNITS, actives - 1, piece, half), BF16),
                vmem((UNITS, piece, half), BF16),
                dma((8,)),
                dma((LAYERS, 3)),
                dma((6,)),
                dma((6,)),
                dma((3,)),
                dma((3,)),
                dma((rounds, chips)),
                dma((rounds, chips)),
                dma((rounds, PLANE)),
                dma((rounds, PLANE)),
                dma((LAYERS, 2)),
                dma((LAYERS, 2)),
                dma((LAYERS, 2)),
                dma((LAYERS, 2)),
                dma((LAYERS, maps_here)),
                dma((LAYERS, maps_here)),
                dma((LAYERS, maps_here)),
                dma((LAYERS, maps_here)),
                dma((3,)),
                dma((3,)),
                dma((3,)),
                dma((LAYERS,)),
                dma((LAYERS,)),
                dma((LAYERS, 2, maps_here)),
                dma((LAYERS, maps_here)),
                dma((UNITS,)),
                dma((UNITS,)),
                dma((UNITS,)),
                dma((UNITS,)),
                dma((UNITS, owners)),
                dma((UNITS, actives - 1)),
                dma((UNITS, actives)),
                dma((UNITS, owners)),
                dma((UNITS,)),
                dma((UNITS,)),
                dma((UNITS,)),
                dma((UNITS,)),
                dma((UNITS,)),
                dma((UNITS,)),
                dma((UNITS,)),
                dma((UNITS,)),
                dma((UNITS,)),
                dma((UNITS,)),
                dma((UNITS,)),
            ],
            compiler_params=pltpu.CompilerParams(
                collective_id=0,
                has_side_effects=True,
                vmem_limit_bytes=grant,
            ),
        )(
            block_input,
            conv_weights,
            *(
                pltpu.with_memory_space_constraint(v, pltpu.HBM)
                for v in (
                    norm_gains,
                    norm_shifts,
                    map_width,
                    map_group,
                    index_rows,
                    task_mask,
                    task_weights,
                    task_grads,
                )
            ),
        )
        input_grad = jnp.concatenate([ig[0], ig[1]], -1)[:, :, :columns]
        kernel_grads, pooled, gain_grads, shift_grads = pl.pallas_call(
            finish_kernel,
            out_shape=(
                jax.ShapeDtypeStruct(kg.shape, F32),
                jax.ShapeDtypeStruct(pool_index.shape, BF16),
                jax.ShapeDtypeStruct(norm_gains.shape, F32),
                jax.ShapeDtypeStruct(norm_shifts.shape, F32),
            ),
            in_specs=[whole] * 3,
            out_specs=(anywhere, whole, whole, whole),
            scratch_shapes=[vmem((RING,) + kg.shape[1:], F32), dma((RING,))],
            compiler_params=pltpu.CompilerParams(vmem_limit_bytes=24 * 1024 * 1024),
        )(kg, pooled, sums)
        return (
            pooled,
            input_grad,
            kernel_grads.reshape(conv_weights.shape),
            gain_grads,
            shift_grads,
        )

    return jax.shard_map(
        per_device,
        mesh=mesh,
        in_specs=(
            P("maps", "rows", None, None),
            P(),
            P(),
            P(),
            P(),
            P(),
            P("maps", "rows", None, None),
            P("maps", None),
            P(),
            P(None, "maps", "rows", None, None),
        ),
        out_specs=(P("maps", "rows", None, None), P("maps", "rows", None, None), P(), P(), P()),
        check_vma=False,
    )
```
